32 devices in a mesh: section: 2 (over y), seq: 2 (over x), dp: 8 (over z, core).
Axes of the slice: x: 2, y: 2, z: 4, core: 2. Of those that a mesh axis runs over, the one named last changes fastest.
Arguments:
- layer_input: bfloat16 [2, 2, 8, 1024, 512], P('section', None, 'dp', 'seq'), may hold values from -6 to 6
- segment_ids: int32 [2, 2, 8, 1024], P('section', None, 'dp', 'seq'), may hold values from 0 to 3, as said below
- attn_qkv: bfloat16 [2, 512, 1536], P('section'), may hold values from -0.25 to 0.25
- attn_out: bfloat16 [2, 512, 512], P('section'), may hold values from -2 to 2
- ffn_in: bfloat16 [2, 512, 2048], P('section'), may hold values from -0.25 to 0.25
- ffn_out: bfloat16 [2, 2048, 512], P('section'), may hold values from -0.1875 to 0.1875
- norm_gain: float32 [2, 2, 512], P('section'), may hold values from 0.25 to 1.75
- cross_query: bfloat16 [512, 512], replicated, may hold values from -0.25 to 0.25
- cross_pair: bfloat16 [512, 1024], replicated, may hold values from -0.25 to 0.25
- cross_out: bfloat16 [512, 512], replicated, may hold values from -2 to 2
- cross_gain: float32 [512], replicated, may hold values from 0.25 to 1.75
- out_cotangent: bfloat16 [2, 8, 1024, 512], P(None, 'dp', 'seq'), may hold values from -6 to 6
Outputs:
- layer_output: bfloat16 [2, 2, 8, 1024, 512], P('section', None, 'dp', 'seq')
- input_grad: float32 [2, 2, 8, 1024, 512], P('section', None, 'dp', 'seq')
- grad_attn_qkv: float32 [2, 512, 1536], P('section')
- grad_attn_out: float32 [2, 512, 512], P('section')
- grad_ffn_in: float32 [2, 512, 2048], P('section')
- grad_ffn_out: float32 [2, 2048, 512], P('section')
- grad_norm_gain: float32 [2, 2, 512], P('section')
- grad_cross_query: float32 [512, 512], replicated
- grad_cross_pair: float32 [512, 1024], replicated
- grad_cross_out: float32 [512, 512], replicated
- grad_cross_gain: float32 [512], replicated
The draws below stay inside these ranges and needn't reach their ends.
Inputs may be any that keep to these rules, and one draw needn't show every extreme that they name: `segment_ids`: along a row the numbers never fall and rise by one where a document starts. The source side (index 0) and the target side (index 1) of a row hold the same number of documents: 4 in every row except one of the 2 rows that one index of dp holds, which is a single document on both sides.
All inputs are finite; a program needn't handle non-finite values.
Results may differ from the reference program's by a relative error of at most 0.033.
Values may be sent and summed in bfloat16 or wider, within the bound.
No kernel may reach another device: no remote copies, remote signals or barrier semaphores. Data moves between devices by JAX's collectives and lax.ppermute only.
A program may use at most 320 MiB of HBM per device.

```python
import jax
import jax.numpy as jnp
from jax import lax

D = 512
HEADS = 8
FF = 2048
HEAD_DIM = 64
ROW_LEN = 1024
SEGS = 4
MICRO = 2
ROWS_MB = 1
BATCH = 8


def draw_segment_ids(key, part):
    key = jax.random.fold_in(key, 11)
    row_count = 2 * MICRO * BATCH
    row_keys = jax.random.split(key, row_count)

    def cut_points(row_key):
        return jax.random.permutation(row_key, ROW_LEN - 1)[:SEGS - 1] + 1
    cut_places = jax.vmap(cut_points)(row_keys).astype(jnp.int32)
    places = jnp.arange(ROW_LEN, dtype=jnp.int32)
    numbers = jnp.sum((places[None, :, None] >= cut_places[:, None, :]).astype(jnp.int32), axis=-1)
    numbers = numbers.reshape(2, MICRO, BATCH, ROW_LEN)
    group_pick = jax.random.randint(jax.random.fold_in(key, 1), (BATCH // ROWS_MB,), 0, MICRO * ROWS_MB)
    row_index = jnp.arange(BATCH)
    picked = group_pick[row_index // ROWS_MB]
    single_doc = (jnp.arange(MICRO)[:, None] == picked[None, :] // ROWS_MB) & ((row_index % ROWS_MB)[None, :] == picked[None, :] % ROWS_MB)
    return jnp.where(single_doc[None, :, :, None], 0, numbers).astype(jnp.int32)


def level_of(own_key, dims, shards, low, high):
    gain = 1.0
    for position, shards_of in shards:
        heights = jax.random.uniform(jax.random.fold_in(jax.random.fold_in(own_key, 6), position), (shards_of,), jnp.float32, low / len(shards), high / len(shards))
        gain = gain * jnp.repeat(jnp.exp(heights), dims[position] // shards_of).reshape((-1,) + (1,) * (len(dims) - 1 - position))
    return gain


def bell_draw(key, shape, scale, most, cuts=(), kind=jnp.bfloat16):
    entries = scale * jax.random.normal(key, shape, jnp.float32)
    if cuts:
        entries = entries * level_of(key, shape, cuts, -0.22, 0.18)
    return jnp.clip(entries, -most, most).astype(kind)


def setup_inputs(seed: int = 0) -> dict:
    key_of = jax.random.split(jax.random.key(seed), 13)
    layer_input = bell_draw(key_of[0], (2, MICRO, BATCH, ROW_LEN, D), 1.0, 6.0, ((0, 2), (2, 8), (3, 2)))
    segment_ids = draw_segment_ids(jax.random.fold_in(key_of[12], 71), 0)
    attn_qkv = bell_draw(key_of[2], (2, D, 3 * D), D ** -0.5, 0.25, ((0, 2),))
    attn_out = bell_draw(key_of[3], (2, D, D), (max(D // 64, 8)) ** -0.5, 2.0, ((0, 2),))
    ffn_in = bell_draw(key_of[4], (2, D, FF), D ** -0.5, 0.25, ((0, 2),))
    ffn_out = bell_draw(key_of[5], (2, FF, D), (FF // 2) ** -0.5, 0.1875, ((0, 2),))
    norm_gain = jnp.clip(1.0 + 0.15 * jax.random.normal(key_of[6], (2, 2, D), jnp.float32), 0.25, 1.75)
    cross_query = bell_draw(key_of[7], (D, D), D ** -0.5, 0.25)
    cross_pair = bell_draw(key_of[8], (D, 2 * D), D ** -0.5, 0.25)
    cross_out = bell_draw(key_of[9], (D, D), (max(D // 64, 8)) ** -0.5, 2.0)
    cross_gain = jnp.clip(1.0 + 0.15 * jax.random.normal(key_of[10], (D,), jnp.float32), 0.25, 1.75)
    out_cotangent = bell_draw(key_of[11], (MICRO, BATCH, ROW_LEN, D), 1.0, 6.0, ((1, 8), (2, 2)))
    return {"layer_input": layer_input, "segment_ids": segment_ids, "attn_qkv": attn_qkv, "attn_out": attn_out, "ffn_in": ffn_in, "ffn_out": ffn_out, "norm_gain": norm_gain, "cross_query": cross_query, "cross_pair": cross_pair, "cross_out": cross_out, "cross_gain": cross_gain, "out_cotangent": out_cotangent}


@jax.custom_vjp
def low(v):
    return lax.optimization_barrier(v.astype(jnp.bfloat16)).astype(jnp.float32)

@jax.custom_vjp
def low_back(v):
    return v

def low_keep(v):
    return (low(v), None)

def low_pass(kept, grad):
    return (grad,)

def back_keep(v):
    return (v, None)

def back_low(kept, grad):
    return (low(grad),)
low.defvjp(low_keep, low_pass)
low_back.defvjp(back_keep, back_low)
highest = lax.Precision.HIGHEST
negative_big = -1e+30
epsilon = 1e-05

def low_both(values):
    return low_back(low(values))

def project(left_side, right_side):
    return jnp.einsum('rsd,de->rse', left_side, right_side, precision=highest)

def layer_norm(values, gain_row):
    center = values - lax.optimization_barrier(jnp.mean(values, axis=-1, keepdims=True))
    spread = lax.optimization_barrier(jnp.mean(center * center, axis=-1, keepdims=True))
    return center * lax.rsqrt(spread + epsilon) * gain_row

def attention(queries, keys_all, values_all, query_docs, key_docs, causal):
    score_scale = HEAD_DIM ** (-0.5)

    def one_row(row_args):
        query_row, key_row, value_row, query_doc, key_doc = row_args
        query_heads = query_row.reshape(ROW_LEN, HEADS, HEAD_DIM)
        key_heads = key_row.reshape(ROW_LEN, HEADS, HEAD_DIM)
        value_heads = value_row.reshape(ROW_LEN, HEADS, HEAD_DIM)
        raw_scores = low_back(jnp.einsum('qhd,khd->hqk', query_heads, key_heads, precision=highest))
        scores = raw_scores * score_scale
        allowed = query_doc[:, None] == key_doc[None, :]
        if causal:
            places = jnp.arange(ROW_LEN)
            allowed = allowed & (places[:, None] >= places[None, :])
        scores = jnp.where(allowed[None], scores, negative_big)
        row_top = lax.optimization_barrier(jnp.max(scores, axis=-1, keepdims=True))
        expo_vals = jnp.where(allowed[None], jnp.exp(scores - row_top), 0.0)
        probs = expo_vals / lax.optimization_barrier(jnp.sum(expo_vals, axis=-1, keepdims=True))
        output = jnp.einsum('hqk,khd->qhd', low(probs), value_heads, precision=highest)
        return output.reshape(ROW_LEN, D)
    return lax.map(jax.checkpoint(one_row), (queries, keys_all, values_all, query_docs, key_docs))

def forward(params_in, source, target, source_docs, target_docs):
    qkv_all, out_all, in_all, down_all, gains_all, query_weight, pair_weight, cross_weight, cross_gains = params_in

    def self_block(hidden_in, section_at, doc_ids, causal):
        mixed = low_both(project(low(hidden_in), qkv_all[section_at]))
        attended = low_both(attention(mixed[..., :D], mixed[..., D:2 * D], mixed[..., 2 * D:], doc_ids, doc_ids, causal))
        branch = low_back(project(attended, out_all[section_at]))
        return layer_norm(hidden_in + branch, gains_all[section_at, 0])

    def feed_block(hidden_in, section_at):
        upward = low_back(project(low(hidden_in), in_all[section_at]))
        active = low_both(jax.nn.silu(upward))
        branch = low_back(project(active, down_all[section_at]))
        return layer_norm(hidden_in + branch, gains_all[section_at, 1])
    encoded = feed_block(self_block(source, 0, source_docs, False), 0)
    memory = low(encoded)
    first = self_block(target, 1, target_docs, True)
    cross_queries = low_both(project(low(first), query_weight))
    pair = low_both(project(memory, pair_weight))
    cross_att = low_both(attention(cross_queries, pair[..., :D], pair[..., D:], target_docs, source_docs, False))
    branch = low_back(project(cross_att, cross_weight))
    second = layer_norm(first + branch, cross_gains)
    return (memory, feed_block(second, 1))

def reference(layer_input, segment_ids, attn_qkv, attn_out, ffn_in, ffn_out, norm_gain, cross_query, cross_pair, cross_out, cross_gain, out_cotangent):
    row_total = MICRO * BATCH
    inputs_all = layer_input.astype(jnp.float32).reshape(2, row_total, ROW_LEN, D)
    docs_all = segment_ids.reshape(2, row_total, ROW_LEN)
    params = (attn_qkv.astype(jnp.float32), attn_out.astype(jnp.float32), ffn_in.astype(jnp.float32), ffn_out.astype(jnp.float32), norm_gain.astype(jnp.float32), cross_query.astype(jnp.float32), cross_pair.astype(jnp.float32), cross_out.astype(jnp.float32), cross_gain.astype(jnp.float32))

    def whole_layer(params_in, source, target):
        return forward(params_in, source, target, docs_all[0], docs_all[1])
    (memory, decoded), pullback = jax.vjp(whole_layer, params, inputs_all[0], inputs_all[1])
    cotangent = out_cotangent.astype(jnp.float32).reshape(row_total, ROW_LEN, D)
    weight_grads, grad_source, grad_target = pullback((jnp.zeros_like(memory), cotangent))
    layer_output = jnp.stack([memory, decoded]).astype(jnp.bfloat16).reshape(2, MICRO, BATCH, ROW_LEN, D)
    input_grad = jnp.stack([grad_source, grad_target]).reshape(2, MICRO, BATCH, ROW_LEN, D)
    return (layer_output, input_grad, weight_grads[0], weight_grads[1], weight_grads[2], weight_grads[3], weight_grads[4], weight_grads[5], weight_grads[6], weight_grads[7], weight_grads[8])
```

```python
import types

import jax
import jax.numpy as jnp
from jax import lax
from jax.experimental import pallas as pl
from jax.experimental.pallas import tpu as pltpu
from jax.sharding import PartitionSpec as P

HEADS = 8
TILE = 256
LANES = 128
CHUNK = 512

f32 = jnp.float32
bf16 = jnp.bfloat16
negative_big = -1e30
epsilon = 1e-05


def dot(left, right):
    return lax.dot_general(left, right, (((1,), (0,)), ((), ())), preferred_element_type=f32)


def dot_nt(left, right):
    return lax.dot_general(left, right, (((1,), (1,)), ((), ())), preferred_element_type=f32)


def dot_tn(left, right):
    return lax.dot_general(left, right, (((0,), (0,)), ((), ())), preferred_element_type=f32)


def standardize(values):
    center = values - jnp.mean(values, axis=-1, keepdims=True)
    inverse = lax.rsqrt(jnp.mean(center * center, axis=-1, keepdims=True) + epsilon)
    return center * inverse, inverse


def standardize_back(grad_out, standard, gain_row, inverse):
    scaled = grad_out * gain_row
    grad_in = inverse * (
        scaled
        - jnp.mean(scaled, axis=-1, keepdims=True)
        - standard * jnp.mean(scaled * standard, axis=-1, keepdims=True)
    )
    return grad_in, jnp.sum(grad_out * standard, axis=0, keepdims=True)


class Copies:
    def __init__(self, sems):
        self.sems = sems
        self.used = 0

    def start(self, source, target):
        copy = pltpu.make_async_copy(source, target, self.sems.at[self.used])
        self.used += 1
        copy.start()
        return copy


def wait_all(copies):
    for copy in copies:
        copy.wait()


def spread_pairs(target, source, factor):
    pairs, tiles = target.shape[:2]
    half = lax.broadcasted_iota(jnp.int32, (TILE, LANES), 1) < LANES // 2
    first = jnp.where(half, factor, 0.0).astype(bf16)
    second = jnp.where(half, 0.0, factor).astype(bf16)
    for tile in range(tiles):
        for pair in range(pairs):
            block = source[tile * TILE : (tile + 1) * TILE, pair * LANES : (pair + 1) * LANES]
            target[pair, tile, :TILE, :] = block * first
            target[pair, tile, TILE:, :] = block * second


def turn_tiles(target, source, column):
    tiles, width, _ = target.shape
    for tile in range(tiles):
        block = source[tile * TILE : (tile + 1) * TILE, column : column + width]
        target[tile] = jnp.transpose(block.astype(f32)).astype(bf16)


def turn_documents(target, key_docs):
    for start in range(0, target.shape[0], LANES):
        row = key_docs[:, start : start + LANES]
        target[start : start + LANES, :] = jnp.transpose(jnp.broadcast_to(row, (LANES, LANES)))


def tile_place(r, core, causal, q_tile, k_tile):
    q_tiles = r.qd.shape[0]
    length = q_tiles * TILE
    owner = jnp.where(k_tile < q_tiles, core, 1 - core)
    k_start = owner * length + lax.rem(k_tile, q_tiles) * TILE
    ahead = core * length + q_tile * TILE - k_start
    ahead = jnp.where(causal == 1, ahead, 2 * length * TILE)
    q_low, q_high = r.qd_s[q_tile * TILE], r.qd_s[q_tile * TILE + TILE - 1]
    k_low, k_high = r.kd_s[k_tile * TILE], r.kd_s[k_tile * TILE + TILE - 1]
    active = (q_low <= k_high) & (k_low <= q_high) & (ahead > -TILE)
    return active, ahead


def fill_bias(r, q_tile, k_tile, ahead):
    keys = r.kdc[pl.ds(pl.multiple_of(k_tile * TILE, TILE), TILE), :]
    shift = lax.broadcasted_iota(jnp.int32, (TILE, LANES), 0) - lax.broadcasted_iota(
        jnp.int32, (TILE, LANES), 1
    )
    queries = r.qd[q_tile]
    for start in range(0, TILE, LANES):
        same = keys == queries[:, start : start + LANES]
        allowed = same & (shift - start <= ahead)
        r.bias[:, start : start + LANES] = jnp.where(allowed, 0.0, negative_big)


def attention_forward(r, core, causal):
    pairs, q_tiles = r.qm.shape[:2]
    k_tiles = r.vt.shape[0]

    def one_query_tile(q_tile, carry):
        r.top[...] = jnp.full(r.top.shape, negative_big, f32)
        r.total[...] = jnp.zeros(r.total.shape, f32)
        r.turned[...] = jnp.zeros(r.turned.shape, f32)

        def one_key_tile(k_tile, inner):
            active, ahead = tile_place(r, core, causal, q_tile, k_tile)

            @pl.when(active)
            def _():
                fill_bias(r, q_tile, k_tile, ahead)
                rows = pl.ds(pl.multiple_of(k_tile * TILE, TILE), TILE)

                def raw(pair):
                    keys = r.kv[rows, pair * LANES : (pair + 1) * LANES]
                    return dot_nt(keys, r.qm[pair, q_tile])

                raw_next = raw(0)
                for pair in range(pairs):
                    bias = r.bias[...]
                    scores = raw_next + jnp.concatenate([bias, bias], axis=1)
                    if pair + 1 < pairs:
                        raw_next = raw(pair + 1)
                    old_top = r.top[pair : pair + 1, :]
                    new_top = jnp.maximum(old_top, jnp.max(scores, axis=0, keepdims=True))
                    weights = jnp.exp(scores - new_top)
                    shrink = jnp.exp(old_top - new_top)
                    r.top[pair : pair + 1, :] = new_top
                    r.total[pair : pair + 1, :] = r.total[
                        pair : pair + 1, :
                    ] * shrink + jnp.sum(weights, axis=0, keepdims=True)
                    low = weights.astype(bf16)
                    for side in range(2):
                        span = slice(side * TILE, (side + 1) * TILE)
                        head = slice((2 * pair + side) * 64, (2 * pair + side + 1) * 64)
                        r.turned[head, :] = r.turned[head, :] * shrink[:, span] + dot(
                            r.vt[k_tile, head, :], low[:, span]
                        )

            return inner

        lax.fori_loop(0, k_tiles, one_key_tile, 0)
        for pair in range(pairs):
            total = r.total[pair : pair + 1, :]
            r.lse[q_tile, pair : pair + 1, :] = r.top[pair : pair + 1, :] + jnp.log(total)
            share = 1.0 / total
            for side in range(2):
                span = slice(side * TILE, (side + 1) * TILE)
                head = slice((2 * pair + side) * 64, (2 * pair + side + 1) * 64)
                r.turned[head, :] = r.turned[head, :] * share[:, span]
        rows = pl.ds(pl.multiple_of(q_tile * TILE, TILE), TILE)
        r.att[rows, :] = jnp.transpose(r.turned[...]).astype(bf16)
        return carry

    lax.fori_loop(0, q_tiles, one_query_tile, 0)


def row_products(r, grad_att):
    pairs, q_tiles = r.qm.shape[:2]
    for tile in range(q_tiles):
        rows = slice(tile * TILE, (tile + 1) * TILE)
        product = jnp.transpose(grad_att[rows, :].astype(f32) * r.att[rows, :].astype(f32))
        for pair in range(pairs):
            for side in range(2):
                head = (2 * pair + side) * 64
                r.delta[tile, pair : pair + 1, side * TILE : (side + 1) * TILE] = jnp.sum(
                    product[head : head + 64, :], axis=0, keepdims=True
                )


def attention_backward(r, core, causal):
    pairs, q_tiles = r.qm.shape[:2]
    k_tiles = r.kt.shape[0]
    width = pairs * LANES
    r.dkv[...] = jnp.zeros(r.dkv.shape, f32)

    def one_query_tile(q_tile, carry):
        r.turned[...] = jnp.zeros(r.turned.shape, f32)

        def one_key_tile(k_tile, inner):
            active, ahead = tile_place(r, core, causal, q_tile, k_tile)

            @pl.when(active)
            def _():
                fill_bias(r, q_tile, k_tile, ahead)
                rows = pl.ds(pl.multiple_of(k_tile * TILE, TILE), TILE)

                def raw(pair):
                    lanes = slice(pair * LANES, (pair + 1) * LANES)
                    lanes_v = slice(width + pair * LANES, width + (pair + 1) * LANES)
                    return (
                        dot_nt(r.kv[rows, lanes], r.qm[pair, q_tile]),
                        dot_nt(r.kv[rows, lanes_v], r.gm[pair, q_tile]),
                    )

                raw_next = raw(0)
                for pair in range(pairs):
                    bias = r.bias[...]
                    scores, grad_probs = raw_next
                    scores = scores + jnp.concatenate([bias, bias], axis=1)
                    if pair + 1 < pairs:
                        raw_next = raw(pair + 1)
                    probs = jnp.exp(scores - r.lse[q_tile, pair : pair + 1, :])
                    grad_scores = probs * (grad_probs - r.delta[q_tile, pair : pair + 1, :])
                    probs_low = probs.astype(bf16)
                    grad_low = grad_scores.astype(bf16)
                    lanes = slice(pair * LANES, (pair + 1) * LANES)
                    lanes_v = slice(width + pair * LANES, width + (pair + 1) * LANES)
                    r.dkv[rows, lanes] += dot(grad_low, r.qm[pair, q_tile])
                    r.dkv[rows, lanes_v] += dot(probs_low, r.gm[pair, q_tile])
                    for side in range(2):
                        span = slice(side * TILE, (side + 1) * TILE)
                        head = slice((2 * pair + side) * 64, (2 * pair + side + 1) * 64)
                        r.turned[head, :] += dot(r.kt[k_tile, head, :], grad_low[:, span])

            return inner

        lax.fori_loop(0, k_tiles, one_key_tile, 0)
        rows = pl.ds(pl.multiple_of(q_tile * TILE, TILE), TILE)
        r.dq[rows, :] = jnp.transpose(r.turned[...]) * (64**-0.5)
        return carry

    lax.fori_loop(0, q_tiles, one_query_tile, 0)


def feed_forward(r, low):
    r.sum[...] = jnp.zeros(r.sum.shape, f32)

    def one_chunk(chunk, carry):
        span = pl.ds(pl.multiple_of(chunk * CHUNK, CHUNK), CHUNK)
        upward = dot(low[...], r.w_in[:, span])
        gate = jax.nn.sigmoid(upward)
        active = (upward * gate).astype(bf16)
        r.act[:, span] = active
        r.slope[:, span] = (gate + upward * gate * (1.0 - gate)).astype(r.slope.dtype)
        r.sum[...] += dot(active, r.w_down[span, :])
        return carry

    lax.fori_loop(0, r.w_in.shape[1] // CHUNK, one_chunk, 0)


def feed_backward(r):
    r.sum[...] = jnp.zeros(r.sum.shape, f32)

    def one_chunk(chunk, carry):
        span = pl.ds(pl.multiple_of(chunk * CHUNK, CHUNK), CHUNK)
        grad_active = dot_nt(r.down_grad[...], r.w_down[span, :]).astype(bf16)
        grad_up = (grad_active.astype(f32) * r.slope[:, span].astype(f32)).astype(bf16)
        r.up_grad[:, span] = grad_up
        r.sum[...] += dot_nt(grad_up, r.w_in[:, span])
        return carry

    lax.fori_loop(0, r.w_in.shape[1] // CHUNK, one_chunk, 0)


def self_forward_kernel(r):
    length, width = r.x_h.shape
    core = r.meta[2]
    decoder = r.meta[1]
    move = Copies(r.sems)
    moves = [
        move.start(r.q_h, r.q),
        move.start(r.kv_h, r.kv.at[pl.ds(0, length)]),
        move.start(r.kv_other_h, r.kv.at[pl.ds(length, length)]),
        move.start(r.x_h, r.x),
        move.start(r.w_out_h, r.w_out),
    ]
    turn_documents(r.kdc, r.kd)
    wait_all(moves[:3])
    spread_pairs(r.qm, r.q, 64**-0.5)
    turn_tiles(r.vt, r.kv, width)
    attention_forward(r, core, decoder)
    wait_all(moves[3:])
    outs = [move.start(r.att, r.att_o), move.start(r.lse, r.lse_o)]
    unit, inverse = standardize(r.x[...].astype(f32) + dot(r.att[...], r.w_out[...]))
    r.unit1[...] = unit
    r.inv1[...] = jnp.broadcast_to(inverse, r.inv1.shape)
    first = unit * r.gains[0:1, :]
    r.first_low[...] = first.astype(bf16)
    outs += [
        move.start(r.unit1, r.unit1_o),
        move.start(r.inv1, r.inv1_o),
        move.start(r.first_low, r.first_low_o),
    ]

    @pl.when(decoder == 0)
    def _():
        weights = [move.start(r.w_in_h, r.w_in), move.start(r.w_down_h, r.w_down)]
        wait_all(weights)
        feed_forward(r, r.first_low)
        late = [
            move.start(r.first_low, r.ffn_low_o),
            move.start(r.act, r.act_o),
            move.start(r.slope, r.slope_o),
        ]
        unit2, inverse2 = standardize(r.unit1[...] * r.gains[0:1, :] + r.sum[...])
        r.unit2[...] = unit2
        r.inv2[...] = jnp.broadcast_to(inverse2, r.inv2.shape)
        r.memory[...] = (unit2 * r.gains[1:2, :]).astype(bf16)
        late += [
            move.start(r.memory, r.memory_o),
            move.start(r.unit2, r.unit2_o),
            move.start(r.inv2, r.inv2_o),
        ]
        wait_all(late)

    wait_all(outs)


def cross_kernel(r):
    @pl.when(r.meta[0] == 1)
    def _():
        cross_body(r)


def cross_body(r):
    length, width = r.unit1_h.shape
    core = r.meta[2]
    move = Copies(r.sems)
    moves = [
        move.start(r.pair_h, r.kv.at[pl.ds(0, length)]),
        move.start(r.pair_other_h, r.kv.at[pl.ds(length, length)]),
        move.start(r.first_low_h, r.first_low),
        move.start(r.w_query_h, r.w_query),
    ]
    later = [
        move.start(r.unit1_h, r.unit1),
        move.start(r.w_cross_h, r.w_cross),
        move.start(r.w_in_h, r.w_in),
        move.start(r.w_down_h, r.w_down),
        move.start(r.cot_h, r.cot),
    ]
    turn_documents(r.kdc, r.kd)
    wait_all(moves)
    r.q[...] = dot(r.first_low[...], r.w_query[...]).astype(bf16)
    spread_pairs(r.qm, r.q, 64**-0.5)
    turn_tiles(r.vt, r.kv, width)
    turn_tiles(r.kt, r.kv, 0)
    attention_forward(r, core, 0)
    outs = [move.start(r.att, r.att_o)]
    wait_all(later)
    first = r.unit1[...] * r.gains[0:1, :]
    unit, inverse = standardize(first + dot(r.att[...], r.w_cross[...]))
    r.unit2[...] = unit
    r.inv2[...] = jnp.broadcast_to(inverse, r.inv2.shape)
    r.second_low[...] = (unit * r.cross_gain[...]).astype(bf16)
    outs += [move.start(r.second_low, r.ffn_low_o)]
    feed_forward(r, r.second_low)
    outs += [move.start(r.act, r.act_o)]
    unit3, inverse3 = standardize(r.unit2[...] * r.cross_gain[...] + r.sum[...])
    r.decoded[...] = (unit3 * r.gains[1:2, :]).astype(bf16)
    outs += [move.start(r.decoded, r.decoded_o)]
    grad_third, gain_late = standardize_back(
        r.cot[...].astype(f32), unit3, r.gains[1:2, :], inverse3
    )
    r.keep[...] = grad_third
    r.down_grad[...] = grad_third.astype(bf16)
    outs += [move.start(r.down_grad, r.down_grad_o)]
    feed_backward(r)
    outs += [move.start(r.up_grad, r.up_grad_o)]
    grad_sum, gain_cross = standardize_back(
        r.keep[...] + r.sum[...], r.unit2[...], r.cross_gain[...], r.inv2[:, 0:1]
    )
    r.gain_grads[...] = jnp.zeros(r.gain_grads.shape, f32)
    r.gain_grads[0:1, :] = gain_late
    r.gain_grads[1:2, :] = gain_cross
    r.keep[...] = grad_sum
    r.branch[...] = grad_sum.astype(bf16)
    outs += [move.start(r.gain_grads, r.gain_grads_o), move.start(r.branch, r.branch_o)]
    r.q[...] = dot_nt(r.branch[...], r.w_cross[...]).astype(bf16)
    spread_pairs(r.gm, r.q, 1.0)
    row_products(r, r.q)
    attention_backward(r, core, 0)
    r.dkv_other[...] = r.dkv[length:, :].astype(bf16)
    outs += [move.start(r.dkv.at[pl.ds(0, length)], r.dkv_own_o), move.start(r.dkv_other, r.dkv_other_o)]
    r.dq_low[...] = r.dq[...].astype(bf16)
    r.keep[...] += dot_nt(r.dq_low[...], r.w_query[...])
    outs += [move.start(r.dq_low, r.dq_low_o), move.start(r.keep, r.grad_first_o)]
    wait_all(outs)


def self_backward_kernel(r):
    @pl.when(r.meta[0] == 1)
    def _():
        self_backward_body(r)


def self_backward_body(r):
    length, width = r.unit1_h.shape
    core = r.meta[2]
    decoder = r.meta[1]
    move = Copies(r.sems)
    moves = [
        move.start(r.unit1_h, r.unit1),
        move.start(r.inv1_h, r.inv1),
        move.start(r.w_out_h, r.w_out),
        move.start(r.q_h, r.q),
        move.start(r.kv_h, r.kv.at[pl.ds(0, length)]),
        move.start(r.kv_other_h, r.kv.at[pl.ds(length, length)]),
        move.start(r.att_h, r.att),
        move.start(r.lse_h, r.lse),
    ]
    turn_documents(r.kdc, r.kd)
    r.gain_grads[...] = jnp.zeros(r.gain_grads.shape, f32)

    @pl.when(decoder == 1)
    def _():
        wait_all([move.start(r.grad_first_h, r.keep)])

    @pl.when(decoder == 0)
    def _():
        loads = [
            move.start(r.grad_memory_h, r.cot),
            move.start(r.unit2_h, r.unit2),
            move.start(r.inv2_h, r.inv2),
            move.start(r.w_in_h, r.w_in),
            move.start(r.w_down_h, r.w_down),
            move.start(r.slope_h, r.slope),
        ]
        wait_all(loads)
        grad_third, gain_late = standardize_back(
            r.cot[...].astype(f32), r.unit2[...], r.gains[1:2, :], r.inv2[:, 0:1]
        )
        r.gain_grads[1:2, :] = gain_late
        r.keep[...] = grad_third
        r.down_grad[...] = grad_third.astype(bf16)
        stores = [move.start(r.down_grad, r.down_grad_o)]
        feed_backward(r)
        r.keep[...] += r.sum[...]
        stores += [move.start(r.up_grad, r.up_grad_o)]
        wait_all(stores)

    wait_all(moves)
    grad_sum, gain_early = standardize_back(
        r.keep[...], r.unit1[...], r.gains[0:1, :], r.inv1[:, 0:1]
    )
    r.gain_grads[0:1, :] = gain_early
    r.keep[...] = grad_sum
    r.branch[...] = grad_sum.astype(bf16)
    outs = [
        move.start(r.gain_grads, r.gain_grads_o),
        move.start(r.keep, r.grad_sum_o),
        move.start(r.branch, r.branch_o),
    ]
    spread_pairs(r.qm, r.q, 64**-0.5)
    turn_tiles(r.kt, r.kv, 0)
    r.grad_att[...] = dot_nt(r.branch[...], r.w_out[...]).astype(bf16)
    spread_pairs(r.gm, r.grad_att, 1.0)
    row_products(r, r.grad_att)
    attention_backward(r, core, decoder)
    r.dkv_other[...] = r.dkv[length:, :].astype(bf16)
    r.dq_low[...] = r.dq[...].astype(bf16)
    outs += [
        move.start(r.dkv.at[pl.ds(0, length)], r.dkv_own_o),
        move.start(r.dkv_other, r.dkv_other_o),
        move.start(r.dq_low, r.dq_low_o),
    ]
    wait_all(outs)


def launch(kernel, scalars, small, large, outs, scratch, copies, flops, previous=None):
    names = list(scalars) + list(small) + list(large)
    arrays = list(scalars.values()) + list(small.values()) + list(large.values())
    specs = (
        [pl.BlockSpec(memory_space=pltpu.SMEM)] * len(scalars)
        + [pl.BlockSpec(memory_space=pltpu.VMEM)] * len(small)
        + [pl.BlockSpec(memory_space=pl.ANY)] * len(large)
    )
    aliases = dict()
    for position, name in enumerate(outs):
        if previous and name in previous:
            aliases[len(arrays)] = position
            names.append("previous_" + name)
            arrays.append(previous[name])
            specs.append(pl.BlockSpec(memory_space=pl.ANY))
    names += list(outs) + list(scratch) + ["sems"]

    def body(*refs):
        kernel(types.SimpleNamespace(**dict(zip(names, refs))))

    moved = sum(a.size * a.dtype.itemsize for a in large.values())
    results = pl.pallas_call(
        body,
        out_shape=[jax.ShapeDtypeStruct(*shape) for shape in outs.values()],
        in_specs=specs,
        out_specs=[pl.BlockSpec(memory_space=pl.ANY)] * len(outs),
        scratch_shapes=[pltpu.VMEM(*shape) for shape in scratch.values()]
        + [pltpu.SemaphoreType.DMA((copies,))],
        input_output_aliases=aliases,
        compiler_params=pltpu.CompilerParams(vmem_limit_bytes=56 * 1024 * 1024),
        cost_estimate=pl.CostEstimate(flops=flops, bytes_accessed=moved, transcendentals=0),
    )(*arrays)
    return types.SimpleNamespace(**dict(zip(outs, results)))


def attention_scratch(length, width):
    pairs, q_tiles, k_tiles = width // LANES, length // TILE, 2 * length // TILE
    return dict(
        q=((length, width), bf16),
        kv=((2 * length, 2 * width), bf16),
        qm=((pairs, q_tiles, 2 * TILE, LANES), bf16),
        kdc=((2 * length, LANES), f32),
        bias=((TILE, TILE), f32),
        lse=((q_tiles, 8, 2 * TILE), f32),
        att=((length, width), bf16),
        turned=((width, TILE), f32),
    )


def forward_scratch(length, width):
    k_tiles = 2 * length // TILE
    return dict(
        vt=((k_tiles, width, TILE), bf16),
        top=((8, 2 * TILE), f32),
        total=((8, 2 * TILE), f32),
    )


def backward_scratch(length, width):
    pairs, q_tiles, k_tiles = width // LANES, length // TILE, 2 * length // TILE
    return dict(
        kt=((k_tiles, width, TILE), bf16),
        gm=((pairs, q_tiles, 2 * TILE, LANES), bf16),
        delta=((q_tiles, 8, 2 * TILE), f32),
        dkv=((2 * length, 2 * width), f32),
        dq=((length, width), f32),
        dkv_other=((length, 2 * width), bf16),
        dq_low=((length, width), bf16),
    )


def for_sending(shard):

    def short(part):
        return part.astype(jnp.bfloat16) if part.dtype == jnp.float32 else part

    return jax.tree.map(short, shard)


def from_behind(block, axis, distance):
    devices = range(lax.axis_size(axis))
    route = [(i - distance, i) for i in devices if i - distance in devices]
    return lax.ppermute(block, axis, route)


def from_root(shard, axis, root):
    mine = lax.axis_index(axis) == root
    return lax.psum(jnp.where(mine, shard, jnp.zeros_like(shard)), axis)


def matmul(left_side, right_side):
    return jnp.einsum("rsd,de->rse", left_side, right_side, preferred_element_type=jnp.float32)


def matmul_back(left_side, right_side):
    return jnp.einsum("rse,de->rsd", left_side, right_side, preferred_element_type=jnp.float32)


def contract(left_side, right_side):
    return jnp.einsum("rsd,rse->de", left_side, right_side, preferred_element_type=jnp.float32)


def normalize(values, gain_row):
    center = values - jnp.mean(values, axis=-1, keepdims=True)
    inverse = lax.rsqrt(jnp.mean(center * center, axis=-1, keepdims=True) + epsilon)
    standard = center * inverse
    return (standard * gain_row, standard, inverse)


def normalize_back(grad_out, standard, gain_row, inverse):
    scaled = grad_out * gain_row
    grad_in = inverse * (
        scaled
        - jnp.mean(scaled, axis=-1, keepdims=True)
        - standard * jnp.mean(scaled * standard, axis=-1, keepdims=True)
    )
    return (grad_in, jnp.sum(grad_out * standard, axis=(0, 1)))


def allowed_mask(query_docs, key_docs, query_place, key_place, causal):
    same_doc = query_docs[:, :, None] == key_docs[:, None, :]
    earlier = query_place[:, None] >= key_place[None, :]
    return (same_doc & (earlier | jnp.logical_not(causal)))[:, None]


def attend(queries, keys_local, values_local, query_docs, key_docs, causal, is_cross):
    rows_here, shard_len, model_width = queries.shape
    head_dim = model_width // HEADS
    score_scale = head_dim ** (-0.5)
    query_place = lax.axis_index("seq") * shard_len + jnp.arange(shard_len)
    query_heads = queries.reshape(rows_here, shard_len, HEADS, head_dim)

    def absorb(state_tuple, pieces):
        running_top, running_total, running_sum = state_tuple
        key_piece, value_piece, doc_piece = pieces
        piece_len = key_piece.shape[1]
        raw_scores = jnp.einsum(
            "rqhd,rkhd->rhqk",
            query_heads,
            key_piece.reshape(rows_here, piece_len, HEADS, head_dim),
            preferred_element_type=jnp.float32,
        )
        allowed = allowed_mask(query_docs, doc_piece, query_place, jnp.arange(piece_len), causal)
        scores = jnp.where(allowed, raw_scores * score_scale, negative_big)
        new_top = jnp.maximum(running_top, jnp.max(scores, axis=-1))
        weights = jnp.where(allowed, jnp.exp(scores - new_top[..., None]), 0.0)
        new_total = jnp.sum(weights, axis=-1)
        product = jnp.einsum(
            "rhqk,rkhd->rhqd",
            weights.astype(jnp.bfloat16),
            value_piece.reshape(rows_here, piece_len, HEADS, head_dim),
            preferred_element_type=jnp.float32,
        )
        return (new_top, new_total, product)

    init_state = (
        jnp.full((rows_here, HEADS, shard_len), negative_big, jnp.float32),
        jnp.zeros((rows_here, HEADS, shard_len), jnp.float32),
        jnp.zeros((rows_here, HEADS, shard_len, head_dim), jnp.float32),
    )
    if is_cross:
        final_top, final_total, final_sum = absorb(
            init_state,
            (
                lax.all_gather(keys_local, "seq", axis=1, tiled=True),
                lax.all_gather(values_local, "seq", axis=1, tiled=True),
                lax.all_gather(for_sending(key_docs), "seq", axis=1, tiled=True),
            ),
        )
    else:
        final_top, final_total, final_sum = absorb(
            init_state,
            (
                lax.all_gather(keys_local, "seq", axis=1, tiled=True),
                lax.all_gather(values_local, "seq", axis=1, tiled=True),
                lax.all_gather(key_docs, "seq", axis=1, tiled=True),
            ),
        )
    attended = (
        (final_sum / final_total[..., None])
        .transpose(0, 2, 1, 3)
        .reshape(rows_here, shard_len, model_width)
    )
    return (attended, final_top + jnp.log(final_total))


def attend_back(
    queries,
    keys_local,
    values_local,
    query_docs,
    key_docs,
    causal,
    log_total,
    grad_attended,
    is_cross,
):
    rows_here, shard_len, model_width = queries.shape
    head_dim = model_width // HEADS
    score_scale = head_dim ** (-0.5)
    query_place = lax.axis_index("seq") * shard_len + jnp.arange(shard_len)
    if is_cross:
        keys_full, values_full, docs_full = (
            lax.all_gather(keys_local, "seq", axis=1, tiled=True),
            lax.all_gather(values_local, "seq", axis=1, tiled=True),
            lax.all_gather(for_sending(key_docs), "seq", axis=1, tiled=True).astype(key_docs.dtype),
        )
    else:
        keys_full, values_full, docs_full = (
            lax.all_gather(keys_local, "seq", axis=1, tiled=True),
            lax.all_gather(values_local, "seq", axis=1, tiled=True),
            lax.all_gather(key_docs, "seq", axis=1, tiled=True),
        )
    full_len = keys_full.shape[1]
    query_heads = queries.reshape(rows_here, shard_len, HEADS, head_dim)
    key_heads = keys_full.reshape(rows_here, full_len, HEADS, head_dim)
    value_heads = values_full.reshape(rows_here, full_len, HEADS, head_dim)
    grad_heads = grad_attended.reshape(rows_here, shard_len, HEADS, head_dim)
    raw_scores = jnp.einsum(
        "rqhd,rkhd->rhqk", query_heads, key_heads, preferred_element_type=jnp.float32
    )
    allowed = allowed_mask(query_docs, docs_full, query_place, jnp.arange(full_len), causal)
    shifted = jnp.where(allowed, raw_scores * score_scale - log_total[..., None], negative_big)
    probs = jnp.where(allowed, jnp.exp(shifted), 0.0)
    grad_probs = jnp.einsum(
        "rqhd,rkhd->rhqk", grad_heads, value_heads, preferred_element_type=jnp.float32
    )
    delta = jnp.sum(probs * grad_probs, axis=-1)
    grad_scores = (probs * (grad_probs - delta[..., None]) * score_scale).astype(jnp.bfloat16)
    grad_queries = jnp.einsum(
        "rhqk,rkhd->rqhd", grad_scores, key_heads, preferred_element_type=jnp.float32
    ).reshape(rows_here, shard_len, model_width)
    probs_low = probs.astype(jnp.bfloat16)

    def key_terms(span):
        grad_keys = jnp.einsum(
            "rhqk,rqhd->krhd", grad_scores, query_heads, preferred_element_type=jnp.float32
        )
        grad_values = jnp.einsum(
            "rhqk,rqhd->krhd", probs_low, grad_heads, preferred_element_type=jnp.float32
        )
        return jnp.concatenate(
            [
                grad_keys.reshape(span, rows_here, model_width),
                grad_values.reshape(span, rows_here, model_width),
            ],
            axis=-1,
        )

    if is_cross:
        pair_terms = lax.psum_scatter(
            key_terms(shard_len * lax.axis_size("seq")).astype(jnp.bfloat16),
            "seq",
            scatter_dimension=0,
            tiled=True,
        ).astype(jnp.float32)
    else:
        pair_terms = lax.psum_scatter(
            key_terms(shard_len * lax.axis_size("seq")).astype(jnp.bfloat16),
            "seq",
            scatter_dimension=0,
            tiled=True,
        ).astype(jnp.float32)
    return (grad_queries, pair_terms.transpose(1, 0, 2))


def layer_forward(hidden_in, doc_own, memory, memory_docs, weights, is_decoder):
    (
        qkv_weight,
        out_weight,
        in_weight,
        down_weight,
        gains_pair,
        query_weight,
        pair_weight,
        cross_weight,
        cross_gains,
    ) = weights
    model_width = hidden_in.shape[-1]
    mixed = matmul(hidden_in, qkv_weight).astype(jnp.bfloat16)
    attended, self_lse = attend(
        mixed[..., :model_width],
        mixed[..., model_width : 2 * model_width],
        mixed[..., 2 * model_width :],
        doc_own,
        doc_own,
        is_decoder,
        False,
    )
    attended = attended.astype(jnp.bfloat16)
    first, first_unit, first_inv = normalize(
        hidden_in.astype(jnp.float32) + matmul(attended, out_weight), gains_pair[0]
    )
    first_low = first.astype(jnp.bfloat16)
    cross_queries = matmul(first_low, query_weight).astype(jnp.bfloat16)
    pair = matmul(memory, pair_weight).astype(jnp.bfloat16)
    cross_att, cross_lse = attend(
        cross_queries,
        pair[..., :model_width],
        pair[..., model_width:],
        doc_own,
        memory_docs,
        False,
        True,
    )
    cross_att = cross_att.astype(jnp.bfloat16)
    second_cross, second_unit, second_inv = normalize(
        first + matmul(cross_att, cross_weight), cross_gains
    )
    second = jnp.where(is_decoder, second_cross, first)
    second_low = second.astype(jnp.bfloat16)
    upward = matmul(second_low, in_weight)
    active = jax.nn.silu(upward).astype(jnp.bfloat16)
    result, third_unit, third_inv = normalize(second + matmul(active, down_weight), gains_pair[1])
    saved = {
        "mixed": mixed,
        "attended": attended,
        "self_lse": self_lse,
        "first_unit": first_unit,
        "first_inv": first_inv,
        "first_low": first_low,
        "cross_queries": cross_queries,
        "pair": pair,
        "cross_att": cross_att,
        "cross_lse": cross_lse,
        "second_unit": second_unit,
        "second_inv": second_inv,
        "second_low": second_low,
        "upward": upward,
        "active": active,
        "third_unit": third_unit,
        "third_inv": third_inv,
    }
    return (result, saved)


def layer_backward(
    grad_result, saved, hidden_in, doc_own, memory, memory_docs, weights, is_decoder
):
    (
        qkv_weight,
        out_weight,
        in_weight,
        down_weight,
        gains_pair,
        query_weight,
        pair_weight,
        cross_weight,
        cross_gains,
    ) = weights
    model_width = hidden_in.shape[-1]
    grad_third, grad_gain_late = normalize_back(
        grad_result, saved["third_unit"], gains_pair[1], saved["third_inv"]
    )
    down_grad = grad_third.astype(jnp.bfloat16)
    grad_down_w = contract(saved["active"], down_grad)
    grad_active = matmul_back(down_grad, down_weight).astype(jnp.bfloat16)
    sigmoid_up = jax.nn.sigmoid(saved["upward"])
    grad_upward = (
        grad_active.astype(jnp.float32)
        * (sigmoid_up + saved["upward"] * sigmoid_up * (1.0 - sigmoid_up))
    ).astype(jnp.bfloat16)
    grad_in_w = contract(saved["second_low"], grad_upward)
    grad_second = grad_third + matmul_back(grad_upward, in_weight)
    grad_cross_sum, grad_cross_gain = normalize_back(
        grad_second, saved["second_unit"], cross_gains, saved["second_inv"]
    )
    decoder_flag = is_decoder.astype(jnp.float32)
    grad_cross_sum = grad_cross_sum * decoder_flag
    grad_cross_gain = grad_cross_gain * decoder_flag
    cross_branch = grad_cross_sum.astype(jnp.bfloat16)
    grad_cross_w = contract(saved["cross_att"], cross_branch)
    grad_cross_att = matmul_back(cross_branch, cross_weight).astype(jnp.bfloat16)
    pair = saved["pair"]
    grad_cross_q, grad_pair = attend_back(
        saved["cross_queries"],
        pair[..., :model_width],
        pair[..., model_width:],
        doc_own,
        memory_docs,
        False,
        saved["cross_lse"],
        grad_cross_att,
        True,
    )
    grad_cross_q = grad_cross_q.astype(jnp.bfloat16)
    grad_pair = grad_pair.astype(jnp.bfloat16)
    grad_query_w = contract(saved["first_low"], grad_cross_q)
    grad_pair_w = contract(memory, grad_pair)
    grad_memory = matmul_back(grad_pair, pair_weight)
    grad_first = jnp.where(
        is_decoder, grad_cross_sum + matmul_back(grad_cross_q, query_weight), grad_second
    )
    grad_first_sum, grad_gain_early = normalize_back(
        grad_first, saved["first_unit"], gains_pair[0], saved["first_inv"]
    )
    self_branch = grad_first_sum.astype(jnp.bfloat16)
    grad_out_w = contract(saved["attended"], self_branch)
    grad_attended = matmul_back(self_branch, out_weight).astype(jnp.bfloat16)
    mixed = saved["mixed"]
    grad_queries, grad_pair_self = attend_back(
        mixed[..., :model_width],
        mixed[..., model_width : 2 * model_width],
        mixed[..., 2 * model_width :],
        doc_own,
        doc_own,
        is_decoder,
        saved["self_lse"],
        grad_attended,
        False,
    )
    grad_mixed = jnp.concatenate([grad_queries, grad_pair_self], axis=-1).astype(jnp.bfloat16)
    grad_qkv_w = contract(hidden_in, grad_mixed)
    grad_hidden = grad_first_sum + matmul_back(grad_mixed, qkv_weight)
    layer_grads = (
        grad_qkv_w,
        grad_out_w,
        grad_in_w,
        grad_down_w,
        jnp.stack([grad_gain_early, grad_gain_late]),
        grad_query_w,
        grad_pair_w,
        grad_cross_w,
        grad_cross_gain,
    )
    return (grad_hidden, grad_memory, layer_grads)


def any_rows(
    layer_input,
    segment_ids,
    attn_qkv,
    attn_out,
    ffn_in,
    ffn_out,
    norm_gain,
    cross_query,
    cross_pair,
    cross_out,
    cross_gain,
    out_cotangent,
):
    micro_count = layer_input.shape[1]
    section_index = lax.axis_index("section")
    is_decoder = section_index == 1
    weights = (
        attn_qkv[0],
        attn_out[0],
        ffn_in[0],
        ffn_out[0],
        norm_gain[0],
        cross_query,
        cross_pair,
        cross_out,
        cross_gain,
    )
    inputs_all = layer_input[0]
    docs_all = segment_ids[0]
    slot_ids = jnp.arange(micro_count)
    received = (jnp.zeros_like(inputs_all[0]), jnp.zeros_like(docs_all[0]))
    results = jnp.zeros_like(inputs_all)
    memories = []
    memory_doc_list = []
    for step_index in range(micro_count + 1):
        batch_index = step_index - section_index
        is_valid = (batch_index >= 0) & (batch_index < micro_count)
        chosen = jnp.clip(batch_index, 0, micro_count - 1)
        hidden_in = lax.dynamic_index_in_dim(inputs_all, chosen, 0, keepdims=False)
        doc_own = lax.dynamic_index_in_dim(docs_all, chosen, 0, keepdims=False)
        memory = received[0]
        memory_docs = jnp.where(is_valid & is_decoder, received[1], doc_own)
        memories.append(memory)
        memory_doc_list.append(memory_docs)
        result, saved = layer_forward(hidden_in, doc_own, memory, memory_docs, weights, is_decoder)
        low_result = result.astype(jnp.bfloat16)
        writing = (slot_ids == chosen) & is_valid
        results = jnp.where(writing[:, None, None, None], low_result[None], results)
        if step_index < micro_count:
            received = from_behind((low_result, doc_own), "section", 1)
    memory_stack = jnp.stack(memories)
    memory_doc_stack = jnp.stack(memory_doc_list)
    totals = tuple((jnp.zeros(weight.shape, jnp.float32) for weight in weights))
    input_grads = jnp.zeros(inputs_all.shape, jnp.float32)
    returned = jnp.zeros(inputs_all.shape[1:], jnp.float32)
    for step_index in range(micro_count + 1):
        batch_index = micro_count - step_index - section_index
        is_valid = (batch_index >= 0) & (batch_index < micro_count)
        chosen = jnp.clip(batch_index, 0, micro_count - 1)
        forward_step = jnp.clip(batch_index + section_index, 0, micro_count)
        hidden_in = lax.dynamic_index_in_dim(inputs_all, chosen, 0, keepdims=False)
        doc_own = lax.dynamic_index_in_dim(docs_all, chosen, 0, keepdims=False)
        memory = lax.dynamic_index_in_dim(memory_stack, forward_step, 0, keepdims=False)
        memory_docs = lax.dynamic_index_in_dim(memory_doc_stack, forward_step, 0, keepdims=False)
        discarded, saved = layer_forward(
            hidden_in, doc_own, memory, memory_docs, weights, is_decoder
        )
        cotangent = jnp.where(
            is_decoder,
            lax.dynamic_index_in_dim(out_cotangent, chosen, 0, keepdims=False).astype(jnp.float32),
            returned,
        )
        grad_hidden, grad_memory, layer_grads = layer_backward(
            cotangent, saved, hidden_in, doc_own, memory, memory_docs, weights, is_decoder
        )
        valid_flag = is_valid.astype(jnp.float32)
        totals = tuple(
            (running + valid_flag * fresh for running, fresh in zip(totals, layer_grads))
        )
        writing = (slot_ids == chosen) & is_valid
        input_grads = jnp.where(writing[:, None, None, None], grad_hidden[None], input_grads)
        if step_index < micro_count:
            returned = from_behind(grad_memory.astype(jnp.bfloat16), "section", -1).astype(
                grad_memory.dtype
            )
    group_sums = lax.psum(
        (
            totals[0],
            totals[1],
            totals[2],
            totals[3],
            totals[4],
            totals[5],
            totals[6],
            totals[7],
            totals[8],
        ),
        ("seq", "dp"),
    )
    section_sums = group_sums[:5]
    cross_sums = (
        from_root(group_sums[5].astype(jnp.bfloat16), "section", 1).astype(jnp.float32),
        from_root(group_sums[6].astype(jnp.bfloat16), "section", 1).astype(jnp.float32),
        from_root(group_sums[7].astype(jnp.bfloat16), "section", 1).astype(jnp.float32),
        from_root(group_sums[8].astype(jnp.bfloat16), "section", 1).astype(jnp.float32),
    )
    return (
        results[None],
        input_grads[None],
        section_sums[0][None],
        section_sums[1][None],
        section_sums[2][None],
        section_sums[3][None],
        section_sums[4][None],
        cross_sums[0],
        cross_sums[1],
        cross_sums[2],
        cross_sums[3],
    )


def split_rows(
    layer_input,
    segment_ids,
    attn_qkv,
    attn_out,
    ffn_in,
    ffn_out,
    norm_gain,
    cross_query,
    cross_pair,
    cross_out,
    cross_gain,
    out_cotangent,
):
    micros = layer_input.shape[1]
    length, width = layer_input.shape[3:]
    hidden = ffn_in.shape[-1]
    half_groups = lax.axis_size("dp") // 2
    decoder = lax.axis_index("section") == 1
    core = lax.rem(lax.axis_index("dp"), 2)

    places = [(x, z, c) for x in range(2) for z in range(half_groups) for c in range(2)]

    def place(x, z, c):
        return (x * half_groups + z) * 2 + c

    swap = [(place(c, z, x), place(x, z, c)) for x, z, c in places]
    swap_other = [(place(1 - c, z, x), place(x, z, c)) for x, z, c in places]
    cores = [(i, i ^ 1) for i in range(2 * half_groups)]

    def exchange(values):
        return lax.ppermute(values, "dp", cores)

    inputs = lax.ppermute(layer_input[0, :, 0], ("seq", "dp"), swap)
    docs_own = lax.ppermute(segment_ids[0, :, 0], ("seq", "dp"), swap)
    docs_other = lax.ppermute(segment_ids[0, :, 0], ("seq", "dp"), swap_other)
    cotangent = lax.ppermute(out_cotangent[:, 0], ("seq", "dp"), swap)
    docs_row = jnp.concatenate([docs_own, docs_other], axis=1)
    docs_source = lax.ppermute(docs_row, "section", [(0, 1)])

    flag = decoder.astype(jnp.int32)

    def meta(run):
        return jnp.stack([run, flag, core]).astype(jnp.int32)

    def documents(micro, keys):
        queries = docs_own[micro]
        return (
            dict(qd_s=queries, kd_s=keys[micro]),
            dict(
                qd=queries.astype(f32).reshape(length // TILE, 1, TILE),
                kd=keys[micro].astype(f32)[None],
            ),
        )

    gains = norm_gain[0]
    w_query, w_pair = attn_qkv[0, :, :width], attn_qkv[0, :, width:]
    q_tiles = length // TILE
    low = ((length, width), bf16)
    wide = ((length, width), f32)
    inner = ((length, hidden), bf16)
    lse = ((q_tiles, 8, 2 * TILE), f32)
    stat = ((length, LANES), f32)

    queries, pairs, pairs_other = [], [], []
    for micro in range(micros):
        queries.append(dot(inputs[micro], w_query).astype(bf16))
        pairs.append(dot(inputs[micro], w_pair).astype(bf16))
        pairs_other.append(exchange(pairs[micro]))

    forward, memories = [], []
    forward_flops = 2 * length * width * (width + 2 * hidden) + 16 * length * length * width
    for micro in range(micros):
        scalars, small = documents(micro, docs_row)
        forward.append(
            launch(
                self_forward_kernel,
                dict(meta=meta(1), **scalars),
                dict(**small, gains=gains),
                dict(
                    q_h=queries[micro],
                    kv_h=pairs[micro],
                    kv_other_h=pairs_other[micro],
                    x_h=inputs[micro],
                    w_out_h=attn_out[0],
                    w_in_h=ffn_in[0],
                    w_down_h=ffn_out[0],
                ),
                dict(
                    att_o=low,
                    lse_o=lse,
                    unit1_o=wide,
                    inv1_o=stat,
                    first_low_o=low,
                    memory_o=low,
                    ffn_low_o=low,
                    act_o=inner,
                    slope_o=inner,
                    unit2_o=wide,
                    inv2_o=stat,
                ),
                dict(
                    **attention_scratch(length, width),
                    **forward_scratch(length, width),
                    x=low,
                    w_out=((width, width), bf16),
                    w_in=((width, hidden), bf16),
                    w_down=((hidden, width), bf16),
                    unit1=wide,
                    inv1=stat,
                    first_low=low,
                    memory=low,
                    act=inner,
                    slope=inner,
                    unit2=wide,
                    inv2=stat,
                    sum=wide,
                ),
                24,
                forward_flops,
            )
        )
        memories.append(lax.ppermute(forward[micro].memory_o, "section", [(0, 1)]))

    cross, grads_pair, grads_memory = [], [], []
    for micro in range(micros):
        pair = dot(memories[micro], cross_pair).astype(bf16)
        scalars, small = documents(micro, docs_source)
        done = forward[micro]
        cross.append(
            launch(
                cross_kernel,
                dict(meta=meta(flag), **scalars),
                dict(**small, gains=gains, cross_gain=cross_gain[None]),
                dict(
                    pair_h=pair,
                    pair_other_h=exchange(pair),
                    first_low_h=done.first_low_o,
                    unit1_h=done.unit1_o,
                    w_query_h=cross_query,
                    w_cross_h=cross_out,
                    w_in_h=ffn_in[0],
                    w_down_h=ffn_out[0],
                    cot_h=cotangent[micro],
                ),
                dict(
                    att_o=low,
                    ffn_low_o=low,
                    act_o=inner,
                    decoded_o=low,
                    down_grad_o=low,
                    up_grad_o=inner,
                    gain_grads_o=((8, width), f32),
                    branch_o=low,
                    dkv_own_o=((length, 2 * width), f32),
                    dkv_other_o=((length, 2 * width), bf16),
                    dq_low_o=low,
                    grad_first_o=wide,
                ),
                dict(
                    **attention_scratch(length, width),
                    **forward_scratch(length, width),
                    **backward_scratch(length, width),
                    first_low=low,
                    unit1=wide,
                    w_query=((width, width), bf16),
                    w_cross=((width, width), bf16),
                    w_in=((width, hidden), bf16),
                    w_down=((hidden, width), bf16),
                    cot=low,
                    unit2=wide,
                    inv2=stat,
                    second_low=low,
                    act=inner,
                    slope=((length, hidden), f32),
                    sum=wide,
                    decoded=low,
                    keep=wide,
                    down_grad=low,
                    up_grad=inner,
                    gain_grads=((8, width), f32),
                    branch=low,
                ),
                32,
                3 * forward_flops,
                dict(act_o=done.act_o, ffn_low_o=done.ffn_low_o),
            )
        )
        own, other = cross[micro].dkv_own_o, cross[micro].dkv_other_o
        grads_pair.append((own + exchange(other).astype(f32)).astype(bf16))
        grad_memory = dot_nt(grads_pair[micro], cross_pair).astype(bf16)
        grads_memory.append(lax.ppermute(grad_memory, "section", [(1, 0)]))

    def backward(micro, run, grad_first, previous):
        scalars, small = documents(micro, docs_row)
        done = forward[micro]
        return launch(
            self_backward_kernel,
            dict(meta=meta(run), **scalars),
            dict(**small, gains=gains),
            dict(
                q_h=queries[micro],
                kv_h=pairs[micro],
                kv_other_h=pairs_other[micro],
                w_out_h=attn_out[0],
                w_in_h=ffn_in[0],
                w_down_h=ffn_out[0],
                att_h=done.att_o,
                lse_h=done.lse_o,
                unit1_h=done.unit1_o,
                inv1_h=done.inv1_o,
                unit2_h=done.unit2_o,
                inv2_h=done.inv2_o,
                slope_h=done.slope_o,
                grad_memory_h=grads_memory[micro],
                grad_first_h=grad_first,
            ),
            dict(
                gain_grads_o=((8, width), f32),
                grad_sum_o=wide,
                branch_o=low,
                dkv_own_o=((length, 2 * width), f32),
                dkv_other_o=((length, 2 * width), bf16),
                dq_low_o=low,
                down_grad_o=low,
                up_grad_o=inner,
            ),
            dict(
                **attention_scratch(length, width),
                **backward_scratch(length, width),
                w_out=((width, width), bf16),
                w_in=((width, hidden), bf16),
                w_down=((hidden, width), bf16),
                unit1=wide,
                inv1=stat,
                unit2=wide,
                inv2=stat,
                slope=inner,
                cot=low,
                keep=wide,
                sum=wide,
                down_grad=low,
                up_grad=inner,
                branch=low,
                grad_att=low,
                gain_grads=((8, width), f32),
            ),
            32,
            2 * forward_flops,
            previous,
        )

    def share(call):
        return dict(down_grad_o=call.down_grad_o, up_grad_o=call.up_grad_o)

    ends = [None] * micros
    for micro in range(micros - 1):
        ends[micro] = backward(
            micro,
            1 - flag,
            cross[micro].grad_first_o,
            share(cross[micro]),
        )
    last = micros - 1
    ends[last] = backward(
        last, 1, cross[last].grad_first_o, share(cross[last])
    )
    for micro in range(micros - 1):
        grad_first, _ = lax.optimization_barrier(
            (cross[micro].grad_first_o, cross[last].gain_grads_o)
        )
        ends[micro] = backward(micro, flag, grad_first, vars(ends[micro]))

    grad_inputs, grads_mixed = [], []
    for micro in range(micros):
        end = ends[micro]
        grad_keys = (end.dkv_own_o + exchange(end.dkv_other_o).astype(f32)).astype(bf16)
        grads_mixed.append(jnp.concatenate([end.dq_low_o, grad_keys], axis=1))
        grad_inputs.append(end.grad_sum_o + dot_nt(grads_mixed[micro], attn_qkv[0]))

    def contract(lefts, rights):
        terms = [
            dot_tn(left, right)
            for left, right in zip(lefts, rights)
        ]
        total = terms[0]
        for term in terms[1:]:
            total = total + term
        return total.astype(bf16)

    cross_local = (
        contract([call.first_low_o for call in forward], [call.dq_low_o for call in cross]),
        contract(memories, grads_pair),
        contract([call.att_o for call in cross], [call.branch_o for call in cross]),
    )
    everywhere = ("section", "seq", "dp")
    cross_sums = lax.psum(
        tuple(jnp.where(decoder, term, jnp.zeros_like(term)) for term in cross_local), everywhere
    )
    feed_sums = lax.psum(
        (
            contract([call.ffn_low_o for call in cross], [call.up_grad_o for call in ends]),
            contract([call.act_o for call in cross], [call.down_grad_o for call in ends]),
        ),
        ("seq", "dp"),
    )
    self_sums = lax.psum(
        (
            contract(inputs, grads_mixed),
            contract([call.att_o for call in forward], [call.branch_o for call in ends]),
        ),
        ("seq", "dp"),
    )
    early = sum(end.gain_grads_o[0] for end in ends)
    late = jnp.where(
        decoder,
        sum(call.gain_grads_o[0] for call in cross),
        sum(end.gain_grads_o[1] for end in ends),
    )
    third = jnp.where(decoder, sum(call.gain_grads_o[1] for call in cross), 0.0)
    mine = jnp.stack([early, late])
    rows = jnp.where(decoder, 1, 0) == jnp.arange(2)
    gain_parts = jnp.concatenate(
        [jnp.where(rows[:, None, None], mine[None], 0.0).reshape(4, width), third[None]]
    )
    gain_sums = lax.psum(gain_parts, everywhere)
    own_gains = jnp.where(decoder, gain_sums[2:4], gain_sums[0:2])

    results = jnp.stack(
        [
            jnp.where(decoder, call.decoded_o, done.memory_o)
            for call, done in zip(cross, forward)
        ]
    )
    results = lax.ppermute(results, ("seq", "dp"), swap)
    grad_input = lax.ppermute(jnp.stack(grad_inputs).astype(bf16), ("seq", "dp"), swap)
    return (
        results[None, :, None],
        grad_input.astype(f32)[None, :, None],
        self_sums[0].astype(f32)[None],
        self_sums[1].astype(f32)[None],
        feed_sums[0].astype(f32)[None],
        feed_sums[1].astype(f32)[None],
        own_gains[None],
        cross_sums[0].astype(f32),
        cross_sums[1].astype(f32),
        cross_sums[2].astype(f32),
        gain_sums[4],
    )


def shards(*arrays):
    layer_input = arrays[0]
    rows, length = layer_input.shape[2:4]
    simple = (
        lax.axis_size("section") == 2
        and lax.axis_size("seq") == 2
        and lax.axis_size("dp") % 2 == 0
        and rows == 1
        and length % TILE == 0
    )
    return split_rows(*arrays) if simple else any_rows(*arrays)


def solution(mesh):
    in_specs = (
        P("section", None, "dp", "seq", None),
        P("section", None, "dp", "seq"),
        P("section", None, None),
        P("section", None, None),
        P("section", None, None),
        P("section", None, None),
        P("section", None, None),
        P(),
        P(),
        P(),
        P(),
        P(None, "dp", "seq", None),
    )
    out_specs = (
        P("section", None, "dp", "seq", None),
        P("section", None, "dp", "seq", None),
        P("section", None, None),
        P("section", None, None),
        P("section", None, None),
        P("section", None, None),
        P("section", None, None),
        P(),
        P(),
        P(),
        P(),
    )
    return jax.shard_map(shards, mesh=mesh, in_specs=in_specs, out_specs=out_specs, check_vma=False)
```

```python
import types

import jax
import jax.numpy as jnp
from jax import lax
from jax.experimental import pallas as pl
from jax.experimental.pallas import tpu as pltpu
from jax.sharding import PartitionSpec as P

HEADS = 8
TILE = 256
LANES = 128
CHUNK = 512

f32 = jnp.float32
bf16 = jnp.bfloat16
negative_big = -1e30
epsilon = 1e-05


def dot(left, right):
    return lax.dot_general(left, right, (((1,), (0,)), ((), ())), preferred_element_type=f32)


def dot_nt(left, right):
    return lax.dot_general(left, right, (((1,), (1,)), ((), ())), preferred_element_type=f32)


def dot_tn(left, right):
    return lax.dot_general(left, right, (((0,), (0,)), ((), ())), preferred_element_type=f32)


def standardize(values):
    center = values - jnp.mean(values, axis=-1, keepdims=True)
    inverse = lax.rsqrt(jnp.mean(center * center, axis=-1, keepdims=True) + epsilon)
    return center * inverse, inverse


def standardize_back(grad_out, standard, gain_row, inverse):
    scaled = grad_out * gain_row
    grad_in = inverse * (
        scaled
        - jnp.mean(scaled, axis=-1, keepdims=True)
        - standard * jnp.mean(scaled * standard, axis=-1, keepdims=True)
    )
    return grad_in, jnp.sum(grad_out * standard, axis=0, keepdims=True)


class Copies:
    def __init__(self, sems):
        self.sems = sems
        self.used = 0

    def start(self, source, target):
        copy = pltpu.make_async_copy(source, target, self.sems.at[self.used])
        self.used += 1
        copy.start()
        return copy


def wait_all(copies):
    for copy in copies:
        copy.wait()


def spread_pairs(target, source, factor):
    pairs, tiles = target.shape[:2]
    half = lax.broadcasted_iota(jnp.int32, (TILE, LANES), 1) < LANES // 2
    first = jnp.where(half, factor, 0.0).astype(bf16)
    second = jnp.where(half, 0.0, factor).astype(bf16)
    for tile in range(tiles):
        for pair in range(pairs):
            block = source[tile * TILE : (tile + 1) * TILE, pair * LANES : (pair + 1) * LANES]
            target[pair, tile, :TILE, :] = block * first
            target[pair, tile, TILE:, :] = block * second


def turn_tiles(target, source, column):
    tiles, width, _ = target.shape
    for tile in range(tiles):
        block = source[tile * TILE : (tile + 1) * TILE, column : column + width]
        target[tile] = jnp.transpose(block.astype(f32)).astype(bf16)


def turn_documents(target, key_docs):
    for start in range(0, target.shape[0], LANES):
        row = key_docs[:, start : start + LANES]
        target[start : start + LANES, :] = jnp.transpose(jnp.broadcast_to(row, (LANES, LANES)))


def tile_place(r, core, causal, q_tile, k_tile):
    q_tiles = r.qd.shape[0]
    length = q_tiles * TILE
    owner = jnp.where(k_tile < q_tiles, core, 1 - core)
    k_start = owner * length + lax.rem(k_tile, q_tiles) * TILE
    ahead = core * length + q_tile * TILE - k_start
    ahead = jnp.where(causal == 1, ahead, 2 * length * TILE)
    q_low, q_high = r.qd_s[q_tile * TILE], r.qd_s[q_tile * TILE + TILE - 1]
    k_low, k_high = r.kd_s[k_tile * TILE], r.kd_s[k_tile * TILE + TILE - 1]
    active = (q_low <= k_high) & (k_low <= q_high) & (ahead > -TILE)
    return active, ahead


def fill_bias(r, q_tile, k_tile, ahead):
    keys = r.kdc[pl.ds(pl.multiple_of(k_tile * TILE, TILE), TILE), :]
    shift = lax.broadcasted_iota(jnp.int32, (TILE, LANES), 0) - lax.broadcasted_iota(
        jnp.int32, (TILE, LANES), 1
    )
    queries = r.qd[q_tile]
    for start in range(0, TILE, LANES):
        same = keys == queries[:, start : start + LANES]
        allowed = same & (shift - start <= ahead)
        r.bias[:, start : start + LANES] = jnp.where(allowed, 0.0, negative_big)


def attention_forward(r, core, causal):
    pairs, q_tiles = r.qm.shape[:2]
    k_tiles = r.vt.shape[0]

    def one_query_tile(q_tile, carry):
        r.top[...] = jnp.full(r.top.shape, negative_big, f32)
        r.total[...] = jnp.zeros(r.total.shape, f32)
        r.turned[...] = jnp.zeros(r.turned.shape, f32)

        def one_key_tile(k_tile, inner):
            active, ahead = tile_place(r, core, causal, q_tile, k_tile)

            @pl.when(active)
            def _():
                fill_bias(r, q_tile, k_tile, ahead)
                rows = pl.ds(pl.multiple_of(k_tile * TILE, TILE), TILE)

                def raw(pair):
                    keys = r.kv[rows, pair * LANES : (pair + 1) * LANES]
                    return dot_nt(keys, r.qm[pair, q_tile])

                raw_next = raw(0)
                for pair in range(pairs):
                    bias = r.bias[...]
                    scores = raw_next + jnp.concatenate([bias, bias], axis=1)
                    if pair + 1 < pairs:
                        raw_next = raw(pair + 1)
                    old_top = r.top[pair : pair + 1, :]
                    new_top = jnp.maximum(old_top, jnp.max(scores, axis=0, keepdims=True))
                    weights = jnp.exp(scores - new_top)
                    shrink = jnp.exp(old_top - new_top)
                    r.top[pair : pair + 1, :] = new_top
                    r.total[pair : pair + 1, :] = r.total[
                        pair : pair + 1, :
                    ] * shrink + jnp.sum(weights, axis=0, keepdims=True)
                    low = weights.astype(bf16)
                    for side in range(2):
                        span = slice(side * TILE, (side + 1) * TILE)
                        head = slice((2 * pair + side) * 64, (2 * pair + side + 1) * 64)
                        r.turned[head, :] = r.turned[head, :] * shrink[:, span] + dot(
                            r.vt[k_tile, head, :], low[:, span]
                        )

            return inner

        lax.fori_loop(0, k_tiles, one_key_tile, 0)
        for pair in range(pairs):
            total = r.total[pair : pair + 1, :]
            r.lse[q_tile, pair : pair + 1, :] = r.top[pair : pair + 1, :] + jnp.log(total)
            share = 1.0 / total
            for side in range(2):
                span = slice(side * TILE, (side + 1) * TILE)
                head = slice((2 * pair + side) * 64, (2 * pair + side + 1) * 64)
                r.turned[head, :] = r.turned[head, :] * share[:, span]
        rows = pl.ds(pl.multiple_of(q_tile * TILE, TILE), TILE)
        r.att[rows, :] = jnp.transpose(r.turned[...]).astype(bf16)
        return carry

    lax.fori_loop(0, q_tiles, one_query_tile, 0)


def row_products(r, grad_att):
    pairs, q_tiles = r.qm.shape[:2]
    for tile in range(q_tiles):
        rows = slice(tile * TILE, (tile + 1) * TILE)
        product = jnp.transpose(grad_att[rows, :].astype(f32) * r.att[rows, :].astype(f32))
        for pair in range(pairs):
            for side in range(2):
                head = (2 * pair + side) * 64
                r.delta[tile, pair : pair + 1, side * TILE : (side + 1) * TILE] = jnp.sum(
                    product[head : head + 64, :], axis=0, keepdims=True
                )


def attention_backward(r, core, causal):
    pairs, q_tiles = r.qm.shape[:2]
    k_tiles = r.kt.shape[0]
    width = pairs * LANES
    r.dkv[...] = jnp.zeros(r.dkv.shape, f32)

    def one_query_tile(q_tile, carry):
        r.turned[...] = jnp.zeros(r.turned.shape, f32)

        def one_key_tile(k_tile, inner):
            active, ahead = tile_place(r, core, causal, q_tile, k_tile)

            @pl.when(active)
            def _():
                fill_bias(r, q_tile, k_tile, ahead)
                rows = pl.ds(pl.multiple_of(k_tile * TILE, TILE), TILE)

                def raw(pair):
                    lanes = slice(pair * LANES, (pair + 1) * LANES)
                    lanes_v = slice(width + pair * LANES, width + (pair + 1) * LANES)
                    return (
                        dot_nt(r.kv[rows, lanes], r.qm[pair, q_tile]),
                        dot_nt(r.kv[rows, lanes_v], r.gm[pair, q_tile]),
                    )

                raw_next = raw(0)
                for pair in range(pairs):
                    bias = r.bias[...]
                    scores, grad_probs = raw_next
                    scores = scores + jnp.concatenate([bias, bias], axis=1)
                    if pair + 1 < pairs:
                        raw_next = raw(pair + 1)
                    probs = jnp.exp(scores - r.lse[q_tile, pair : pair + 1, :])
                    grad_scores = probs * (grad_probs - r.delta[q_tile, pair : pair + 1, :])
                    probs_low = probs.astype(bf16)
                    grad_low = grad_scores.astype(bf16)
                    lanes = slice(pair * LANES, (pair + 1) * LANES)
                    lanes_v = slice(width + pair * LANES, width + (pair + 1) * LANES)
                    r.dkv[rows, lanes] += dot(grad_low, r.qm[pair, q_tile])
                    r.dkv[rows, lanes_v] += dot(probs_low, r.gm[pair, q_tile])
                    for side in range(2):
                        span = slice(side * TILE, (side + 1) * TILE)
                        head = slice((2 * pair + side) * 64, (2 * pair + side + 1) * 64)
                        r.turned[head, :] += dot(r.kt[k_tile, head, :], grad_low[:, span])

            return inner

        lax.fori_loop(0, k_tiles, one_key_tile, 0)
        rows = pl.ds(pl.multiple_of(q_tile * TILE, TILE), TILE)
        r.dq[rows, :] = jnp.transpose(r.turned[...]) * (64**-0.5)
        return carry

    lax.fori_loop(0, q_tiles, one_query_tile, 0)


def feed_forward(r, low):
    r.sum[...] = jnp.zeros(r.sum.shape, f32)

    def one_chunk(chunk, carry):
        span = pl.ds(pl.multiple_of(chunk * CHUNK, CHUNK), CHUNK)
        upward = dot(low[...], r.w_in[:, span])
        gate = jax.nn.sigmoid(upward)
        active = (upward * gate).astype(bf16)
        r.act[:, span] = active
        r.slope[:, span] = (gate + upward * gate * (1.0 - gate)).astype(r.slope.dtype)
        r.sum[...] += dot(active, r.w_down[span, :])
        return carry

    lax.fori_loop(0, r.w_in.shape[1] // CHUNK, one_chunk, 0)


def feed_backward(r):
    r.sum[...] = jnp.zeros(r.sum.shape, f32)

    def one_chunk(chunk, carry):
        span = pl.ds(pl.multiple_of(chunk * CHUNK, CHUNK), CHUNK)
        grad_active = dot_nt(r.down_grad[...], r.w_down[span, :]).astype(bf16)
        grad_up = (grad_active.astype(f32) * r.slope[:, span].astype(f32)).astype(bf16)
        r.up_grad[:, span] = grad_up
        r.sum[...] += dot_nt(grad_up, r.w_in[:, span])
        return carry

    lax.fori_loop(0, r.w_in.shape[1] // CHUNK, one_chunk, 0)


def self_forward_kernel(r, micro):
    length, width = r.q_h.shape
    core = r.meta[2]
    decoder = r.meta[1]
    move = Copies(r.sems)
    moves = [
        move.start(r.q_h, r.q),
        move.start(r.kv_h, r.kv.at[pl.ds(0, length)]),
        move.start(r.kv_other_h, r.kv.at[pl.ds(length, length)]),
        move.start(r.x_h.at[micro], r.x),
        move.start(r.w_out_h, r.w_out),
    ]
    turn_documents(r.kdc, r.kd)
    wait_all(moves[:3])
    spread_pairs(r.qm, r.q, 64**-0.5)
    turn_tiles(r.vt, r.kv, width)
    attention_forward(r, core, decoder)
    wait_all(moves[3:])
    outs = [move.start(r.att, r.att_o), move.start(r.lse, r.lse_o)]
    unit, inverse = standardize(r.x[...].astype(f32) + dot(r.att[...], r.w_out[...]))
    r.unit1[...] = unit
    r.inv1[...] = jnp.broadcast_to(inverse, r.inv1.shape)
    first = unit * r.gains[0:1, :]
    r.first_low[...] = first.astype(bf16)
    outs += [
        move.start(r.unit1, r.unit1_o),
        move.start(r.inv1, r.inv1_o),
        move.start(r.first_low, r.first_low_o),
    ]

    @pl.when(decoder == 0)
    def _():
        weights = [move.start(r.w_in_h, r.w_in), move.start(r.w_down_h, r.w_down)]
        wait_all(weights)
        feed_forward(r, r.first_low)
        late = [
            move.start(r.first_low, r.ffn_low_o),
            move.start(r.act, r.act_o),
            move.start(r.slope, r.slope_o),
        ]
        unit2, inverse2 = standardize(r.unit1[...] * r.gains[0:1, :] + r.sum[...])
        r.unit2[...] = unit2
        r.inv2[...] = jnp.broadcast_to(inverse2, r.inv2.shape)
        r.memory[...] = (unit2 * r.gains[1:2, :]).astype(bf16)
        late += [
            move.start(r.memory, r.memory_o),
            move.start(r.unit2, r.unit2_o),
            move.start(r.inv2, r.inv2_o),
        ]
        wait_all(late)

    wait_all(outs)


def cross_kernel(r, micro):
    @pl.when(r.meta[0] == 1)
    def _():
        cross_body(r, micro)


def cross_body(r, micro):
    length, width = r.unit1_h.shape
    core = r.meta[2]
    move = Copies(r.sems)
    moves = [
        move.start(r.pair_h, r.kv.at[pl.ds(0, length)]),
        move.start(r.pair_other_h, r.kv.at[pl.ds(length, length)]),
        move.start(r.first_low_h, r.first_low),
        move.start(r.w_query_h, r.w_query),
    ]
    later = [
        move.start(r.unit1_h, r.unit1),
        move.start(r.w_cross_h, r.w_cross),
        move.start(r.w_in_h, r.w_in),
        move.start(r.w_down_h, r.w_down),
        move.start(r.cot_h.at[micro], r.cot),
    ]
    turn_documents(r.kdc, r.kd)
    wait_all(moves)
    r.q[...] = dot(r.first_low[...], r.w_query[...]).astype(bf16)
    spread_pairs(r.qm, r.q, 64**-0.5)
    turn_tiles(r.vt, r.kv, width)
    turn_tiles(r.kt, r.kv, 0)
    attention_forward(r, core, 0)
    outs = [move.start(r.att, r.att_o)]
    wait_all(later)
    first = r.unit1[...] * r.gains[0:1, :]
    unit, inverse = standardize(first + dot(r.att[...], r.w_cross[...]))
    r.unit2[...] = unit
    r.inv2[...] = jnp.broadcast_to(inverse, r.inv2.shape)
    r.second_low[...] = (unit * r.cross_gain[...]).astype(bf16)
    outs += [move.start(r.second_low, r.ffn_low_o)]
    feed_forward(r, r.second_low)
    outs += [move.start(r.act, r.act_o)]
    unit3, inverse3 = standardize(r.unit2[...] * r.cross_gain[...] + r.sum[...])
    r.decoded[...] = (unit3 * r.gains[1:2, :]).astype(bf16)
    outs += [move.start(r.decoded, r.decoded_o)]
    grad_third, gain_late = standardize_back(
        r.cot[...].astype(f32), unit3, r.gains[1:2, :], inverse3
    )
    r.keep[...] = grad_third
    r.down_grad[...] = grad_third.astype(bf16)
    outs += [move.start(r.down_grad, r.down_grad_o)]
    feed_backward(r)
    outs += [move.start(r.up_grad, r.up_grad_o)]
    grad_sum, gain_cross = standardize_back(
        r.keep[...] + r.sum[...], r.unit2[...], r.cross_gain[...], r.inv2[:, 0:1]
    )
    r.gain_grads[...] = jnp.zeros(r.gain_grads.shape, f32)
    r.gain_grads[0:1, :] = gain_late
    r.gain_grads[1:2, :] = gain_cross
    r.keep[...] = grad_sum
    r.branch[...] = grad_sum.astype(bf16)
    outs += [move.start(r.gain_grads, r.gain_grads_o), move.start(r.branch, r.branch_o)]
    r.q[...] = dot_nt(r.branch[...], r.w_cross[...]).astype(bf16)
    spread_pairs(r.gm, r.q, 1.0)
    row_products(r, r.q)
    attention_backward(r, core, 0)
    r.dkv_other[...] = r.dkv[length:, :].astype(bf16)
    outs += [move.start(r.dkv.at[pl.ds(0, length)], r.dkv_own_o), move.start(r.dkv_other, r.dkv_other_o)]
    r.dq_low[...] = r.dq[...].astype(bf16)
    r.keep[...] += dot_nt(r.dq_low[...], r.w_query[...])
    outs += [move.start(r.dq_low, r.dq_low_o), move.start(r.keep, r.grad_first_o)]
    wait_all(outs)


def feed_backward_kernel(r, micro):
    @pl.when(r.meta[0] == 1)
    def _():
        feed_backward_body(r)


def feed_backward_body(r):
    move = Copies(r.sems)
    early = [
        move.start(r.grad_memory_h, r.cot),
        move.start(r.unit2_h, r.unit2),
        move.start(r.inv2_h, r.inv2),
    ]
    later = [
        move.start(r.w_down_h, r.w_down),
        move.start(r.slope_h, r.slope),
        move.start(r.w_in_h, r.w_in),
    ]
    wait_all(early)
    grad_third, gain_late = standardize_back(
        r.cot[...].astype(f32), r.unit2[...], r.gains[1:2, :], r.inv2[:, 0:1]
    )
    r.gain_grads[...] = jnp.broadcast_to(gain_late, r.gain_grads.shape)
    r.keep[...] = grad_third
    r.down_grad[...] = grad_third.astype(bf16)
    outs = [move.start(r.down_grad, r.down_grad_o), move.start(r.gain_grads, r.gain_late_o)]
    wait_all(later)
    feed_backward(r)
    outs += [move.start(r.up_grad, r.up_grad_o)]
    r.keep[...] += r.sum[...]
    outs += [move.start(r.keep, r.grad_first_o)]
    wait_all(outs)


def self_backward_kernel(r, micro):
    @pl.when(r.meta[0] == 1)
    def _():
        self_backward_body(r)


def self_backward_body(r):
    length, width = r.unit1_h.shape
    core = r.meta[2]
    decoder = r.meta[1]
    move = Copies(r.sems)
    early = [
        move.start(r.grad_first_h, r.keep),
        move.start(r.unit1_h, r.unit1),
        move.start(r.inv1_h, r.inv1),
    ]
    later = [
        move.start(r.w_out_h, r.w_out),
        move.start(r.q_h, r.q),
        move.start(r.kv_h, r.kv.at[pl.ds(0, length)]),
        move.start(r.kv_other_h, r.kv.at[pl.ds(length, length)]),
        move.start(r.att_h, r.att),
        move.start(r.lse_h, r.lse),
    ]
    turn_documents(r.kdc, r.kd)
    wait_all(early)
    grad_sum, gain_early = standardize_back(
        r.keep[...], r.unit1[...], r.gains[0:1, :], r.inv1[:, 0:1]
    )
    r.gain_grads[...] = jnp.broadcast_to(gain_early, r.gain_grads.shape)
    r.keep[...] = grad_sum
    r.branch[...] = grad_sum.astype(bf16)
    outs = [
        move.start(r.gain_grads, r.gain_early_o),
        move.start(r.keep, r.grad_sum_o),
        move.start(r.branch, r.branch_o),
    ]
    wait_all(later)
    spread_pairs(r.qm, r.q, 64**-0.5)
    turn_tiles(r.kt, r.kv, 0)
    r.grad_att[...] = dot_nt(r.branch[...], r.w_out[...]).astype(bf16)
    spread_pairs(r.gm, r.grad_att, 1.0)
    row_products(r, r.grad_att)
    attention_backward(r, core, decoder)
    r.dkv_other[...] = r.dkv[length:, :].astype(bf16)
    outs += [
        move.start(r.dkv_other, r.dkv_other_o),
        move.start(r.dkv.at[pl.ds(0, length)], r.dkv_own_o),
    ]
    r.dq_low[...] = r.dq[...].astype(bf16)
    outs += [move.start(r.dq_low, r.dq_low_o)]
    wait_all(outs)


def project_kernel(r, micro):
    width = r.x.shape[1]
    move = Copies(r.sems)
    loads = [move.start(r.x_h.at[micro], r.x), move.start(r.w_h, r.w)]
    wait_all(loads)
    r.pair[...] = dot(r.x[...], r.w[:, width:]).astype(bf16)
    outs = [move.start(r.pair, r.pair_o)]
    r.q[...] = dot(r.x[...], r.w[:, :width]).astype(bf16)
    outs += [move.start(r.q, r.q_o)]
    wait_all(outs)


def pair_kernel(r, micro):
    @pl.when(r.meta[0] == 1)
    def _():
        move = Copies(r.sems)
        wait_all([move.start(r.memory_h, r.x), move.start(r.w_h, r.w)])
        r.pair[...] = dot(r.x[...], r.w[...]).astype(bf16)
        wait_all([move.start(r.pair, r.pair_o)])


def memory_backward_kernel(r, micro):
    @pl.when(r.meta[0] == 1)
    def _():
        move = Copies(r.sems)
        loads = [
            move.start(r.own_h, r.own),
            move.start(r.got_h, r.got),
            move.start(r.w_h, r.w),
        ]
        wait_all(loads)
        r.pair[...] = (r.own[...] + r.got[...].astype(f32)).astype(bf16)
        outs = [move.start(r.pair, r.grad_pair_o)]
        r.x[...] = dot_nt(r.pair[...], r.w[...]).astype(bf16)
        outs += [move.start(r.x, r.grad_memory_o)]
        wait_all(outs)


def input_backward_kernel(r, micro):
    width = r.x.shape[1]
    move = Copies(r.sems)
    loads = [
        move.start(r.own_h, r.own),
        move.start(r.got_h, r.got),
        move.start(r.w_h, r.w),
        move.start(r.dq_h, r.dq),
        move.start(r.grad_sum_h, r.keep),
    ]
    wait_all(loads)
    r.pair[...] = (r.own[...] + r.got[...].astype(f32)).astype(bf16)
    outs = [move.start(r.pair, r.grad_pair_o)]
    total = r.keep[...] + dot_nt(r.dq[...], r.w[:, :width])
    r.x[...] = (total + dot_nt(r.pair[...], r.w[:, width:])).astype(bf16)
    outs += [move.start(r.x, r.grad_input_o)]
    wait_all(outs)


def contract_kernel(r, plan):
    for half, (operands, blocks) in enumerate(plan(r)):

        @pl.when((r.meta[0] == 1) & (r.meta[1] == half))
        def _(operands=operands, blocks=blocks):
            move = Copies(r.sems)
            loads = []
            for target, sources in operands:
                for place, source in enumerate(sources):
                    rows = pl.ds(place * source.shape[0], source.shape[0])
                    loads.append(move.start(source, target.at[rows]))
            wait_all(loads)
            outs = []
            before = None
            for place, (left, left_at, right, right_at) in enumerate(blocks):
                if before != (id(left), left_at):
                    block = left[:, left_at * CHUNK : (left_at + 1) * CHUNK]
                    r.turn[...] = jnp.transpose(block.astype(f32)).astype(bf16)
                    before = (id(left), left_at)
                block = right[:, right_at * CHUNK : (right_at + 1) * CHUNK]
                r.blocks[place] = dot(r.turn[...], block).astype(bf16)
                outs.append(move.start(r.blocks.at[place], r.blocks_o.at[place]))
            wait_all(outs)


def spread_kernel(r, targets):
    z = r.meta[2]
    group, rows = r.own_h.shape[:2]
    for core in range(2):
        for x in range(2):

            @pl.when((r.meta[0] == core) & (r.meta[1] == x))
            def _(core=core, x=x):
                move = Copies(r.sems)
                parts = [
                    (r.own_h, core, x),
                    (r.own_x_h, core, 1 - x),
                    (r.other_h, 1 - core, x),
                    (r.other_x_h, 1 - core, 1 - x),
                ]
                loads = [
                    move.start(source, r.pieces.at[place])
                    for place, (source, _, _) in enumerate(parts)
                ]
                outs = []
                for place, (_, half, side) in enumerate(parts):
                    loads[place].wait()
                    for step in range(group):
                        slot = place * group + step
                        r.wide[slot] = r.pieces[place, step].astype(f32)
                        row = pl.multiple_of(lax.rem(z + (group - step), group) * rows, rows)
                        target = targets(r, half, side, row, rows)
                        outs.append(move.start(r.wide.at[slot], target))
                wait_all(outs)


def launch(kernel, plan, scalars, small, large, outs, scratch, copies, flops, previous=None, after=()):
    names = list(scalars) + list(small) + list(large)
    arrays = list(scalars.values()) + list(small.values()) + list(large.values())
    specs = (
        [pl.BlockSpec(memory_space=pltpu.SMEM)] * len(scalars)
        + [pl.BlockSpec(memory_space=pltpu.VMEM)] * len(small)
        + [pl.BlockSpec(memory_space=pl.ANY)] * len(large)
    )
    aliases = dict()
    for position, name in enumerate(outs):
        if previous and name in previous:
            aliases[len(arrays)] = position
            names.append("previous_" + name)
            arrays.append(previous[name])
            specs.append(pl.BlockSpec(memory_space=pl.ANY))
    for array in after:
        names.append("")
        arrays.append(array)
        specs.append(pl.BlockSpec(memory_space=pl.ANY))
    names += list(outs) + list(scratch) + ["sems"]

    def body(*refs):
        kernel(types.SimpleNamespace(**dict(zip(names, refs))), plan)

    moved = sum(a.size * a.dtype.itemsize for a in large.values())
    results = pl.pallas_call(
        body,
        out_shape=[jax.ShapeDtypeStruct(*shape) for shape in outs.values()],
        in_specs=specs,
        out_specs=[pl.BlockSpec(memory_space=pl.ANY)] * len(outs),
        scratch_shapes=[pltpu.VMEM(*shape) for shape in scratch.values()]
        + [pltpu.SemaphoreType.DMA((copies,))],
        input_output_aliases=aliases,
        compiler_params=pltpu.CompilerParams(vmem_limit_bytes=56 * 1024 * 1024),
        cost_estimate=pl.CostEstimate(flops=flops, bytes_accessed=moved, transcendentals=0),
    )(*arrays)
    return types.SimpleNamespace(**dict(zip(outs, results)))


def attention_scratch(length, width):
    pairs, q_tiles, k_tiles = width // LANES, length // TILE, 2 * length // TILE
    return dict(
        q=((length, width), bf16),
        kv=((2 * length, 2 * width), bf16),
        qm=((pairs, q_tiles, 2 * TILE, LANES), bf16),
        kdc=((2 * length, LANES), f32),
        bias=((TILE, TILE), f32),
        lse=((q_tiles, 8, 2 * TILE), f32),
        att=((length, width), bf16),
        turned=((width, TILE), f32),
    )


def forward_scratch(length, width):
    k_tiles = 2 * length // TILE
    return dict(
        vt=((k_tiles, width, TILE), bf16),
        top=((8, 2 * TILE), f32),
        total=((8, 2 * TILE), f32),
    )


def backward_scratch(length, width):
    pairs, q_tiles, k_tiles = width // LANES, length // TILE, 2 * length // TILE
    return dict(
        kt=((k_tiles, width, TILE), bf16),
        gm=((pairs, q_tiles, 2 * TILE, LANES), bf16),
        delta=((q_tiles, 8, 2 * TILE), f32),
        dkv=((2 * length, 2 * width), f32),
        dq=((length, width), f32),
        dkv_other=((length, 2 * width), bf16),
        dq_low=((length, width), bf16),
    )


def for_sending(shard):

    def short(part):
        return part.astype(jnp.bfloat16) if part.dtype == jnp.float32 else part

    return jax.tree.map(short, shard)


def from_behind(block, axis, distance):
    devices = range(lax.axis_size(axis))
    route = [(i - distance, i) for i in devices if i - distance in devices]
    return lax.ppermute(block, axis, route)


def from_root(shard, axis, root):
    mine = lax.axis_index(axis) == root
    return lax.psum(jnp.where(mine, shard, jnp.zeros_like(shard)), axis)


def matmul(left_side, right_side):
    return jnp.einsum("rsd,de->rse", left_side, right_side, preferred_element_type=jnp.float32)


def matmul_back(left_side, right_side):
    return jnp.einsum("rse,de->rsd", left_side, right_side, preferred_element_type=jnp.float32)


def contract(left_side, right_side):
    return jnp.einsum("rsd,rse->de", left_side, right_side, preferred_element_type=jnp.float32)


def normalize(values, gain_row):
    center = values - jnp.mean(values, axis=-1, keepdims=True)
    inverse = lax.rsqrt(jnp.mean(center * center, axis=-1, keepdims=True) + epsilon)
    standard = center * inverse
    return (standard * gain_row, standard, inverse)


def normalize_back(grad_out, standard, gain_row, inverse):
    scaled = grad_out * gain_row
    grad_in = inverse * (
        scaled
        - jnp.mean(scaled, axis=-1, keepdims=True)
        - standard * jnp.mean(scaled * standard, axis=-1, keepdims=True)
    )
    return (grad_in, jnp.sum(grad_out * standard, axis=(0, 1)))


def allowed_mask(query_docs, key_docs, query_place, key_place, causal):
    same_doc = query_docs[:, :, None] == key_docs[:, None, :]
    earlier = query_place[:, None] >= key_place[None, :]
    return (same_doc & (earlier | jnp.logical_not(causal)))[:, None]


def attend(queries, keys_local, values_local, query_docs, key_docs, causal, is_cross):
    rows_here, shard_len, model_width = queries.shape
    head_dim = model_width // HEADS
    score_scale = head_dim ** (-0.5)
    query_place = lax.axis_index("seq") * shard_len + jnp.arange(shard_len)
    query_heads = queries.reshape(rows_here, shard_len, HEADS, head_dim)

    def absorb(state_tuple, pieces):
        running_top, running_total, running_sum = state_tuple
        key_piece, value_piece, doc_piece = pieces
        piece_len = key_piece.shape[1]
        raw_scores = jnp.einsum(
            "rqhd,rkhd->rhqk",
            query_heads,
            key_piece.reshape(rows_here, piece_len, HEADS, head_dim),
            preferred_element_type=jnp.float32,
        )
        allowed = allowed_mask(query_docs, doc_piece, query_place, jnp.arange(piece_len), causal)
        scores = jnp.where(allowed, raw_scores * score_scale, negative_big)
        new_top = jnp.maximum(running_top, jnp.max(scores, axis=-1))
        weights = jnp.where(allowed, jnp.exp(scores - new_top[..., None]), 0.0)
        new_total = jnp.sum(weights, axis=-1)
        product = jnp.einsum(
            "rhqk,rkhd->rhqd",
            weights.astype(jnp.bfloat16),
            value_piece.reshape(rows_here, piece_len, HEADS, head_dim),
            preferred_element_type=jnp.float32,
        )
        return (new_top, new_total, product)

    init_state = (
        jnp.full((rows_here, HEADS, shard_len), negative_big, jnp.float32),
        jnp.zeros((rows_here, HEADS, shard_len), jnp.float32),
        jnp.zeros((rows_here, HEADS, shard_len, head_dim), jnp.float32),
    )
    if is_cross:
        final_top, final_total, final_sum = absorb(
            init_state,
            (
                lax.all_gather(keys_local, "seq", axis=1, tiled=True),
                lax.all_gather(values_local, "seq", axis=1, tiled=True),
                lax.all_gather(for_sending(key_docs), "seq", axis=1, tiled=True),
            ),
        )
    else:
        final_top, final_total, final_sum = absorb(
            init_state,
            (
                lax.all_gather(keys_local, "seq", axis=1, tiled=True),
                lax.all_gather(values_local, "seq", axis=1, tiled=True),
                lax.all_gather(key_docs, "seq", axis=1, tiled=True),
            ),
        )
    attended = (
        (final_sum / final_total[..., None])
        .transpose(0, 2, 1, 3)
        .reshape(rows_here, shard_len, model_width)
    )
    return (attended, final_top + jnp.log(final_total))


def attend_back(
    queries,
    keys_local,
    values_local,
    query_docs,
    key_docs,
    causal,
    log_total,
    grad_attended,
    is_cross,
):
    rows_here, shard_len, model_width = queries.shape
    head_dim = model_width // HEADS
    score_scale = head_dim ** (-0.5)
    query_place = lax.axis_index("seq") * shard_len + jnp.arange(shard_len)
    if is_cross:
        keys_full, values_full, docs_full = (
            lax.all_gather(keys_local, "seq", axis=1, tiled=True),
            lax.all_gather(values_local, "seq", axis=1, tiled=True),
            lax.all_gather(for_sending(key_docs), "seq", axis=1, tiled=True).astype(key_docs.dtype),
        )
    else:
        keys_full, values_full, docs_full = (
            lax.all_gather(keys_local, "seq", axis=1, tiled=True),
            lax.all_gather(values_local, "seq", axis=1, tiled=True),
            lax.all_gather(key_docs, "seq", axis=1, tiled=True),
        )
    full_len = keys_full.shape[1]
    query_heads = queries.reshape(rows_here, shard_len, HEADS, head_dim)
    key_heads = keys_full.reshape(rows_here, full_len, HEADS, head_dim)
    value_heads = values_full.reshape(rows_here, full_len, HEADS, head_dim)
    grad_heads = grad_attended.reshape(rows_here, shard_len, HEADS, head_dim)
    raw_scores = jnp.einsum(
        "rqhd,rkhd->rhqk", query_heads, key_heads, preferred_element_type=jnp.float32
    )
    allowed = allowed_mask(query_docs, docs_full, query_place, jnp.arange(full_len), causal)
    shifted = jnp.where(allowed, raw_scores * score_scale - log_total[..., None], negative_big)
    probs = jnp.where(allowed, jnp.exp(shifted), 0.0)
    grad_probs = jnp.einsum(
        "rqhd,rkhd->rhqk", grad_heads, value_heads, preferred_element_type=jnp.float32
    )
    delta = jnp.sum(probs * grad_probs, axis=-1)
    grad_scores = (probs * (grad_probs - delta[..., None]) * score_scale).astype(jnp.bfloat16)
    grad_queries = jnp.einsum(
        "rhqk,rkhd->rqhd", grad_scores, key_heads, preferred_element_type=jnp.float32
    ).reshape(rows_here, shard_len, model_width)
    probs_low = probs.astype(jnp.bfloat16)

    def key_terms(span):
        grad_keys = jnp.einsum(
            "rhqk,rqhd->krhd", grad_scores, query_heads, preferred_element_type=jnp.float32
        )
        grad_values = jnp.einsum(
            "rhqk,rqhd->krhd", probs_low, grad_heads, preferred_element_type=jnp.float32
        )
        return jnp.concatenate(
            [
                grad_keys.reshape(span, rows_here, model_width),
                grad_values.reshape(span, rows_here, model_width),
            ],
            axis=-1,
        )

    if is_cross:
        pair_terms = lax.psum_scatter(
            key_terms(shard_len * lax.axis_size("seq")).astype(jnp.bfloat16),
            "seq",
            scatter_dimension=0,
            tiled=True,
        ).astype(jnp.float32)
    else:
        pair_terms = lax.psum_scatter(
            key_terms(shard_len * lax.axis_size("seq")).astype(jnp.bfloat16),
            "seq",
            scatter_dimension=0,
            tiled=True,
        ).astype(jnp.float32)
    return (grad_queries, pair_terms.transpose(1, 0, 2))


def layer_forward(hidden_in, doc_own, memory, memory_docs, weights, is_decoder):
    (
        qkv_weight,
        out_weight,
        in_weight,
        down_weight,
        gains_pair,
        query_weight,
        pair_weight,
        cross_weight,
        cross_gains,
    ) = weights
    model_width = hidden_in.shape[-1]
    mixed = matmul(hidden_in, qkv_weight).astype(jnp.bfloat16)
    attended, self_lse = attend(
        mixed[..., :model_width],
        mixed[..., model_width : 2 * model_width],
        mixed[..., 2 * model_width :],
        doc_own,
        doc_own,
        is_decoder,
        False,
    )
    attended = attended.astype(jnp.bfloat16)
    first, first_unit, first_inv = normalize(
        hidden_in.astype(jnp.float32) + matmul(attended, out_weight), gains_pair[0]
    )
    first_low = first.astype(jnp.bfloat16)
    cross_queries = matmul(first_low, query_weight).astype(jnp.bfloat16)
    pair = matmul(memory, pair_weight).astype(jnp.bfloat16)
    cross_att, cross_lse = attend(
        cross_queries,
        pair[..., :model_width],
        pair[..., model_width:],
        doc_own,
        memory_docs,
        False,
        True,
    )
    cross_att = cross_att.astype(jnp.bfloat16)
    second_cross, second_unit, second_inv = normalize(
        first + matmul(cross_att, cross_weight), cross_gains
    )
    second = jnp.where(is_decoder, second_cross, first)
    second_low = second.astype(jnp.bfloat16)
    upward = matmul(second_low, in_weight)
    active = jax.nn.silu(upward).astype(jnp.bfloat16)
    result, third_unit, third_inv = normalize(second + matmul(active, down_weight), gains_pair[1])
    saved = {
        "mixed": mixed,
        "attended": attended,
        "self_lse": self_lse,
        "first_unit": first_unit,
        "first_inv": first_inv,
        "first_low": first_low,
        "cross_queries": cross_queries,
        "pair": pair,
        "cross_att": cross_att,
        "cross_lse": cross_lse,
        "second_unit": second_unit,
        "second_inv": second_inv,
        "second_low": second_low,
        "upward": upward,
        "active": active,
        "third_unit": third_unit,
        "third_inv": third_inv,
    }
    return (result, saved)


def layer_backward(
    grad_result, saved, hidden_in, doc_own, memory, memory_docs, weights, is_decoder
):
    (
        qkv_weight,
        out_weight,
        in_weight,
        down_weight,
        gains_pair,
        query_weight,
        pair_weight,
        cross_weight,
        cross_gains,
    ) = weights
    model_width = hidden_in.shape[-1]
    grad_third, grad_gain_late = normalize_back(
        grad_result, saved["third_unit"], gains_pair[1], saved["third_inv"]
    )
    down_grad = grad_third.astype(jnp.bfloat16)
    grad_down_w = contract(saved["active"], down_grad)
    grad_active = matmul_back(down_grad, down_weight).astype(jnp.bfloat16)
    sigmoid_up = jax.nn.sigmoid(saved["upward"])
    grad_upward = (
        grad_active.astype(jnp.float32)
        * (sigmoid_up + saved["upward"] * sigmoid_up * (1.0 - sigmoid_up))
    ).astype(jnp.bfloat16)
    grad_in_w = contract(saved["second_low"], grad_upward)
    grad_second = grad_third + matmul_back(grad_upward, in_weight)
    grad_cross_sum, grad_cross_gain = normalize_back(
        grad_second, saved["second_unit"], cross_gains, saved["second_inv"]
    )
    decoder_flag = is_decoder.astype(jnp.float32)
    grad_cross_sum = grad_cross_sum * decoder_flag
    grad_cross_gain = grad_cross_gain * decoder_flag
    cross_branch = grad_cross_sum.astype(jnp.bfloat16)
    grad_cross_w = contract(saved["cross_att"], cross_branch)
    grad_cross_att = matmul_back(cross_branch, cross_weight).astype(jnp.bfloat16)
    pair = saved["pair"]
    grad_cross_q, grad_pair = attend_back(
        saved["cross_queries"],
        pair[..., :model_width],
        pair[..., model_width:],
        doc_own,
        memory_docs,
        False,
        saved["cross_lse"],
        grad_cross_att,
        True,
    )
    grad_cross_q = grad_cross_q.astype(jnp.bfloat16)
    grad_pair = grad_pair.astype(jnp.bfloat16)
    grad_query_w = contract(saved["first_low"], grad_cross_q)
    grad_pair_w = contract(memory, grad_pair)
    grad_memory = matmul_back(grad_pair, pair_weight)
    grad_first = jnp.where(
        is_decoder, grad_cross_sum + matmul_back(grad_cross_q, query_weight), grad_second
    )
    grad_first_sum, grad_gain_early = normalize_back(
        grad_first, saved["first_unit"], gains_pair[0], saved["first_inv"]
    )
    self_branch = grad_first_sum.astype(jnp.bfloat16)
    grad_out_w = contract(saved["attended"], self_branch)
    grad_attended = matmul_back(self_branch, out_weight).astype(jnp.bfloat16)
    mixed = saved["mixed"]
    grad_queries, grad_pair_self = attend_back(
        mixed[..., :model_width],
        mixed[..., model_width : 2 * model_width],
        mixed[..., 2 * model_width :],
        doc_own,
        doc_own,
        is_decoder,
        saved["self_lse"],
        grad_attended,
        False,
    )
    grad_mixed = jnp.concatenate([grad_queries, grad_pair_self], axis=-1).astype(jnp.bfloat16)
    grad_qkv_w = contract(hidden_in, grad_mixed)
    grad_hidden = grad_first_sum + matmul_back(grad_mixed, qkv_weight)
    layer_grads = (
        grad_qkv_w,
        grad_out_w,
        grad_in_w,
        grad_down_w,
        jnp.stack([grad_gain_early, grad_gain_late]),
        grad_query_w,
        grad_pair_w,
        grad_cross_w,
        grad_cross_gain,
    )
    return (grad_hidden, grad_memory, layer_grads)


def any_rows(
    layer_input,
    segment_ids,
    attn_qkv,
    attn_out,
    ffn_in,
    ffn_out,
    norm_gain,
    cross_query,
    cross_pair,
    cross_out,
    cross_gain,
    out_cotangent,
):
    micro_count = layer_input.shape[1]
    section_index = lax.axis_index("section")
    is_decoder = section_index == 1
    weights = (
        attn_qkv[0],
        attn_out[0],
        ffn_in[0],
        ffn_out[0],
        norm_gain[0],
        cross_query,
        cross_pair,
        cross_out,
        cross_gain,
    )
    inputs_all = layer_input[0]
    docs_all = segment_ids[0]
    slot_ids = jnp.arange(micro_count)
    received = (jnp.zeros_like(inputs_all[0]), jnp.zeros_like(docs_all[0]))
    results = jnp.zeros_like(inputs_all)
    memories = []
    memory_doc_list = []
    for step_index in range(micro_count + 1):
        batch_index = step_index - section_index
        is_valid = (batch_index >= 0) & (batch_index < micro_count)
        chosen = jnp.clip(batch_index, 0, micro_count - 1)
        hidden_in = lax.dynamic_index_in_dim(inputs_all, chosen, 0, keepdims=False)
        doc_own = lax.dynamic_index_in_dim(docs_all, chosen, 0, keepdims=False)
        memory = received[0]
        memory_docs = jnp.where(is_valid & is_decoder, received[1], doc_own)
        memories.append(memory)
        memory_doc_list.append(memory_docs)
        result, saved = layer_forward(hidden_in, doc_own, memory, memory_docs, weights, is_decoder)
        low_result = result.astype(jnp.bfloat16)
        writing = (slot_ids == chosen) & is_valid
        results = jnp.where(writing[:, None, None, None], low_result[None], results)
        if step_index < micro_count:
            received = from_behind((low_result, doc_own), "section", 1)
    memory_stack = jnp.stack(memories)
    memory_doc_stack = jnp.stack(memory_doc_list)
    totals = tuple((jnp.zeros(weight.shape, jnp.float32) for weight in weights))
    input_grads = jnp.zeros(inputs_all.shape, jnp.float32)
    returned = jnp.zeros(inputs_all.shape[1:], jnp.float32)
    for step_index in range(micro_count + 1):
        batch_index = micro_count - step_index - section_index
        is_valid = (batch_index >= 0) & (batch_index < micro_count)
        chosen = jnp.clip(batch_index, 0, micro_count - 1)
        forward_step = jnp.clip(batch_index + section_index, 0, micro_count)
        hidden_in = lax.dynamic_index_in_dim(inputs_all, chosen, 0, keepdims=False)
        doc_own = lax.dynamic_index_in_dim(docs_all, chosen, 0, keepdims=False)
        memory = lax.dynamic_index_in_dim(memory_stack, forward_step, 0, keepdims=False)
        memory_docs = lax.dynamic_index_in_dim(memory_doc_stack, forward_step, 0, keepdims=False)
        discarded, saved = layer_forward(
            hidden_in, doc_own, memory, memory_docs, weights, is_decoder
        )
        cotangent = jnp.where(
            is_decoder,
            lax.dynamic_index_in_dim(out_cotangent, chosen, 0, keepdims=False).astype(jnp.float32),
            returned,
        )
        grad_hidden, grad_memory, layer_grads = layer_backward(
            cotangent, saved, hidden_in, doc_own, memory, memory_docs, weights, is_decoder
        )
        valid_flag = is_valid.astype(jnp.float32)
        totals = tuple(
            (running + valid_flag * fresh for running, fresh in zip(totals, layer_grads))
        )
        writing = (slot_ids == chosen) & is_valid
        input_grads = jnp.where(writing[:, None, None, None], grad_hidden[None], input_grads)
        if step_index < micro_count:
            returned = from_behind(grad_memory.astype(jnp.bfloat16), "section", -1).astype(
                grad_memory.dtype
            )
    group_sums = lax.psum(
        (
            totals[0],
            totals[1],
            totals[2],
            totals[3],
            totals[4],
            totals[5],
            totals[6],
            totals[7],
            totals[8],
        ),
        ("seq", "dp"),
    )
    section_sums = group_sums[:5]
    cross_sums = (
        from_root(group_sums[5].astype(jnp.bfloat16), "section", 1).astype(jnp.float32),
        from_root(group_sums[6].astype(jnp.bfloat16), "section", 1).astype(jnp.float32),
        from_root(group_sums[7].astype(jnp.bfloat16), "section", 1).astype(jnp.float32),
        from_root(group_sums[8].astype(jnp.bfloat16), "section", 1).astype(jnp.float32),
    )
    return (
        results[None],
        input_grads[None],
        section_sums[0][None],
        section_sums[1][None],
        section_sums[2][None],
        section_sums[3][None],
        section_sums[4][None],
        cross_sums[0],
        cross_sums[1],
        cross_sums[2],
        cross_sums[3],
    )


def split_rows(
    layer_input,
    segment_ids,
    attn_qkv,
    attn_out,
    ffn_in,
    ffn_out,
    norm_gain,
    cross_query,
    cross_pair,
    cross_out,
    cross_gain,
    out_cotangent,
):
    micros = layer_input.shape[1]
    length, width = layer_input.shape[3:]
    hidden = ffn_in.shape[-1]
    q_tiles = length // TILE
    group = lax.axis_size("dp") // 2
    axes = ("section", "seq", "dp")
    decoder = lax.axis_index("section") == 1
    flag = decoder.astype(jnp.int32)
    x = lax.axis_index("seq")
    core = lax.rem(lax.axis_index("dp"), 2)
    z = lax.axis_index("dp") // 2
    places = [(t, i, k, c) for t in range(2) for i in range(2) for k in range(group) for c in range(2)]

    def number(t, i, k, c):
        return ((t * 2 + i) * group + k) * 2 + c

    def send(values, target, section=None):
        route = [
            (number(*place), number(*target(*place)))
            for place in places
            if section in (None, place[0]) and target(*place)
        ]
        return lax.ppermute(values, axes, route)

    def to_core(t, i, k, c):
        return (t, i, k, 1 - c)

    def to_x(t, i, k, c):
        return (t, 1 - i, k, c)

    def to_row(t, i, k, c):
        return (t, c, k, i)

    def to_decoder(t, i, k, c):
        return (1, i, k, c) if t == 0 else None

    def to_encoder(t, i, k, c):
        return (0, i, k, c) if t == 1 else None

    def exchange(values):
        return send(values, to_core)

    low = ((length, width), bf16)
    wide = ((length, width), f32)
    pair = ((length, 2 * width), bf16)
    inner = ((length, hidden), bf16)
    lse = ((q_tiles, 8, 2 * TILE), f32)
    stat = ((length, LANES), f32)
    square = ((width, width), bf16)
    rising = ((width, hidden), bf16)
    falling = ((hidden, width), bf16)
    gain_rows = ((8, width), f32)
    dense = 2 * length * width * width

    inputs = send(layer_input[0, :, 0], to_row)
    documents = segment_ids[0, :, 0]
    docs_own = send(documents, to_row)
    docs_other = send(documents, lambda t, i, k, c: (t, c, k, 1 - i))
    docs_row = jnp.concatenate([docs_own, docs_other], axis=1)
    cotangent = send(out_cotangent[:, 0], to_row)

    def meta(*values):
        return jnp.stack(values).astype(jnp.int32)

    always = meta(1, flag, core)
    here = [meta(1 - flag, flag, core), meta(flag, flag, core)]

    def places_of(micro, keys):
        queries = docs_own[micro]
        return (
            dict(qd_s=queries, kd_s=keys[micro]),
            dict(
                qd=queries.astype(f32).reshape(q_tiles, 1, TILE),
                kd=keys[micro].astype(f32)[None],
            ),
        )

    gains = norm_gain[0]

    projected, others = [], []
    for micro in range(micros):
        call = launch(
            project_kernel,
            micro,
            dict(),
            dict(),
            dict(x_h=inputs, w_h=attn_qkv[0]),
            dict(pair_o=pair, q_o=low),
            dict(x=low, w=((width, 3 * width), bf16), pair=pair, q=low),
            4,
            3 * dense,
        )
        projected.append(call)
        others.append(exchange(call.pair_o))

    docs_source = send(docs_row, to_decoder)

    forward, memories = [], []
    for micro in range(micros):
        scalars, small = places_of(micro, docs_row)
        call = launch(
            self_forward_kernel,
            micro,
            dict(meta=always, **scalars),
            dict(**small, gains=gains),
            dict(
                q_h=projected[micro].q_o,
                kv_h=projected[micro].pair_o,
                kv_other_h=others[micro],
                x_h=inputs,
                w_out_h=attn_out[0],
                w_in_h=ffn_in[0],
                w_down_h=ffn_out[0],
            ),
            dict(
                att_o=low,
                lse_o=lse,
                unit1_o=wide,
                inv1_o=stat,
                first_low_o=low,
                memory_o=low,
                ffn_low_o=low,
                act_o=inner,
                slope_o=inner,
                unit2_o=wide,
                inv2_o=stat,
            ),
            dict(
                **attention_scratch(length, width),
                **forward_scratch(length, width),
                x=low,
                w_out=square,
                w_in=rising,
                w_down=falling,
                unit1=wide,
                inv1=stat,
                first_low=low,
                memory=low,
                act=inner,
                slope=inner,
                unit2=wide,
                inv2=stat,
                sum=wide,
            ),
            24,
            30 * dense,
        )
        forward.append(call)
        memories.append(send(call.memory_o, to_decoder))

    cross, grads_pair, grads_memory = [], [], []
    latest = forward[-1].lse_o
    for micro in range(micros):
        pair_call = launch(
            pair_kernel,
            micro,
            dict(meta=here[1]),
            dict(),
            dict(memory_h=memories[micro], w_h=cross_pair),
            dict(pair_o=pair),
            dict(x=low, w=((width, 2 * width), bf16), pair=pair),
            3,
            2 * dense,
            after=(latest,),
        )
        scalars, small = places_of(micro, docs_source)
        done = forward[micro]
        after = (grads_pair[-1].grad_memory_o,) if micro else ()
        call = launch(
            cross_kernel,
            micro,
            dict(meta=here[1], **scalars),
            dict(**small, gains=gains, cross_gain=cross_gain[None]),
            dict(
                pair_h=pair_call.pair_o,
                pair_other_h=exchange(pair_call.pair_o),
                first_low_h=done.first_low_o,
                unit1_h=done.unit1_o,
                w_query_h=cross_query,
                w_cross_h=cross_out,
                w_in_h=ffn_in[0],
                w_down_h=ffn_out[0],
                cot_h=cotangent,
            ),
            dict(
                att_o=low,
                ffn_low_o=low,
                act_o=inner,
                decoded_o=low,
                down_grad_o=low,
                up_grad_o=inner,
                gain_grads_o=gain_rows,
                branch_o=low,
                dkv_own_o=((length, 2 * width), f32),
                dkv_other_o=pair,
                dq_low_o=low,
                grad_first_o=wide,
            ),
            dict(
                **attention_scratch(length, width),
                **forward_scratch(length, width),
                **backward_scratch(length, width),
                first_low=low,
                unit1=wide,
                w_query=square,
                w_cross=square,
                w_in=rising,
                w_down=falling,
                cot=low,
                unit2=wide,
                inv2=stat,
                second_low=low,
                act=inner,
                slope=((length, hidden), f32),
                sum=wide,
                decoded=low,
                keep=wide,
                down_grad=low,
                up_grad=inner,
                gain_grads=gain_rows,
                branch=low,
            ),
            32,
            80 * dense,
            dict(act_o=done.act_o, ffn_low_o=done.ffn_low_o),
            after,
        )
        cross.append(call)
        latest = call.gain_grads_o
        back = launch(
            memory_backward_kernel,
            micro,
            dict(meta=here[1]),
            dict(),
            dict(own_h=call.dkv_own_o, got_h=exchange(call.dkv_other_o), w_h=cross_pair),
            dict(grad_pair_o=pair, grad_memory_o=low),
            dict(
                own=((length, 2 * width), f32),
                got=pair,
                pair=pair,
                x=low,
                w=((width, 2 * width), bf16),
            ),
            6,
            2 * dense,
        )
        grads_pair.append(back)
        grads_memory.append(send(back.grad_memory_o, to_encoder))

    def backward_feed(micro, after):
        done, late = forward[micro], cross[micro]
        return launch(
            feed_backward_kernel,
            micro,
            dict(meta=here[0]),
            dict(gains=gains),
            dict(
                grad_memory_h=grads_memory[micro],
                unit2_h=done.unit2_o,
                inv2_h=done.inv2_o,
                slope_h=done.slope_o,
                w_in_h=ffn_in[0],
                w_down_h=ffn_out[0],
            ),
            dict(gain_late_o=gain_rows, down_grad_o=low, up_grad_o=inner, grad_first_o=wide),
            dict(
                cot=low,
                unit2=wide,
                inv2=stat,
                slope=inner,
                w_in=rising,
                w_down=falling,
                gain_grads=gain_rows,
                keep=wide,
                down_grad=low,
                up_grad=inner,
                sum=wide,
            ),
            12,
            8 * dense,
            dict(
                down_grad_o=late.down_grad_o, up_grad_o=late.up_grad_o, grad_first_o=late.grad_first_o
            ),
            after,
        )

    def backward_self(micro, run, grad_first, previous, after):
        scalars, small = places_of(micro, docs_row)
        done = forward[micro]
        return launch(
            self_backward_kernel,
            micro,
            dict(meta=run, **scalars),
            dict(**small, gains=gains),
            dict(
                q_h=projected[micro].q_o,
                kv_h=projected[micro].pair_o,
                kv_other_h=others[micro],
                w_out_h=attn_out[0],
                att_h=done.att_o,
                lse_h=done.lse_o,
                unit1_h=done.unit1_o,
                inv1_h=done.inv1_o,
                grad_first_h=grad_first,
            ),
            dict(
                gain_early_o=gain_rows,
                grad_sum_o=wide,
                branch_o=low,
                dkv_own_o=((length, 2 * width), f32),
                dkv_other_o=pair,
                dq_low_o=low,
            ),
            dict(
                **attention_scratch(length, width),
                **backward_scratch(length, width),
                w_out=square,
                unit1=wide,
                inv1=stat,
                keep=wide,
                branch=low,
                grad_att=low,
                gain_grads=gain_rows,
            ),
            20,
            30 * dense,
            previous,
            after,
        )

    def weight_grads(plan, run, arrays, scratch, count, after=()):
        halves = [
            launch(
                contract_kernel,
                plan,
                dict(meta=meta(run, half)),
                dict(),
                arrays,
                dict(blocks_o=((count, width, width), bf16)),
                dict(
                    **{
                        name: ((micros * shape[0][0],) + shape[0][1:], shape[1])
                        for name, shape in scratch.items()
                    },
                    turn=((width, micros * length), bf16),
                    blocks=((count, width, width), bf16),
                ),
                16,
                2 * count * dense,
                after=after,
            ).blocks_o
            for half in (1 - core, core)
        ]
        return halves

    def sum_blocks(sent, kept, section=None):
        got = send(sent, to_core, section)
        half = kept.shape[0] // 2

        def both(side):
            return sum(
                lax.dynamic_slice_in_dim(part, side * half, half).astype(f32) for part in (kept, got)
            )

        arrived = send(both(1 - x).astype(bf16), to_x, section)
        total = both(x) + arrived.astype(f32)
        shares = total.astype(bf16).reshape(group, half * width // group, width)

        def share(step):
            return lax.dynamic_index_in_dim(shares, lax.rem(z + step, group), 0, keepdims=False)

        parts = [share(0)]
        for step in range(1, group):
            parts.append(
                send(share(step), lambda t, i, k, c, s=step: (t, i, (k + s) % group, c), section)
            )
        return sum(part.astype(f32) for part in parts).astype(bf16)

    def gather_z(share, section=None):
        parts = [share]
        for step in range(1, group):
            parts.append(
                send(share, lambda t, i, k, c, s=step: (t, i, (k + s) % group, c), section)
            )
        return jnp.stack(parts)

    def spread(targets, own, own_x, other, other_x, outs):
        scale = own.shape[0] * own.shape[1]
        return launch(
            spread_kernel,
            targets,
            dict(meta=meta(core, x, z)),
            dict(),
            dict(own_h=own, own_x_h=own_x, other_h=other, other_x_h=other_x),
            outs,
            dict(
                pieces=((4,) + own.shape, bf16),
                wide=((4 * group,) + own.shape[1:], f32),
            ),
            4 + 4 * group,
            scale,
        )

    last = micros - 1
    latest = cross[last].gain_grads_o
    feeds, ends = [None] * micros, [None] * micros
    for micro in range(last):
        feeds[micro] = backward_feed(micro, (latest,))
        first = feeds[micro].grad_first_o
        ends[micro] = backward_self(micro, here[0], first, None, ())
        ends[micro] = backward_self(
            micro, here[1], first, vars(ends[micro]), (grads_pair[last].grad_memory_o,)
        )
        latest = ends[micro].gain_early_o
    feeds[last] = backward_feed(last, (latest,))

    def cross_plan(r):
        return [
            (
                [
                    (r.low, (r.low0_h, r.low1_h)),
                    (r.dq, (r.dq0_h, r.dq1_h)),
                    (r.att, (r.att0_h, r.att1_h)),
                    (r.branch, (r.branch0_h, r.branch1_h)),
                ],
                [(r.low, 0, r.dq, 0), (r.att, 0, r.branch, 0)],
            ),
            (
                [(r.mem, (r.mem0_h, r.mem1_h)), (r.pair, (r.pair0_h, r.pair1_h))],
                [(r.mem, 0, r.pair, 0), (r.mem, 0, r.pair, 1)],
            ),
        ]

    def feed_plan(r):
        return [
            (
                [(r.low, (r.low0_h, r.low1_h)), (r.up, (r.up0_h, r.up1_h))],
                [(r.low, 0, r.up, block) for block in range(hidden // CHUNK)],
            ),
            (
                [(r.act, (r.act0_h, r.act1_h)), (r.down, (r.down0_h, r.down1_h))],
                [(r.act, block, r.down, 0) for block in range(hidden // CHUNK)],
            ),
        ]

    def self_plan(r):
        return [
            (
                [(r.x, (r.x_h.at[0], r.x_h.at[1])), (r.dq, (r.dq0_h, r.dq1_h)), (r.pair, (r.pair0_h, r.pair1_h))],
                [(r.x, 0, r.dq, 0), (r.x, 0, r.pair, 0)],
            ),
            (
                [
                    (r.x, (r.x_h.at[0], r.x_h.at[1])),
                    (r.pair, (r.pair0_h, r.pair1_h)),
                    (r.att, (r.att0_h, r.att1_h)),
                    (r.branch, (r.branch0_h, r.branch1_h)),
                ],
                [(r.x, 0, r.pair, 1), (r.att, 0, r.branch, 0)],
            ),
        ]

    cross_sent, cross_kept = weight_grads(
        cross_plan,
        flag,
        dict(
            low0_h=forward[0].first_low_o,
            low1_h=forward[1].first_low_o,
            dq0_h=cross[0].dq_low_o,
            dq1_h=cross[1].dq_low_o,
            att0_h=cross[0].att_o,
            att1_h=cross[1].att_o,
            branch0_h=cross[0].branch_o,
            branch1_h=cross[1].branch_o,
            mem0_h=memories[0],
            mem1_h=memories[1],
            pair0_h=grads_pair[0].grad_pair_o,
            pair1_h=grads_pair[1].grad_pair_o,
        ),
        dict(low=low, dq=low, att=low, branch=low, mem=low, pair=pair),
        2,
    )
    cross_share = sum_blocks(cross_sent, cross_kept, 1)

    feed_sent, feed_kept = weight_grads(
        feed_plan,
        1,
        dict(
            low0_h=cross[0].ffn_low_o,
            low1_h=cross[1].ffn_low_o,
            up0_h=feeds[0].up_grad_o,
            up1_h=feeds[1].up_grad_o,
            act0_h=cross[0].act_o,
            act1_h=cross[1].act_o,
            down0_h=feeds[0].down_grad_o,
            down1_h=feeds[1].down_grad_o,
        ),
        dict(low=low, up=inner, act=inner, down=low),
        hidden // CHUNK,
    )
    feed_share = sum_blocks(feed_sent, feed_kept)

    ends[last] = backward_self(last, always, feeds[last].grad_first_o, None, (feed_kept,))

    steps = []
    for micro in range(micros):
        end = ends[micro]
        steps.append(
            launch(
                input_backward_kernel,
                micro,
                dict(),
                dict(),
                dict(
                    own_h=end.dkv_own_o,
                    got_h=exchange(end.dkv_other_o),
                    w_h=attn_qkv[0],
                    dq_h=end.dq_low_o,
                    grad_sum_h=end.grad_sum_o,
                ),
                dict(grad_pair_o=pair, grad_input_o=low),
                dict(
                    own=((length, 2 * width), f32),
                    got=pair,
                    pair=pair,
                    x=low,
                    dq=low,
                    keep=wide,
                    w=((width, 3 * width), bf16),
                ),
                8,
                3 * dense,
            )
        )
    self_sent, self_kept = weight_grads(
        self_plan,
        1,
        dict(
            x_h=inputs,
            dq0_h=ends[0].dq_low_o,
            dq1_h=ends[1].dq_low_o,
            pair0_h=steps[0].grad_pair_o,
            pair1_h=steps[1].grad_pair_o,
            att0_h=forward[0].att_o,
            att1_h=forward[1].att_o,
            branch0_h=ends[0].branch_o,
            branch1_h=ends[1].branch_o,
        ),
        dict(x=low, dq=low, pair=pair, att=low, branch=low),
        2,
    )
    self_share = sum_blocks(self_sent, self_kept)

    def gather(share):
        own = gather_z(share)
        own_x = send(own, to_x)
        return own, own_x, exchange(own), exchange(own_x)

    cross_own = gather_z(cross_share, 1)
    cross_own_x = send(cross_own, to_x, 1)
    cross_own, cross_own_x = (
        jnp.where(decoder, part, send(part, to_encoder)) for part in (cross_own, cross_own_x)
    )

    def feed_targets(r, half, side, row, rows):
        start = side * (hidden // CHUNK // 2) * width
        line = start + row
        if half == 1:
            return r.down_o.at[pl.ds(line, rows)]
        column = pl.multiple_of(line // width * CHUNK, CHUNK)
        return r.up_o.at[pl.ds(pl.multiple_of(lax.rem(line, width), rows), rows), pl.ds(column, CHUNK)]

    def self_targets(r, half, side, row, rows):
        if (half, side) == (1, 1):
            return r.out_o.at[pl.ds(row, rows)]
        return r.mixed_o.at[pl.ds(row, rows), pl.ds((2 * half + side) * width, width)]

    def cross_targets(r, half, side, row, rows):
        if half == 1:
            return r.pair_o.at[pl.ds(row, rows), pl.ds(side * width, width)]
        return (r.out_o if side else r.query_o).at[pl.ds(row, rows)]

    square_out = ((width, width), f32)
    cross_grads = spread(
        cross_targets,
        cross_own,
        cross_own_x,
        exchange(cross_own),
        exchange(cross_own_x),
        dict(query_o=square_out, pair_o=((width, 2 * width), f32), out_o=square_out),
    )
    feed_grads = spread(
        feed_targets,
        *gather(feed_share),
        dict(up_o=((width, hidden), f32), down_o=((hidden, width), f32)),
    )
    self_grads = spread(
        self_targets,
        *gather(self_share),
        dict(mixed_o=((width, 3 * width), f32), out_o=square_out),
    )

    early = sum(end.gain_early_o[0] for end in ends)
    late = jnp.where(
        decoder,
        sum(call.gain_grads_o[0] for call in cross),
        sum(call.gain_late_o[0] for call in feeds),
    )
    third = jnp.where(decoder, sum(call.gain_grads_o[1] for call in cross), 0.0)
    gain_sums = jnp.stack([early, late, third])
    gain_sums += exchange(gain_sums)
    gain_sums += send(gain_sums, to_x)
    step = 1
    while step < group:
        gain_sums += send(gain_sums, lambda t, i, k, c, s=step: (t, i, k ^ s, c))
        step *= 2
    third = jnp.where(decoder, gain_sums[2], send(gain_sums[2], to_encoder))

    results = jnp.stack(
        [
            jnp.where(decoder, call.decoded_o, done.memory_o)
            for call, done in zip(cross, forward)
        ]
    )
    results = send(results, to_row)
    grad_input = jnp.stack([send(step.grad_input_o, to_row) for step in steps])
    return (
        results[None, :, None],
        grad_input.astype(f32)[None, :, None],
        self_grads.mixed_o[None],
        self_grads.out_o[None],
        feed_grads.up_o[None],
        feed_grads.down_o[None],
        gain_sums[None, :2],
        cross_grads.query_o,
        cross_grads.pair_o,
        cross_grads.out_o,
        third,
    )


def shards(*arrays):
    layer_input = arrays[0]
    micros, rows, length = layer_input.shape[1:4]
    simple = (
        lax.axis_size("section") == 2
        and lax.axis_size("seq") == 2
        and lax.axis_size("dp") in (4, 8, 16)
        and (micros, rows) == (2, 1)
        and length % TILE == 0
    )
    return split_rows(*arrays) if simple else any_rows(*arrays)


def solution(mesh):
    in_specs = (
        P("section", None, "dp", "seq", None),
        P("section", None, "dp", "seq"),
        P("section", None, None),
        P("section", None, None),
        P("section", None, None),
        P("section", None, None),
        P("section", None, None),
        P(),
        P(),
        P(),
        P(),
        P(None, "dp", "seq", None),
    )
    out_specs = (
        P("section", None, "dp", "seq", None),
        P("section", None, "dp", "seq", None),
        P("section", None, None),
        P("section", None, None),
        P("section", None, None),
        P("section", None, None),
        P("section", None, None),
        P(),
        P(),
        P(),
        P(),
    )
    return jax.shard_map(shards, mesh=mesh, in_specs=in_specs, out_specs=out_specs, check_vma=False)
```

```python
import types

import jax
import jax.numpy as jnp
from jax import lax
from jax.experimental import pallas as pl
from jax.experimental.pallas import tpu as pltpu
from jax.sharding import PartitionSpec as P

HEADS = 8
TILE = 256
LANES = 128
CHUNK = 512

f32 = jnp.float32
bf16 = jnp.bfloat16
negative_big = -1e30
epsilon = 1e-05


def dot(left, right):
    return lax.dot_general(left, right, (((1,), (0,)), ((), ())), preferred_element_type=f32)


def dot_nt(left, right):
    return lax.dot_general(left, right, (((1,), (1,)), ((), ())), preferred_element_type=f32)


def dot_tn(left, right):
    return lax.dot_general(left, right, (((0,), (0,)), ((), ())), preferred_element_type=f32)


def standardize(values):
    center = values - jnp.mean(values, axis=-1, keepdims=True)
    inverse = lax.rsqrt(jnp.mean(center * center, axis=-1, keepdims=True) + epsilon)
    return center * inverse, inverse


def standardize_back(grad_out, standard, gain_row, inverse):
    scaled = grad_out * gain_row
    grad_in = inverse * (
        scaled
        - jnp.mean(scaled, axis=-1, keepdims=True)
        - standard * jnp.mean(scaled * standard, axis=-1, keepdims=True)
    )
    return grad_in, jnp.sum(grad_out * standard, axis=0, keepdims=True)


class Copies:
    def __init__(self, sems):
        self.sems = sems
        self.used = 0

    def start(self, source, target):
        copy = pltpu.make_async_copy(source, target, self.sems.at[self.used])
        self.used += 1
        copy.start()
        return copy


def wait_all(copies):
    for copy in copies:
        copy.wait()


def spread_pairs(target, source, factor):
    pairs, tiles = target.shape[:2]
    half = lax.broadcasted_iota(jnp.int32, (TILE, LANES), 1) < LANES // 2
    first = jnp.where(half, factor, 0.0).astype(bf16)
    second = jnp.where(half, 0.0, factor).astype(bf16)
    for tile in range(tiles):
        for pair in range(pairs):
            block = source[tile * TILE : (tile + 1) * TILE, pair * LANES : (pair + 1) * LANES]
            target[pair, tile, :TILE, :] = block * first
            target[pair, tile, TILE:, :] = block * second


def turn_tiles(target, source, column):
    tiles, width, _ = target.shape
    for tile in range(tiles):
        block = source[tile * TILE : (tile + 1) * TILE, column : column + width]
        target[tile] = jnp.transpose(block.astype(f32)).astype(bf16)


def turn_documents(target, key_docs):
    for start in range(0, target.shape[0], LANES):
        row = key_docs[:, start : start + LANES]
        target[start : start + LANES, :] = jnp.transpose(jnp.broadcast_to(row, (LANES, LANES)))


def tile_place(r, core, causal, q_tile, k_tile):
    q_tiles = r.qd.shape[1]
    length = q_tiles * TILE
    owner = jnp.where(k_tile < q_tiles, core, 1 - core)
    k_start = owner * length + lax.rem(k_tile, q_tiles) * TILE
    ahead = core * length + q_tile * TILE - k_start
    ahead = jnp.where(causal == 1, ahead, 2 * length * TILE)
    q_low, q_high = r.qd_s[r.micro, q_tile * TILE], r.qd_s[r.micro, q_tile * TILE + TILE - 1]
    k_low, k_high = r.kd_s[r.micro, k_tile * TILE], r.kd_s[r.micro, k_tile * TILE + TILE - 1]
    active = (q_low <= k_high) & (k_low <= q_high) & (ahead > -TILE)
    return active, ahead


def fill_bias(r, q_tile, k_tile, ahead):
    keys = r.kdc[pl.ds(pl.multiple_of(k_tile * TILE, TILE), TILE), :]
    shift = lax.broadcasted_iota(jnp.int32, (TILE, LANES), 0) - lax.broadcasted_iota(
        jnp.int32, (TILE, LANES), 1
    )
    queries = r.qd[r.micro, q_tile]
    for start in range(0, TILE, LANES):
        same = keys == queries[:, start : start + LANES]
        allowed = same & (shift - start <= ahead)
        r.bias[:, start : start + LANES] = jnp.where(allowed, 0.0, negative_big)


def attention_forward(r, core, causal):
    pairs, q_tiles = r.qm.shape[:2]
    k_tiles = r.vt.shape[0]

    def one_query_tile(q_tile, carry):
        r.top[...] = jnp.full(r.top.shape, negative_big, f32)
        r.total[...] = jnp.zeros(r.total.shape, f32)
        r.turned[...] = jnp.zeros(r.turned.shape, f32)

        def one_key_tile(k_tile, inner):
            active, ahead = tile_place(r, core, causal, q_tile, k_tile)

            @pl.when(active)
            def _():
                fill_bias(r, q_tile, k_tile, ahead)
                rows = pl.ds(pl.multiple_of(k_tile * TILE, TILE), TILE)

                def raw(pair):
                    keys = r.kv[rows, pair * LANES : (pair + 1) * LANES]
                    return dot_nt(keys, r.qm[pair, q_tile])

                raw_next = raw(0)
                for pair in range(pairs):
                    bias = r.bias[...]
                    scores = raw_next + jnp.concatenate([bias, bias], axis=1)
                    if pair + 1 < pairs:
                        raw_next = raw(pair + 1)
                    old_top = r.top[pair : pair + 1, :]
                    new_top = jnp.maximum(old_top, jnp.max(scores, axis=0, keepdims=True))
                    weights = jnp.exp(scores - new_top)
                    shrink = jnp.exp(old_top - new_top)
                    r.top[pair : pair + 1, :] = new_top
                    r.total[pair : pair + 1, :] = r.total[
                        pair : pair + 1, :
                    ] * shrink + jnp.sum(weights, axis=0, keepdims=True)
                    low = weights.astype(bf16)
                    for side in range(2):
                        span = slice(side * TILE, (side + 1) * TILE)
                        head = slice((2 * pair + side) * 64, (2 * pair + side + 1) * 64)
                        r.turned[head, :] = r.turned[head, :] * shrink[:, span] + dot(
                            r.vt[k_tile, head, :], low[:, span]
                        )

            return inner

        lax.fori_loop(0, k_tiles, one_key_tile, 0)
        for pair in range(pairs):
            total = r.total[pair : pair + 1, :]
            r.lse[q_tile, pair : pair + 1, :] = r.top[pair : pair + 1, :] + jnp.log(total)
            share = 1.0 / total
            for side in range(2):
                span = slice(side * TILE, (side + 1) * TILE)
                head = slice((2 * pair + side) * 64, (2 * pair + side + 1) * 64)
                r.turned[head, :] = r.turned[head, :] * share[:, span]
        rows = pl.ds(pl.multiple_of(q_tile * TILE, TILE), TILE)
        r.att[rows, :] = jnp.transpose(r.turned[...]).astype(bf16)
        return carry

    lax.fori_loop(0, q_tiles, one_query_tile, 0)


def row_products(r, grad_att):
    pairs, q_tiles = r.qm.shape[:2]
    for tile in range(q_tiles):
        rows = slice(tile * TILE, (tile + 1) * TILE)
        product = jnp.transpose(grad_att[rows, :].astype(f32) * r.att[rows, :].astype(f32))
        for pair in range(pairs):
            for side in range(2):
                head = (2 * pair + side) * 64
                r.delta[tile, pair : pair + 1, side * TILE : (side + 1) * TILE] = jnp.sum(
                    product[head : head + 64, :], axis=0, keepdims=True
                )


def attention_backward(r, core, causal):
    pairs, q_tiles = r.qm.shape[:2]
    k_tiles = r.kt.shape[0]
    width = pairs * LANES
    r.dkv[...] = jnp.zeros(r.dkv.shape, f32)

    def one_query_tile(q_tile, carry):
        r.turned[...] = jnp.zeros(r.turned.shape, f32)

        def one_key_tile(k_tile, inner):
            active, ahead = tile_place(r, core, causal, q_tile, k_tile)

            @pl.when(active)
            def _():
                fill_bias(r, q_tile, k_tile, ahead)
                rows = pl.ds(pl.multiple_of(k_tile * TILE, TILE), TILE)

                def raw(pair):
                    lanes = slice(pair * LANES, (pair + 1) * LANES)
                    lanes_v = slice(width + pair * LANES, width + (pair + 1) * LANES)
                    return (
                        dot_nt(r.kv[rows, lanes], r.qm[pair, q_tile]),
                        dot_nt(r.kv[rows, lanes_v], r.gm[pair, q_tile]),
                    )

                raw_next = raw(0)
                for pair in range(pairs):
                    bias = r.bias[...]
                    scores, grad_probs = raw_next
                    scores = scores + jnp.concatenate([bias, bias], axis=1)
                    if pair + 1 < pairs:
                        raw_next = raw(pair + 1)
                    probs = jnp.exp(scores - r.lse[q_tile, pair : pair + 1, :])
                    grad_scores = probs * (grad_probs - r.delta[q_tile, pair : pair + 1, :])
                    probs_low = probs.astype(bf16)
                    grad_low = grad_scores.astype(bf16)
                    lanes = slice(pair * LANES, (pair + 1) * LANES)
                    lanes_v = slice(width + pair * LANES, width + (pair + 1) * LANES)
                    r.dkv[rows, lanes] += dot(grad_low, r.qm[pair, q_tile])
                    r.dkv[rows, lanes_v] += dot(probs_low, r.gm[pair, q_tile])
                    for side in range(2):
                        span = slice(side * TILE, (side + 1) * TILE)
                        head = slice((2 * pair + side) * 64, (2 * pair + side + 1) * 64)
                        r.turned[head, :] += dot(r.kt[k_tile, head, :], grad_low[:, span])

            return inner

        lax.fori_loop(0, k_tiles, one_key_tile, 0)
        rows = pl.ds(pl.multiple_of(q_tile * TILE, TILE), TILE)
        r.dq[rows, :] = jnp.transpose(r.turned[...]) * (64**-0.5)
        return carry

    lax.fori_loop(0, q_tiles, one_query_tile, 0)


def feed_forward(r, low):
    r.sum[...] = jnp.zeros(r.sum.shape, f32)

    def one_chunk(chunk, carry):
        span = pl.ds(pl.multiple_of(chunk * CHUNK, CHUNK), CHUNK)
        upward = dot(low[...], r.w_in[:, span])
        gate = jax.nn.sigmoid(upward)
        active = (upward * gate).astype(bf16)
        r.act[:, span] = active
        r.slope[:, span] = (gate + upward * gate * (1.0 - gate)).astype(r.slope.dtype)
        r.sum[...] += dot(active, r.w_down[span, :])
        return carry

    lax.fori_loop(0, r.w_in.shape[1] // CHUNK, one_chunk, 0)


def feed_backward(r):
    r.sum[...] = jnp.zeros(r.sum.shape, f32)

    def one_chunk(chunk, carry):
        span = pl.ds(pl.multiple_of(chunk * CHUNK, CHUNK), CHUNK)
        grad_active = dot_nt(r.down_grad[...], r.w_down[span, :]).astype(bf16)
        grad_up = (grad_active.astype(f32) * r.slope[:, span].astype(f32)).astype(bf16)
        r.up_grad[:, span] = grad_up
        r.sum[...] += dot_nt(grad_up, r.w_in[:, span])
        return carry

    lax.fori_loop(0, r.w_in.shape[1] // CHUNK, one_chunk, 0)


def self_forward(r):
    length, width = r.x_own_h.shape
    decoder, core = r.meta[0], r.meta[1]
    move = Copies(r.sems)
    early = [
        move.start(r.x_own_h, r.x.at[pl.ds(0, length)]),
        move.start(r.x_other_h, r.x.at[pl.ds(length, length)]),
        move.start(r.w_mixed_h, r.w_mixed),
    ]
    later = [
        move.start(r.w_out_h, r.w_out),
        move.start(r.w_in_h, r.w_in),
        move.start(r.w_down_h, r.w_down),
    ]
    turn_documents(r.kdc, r.kd[r.micro])
    wait_all(early)
    r.q[...] = dot(r.x[:length, :], r.w_mixed[:, :width]).astype(bf16)
    r.kv[...] = dot(r.x[...], r.w_mixed[:, width:]).astype(bf16)
    outs = [move.start(r.q, r.q_o), move.start(r.kv, r.kv_o)]
    spread_pairs(r.qm, r.q, 64**-0.5)
    turn_tiles(r.vt, r.kv, width)
    attention_forward(r, core, decoder)
    wait_all(later)
    outs += [move.start(r.att, r.att_o), move.start(r.lse, r.lse_o)]
    unit, inverse = standardize(r.x[:length, :].astype(f32) + dot(r.att[...], r.w_out[...]))
    r.unit1[...] = unit
    r.inv1[...] = jnp.broadcast_to(inverse, r.inv1.shape)
    r.first_low[...] = (unit * r.gains[0:1, :]).astype(bf16)
    outs += [
        move.start(r.unit1, r.unit1_o),
        move.start(r.inv1, r.inv1_o),
        move.start(r.first_low, r.first_low_o),
    ]

    @pl.when(decoder == 0)
    def _():
        feed_forward(r, r.first_low)
        late = [
            move.start(r.first_low, r.ffn_low_o),
            move.start(r.act, r.act_o),
            move.start(r.slope, r.slope_o),
        ]
        unit2, inverse2 = standardize(r.unit1[...] * r.gains[0:1, :] + r.sum[...])
        r.memory[...] = (unit2 * r.gains[1:2, :]).astype(bf16)
        late += [move.start(r.memory, r.memory_o)]
        r.unit2[...] = unit2
        r.inv2[...] = jnp.broadcast_to(inverse2, r.inv2.shape)
        late += [move.start(r.unit2, r.unit2_o), move.start(r.inv2, r.inv2_o)]
        wait_all(late)

    wait_all(outs)


def cross_both_ways(r):
    length, width = r.unit1_h.shape
    core = r.meta[1]
    move = Copies(r.sems)
    moves = [
        move.start(r.memory_own_h, r.x.at[pl.ds(0, length)]),
        move.start(r.memory_other_h, r.x.at[pl.ds(length, length)]),
        move.start(r.w_pair_h, r.w_pair),
        move.start(r.first_low_h, r.first_low),
        move.start(r.w_query_h, r.w_query),
    ]
    later = [
        move.start(r.unit1_h, r.unit1),
        move.start(r.w_cross_h, r.w_cross),
        move.start(r.w_in_h, r.w_in),
        move.start(r.w_down_h, r.w_down),
        move.start(r.cot_h.at[r.micro], r.cot),
    ]
    turn_documents(r.kdc, r.kd[r.micro])
    wait_all(moves)
    r.kv[...] = dot(r.x[...], r.w_pair[...]).astype(bf16)
    r.q[...] = dot(r.first_low[...], r.w_query[...]).astype(bf16)
    spread_pairs(r.qm, r.q, 64**-0.5)
    turn_tiles(r.vt, r.kv, width)
    turn_tiles(r.kt, r.kv, 0)
    attention_forward(r, core, 0)
    outs = [move.start(r.att, r.att_o)]
    wait_all(later)
    first = r.unit1[...] * r.gains[0:1, :]
    unit, inverse = standardize(first + dot(r.att[...], r.w_cross[...]))
    r.unit2[...] = unit
    r.inv2[...] = jnp.broadcast_to(inverse, r.inv2.shape)
    r.second_low[...] = (unit * r.cross_gain[...]).astype(bf16)
    outs += [move.start(r.second_low, r.ffn_low_o)]
    feed_forward(r, r.second_low)
    outs += [move.start(r.act, r.act_o)]
    unit3, inverse3 = standardize(r.unit2[...] * r.cross_gain[...] + r.sum[...])
    r.decoded[...] = (unit3 * r.gains[1:2, :]).astype(bf16)
    outs += [move.start(r.decoded, r.decoded_o)]
    grad_third, gain_late = standardize_back(
        r.cot[...].astype(f32), unit3, r.gains[1:2, :], inverse3
    )
    r.keep[...] = grad_third
    r.down_grad[...] = grad_third.astype(bf16)
    outs += [move.start(r.down_grad, r.down_grad_o)]
    feed_backward(r)
    outs += [move.start(r.up_grad, r.up_grad_o)]
    grad_sum, gain_cross = standardize_back(
        r.keep[...] + r.sum[...], r.unit2[...], r.cross_gain[...], r.inv2[:, 0:1]
    )
    r.gain_grads[...] = jnp.zeros(r.gain_grads.shape, f32)
    r.gain_grads[0:1, :] = gain_late
    r.gain_grads[1:2, :] = gain_cross
    r.keep[...] = grad_sum
    r.branch[...] = grad_sum.astype(bf16)
    outs += [move.start(r.gain_grads, r.gain_grads_o), move.start(r.branch, r.branch_o)]
    r.q[...] = dot_nt(r.branch[...], r.w_cross[...]).astype(bf16)
    spread_pairs(r.gm, r.q, 1.0)
    row_products(r, r.q)
    attention_backward(r, core, 0)
    r.dq_low[...] = r.dq[...].astype(bf16)
    r.keep[...] += dot_nt(r.dq_low[...], r.w_query[...])
    outs += [move.start(r.dq_low, r.dq_low_o), move.start(r.keep, r.grad_first_o)]
    r.dkv_low[...] = r.dkv[...].astype(bf16)
    outs += [move.start(r.dkv_low, r.dkv_o)]
    part = dot_nt(r.dkv_low[...], r.w_pair[...])
    r.part_other[...] = part[length:, :].astype(bf16)
    r.part_own[...] = part[:length, :]
    outs += [move.start(r.part_other, r.part_other_o), move.start(r.part_own, r.part_own_o)]
    wait_all(outs)


def feed_backward_alone(r):
    move = Copies(r.sems)
    early = [
        move.start(r.grad_memory_h, r.cot),
        move.start(r.unit2_h, r.unit2),
        move.start(r.inv2_h, r.inv2),
    ]
    later = [
        move.start(r.w_down_h, r.w_down),
        move.start(r.slope_h, r.slope),
        move.start(r.w_in_h, r.w_in),
    ]
    wait_all(early)
    grad_third, gain_late = standardize_back(
        r.cot[...].astype(f32), r.unit2[...], r.gains[1:2, :], r.inv2[:, 0:1]
    )
    r.gain_grads[...] = jnp.broadcast_to(gain_late, r.gain_grads.shape)
    r.keep[...] = grad_third
    r.down_grad[...] = grad_third.astype(bf16)
    outs = [move.start(r.down_grad, r.down_grad_o), move.start(r.gain_grads, r.gain_late_o)]
    wait_all(later)
    feed_backward(r)
    outs += [move.start(r.up_grad, r.up_grad_o)]
    r.keep[...] += r.sum[...]
    outs += [move.start(r.keep, r.grad_first_o)]
    wait_all(outs)


def self_backward(r):
    length, width = r.unit1_h.shape
    decoder, core = r.meta[0], r.meta[1]
    move = Copies(r.sems)
    early = [
        move.start(r.grad_first_h, r.keep),
        move.start(r.unit1_h, r.unit1),
        move.start(r.inv1_h, r.inv1),
    ]
    later = [
        move.start(r.w_out_h, r.w_out),
        move.start(r.q_h, r.q),
        move.start(r.kv_h, r.kv),
        move.start(r.att_h, r.att),
        move.start(r.lse_h, r.lse),
        move.start(r.w_mixed_h, r.w_mixed),
    ]
    turn_documents(r.kdc, r.kd[r.micro])
    wait_all(early)
    grad_sum, gain_early = standardize_back(
        r.keep[...], r.unit1[...], r.gains[0:1, :], r.inv1[:, 0:1]
    )
    r.gain_grads[...] = jnp.broadcast_to(gain_early, r.gain_grads.shape)
    r.keep[...] = grad_sum
    r.branch[...] = grad_sum.astype(bf16)
    outs = [move.start(r.gain_grads, r.gain_early_o), move.start(r.branch, r.branch_o)]
    wait_all(later)
    spread_pairs(r.qm, r.q, 64**-0.5)
    turn_tiles(r.kt, r.kv, 0)
    r.grad_att[...] = dot_nt(r.branch[...], r.w_out[...]).astype(bf16)
    spread_pairs(r.gm, r.grad_att, 1.0)
    row_products(r, r.grad_att)
    attention_backward(r, core, decoder)
    r.dq_low[...] = r.dq[...].astype(bf16)
    outs += [move.start(r.dq_low, r.dq_low_o)]
    r.keep[...] += dot_nt(r.dq_low[...], r.w_mixed[:, :width])
    r.dkv_low[...] = r.dkv[...].astype(bf16)
    outs += [move.start(r.dkv_low, r.dkv_o)]
    part = dot_nt(r.dkv_low[...], r.w_mixed[:, width:])
    r.part_other[...] = part[length:, :].astype(bf16)
    r.keep[...] += part[:length, :]
    outs += [move.start(r.part_other, r.part_other_o), move.start(r.keep, r.part_own_o)]
    wait_all(outs)


def contract_blocks(r, plan):
    operands, blocks = plan(r)
    for core in range(2):

        @pl.when(r.meta[1] == core)
        def _(core=core):
            move = Copies(r.sems)
            loads = []
            for target, sources in operands:
                row = 0
                for source in sources:
                    loads.append(move.start(source, target.at[pl.ds(row, source.shape[0])]))
                    row += source.shape[0]
            wait_all(loads)
            outs = []
            held = dict()
            for half in (1 - core, core):
                for place in range(2):
                    slot = 2 * half + place
                    turn, left, left_at, right, right_at = blocks[slot]
                    if held.get(id(turn)) != left_at:
                        for row in range(0, left.shape[0], CHUNK):
                            block = left[
                                row : row + CHUNK, left_at * CHUNK : (left_at + 1) * CHUNK
                            ]
                            turn[:, row : row + CHUNK] = jnp.transpose(block)
                        held[id(turn)] = left_at
                    block = right[:, right_at * CHUNK : (right_at + 1) * CHUNK]
                    r.blocks[slot] = dot(turn[:, : right.shape[0]], block).astype(bf16)
                    target = r.kept_o if half == core else r.sent_o
                    outs.append(move.start(r.blocks.at[slot], target.at[place]))
            wait_all(outs)


def spread_pieces(r, targets):
    z = r.meta[3]
    group, height = r.own_h.shape[:2]
    rows = r.own_h.shape[2] // group
    for core in range(2):
        for x in range(2):

            @pl.when((r.meta[1] == core) & (r.meta[2] == x))
            def _(core=core, x=x):
                move = Copies(r.sems)
                parts = [
                    (r.own_h, core, x),
                    (r.own_x_h, core, 1 - x),
                    (r.other_h, 1 - core, x),
                    (r.other_x_h, 1 - core, 1 - x),
                ]
                loads = [
                    move.start(source, r.pieces.at[place])
                    for place, (source, _, _) in enumerate(parts)
                ]
                outs = []
                slot = 0
                gains = None
                for place, (_, half, side) in enumerate(parts):
                    loads[place].wait()
                    for step in range(group):
                        row = pl.multiple_of(lax.rem(z + (group - step), group) * rows, rows)
                        start = 0
                        for target in targets(r, 2 * half + side, row, rows):
                            r.wide[slot] = r.pieces[place, step, start : start + rows].astype(f32)
                            outs.append(move.start(r.wide.at[slot], target))
                            slot += 1
                            start += rows
                        if start < height:
                            extra = r.pieces[place, step, start:height].astype(f32)
                            gains = extra if gains is None else gains + extra
                if gains is not None:
                    r.gain_grads[...] = gains
                    outs.append(move.start(r.gain_grads, r.gains_o))
                wait_all(outs)


def launch(kernel, plan, side, scalars, small, large, outs, scratch, copies, previous=None, after=()):
    names = list(scalars) + list(small) + list(large)
    arrays = list(scalars.values()) + list(small.values()) + list(large.values())
    specs = (
        [pl.BlockSpec(memory_space=pltpu.SMEM)] * len(scalars)
        + [pl.BlockSpec(memory_space=pltpu.VMEM)] * len(small)
        + [pl.BlockSpec(memory_space=pl.ANY)] * len(large)
    )
    aliases = dict()
    for position, name in enumerate(outs):
        if previous and name in previous:
            aliases[len(arrays)] = position
            names.append("previous_" + name)
            arrays.append(previous[name])
            specs.append(pl.BlockSpec(memory_space=pl.ANY))
    for array in after:
        names.append("")
        arrays.append(array)
        specs.append(pl.BlockSpec(memory_space=pl.ANY))
    names += list(outs) + list(scratch) + ["sems"]

    def body(*refs):
        r = types.SimpleNamespace(**dict(zip(names, refs)))

        def run():
            if isinstance(plan, int):
                r.micro = plan
                kernel(r)
            else:
                kernel(r, plan)

        if side is None:
            run()
        else:
            pl.when(r.meta[0] == side)(run)

    results = pl.pallas_call(
        body,
        out_shape=[jax.ShapeDtypeStruct(*shape) for shape in outs.values()],
        in_specs=specs,
        out_specs=[pl.BlockSpec(memory_space=pl.ANY)] * len(outs),
        scratch_shapes=[pltpu.VMEM(*shape) for shape in scratch.values()]
        + [pltpu.SemaphoreType.DMA((copies,))],
        input_output_aliases=aliases,
        compiler_params=pltpu.CompilerParams(vmem_limit_bytes=58 * 1024 * 1024),
        cost_estimate=pl.CostEstimate(flops=1 << 28, bytes_accessed=1 << 20, transcendentals=0),
    )(*arrays)
    return types.SimpleNamespace(**dict(zip(outs, results)))


def attention_scratch(length, width):
    pairs, q_tiles, k_tiles = width // LANES, length // TILE, 2 * length // TILE
    return dict(
        q=((length, width), bf16),
        kv=((2 * length, 2 * width), bf16),
        qm=((pairs, q_tiles, 2 * TILE, LANES), bf16),
        kdc=((2 * length, LANES), f32),
        bias=((TILE, TILE), f32),
        lse=((q_tiles, 8, 2 * TILE), f32),
        att=((length, width), bf16),
        turned=((width, TILE), f32),
    )


def forward_scratch(length, width):
    k_tiles = 2 * length // TILE
    return dict(
        vt=((k_tiles, width, TILE), bf16),
        top=((8, 2 * TILE), f32),
        total=((8, 2 * TILE), f32),
    )


def backward_scratch(length, width):
    pairs, q_tiles, k_tiles = width // LANES, length // TILE, 2 * length // TILE
    return dict(
        kt=((k_tiles, width, TILE), bf16),
        gm=((pairs, q_tiles, 2 * TILE, LANES), bf16),
        delta=((q_tiles, 8, 2 * TILE), f32),
        dkv=((2 * length, 2 * width), f32),
        dq=((length, width), f32),
        dkv_low=((2 * length, 2 * width), bf16),
        part_other=((length, width), bf16),
        dq_low=((length, width), bf16),
    )


def for_sending(shard):

    def short(part):
        return part.astype(jnp.bfloat16) if part.dtype == jnp.float32 else part

    return jax.tree.map(short, shard)


def from_behind(block, axis, distance):
    devices = range(lax.axis_size(axis))
    route = [(i - distance, i) for i in devices if i - distance in devices]
    return lax.ppermute(block, axis, route)


def from_root(shard, axis, root):
    mine = lax.axis_index(axis) == root
    return lax.psum(jnp.where(mine, shard, jnp.zeros_like(shard)), axis)


def matmul(left_side, right_side):
    return jnp.einsum("rsd,de->rse", left_side, right_side, preferred_element_type=jnp.float32)


def matmul_back(left_side, right_side):
    return jnp.einsum("rse,de->rsd", left_side, right_side, preferred_element_type=jnp.float32)


def contract(left_side, right_side):
    return jnp.einsum("rsd,rse->de", left_side, right_side, preferred_element_type=jnp.float32)


def normalize(values, gain_row):
    center = values - jnp.mean(values, axis=-1, keepdims=True)
    inverse = lax.rsqrt(jnp.mean(center * center, axis=-1, keepdims=True) + epsilon)
    standard = center * inverse
    return (standard * gain_row, standard, inverse)


def normalize_back(grad_out, standard, gain_row, inverse):
    scaled = grad_out * gain_row
    grad_in = inverse * (
        scaled
        - jnp.mean(scaled, axis=-1, keepdims=True)
        - standard * jnp.mean(scaled * standard, axis=-1, keepdims=True)
    )
    return (grad_in, jnp.sum(grad_out * standard, axis=(0, 1)))


def allowed_mask(query_docs, key_docs, query_place, key_place, causal):
    same_doc = query_docs[:, :, None] == key_docs[:, None, :]
    earlier = query_place[:, None] >= key_place[None, :]
    return (same_doc & (earlier | jnp.logical_not(causal)))[:, None]


def attend(queries, keys_local, values_local, query_docs, key_docs, causal, is_cross):
    rows_here, shard_len, model_width = queries.shape
    head_dim = model_width // HEADS
    score_scale = head_dim ** (-0.5)
    query_place = lax.axis_index("seq") * shard_len + jnp.arange(shard_len)
    query_heads = queries.reshape(rows_here, shard_len, HEADS, head_dim)

    def absorb(state_tuple, pieces):
        running_top, running_total, running_sum = state_tuple
        key_piece, value_piece, doc_piece = pieces
        piece_len = key_piece.shape[1]
        raw_scores = jnp.einsum(
            "rqhd,rkhd->rhqk",
            query_heads,
            key_piece.reshape(rows_here, piece_len, HEADS, head_dim),
            preferred_element_type=jnp.float32,
        )
        allowed = allowed_mask(query_docs, doc_piece, query_place, jnp.arange(piece_len), causal)
        scores = jnp.where(allowed, raw_scores * score_scale, negative_big)
        new_top = jnp.maximum(running_top, jnp.max(scores, axis=-1))
        weights = jnp.where(allowed, jnp.exp(scores - new_top[..., None]), 0.0)
        new_total = jnp.sum(weights, axis=-1)
        product = jnp.einsum(
            "rhqk,rkhd->rhqd",
            weights.astype(jnp.bfloat16),
            value_piece.reshape(rows_here, piece_len, HEADS, head_dim),
            preferred_element_type=jnp.float32,
        )
        return (new_top, new_total, product)

    init_state = (
        jnp.full((rows_here, HEADS, shard_len), negative_big, jnp.float32),
        jnp.zeros((rows_here, HEADS, shard_len), jnp.float32),
        jnp.zeros((rows_here, HEADS, shard_len, head_dim), jnp.float32),
    )
    if is_cross:
        final_top, final_total, final_sum = absorb(
            init_state,
            (
                lax.all_gather(keys_local, "seq", axis=1, tiled=True),
                lax.all_gather(values_local, "seq", axis=1, tiled=True),
                lax.all_gather(for_sending(key_docs), "seq", axis=1, tiled=True),
            ),
        )
    else:
        final_top, final_total, final_sum = absorb(
            init_state,
            (
                lax.all_gather(keys_local, "seq", axis=1, tiled=True),
                lax.all_gather(values_local, "seq", axis=1, tiled=True),
                lax.all_gather(key_docs, "seq", axis=1, tiled=True),
            ),
        )
    attended = (
        (final_sum / final_total[..., None])
        .transpose(0, 2, 1, 3)
        .reshape(rows_here, shard_len, model_width)
    )
    return (attended, final_top + jnp.log(final_total))


def attend_back(
    queries,
    keys_local,
    values_local,
    query_docs,
    key_docs,
    causal,
    log_total,
    grad_attended,
    is_cross,
):
    rows_here, shard_len, model_width = queries.shape
    head_dim = model_width // HEADS
    score_scale = head_dim ** (-0.5)
    query_place = lax.axis_index("seq") * shard_len + jnp.arange(shard_len)
    if is_cross:
        keys_full, values_full, docs_full = (
            lax.all_gather(keys_local, "seq", axis=1, tiled=True),
            lax.all_gather(values_local, "seq", axis=1, tiled=True),
            lax.all_gather(for_sending(key_docs), "seq", axis=1, tiled=True).astype(key_docs.dtype),
        )
    else:
        keys_full, values_full, docs_full = (
            lax.all_gather(keys_local, "seq", axis=1, tiled=True),
            lax.all_gather(values_local, "seq", axis=1, tiled=True),
            lax.all_gather(key_docs, "seq", axis=1, tiled=True),
        )
    full_len = keys_full.shape[1]
    query_heads = queries.reshape(rows_here, shard_len, HEADS, head_dim)
    key_heads = keys_full.reshape(rows_here, full_len, HEADS, head_dim)
    value_heads = values_full.reshape(rows_here, full_len, HEADS, head_dim)
    grad_heads = grad_attended.reshape(rows_here, shard_len, HEADS, head_dim)
    raw_scores = jnp.einsum(
        "rqhd,rkhd->rhqk", query_heads, key_heads, preferred_element_type=jnp.float32
    )
    allowed = allowed_mask(query_docs, docs_full, query_place, jnp.arange(full_len), causal)
    shifted = jnp.where(allowed, raw_scores * score_scale - log_total[..., None], negative_big)
    probs = jnp.where(allowed, jnp.exp(shifted), 0.0)
    grad_probs = jnp.einsum(
        "rqhd,rkhd->rhqk", grad_heads, value_heads, preferred_element_type=jnp.float32
    )
    delta = jnp.sum(probs * grad_probs, axis=-1)
    grad_scores = (probs * (grad_probs - delta[..., None]) * score_scale).astype(jnp.bfloat16)
    grad_queries = jnp.einsum(
        "rhqk,rkhd->rqhd", grad_scores, key_heads, preferred_element_type=jnp.float32
    ).reshape(rows_here, shard_len, model_width)
    probs_low = probs.astype(jnp.bfloat16)

    def key_terms(span):
        grad_keys = jnp.einsum(
            "rhqk,rqhd->krhd", grad_scores, query_heads, preferred_element_type=jnp.float32
        )
        grad_values = jnp.einsum(
            "rhqk,rqhd->krhd", probs_low, grad_heads, preferred_element_type=jnp.float32
        )
        return jnp.concatenate(
            [
                grad_keys.reshape(span, rows_here, model_width),
                grad_values.reshape(span, rows_here, model_width),
            ],
            axis=-1,
        )

    if is_cross:
        pair_terms = lax.psum_scatter(
            key_terms(shard_len * lax.axis_size("seq")).astype(jnp.bfloat16),
            "seq",
            scatter_dimension=0,
            tiled=True,
        ).astype(jnp.float32)
    else:
        pair_terms = lax.psum_scatter(
            key_terms(shard_len * lax.axis_size("seq")).astype(jnp.bfloat16),
            "seq",
            scatter_dimension=0,
            tiled=True,
        ).astype(jnp.float32)
    return (grad_queries, pair_terms.transpose(1, 0, 2))


def layer_forward(hidden_in, doc_own, memory, memory_docs, weights, is_decoder):
    (
        qkv_weight,
        out_weight,
        in_weight,
        down_weight,
        gains_pair,
        query_weight,
        pair_weight,
        cross_weight,
        cross_gains,
    ) = weights
    model_width = hidden_in.shape[-1]
    mixed = matmul(hidden_in, qkv_weight).astype(jnp.bfloat16)
    attended, self_lse = attend(
        mixed[..., :model_width],
        mixed[..., model_width : 2 * model_width],
        mixed[..., 2 * model_width :],
        doc_own,
        doc_own,
        is_decoder,
        False,
    )
    attended = attended.astype(jnp.bfloat16)
    first, first_unit, first_inv = normalize(
        hidden_in.astype(jnp.float32) + matmul(attended, out_weight), gains_pair[0]
    )
    first_low = first.astype(jnp.bfloat16)
    cross_queries = matmul(first_low, query_weight).astype(jnp.bfloat16)
    pair = matmul(memory, pair_weight).astype(jnp.bfloat16)
    cross_att, cross_lse = attend(
        cross_queries,
        pair[..., :model_width],
        pair[..., model_width:],
        doc_own,
        memory_docs,
        False,
        True,
    )
    cross_att = cross_att.astype(jnp.bfloat16)
    second_cross, second_unit, second_inv = normalize(
        first + matmul(cross_att, cross_weight), cross_gains
    )
    second = jnp.where(is_decoder, second_cross, first)
    second_low = second.astype(jnp.bfloat16)
    upward = matmul(second_low, in_weight)
    active = jax.nn.silu(upward).astype(jnp.bfloat16)
    result, third_unit, third_inv = normalize(second + matmul(active, down_weight), gains_pair[1])
    saved = {
        "mixed": mixed,
        "attended": attended,
        "self_lse": self_lse,
        "first_unit": first_unit,
        "first_inv": first_inv,
        "first_low": first_low,
        "cross_queries": cross_queries,
        "pair": pair,
        "cross_att": cross_att,
        "cross_lse": cross_lse,
        "second_unit": second_unit,
        "second_inv": second_inv,
        "second_low": second_low,
        "upward": upward,
        "active": active,
        "third_unit": third_unit,
        "third_inv": third_inv,
    }
    return (result, saved)


def layer_backward(
    grad_result, saved, hidden_in, doc_own, memory, memory_docs, weights, is_decoder
):
    (
        qkv_weight,
        out_weight,
        in_weight,
        down_weight,
        gains_pair,
        query_weight,
        pair_weight,
        cross_weight,
        cross_gains,
    ) = weights
    model_width = hidden_in.shape[-1]
    grad_third, grad_gain_late = normalize_back(
        grad_result, saved["third_unit"], gains_pair[1], saved["third_inv"]
    )
    down_grad = grad_third.astype(jnp.bfloat16)
    grad_down_w = contract(saved["active"], down_grad)
    grad_active = matmul_back(down_grad, down_weight).astype(jnp.bfloat16)
    sigmoid_up = jax.nn.sigmoid(saved["upward"])
    grad_upward = (
        grad_active.astype(jnp.float32)
        * (sigmoid_up + saved["upward"] * sigmoid_up * (1.0 - sigmoid_up))
    ).astype(jnp.bfloat16)
    grad_in_w = contract(saved["second_low"], grad_upward)
    grad_second = grad_third + matmul_back(grad_upward, in_weight)
    grad_cross_sum, grad_cross_gain = normalize_back(
        grad_second, saved["second_unit"], cross_gains, saved["second_inv"]
    )
    decoder_flag = is_decoder.astype(jnp.float32)
    grad_cross_sum = grad_cross_sum * decoder_flag
    grad_cross_gain = grad_cross_gain * decoder_flag
    cross_branch = grad_cross_sum.astype(jnp.bfloat16)
    grad_cross_w = contract(saved["cross_att"], cross_branch)
    grad_cross_att = matmul_back(cross_branch, cross_weight).astype(jnp.bfloat16)
    pair = saved["pair"]
    grad_cross_q, grad_pair = attend_back(
        saved["cross_queries"],
        pair[..., :model_width],
        pair[..., model_width:],
        doc_own,
        memory_docs,
        False,
        saved["cross_lse"],
        grad_cross_att,
        True,
    )
    grad_cross_q = grad_cross_q.astype(jnp.bfloat16)
    grad_pair = grad_pair.astype(jnp.bfloat16)
    grad_query_w = contract(saved["first_low"], grad_cross_q)
    grad_pair_w = contract(memory, grad_pair)
    grad_memory = matmul_back(grad_pair, pair_weight)
    grad_first = jnp.where(
        is_decoder, grad_cross_sum + matmul_back(grad_cross_q, query_weight), grad_second
    )
    grad_first_sum, grad_gain_early = normalize_back(
        grad_first, saved["first_unit"], gains_pair[0], saved["first_inv"]
    )
    self_branch = grad_first_sum.astype(jnp.bfloat16)
    grad_out_w = contract(saved["attended"], self_branch)
    grad_attended = matmul_back(self_branch, out_weight).astype(jnp.bfloat16)
    mixed = saved["mixed"]
    grad_queries, grad_pair_self = attend_back(
        mixed[..., :model_width],
        mixed[..., model_width : 2 * model_width],
        mixed[..., 2 * model_width :],
        doc_own,
        doc_own,
        is_decoder,
        saved["self_lse"],
        grad_attended,
        False,
    )
    grad_mixed = jnp.concatenate([grad_queries, grad_pair_self], axis=-1).astype(jnp.bfloat16)
    grad_qkv_w = contract(hidden_in, grad_mixed)
    grad_hidden = grad_first_sum + matmul_back(grad_mixed, qkv_weight)
    layer_grads = (
        grad_qkv_w,
        grad_out_w,
        grad_in_w,
        grad_down_w,
        jnp.stack([grad_gain_early, grad_gain_late]),
        grad_query_w,
        grad_pair_w,
        grad_cross_w,
        grad_cross_gain,
    )
    return (grad_hidden, grad_memory, layer_grads)


def any_rows(
    layer_input,
    segment_ids,
    attn_qkv,
    attn_out,
    ffn_in,
    ffn_out,
    norm_gain,
    cross_query,
    cross_pair,
    cross_out,
    cross_gain,
    out_cotangent,
):
    micro_count = layer_input.shape[1]
    section_index = lax.axis_index("section")
    is_decoder = section_index == 1
    weights = (
        attn_qkv[0],
        attn_out[0],
        ffn_in[0],
        ffn_out[0],
        norm_gain[0],
        cross_query,
        cross_pair,
        cross_out,
        cross_gain,
    )
    inputs_all = layer_input[0]
    docs_all = segment_ids[0]
    slot_ids = jnp.arange(micro_count)
    received = (jnp.zeros_like(inputs_all[0]), jnp.zeros_like(docs_all[0]))
    results = jnp.zeros_like(inputs_all)
    memories = []
    memory_doc_list = []
    for step_index in range(micro_count + 1):
        batch_index = step_index - section_index
        is_valid = (batch_index >= 0) & (batch_index < micro_count)
        chosen = jnp.clip(batch_index, 0, micro_count - 1)
        hidden_in = lax.dynamic_index_in_dim(inputs_all, chosen, 0, keepdims=False)
        doc_own = lax.dynamic_index_in_dim(docs_all, chosen, 0, keepdims=False)
        memory = received[0]
        memory_docs = jnp.where(is_valid & is_decoder, received[1], doc_own)
        memories.append(memory)
        memory_doc_list.append(memory_docs)
        result, saved = layer_forward(hidden_in, doc_own, memory, memory_docs, weights, is_decoder)
        low_result = result.astype(jnp.bfloat16)
        writing = (slot_ids == chosen) & is_valid
        results = jnp.where(writing[:, None, None, None], low_result[None], results)
        if step_index < micro_count:
            received = from_behind((low_result, doc_own), "section", 1)
    memory_stack = jnp.stack(memories)
    memory_doc_stack = jnp.stack(memory_doc_list)
    totals = tuple((jnp.zeros(weight.shape, jnp.float32) for weight in weights))
    input_grads = jnp.zeros(inputs_all.shape, jnp.float32)
    returned = jnp.zeros(inputs_all.shape[1:], jnp.float32)
    for step_index in range(micro_count + 1):
        batch_index = micro_count - step_index - section_index
        is_valid = (batch_index >= 0) & (batch_index < micro_count)
        chosen = jnp.clip(batch_index, 0, micro_count - 1)
        forward_step = jnp.clip(batch_index + section_index, 0, micro_count)
        hidden_in = lax.dynamic_index_in_dim(inputs_all, chosen, 0, keepdims=False)
        doc_own = lax.dynamic_index_in_dim(docs_all, chosen, 0, keepdims=False)
        memory = lax.dynamic_index_in_dim(memory_stack, forward_step, 0, keepdims=False)
        memory_docs = lax.dynamic_index_in_dim(memory_doc_stack, forward_step, 0, keepdims=False)
        discarded, saved = layer_forward(
            hidden_in, doc_own, memory, memory_docs, weights, is_decoder
        )
        cotangent = jnp.where(
            is_decoder,
            lax.dynamic_index_in_dim(out_cotangent, chosen, 0, keepdims=False).astype(jnp.float32),
            returned,
        )
        grad_hidden, grad_memory, layer_grads = layer_backward(
            cotangent, saved, hidden_in, doc_own, memory, memory_docs, weights, is_decoder
        )
        valid_flag = is_valid.astype(jnp.float32)
        totals = tuple(
            (running + valid_flag * fresh for running, fresh in zip(totals, layer_grads))
        )
        writing = (slot_ids == chosen) & is_valid
        input_grads = jnp.where(writing[:, None, None, None], grad_hidden[None], input_grads)
        if step_index < micro_count:
            returned = from_behind(grad_memory.astype(jnp.bfloat16), "section", -1).astype(
                grad_memory.dtype
            )
    group_sums = lax.psum(
        (
            totals[0],
            totals[1],
            totals[2],
            totals[3],
            totals[4],
            totals[5],
            totals[6],
            totals[7],
            totals[8],
        ),
        ("seq", "dp"),
    )
    section_sums = group_sums[:5]
    cross_sums = (
        from_root(group_sums[5].astype(jnp.bfloat16), "section", 1).astype(jnp.float32),
        from_root(group_sums[6].astype(jnp.bfloat16), "section", 1).astype(jnp.float32),
        from_root(group_sums[7].astype(jnp.bfloat16), "section", 1).astype(jnp.float32),
        from_root(group_sums[8].astype(jnp.bfloat16), "section", 1).astype(jnp.float32),
    )
    return (
        results[None],
        input_grads[None],
        section_sums[0][None],
        section_sums[1][None],
        section_sums[2][None],
        section_sums[3][None],
        section_sums[4][None],
        cross_sums[0],
        cross_sums[1],
        cross_sums[2],
        cross_sums[3],
    )


def split_rows(
    layer_input,
    segment_ids,
    attn_qkv,
    attn_out,
    ffn_in,
    ffn_out,
    norm_gain,
    cross_query,
    cross_pair,
    cross_out,
    cross_gain,
    out_cotangent,
):
    micros = layer_input.shape[1]
    length, width = layer_input.shape[3:]
    hidden = ffn_in.shape[-1]
    q_tiles = length // TILE
    group = lax.axis_size("dp") // 2
    axes = ("section", "seq", "dp")
    decoder = lax.axis_index("section") == 1
    flag = decoder.astype(jnp.int32)
    x = lax.axis_index("seq")
    core = lax.rem(lax.axis_index("dp"), 2)
    z = lax.axis_index("dp") // 2
    places = [(t, i, k, c) for t in range(2) for i in range(2) for k in range(group) for c in range(2)]

    def number(t, i, k, c):
        return ((t * 2 + i) * group + k) * 2 + c

    def send(values, target, section=None):
        route = [
            (number(*place), number(*target(*place)))
            for place in places
            if section in (None, place[0]) and target(*place)
        ]
        return lax.ppermute(values, axes, route)

    def to_core(t, i, k, c):
        return (t, i, k, 1 - c)

    def to_x(t, i, k, c):
        return (t, 1 - i, k, c)

    def to_row(t, i, k, c):
        return (t, c, k, i)

    def to_decoder(t, i, k, c):
        return (1, i, k, c) if t == 0 else None

    def to_encoder(t, i, k, c):
        return (0, i, k, c) if t == 1 else None

    def exchange(values):
        return send(values, to_core)

    low = ((length, width), bf16)
    wide = ((length, width), f32)
    both = ((2 * length, width), bf16)
    keys_all = ((2 * length, 2 * width), bf16)
    mixing = ((width, 3 * width), bf16)
    inner = ((length, hidden), bf16)
    lse = ((q_tiles, 8, 2 * TILE), f32)
    stat = ((length, LANES), f32)
    square = ((width, width), bf16)
    rising = ((width, hidden), bf16)
    falling = ((hidden, width), bf16)
    gain_rows = ((8, width), f32)

    def halves(ref, section_rows):
        return ref.at[pl.ds(0, section_rows)], ref.at[pl.ds(section_rows, section_rows)]

    meta = jnp.stack([flag, core, x, z]).astype(jnp.int32)
    documents = segment_ids[0, :, 0]
    own = [send(layer_input[0, micro, 0], to_row) for micro in range(micros)]
    docs_own = send(documents, to_row)
    docs_row = jnp.concatenate([docs_own, exchange(docs_own)], axis=1)
    docs_source = send(docs_row, to_decoder)
    other = [exchange(part) for part in own]

    def places_of(keys):
        return (
            dict(meta=meta, qd_s=docs_own, kd_s=keys),
            dict(
                qd=docs_own.astype(f32).reshape(micros, q_tiles, 1, TILE),
                kd=keys.astype(f32).reshape(micros, 1, 2 * length),
                gains=norm_gain[0],
            ),
        )

    plain = dict(meta=meta)
    scalars, small = places_of(docs_row)
    forward, memories, memories_other = [], [], []
    for micro in range(micros):
        call = launch(
            self_forward,
            micro,
            None,
            scalars,
            small,
            dict(
                x_own_h=own[micro],
                x_other_h=other[micro],
                w_mixed_h=attn_qkv[0],
                w_out_h=attn_out[0],
                w_in_h=ffn_in[0],
                w_down_h=ffn_out[0],
            ),
            dict(
                q_o=low,
                kv_o=keys_all,
                att_o=low,
                lse_o=lse,
                unit1_o=wide,
                inv1_o=stat,
                first_low_o=low,
                memory_o=low,
                ffn_low_o=low,
                act_o=inner,
                slope_o=inner,
                unit2_o=wide,
                inv2_o=stat,
            ),
            dict(
                **attention_scratch(length, width),
                **forward_scratch(length, width),
                x=both,
                w_mixed=mixing,
                w_out=square,
                w_in=rising,
                w_down=falling,
                unit1=wide,
                inv1=stat,
                first_low=low,
                memory=low,
                act=inner,
                slope=inner,
                unit2=wide,
                inv2=stat,
                sum=wide,
            ),
            24,
            after=(docs_source,) if micro == 0 else (forward[0].lse_o,),
        )
        forward.append(call)
        memories.append(send(call.memory_o, to_decoder))
        memories_other.append(exchange(memories[micro]))

    cotangent, _ = lax.optimization_barrier((out_cotangent[:, 0], forward[0].lse_o))
    cotangent = send(cotangent, to_row)

    cross_scalars, cross_small = places_of(docs_source)
    cross, grads_memory, made = [], [], []
    after = (forward[-1].lse_o,)
    for micro in range(micros):
        done = forward[micro]
        call = launch(
            cross_both_ways,
            micro,
            1,
            cross_scalars,
            dict(**cross_small, cross_gain=cross_gain[None]),
            dict(
                memory_own_h=memories[micro],
                memory_other_h=memories_other[micro],
                w_pair_h=cross_pair,
                first_low_h=done.first_low_o,
                unit1_h=done.unit1_o,
                w_query_h=cross_query,
                w_cross_h=cross_out,
                w_in_h=ffn_in[0],
                w_down_h=ffn_out[0],
                cot_h=cotangent,
            ),
            dict(
                att_o=low,
                ffn_low_o=low,
                act_o=inner,
                decoded_o=low,
                down_grad_o=low,
                up_grad_o=inner,
                gain_grads_o=gain_rows,
                branch_o=low,
                dq_low_o=low,
                dkv_o=keys_all,
                part_own_o=wide,
                part_other_o=low,
                grad_first_o=wide,
            ),
            dict(
                **attention_scratch(length, width),
                **forward_scratch(length, width),
                **backward_scratch(length, width),
                x=both,
                w_pair=((width, 2 * width), bf16),
                first_low=low,
                unit1=wide,
                w_query=square,
                w_cross=square,
                w_in=rising,
                w_down=falling,
                cot=low,
                unit2=wide,
                inv2=stat,
                second_low=low,
                act=inner,
                slope=inner,
                sum=wide,
                decoded=low,
                keep=wide,
                down_grad=low,
                up_grad=inner,
                gain_grads=gain_rows,
                branch=low,
                part_own=wide,
            ),
            32,
            dict(act_o=done.act_o, ffn_low_o=done.ffn_low_o),
            after,
        )
        cross.append(call)
        total = call.part_own_o + exchange(call.part_other_o).astype(f32)
        made.append(total.astype(bf16))
        after = (made[micro],)
        grads_memory.append(send(made[micro], to_encoder))

    def backward_feed(micro, after):
        done, late = forward[micro], cross[micro]
        return launch(
            feed_backward_alone,
            micro,
            0,
            plain,
            dict(gains=norm_gain[0]),
            dict(
                grad_memory_h=grads_memory[micro],
                unit2_h=done.unit2_o,
                inv2_h=done.inv2_o,
                slope_h=done.slope_o,
                w_in_h=ffn_in[0],
                w_down_h=ffn_out[0],
            ),
            dict(gain_late_o=gain_rows, down_grad_o=low, up_grad_o=inner, grad_first_o=wide),
            dict(
                cot=low,
                unit2=wide,
                inv2=stat,
                slope=inner,
                w_in=rising,
                w_down=falling,
                gain_grads=gain_rows,
                keep=wide,
                down_grad=low,
                up_grad=inner,
                sum=wide,
            ),
            12,
            dict(
                down_grad_o=late.down_grad_o, up_grad_o=late.up_grad_o, grad_first_o=late.grad_first_o
            ),
            after,
        )

    def backward_self(micro, side, grad_first, previous, after):
        done = forward[micro]
        return launch(
            self_backward,
            micro,
            side,
            scalars,
            small,
            dict(
                q_h=done.q_o,
                kv_h=done.kv_o,
                w_out_h=attn_out[0],
                w_mixed_h=attn_qkv[0],
                att_h=done.att_o,
                lse_h=done.lse_o,
                unit1_h=done.unit1_o,
                inv1_h=done.inv1_o,
                grad_first_h=grad_first,
            ),
            dict(
                gain_early_o=gain_rows,
                branch_o=low,
                dq_low_o=low,
                dkv_o=keys_all,
                part_own_o=wide,
                part_other_o=low,
            ),
            dict(
                **attention_scratch(length, width),
                **backward_scratch(length, width),
                w_out=square,
                w_mixed=mixing,
                unit1=wide,
                inv1=stat,
                keep=wide,
                branch=low,
                grad_att=low,
                gain_grads=gain_rows,
            ),
            20,
            previous,
            after,
        )

    def weight_grads(plan, side, arrays, scratch, after=()):
        blocks = ((2, width, width), bf16)
        call = launch(
            contract_blocks,
            plan,
            side,
            plain,
            dict(),
            arrays,
            dict(sent_o=blocks, kept_o=blocks),
            dict(**scratch, blocks=((4, width, width), bf16)),
            24,
            after=after,
        )
        return call.sent_o, call.kept_o

    def first_sums(halves, section=None):
        sent, kept = halves
        got = send(sent, to_core, section)

        def block(side):
            return sum(
                lax.dynamic_index_in_dim(part, side, 0, keepdims=False).astype(f32)
                for part in (kept, got)
            )

        return block(1 - x).astype(bf16), block(x)

    def last_sums(sums, section=None):
        away, total = sums
        total = (total + send(away, to_x, section).astype(f32)).astype(bf16)
        shares = total.reshape(group, width // group, width)

        def share(step):
            return lax.dynamic_index_in_dim(shares, lax.rem(z + step, group), 0, keepdims=False)

        parts = [share(0)]
        for step in range(1, group):
            parts.append(send(share(step), along_z(step), section))
        return sum(part.astype(f32) for part in parts).astype(bf16)

    def along_z(step):
        return lambda t, i, k, c: (t, i, (k + step) % group, c)

    def gather(share, section=None):
        own = jnp.stack(
            [share] + [send(share, along_z(step), section) for step in range(1, group)]
        )
        return own, send(own, to_x, section)

    def gain_block(rows):
        filled = jnp.concatenate([jnp.stack(rows), jnp.zeros((16 - len(rows), width), f32)])
        return filled.astype(bf16)

    def spread(targets, own, own_x, outs, parts):
        return launch(
            spread_pieces,
            targets,
            None,
            plain,
            dict(),
            dict(own_h=own, own_x_h=own_x, other_h=exchange(own), other_x_h=exchange(own_x)),
            outs,
            dict(
                pieces=((4,) + own.shape, bf16),
                wide=((4 * group * parts, width // group, width), f32),
                gain_grads=((16, width), f32),
            ),
            8 + 4 * group * parts,
        )

    tokens, all_tokens = micros * length, 2 * micros * length
    turn, turn_all = ((width, tokens), bf16), ((width, all_tokens), bf16)
    narrow, narrow_all = ((tokens, width), bf16), ((all_tokens, width), bf16)
    pair_all = ((all_tokens, 2 * width), bf16)
    deep = ((tokens, hidden), bf16)

    def rows_of(first, second):
        starts = [halves(first, length), halves(second, length)]
        return [part[0] for part in starts] + [part[1] for part in starts]

    def cross_plan(r):
        return (
            [
                (r.low, (r.low0_h, r.low1_h)),
                (r.dq, (r.dq0_h, r.dq1_h)),
                (r.att, (r.att0_h, r.att1_h)),
                (r.branch, (r.branch0_h, r.branch1_h)),
                (r.mem, (r.mem0_h, r.mem1_h, r.mem2_h, r.mem3_h)),
                (r.pair, rows_of(r.pair0_h, r.pair1_h)),
            ],
            [
                (r.turn, r.low, 0, r.dq, 0),
                (r.turn_att, r.att, 0, r.branch, 0),
                (r.turn_all, r.mem, 0, r.pair, 0),
                (r.turn_all, r.mem, 0, r.pair, 1),
            ],
        )

    def rising_plan(r):
        return (
            [(r.low, (r.low0_h, r.low1_h)), (r.up, (r.up0_h, r.up1_h))],
            [(r.turn, r.low, 0, r.up, block) for block in range(4)],
        )

    def falling_plan(r):
        return (
            [(r.act, (r.act0_h, r.act1_h)), (r.down, (r.down0_h, r.down1_h))],
            [(r.turn, r.act, block, r.down, 0) for block in range(4)],
        )

    def self_plan(r):
        return (
            [
                (r.x, (r.x0_h, r.x1_h, r.x2_h, r.x3_h)),
                (r.dq, (r.dq0_h, r.dq1_h)),
                (r.pair, rows_of(r.pair0_h, r.pair1_h)),
                (r.att, (r.att0_h, r.att1_h)),
                (r.branch, (r.branch0_h, r.branch1_h)),
            ],
            [
                (r.turn_all, r.x, 0, r.dq, 0),
                (r.turn_all, r.x, 0, r.pair, 0),
                (r.turn_all, r.x, 0, r.pair, 1),
                (r.turn, r.att, 0, r.branch, 0),
            ],
        )

    last = micros - 1
    feeds, ends = [None] * micros, [None] * micros
    cross_halves = weight_grads(
        cross_plan,
        1,
        dict(
            low0_h=forward[0].first_low_o,
            low1_h=forward[1].first_low_o,
            dq0_h=cross[0].dq_low_o,
            dq1_h=cross[1].dq_low_o,
            att0_h=cross[0].att_o,
            att1_h=cross[1].att_o,
            branch0_h=cross[0].branch_o,
            branch1_h=cross[1].branch_o,
            mem0_h=memories[0],
            mem1_h=memories[1],
            mem2_h=memories_other[0],
            mem3_h=memories_other[1],
            pair0_h=cross[0].dkv_o,
            pair1_h=cross[1].dkv_o,
        ),
        dict(
            low=narrow,
            dq=narrow,
            att=narrow,
            branch=narrow,
            mem=narrow_all,
            pair=pair_all,
            turn=turn,
            turn_att=turn,
            turn_all=turn_all,
        ),
        (made[last],),
    )
    cross_sums = first_sums(cross_halves, 1)
    latest = made[last]
    for micro in range(last):
        feeds[micro] = backward_feed(micro, (latest,))
        first = feeds[micro].grad_first_o
        ends[micro] = backward_self(micro, 0, first, None, ())
        ends[micro] = backward_self(micro, 1, first, vars(ends[micro]), (cross_sums[0],))
        latest = ends[micro].gain_early_o
    cross_share = last_sums(cross_sums, 1)
    feeds[last] = backward_feed(last, (latest,))

    rising_halves = weight_grads(
        rising_plan,
        None,
        dict(
            low0_h=cross[0].ffn_low_o,
            low1_h=cross[1].ffn_low_o,
            up0_h=feeds[0].up_grad_o,
            up1_h=feeds[1].up_grad_o,
        ),
        dict(low=narrow, up=deep, turn=turn),
    )
    falling_halves = weight_grads(
        falling_plan,
        None,
        dict(
            act0_h=cross[0].act_o,
            act1_h=cross[1].act_o,
            down0_h=feeds[0].down_grad_o,
            down1_h=feeds[1].down_grad_o,
        ),
        dict(act=deep, down=narrow, turn=turn),
        (rising_halves[0],),
    )
    rising_sums, falling_sums = first_sums(rising_halves), first_sums(falling_halves)
    third = sum(call.gain_grads_o[1] for call in cross)
    cross_own, cross_own_x = gather(jnp.concatenate([cross_share, gain_block([third])]), 1)

    def part_sum(micro):
        end = ends[micro]
        return (end.part_own_o + exchange(end.part_other_o).astype(f32)).astype(bf16)

    steps = [part_sum(micro) for micro in range(last)]
    ends[last] = backward_self(
        last,
        None,
        feeds[last].grad_first_o,
        None,
        (rising_sums[0], falling_sums[0]) + tuple(steps),
    )
    rising_share, falling_share = last_sums(rising_sums), last_sums(falling_sums)

    self_halves = weight_grads(
        self_plan,
        None,
        dict(
            x0_h=own[0],
            x1_h=own[1],
            x2_h=other[0],
            x3_h=other[1],
            dq0_h=ends[0].dq_low_o,
            dq1_h=ends[1].dq_low_o,
            pair0_h=ends[0].dkv_o,
            pair1_h=ends[1].dkv_o,
            att0_h=forward[0].att_o,
            att1_h=forward[1].att_o,
            branch0_h=ends[0].branch_o,
            branch1_h=ends[1].branch_o,
        ),
        dict(
            x=narrow_all,
            dq=narrow,
            pair=pair_all,
            att=narrow,
            branch=narrow,
            turn=turn,
            turn_all=turn_all,
        ),
    )
    self_share = last_sums(first_sums(self_halves))
    steps.append(part_sum(last))

    feed_own, feed_own_x = gather(jnp.concatenate([rising_share, falling_share]))
    early = sum(end.gain_early_o[0] for end in ends)
    late = jnp.where(
        decoder,
        sum(call.gain_grads_o[0] for call in cross),
        sum(call.gain_late_o[0] for call in feeds),
    )
    self_own, self_own_x = gather(jnp.concatenate([self_share, gain_block([early, late])]))
    cross_own, cross_own_x = (
        jnp.where(decoder, part, send(part, to_encoder)) for part in (cross_own, cross_own_x)
    )

    def columns(block):
        return pl.ds(block * width, width)

    def feed_targets(r, block, row, rows):
        return [
            r.up_o.at[pl.ds(row, rows), columns(block)],
            r.down_o.at[pl.ds(block * width + row, rows)],
        ]

    def self_targets(r, block, row, rows):
        if block == 3:
            return [r.out_o.at[pl.ds(row, rows)]]
        return [r.mixed_o.at[pl.ds(row, rows), columns(block)]]

    def cross_targets(r, block, row, rows):
        if block >= 2:
            return [r.pair_o.at[pl.ds(row, rows), columns(block - 2)]]
        return [(r.out_o if block else r.query_o).at[pl.ds(row, rows)]]

    square_out, gains_out = ((width, width), f32), ((16, width), f32)
    cross_grads = spread(
        cross_targets,
        cross_own,
        cross_own_x,
        dict(query_o=square_out, pair_o=((width, 2 * width), f32), out_o=square_out, gains_o=gains_out),
        1,
    )
    feed_grads = spread(
        feed_targets,
        feed_own,
        feed_own_x,
        dict(up_o=((width, hidden), f32), down_o=((hidden, width), f32)),
        2,
    )
    self_grads = spread(
        self_targets,
        self_own,
        self_own_x,
        dict(mixed_o=((width, 3 * width), f32), out_o=square_out, gains_o=gains_out),
        1,
    )

    results = jnp.stack(
        [
            jnp.where(decoder, call.decoded_o, done.memory_o)
            for call, done in zip(cross, forward)
        ]
    )
    results = send(results, to_row)
    grad_input = jnp.stack([send(step, to_row) for step in steps])
    return (
        results[None, :, None],
        grad_input.astype(f32)[None, :, None],
        self_grads.mixed_o[None],
        self_grads.out_o[None],
        feed_grads.up_o[None],
        feed_grads.down_o[None],
        self_grads.gains_o[None, :2],
        cross_grads.query_o,
        cross_grads.pair_o,
        cross_grads.out_o,
        cross_grads.gains_o[0],
    )


def shards(*arrays):
    layer_input = arrays[0]
    micros, rows, length = layer_input.shape[1:4]
    simple = (
        lax.axis_size("section") == 2
        and lax.axis_size("seq") == 2
        and lax.axis_size("dp") in (4, 8, 16)
        and (micros, rows) == (2, 1)
        and length % TILE == 0
        and arrays[4].shape[-1] == 4 * layer_input.shape[-1] == 4 * CHUNK
    )
    return split_rows(*arrays) if simple else any_rows(*arrays)


def solution(mesh):
    in_specs = (
        P("section", None, "dp", "seq", None),
        P("section", None, "dp", "seq"),
        P("section", None, None),
        P("section", None, None),
        P("section", None, None),
        P("section", None, None),
        P("section", None, None),
        P(),
        P(),
        P(),
        P(),
        P(None, "dp", "seq", None),
    )
    out_specs = (
        P("section", None, "dp", "seq", None),
        P("section", None, "dp", "seq", None),
        P("section", None, None),
        P("section", None, None),
        P("section", None, None),
        P("section", None, None),
        P("section", None, None),
        P(),
        P(),
        P(),
        P(),
    )
    return jax.shard_map(shards, mesh=mesh, in_specs=in_specs, out_specs=out_specs, check_vma=False)
```

```python
import types

import jax
import jax.numpy as jnp
from jax import lax
from jax.experimental import pallas as pl
from jax.experimental.pallas import tpu as pltpu
from jax.sharding import PartitionSpec as P

HEADS = 8
TILE = 256
LANES = 128
CHUNK = 512

f32 = jnp.float32
bf16 = jnp.bfloat16
negative_big = -1e30
epsilon = 1e-05


def dot(left, right):
    return lax.dot_general(left, right, (((1,), (0,)), ((), ())), preferred_element_type=f32)


def dot_nt(left, right):
    return lax.dot_general(left, right, (((1,), (1,)), ((), ())), preferred_element_type=f32)


def dot_tn(left, right):
    return lax.dot_general(left, right, (((0,), (0,)), ((), ())), preferred_element_type=f32)


def standardize(values):
    center = values - jnp.mean(values, axis=-1, keepdims=True)
    inverse = lax.rsqrt(jnp.mean(center * center, axis=-1, keepdims=True) + epsilon)
    return center * inverse, inverse


def standardize_back(grad_out, standard, gain_row, inverse):
    scaled = grad_out * gain_row
    grad_in = inverse * (
        scaled
        - jnp.mean(scaled, axis=-1, keepdims=True)
        - standard * jnp.mean(scaled * standard, axis=-1, keepdims=True)
    )
    return grad_in, jnp.sum(grad_out * standard, axis=0, keepdims=True)


class Copies:
    def __init__(self, sems):
        self.sems = sems
        self.used = 0

    def start(self, source, target):
        copy = pltpu.make_async_copy(source, target, self.sems.at[self.used])
        self.used += 1
        copy.start()
        return copy


def wait_all(copies):
    for copy in copies:
        copy.wait()


def spread_pairs(target, source, factor, pairs):
    tiles = target.shape[1]
    half = lax.broadcasted_iota(jnp.int32, (TILE, LANES), 1) < LANES // 2
    first = jnp.where(half, factor, 0.0).astype(bf16)
    second = jnp.where(half, 0.0, factor).astype(bf16)
    for tile in range(tiles):
        for pair in pairs:
            block = source[tile * TILE : (tile + 1) * TILE, pair * LANES : (pair + 1) * LANES]
            target[pair, tile, :TILE, :] = block * first
            target[pair, tile, TILE:, :] = block * second


def turn_tiles(target, source, column, pairs):
    low, high = pairs[0] * LANES, (pairs[-1] + 1) * LANES
    for tile in range(target.shape[0]):
        block = source[tile * TILE : (tile + 1) * TILE, column + low : column + high]
        target[tile, low:high, :] = jnp.transpose(block)


def turn_documents(target, key_docs):
    for start in range(0, target.shape[0], LANES):
        row = key_docs[:, start : start + LANES]
        target[start : start + LANES, :] = jnp.transpose(jnp.broadcast_to(row, (LANES, LANES)))


def tile_place(r, core, causal, q_tile, k_tile):
    q_tiles = r.qd.shape[1]
    length = q_tiles * TILE
    owner = jnp.where(k_tile < q_tiles, core, 1 - core)
    k_start = owner * length + lax.rem(k_tile, q_tiles) * TILE
    ahead = core * length + q_tile * TILE - k_start
    ahead = jnp.where(causal == 1, ahead, 2 * length * TILE)
    q_low, q_high = r.qd_s[r.micro, q_tile * TILE], r.qd_s[r.micro, q_tile * TILE + TILE - 1]
    k_low, k_high = r.kd_s[r.micro, k_tile * TILE], r.kd_s[r.micro, k_tile * TILE + TILE - 1]
    active = (q_low <= k_high) & (k_low <= q_high) & (ahead > -TILE)
    return active, ahead


def fill_bias(r, q_tile, k_tile, ahead):
    keys = r.kdc[pl.ds(pl.multiple_of(k_tile * TILE, TILE), TILE), :]
    shift = lax.broadcasted_iota(jnp.int32, (TILE, LANES), 0) - lax.broadcasted_iota(
        jnp.int32, (TILE, LANES), 1
    )
    queries = r.qd[r.micro, q_tile]
    for start in range(0, TILE, LANES):
        same = keys == queries[:, start : start + LANES]
        allowed = same & (shift - start <= ahead)
        r.bias[:, start : start + LANES] = jnp.where(allowed, 0.0, negative_big)


def attention_forward(r, core, causal):
    pairs, q_tiles = r.qm.shape[:2]
    k_tiles = r.vt.shape[0]

    def one_query_tile(q_tile, carry):
        r.top[...] = jnp.full(r.top.shape, negative_big, f32)
        r.total[...] = jnp.zeros(r.total.shape, f32)
        r.turned[...] = jnp.zeros(r.turned.shape, f32)

        def one_key_tile(k_tile, inner):
            active, ahead = tile_place(r, core, causal, q_tile, k_tile)

            @pl.when(active)
            def _():
                fill_bias(r, q_tile, k_tile, ahead)
                rows = pl.ds(pl.multiple_of(k_tile * TILE, TILE), TILE)

                def raw(pair):
                    keys = r.kv[rows, pair * LANES : (pair + 1) * LANES]
                    return dot_nt(keys, r.qm[pair, q_tile])

                raw_next = raw(0)
                for pair in range(pairs):
                    bias = r.bias[...]
                    scores = raw_next + jnp.concatenate([bias, bias], axis=1)
                    if pair + 1 < pairs:
                        raw_next = raw(pair + 1)
                    old_top = r.top[pair : pair + 1, :]
                    new_top = jnp.maximum(old_top, jnp.max(scores, axis=0, keepdims=True))
                    weights = jnp.exp(scores - new_top)
                    shrink = jnp.exp(old_top - new_top)
                    r.top[pair : pair + 1, :] = new_top
                    r.total[pair : pair + 1, :] = r.total[
                        pair : pair + 1, :
                    ] * shrink + jnp.sum(weights, axis=0, keepdims=True)
                    low = weights.astype(bf16)
                    for side in range(2):
                        span = slice(side * TILE, (side + 1) * TILE)
                        head = slice((2 * pair + side) * 64, (2 * pair + side + 1) * 64)
                        r.turned[head, :] = r.turned[head, :] * shrink[:, span] + dot(
                            r.vt[k_tile, head, :], low[:, span]
                        )

            return inner

        lax.fori_loop(0, k_tiles, one_key_tile, 0)
        for pair in range(pairs):
            total = r.total[pair : pair + 1, :]
            r.lse[q_tile, pair : pair + 1, :] = r.top[pair : pair + 1, :] + jnp.log(total)
            share = 1.0 / total
            for side in range(2):
                span = slice(side * TILE, (side + 1) * TILE)
                head = slice((2 * pair + side) * 64, (2 * pair + side + 1) * 64)
                r.turned[head, :] = r.turned[head, :] * share[:, span]
        rows = pl.ds(pl.multiple_of(q_tile * TILE, TILE), TILE)
        r.att[rows, :] = jnp.transpose(r.turned[...]).astype(bf16)
        return carry

    lax.fori_loop(0, q_tiles, one_query_tile, 0)


def row_products(r, grad_att, pairs):
    low, high = pairs[0] * LANES, (pairs[-1] + 1) * LANES
    for tile in range(r.qm.shape[1]):
        rows = slice(tile * TILE, (tile + 1) * TILE)
        product = jnp.transpose(
            grad_att[rows, low:high].astype(f32) * r.att[rows, low:high].astype(f32)
        )
        for pair in pairs:
            for side in range(2):
                head = (2 * pair + side) * 64 - low
                r.delta[tile, pair : pair + 1, side * TILE : (side + 1) * TILE] = jnp.sum(
                    product[head : head + 64, :], axis=0, keepdims=True
                )


def attention_backward(r, core, causal, pairs):
    q_tiles, k_tiles = r.qm.shape[1], r.kt.shape[0]
    width = r.kt.shape[1]
    low, high = pairs[0] * LANES, (pairs[-1] + 1) * LANES
    for start in (0, width):
        r.dkv[:, start + low : start + high] = jnp.zeros((r.dkv.shape[0], high - low), f32)

    def one_query_tile(q_tile, carry):
        r.turned[low:high, :] = jnp.zeros((high - low, TILE), f32)

        def one_key_tile(k_tile, inner):
            active, ahead = tile_place(r, core, causal, q_tile, k_tile)

            @pl.when(active)
            def _():
                fill_bias(r, q_tile, k_tile, ahead)
                rows = pl.ds(pl.multiple_of(k_tile * TILE, TILE), TILE)

                def raw(pair):
                    lanes = slice(pair * LANES, (pair + 1) * LANES)
                    lanes_v = slice(width + pair * LANES, width + (pair + 1) * LANES)
                    return (
                        dot_nt(r.kv[rows, lanes], r.qm[pair, q_tile]),
                        dot_nt(r.kv[rows, lanes_v], r.gm[pair, q_tile]),
                    )

                raw_next = raw(pairs[0])
                for pair in pairs:
                    bias = r.bias[...]
                    scores, grad_probs = raw_next
                    scores = scores + jnp.concatenate([bias, bias], axis=1)
                    if pair < pairs[-1]:
                        raw_next = raw(pair + 1)
                    probs = jnp.exp(scores - r.lse[q_tile, pair : pair + 1, :])
                    grad_scores = probs * (grad_probs - r.delta[q_tile, pair : pair + 1, :])
                    probs_low = probs.astype(bf16)
                    grad_low = grad_scores.astype(bf16)
                    lanes = slice(pair * LANES, (pair + 1) * LANES)
                    lanes_v = slice(width + pair * LANES, width + (pair + 1) * LANES)
                    r.dkv[rows, lanes] += dot(grad_low, r.qm[pair, q_tile])
                    r.dkv[rows, lanes_v] += dot(probs_low, r.gm[pair, q_tile])
                    for side in range(2):
                        span = slice(side * TILE, (side + 1) * TILE)
                        head = slice((2 * pair + side) * 64, (2 * pair + side + 1) * 64)
                        r.turned[head, :] += dot(r.kt[k_tile, head, :], grad_low[:, span])

            return inner

        lax.fori_loop(0, k_tiles, one_key_tile, 0)
        rows = pl.ds(pl.multiple_of(q_tile * TILE, TILE), TILE)
        r.dq[rows, low:high] = jnp.transpose(r.turned[low:high, :]) * (64**-0.5)
        return carry

    lax.fori_loop(0, q_tiles, one_query_tile, 0)


def feed_forward(r, low):
    r.sum[...] = jnp.zeros(r.sum.shape, f32)

    def one_chunk(chunk, carry):
        span = pl.ds(pl.multiple_of(chunk * CHUNK, CHUNK), CHUNK)
        upward = dot(low[...], r.w_in[:, span])
        gate = jax.nn.sigmoid(upward)
        active = (upward * gate).astype(bf16)
        r.act[:, span] = active
        r.slope[:, span] = (gate + upward * gate * (1.0 - gate)).astype(r.slope.dtype)
        r.sum[...] += dot(active, r.w_down[span, :])
        return carry

    lax.fori_loop(0, r.w_in.shape[1] // CHUNK, one_chunk, 0)


def feed_backward(r):
    r.sum[...] = jnp.zeros(r.sum.shape, f32)

    def one_chunk(chunk, carry):
        span = pl.ds(pl.multiple_of(chunk * CHUNK, CHUNK), CHUNK)
        grad_active = dot_nt(r.down_grad[...], r.w_down[span, :]).astype(bf16)
        grad_up = (grad_active.astype(f32) * r.slope[:, span].astype(f32)).astype(bf16)
        r.up_grad[:, span] = grad_up
        r.sum[...] += dot_nt(grad_up, r.w_in[:, span])
        return carry

    lax.fori_loop(0, r.w_in.shape[1] // CHUNK, one_chunk, 0)


def self_forward(r):
    length, width = r.x_own_h.shape
    decoder, core = r.meta[0], r.meta[1]
    move = Copies(r.sems)
    early = [
        move.start(r.x_own_h, r.x.at[pl.ds(0, length)]),
        move.start(r.x_other_h, r.x.at[pl.ds(length, length)]),
        move.start(r.w_mixed_h, r.w_mixed),
    ]
    later = [
        move.start(r.w_out_h, r.w_out),
        move.start(r.w_in_h, r.w_in),
        move.start(r.w_down_h, r.w_down),
    ]
    turn_documents(r.kdc, r.kd[r.micro])
    wait_all(early)
    r.q[...] = dot(r.x[:length, :], r.w_mixed[:, :width]).astype(bf16)
    r.kv[...] = dot(r.x[...], r.w_mixed[:, width:]).astype(bf16)
    outs = [move.start(r.q, r.q_o), move.start(r.kv, r.kv_o)]
    pairs = range(width // LANES)
    spread_pairs(r.qm, r.q, 64**-0.5, pairs)
    turn_tiles(r.vt, r.kv, width, pairs)
    attention_forward(r, core, decoder)
    wait_all(later)
    outs += [move.start(r.att, r.att_o), move.start(r.lse, r.lse_o)]
    unit, inverse = standardize(r.x[:length, :].astype(f32) + dot(r.att[...], r.w_out[...]))
    r.unit1[...] = unit
    r.inv1[...] = jnp.broadcast_to(inverse, r.inv1.shape)
    r.first_low[...] = (unit * r.gains[0:1, :]).astype(bf16)
    outs += [
        move.start(r.unit1, r.unit1_o),
        move.start(r.inv1, r.inv1_o),
        move.start(r.first_low, r.first_low_o),
    ]

    @pl.when(decoder == 0)
    def _():
        feed_forward(r, r.first_low)
        late = [
            move.start(r.first_low, r.ffn_low_o),
            move.start(r.act, r.act_o),
            move.start(r.slope, r.slope_o),
        ]
        unit2, inverse2 = standardize(r.unit1[...] * r.gains[0:1, :] + r.sum[...])
        r.memory[...] = (unit2 * r.gains[1:2, :]).astype(bf16)
        late += [move.start(r.memory, r.memory_o)]
        r.unit2[...] = unit2
        r.inv2[...] = jnp.broadcast_to(inverse2, r.inv2.shape)
        late += [move.start(r.unit2, r.unit2_o), move.start(r.inv2, r.inv2_o)]
        wait_all(late)

    wait_all(outs)


def cross_both_ways(r):
    length, width = r.unit1_h.shape
    core = r.meta[1]
    move = Copies(r.sems)
    moves = [
        move.start(r.memory_own_h, r.x.at[pl.ds(0, length)]),
        move.start(r.memory_other_h, r.x.at[pl.ds(length, length)]),
        move.start(r.w_pair_h, r.w_pair),
        move.start(r.first_low_h, r.first_low),
        move.start(r.w_query_h, r.w_query),
    ]
    later = [
        move.start(r.unit1_h, r.unit1),
        move.start(r.w_cross_h, r.w_cross),
        move.start(r.w_in_h, r.w_in),
        move.start(r.w_down_h, r.w_down),
        move.start(r.cot_h.at[r.micro], r.cot),
    ]
    turn_documents(r.kdc, r.kd[r.micro])
    wait_all(moves)
    r.kv[...] = dot(r.x[...], r.w_pair[...]).astype(bf16)
    r.q[...] = dot(r.first_low[...], r.w_query[...]).astype(bf16)
    pairs = range(width // LANES)
    spread_pairs(r.qm, r.q, 64**-0.5, pairs)
    turn_tiles(r.vt, r.kv, width, pairs)
    turn_tiles(r.kt, r.kv, 0, pairs)
    attention_forward(r, core, 0)
    outs = [move.start(r.att, r.att_o)]
    wait_all(later)
    first = r.unit1[...] * r.gains[0:1, :]
    unit, inverse = standardize(first + dot(r.att[...], r.w_cross[...]))
    r.unit2[...] = unit
    r.inv2[...] = jnp.broadcast_to(inverse, r.inv2.shape)
    r.second_low[...] = (unit * r.cross_gain[...]).astype(bf16)
    outs += [move.start(r.second_low, r.ffn_low_o)]
    feed_forward(r, r.second_low)
    outs += [move.start(r.act, r.act_o)]
    unit3, inverse3 = standardize(r.unit2[...] * r.cross_gain[...] + r.sum[...])
    r.decoded[...] = (unit3 * r.gains[1:2, :]).astype(bf16)
    outs += [move.start(r.decoded, r.decoded_o)]
    grad_third, gain_late = standardize_back(
        r.cot[...].astype(f32), unit3, r.gains[1:2, :], inverse3
    )
    r.keep[...] = grad_third
    r.down_grad[...] = grad_third.astype(bf16)
    outs += [move.start(r.down_grad, r.down_grad_o)]
    feed_backward(r)
    outs += [move.start(r.up_grad, r.up_grad_o)]
    grad_sum, gain_cross = standardize_back(
        r.keep[...] + r.sum[...], r.unit2[...], r.cross_gain[...], r.inv2[:, 0:1]
    )
    r.gain_grads[...] = jnp.zeros(r.gain_grads.shape, f32)
    r.gain_grads[0:1, :] = gain_late
    r.gain_grads[1:2, :] = gain_cross
    r.keep[...] = grad_sum
    r.branch[...] = grad_sum.astype(bf16)
    outs += [move.start(r.gain_grads, r.gain_grads_o), move.start(r.branch, r.branch_o)]
    r.q[...] = dot_nt(r.branch[...], r.w_cross[...]).astype(bf16)
    spread_pairs(r.gm, r.q, 1.0, pairs)
    row_products(r, r.q, pairs)
    attention_backward(r, core, 0, pairs)
    r.dq_low[...] = r.dq[...].astype(bf16)
    r.keep[...] += dot_nt(r.dq_low[...], r.w_query[...])
    outs += [move.start(r.dq_low, r.dq_low_o), move.start(r.keep, r.grad_first_o)]
    r.dkv_low[...] = r.dkv[...].astype(bf16)
    outs += [move.start(r.dkv_low, r.dkv_o)]
    part = dot_nt(r.dkv_low[...], r.w_pair[...])
    r.part_other[...] = part[length:, :].astype(bf16)
    r.part_own[...] = part[:length, :]
    outs += [move.start(r.part_other, r.part_other_o), move.start(r.part_own, r.part_own_o)]
    wait_all(outs)


def feed_backward_alone(r):
    move = Copies(r.sems)
    early = [
        move.start(r.grad_memory_h, r.cot),
        move.start(r.unit2_h, r.unit2),
        move.start(r.inv2_h, r.inv2),
    ]
    later = [
        move.start(r.w_down_h, r.w_down),
        move.start(r.slope_h, r.slope),
        move.start(r.w_in_h, r.w_in),
    ]
    wait_all(early)
    grad_third, gain_late = standardize_back(
        r.cot[...].astype(f32), r.unit2[...], r.gains[1:2, :], r.inv2[:, 0:1]
    )
    r.gain_grads[...] = jnp.broadcast_to(gain_late, r.gain_grads.shape)
    r.keep[...] = grad_third
    r.down_grad[...] = grad_third.astype(bf16)
    outs = [move.start(r.down_grad, r.down_grad_o), move.start(r.gain_grads, r.gain_late_o)]
    wait_all(later)
    feed_backward(r)
    outs += [move.start(r.up_grad, r.up_grad_o)]
    r.keep[...] += r.sum[...]
    outs += [move.start(r.keep, r.grad_first_o)]
    wait_all(outs)


def self_backward(r, plan):
    r.micro, first, last = plan
    length, width = r.att_h.shape
    decoder, core = r.meta[0], r.meta[1]
    pairs = range(first, last)
    low, high = first * LANES, last * LANES
    move = Copies(r.sems)
    later = [
        move.start(r.q_h, r.q),
        move.start(r.kv_h, r.kv),
        move.start(r.att_h, r.att),
        move.start(r.lse_h, r.lse),
    ]
    if first == 0:
        early = [
            move.start(r.grad_first_h, r.keep),
            move.start(r.unit1_h, r.unit1),
            move.start(r.inv1_h, r.inv1),
            move.start(r.w_out_h, r.w_out),
        ]
    else:
        early = [move.start(r.grad_att_h, r.grad_att)]
    outs = []
    turn_documents(r.kdc, r.kd[r.micro])
    wait_all(early)
    if first == 0:
        grad_sum, gain_early = standardize_back(
            r.keep[...], r.unit1[...], r.gains[0:1, :], r.inv1[:, 0:1]
        )
        r.gain_grads[...] = jnp.broadcast_to(gain_early, r.gain_grads.shape)
        r.keep[...] = grad_sum
        r.branch[...] = grad_sum.astype(bf16)
        r.grad_att[...] = dot_nt(r.branch[...], r.w_out[...]).astype(bf16)
        outs += [move.start(r.gain_grads, r.gain_early_o), move.start(r.branch, r.branch_o)]
        if last < width // LANES:
            outs += [move.start(r.keep, r.grad_sum_o), move.start(r.grad_att, r.grad_att_o)]
    wait_all(later)
    if last == width // LANES:
        ends = [move.start(r.w_mixed_h, r.w_mixed)]
        if first > 0:
            ends += [
                move.start(r.grad_sum_h, r.keep),
                move.start(r.dq_h.at[:, pl.ds(0, low)], r.dq_low.at[:, pl.ds(0, low)]),
                move.start(r.dkv_h.at[:, pl.ds(0, low)], r.dkv_low.at[:, pl.ds(0, low)]),
                move.start(
                    r.dkv_h.at[:, pl.ds(width, low)], r.dkv_low.at[:, pl.ds(width, low)]
                ),
            ]
    spread_pairs(r.qm, r.q, 64**-0.5, pairs)
    turn_tiles(r.kt, r.kv, 0, pairs)
    spread_pairs(r.gm, r.grad_att, 1.0, pairs)
    row_products(r, r.grad_att, pairs)
    attention_backward(r, core, decoder, pairs)
    r.dq_low[:, low:high] = r.dq[:, low:high].astype(bf16)
    for start in (0, width):
        span = slice(start + low, start + high)
        r.dkv_low[:, span] = r.dkv[:, span].astype(bf16)
    if last == width // LANES:
        wait_all(ends)
        outs += [move.start(r.dq_low, r.dq_low_o), move.start(r.dkv_low, r.dkv_o)]
        r.keep[...] += dot_nt(r.dq_low[...], r.w_mixed[:, :width])
        part = dot_nt(r.dkv_low[...], r.w_mixed[:, width:])
        r.part_other[...] = part[length:, :].astype(bf16)
        r.keep[...] += part[:length, :]
        outs += [move.start(r.part_other, r.part_other_o), move.start(r.keep, r.part_own_o)]
    else:
        outs.append(move.start(r.dq_low.at[:, pl.ds(low, high - low)], r.dq_low_o.at[:, pl.ds(low, high - low)]))
        for start in (0, width):
            span = pl.ds(start + low, high - low)
            outs.append(move.start(r.dkv_low.at[:, span], r.dkv_o.at[:, span]))
    wait_all(outs)


def contract_blocks(r, plan):
    operands, blocks = plan(r)
    for core in range(2):

        @pl.when(r.meta[1] == core)
        def _(core=core):
            move = Copies(r.sems)
            loads = []
            for target, sources in operands:
                row = 0
                for source in sources:
                    loads.append(move.start(source, target.at[pl.ds(row, source.shape[0])]))
                    row += source.shape[0]
            wait_all(loads)
            outs = []
            held = dict()
            for half in (1 - core, core):
                for place in range(2):
                    slot = 2 * half + place
                    turn, left, left_at, right, right_at = blocks[slot]
                    if held.get(id(turn)) != left_at:
                        for row in range(0, left.shape[0], CHUNK):
                            block = left[
                                row : row + CHUNK, left_at * CHUNK : (left_at + 1) * CHUNK
                            ]
                            turn[:, row : row + CHUNK] = jnp.transpose(block)
                        held[id(turn)] = left_at
                    block = right[:, right_at * CHUNK : (right_at + 1) * CHUNK]
                    r.blocks[slot] = dot(turn[:, : right.shape[0]], block).astype(bf16)
                    target = r.kept_o if half == core else r.sent_o
                    outs.append(move.start(r.blocks.at[slot], target.at[place]))
            wait_all(outs)


def spread_pieces(r, targets):
    z = r.meta[3]
    group, height = r.own_h.shape[:2]
    rows = r.own_h.shape[2] // group
    for core in range(2):
        for x in range(2):

            @pl.when((r.meta[1] == core) & (r.meta[2] == x))
            def _(core=core, x=x):
                move = Copies(r.sems)
                parts = [
                    (r.own_h, core, x),
                    (r.own_x_h, core, 1 - x),
                    (r.other_h, 1 - core, x),
                    (r.other_x_h, 1 - core, 1 - x),
                ]
                loads = [
                    move.start(source, r.pieces.at[place])
                    for place, (source, _, _) in enumerate(parts)
                ]
                outs = []
                slot = 0
                gains = None
                for place, (_, half, side) in enumerate(parts):
                    loads[place].wait()
                    for step in range(group):
                        row = pl.multiple_of(lax.rem(z + (group - step), group) * rows, rows)
                        start = 0
                        for target in targets(r, 2 * half + side, row, rows):
                            r.wide[slot] = r.pieces[place, step, start : start + rows].astype(f32)
                            outs.append(move.start(r.wide.at[slot], target))
                            slot += 1
                            start += rows
                        if start < height:
                            extra = r.pieces[place, step, start:height].astype(f32)
                            gains = extra if gains is None else gains + extra
                if gains is not None:
                    r.gain_grads[...] = gains
                    outs.append(move.start(r.gain_grads, r.gains_o))
                wait_all(outs)


def launch(kernel, plan, side, scalars, small, large, outs, scratch, copies, work, previous=None, after=()):
    names = list(scalars) + list(small) + list(large)
    arrays = list(scalars.values()) + list(small.values()) + list(large.values())
    specs = (
        [pl.BlockSpec(memory_space=pltpu.SMEM)] * len(scalars)
        + [pl.BlockSpec(memory_space=pltpu.VMEM)] * len(small)
        + [pl.BlockSpec(memory_space=pl.ANY)] * len(large)
    )
    aliases = dict()
    for position, name in enumerate(outs):
        if previous and name in previous:
            aliases[len(arrays)] = position
            names.append("previous_" + name)
            arrays.append(previous[name])
            specs.append(pl.BlockSpec(memory_space=pl.ANY))
    for array in after:
        names.append("")
        arrays.append(array)
        specs.append(pl.BlockSpec(memory_space=pl.ANY))
    names += list(outs) + list(scratch) + ["sems"]

    def body(*refs):
        r = types.SimpleNamespace(**dict(zip(names, refs)))

        def run():
            if isinstance(plan, int):
                r.micro = plan
                kernel(r)
            else:
                kernel(r, plan)

        if side is None:
            run()
        else:
            pl.when(r.meta[0] == side)(run)

    results = pl.pallas_call(
        body,
        out_shape=[jax.ShapeDtypeStruct(*shape) for shape in outs.values()],
        in_specs=specs,
        out_specs=[pl.BlockSpec(memory_space=pl.ANY)] * len(outs),
        scratch_shapes=[pltpu.VMEM(*shape) for shape in scratch.values()]
        + [pltpu.SemaphoreType.DMA((copies,))],
        input_output_aliases=aliases,
        compiler_params=pltpu.CompilerParams(vmem_limit_bytes=58 * 1024 * 1024),
        cost_estimate=pl.CostEstimate(
            flops=work * 10**9, bytes_accessed=1 << 20, transcendentals=0
        ),
    )(*arrays)
    return types.SimpleNamespace(**dict(zip(outs, results)))


def attention_scratch(length, width):
    pairs, q_tiles, k_tiles = width // LANES, length // TILE, 2 * length // TILE
    return dict(
        q=((length, width), bf16),
        kv=((2 * length, 2 * width), bf16),
        qm=((pairs, q_tiles, 2 * TILE, LANES), bf16),
        kdc=((2 * length, LANES), f32),
        bias=((TILE, TILE), f32),
        lse=((q_tiles, 8, 2 * TILE), f32),
        att=((length, width), bf16),
        turned=((width, TILE), f32),
    )


def forward_scratch(length, width):
    k_tiles = 2 * length // TILE
    return dict(
        vt=((k_tiles, width, TILE), bf16),
        top=((8, 2 * TILE), f32),
        total=((8, 2 * TILE), f32),
    )


def backward_scratch(length, width):
    pairs, q_tiles, k_tiles = width // LANES, length // TILE, 2 * length // TILE
    return dict(
        kt=((k_tiles, width, TILE), bf16),
        gm=((pairs, q_tiles, 2 * TILE, LANES), bf16),
        delta=((q_tiles, 8, 2 * TILE), f32),
        dkv=((2 * length, 2 * width), f32),
        dq=((length, width), f32),
        dkv_low=((2 * length, 2 * width), bf16),
        part_other=((length, width), bf16),
        dq_low=((length, width), bf16),
    )


def for_sending(shard):

    def short(part):
        return part.astype(jnp.bfloat16) if part.dtype == jnp.float32 else part

    return jax.tree.map(short, shard)


def from_behind(block, axis, distance):
    devices = range(lax.axis_size(axis))
    route = [(i - distance, i) for i in devices if i - distance in devices]
    return lax.ppermute(block, axis, route)


def from_root(shard, axis, root):
    mine = lax.axis_index(axis) == root
    return lax.psum(jnp.where(mine, shard, jnp.zeros_like(shard)), axis)


def matmul(left_side, right_side):
    return jnp.einsum("rsd,de->rse", left_side, right_side, preferred_element_type=jnp.float32)


def matmul_back(left_side, right_side):
    return jnp.einsum("rse,de->rsd", left_side, right_side, preferred_element_type=jnp.float32)


def contract(left_side, right_side):
    return jnp.einsum("rsd,rse->de", left_side, right_side, preferred_element_type=jnp.float32)


def normalize(values, gain_row):
    center = values - jnp.mean(values, axis=-1, keepdims=True)
    inverse = lax.rsqrt(jnp.mean(center * center, axis=-1, keepdims=True) + epsilon)
    standard = center * inverse
    return (standard * gain_row, standard, inverse)


def normalize_back(grad_out, standard, gain_row, inverse):
    scaled = grad_out * gain_row
    grad_in = inverse * (
        scaled
        - jnp.mean(scaled, axis=-1, keepdims=True)
        - standard * jnp.mean(scaled * standard, axis=-1, keepdims=True)
    )
    return (grad_in, jnp.sum(grad_out * standard, axis=(0, 1)))


def allowed_mask(query_docs, key_docs, query_place, key_place, causal):
    same_doc = query_docs[:, :, None] == key_docs[:, None, :]
    earlier = query_place[:, None] >= key_place[None, :]
    return (same_doc & (earlier | jnp.logical_not(causal)))[:, None]


def attend(queries, keys_local, values_local, query_docs, key_docs, causal, is_cross):
    rows_here, shard_len, model_width = queries.shape
    head_dim = model_width // HEADS
    score_scale = head_dim ** (-0.5)
    query_place = lax.axis_index("seq") * shard_len + jnp.arange(shard_len)
    query_heads = queries.reshape(rows_here, shard_len, HEADS, head_dim)

    def absorb(state_tuple, pieces):
        running_top, running_total, running_sum = state_tuple
        key_piece, value_piece, doc_piece = pieces
        piece_len = key_piece.shape[1]
        raw_scores = jnp.einsum(
            "rqhd,rkhd->rhqk",
            query_heads,
            key_piece.reshape(rows_here, piece_len, HEADS, head_dim),
            preferred_element_type=jnp.float32,
        )
        allowed = allowed_mask(query_docs, doc_piece, query_place, jnp.arange(piece_len), causal)
        scores = jnp.where(allowed, raw_scores * score_scale, negative_big)
        new_top = jnp.maximum(running_top, jnp.max(scores, axis=-1))
        weights = jnp.where(allowed, jnp.exp(scores - new_top[..., None]), 0.0)
        new_total = jnp.sum(weights, axis=-1)
        product = jnp.einsum(
            "rhqk,rkhd->rhqd",
            weights.astype(jnp.bfloat16),
            value_piece.reshape(rows_here, piece_len, HEADS, head_dim),
            preferred_element_type=jnp.float32,
        )
        return (new_top, new_total, product)

    init_state = (
        jnp.full((rows_here, HEADS, shard_len), negative_big, jnp.float32),
        jnp.zeros((rows_here, HEADS, shard_len), jnp.float32),
        jnp.zeros((rows_here, HEADS, shard_len, head_dim), jnp.float32),
    )
    if is_cross:
        final_top, final_total, final_sum = absorb(
            init_state,
            (
                lax.all_gather(keys_local, "seq", axis=1, tiled=True),
                lax.all_gather(values_local, "seq", axis=1, tiled=True),
                lax.all_gather(for_sending(key_docs), "seq", axis=1, tiled=True),
            ),
        )
    else:
        final_top, final_total, final_sum = absorb(
            init_state,
            (
                lax.all_gather(keys_local, "seq", axis=1, tiled=True),
                lax.all_gather(values_local, "seq", axis=1, tiled=True),
                lax.all_gather(key_docs, "seq", axis=1, tiled=True),
            ),
        )
    attended = (
        (final_sum / final_total[..., None])
        .transpose(0, 2, 1, 3)
        .reshape(rows_here, shard_len, model_width)
    )
    return (attended, final_top + jnp.log(final_total))


def attend_back(
    queries,
    keys_local,
    values_local,
    query_docs,
    key_docs,
    causal,
    log_total,
    grad_attended,
    is_cross,
):
    rows_here, shard_len, model_width = queries.shape
    head_dim = model_width // HEADS
    score_scale = head_dim ** (-0.5)
    query_place = lax.axis_index("seq") * shard_len + jnp.arange(shard_len)
    if is_cross:
        keys_full, values_full, docs_full = (
            lax.all_gather(keys_local, "seq", axis=1, tiled=True),
            lax.all_gather(values_local, "seq", axis=1, tiled=True),
            lax.all_gather(for_sending(key_docs), "seq", axis=1, tiled=True).astype(key_docs.dtype),
        )
    else:
        keys_full, values_full, docs_full = (
            lax.all_gather(keys_local, "seq", axis=1, tiled=True),
            lax.all_gather(values_local, "seq", axis=1, tiled=True),
            lax.all_gather(key_docs, "seq", axis=1, tiled=True),
        )
    full_len = keys_full.shape[1]
    query_heads = queries.reshape(rows_here, shard_len, HEADS, head_dim)
    key_heads = keys_full.reshape(rows_here, full_len, HEADS, head_dim)
    value_heads = values_full.reshape(rows_here, full_len, HEADS, head_dim)
    grad_heads = grad_attended.reshape(rows_here, shard_len, HEADS, head_dim)
    raw_scores = jnp.einsum(
        "rqhd,rkhd->rhqk", query_heads, key_heads, preferred_element_type=jnp.float32
    )
    allowed = allowed_mask(query_docs, docs_full, query_place, jnp.arange(full_len), causal)
    shifted = jnp.where(allowed, raw_scores * score_scale - log_total[..., None], negative_big)
    probs = jnp.where(allowed, jnp.exp(shifted), 0.0)
    grad_probs = jnp.einsum(
        "rqhd,rkhd->rhqk", grad_heads, value_heads, preferred_element_type=jnp.float32
    )
    delta = jnp.sum(probs * grad_probs, axis=-1)
    grad_scores = (probs * (grad_probs - delta[..., None]) * score_scale).astype(jnp.bfloat16)
    grad_queries = jnp.einsum(
        "rhqk,rkhd->rqhd", grad_scores, key_heads, preferred_element_type=jnp.float32
    ).reshape(rows_here, shard_len, model_width)
    probs_low = probs.astype(jnp.bfloat16)

    def key_terms(span):
        grad_keys = jnp.einsum(
            "rhqk,rqhd->krhd", grad_scores, query_heads, preferred_element_type=jnp.float32
        )
        grad_values = jnp.einsum(
            "rhqk,rqhd->krhd", probs_low, grad_heads, preferred_element_type=jnp.float32
        )
        return jnp.concatenate(
            [
                grad_keys.reshape(span, rows_here, model_width),
                grad_values.reshape(span, rows_here, model_width),
            ],
            axis=-1,
        )

    if is_cross:
        pair_terms = lax.psum_scatter(
            key_terms(shard_len * lax.axis_size("seq")).astype(jnp.bfloat16),
            "seq",
            scatter_dimension=0,
            tiled=True,
        ).astype(jnp.float32)
    else:
        pair_terms = lax.psum_scatter(
            key_terms(shard_len * lax.axis_size("seq")).astype(jnp.bfloat16),
            "seq",
            scatter_dimension=0,
            tiled=True,
        ).astype(jnp.float32)
    return (grad_queries, pair_terms.transpose(1, 0, 2))


def layer_forward(hidden_in, doc_own, memory, memory_docs, weights, is_decoder):
    (
        qkv_weight,
        out_weight,
        in_weight,
        down_weight,
        gains_pair,
        query_weight,
        pair_weight,
        cross_weight,
        cross_gains,
    ) = weights
    model_width = hidden_in.shape[-1]
    mixed = matmul(hidden_in, qkv_weight).astype(jnp.bfloat16)
    attended, self_lse = attend(
        mixed[..., :model_width],
        mixed[..., model_width : 2 * model_width],
        mixed[..., 2 * model_width :],
        doc_own,
        doc_own,
        is_decoder,
        False,
    )
    attended = attended.astype(jnp.bfloat16)
    first, first_unit, first_inv = normalize(
        hidden_in.astype(jnp.float32) + matmul(attended, out_weight), gains_pair[0]
    )
    first_low = first.astype(jnp.bfloat16)
    cross_queries = matmul(first_low, query_weight).astype(jnp.bfloat16)
    pair = matmul(memory, pair_weight).astype(jnp.bfloat16)
    cross_att, cross_lse = attend(
        cross_queries,
        pair[..., :model_width],
        pair[..., model_width:],
        doc_own,
        memory_docs,
        False,
        True,
    )
    cross_att = cross_att.astype(jnp.bfloat16)
    second_cross, second_unit, second_inv = normalize(
        first + matmul(cross_att, cross_weight), cross_gains
    )
    second = jnp.where(is_decoder, second_cross, first)
    second_low = second.astype(jnp.bfloat16)
    upward = matmul(second_low, in_weight)
    active = jax.nn.silu(upward).astype(jnp.bfloat16)
    result, third_unit, third_inv = normalize(second + matmul(active, down_weight), gains_pair[1])
    saved = {
        "mixed": mixed,
        "attended": attended,
        "self_lse": self_lse,
        "first_unit": first_unit,
        "first_inv": first_inv,
        "first_low": first_low,
        "cross_queries": cross_queries,
        "pair": pair,
        "cross_att": cross_att,
        "cross_lse": cross_lse,
        "second_unit": second_unit,
        "second_inv": second_inv,
        "second_low": second_low,
        "upward": upward,
        "active": active,
        "third_unit": third_unit,
        "third_inv": third_inv,
    }
    return (result, saved)


def layer_backward(
    grad_result, saved, hidden_in, doc_own, memory, memory_docs, weights, is_decoder
):
    (
        qkv_weight,
        out_weight,
        in_weight,
        down_weight,
        gains_pair,
        query_weight,
        pair_weight,
        cross_weight,
        cross_gains,
    ) = weights
    model_width = hidden_in.shape[-1]
    grad_third, grad_gain_late = normalize_back(
        grad_result, saved["third_unit"], gains_pair[1], saved["third_inv"]
    )
    down_grad = grad_third.astype(jnp.bfloat16)
    grad_down_w = contract(saved["active"], down_grad)
    grad_active = matmul_back(down_grad, down_weight).astype(jnp.bfloat16)
    sigmoid_up = jax.nn.sigmoid(saved["upward"])
    grad_upward = (
        grad_active.astype(jnp.float32)
        * (sigmoid_up + saved["upward"] * sigmoid_up * (1.0 - sigmoid_up))
    ).astype(jnp.bfloat16)
    grad_in_w = contract(saved["second_low"], grad_upward)
    grad_second = grad_third + matmul_back(grad_upward, in_weight)
    grad_cross_sum, grad_cross_gain = normalize_back(
        grad_second, saved["second_unit"], cross_gains, saved["second_inv"]
    )
    decoder_flag = is_decoder.astype(jnp.float32)
    grad_cross_sum = grad_cross_sum * decoder_flag
    grad_cross_gain = grad_cross_gain * decoder_flag
    cross_branch = grad_cross_sum.astype(jnp.bfloat16)
    grad_cross_w = contract(saved["cross_att"], cross_branch)
    grad_cross_att = matmul_back(cross_branch, cross_weight).astype(jnp.bfloat16)
    pair = saved["pair"]
    grad_cross_q, grad_pair = attend_back(
        saved["cross_queries"],
        pair[..., :model_width],
        pair[..., model_width:],
        doc_own,
        memory_docs,
        False,
        saved["cross_lse"],
        grad_cross_att,
        True,
    )
    grad_cross_q = grad_cross_q.astype(jnp.bfloat16)
    grad_pair = grad_pair.astype(jnp.bfloat16)
    grad_query_w = contract(saved["first_low"], grad_cross_q)
    grad_pair_w = contract(memory, grad_pair)
    grad_memory = matmul_back(grad_pair, pair_weight)
    grad_first = jnp.where(
        is_decoder, grad_cross_sum + matmul_back(grad_cross_q, query_weight), grad_second
    )
    grad_first_sum, grad_gain_early = normalize_back(
        grad_first, saved["first_unit"], gains_pair[0], saved["first_inv"]
    )
    self_branch = grad_first_sum.astype(jnp.bfloat16)
    grad_out_w = contract(saved["attended"], self_branch)
    grad_attended = matmul_back(self_branch, out_weight).astype(jnp.bfloat16)
    mixed = saved["mixed"]
    grad_queries, grad_pair_self = attend_back(
        mixed[..., :model_width],
        mixed[..., model_width : 2 * model_width],
        mixed[..., 2 * model_width :],
        doc_own,
        doc_own,
        is_decoder,
        saved["self_lse"],
        grad_attended,
        False,
    )
    grad_mixed = jnp.concatenate([grad_queries, grad_pair_self], axis=-1).astype(jnp.bfloat16)
    grad_qkv_w = contract(hidden_in, grad_mixed)
    grad_hidden = grad_first_sum + matmul_back(grad_mixed, qkv_weight)
    layer_grads = (
        grad_qkv_w,
        grad_out_w,
        grad_in_w,
        grad_down_w,
        jnp.stack([grad_gain_early, grad_gain_late]),
        grad_query_w,
        grad_pair_w,
        grad_cross_w,
        grad_cross_gain,
    )
    return (grad_hidden, grad_memory, layer_grads)


def any_rows(
    layer_input,
    segment_ids,
    attn_qkv,
    attn_out,
    ffn_in,
    ffn_out,
    norm_gain,
    cross_query,
    cross_pair,
    cross_out,
    cross_gain,
    out_cotangent,
):
    micro_count = layer_input.shape[1]
    section_index = lax.axis_index("section")
    is_decoder = section_index == 1
    weights = (
        attn_qkv[0],
        attn_out[0],
        ffn_in[0],
        ffn_out[0],
        norm_gain[0],
        cross_query,
        cross_pair,
        cross_out,
        cross_gain,
    )
    inputs_all = layer_input[0]
    docs_all = segment_ids[0]
    slot_ids = jnp.arange(micro_count)
    received = (jnp.zeros_like(inputs_all[0]), jnp.zeros_like(docs_all[0]))
    results = jnp.zeros_like(inputs_all)
    memories = []
    memory_doc_list = []
    for step_index in range(micro_count + 1):
        batch_index = step_index - section_index
        is_valid = (batch_index >= 0) & (batch_index < micro_count)
        chosen = jnp.clip(batch_index, 0, micro_count - 1)
        hidden_in = lax.dynamic_index_in_dim(inputs_all, chosen, 0, keepdims=False)
        doc_own = lax.dynamic_index_in_dim(docs_all, chosen, 0, keepdims=False)
        memory = received[0]
        memory_docs = jnp.where(is_valid & is_decoder, received[1], doc_own)
        memories.append(memory)
        memory_doc_list.append(memory_docs)
        result, saved = layer_forward(hidden_in, doc_own, memory, memory_docs, weights, is_decoder)
        low_result = result.astype(jnp.bfloat16)
        writing = (slot_ids == chosen) & is_valid
        results = jnp.where(writing[:, None, None, None], low_result[None], results)
        if step_index < micro_count:
            received = from_behind((low_result, doc_own), "section", 1)
    memory_stack = jnp.stack(memories)
    memory_doc_stack = jnp.stack(memory_doc_list)
    totals = tuple((jnp.zeros(weight.shape, jnp.float32) for weight in weights))
    input_grads = jnp.zeros(inputs_all.shape, jnp.float32)
    returned = jnp.zeros(inputs_all.shape[1:], jnp.float32)
    for step_index in range(micro_count + 1):
        batch_index = micro_count - step_index - section_index
        is_valid = (batch_index >= 0) & (batch_index < micro_count)
        chosen = jnp.clip(batch_index, 0, micro_count - 1)
        forward_step = jnp.clip(batch_index + section_index, 0, micro_count)
        hidden_in = lax.dynamic_index_in_dim(inputs_all, chosen, 0, keepdims=False)
        doc_own = lax.dynamic_index_in_dim(docs_all, chosen, 0, keepdims=False)
        memory = lax.dynamic_index_in_dim(memory_stack, forward_step, 0, keepdims=False)
        memory_docs = lax.dynamic_index_in_dim(memory_doc_stack, forward_step, 0, keepdims=False)
        discarded, saved = layer_forward(
            hidden_in, doc_own, memory, memory_docs, weights, is_decoder
        )
        cotangent = jnp.where(
            is_decoder,
            lax.dynamic_index_in_dim(out_cotangent, chosen, 0, keepdims=False).astype(jnp.float32),
            returned,
        )
        grad_hidden, grad_memory, layer_grads = layer_backward(
            cotangent, saved, hidden_in, doc_own, memory, memory_docs, weights, is_decoder
        )
        valid_flag = is_valid.astype(jnp.float32)
        totals = tuple(
            (running + valid_flag * fresh for running, fresh in zip(totals, layer_grads))
        )
        writing = (slot_ids == chosen) & is_valid
        input_grads = jnp.where(writing[:, None, None, None], grad_hidden[None], input_grads)
        if step_index < micro_count:
            returned = from_behind(grad_memory.astype(jnp.bfloat16), "section", -1).astype(
                grad_memory.dtype
            )
    group_sums = lax.psum(
        (
            totals[0],
            totals[1],
            totals[2],
            totals[3],
            totals[4],
            totals[5],
            totals[6],
            totals[7],
            totals[8],
        ),
        ("seq", "dp"),
    )
    section_sums = group_sums[:5]
    cross_sums = (
        from_root(group_sums[5].astype(jnp.bfloat16), "section", 1).astype(jnp.float32),
        from_root(group_sums[6].astype(jnp.bfloat16), "section", 1).astype(jnp.float32),
        from_root(group_sums[7].astype(jnp.bfloat16), "section", 1).astype(jnp.float32),
        from_root(group_sums[8].astype(jnp.bfloat16), "section", 1).astype(jnp.float32),
    )
    return (
        results[None],
        input_grads[None],
        section_sums[0][None],
        section_sums[1][None],
        section_sums[2][None],
        section_sums[3][None],
        section_sums[4][None],
        cross_sums[0],
        cross_sums[1],
        cross_sums[2],
        cross_sums[3],
    )


def split_rows(
    layer_input,
    segment_ids,
    attn_qkv,
    attn_out,
    ffn_in,
    ffn_out,
    norm_gain,
    cross_query,
    cross_pair,
    cross_out,
    cross_gain,
    out_cotangent,
):
    micros = layer_input.shape[1]
    length, width = layer_input.shape[3:]
    hidden = ffn_in.shape[-1]
    q_tiles = length // TILE
    group = lax.axis_size("dp") // 2
    axes = ("section", "seq", "dp")
    decoder = lax.axis_index("section") == 1
    flag = decoder.astype(jnp.int32)
    x = lax.axis_index("seq")
    core = lax.rem(lax.axis_index("dp"), 2)
    z = lax.axis_index("dp") // 2
    places = [(t, i, k, c) for t in range(2) for i in range(2) for k in range(group) for c in range(2)]

    def number(t, i, k, c):
        return ((t * 2 + i) * group + k) * 2 + c

    def send(values, target, section=None):
        route = [
            (number(*place), number(*target(*place)))
            for place in places
            if section in (None, place[0]) and target(*place)
        ]
        return lax.ppermute(values, axes, route)

    def to_core(t, i, k, c):
        return (t, i, k, 1 - c)

    def to_x(t, i, k, c):
        return (t, 1 - i, k, c)

    def to_row(t, i, k, c):
        return (t, c, k, i)

    def to_decoder(t, i, k, c):
        return (1, i, k, c) if t == 0 else None

    def to_encoder(t, i, k, c):
        return (0, i, k, c) if t == 1 else None

    def exchange(values):
        return send(values, to_core)

    low = ((length, width), bf16)
    wide = ((length, width), f32)
    both = ((2 * length, width), bf16)
    keys_all = ((2 * length, 2 * width), bf16)
    mixing = ((width, 3 * width), bf16)
    inner = ((length, hidden), bf16)
    lse = ((q_tiles, 8, 2 * TILE), f32)
    stat = ((length, LANES), f32)
    square = ((width, width), bf16)
    rising = ((width, hidden), bf16)
    falling = ((hidden, width), bf16)
    gain_rows = ((8, width), f32)

    def halves(ref, section_rows):
        return ref.at[pl.ds(0, section_rows)], ref.at[pl.ds(section_rows, section_rows)]

    meta = jnp.stack([flag, core, x, z]).astype(jnp.int32)
    documents = segment_ids[0, :, 0]
    own = [send(layer_input[0, micro, 0], to_row) for micro in range(micros)]
    docs_own = send(documents, to_row)
    docs_row = jnp.concatenate([docs_own, exchange(docs_own)], axis=1)
    docs_source = send(docs_row, to_decoder)
    other = [exchange(part) for part in own]

    def places_of(keys):
        return (
            dict(meta=meta, qd_s=docs_own, kd_s=keys),
            dict(
                qd=docs_own.astype(f32).reshape(micros, q_tiles, 1, TILE),
                kd=keys.astype(f32).reshape(micros, 1, 2 * length),
                gains=norm_gain[0],
            ),
        )

    plain = dict(meta=meta)
    scalars, small = places_of(docs_row)
    forward, memories, memories_other = [], [], []
    for micro in range(micros):
        call = launch(
            self_forward,
            micro,
            None,
            scalars,
            small,
            dict(
                x_own_h=own[micro],
                x_other_h=other[micro],
                w_mixed_h=attn_qkv[0],
                w_out_h=attn_out[0],
                w_in_h=ffn_in[0],
                w_down_h=ffn_out[0],
            ),
            dict(
                q_o=low,
                kv_o=keys_all,
                att_o=low,
                lse_o=lse,
                unit1_o=wide,
                inv1_o=stat,
                first_low_o=low,
                memory_o=low,
                ffn_low_o=low,
                act_o=inner,
                slope_o=inner,
                unit2_o=wide,
                inv2_o=stat,
            ),
            dict(
                **attention_scratch(length, width),
                **forward_scratch(length, width),
                x=both,
                w_mixed=mixing,
                w_out=square,
                w_in=rising,
                w_down=falling,
                unit1=wide,
                inv1=stat,
                first_low=low,
                memory=low,
                act=inner,
                slope=inner,
                unit2=wide,
                inv2=stat,
                sum=wide,
            ),
            24,
            26,
            after=(docs_source,) if micro == 0 else (forward[0].lse_o,),
        )
        forward.append(call)
        memories.append(send(call.memory_o, to_decoder))

    for micro in range(micros):
        arrived, _ = lax.optimization_barrier((memories[micro], forward[-1].lse_o))
        memories_other.append(exchange(arrived))
    cotangent, _ = lax.optimization_barrier((out_cotangent[:, 0], forward[0].lse_o))
    cotangent = send(cotangent, to_row)

    cross_scalars, cross_small = places_of(docs_source)
    cross, grads_memory, made = [], [], []
    after = (forward[-1].lse_o,)
    for micro in range(micros):
        done = forward[micro]
        call = launch(
            cross_both_ways,
            micro,
            1,
            cross_scalars,
            dict(**cross_small, cross_gain=cross_gain[None]),
            dict(
                memory_own_h=memories[micro],
                memory_other_h=memories_other[micro],
                w_pair_h=cross_pair,
                first_low_h=done.first_low_o,
                unit1_h=done.unit1_o,
                w_query_h=cross_query,
                w_cross_h=cross_out,
                w_in_h=ffn_in[0],
                w_down_h=ffn_out[0],
                cot_h=cotangent,
            ),
            dict(
                att_o=low,
                ffn_low_o=low,
                act_o=inner,
                decoded_o=low,
                down_grad_o=low,
                up_grad_o=inner,
                gain_grads_o=gain_rows,
                branch_o=low,
                dq_low_o=low,
                dkv_o=keys_all,
                part_own_o=wide,
                part_other_o=low,
                grad_first_o=wide,
            ),
            dict(
                **attention_scratch(length, width),
                **forward_scratch(length, width),
                **backward_scratch(length, width),
                x=both,
                w_pair=((width, 2 * width), bf16),
                first_low=low,
                unit1=wide,
                w_query=square,
                w_cross=square,
                w_in=rising,
                w_down=falling,
                cot=low,
                unit2=wide,
                inv2=stat,
                second_low=low,
                act=inner,
                slope=inner,
                sum=wide,
                decoded=low,
                keep=wide,
                down_grad=low,
                up_grad=inner,
                gain_grads=gain_rows,
                branch=low,
                part_own=wide,
            ),
            32,
            44,
            dict(act_o=done.act_o, ffn_low_o=done.ffn_low_o),
            after,
        )
        cross.append(call)
        away = call.part_other_o
        if micro:
            away, _ = lax.optimization_barrier((away, grads_memory[-1]))
        total = call.part_own_o + exchange(away).astype(f32)
        made.append(total.astype(bf16))
        after = (made[micro],)
        grads_memory.append(send(made[micro], to_encoder))

    def backward_feed(micro, after):
        done, late = forward[micro], cross[micro]
        return launch(
            feed_backward_alone,
            micro,
            0,
            plain,
            dict(gains=norm_gain[0]),
            dict(
                grad_memory_h=grads_memory[micro],
                unit2_h=done.unit2_o,
                inv2_h=done.inv2_o,
                slope_h=done.slope_o,
                w_in_h=ffn_in[0],
                w_down_h=ffn_out[0],
            ),
            dict(gain_late_o=gain_rows, down_grad_o=low, up_grad_o=inner, grad_first_o=wide),
            dict(
                cot=low,
                unit2=wide,
                inv2=stat,
                slope=inner,
                w_in=rising,
                w_down=falling,
                gain_grads=gain_rows,
                keep=wide,
                down_grad=low,
                up_grad=inner,
                sum=wide,
            ),
            12,
            10,
            dict(
                down_grad_o=late.down_grad_o, up_grad_o=late.up_grad_o, grad_first_o=late.grad_first_o
            ),
            after,
        )

    def backward_self(micro, side, grad_first, previous=None, after=(), halfway=None):
        done = forward[micro]
        heads = width // LANES
        given = dict(q_h=done.q_o, kv_h=done.kv_o, att_h=done.att_o, lse_h=done.lse_o)
        ahead = dict(
            grad_first_h=grad_first,
            unit1_h=done.unit1_o,
            inv1_h=done.inv1_o,
            w_out_h=attn_out[0],
        )
        makes = dict(dq_low_o=low, dkv_o=keys_all)
        makes_first = dict(gain_early_o=gain_rows, branch_o=low)
        makes_last = dict(part_own_o=wide, part_other_o=low)
        scratch = dict(
            **attention_scratch(length, width),
            **backward_scratch(length, width),
            w_out=square,
            w_mixed=mixing,
            unit1=wide,
            inv1=stat,
            keep=wide,
            branch=low,
            grad_att=low,
            gain_grads=gain_rows,
        )

        def part(first, last, large, outs, work, previous, after):
            return launch(
                self_backward,
                (micro, first, last),
                side,
                scalars,
                small,
                dict(**given, **large),
                dict(**makes, **outs),
                scratch,
                20,
                work,
                previous,
                after,
            )

        if halfway is None:
            large = dict(**ahead, w_mixed_h=attn_qkv[0])
            outs = dict(**makes_first, **makes_last)
            return part(0, heads, large, outs, 22, previous, after)
        outs = dict(**makes_first, grad_sum_o=wide, grad_att_o=low)
        one = part(0, heads // 2, ahead, outs, 12, None, after)
        large = dict(
            w_mixed_h=attn_qkv[0],
            grad_sum_h=one.grad_sum_o,
            grad_att_h=one.grad_att_o,
            dq_h=one.dq_low_o,
            dkv_h=one.dkv_o,
        )
        two = part(heads // 2, heads, large, makes_last, 12, None, halfway)
        return types.SimpleNamespace(**{**vars(one), **vars(two)})

    def weight_grads(plan, side, arrays, scratch, after=()):
        blocks = ((2, width, width), bf16)
        call = launch(
            contract_blocks,
            plan,
            side,
            plain,
            dict(),
            arrays,
            dict(sent_o=blocks, kept_o=blocks),
            dict(**scratch, blocks=((4, width, width), bf16)),
            24,
            8,
            after=after,
        )
        return call.sent_o, call.kept_o

    def first_sums(halves, section=None):
        sent, kept = halves
        got = send(sent, to_core, section)

        def block(side):
            return sum(
                lax.dynamic_index_in_dim(part, side, 0, keepdims=False).astype(f32)
                for part in (kept, got)
            )

        return block(1 - x).astype(bf16), block(x)

    def middle_sums(sums, section=None):
        away, total = sums
        return (total + send(away, to_x, section).astype(f32)).astype(bf16)

    def last_sums(total, section=None):
        shares = total.reshape(group, width // group, width)

        def share(step):
            return lax.dynamic_index_in_dim(shares, lax.rem(z + step, group), 0, keepdims=False)

        parts = [share(0)]
        for step in range(1, group):
            parts.append(send(share(step), along_z(step), section))
        return sum(part.astype(f32) for part in parts).astype(bf16)

    def along_z(step):
        return lambda t, i, k, c: (t, i, (k + step) % group, c)

    def gather(share, section=None):
        own = jnp.stack(
            [share] + [send(share, along_z(step), section) for step in range(1, group)]
        )
        return own, send(own, to_x, section)

    def gain_block(rows):
        filled = jnp.concatenate([jnp.stack(rows), jnp.zeros((16 - len(rows), width), f32)])
        return filled.astype(bf16)

    def spread(targets, own, own_x, outs, parts):
        return launch(
            spread_pieces,
            targets,
            None,
            plain,
            dict(),
            dict(own_h=own, own_x_h=own_x, other_h=exchange(own), other_x_h=exchange(own_x)),
            outs,
            dict(
                pieces=((4,) + own.shape, bf16),
                wide=((4 * group * parts, width // group, width), f32),
                gain_grads=((16, width), f32),
            ),
            8 + 4 * group * parts,
            5,
        )

    tokens, all_tokens = micros * length, 2 * micros * length
    turn, turn_all = ((width, tokens), bf16), ((width, all_tokens), bf16)
    narrow, narrow_all = ((tokens, width), bf16), ((all_tokens, width), bf16)
    pair_all = ((all_tokens, 2 * width), bf16)
    deep = ((tokens, hidden), bf16)

    def rows_of(first, second):
        starts = [halves(first, length), halves(second, length)]
        return [part[0] for part in starts] + [part[1] for part in starts]

    def cross_plan(r):
        return (
            [
                (r.low, (r.low0_h, r.low1_h)),
                (r.dq, (r.dq0_h, r.dq1_h)),
                (r.att, (r.att0_h, r.att1_h)),
                (r.branch, (r.branch0_h, r.branch1_h)),
                (r.mem, (r.mem0_h, r.mem1_h, r.mem2_h, r.mem3_h)),
                (r.pair, rows_of(r.pair0_h, r.pair1_h)),
            ],
            [
                (r.turn, r.low, 0, r.dq, 0),
                (r.turn_att, r.att, 0, r.branch, 0),
                (r.turn_all, r.mem, 0, r.pair, 0),
                (r.turn_all, r.mem, 0, r.pair, 1),
            ],
        )

    def rising_plan(r):
        return (
            [(r.low, (r.low0_h, r.low1_h)), (r.up, (r.up0_h, r.up1_h))],
            [(r.turn, r.low, 0, r.up, block) for block in range(4)],
        )

    def falling_plan(r):
        return (
            [(r.act, (r.act0_h, r.act1_h)), (r.down, (r.down0_h, r.down1_h))],
            [(r.turn, r.act, block, r.down, 0) for block in range(4)],
        )

    def self_plan(r):
        return (
            [
                (r.x, (r.x0_h, r.x1_h, r.x2_h, r.x3_h)),
                (r.dq, (r.dq0_h, r.dq1_h)),
                (r.pair, rows_of(r.pair0_h, r.pair1_h)),
                (r.att, (r.att0_h, r.att1_h)),
                (r.branch, (r.branch0_h, r.branch1_h)),
            ],
            [
                (r.turn_all, r.x, 0, r.dq, 0),
                (r.turn_all, r.x, 0, r.pair, 0),
                (r.turn_all, r.x, 0, r.pair, 1),
                (r.turn, r.att, 0, r.branch, 0),
            ],
        )

    last = micros - 1
    feeds, ends = [None] * micros, [None] * micros
    cross_halves = weight_grads(
        cross_plan,
        1,
        dict(
            low0_h=forward[0].first_low_o,
            low1_h=forward[1].first_low_o,
            dq0_h=cross[0].dq_low_o,
            dq1_h=cross[1].dq_low_o,
            att0_h=cross[0].att_o,
            att1_h=cross[1].att_o,
            branch0_h=cross[0].branch_o,
            branch1_h=cross[1].branch_o,
            mem0_h=memories[0],
            mem1_h=memories[1],
            mem2_h=memories_other[0],
            mem3_h=memories_other[1],
            pair0_h=cross[0].dkv_o,
            pair1_h=cross[1].dkv_o,
        ),
        dict(
            low=narrow,
            dq=narrow,
            att=narrow,
            branch=narrow,
            mem=narrow_all,
            pair=pair_all,
            turn=turn,
            turn_att=turn,
            turn_all=turn_all,
        ),
        (made[last],),
    )
    cross_sums = first_sums(cross_halves, 1)
    latest = made[last]
    for micro in range(last):
        feeds[micro] = backward_feed(micro, (latest,))
        first = feeds[micro].grad_first_o
        ends[micro] = backward_self(micro, 0, first)
        ends[micro] = backward_self(micro, 1, first, vars(ends[micro]), (cross_sums[0],))
        latest = ends[micro].gain_early_o
    cross_share = last_sums(middle_sums(cross_sums, 1), 1)
    feeds[last] = backward_feed(last, (latest,))

    rising_halves = weight_grads(
        rising_plan,
        None,
        dict(
            low0_h=cross[0].ffn_low_o,
            low1_h=cross[1].ffn_low_o,
            up0_h=feeds[0].up_grad_o,
            up1_h=feeds[1].up_grad_o,
        ),
        dict(low=narrow, up=deep, turn=turn),
    )
    falling_halves = weight_grads(
        falling_plan,
        None,
        dict(
            act0_h=cross[0].act_o,
            act1_h=cross[1].act_o,
            down0_h=feeds[0].down_grad_o,
            down1_h=feeds[1].down_grad_o,
        ),
        dict(act=deep, down=narrow, turn=turn),
        (rising_halves[0],),
    )
    rising_sums, falling_sums = first_sums(rising_halves), first_sums(falling_halves)
    third = sum(call.gain_grads_o[1] for call in cross)
    cross_own, cross_own_x = gather(jnp.concatenate([cross_share, gain_block([third])]), 1)

    def part_sum(micro):
        end = ends[micro]
        return (end.part_own_o + exchange(end.part_other_o).astype(f32)).astype(bf16)

    steps = [part_sum(micro) for micro in range(last)]
    rising_total = middle_sums(rising_sums)
    falling_total = middle_sums(falling_sums)
    ends[last] = backward_self(
        last,
        None,
        feeds[last].grad_first_o,
        None,
        (rising_sums[0], falling_sums[0]) + tuple(steps),
        (rising_total,),
    )
    rising_share, falling_share = last_sums(rising_total), last_sums(falling_total)

    self_halves = weight_grads(
        self_plan,
        None,
        dict(
            x0_h=own[0],
            x1_h=own[1],
            x2_h=other[0],
            x3_h=other[1],
            dq0_h=ends[0].dq_low_o,
            dq1_h=ends[1].dq_low_o,
            pair0_h=ends[0].dkv_o,
            pair1_h=ends[1].dkv_o,
            att0_h=forward[0].att_o,
            att1_h=forward[1].att_o,
            branch0_h=ends[0].branch_o,
            branch1_h=ends[1].branch_o,
        ),
        dict(
            x=narrow_all,
            dq=narrow,
            pair=pair_all,
            att=narrow,
            branch=narrow,
            turn=turn,
            turn_all=turn_all,
        ),
        (rising_share, falling_total),
    )
    self_share = last_sums(middle_sums(first_sums(self_halves)))
    steps.append(part_sum(last))

    feed_own, feed_own_x = gather(jnp.concatenate([rising_share, falling_share]))
    early = sum(end.gain_early_o[0] for end in ends)
    late = jnp.where(
        decoder,
        sum(call.gain_grads_o[0] for call in cross),
        sum(call.gain_late_o[0] for call in feeds),
    )
    self_own, self_own_x = gather(jnp.concatenate([self_share, gain_block([early, late])]))
    cross_own, cross_own_x = (
        jnp.where(decoder, part, send(part, to_encoder)) for part in (cross_own, cross_own_x)
    )

    def columns(block):
        return pl.ds(block * width, width)

    def feed_targets(r, block, row, rows):
        return [
            r.up_o.at[pl.ds(row, rows), columns(block)],
            r.down_o.at[pl.ds(block * width + row, rows)],
        ]

    def self_targets(r, block, row, rows):
        if block == 3:
            return [r.out_o.at[pl.ds(row, rows)]]
        return [r.mixed_o.at[pl.ds(row, rows), columns(block)]]

    def cross_targets(r, block, row, rows):
        if block >= 2:
            return [r.pair_o.at[pl.ds(row, rows), columns(block - 2)]]
        return [(r.out_o if block else r.query_o).at[pl.ds(row, rows)]]

    square_out, gains_out = ((width, width), f32), ((16, width), f32)
    cross_grads = spread(
        cross_targets,
        cross_own,
        cross_own_x,
        dict(query_o=square_out, pair_o=((width, 2 * width), f32), out_o=square_out, gains_o=gains_out),
        1,
    )
    feed_grads = spread(
        feed_targets,
        feed_own,
        feed_own_x,
        dict(up_o=((width, hidden), f32), down_o=((hidden, width), f32)),
        2,
    )
    self_grads = spread(
        self_targets,
        self_own,
        self_own_x,
        dict(mixed_o=((width, 3 * width), f32), out_o=square_out, gains_o=gains_out),
        1,
    )

    results = jnp.stack(
        [
            jnp.where(decoder, call.decoded_o, done.memory_o)
            for call, done in zip(cross, forward)
        ]
    )
    results = send(results, to_row)
    grad_input = jnp.stack([send(step, to_row) for step in steps])
    return (
        results[None, :, None],
        grad_input.astype(f32)[None, :, None],
        self_grads.mixed_o[None],
        self_grads.out_o[None],
        feed_grads.up_o[None],
        feed_grads.down_o[None],
        self_grads.gains_o[None, :2],
        cross_grads.query_o,
        cross_grads.pair_o,
        cross_grads.out_o,
        cross_grads.gains_o[0],
    )


def shards(*arrays):
    layer_input = arrays[0]
    micros, rows, length = layer_input.shape[1:4]
    simple = (
        lax.axis_size("section") == 2
        and lax.axis_size("seq") == 2
        and lax.axis_size("dp") in (4, 8, 16)
        and (micros, rows) == (2, 1)
        and length % TILE == 0
        and arrays[4].shape[-1] == 4 * layer_input.shape[-1] == 4 * CHUNK
    )
    return split_rows(*arrays) if simple else any_rows(*arrays)


def solution(mesh):
    in_specs = (
        P("section", None, "dp", "seq", None),
        P("section", None, "dp", "seq"),
        P("section", None, None),
        P("section", None, None),
        P("section", None, None),
        P("section", None, None),
        P("section", None, None),
        P(),
        P(),
        P(),
        P(),
        P(None, "dp", "seq", None),
    )
    out_specs = (
        P("section", None, "dp", "seq", None),
        P("section", None, "dp", "seq", None),
        P("section", None, None),
        P("section", None, None),
        P("section", None, None),
        P("section", None, None),
        P("section", None, None),
        P(),
        P(),
        P(),
        P(),
    )
    return jax.shard_map(shards, mesh=mesh, in_specs=in_specs, out_specs=out_specs, check_vma=False)
```

```python
import types

import jax
import jax.numpy as jnp
from jax import lax
from jax.experimental import pallas as pl
from jax.experimental.pallas import tpu as pltpu
from jax.sharding import PartitionSpec as P

HEADS = 8
TILE = 256
LANES = 128
CHUNK = 512

f32 = jnp.float32
bf16 = jnp.bfloat16
negative_big = -1e30
epsilon = 1e-05


def dot(left, right):
    return lax.dot_general(left, right, (((1,), (0,)), ((), ())), preferred_element_type=f32)


def dot_nt(left, right):
    return lax.dot_general(left, right, (((1,), (1,)), ((), ())), preferred_element_type=f32)


def dot_tn(left, right):
    return lax.dot_general(left, right, (((0,), (0,)), ((), ())), preferred_element_type=f32)


def standardize(values):
    center = values - jnp.mean(values, axis=-1, keepdims=True)
    inverse = lax.rsqrt(jnp.mean(center * center, axis=-1, keepdims=True) + epsilon)
    return center * inverse, inverse


def standardize_back(grad_out, standard, gain_row, inverse):
    scaled = grad_out * gain_row
    grad_in = inverse * (
        scaled
        - jnp.mean(scaled, axis=-1, keepdims=True)
        - standard * jnp.mean(scaled * standard, axis=-1, keepdims=True)
    )
    return grad_in, jnp.sum(grad_out * standard, axis=0, keepdims=True)


class Copies:
    def __init__(self, sems):
        self.sems = sems
        self.used = 0

    def start(self, source, target):
        copy = pltpu.make_async_copy(source, target, self.sems.at[self.used])
        self.used += 1
        copy.start()
        return copy


def wait_all(copies):
    for copy in copies:
        copy.wait()


def spread_pairs(target, source, factor, pairs):
    tiles = target.shape[1]
    half = lax.broadcasted_iota(jnp.int32, (TILE, LANES), 1) < LANES // 2
    first = jnp.where(half, factor, 0.0).astype(bf16)
    second = jnp.where(half, 0.0, factor).astype(bf16)
    for tile in range(tiles):
        for pair in pairs:
            block = source[tile * TILE : (tile + 1) * TILE, pair * LANES : (pair + 1) * LANES]
            target[pair, tile, :TILE, :] = block * first
            target[pair, tile, TILE:, :] = block * second


def turn_tiles(target, source, column, pairs):
    low, high = pairs[0] * LANES, (pairs[-1] + 1) * LANES
    for tile in range(target.shape[0]):
        block = source[tile * TILE : (tile + 1) * TILE, column + low : column + high]
        target[tile, low:high, :] = jnp.transpose(block)


def turn_documents(target, key_docs):
    for start in range(0, target.shape[0], LANES):
        row = key_docs[:, start : start + LANES]
        target[start : start + LANES, :] = jnp.transpose(jnp.broadcast_to(row, (LANES, LANES)))


def tile_place(r, core, causal, q_tile, k_tile):
    q_tiles = r.qd.shape[1]
    length = q_tiles * TILE
    owner = jnp.where(k_tile < q_tiles, core, 1 - core)
    k_start = owner * length + lax.rem(k_tile, q_tiles) * TILE
    ahead = core * length + q_tile * TILE - k_start
    ahead = jnp.where(causal == 1, ahead, 2 * length * TILE)
    q_low, q_high = r.qd_s[r.micro, q_tile * TILE], r.qd_s[r.micro, q_tile * TILE + TILE - 1]
    k_low, k_high = r.kd_s[r.micro, k_tile * TILE], r.kd_s[r.micro, k_tile * TILE + TILE - 1]
    active = (q_low <= k_high) & (k_low <= q_high) & (ahead > -TILE)
    return active, ahead


def fill_bias(r, q_tile, k_tile, ahead):
    keys = r.kdc[pl.ds(pl.multiple_of(k_tile * TILE, TILE), TILE), :]
    shift = lax.broadcasted_iota(jnp.int32, (TILE, LANES), 0) - lax.broadcasted_iota(
        jnp.int32, (TILE, LANES), 1
    )
    queries = r.qd[r.micro, q_tile]
    for start in range(0, TILE, LANES):
        same = keys == queries[:, start : start + LANES]
        allowed = same & (shift - start <= ahead)
        r.bias[:, start : start + LANES] = jnp.where(allowed, 0.0, negative_big)


def attention_forward(r, core, causal):
    pairs, q_tiles = r.qm.shape[:2]
    k_tiles = r.vt.shape[0]

    def one_query_tile(q_tile, carry):
        r.top[...] = jnp.full(r.top.shape, negative_big, f32)
        r.total[...] = jnp.zeros(r.total.shape, f32)
        r.turned[...] = jnp.zeros(r.turned.shape, f32)

        def one_key_tile(k_tile, inner):
            active, ahead = tile_place(r, core, causal, q_tile, k_tile)

            @pl.when(active)
            def _():
                fill_bias(r, q_tile, k_tile, ahead)
                rows = pl.ds(pl.multiple_of(k_tile * TILE, TILE), TILE)

                def raw(pair):
                    keys = r.kv[rows, pair * LANES : (pair + 1) * LANES]
                    return dot_nt(keys, r.qm[pair, q_tile])

                raw_next = raw(0)
                for pair in range(pairs):
                    bias = r.bias[...]
                    scores = raw_next + jnp.concatenate([bias, bias], axis=1)
                    if pair + 1 < pairs:
                        raw_next = raw(pair + 1)
                    old_top = r.top[pair : pair + 1, :]
                    new_top = jnp.maximum(old_top, jnp.max(scores, axis=0, keepdims=True))
                    weights = jnp.exp(scores - new_top)
                    shrink = jnp.exp(old_top - new_top)
                    r.top[pair : pair + 1, :] = new_top
                    r.total[pair : pair + 1, :] = r.total[
                        pair : pair + 1, :
                    ] * shrink + jnp.sum(weights, axis=0, keepdims=True)
                    low = weights.astype(bf16)
                    for side in range(2):
                        span = slice(side * TILE, (side + 1) * TILE)
                        head = slice((2 * pair + side) * 64, (2 * pair + side + 1) * 64)
                        r.turned[head, :] = r.turned[head, :] * shrink[:, span] + dot(
                            r.vt[k_tile, head, :], low[:, span]
                        )

            return inner

        lax.fori_loop(0, k_tiles, one_key_tile, 0)
        for pair in range(pairs):
            total = r.total[pair : pair + 1, :]
            r.lse[q_tile, pair : pair + 1, :] = r.top[pair : pair + 1, :] + jnp.log(total)
            share = 1.0 / total
            for side in range(2):
                span = slice(side * TILE, (side + 1) * TILE)
                head = slice((2 * pair + side) * 64, (2 * pair + side + 1) * 64)
                r.turned[head, :] = r.turned[head, :] * share[:, span]
        rows = pl.ds(pl.multiple_of(q_tile * TILE, TILE), TILE)
        r.att[rows, :] = jnp.transpose(r.turned[...]).astype(bf16)
        return carry

    lax.fori_loop(0, q_tiles, one_query_tile, 0)


def row_products(r, grad_att, pairs):
    low, high = pairs[0] * LANES, (pairs[-1] + 1) * LANES
    for tile in range(r.qm.shape[1]):
        rows = slice(tile * TILE, (tile + 1) * TILE)
        product = jnp.transpose(
            grad_att[rows, low:high].astype(f32) * r.att[rows, low:high].astype(f32)
        )
        for pair in pairs:
            for side in range(2):
                head = (2 * pair + side) * 64 - low
                r.delta[tile, pair : pair + 1, side * TILE : (side + 1) * TILE] = jnp.sum(
                    product[head : head + 64, :], axis=0, keepdims=True
                )


def attention_backward(r, core, causal, pairs):
    q_tiles, k_tiles = r.qm.shape[1], r.kt.shape[0]
    width = r.kt.shape[1]
    low, high = pairs[0] * LANES, (pairs[-1] + 1) * LANES
    for start in (0, width):
        r.dkv[:, start + low : start + high] = jnp.zeros((r.dkv.shape[0], high - low), f32)

    def one_query_tile(q_tile, carry):
        r.turned[low:high, :] = jnp.zeros((high - low, TILE), f32)

        def one_key_tile(k_tile, inner):
            active, ahead = tile_place(r, core, causal, q_tile, k_tile)

            @pl.when(active)
            def _():
                fill_bias(r, q_tile, k_tile, ahead)
                rows = pl.ds(pl.multiple_of(k_tile * TILE, TILE), TILE)

                def raw(pair):
                    lanes = slice(pair * LANES, (pair + 1) * LANES)
                    lanes_v = slice(width + pair * LANES, width + (pair + 1) * LANES)
                    return (
                        dot_nt(r.kv[rows, lanes], r.qm[pair, q_tile]),
                        dot_nt(r.kv[rows, lanes_v], r.gm[pair, q_tile]),
                    )

                raw_next = raw(pairs[0])
                for pair in pairs:
                    bias = r.bias[...]
                    scores, grad_probs = raw_next
                    scores = scores + jnp.concatenate([bias, bias], axis=1)
                    if pair < pairs[-1]:
                        raw_next = raw(pair + 1)
                    probs = jnp.exp(scores - r.lse[q_tile, pair : pair + 1, :])
                    grad_scores = probs * (grad_probs - r.delta[q_tile, pair : pair + 1, :])
                    probs_low = probs.astype(bf16)
                    grad_low = grad_scores.astype(bf16)
                    lanes = slice(pair * LANES, (pair + 1) * LANES)
                    lanes_v = slice(width + pair * LANES, width + (pair + 1) * LANES)
                    r.dkv[rows, lanes] += dot(grad_low, r.qm[pair, q_tile])
                    r.dkv[rows, lanes_v] += dot(probs_low, r.gm[pair, q_tile])
                    for side in range(2):
                        span = slice(side * TILE, (side + 1) * TILE)
                        head = slice((2 * pair + side) * 64, (2 * pair + side + 1) * 64)
                        r.turned[head, :] += dot(r.kt[k_tile, head, :], grad_low[:, span])

            return inner

        lax.fori_loop(0, k_tiles, one_key_tile, 0)
        rows = pl.ds(pl.multiple_of(q_tile * TILE, TILE), TILE)
        r.dq[rows, low:high] = jnp.transpose(r.turned[low:high, :]) * (64**-0.5)
        return carry

    lax.fori_loop(0, q_tiles, one_query_tile, 0)


def feed_forward(r, low):
    r.sum[...] = jnp.zeros(r.sum.shape, f32)

    def one_chunk(chunk, carry):
        span = pl.ds(pl.multiple_of(chunk * CHUNK, CHUNK), CHUNK)
        upward = dot(low[...], r.w_in[:, span])
        gate = jax.nn.sigmoid(upward)
        active = (upward * gate).astype(bf16)
        r.act[:, span] = active
        r.slope[:, span] = (gate + upward * gate * (1.0 - gate)).astype(r.slope.dtype)
        r.sum[...] += dot(active, r.w_down[span, :])
        return carry

    lax.fori_loop(0, r.w_in.shape[1] // CHUNK, one_chunk, 0)


def feed_backward(r):
    r.sum[...] = jnp.zeros(r.sum.shape, f32)

    def one_chunk(chunk, carry):
        span = pl.ds(pl.multiple_of(chunk * CHUNK, CHUNK), CHUNK)
        grad_active = dot_nt(r.down_grad[...], r.w_down[span, :]).astype(bf16)
        grad_up = (grad_active.astype(f32) * r.slope[:, span].astype(f32)).astype(bf16)
        r.up_grad[:, span] = grad_up
        r.sum[...] += dot_nt(grad_up, r.w_in[:, span])
        return carry

    lax.fori_loop(0, r.w_in.shape[1] // CHUNK, one_chunk, 0)


def self_forward(r):
    length, width = r.x_own_h.shape
    decoder, core = r.meta[0], r.meta[1]
    move = Copies(r.sems)
    early = [
        move.start(r.x_own_h, r.x.at[pl.ds(0, length)]),
        move.start(r.x_other_h, r.x.at[pl.ds(length, length)]),
        move.start(r.w_mixed_h, r.w_mixed),
    ]
    later = [
        move.start(r.w_out_h, r.w_out),
        move.start(r.w_in_h, r.w_in),
        move.start(r.w_down_h, r.w_down),
    ]
    turn_documents(r.kdc, r.kd[r.micro])
    wait_all(early)
    r.q[...] = dot(r.x[:length, :], r.w_mixed[:, :width]).astype(bf16)
    r.kv[...] = dot(r.x[...], r.w_mixed[:, width:]).astype(bf16)
    outs = [move.start(r.q, r.q_o), move.start(r.kv, r.kv_o)]
    pairs = range(width // LANES)
    spread_pairs(r.qm, r.q, 64**-0.5, pairs)
    turn_tiles(r.vt, r.kv, width, pairs)
    attention_forward(r, core, decoder)
    wait_all(later)
    outs += [move.start(r.att, r.att_o), move.start(r.lse, r.lse_o)]
    unit, inverse = standardize(r.x[:length, :].astype(f32) + dot(r.att[...], r.w_out[...]))
    r.unit1[...] = unit
    r.inv1[...] = jnp.broadcast_to(inverse, r.inv1.shape)
    r.first_low[...] = (unit * r.gains[0:1, :]).astype(bf16)
    outs += [
        move.start(r.unit1, r.unit1_o),
        move.start(r.inv1, r.inv1_o),
        move.start(r.first_low, r.first_low_o),
    ]

    @pl.when(decoder == 0)
    def _():
        feed_forward(r, r.first_low)
        late = [
            move.start(r.first_low, r.ffn_low_o),
            move.start(r.act, r.act_o),
            move.start(r.slope, r.slope_o),
        ]
        unit2, inverse2 = standardize(r.unit1[...] * r.gains[0:1, :] + r.sum[...])
        r.memory[...] = (unit2 * r.gains[1:2, :]).astype(bf16)
        late += [move.start(r.memory, r.memory_o)]
        r.unit2[...] = unit2
        r.inv2[...] = jnp.broadcast_to(inverse2, r.inv2.shape)
        late += [move.start(r.unit2, r.unit2_o), move.start(r.inv2, r.inv2_o)]
        wait_all(late)

    wait_all(outs)


def cross_both_ways(r):
    length, width = r.unit1_h.shape
    core = r.meta[1]
    move = Copies(r.sems)
    moves = [
        move.start(r.memory_own_h, r.x.at[pl.ds(0, length)]),
        move.start(r.memory_other_h, r.x.at[pl.ds(length, length)]),
        move.start(r.w_pair_h, r.w_pair),
        move.start(r.first_low_h, r.first_low),
        move.start(r.w_query_h, r.w_query),
    ]
    later = [
        move.start(r.unit1_h, r.unit1),
        move.start(r.w_cross_h, r.w_cross),
        move.start(r.w_in_h, r.w_in),
        move.start(r.w_down_h, r.w_down),
        move.start(r.cot_h.at[r.micro], r.cot),
    ]
    turn_documents(r.kdc, r.kd[r.micro])
    wait_all(moves)
    r.kv[...] = dot(r.x[...], r.w_pair[...]).astype(bf16)
    r.q[...] = dot(r.first_low[...], r.w_query[...]).astype(bf16)
    pairs = range(width // LANES)
    spread_pairs(r.qm, r.q, 64**-0.5, pairs)
    turn_tiles(r.vt, r.kv, width, pairs)
    turn_tiles(r.kt, r.kv, 0, pairs)
    attention_forward(r, core, 0)
    outs = [move.start(r.att, r.att_o)]
    wait_all(later)
    first = r.unit1[...] * r.gains[0:1, :]
    unit, inverse = standardize(first + dot(r.att[...], r.w_cross[...]))
    r.unit2[...] = unit
    r.inv2[...] = jnp.broadcast_to(inverse, r.inv2.shape)
    r.second_low[...] = (unit * r.cross_gain[...]).astype(bf16)
    outs += [move.start(r.second_low, r.ffn_low_o)]
    feed_forward(r, r.second_low)
    outs += [move.start(r.act, r.act_o)]
    unit3, inverse3 = standardize(r.unit2[...] * r.cross_gain[...] + r.sum[...])
    r.decoded[...] = (unit3 * r.gains[1:2, :]).astype(bf16)
    outs += [move.start(r.decoded, r.decoded_o)]
    grad_third, gain_late = standardize_back(
        r.cot[...].astype(f32), unit3, r.gains[1:2, :], inverse3
    )
    r.keep[...] = grad_third
    r.down_grad[...] = grad_third.astype(bf16)
    outs += [move.start(r.down_grad, r.down_grad_o)]
    feed_backward(r)
    outs += [move.start(r.up_grad, r.up_grad_o)]
    grad_sum, gain_cross = standardize_back(
        r.keep[...] + r.sum[...], r.unit2[...], r.cross_gain[...], r.inv2[:, 0:1]
    )
    r.gain_grads[...] = jnp.zeros(r.gain_grads.shape, f32)
    r.gain_grads[0:1, :] = gain_late
    r.gain_grads[1:2, :] = gain_cross
    r.keep[...] = grad_sum
    r.branch[...] = grad_sum.astype(bf16)
    outs += [move.start(r.gain_grads, r.gain_grads_o), move.start(r.branch, r.branch_o)]
    r.q[...] = dot_nt(r.branch[...], r.w_cross[...]).astype(bf16)
    spread_pairs(r.gm, r.q, 1.0, pairs)
    row_products(r, r.q, pairs)
    attention_backward(r, core, 0, pairs)
    r.dq_low[...] = r.dq[...].astype(bf16)
    r.keep[...] += dot_nt(r.dq_low[...], r.w_query[...])
    outs += [move.start(r.dq_low, r.dq_low_o), move.start(r.keep, r.grad_first_o)]
    r.dkv_low[...] = r.dkv[...].astype(bf16)
    outs += [move.start(r.dkv_low, r.dkv_o)]
    part = dot_nt(r.dkv_low[...], r.w_pair[...])
    r.part_other[...] = part[length:, :].astype(bf16)
    r.part_own[...] = part[:length, :]
    outs += [move.start(r.part_other, r.part_other_o), move.start(r.part_own, r.part_own_o)]
    wait_all(outs)


def feed_backward_alone(r):
    move = Copies(r.sems)
    early = [
        move.start(r.grad_memory_h, r.cot),
        move.start(r.unit2_h, r.unit2),
        move.start(r.inv2_h, r.inv2),
    ]
    later = [
        move.start(r.w_down_h, r.w_down),
        move.start(r.slope_h, r.slope),
        move.start(r.w_in_h, r.w_in),
    ]
    wait_all(early)
    grad_third, gain_late = standardize_back(
        r.cot[...].astype(f32), r.unit2[...], r.gains[1:2, :], r.inv2[:, 0:1]
    )
    r.gain_grads[...] = jnp.broadcast_to(gain_late, r.gain_grads.shape)
    r.keep[...] = grad_third
    r.down_grad[...] = grad_third.astype(bf16)
    outs = [move.start(r.down_grad, r.down_grad_o), move.start(r.gain_grads, r.gain_late_o)]
    wait_all(later)
    feed_backward(r)
    outs += [move.start(r.up_grad, r.up_grad_o)]
    r.keep[...] += r.sum[...]
    outs += [move.start(r.keep, r.grad_first_o)]
    wait_all(outs)


def self_backward(r, plan):
    r.micro, first, last = plan
    length, width = r.att_h.shape
    decoder, core = r.meta[0], r.meta[1]
    pairs = range(first, last)
    low, high = first * LANES, last * LANES
    move = Copies(r.sems)
    later = [
        move.start(r.q_h, r.q),
        move.start(r.kv_h, r.kv),
        move.start(r.att_h, r.att),
        move.start(r.lse_h, r.lse),
    ]
    if first == 0:
        early = [
            move.start(r.grad_first_h, r.keep),
            move.start(r.unit1_h, r.unit1),
            move.start(r.inv1_h, r.inv1),
            move.start(r.w_out_h, r.w_out),
        ]
    else:
        early = [move.start(r.grad_att_h, r.grad_att)]
    outs = []
    turn_documents(r.kdc, r.kd[r.micro])
    wait_all(early)
    if first == 0:
        grad_sum, gain_early = standardize_back(
            r.keep[...], r.unit1[...], r.gains[0:1, :], r.inv1[:, 0:1]
        )
        r.gain_grads[...] = jnp.broadcast_to(gain_early, r.gain_grads.shape)
        r.keep[...] = grad_sum
        r.branch[...] = grad_sum.astype(bf16)
        r.grad_att[...] = dot_nt(r.branch[...], r.w_out[...]).astype(bf16)
        outs += [move.start(r.gain_grads, r.gain_early_o), move.start(r.branch, r.branch_o)]
        if last < width // LANES:
            outs += [move.start(r.keep, r.grad_sum_o), move.start(r.grad_att, r.grad_att_o)]
    wait_all(later)
    if last == width // LANES:
        ends = [move.start(r.w_mixed_h, r.w_mixed)]
        if first > 0:
            ends += [
                move.start(r.grad_sum_h, r.keep),
                move.start(r.dq_h.at[:, pl.ds(0, low)], r.dq_low.at[:, pl.ds(0, low)]),
                move.start(r.dkv_h.at[:, pl.ds(0, low)], r.dkv_low.at[:, pl.ds(0, low)]),
                move.start(
                    r.dkv_h.at[:, pl.ds(width, low)], r.dkv_low.at[:, pl.ds(width, low)]
                ),
            ]
    spread_pairs(r.qm, r.q, 64**-0.5, pairs)
    turn_tiles(r.kt, r.kv, 0, pairs)
    spread_pairs(r.gm, r.grad_att, 1.0, pairs)
    row_products(r, r.grad_att, pairs)
    attention_backward(r, core, decoder, pairs)
    r.dq_low[:, low:high] = r.dq[:, low:high].astype(bf16)
    for start in (0, width):
        span = slice(start + low, start + high)
        r.dkv_low[:, span] = r.dkv[:, span].astype(bf16)
    if last == width // LANES:
        wait_all(ends)
        outs += [move.start(r.dq_low, r.dq_low_o), move.start(r.dkv_low, r.dkv_o)]
        r.keep[...] += dot_nt(r.dq_low[...], r.w_mixed[:, :width])
        part = dot_nt(r.dkv_low[...], r.w_mixed[:, width:])
        r.part_other[...] = part[length:, :].astype(bf16)
        r.keep[...] += part[:length, :]
        outs += [move.start(r.part_other, r.part_other_o), move.start(r.keep, r.part_own_o)]
    else:
        outs.append(move.start(r.dq_low.at[:, pl.ds(low, high - low)], r.dq_low_o.at[:, pl.ds(low, high - low)]))
        for start in (0, width):
            span = pl.ds(start + low, high - low)
            outs.append(move.start(r.dkv_low.at[:, span], r.dkv_o.at[:, span]))
    wait_all(outs)


def contract_blocks(r, plan):
    operands, blocks = plan(r)
    for core in range(2):

        @pl.when(r.meta[1] == core)
        def _(core=core):
            targets = [None] * 4
            for half in range(2):
                target = r.kept_o if half == core else r.sent_o
                targets[2 * half], targets[2 * half + 1] = target.at[0], target.at[1]
            contract_in_order(r, operands, blocks, (1 - core, core), targets)


def contract_cross(r, plan):
    operands, blocks = plan(r)
    width = r.all_o.shape[1]
    extra = r.all_o.at[pl.ds(4 * width, 16)]

    @pl.when(r.meta[0] == 1)
    def _():
        move = Copies(r.sems)
        wait_all([move.start(r.gain0_h, r.gain0), move.start(r.gain1_h, r.gain1)])
        gain = (r.gain0[1:2, :] + r.gain1[1:2, :]).astype(bf16)
        r.extra[...] = jnp.broadcast_to(gain, r.extra.shape)
        wait_all([move.start(r.extra, extra)])
        targets = [r.all_o.at[pl.ds(block * width, width)] for block in range(4)]
        contract_in_order(r, operands, blocks, (0, 1), targets, move)

    @pl.when(r.meta[0] == 0)
    def _():
        r.blocks[0] = jnp.zeros((width, width), bf16)
        r.extra[...] = jnp.zeros(r.extra.shape, bf16)
        move = Copies(r.sems)
        outs = [move.start(r.extra, extra)]
        for block in range(4):
            outs.append(move.start(r.blocks.at[0], r.all_o.at[pl.ds(block * width, width)]))
        wait_all(outs)


def contract_in_order(r, operands, blocks, halves, targets, move=None):
    move = move or Copies(r.sems)
    loads = []
    for target, sources in operands:
        row = 0
        for source in sources:
            loads.append(move.start(source, target.at[pl.ds(row, source.shape[0])]))
            row += source.shape[0]
    wait_all(loads)
    outs = []
    held = dict()
    for half in halves:
        for place in range(2):
            slot = 2 * half + place
            turn, left, left_at, right, right_at = blocks[slot]
            if held.get(id(turn)) != left_at:
                for row in range(0, left.shape[0], CHUNK):
                    block = left[row : row + CHUNK, left_at * CHUNK : (left_at + 1) * CHUNK]
                    turn[:, row : row + CHUNK] = jnp.transpose(block)
                held[id(turn)] = left_at
            block = right[:, right_at * CHUNK : (right_at + 1) * CHUNK]
            r.blocks[slot] = dot(turn[:, : right.shape[0]], block).astype(bf16)
            outs.append(move.start(r.blocks.at[slot], targets[slot]))
    wait_all(outs)


def spread_pieces(r, targets):
    z = r.meta[3]
    group, height = r.own_h.shape[:2]
    rows = r.own_h.shape[2] // group
    for core in range(2):
        for x in range(2):

            @pl.when((r.meta[1] == core) & (r.meta[2] == x))
            def _(core=core, x=x):
                move = Copies(r.sems)
                parts = [
                    (r.own_h, core, x),
                    (r.own_x_h, core, 1 - x),
                    (r.other_h, 1 - core, x),
                    (r.other_x_h, 1 - core, 1 - x),
                ]
                loads = [
                    move.start(source, r.pieces.at[place])
                    for place, (source, _, _) in enumerate(parts)
                ]
                outs = []
                slot = 0
                gains = None
                for place, (_, half, side) in enumerate(parts):
                    loads[place].wait()
                    for step in range(group):
                        row = pl.multiple_of(lax.rem(z + (group - step), group) * rows, rows)
                        start = 0
                        for target in targets(r, 2 * half + side, row, rows):
                            r.wide[slot] = r.pieces[place, step, start : start + rows].astype(f32)
                            outs.append(move.start(r.wide.at[slot], target))
                            slot += 1
                            start += rows
                        if start < height:
                            extra = r.pieces[place, step, start:height].astype(f32)
                            gains = extra if gains is None else gains + extra
                if gains is not None:
                    r.gain_grads[...] = gains
                    outs.append(move.start(r.gain_grads, r.gains_o))
                wait_all(outs)


def launch(kernel, plan, side, scalars, small, large, outs, scratch, copies, work, previous=None, after=()):
    names = list(scalars) + list(small) + list(large)
    arrays = list(scalars.values()) + list(small.values()) + list(large.values())
    specs = (
        [pl.BlockSpec(memory_space=pltpu.SMEM)] * len(scalars)
        + [pl.BlockSpec(memory_space=pltpu.VMEM)] * len(small)
        + [pl.BlockSpec(memory_space=pl.ANY)] * len(large)
    )
    aliases = dict()
    for position, name in enumerate(outs):
        if previous and name in previous:
            aliases[len(arrays)] = position
            names.append("previous_" + name)
            arrays.append(previous[name])
            specs.append(pl.BlockSpec(memory_space=pl.ANY))
    for array in after:
        names.append("")
        arrays.append(array)
        specs.append(pl.BlockSpec(memory_space=pl.ANY))
    names += list(outs) + list(scratch) + ["sems"]

    def body(*refs):
        r = types.SimpleNamespace(**dict(zip(names, refs)))

        def run():
            if isinstance(plan, int):
                r.micro = plan
                kernel(r)
            else:
                kernel(r, plan)

        if side is None:
            run()
        else:
            pl.when(r.meta[0] == side)(run)

    results = pl.pallas_call(
        body,
        out_shape=[jax.ShapeDtypeStruct(*shape) for shape in outs.values()],
        in_specs=specs,
        out_specs=[pl.BlockSpec(memory_space=pl.ANY)] * len(outs),
        scratch_shapes=[pltpu.VMEM(*shape) for shape in scratch.values()]
        + [pltpu.SemaphoreType.DMA((copies,))],
        input_output_aliases=aliases,
        compiler_params=pltpu.CompilerParams(vmem_limit_bytes=58 * 1024 * 1024),
        cost_estimate=pl.CostEstimate(
            flops=work * 10**9, bytes_accessed=1 << 20, transcendentals=0
        ),
    )(*arrays)
    return types.SimpleNamespace(**dict(zip(outs, results)))


def attention_scratch(length, width):
    pairs, q_tiles, k_tiles = width // LANES, length // TILE, 2 * length // TILE
    return dict(
        q=((length, width), bf16),
        kv=((2 * length, 2 * width), bf16),
        qm=((pairs, q_tiles, 2 * TILE, LANES), bf16),
        kdc=((2 * length, LANES), f32),
        bias=((TILE, TILE), f32),
        lse=((q_tiles, 8, 2 * TILE), f32),
        att=((length, width), bf16),
        turned=((width, TILE), f32),
    )


def forward_scratch(length, width):
    k_tiles = 2 * length // TILE
    return dict(
        vt=((k_tiles, width, TILE), bf16),
        top=((8, 2 * TILE), f32),
        total=((8, 2 * TILE), f32),
    )


def backward_scratch(length, width):
    pairs, q_tiles, k_tiles = width // LANES, length // TILE, 2 * length // TILE
    return dict(
        kt=((k_tiles, width, TILE), bf16),
        gm=((pairs, q_tiles, 2 * TILE, LANES), bf16),
        delta=((q_tiles, 8, 2 * TILE), f32),
        dkv=((2 * length, 2 * width), f32),
        dq=((length, width), f32),
        dkv_low=((2 * length, 2 * width), bf16),
        part_other=((length, width), bf16),
        dq_low=((length, width), bf16),
    )


def for_sending(shard):

    def short(part):
        return part.astype(jnp.bfloat16) if part.dtype == jnp.float32 else part

    return jax.tree.map(short, shard)


def from_behind(block, axis, distance):
    devices = range(lax.axis_size(axis))
    route = [(i - distance, i) for i in devices if i - distance in devices]
    return lax.ppermute(block, axis, route)


def from_root(shard, axis, root):
    mine = lax.axis_index(axis) == root
    return lax.psum(jnp.where(mine, shard, jnp.zeros_like(shard)), axis)


def matmul(left_side, right_side):
    return jnp.einsum("rsd,de->rse", left_side, right_side, preferred_element_type=jnp.float32)


def matmul_back(left_side, right_side):
    return jnp.einsum("rse,de->rsd", left_side, right_side, preferred_element_type=jnp.float32)


def contract(left_side, right_side):
    return jnp.einsum("rsd,rse->de", left_side, right_side, preferred_element_type=jnp.float32)


def normalize(values, gain_row):
    center = values - jnp.mean(values, axis=-1, keepdims=True)
    inverse = lax.rsqrt(jnp.mean(center * center, axis=-1, keepdims=True) + epsilon)
    standard = center * inverse
    return (standard * gain_row, standard, inverse)


def normalize_back(grad_out, standard, gain_row, inverse):
    scaled = grad_out * gain_row
    grad_in = inverse * (
        scaled
        - jnp.mean(scaled, axis=-1, keepdims=True)
        - standard * jnp.mean(scaled * standard, axis=-1, keepdims=True)
    )
    return (grad_in, jnp.sum(grad_out * standard, axis=(0, 1)))


def allowed_mask(query_docs, key_docs, query_place, key_place, causal):
    same_doc = query_docs[:, :, None] == key_docs[:, None, :]
    earlier = query_place[:, None] >= key_place[None, :]
    return (same_doc & (earlier | jnp.logical_not(causal)))[:, None]


def attend(queries, keys_local, values_local, query_docs, key_docs, causal, is_cross):
    rows_here, shard_len, model_width = queries.shape
    head_dim = model_width // HEADS
    score_scale = head_dim ** (-0.5)
    query_place = lax.axis_index("seq") * shard_len + jnp.arange(shard_len)
    query_heads = queries.reshape(rows_here, shard_len, HEADS, head_dim)

    def absorb(state_tuple, pieces):
        running_top, running_total, running_sum = state_tuple
        key_piece, value_piece, doc_piece = pieces
        piece_len = key_piece.shape[1]
        raw_scores = jnp.einsum(
            "rqhd,rkhd->rhqk",
            query_heads,
            key_piece.reshape(rows_here, piece_len, HEADS, head_dim),
            preferred_element_type=jnp.float32,
        )
        allowed = allowed_mask(query_docs, doc_piece, query_place, jnp.arange(piece_len), causal)
        scores = jnp.where(allowed, raw_scores * score_scale, negative_big)
        new_top = jnp.maximum(running_top, jnp.max(scores, axis=-1))
        weights = jnp.where(allowed, jnp.exp(scores - new_top[..., None]), 0.0)
        new_total = jnp.sum(weights, axis=-1)
        product = jnp.einsum(
            "rhqk,rkhd->rhqd",
            weights.astype(jnp.bfloat16),
            value_piece.reshape(rows_here, piece_len, HEADS, head_dim),
            preferred_element_type=jnp.float32,
        )
        return (new_top, new_total, product)

    init_state = (
        jnp.full((rows_here, HEADS, shard_len), negative_big, jnp.float32),
        jnp.zeros((rows_here, HEADS, shard_len), jnp.float32),
        jnp.zeros((rows_here, HEADS, shard_len, head_dim), jnp.float32),
    )
    if is_cross:
        final_top, final_total, final_sum = absorb(
            init_state,
            (
                lax.all_gather(keys_local, "seq", axis=1, tiled=True),
                lax.all_gather(values_local, "seq", axis=1, tiled=True),
                lax.all_gather(for_sending(key_docs), "seq", axis=1, tiled=True),
            ),
        )
    else:
        final_top, final_total, final_sum = absorb(
            init_state,
            (
                lax.all_gather(keys_local, "seq", axis=1, tiled=True),
                lax.all_gather(values_local, "seq", axis=1, tiled=True),
                lax.all_gather(key_docs, "seq", axis=1, tiled=True),
            ),
        )
    attended = (
        (final_sum / final_total[..., None])
        .transpose(0, 2, 1, 3)
        .reshape(rows_here, shard_len, model_width)
    )
    return (attended, final_top + jnp.log(final_total))


def attend_back(
    queries,
    keys_local,
    values_local,
    query_docs,
    key_docs,
    causal,
    log_total,
    grad_attended,
    is_cross,
):
    rows_here, shard_len, model_width = queries.shape
    head_dim = model_width // HEADS
    score_scale = head_dim ** (-0.5)
    query_place = lax.axis_index("seq") * shard_len + jnp.arange(shard_len)
    if is_cross:
        keys_full, values_full, docs_full = (
            lax.all_gather(keys_local, "seq", axis=1, tiled=True),
            lax.all_gather(values_local, "seq", axis=1, tiled=True),
            lax.all_gather(for_sending(key_docs), "seq", axis=1, tiled=True).astype(key_docs.dtype),
        )
    else:
        keys_full, values_full, docs_full = (
            lax.all_gather(keys_local, "seq", axis=1, tiled=True),
            lax.all_gather(values_local, "seq", axis=1, tiled=True),
            lax.all_gather(key_docs, "seq", axis=1, tiled=True),
        )
    full_len = keys_full.shape[1]
    query_heads = queries.reshape(rows_here, shard_len, HEADS, head_dim)
    key_heads = keys_full.reshape(rows_here, full_len, HEADS, head_dim)
    value_heads = values_full.reshape(rows_here, full_len, HEADS, head_dim)
    grad_heads = grad_attended.reshape(rows_here, shard_len, HEADS, head_dim)
    raw_scores = jnp.einsum(
        "rqhd,rkhd->rhqk", query_heads, key_heads, preferred_element_type=jnp.float32
    )
    allowed = allowed_mask(query_docs, docs_full, query_place, jnp.arange(full_len), causal)
    shifted = jnp.where(allowed, raw_scores * score_scale - log_total[..., None], negative_big)
    probs = jnp.where(allowed, jnp.exp(shifted), 0.0)
    grad_probs = jnp.einsum(
        "rqhd,rkhd->rhqk", grad_heads, value_heads, preferred_element_type=jnp.float32
    )
    delta = jnp.sum(probs * grad_probs, axis=-1)
    grad_scores = (probs * (grad_probs - delta[..., None]) * score_scale).astype(jnp.bfloat16)
    grad_queries = jnp.einsum(
        "rhqk,rkhd->rqhd", grad_scores, key_heads, preferred_element_type=jnp.float32
    ).reshape(rows_here, shard_len, model_width)
    probs_low = probs.astype(jnp.bfloat16)

    def key_terms(span):
        grad_keys = jnp.einsum(
            "rhqk,rqhd->krhd", grad_scores, query_heads, preferred_element_type=jnp.float32
        )
        grad_values = jnp.einsum(
            "rhqk,rqhd->krhd", probs_low, grad_heads, preferred_element_type=jnp.float32
        )
        return jnp.concatenate(
            [
                grad_keys.reshape(span, rows_here, model_width),
                grad_values.reshape(span, rows_here, model_width),
            ],
            axis=-1,
        )

    if is_cross:
        pair_terms = lax.psum_scatter(
            key_terms(shard_len * lax.axis_size("seq")).astype(jnp.bfloat16),
            "seq",
            scatter_dimension=0,
            tiled=True,
        ).astype(jnp.float32)
    else:
        pair_terms = lax.psum_scatter(
            key_terms(shard_len * lax.axis_size("seq")).astype(jnp.bfloat16),
            "seq",
            scatter_dimension=0,
            tiled=True,
        ).astype(jnp.float32)
    return (grad_queries, pair_terms.transpose(1, 0, 2))


def layer_forward(hidden_in, doc_own, memory, memory_docs, weights, is_decoder):
    (
        qkv_weight,
        out_weight,
        in_weight,
        down_weight,
        gains_pair,
        query_weight,
        pair_weight,
        cross_weight,
        cross_gains,
    ) = weights
    model_width = hidden_in.shape[-1]
    mixed = matmul(hidden_in, qkv_weight).astype(jnp.bfloat16)
    attended, self_lse = attend(
        mixed[..., :model_width],
        mixed[..., model_width : 2 * model_width],
        mixed[..., 2 * model_width :],
        doc_own,
        doc_own,
        is_decoder,
        False,
    )
    attended = attended.astype(jnp.bfloat16)
    first, first_unit, first_inv = normalize(
        hidden_in.astype(jnp.float32) + matmul(attended, out_weight), gains_pair[0]
    )
    first_low = first.astype(jnp.bfloat16)
    cross_queries = matmul(first_low, query_weight).astype(jnp.bfloat16)
    pair = matmul(memory, pair_weight).astype(jnp.bfloat16)
    cross_att, cross_lse = attend(
        cross_queries,
        pair[..., :model_width],
        pair[..., model_width:],
        doc_own,
        memory_docs,
        False,
        True,
    )
    cross_att = cross_att.astype(jnp.bfloat16)
    second_cross, second_unit, second_inv = normalize(
        first + matmul(cross_att, cross_weight), cross_gains
    )
    second = jnp.where(is_decoder, second_cross, first)
    second_low = second.astype(jnp.bfloat16)
    upward = matmul(second_low, in_weight)
    active = jax.nn.silu(upward).astype(jnp.bfloat16)
    result, third_unit, third_inv = normalize(second + matmul(active, down_weight), gains_pair[1])
    saved = {
        "mixed": mixed,
        "attended": attended,
        "self_lse": self_lse,
        "first_unit": first_unit,
        "first_inv": first_inv,
        "first_low": first_low,
        "cross_queries": cross_queries,
        "pair": pair,
        "cross_att": cross_att,
        "cross_lse": cross_lse,
        "second_unit": second_unit,
        "second_inv": second_inv,
        "second_low": second_low,
        "upward": upward,
        "active": active,
        "third_unit": third_unit,
        "third_inv": third_inv,
    }
    return (result, saved)


def layer_backward(
    grad_result, saved, hidden_in, doc_own, memory, memory_docs, weights, is_decoder
):
    (
        qkv_weight,
        out_weight,
        in_weight,
        down_weight,
        gains_pair,
        query_weight,
        pair_weight,
        cross_weight,
        cross_gains,
    ) = weights
    model_width = hidden_in.shape[-1]
    grad_third, grad_gain_late = normalize_back(
        grad_result, saved["third_unit"], gains_pair[1], saved["third_inv"]
    )
    down_grad = grad_third.astype(jnp.bfloat16)
    grad_down_w = contract(saved["active"], down_grad)
    grad_active = matmul_back(down_grad, down_weight).astype(jnp.bfloat16)
    sigmoid_up = jax.nn.sigmoid(saved["upward"])
    grad_upward = (
        grad_active.astype(jnp.float32)
        * (sigmoid_up + saved["upward"] * sigmoid_up * (1.0 - sigmoid_up))
    ).astype(jnp.bfloat16)
    grad_in_w = contract(saved["second_low"], grad_upward)
    grad_second = grad_third + matmul_back(grad_upward, in_weight)
    grad_cross_sum, grad_cross_gain = normalize_back(
        grad_second, saved["second_unit"], cross_gains, saved["second_inv"]
    )
    decoder_flag = is_decoder.astype(jnp.float32)
    grad_cross_sum = grad_cross_sum * decoder_flag
    grad_cross_gain = grad_cross_gain * decoder_flag
    cross_branch = grad_cross_sum.astype(jnp.bfloat16)
    grad_cross_w = contract(saved["cross_att"], cross_branch)
    grad_cross_att = matmul_back(cross_branch, cross_weight).astype(jnp.bfloat16)
    pair = saved["pair"]
    grad_cross_q, grad_pair = attend_back(
        saved["cross_queries"],
        pair[..., :model_width],
        pair[..., model_width:],
        doc_own,
        memory_docs,
        False,
        saved["cross_lse"],
        grad_cross_att,
        True,
    )
    grad_cross_q = grad_cross_q.astype(jnp.bfloat16)
    grad_pair = grad_pair.astype(jnp.bfloat16)
    grad_query_w = contract(saved["first_low"], grad_cross_q)
    grad_pair_w = contract(memory, grad_pair)
    grad_memory = matmul_back(grad_pair, pair_weight)
    grad_first = jnp.where(
        is_decoder, grad_cross_sum + matmul_back(grad_cross_q, query_weight), grad_second
    )
    grad_first_sum, grad_gain_early = normalize_back(
        grad_first, saved["first_unit"], gains_pair[0], saved["first_inv"]
    )
    self_branch = grad_first_sum.astype(jnp.bfloat16)
    grad_out_w = contract(saved["attended"], self_branch)
    grad_attended = matmul_back(self_branch, out_weight).astype(jnp.bfloat16)
    mixed = saved["mixed"]
    grad_queries, grad_pair_self = attend_back(
        mixed[..., :model_width],
        mixed[..., model_width : 2 * model_width],
        mixed[..., 2 * model_width :],
        doc_own,
        doc_own,
        is_decoder,
        saved["self_lse"],
        grad_attended,
        False,
    )
    grad_mixed = jnp.concatenate([grad_queries, grad_pair_self], axis=-1).astype(jnp.bfloat16)
    grad_qkv_w = contract(hidden_in, grad_mixed)
    grad_hidden = grad_first_sum + matmul_back(grad_mixed, qkv_weight)
    layer_grads = (
        grad_qkv_w,
        grad_out_w,
        grad_in_w,
        grad_down_w,
        jnp.stack([grad_gain_early, grad_gain_late]),
        grad_query_w,
        grad_pair_w,
        grad_cross_w,
        grad_cross_gain,
    )
    return (grad_hidden, grad_memory, layer_grads)


def any_rows(
    layer_input,
    segment_ids,
    attn_qkv,
    attn_out,
    ffn_in,
    ffn_out,
    norm_gain,
    cross_query,
    cross_pair,
    cross_out,
    cross_gain,
    out_cotangent,
):
    micro_count = layer_input.shape[1]
    section_index = lax.axis_index("section")
    is_decoder = section_index == 1
    weights = (
        attn_qkv[0],
        attn_out[0],
        ffn_in[0],
        ffn_out[0],
        norm_gain[0],
        cross_query,
        cross_pair,
        cross_out,
        cross_gain,
    )
    inputs_all = layer_input[0]
    docs_all = segment_ids[0]
    slot_ids = jnp.arange(micro_count)
    received = (jnp.zeros_like(inputs_all[0]), jnp.zeros_like(docs_all[0]))
    results = jnp.zeros_like(inputs_all)
    memories = []
    memory_doc_list = []
    for step_index in range(micro_count + 1):
        batch_index = step_index - section_index
        is_valid = (batch_index >= 0) & (batch_index < micro_count)
        chosen = jnp.clip(batch_index, 0, micro_count - 1)
        hidden_in = lax.dynamic_index_in_dim(inputs_all, chosen, 0, keepdims=False)
        doc_own = lax.dynamic_index_in_dim(docs_all, chosen, 0, keepdims=False)
        memory = received[0]
        memory_docs = jnp.where(is_valid & is_decoder, received[1], doc_own)
        memories.append(memory)
        memory_doc_list.append(memory_docs)
        result, saved = layer_forward(hidden_in, doc_own, memory, memory_docs, weights, is_decoder)
        low_result = result.astype(jnp.bfloat16)
        writing = (slot_ids == chosen) & is_valid
        results = jnp.where(writing[:, None, None, None], low_result[None], results)
        if step_index < micro_count:
            received = from_behind((low_result, doc_own), "section", 1)
    memory_stack = jnp.stack(memories)
    memory_doc_stack = jnp.stack(memory_doc_list)
    totals = tuple((jnp.zeros(weight.shape, jnp.float32) for weight in weights))
    input_grads = jnp.zeros(inputs_all.shape, jnp.float32)
    returned = jnp.zeros(inputs_all.shape[1:], jnp.float32)
    for step_index in range(micro_count + 1):
        batch_index = micro_count - step_index - section_index
        is_valid = (batch_index >= 0) & (batch_index < micro_count)
        chosen = jnp.clip(batch_index, 0, micro_count - 1)
        forward_step = jnp.clip(batch_index + section_index, 0, micro_count)
        hidden_in = lax.dynamic_index_in_dim(inputs_all, chosen, 0, keepdims=False)
        doc_own = lax.dynamic_index_in_dim(docs_all, chosen, 0, keepdims=False)
        memory = lax.dynamic_index_in_dim(memory_stack, forward_step, 0, keepdims=False)
        memory_docs = lax.dynamic_index_in_dim(memory_doc_stack, forward_step, 0, keepdims=False)
        discarded, saved = layer_forward(
            hidden_in, doc_own, memory, memory_docs, weights, is_decoder
        )
        cotangent = jnp.where(
            is_decoder,
            lax.dynamic_index_in_dim(out_cotangent, chosen, 0, keepdims=False).astype(jnp.float32),
            returned,
        )
        grad_hidden, grad_memory, layer_grads = layer_backward(
            cotangent, saved, hidden_in, doc_own, memory, memory_docs, weights, is_decoder
        )
        valid_flag = is_valid.astype(jnp.float32)
        totals = tuple(
            (running + valid_flag * fresh for running, fresh in zip(totals, layer_grads))
        )
        writing = (slot_ids == chosen) & is_valid
        input_grads = jnp.where(writing[:, None, None, None], grad_hidden[None], input_grads)
        if step_index < micro_count:
            returned = from_behind(grad_memory.astype(jnp.bfloat16), "section", -1).astype(
                grad_memory.dtype
            )
    group_sums = lax.psum(
        (
            totals[0],
            totals[1],
            totals[2],
            totals[3],
            totals[4],
            totals[5],
            totals[6],
            totals[7],
            totals[8],
        ),
        ("seq", "dp"),
    )
    section_sums = group_sums[:5]
    cross_sums = (
        from_root(group_sums[5].astype(jnp.bfloat16), "section", 1).astype(jnp.float32),
        from_root(group_sums[6].astype(jnp.bfloat16), "section", 1).astype(jnp.float32),
        from_root(group_sums[7].astype(jnp.bfloat16), "section", 1).astype(jnp.float32),
        from_root(group_sums[8].astype(jnp.bfloat16), "section", 1).astype(jnp.float32),
    )
    return (
        results[None],
        input_grads[None],
        section_sums[0][None],
        section_sums[1][None],
        section_sums[2][None],
        section_sums[3][None],
        section_sums[4][None],
        cross_sums[0],
        cross_sums[1],
        cross_sums[2],
        cross_sums[3],
    )


def split_rows(
    layer_input,
    segment_ids,
    attn_qkv,
    attn_out,
    ffn_in,
    ffn_out,
    norm_gain,
    cross_query,
    cross_pair,
    cross_out,
    cross_gain,
    out_cotangent,
):
    micros = layer_input.shape[1]
    length, width = layer_input.shape[3:]
    hidden = ffn_in.shape[-1]
    q_tiles = length // TILE
    group = lax.axis_size("dp") // 2
    axes = ("section", "seq", "dp")
    decoder = lax.axis_index("section") == 1
    flag = decoder.astype(jnp.int32)
    x = lax.axis_index("seq")
    core = lax.rem(lax.axis_index("dp"), 2)
    z = lax.axis_index("dp") // 2
    places = [(t, i, k, c) for t in range(2) for i in range(2) for k in range(group) for c in range(2)]

    def number(t, i, k, c):
        return ((t * 2 + i) * group + k) * 2 + c

    def send(values, target, section=None):
        route = [
            (number(*place), number(*target(*place)))
            for place in places
            if section in (None, place[0]) and target(*place)
        ]
        return lax.ppermute(values, axes, route)

    def to_core(t, i, k, c):
        return (t, i, k, 1 - c)

    def to_x(t, i, k, c):
        return (t, 1 - i, k, c)

    def to_row(t, i, k, c):
        return (t, c, k, i)

    def to_decoder(t, i, k, c):
        return (1, i, k, c) if t == 0 else None

    def to_encoder(t, i, k, c):
        return (0, i, k, c) if t == 1 else None

    def to_other_half(t, i, k, c):
        return (t, c, k, 1 - i)

    def fence(values, *before):
        return lax.optimization_barrier((values,) + before)[0]

    def exchange(values):
        return send(values, to_core)

    low = ((length, width), bf16)
    wide = ((length, width), f32)
    both = ((2 * length, width), bf16)
    keys_all = ((2 * length, 2 * width), bf16)
    mixing = ((width, 3 * width), bf16)
    inner = ((length, hidden), bf16)
    lse = ((q_tiles, 8, 2 * TILE), f32)
    stat = ((length, LANES), f32)
    square = ((width, width), bf16)
    rising = ((width, hidden), bf16)
    falling = ((hidden, width), bf16)
    gain_rows = ((8, width), f32)

    def halves(ref, section_rows):
        return ref.at[pl.ds(0, section_rows)], ref.at[pl.ds(section_rows, section_rows)]

    meta = jnp.stack([flag, core, x, z]).astype(jnp.int32)
    documents = segment_ids[0, :, 0]
    own = [send(layer_input[0, 0, 0], to_row)]
    docs_own = send(documents, to_row)
    docs_row = jnp.concatenate([docs_own, send(documents, to_other_half)], axis=1)
    docs_source = jnp.concatenate(
        [
            send(documents, lambda t, i, k, c: (1,) + to_row(t, i, k, c)[1:], 0),
            send(documents, lambda t, i, k, c: (1,) + to_other_half(t, i, k, c)[1:], 0),
        ],
        axis=1,
    )
    for micro in range(1, micros):
        own.append(send(fence(layer_input[0, micro, 0], own[-1]), to_row))
    other = [exchange(part) for part in own]

    def places_of(keys):
        return (
            dict(meta=meta, qd_s=docs_own, kd_s=keys),
            dict(
                qd=docs_own.astype(f32).reshape(micros, q_tiles, 1, TILE),
                kd=keys.astype(f32).reshape(micros, 1, 2 * length),
                gains=norm_gain[0],
            ),
        )

    plain = dict(meta=meta)
    scalars, small = places_of(docs_row)
    forward, memories, memories_other = [], [], []
    for micro in range(micros):
        call = launch(
            self_forward,
            micro,
            None,
            scalars,
            small,
            dict(
                x_own_h=own[micro],
                x_other_h=other[micro],
                w_mixed_h=attn_qkv[0],
                w_out_h=attn_out[0],
                w_in_h=ffn_in[0],
                w_down_h=ffn_out[0],
            ),
            dict(
                q_o=low,
                kv_o=keys_all,
                att_o=low,
                lse_o=lse,
                unit1_o=wide,
                inv1_o=stat,
                first_low_o=low,
                memory_o=low,
                ffn_low_o=low,
                act_o=inner,
                slope_o=inner,
                unit2_o=wide,
                inv2_o=stat,
            ),
            dict(
                **attention_scratch(length, width),
                **forward_scratch(length, width),
                x=both,
                w_mixed=mixing,
                w_out=square,
                w_in=rising,
                w_down=falling,
                unit1=wide,
                inv1=stat,
                first_low=low,
                memory=low,
                act=inner,
                slope=inner,
                unit2=wide,
                inv2=stat,
                sum=wide,
            ),
            24,
            26,
            after=(docs_source,) if micro == 0 else (forward[0].lse_o,),
        )
        forward.append(call)
        memories.append(send(call.memory_o, to_decoder))

    for micro in range(micros):
        memories_other.append(exchange(fence(memories[micro], forward[-1].lse_o)))
    cotangent = send(fence(out_cotangent[:, 0], forward[0].lse_o), to_row)

    cross_scalars, cross_small = places_of(docs_source)
    cross, grads_memory, made = [], [], []
    after = (forward[-1].lse_o,)
    for micro in range(micros):
        done = forward[micro]
        call = launch(
            cross_both_ways,
            micro,
            1,
            cross_scalars,
            dict(**cross_small, cross_gain=cross_gain[None]),
            dict(
                memory_own_h=memories[micro],
                memory_other_h=memories_other[micro],
                w_pair_h=cross_pair,
                first_low_h=done.first_low_o,
                unit1_h=done.unit1_o,
                w_query_h=cross_query,
                w_cross_h=cross_out,
                w_in_h=ffn_in[0],
                w_down_h=ffn_out[0],
                cot_h=cotangent,
            ),
            dict(
                att_o=low,
                ffn_low_o=low,
                act_o=inner,
                decoded_o=low,
                down_grad_o=low,
                up_grad_o=inner,
                gain_grads_o=gain_rows,
                branch_o=low,
                dq_low_o=low,
                dkv_o=keys_all,
                part_own_o=wide,
                part_other_o=low,
                grad_first_o=wide,
            ),
            dict(
                **attention_scratch(length, width),
                **forward_scratch(length, width),
                **backward_scratch(length, width),
                x=both,
                w_pair=((width, 2 * width), bf16),
                first_low=low,
                unit1=wide,
                w_query=square,
                w_cross=square,
                w_in=rising,
                w_down=falling,
                cot=low,
                unit2=wide,
                inv2=stat,
                second_low=low,
                act=inner,
                slope=inner,
                sum=wide,
                decoded=low,
                keep=wide,
                down_grad=low,
                up_grad=inner,
                gain_grads=gain_rows,
                branch=low,
                part_own=wide,
            ),
            32,
            44,
            dict(act_o=done.act_o, ffn_low_o=done.ffn_low_o),
            after,
        )
        cross.append(call)
        away = call.part_other_o
        if micro:
            away = fence(away, grads_memory[-1])
        total = call.part_own_o + exchange(away).astype(f32)
        made.append(total.astype(bf16))
        after = (made[micro],)
        grads_memory.append(send(made[micro], to_encoder))

    def backward_feed(micro, after):
        done, late = forward[micro], cross[micro]
        return launch(
            feed_backward_alone,
            micro,
            0,
            plain,
            dict(gains=norm_gain[0]),
            dict(
                grad_memory_h=grads_memory[micro],
                unit2_h=done.unit2_o,
                inv2_h=done.inv2_o,
                slope_h=done.slope_o,
                w_in_h=ffn_in[0],
                w_down_h=ffn_out[0],
            ),
            dict(gain_late_o=gain_rows, down_grad_o=low, up_grad_o=inner, grad_first_o=wide),
            dict(
                cot=low,
                unit2=wide,
                inv2=stat,
                slope=inner,
                w_in=rising,
                w_down=falling,
                gain_grads=gain_rows,
                keep=wide,
                down_grad=low,
                up_grad=inner,
                sum=wide,
            ),
            12,
            10,
            dict(
                down_grad_o=late.down_grad_o, up_grad_o=late.up_grad_o, grad_first_o=late.grad_first_o
            ),
            after,
        )

    def backward_self(micro, side, grad_first, previous=None, after=(), halfway=None):
        done = forward[micro]
        heads = width // LANES
        given = dict(q_h=done.q_o, kv_h=done.kv_o, att_h=done.att_o, lse_h=done.lse_o)
        ahead = dict(
            grad_first_h=grad_first,
            unit1_h=done.unit1_o,
            inv1_h=done.inv1_o,
            w_out_h=attn_out[0],
        )
        makes = dict(dq_low_o=low, dkv_o=keys_all)
        makes_first = dict(gain_early_o=gain_rows, branch_o=low)
        makes_last = dict(part_own_o=wide, part_other_o=low)
        scratch = dict(
            **attention_scratch(length, width),
            **backward_scratch(length, width),
            w_out=square,
            w_mixed=mixing,
            unit1=wide,
            inv1=stat,
            keep=wide,
            branch=low,
            grad_att=low,
            gain_grads=gain_rows,
        )

        def part(first, last, large, outs, work, previous, after):
            return launch(
                self_backward,
                (micro, first, last),
                side,
                scalars,
                small,
                dict(**given, **large),
                dict(**makes, **outs),
                scratch,
                20,
                work,
                previous,
                after,
            )

        if halfway is None:
            large = dict(**ahead, w_mixed_h=attn_qkv[0])
            outs = dict(**makes_first, **makes_last)
            return part(0, heads, large, outs, 22, previous, after)
        outs = dict(**makes_first, grad_sum_o=wide, grad_att_o=low)
        one = part(0, heads // 2, ahead, outs, 12, None, after)
        large = dict(
            w_mixed_h=attn_qkv[0],
            grad_sum_h=one.grad_sum_o,
            grad_att_h=one.grad_att_o,
            dq_h=one.dq_low_o,
            dkv_h=one.dkv_o,
        )
        two = part(heads // 2, heads, large, makes_last, 12, None, halfway)
        return types.SimpleNamespace(**{**vars(one), **vars(two)})

    def weight_grads(plan, arrays, scratch, after=(), kernel=contract_blocks, outs=None):
        blocks = ((2, width, width), bf16)
        call = launch(
            kernel,
            plan,
            None,
            plain,
            dict(),
            arrays,
            outs or dict(sent_o=blocks, kept_o=blocks),
            dict(**scratch, blocks=((4, width, width), bf16)),
            24,
            8,
            after=after,
        )
        return call.all_o if outs else (call.sent_o, call.kept_o)

    def first_sums(halves):
        sent, kept = halves
        got = exchange(sent)

        def block(side):
            return sum(
                lax.dynamic_index_in_dim(part, side, 0, keepdims=False).astype(f32)
                for part in (kept, got)
            )

        return block(1 - x).astype(bf16), block(x)

    def middle_sums(sums):
        away, total = sums
        return (total + send(away, to_x).astype(f32)).astype(bf16)

    def last_sums(total):
        shares = total.reshape(group, width // group, width)

        def share(step):
            return lax.dynamic_index_in_dim(shares, lax.rem(z + step, group), 0, keepdims=False)

        parts = [share(0)]
        for step in range(1, group):
            parts.append(send(share(step), along_z(step)))
        return sum(part.astype(f32) for part in parts).astype(bf16)

    def along_z(step):
        return lambda t, i, k, c: (t, i, (k + step) % group, c)

    def gather_z(share):
        return jnp.stack([share] + [send(share, along_z(step)) for step in range(1, group)])

    def gain_block(rows):
        filled = jnp.concatenate([jnp.stack(rows), jnp.zeros((16 - len(rows), width), f32)])
        return filled.astype(bf16)

    def spread(targets, own, own_x, outs, parts):
        return launch(
            spread_pieces,
            targets,
            None,
            plain,
            dict(),
            dict(own_h=own, own_x_h=own_x, other_h=exchange(own), other_x_h=exchange(own_x)),
            outs,
            dict(
                pieces=((4,) + own.shape, bf16),
                wide=((4 * group * parts, width // group, width), f32),
                gain_grads=((16, width), f32),
            ),
            8 + 4 * group * parts,
            5,
        )

    tokens, all_tokens = micros * length, 2 * micros * length
    turn, turn_all = ((width, tokens), bf16), ((width, all_tokens), bf16)
    narrow, narrow_all = ((tokens, width), bf16), ((all_tokens, width), bf16)
    pair_all = ((all_tokens, 2 * width), bf16)
    deep = ((tokens, hidden), bf16)

    def rows_of(first, second):
        starts = [halves(first, length), halves(second, length)]
        return [part[0] for part in starts] + [part[1] for part in starts]

    def cross_plan(r):
        return (
            [
                (r.low, (r.low0_h, r.low1_h)),
                (r.dq, (r.dq0_h, r.dq1_h)),
                (r.att, (r.att0_h, r.att1_h)),
                (r.branch, (r.branch0_h, r.branch1_h)),
                (r.mem, (r.mem0_h, r.mem1_h, r.mem2_h, r.mem3_h)),
                (r.pair, rows_of(r.pair0_h, r.pair1_h)),
            ],
            [
                (r.turn, r.low, 0, r.dq, 0),
                (r.turn_att, r.att, 0, r.branch, 0),
                (r.turn_all, r.mem, 0, r.pair, 0),
                (r.turn_all, r.mem, 0, r.pair, 1),
            ],
        )

    def rising_plan(r):
        return (
            [(r.low, (r.low0_h, r.low1_h)), (r.up, (r.up0_h, r.up1_h))],
            [(r.turn, r.low, 0, r.up, block) for block in range(4)],
        )

    def falling_plan(r):
        return (
            [(r.act, (r.act0_h, r.act1_h)), (r.down, (r.down0_h, r.down1_h))],
            [(r.turn, r.act, block, r.down, 0) for block in range(4)],
        )

    def self_plan(r):
        return (
            [
                (r.x, (r.x0_h, r.x1_h, r.x2_h, r.x3_h)),
                (r.dq, (r.dq0_h, r.dq1_h)),
                (r.pair, rows_of(r.pair0_h, r.pair1_h)),
                (r.att, (r.att0_h, r.att1_h)),
                (r.branch, (r.branch0_h, r.branch1_h)),
            ],
            [
                (r.turn_all, r.x, 0, r.dq, 0),
                (r.turn_all, r.x, 0, r.pair, 0),
                (r.turn_all, r.x, 0, r.pair, 1),
                (r.turn, r.att, 0, r.branch, 0),
            ],
        )

    last = micros - 1
    feeds, ends = [None] * micros, [None] * micros
    cross_local = weight_grads(
        cross_plan,
        dict(
            low0_h=forward[0].first_low_o,
            low1_h=forward[1].first_low_o,
            dq0_h=cross[0].dq_low_o,
            dq1_h=cross[1].dq_low_o,
            att0_h=cross[0].att_o,
            att1_h=cross[1].att_o,
            branch0_h=cross[0].branch_o,
            branch1_h=cross[1].branch_o,
            mem0_h=memories[0],
            mem1_h=memories[1],
            mem2_h=memories_other[0],
            mem3_h=memories_other[1],
            pair0_h=cross[0].dkv_o,
            pair1_h=cross[1].dkv_o,
            gain0_h=cross[0].gain_grads_o,
            gain1_h=cross[1].gain_grads_o,
        ),
        dict(
            low=narrow,
            dq=narrow,
            att=narrow,
            branch=narrow,
            mem=narrow_all,
            pair=pair_all,
            turn=turn,
            turn_att=turn,
            turn_all=turn_all,
            gain0=gain_rows,
            gain1=gain_rows,
            extra=((16, width), bf16),
        ),
        (made[last],),
        contract_cross,
        dict(all_o=((4 * width + 16, width), bf16)),
    )
    cross_sums = lax.psum(cross_local, axes)
    results = jnp.stack(
        [
            jnp.where(decoder, call.decoded_o, done.memory_o)
            for call, done in zip(cross, forward)
        ]
    )
    results = send(results, to_row)
    latest = made[last]
    for micro in range(last):
        feeds[micro] = backward_feed(micro, (latest,))
        first = feeds[micro].grad_first_o
        ends[micro] = backward_self(micro, 0, first)
        ends[micro] = backward_self(micro, 1, first, vars(ends[micro]), (cross_local,))
        latest = ends[micro].gain_early_o
    feeds[last] = backward_feed(last, (latest,))

    rising_halves = weight_grads(
        rising_plan,
        dict(
            low0_h=cross[0].ffn_low_o,
            low1_h=cross[1].ffn_low_o,
            up0_h=feeds[0].up_grad_o,
            up1_h=feeds[1].up_grad_o,
        ),
        dict(low=narrow, up=deep, turn=turn),
        (results,),
    )
    falling_halves = weight_grads(
        falling_plan,
        dict(
            act0_h=cross[0].act_o,
            act1_h=cross[1].act_o,
            down0_h=feeds[0].down_grad_o,
            down1_h=feeds[1].down_grad_o,
        ),
        dict(act=deep, down=narrow, turn=turn),
        (rising_halves[0],),
    )
    rising_sums, falling_sums = first_sums(rising_halves), first_sums(falling_halves)
    def part_sum(micro):
        end = ends[micro]
        total = (end.part_own_o + exchange(end.part_other_o).astype(f32)).astype(bf16)
        return total, send(total, to_row)

    steps = [part_sum(micro) for micro in range(last)]
    rising_total = middle_sums(rising_sums)
    falling_total = middle_sums(falling_sums)
    ends[last] = backward_self(
        last,
        None,
        feeds[last].grad_first_o,
        None,
        (rising_sums[0], falling_sums[0]) + tuple(step[0] for step in steps),
        (rising_total,) + tuple(step[1] for step in steps),
    )
    rising_share, falling_share = last_sums(rising_total), last_sums(falling_total)

    self_halves = weight_grads(
        self_plan,
        dict(
            x0_h=own[0],
            x1_h=own[1],
            x2_h=other[0],
            x3_h=other[1],
            dq0_h=ends[0].dq_low_o,
            dq1_h=ends[1].dq_low_o,
            pair0_h=ends[0].dkv_o,
            pair1_h=ends[1].dkv_o,
            att0_h=forward[0].att_o,
            att1_h=forward[1].att_o,
            branch0_h=ends[0].branch_o,
            branch1_h=ends[1].branch_o,
        ),
        dict(
            x=narrow_all,
            dq=narrow,
            pair=pair_all,
            att=narrow,
            branch=narrow,
            turn=turn,
            turn_all=turn_all,
        ),
        (rising_share, falling_total),
    )
    away, total = first_sums(self_halves)
    self_total = middle_sums((fence(away, falling_share), total))
    feed_own = gather_z(jnp.concatenate([rising_share, falling_share]))
    self_share = last_sums(self_total)
    feed_own_x = send(fence(feed_own, self_total), to_x)
    steps.append(part_sum(last))
    early = sum(end.gain_early_o[0] for end in ends)
    late = jnp.where(
        decoder,
        sum(call.gain_grads_o[0] for call in cross),
        sum(call.gain_late_o[0] for call in feeds),
    )
    self_own = gather_z(jnp.concatenate([self_share, gain_block([early, late])]))
    self_own_x = send(fence(self_own, feed_own_x), to_x)

    def columns(block):
        return pl.ds(block * width, width)

    def feed_targets(r, block, row, rows):
        return [
            r.up_o.at[pl.ds(row, rows), columns(block)],
            r.down_o.at[pl.ds(block * width + row, rows)],
        ]

    def self_targets(r, block, row, rows):
        if block == 3:
            return [r.out_o.at[pl.ds(row, rows)]]
        return [r.mixed_o.at[pl.ds(row, rows), columns(block)]]

    square_out, gains_out = ((width, width), f32), ((16, width), f32)
    feed_grads = spread(
        feed_targets,
        feed_own,
        feed_own_x,
        dict(up_o=((width, hidden), f32), down_o=((hidden, width), f32)),
        2,
    )
    self_grads = spread(
        self_targets,
        self_own,
        self_own_x,
        dict(mixed_o=((width, 3 * width), f32), out_o=square_out, gains_o=gains_out),
        1,
    )

    grad_input = jnp.stack([step[1] for step in steps])
    cross_parts = [
        cross_sums[block * width : (block + 1) * width].astype(f32) for block in range(4)
    ]
    return (
        results[None, :, None],
        grad_input.astype(f32)[None, :, None],
        self_grads.mixed_o[None],
        self_grads.out_o[None],
        feed_grads.up_o[None],
        feed_grads.down_o[None],
        self_grads.gains_o[None, :2],
        cross_parts[0],
        jnp.concatenate(cross_parts[2:], axis=1),
        cross_parts[1],
        cross_sums[4 * width].astype(f32),
    )


def shards(*arrays):
    layer_input = arrays[0]
    micros, rows, length = layer_input.shape[1:4]
    simple = (
        lax.axis_size("section") == 2
        and lax.axis_size("seq") == 2
        and lax.axis_size("dp") in (4, 8, 16)
        and (micros, rows) == (2, 1)
        and length % TILE == 0
        and arrays[4].shape[-1] == 4 * layer_input.shape[-1] == 4 * CHUNK
    )
    return split_rows(*arrays) if simple else any_rows(*arrays)


def solution(mesh):
    in_specs = (
        P("section", None, "dp", "seq", None),
        P("section", None, "dp", "seq"),
        P("section", None, None),
        P("section", None, None),
        P("section", None, None),
        P("section", None, None),
        P("section", None, None),
        P(),
        P(),
        P(),
        P(),
        P(None, "dp", "seq", None),
    )
    out_specs = (
        P("section", None, "dp", "seq", None),
        P("section", None, "dp", "seq", None),
        P("section", None, None),
        P("section", None, None),
        P("section", None, None),
        P("section", None, None),
        P("section", None, None),
        P(),
        P(),
        P(),
        P(),
    )
    return jax.shard_map(shards, mesh=mesh, in_specs=in_specs, out_specs=out_specs, check_vma=False)
```

```python
import types

import jax
import jax.numpy as jnp
from jax import lax
from jax.experimental import pallas as pl
from jax.experimental.pallas import tpu as pltpu
from jax.sharding import PartitionSpec as P

HEADS = 8
TILE = 256
LANES = 128
CHUNK = 512

f32 = jnp.float32
bf16 = jnp.bfloat16
negative_big = -1e30
epsilon = 1e-05


def dot(left, right):
    return lax.dot_general(left, right, (((1,), (0,)), ((), ())), preferred_element_type=f32)


def dot_nt(left, right):
    return lax.dot_general(left, right, (((1,), (1,)), ((), ())), preferred_element_type=f32)


def dot_tn(left, right):
    return lax.dot_general(left, right, (((0,), (0,)), ((), ())), preferred_element_type=f32)


def standardize(values):
    center = values - jnp.mean(values, axis=-1, keepdims=True)
    inverse = lax.rsqrt(jnp.mean(center * center, axis=-1, keepdims=True) + epsilon)
    return center * inverse, inverse


def standardize_back(grad_out, standard, gain_row, inverse):
    scaled = grad_out * gain_row
    grad_in = inverse * (
        scaled
        - jnp.mean(scaled, axis=-1, keepdims=True)
        - standard * jnp.mean(scaled * standard, axis=-1, keepdims=True)
    )
    return grad_in, jnp.sum(grad_out * standard, axis=0, keepdims=True)


class Copies:
    def __init__(self, sems):
        self.sems = sems
        self.used = 0

    def start(self, source, target):
        copy = pltpu.make_async_copy(source, target, self.sems.at[self.used])
        self.used += 1
        copy.start()
        return copy


def wait_all(copies):
    for copy in copies:
        copy.wait()


def spread_pairs(target, source, factor, pairs):
    tiles = target.shape[1]
    half = lax.broadcasted_iota(jnp.int32, (TILE, LANES), 1) < LANES // 2
    first = jnp.where(half, factor, 0.0).astype(bf16)
    second = jnp.where(half, 0.0, factor).astype(bf16)
    for tile in range(tiles):
        for pair in pairs:
            block = source[tile * TILE : (tile + 1) * TILE, pair * LANES : (pair + 1) * LANES]
            target[pair, tile, :TILE, :] = block * first
            target[pair, tile, TILE:, :] = block * second


def turn_tiles(target, source, column, pairs):
    low, high = pairs[0] * LANES, (pairs[-1] + 1) * LANES
    for tile in range(target.shape[0]):
        block = source[tile * TILE : (tile + 1) * TILE, column + low : column + high]
        target[tile, low:high, :] = jnp.transpose(block)


def place_documents(r, copies):
    wait_all(copies)
    q_tiles = r.qd.shape[0]
    for part in range(3):
        row = r.docs[part].astype(f32)[0:1, :]
        for tile in range(q_tiles):
            piece = row[:, tile * TILE : (tile + 1) * TILE]
            slot = part * q_tiles + tile
            r.bounds[0, slot] = jnp.min(piece).astype(jnp.int32)
            r.bounds[1, slot] = jnp.max(piece).astype(jnp.int32)
            if part == 0:
                r.qd[tile] = jnp.broadcast_to(piece, (8, TILE))
        if part > 0:
            for start in range(0, row.shape[1], LANES):
                block = jnp.broadcast_to(row[:, start : start + LANES], (LANES, LANES))
                place = (part - 1) * row.shape[1] + start
                r.kdc[place : place + LANES, :] = jnp.transpose(block)


def load_documents(r, move, queries, own, other):
    rows = pl.ds(r.docs.shape[2], r.docs.shape[1])
    return [
        move.start(source.at[rows], r.docs.at[part])
        for part, source in enumerate((queries, own, other))
    ]


def tile_place(r, core, causal, q_tile, k_tile):
    q_tiles = r.qd.shape[0]
    length = q_tiles * TILE
    owner = jnp.where(k_tile < q_tiles, core, 1 - core)
    k_start = owner * length + lax.rem(k_tile, q_tiles) * TILE
    ahead = core * length + q_tile * TILE - k_start
    ahead = jnp.where(causal == 1, ahead, 2 * length * TILE)
    q_low, q_high = r.bounds[0, q_tile], r.bounds[1, q_tile]
    k_low, k_high = r.bounds[0, q_tiles + k_tile], r.bounds[1, q_tiles + k_tile]
    active = (q_low <= k_high) & (k_low <= q_high) & (ahead > -TILE)
    return active, ahead


def fill_bias(r, q_tile, k_tile, ahead):
    keys = r.kdc[pl.ds(pl.multiple_of(k_tile * TILE, TILE), TILE), :]
    shift = lax.broadcasted_iota(jnp.int32, (TILE, LANES), 0) - lax.broadcasted_iota(
        jnp.int32, (TILE, LANES), 1
    )
    queries = r.qd[q_tile]
    for start in range(0, TILE, LANES):
        same = keys == queries[0:1, start : start + LANES]
        allowed = same & (shift - start <= ahead)
        r.bias[:, start : start + LANES] = jnp.where(allowed, 0.0, negative_big)


def attention_forward(r, core, causal):
    pairs, q_tiles = r.qm.shape[:2]
    k_tiles = r.vt.shape[0]

    def one_query_tile(q_tile, carry):
        r.top[...] = jnp.full(r.top.shape, negative_big, f32)
        r.total[...] = jnp.zeros(r.total.shape, f32)
        r.turned[...] = jnp.zeros(r.turned.shape, f32)

        def one_key_tile(k_tile, inner):
            active, ahead = tile_place(r, core, causal, q_tile, k_tile)

            @pl.when(active)
            def _():
                fill_bias(r, q_tile, k_tile, ahead)
                rows = pl.ds(pl.multiple_of(k_tile * TILE, TILE), TILE)

                def raw(pair):
                    keys = r.kv[rows, pair * LANES : (pair + 1) * LANES]
                    return dot_nt(keys, r.qm[pair, q_tile])

                raw_next = raw(0)
                for pair in range(pairs):
                    bias = r.bias[...]
                    scores = raw_next + jnp.concatenate([bias, bias], axis=1)
                    if pair + 1 < pairs:
                        raw_next = raw(pair + 1)
                    old_top = r.top[pair : pair + 1, :]
                    new_top = jnp.maximum(old_top, jnp.max(scores, axis=0, keepdims=True))
                    weights = jnp.exp(scores - new_top)
                    shrink = jnp.exp(old_top - new_top)
                    r.top[pair : pair + 1, :] = new_top
                    r.total[pair : pair + 1, :] = r.total[
                        pair : pair + 1, :
                    ] * shrink + jnp.sum(weights, axis=0, keepdims=True)
                    low = weights.astype(bf16)
                    for side in range(2):
                        span = slice(side * TILE, (side + 1) * TILE)
                        head = slice((2 * pair + side) * 64, (2 * pair + side + 1) * 64)
                        r.turned[head, :] = r.turned[head, :] * shrink[:, span] + dot(
                            r.vt[k_tile, head, :], low[:, span]
                        )

            return inner

        lax.fori_loop(0, k_tiles, one_key_tile, 0)
        for pair in range(pairs):
            total = r.total[pair : pair + 1, :]
            r.lse[q_tile, pair : pair + 1, :] = r.top[pair : pair + 1, :] + jnp.log(total)
            share = 1.0 / total
            for side in range(2):
                span = slice(side * TILE, (side + 1) * TILE)
                head = slice((2 * pair + side) * 64, (2 * pair + side + 1) * 64)
                r.turned[head, :] = r.turned[head, :] * share[:, span]
        rows = pl.ds(pl.multiple_of(q_tile * TILE, TILE), TILE)
        r.att[rows, :] = jnp.transpose(r.turned[...]).astype(bf16)
        return carry

    lax.fori_loop(0, q_tiles, one_query_tile, 0)


def row_products(r, grad_att, pairs):
    low, high = pairs[0] * LANES, (pairs[-1] + 1) * LANES
    for tile in range(r.qm.shape[1]):
        rows = slice(tile * TILE, (tile + 1) * TILE)
        product = jnp.transpose(
            grad_att[rows, low:high].astype(f32) * r.att[rows, low:high].astype(f32)
        )
        for pair in pairs:
            for side in range(2):
                head = (2 * pair + side) * 64 - low
                r.delta[tile, pair : pair + 1, side * TILE : (side + 1) * TILE] = jnp.sum(
                    product[head : head + 64, :], axis=0, keepdims=True
                )


def attention_backward(r, core, causal, pairs):
    q_tiles, k_tiles = r.qm.shape[1], r.kt.shape[0]
    width = r.kt.shape[1]
    low, high = pairs[0] * LANES, (pairs[-1] + 1) * LANES
    for start in (0, width):
        r.dkv[:, start + low : start + high] = jnp.zeros((r.dkv.shape[0], high - low), f32)

    def one_query_tile(q_tile, carry):
        r.turned[low:high, :] = jnp.zeros((high - low, TILE), f32)

        def one_key_tile(k_tile, inner):
            active, ahead = tile_place(r, core, causal, q_tile, k_tile)

            @pl.when(active)
            def _():
                fill_bias(r, q_tile, k_tile, ahead)
                rows = pl.ds(pl.multiple_of(k_tile * TILE, TILE), TILE)

                def raw(pair):
                    lanes = slice(pair * LANES, (pair + 1) * LANES)
                    lanes_v = slice(width + pair * LANES, width + (pair + 1) * LANES)
                    return (
                        dot_nt(r.kv[rows, lanes], r.qm[pair, q_tile]),
                        dot_nt(r.kv[rows, lanes_v], r.gm[pair, q_tile]),
                    )

                raw_next = raw(pairs[0])
                for pair in pairs:
                    bias = r.bias[...]
                    scores, grad_probs = raw_next
                    scores = scores + jnp.concatenate([bias, bias], axis=1)
                    if pair < pairs[-1]:
                        raw_next = raw(pair + 1)
                    probs = jnp.exp(scores - r.lse[q_tile, pair : pair + 1, :])
                    grad_scores = probs * (grad_probs - r.delta[q_tile, pair : pair + 1, :])
                    probs_low = probs.astype(bf16)
                    grad_low = grad_scores.astype(bf16)
                    lanes = slice(pair * LANES, (pair + 1) * LANES)
                    lanes_v = slice(width + pair * LANES, width + (pair + 1) * LANES)
                    r.dkv[rows, lanes] += dot(grad_low, r.qm[pair, q_tile])
                    r.dkv[rows, lanes_v] += dot(probs_low, r.gm[pair, q_tile])
                    for side in range(2):
                        span = slice(side * TILE, (side + 1) * TILE)
                        head = slice((2 * pair + side) * 64, (2 * pair + side + 1) * 64)
                        r.turned[head, :] += dot(r.kt[k_tile, head, :], grad_low[:, span])

            return inner

        lax.fori_loop(0, k_tiles, one_key_tile, 0)
        rows = pl.ds(pl.multiple_of(q_tile * TILE, TILE), TILE)
        r.dq[rows, low:high] = jnp.transpose(r.turned[low:high, :]) * (64**-0.5)
        return carry

    lax.fori_loop(0, q_tiles, one_query_tile, 0)


def feed_forward(r, low):
    r.sum[...] = jnp.zeros(r.sum.shape, f32)

    def one_chunk(chunk, carry):
        span = pl.ds(pl.multiple_of(chunk * CHUNK, CHUNK), CHUNK)
        upward = dot(low[...], r.w_in[:, span])
        gate = jax.nn.sigmoid(upward)
        active = (upward * gate).astype(bf16)
        r.act[:, span] = active
        r.slope[:, span] = (gate + upward * gate * (1.0 - gate)).astype(r.slope.dtype)
        r.sum[...] += dot(active, r.w_down[span, :])
        return carry

    lax.fori_loop(0, r.w_in.shape[1] // CHUNK, one_chunk, 0)


def feed_backward(r):
    r.sum[...] = jnp.zeros(r.sum.shape, f32)

    def one_chunk(chunk, carry):
        span = pl.ds(pl.multiple_of(chunk * CHUNK, CHUNK), CHUNK)
        grad_active = dot_nt(r.down_grad[...], r.w_down[span, :]).astype(bf16)
        grad_up = (grad_active.astype(f32) * r.slope[:, span].astype(f32)).astype(bf16)
        r.up_grad[:, span] = grad_up
        r.sum[...] += dot_nt(grad_up, r.w_in[:, span])
        return carry

    lax.fori_loop(0, r.w_in.shape[1] // CHUNK, one_chunk, 0)


def self_forward(r):
    length, width = r.unit1.shape
    decoder, core = r.meta[0], r.meta[1]
    move = Copies(r.sems)
    whole = pl.ds(0, length)
    documents = load_documents(r, move, r.x_own_h, r.x_own_h, r.x_other_h)
    early = [
        move.start(r.x_own_h.at[whole], r.x.at[whole]),
        move.start(r.x_other_h.at[whole], r.x.at[pl.ds(length, length)]),
        move.start(r.w_mixed_h, r.w_mixed),
    ]
    later = [
        move.start(r.w_out_h, r.w_out),
        move.start(r.w_in_h, r.w_in),
        move.start(r.w_down_h, r.w_down),
    ]
    place_documents(r, documents)
    wait_all(early)
    r.q[...] = dot(r.x[:length, :], r.w_mixed[:, :width]).astype(bf16)
    r.kv[...] = dot(r.x[...], r.w_mixed[:, width:]).astype(bf16)
    outs = [move.start(r.q, r.q_o), move.start(r.kv, r.kv_o)]
    pairs = range(width // LANES)
    spread_pairs(r.qm, r.q, 64**-0.5, pairs)
    turn_tiles(r.vt, r.kv, width, pairs)
    attention_forward(r, core, decoder)
    wait_all(later)
    outs += [move.start(r.att, r.att_o), move.start(r.lse, r.lse_o)]
    unit, inverse = standardize(r.x[:length, :].astype(f32) + dot(r.att[...], r.w_out[...]))
    r.unit1[...] = unit
    r.inv1[...] = jnp.broadcast_to(inverse, r.inv1.shape)
    r.first_low[...] = (unit * r.gains[0:1, :]).astype(bf16)
    outs += [
        move.start(r.unit1, r.unit1_o),
        move.start(r.inv1, r.inv1_o),
        move.start(r.first_low, r.first_low_o),
    ]

    @pl.when(decoder == 0)
    def _():
        feed_forward(r, r.first_low)
        late = [
            move.start(r.first_low, r.ffn_low_o),
            move.start(r.act, r.act_o),
            move.start(r.slope, r.slope_o),
        ]
        unit2, inverse2 = standardize(r.unit1[...] * r.gains[0:1, :] + r.sum[...])
        r.memory[:length, :] = (unit2 * r.gains[1:2, :]).astype(bf16)
        r.memory[length:, :] = r.docs[0]
        late += [move.start(r.memory, r.memory_o)]
        r.unit2[...] = unit2
        r.inv2[...] = jnp.broadcast_to(inverse2, r.inv2.shape)
        late += [move.start(r.unit2, r.unit2_o), move.start(r.inv2, r.inv2_o)]
        wait_all(late)

    wait_all(outs)


def cross_both_ways(r):
    length, width = r.unit1_h.shape
    core = r.meta[1]
    move = Copies(r.sems)
    whole = pl.ds(0, length)
    documents = load_documents(r, move, r.x_own_h, r.memory_own_h, r.memory_other_h)
    moves = [
        move.start(r.memory_own_h.at[whole], r.x.at[whole]),
        move.start(r.memory_other_h.at[whole], r.x.at[pl.ds(length, length)]),
        move.start(r.w_pair_h, r.w_pair),
        move.start(r.first_low_h, r.first_low),
        move.start(r.w_query_h, r.w_query),
    ]
    later = [
        move.start(r.unit1_h, r.unit1),
        move.start(r.w_cross_h, r.w_cross),
        move.start(r.w_in_h, r.w_in),
        move.start(r.w_down_h, r.w_down),
        move.start(r.cot_h.at[r.micro], r.cot),
    ]
    place_documents(r, documents)
    wait_all(moves)
    r.kv[...] = dot(r.x[...], r.w_pair[...]).astype(bf16)
    r.q[...] = dot(r.first_low[...], r.w_query[...]).astype(bf16)
    pairs = range(width // LANES)
    spread_pairs(r.qm, r.q, 64**-0.5, pairs)
    turn_tiles(r.vt, r.kv, width, pairs)
    turn_tiles(r.kt, r.kv, 0, pairs)
    attention_forward(r, core, 0)
    outs = [move.start(r.att, r.att_o)]
    wait_all(later)
    first = r.unit1[...] * r.gains[0:1, :]
    unit, inverse = standardize(first + dot(r.att[...], r.w_cross[...]))
    r.unit2[...] = unit
    r.inv2[...] = jnp.broadcast_to(inverse, r.inv2.shape)
    r.second_low[...] = (unit * r.cross_gain[...]).astype(bf16)
    outs += [move.start(r.second_low, r.ffn_low_o)]
    feed_forward(r, r.second_low)
    outs += [move.start(r.act, r.act_o)]
    unit3, inverse3 = standardize(r.unit2[...] * r.cross_gain[...] + r.sum[...])
    r.decoded[...] = (unit3 * r.gains[1:2, :]).astype(bf16)
    outs += [move.start(r.decoded, r.decoded_o)]
    grad_third, gain_late = standardize_back(
        r.cot[...].astype(f32), unit3, r.gains[1:2, :], inverse3
    )
    r.keep[...] = grad_third
    r.down_grad[...] = grad_third.astype(bf16)
    outs += [move.start(r.down_grad, r.down_grad_o)]
    feed_backward(r)
    outs += [move.start(r.up_grad, r.up_grad_o)]
    grad_sum, gain_cross = standardize_back(
        r.keep[...] + r.sum[...], r.unit2[...], r.cross_gain[...], r.inv2[:, 0:1]
    )
    r.gain_grads[...] = jnp.zeros(r.gain_grads.shape, f32)
    r.gain_grads[0:1, :] = gain_late
    r.gain_grads[1:2, :] = gain_cross
    r.keep[...] = grad_sum
    r.branch[...] = grad_sum.astype(bf16)
    outs += [move.start(r.gain_grads, r.gain_grads_o), move.start(r.branch, r.branch_o)]
    r.q[...] = dot_nt(r.branch[...], r.w_cross[...]).astype(bf16)
    spread_pairs(r.gm, r.q, 1.0, pairs)
    row_products(r, r.q, pairs)
    attention_backward(r, core, 0, pairs)
    r.dq_low[...] = r.dq[...].astype(bf16)
    r.keep[...] += dot_nt(r.dq_low[...], r.w_query[...])
    outs += [move.start(r.dq_low, r.dq_low_o), move.start(r.keep, r.grad_first_o)]
    r.dkv_low[...] = r.dkv[...].astype(bf16)
    outs += [move.start(r.dkv_low, r.dkv_o)]
    part = dot_nt(r.dkv_low[...], r.w_pair[...])
    r.part_other[...] = part[length:, :].astype(bf16)
    r.part_own[...] = part[:length, :]
    outs += [move.start(r.part_other, r.part_other_o), move.start(r.part_own, r.part_own_o)]
    wait_all(outs)


def feed_backward_alone(r):
    move = Copies(r.sems)
    early = [
        move.start(r.grad_memory_h, r.cot),
        move.start(r.unit2_h, r.unit2),
        move.start(r.inv2_h, r.inv2),
    ]
    later = [
        move.start(r.w_down_h, r.w_down),
        move.start(r.slope_h, r.slope),
        move.start(r.w_in_h, r.w_in),
    ]
    wait_all(early)
    grad_third, gain_late = standardize_back(
        r.cot[...].astype(f32), r.unit2[...], r.gains[1:2, :], r.inv2[:, 0:1]
    )
    r.gain_grads[...] = jnp.broadcast_to(gain_late, r.gain_grads.shape)
    r.keep[...] = grad_third
    r.down_grad[...] = grad_third.astype(bf16)
    outs = [move.start(r.down_grad, r.down_grad_o), move.start(r.gain_grads, r.gain_late_o)]
    wait_all(later)
    feed_backward(r)
    outs += [move.start(r.up_grad, r.up_grad_o)]
    r.keep[...] += r.sum[...]
    outs += [move.start(r.keep, r.grad_first_o)]
    wait_all(outs)


def self_backward(r, plan):
    r.micro, first, last = plan
    length, width = r.att_h.shape
    decoder, core = r.meta[0], r.meta[1]
    pairs = range(first, last)
    low, high = first * LANES, last * LANES
    move = Copies(r.sems)
    later = [
        move.start(r.q_h, r.q),
        move.start(r.kv_h, r.kv),
        move.start(r.att_h, r.att),
        move.start(r.lse_h, r.lse),
    ]
    if first == 0:
        early = [
            move.start(r.grad_first_h, r.keep),
            move.start(r.unit1_h, r.unit1),
            move.start(r.inv1_h, r.inv1),
            move.start(r.w_out_h, r.w_out),
        ]
    else:
        early = [move.start(r.grad_att_h, r.grad_att)]
    outs = []
    place_documents(r, load_documents(r, move, r.x_own_h, r.x_own_h, r.x_other_h))
    wait_all(early)
    if first == 0:
        grad_sum, gain_early = standardize_back(
            r.keep[...], r.unit1[...], r.gains[0:1, :], r.inv1[:, 0:1]
        )
        r.gain_grads[...] = jnp.broadcast_to(gain_early, r.gain_grads.shape)
        r.keep[...] = grad_sum
        r.branch[...] = grad_sum.astype(bf16)
        r.grad_att[...] = dot_nt(r.branch[...], r.w_out[...]).astype(bf16)
        outs += [move.start(r.gain_grads, r.gain_early_o), move.start(r.branch, r.branch_o)]
        if last < width // LANES:
            outs += [move.start(r.keep, r.grad_sum_o), move.start(r.grad_att, r.grad_att_o)]
    wait_all(later)
    if last == width // LANES:
        ends = [move.start(r.w_mixed_h, r.w_mixed)]
        if first > 0:
            ends += [
                move.start(r.grad_sum_h, r.keep),
                move.start(r.dq_h.at[:, pl.ds(0, low)], r.dq_low.at[:, pl.ds(0, low)]),
                move.start(r.dkv_h.at[:, pl.ds(0, low)], r.dkv_low.at[:, pl.ds(0, low)]),
                move.start(
                    r.dkv_h.at[:, pl.ds(width, low)], r.dkv_low.at[:, pl.ds(width, low)]
                ),
            ]
    spread_pairs(r.qm, r.q, 64**-0.5, pairs)
    turn_tiles(r.kt, r.kv, 0, pairs)
    spread_pairs(r.gm, r.grad_att, 1.0, pairs)
    row_products(r, r.grad_att, pairs)
    attention_backward(r, core, decoder, pairs)
    r.dq_low[:, low:high] = r.dq[:, low:high].astype(bf16)
    for start in (0, width):
        span = slice(start + low, start + high)
        r.dkv_low[:, span] = r.dkv[:, span].astype(bf16)
    if last == width // LANES:
        wait_all(ends)
        outs += [move.start(r.dq_low, r.dq_low_o), move.start(r.dkv_low, r.dkv_o)]
        r.keep[...] += dot_nt(r.dq_low[...], r.w_mixed[:, :width])
        part = dot_nt(r.dkv_low[...], r.w_mixed[:, width:])
        r.part_other[...] = part[length:, :].astype(bf16)
        r.keep[...] += part[:length, :]
        outs += [move.start(r.part_other, r.part_other_o), move.start(r.keep, r.part_own_o)]
    else:
        outs.append(move.start(r.dq_low.at[:, pl.ds(low, high - low)], r.dq_low_o.at[:, pl.ds(low, high - low)]))
        for start in (0, width):
            span = pl.ds(start + low, high - low)
            outs.append(move.start(r.dkv_low.at[:, span], r.dkv_o.at[:, span]))
    wait_all(outs)


def contract_blocks(r, plan):
    for core in range(2):

        @pl.when(r.meta[1] == core)
        def _(core=core):
            targets = [None] * 4
            for half in range(2):
                target = r.kept_o if half == core else r.sent_o
                targets[2 * half], targets[2 * half + 1] = target.at[0], target.at[1]
            order = (0, 1, 2, 3) if core else (2, 3, 0, 1)
            contract_in_order(r, plan(r), order, targets, Copies(r.sems))


def contract_cross(r, plan):
    width = r.all_o.shape[1]
    extra = r.all_o.at[pl.ds(4 * width, r.extra.shape[0])]

    @pl.when(r.meta[0] == 1)
    def _():
        move = Copies(r.sems)
        wait_all([move.start(r.gain0_h, r.gain0), move.start(r.gain1_h, r.gain1)])
        gain = (r.gain0[1:2, :] + r.gain1[1:2, :]).astype(bf16)
        r.extra[...] = jnp.broadcast_to(gain, r.extra.shape)
        wait_all([move.start(r.extra, extra)])
        targets = [r.all_o.at[pl.ds(block * width, width)] for block in range(4)]
        contract_in_order(r, plan(r), (0, 1, 2, 3), targets, move)

    @pl.when(r.meta[0] == 0)
    def _():
        r.blocks[0] = jnp.zeros((width, width), bf16)
        r.extra[...] = jnp.zeros(r.extra.shape, bf16)
        move = Copies(r.sems)
        outs = [move.start(r.extra, extra)]
        for block in range(4):
            outs.append(move.start(r.blocks.at[0], r.all_o.at[pl.ds(block * width, width)]))
        wait_all(outs)


def contract_in_order(r, blocks, order, targets, move):
    loads = dict()
    for slot in order:
        for buffer, sources, at in blocks[slot][1:]:
            if (id(buffer), at) not in loads:
                span = pl.ds(at * CHUNK, CHUNK)
                row = 0
                copies = []
                for source in sources:
                    rows = pl.ds(row, source.shape[0])
                    copies.append(move.start(source.at[:, span], buffer.at[rows, span]))
                    row += source.shape[0]
                loads[id(buffer), at] = copies
    outs = []
    held = dict()
    for slot in order:
        turn, (left, _, left_at), (right, _, right_at) = blocks[slot]
        wait_all(loads.pop((id(left), left_at), ()))
        wait_all(loads.pop((id(right), right_at), ()))
        if held.get(id(turn)) != left_at:
            for row in range(0, left.shape[0], CHUNK):
                block = left[row : row + CHUNK, left_at * CHUNK : (left_at + 1) * CHUNK]
                turn[:, row : row + CHUNK] = jnp.transpose(block)
            held[id(turn)] = left_at
        block = right[:, right_at * CHUNK : (right_at + 1) * CHUNK]
        r.blocks[slot] = dot(turn[:, : right.shape[0]], block).astype(bf16)
        outs.append(move.start(r.blocks.at[slot], targets[slot]))
    wait_all(outs)


def spread_pieces(r, targets):
    z = r.meta[3]
    group, height = r.own_h.shape[:2]
    rows = r.own_h.shape[2] // group
    for core in range(2):
        for x in range(2):

            @pl.when((r.meta[1] == core) & (r.meta[2] == x))
            def _(core=core, x=x):
                move = Copies(r.sems)
                parts = [
                    (r.own_h, core, x),
                    (r.own_x_h, core, 1 - x),
                    (r.other_h, 1 - core, x),
                    (r.other_x_h, 1 - core, 1 - x),
                ]
                loads = [
                    move.start(source, r.pieces.at[place])
                    for place, (source, _, _) in enumerate(parts)
                ]
                outs = []
                slot = 0
                gains = None
                for place, (_, half, side) in enumerate(parts):
                    loads[place].wait()
                    for step in range(group):
                        row = pl.multiple_of(lax.rem(z + (group - step), group) * rows, rows)
                        start = 0
                        for target in targets(r, 2 * half + side, row, rows):
                            r.wide[slot] = r.pieces[place, step, start : start + rows].astype(f32)
                            outs.append(move.start(r.wide.at[slot], target))
                            slot += 1
                            start += rows
                        if start < height:
                            extra = r.pieces[place, step, start:height].astype(f32)
                            gains = extra if gains is None else gains + extra
                if gains is not None:
                    r.gain_grads[...] = gains
                    outs.append(move.start(r.gain_grads, r.gains_o))
                wait_all(outs)


def launch(kernel, plan, side, scalars, small, large, outs, scratch, copies, work, previous=None, after=()):
    names = list(scalars) + list(small) + list(large)
    arrays = list(scalars.values()) + list(small.values()) + list(large.values())
    specs = (
        [pl.BlockSpec(memory_space=pltpu.SMEM)] * len(scalars)
        + [pl.BlockSpec(memory_space=pltpu.VMEM)] * len(small)
        + [pl.BlockSpec(memory_space=pl.ANY)] * len(large)
    )
    aliases = dict()
    for position, name in enumerate(outs):
        if previous and name in previous:
            aliases[len(arrays)] = position
            names.append("previous_" + name)
            arrays.append(previous[name])
            specs.append(pl.BlockSpec(memory_space=pl.ANY))
    for array in after:
        names.append("")
        arrays.append(array)
        specs.append(pl.BlockSpec(memory_space=pl.ANY))
    names += list(outs) + list(scratch) + ["sems"]

    def body(*refs):
        r = types.SimpleNamespace(**dict(zip(names, refs)))

        def run():
            if isinstance(plan, int):
                r.micro = plan
                kernel(r)
            else:
                kernel(r, plan)

        if side is None:
            run()
        else:
            pl.when(r.meta[0] == side)(run)

    results = pl.pallas_call(
        body,
        out_shape=[jax.ShapeDtypeStruct(*shape) for shape in outs.values()],
        in_specs=specs,
        out_specs=[pl.BlockSpec(memory_space=pl.ANY)] * len(outs),
        scratch_shapes=[
            pltpu.SMEM(*shape) if shape[1] == jnp.int32 else pltpu.VMEM(*shape)
            for shape in scratch.values()
        ]
        + [pltpu.SemaphoreType.DMA((copies,))],
        input_output_aliases=aliases,
        compiler_params=pltpu.CompilerParams(vmem_limit_bytes=58 * 1024 * 1024),
        cost_estimate=pl.CostEstimate(
            flops=work * 10**9, bytes_accessed=1 << 20, transcendentals=0
        ),
    )(*arrays)
    return types.SimpleNamespace(**dict(zip(outs, results)))


def attention_scratch(length, width):
    pairs, q_tiles, k_tiles = width // LANES, length // TILE, 2 * length // TILE
    return dict(
        q=((length, width), bf16),
        kv=((2 * length, 2 * width), bf16),
        qm=((pairs, q_tiles, 2 * TILE, LANES), bf16),
        kdc=((2 * length, LANES), f32),
        docs=((3, 16, width), bf16),
        qd=((length // TILE, 8, TILE), f32),
        bounds=((2, 3 * length // TILE), jnp.int32),
        bias=((TILE, TILE), f32),
        lse=((q_tiles, 8, 2 * TILE), f32),
        att=((length, width), bf16),
        turned=((width, TILE), f32),
    )


def forward_scratch(length, width):
    k_tiles = 2 * length // TILE
    return dict(
        vt=((k_tiles, width, TILE), bf16),
        top=((8, 2 * TILE), f32),
        total=((8, 2 * TILE), f32),
    )


def backward_scratch(length, width):
    pairs, q_tiles, k_tiles = width // LANES, length // TILE, 2 * length // TILE
    return dict(
        kt=((k_tiles, width, TILE), bf16),
        gm=((pairs, q_tiles, 2 * TILE, LANES), bf16),
        delta=((q_tiles, 8, 2 * TILE), f32),
        dkv=((2 * length, 2 * width), f32),
        dq=((length, width), f32),
        dkv_low=((2 * length, 2 * width), bf16),
        part_other=((length, width), bf16),
        dq_low=((length, width), bf16),
    )


def for_sending(shard):

    def short(part):
        return part.astype(jnp.bfloat16) if part.dtype == jnp.float32 else part

    return jax.tree.map(short, shard)


def from_behind(block, axis, distance):
    devices = range(lax.axis_size(axis))
    route = [(i - distance, i) for i in devices if i - distance in devices]
    return lax.ppermute(block, axis, route)


def from_root(shard, axis, root):
    mine = lax.axis_index(axis) == root
    return lax.psum(jnp.where(mine, shard, jnp.zeros_like(shard)), axis)


def matmul(left_side, right_side):
    return jnp.einsum("rsd,de->rse", left_side, right_side, preferred_element_type=jnp.float32)


def matmul_back(left_side, right_side):
    return jnp.einsum("rse,de->rsd", left_side, right_side, preferred_element_type=jnp.float32)


def contract(left_side, right_side):
    return jnp.einsum("rsd,rse->de", left_side, right_side, preferred_element_type=jnp.float32)


def normalize(values, gain_row):
    center = values - jnp.mean(values, axis=-1, keepdims=True)
    inverse = lax.rsqrt(jnp.mean(center * center, axis=-1, keepdims=True) + epsilon)
    standard = center * inverse
    return (standard * gain_row, standard, inverse)


def normalize_back(grad_out, standard, gain_row, inverse):
    scaled = grad_out * gain_row
    grad_in = inverse * (
        scaled
        - jnp.mean(scaled, axis=-1, keepdims=True)
        - standard * jnp.mean(scaled * standard, axis=-1, keepdims=True)
    )
    return (grad_in, jnp.sum(grad_out * standard, axis=(0, 1)))


def allowed_mask(query_docs, key_docs, query_place, key_place, causal):
    same_doc = query_docs[:, :, None] == key_docs[:, None, :]
    earlier = query_place[:, None] >= key_place[None, :]
    return (same_doc & (earlier | jnp.logical_not(causal)))[:, None]


def attend(queries, keys_local, values_local, query_docs, key_docs, causal, is_cross):
    rows_here, shard_len, model_width = queries.shape
    head_dim = model_width // HEADS
    score_scale = head_dim ** (-0.5)
    query_place = lax.axis_index("seq") * shard_len + jnp.arange(shard_len)
    query_heads = queries.reshape(rows_here, shard_len, HEADS, head_dim)

    def absorb(state_tuple, pieces):
        running_top, running_total, running_sum = state_tuple
        key_piece, value_piece, doc_piece = pieces
        piece_len = key_piece.shape[1]
        raw_scores = jnp.einsum(
            "rqhd,rkhd->rhqk",
            query_heads,
            key_piece.reshape(rows_here, piece_len, HEADS, head_dim),
            preferred_element_type=jnp.float32,
        )
        allowed = allowed_mask(query_docs, doc_piece, query_place, jnp.arange(piece_len), causal)
        scores = jnp.where(allowed, raw_scores * score_scale, negative_big)
        new_top = jnp.maximum(running_top, jnp.max(scores, axis=-1))
        weights = jnp.where(allowed, jnp.exp(scores - new_top[..., None]), 0.0)
        new_total = jnp.sum(weights, axis=-1)
        product = jnp.einsum(
            "rhqk,rkhd->rhqd",
            weights.astype(jnp.bfloat16),
            value_piece.reshape(rows_here, piece_len, HEADS, head_dim),
            preferred_element_type=jnp.float32,
        )
        return (new_top, new_total, product)

    init_state = (
        jnp.full((rows_here, HEADS, shard_len), negative_big, jnp.float32),
        jnp.zeros((rows_here, HEADS, shard_len), jnp.float32),
        jnp.zeros((rows_here, HEADS, shard_len, head_dim), jnp.float32),
    )
    if is_cross:
        final_top, final_total, final_sum = absorb(
            init_state,
            (
                lax.all_gather(keys_local, "seq", axis=1, tiled=True),
                lax.all_gather(values_local, "seq", axis=1, tiled=True),
                lax.all_gather(for_sending(key_docs), "seq", axis=1, tiled=True),
            ),
        )
    else:
        final_top, final_total, final_sum = absorb(
            init_state,
            (
                lax.all_gather(keys_local, "seq", axis=1, tiled=True),
                lax.all_gather(values_local, "seq", axis=1, tiled=True),
                lax.all_gather(key_docs, "seq", axis=1, tiled=True),
            ),
        )
    attended = (
        (final_sum / final_total[..., None])
        .transpose(0, 2, 1, 3)
        .reshape(rows_here, shard_len, model_width)
    )
    return (attended, final_top + jnp.log(final_total))


def attend_back(
    queries,
    keys_local,
    values_local,
    query_docs,
    key_docs,
    causal,
    log_total,
    grad_attended,
    is_cross,
):
    rows_here, shard_len, model_width = queries.shape
    head_dim = model_width // HEADS
    score_scale = head_dim ** (-0.5)
    query_place = lax.axis_index("seq") * shard_len + jnp.arange(shard_len)
    if is_cross:
        keys_full, values_full, docs_full = (
            lax.all_gather(keys_local, "seq", axis=1, tiled=True),
            lax.all_gather(values_local, "seq", axis=1, tiled=True),
            lax.all_gather(for_sending(key_docs), "seq", axis=1, tiled=True).astype(key_docs.dtype),
        )
    else:
        keys_full, values_full, docs_full = (
            lax.all_gather(keys_local, "seq", axis=1, tiled=True),
            lax.all_gather(values_local, "seq", axis=1, tiled=True),
            lax.all_gather(key_docs, "seq", axis=1, tiled=True),
        )
    full_len = keys_full.shape[1]
    query_heads = queries.reshape(rows_here, shard_len, HEADS, head_dim)
    key_heads = keys_full.reshape(rows_here, full_len, HEADS, head_dim)
    value_heads = values_full.reshape(rows_here, full_len, HEADS, head_dim)
    grad_heads = grad_attended.reshape(rows_here, shard_len, HEADS, head_dim)
    raw_scores = jnp.einsum(
        "rqhd,rkhd->rhqk", query_heads, key_heads, preferred_element_type=jnp.float32
    )
    allowed = allowed_mask(query_docs, docs_full, query_place, jnp.arange(full_len), causal)
    shifted = jnp.where(allowed, raw_scores * score_scale - log_total[..., None], negative_big)
    probs = jnp.where(allowed, jnp.exp(shifted), 0.0)
    grad_probs = jnp.einsum(
        "rqhd,rkhd->rhqk", grad_heads, value_heads, preferred_element_type=jnp.float32
    )
    delta = jnp.sum(probs * grad_probs, axis=-1)
    grad_scores = (probs * (grad_probs - delta[..., None]) * score_scale).astype(jnp.bfloat16)
    grad_queries = jnp.einsum(
        "rhqk,rkhd->rqhd", grad_scores, key_heads, preferred_element_type=jnp.float32
    ).reshape(rows_here, shard_len, model_width)
    probs_low = probs.astype(jnp.bfloat16)

    def key_terms(span):
        grad_keys = jnp.einsum(
            "rhqk,rqhd->krhd", grad_scores, query_heads, preferred_element_type=jnp.float32
        )
        grad_values = jnp.einsum(
            "rhqk,rqhd->krhd", probs_low, grad_heads, preferred_element_type=jnp.float32
        )
        return jnp.concatenate(
            [
                grad_keys.reshape(span, rows_here, model_width),
                grad_values.reshape(span, rows_here, model_width),
            ],
            axis=-1,
        )

    if is_cross:
        pair_terms = lax.psum_scatter(
            key_terms(shard_len * lax.axis_size("seq")).astype(jnp.bfloat16),
            "seq",
            scatter_dimension=0,
            tiled=True,
        ).astype(jnp.float32)
    else:
        pair_terms = lax.psum_scatter(
            key_terms(shard_len * lax.axis_size("seq")).astype(jnp.bfloat16),
            "seq",
            scatter_dimension=0,
            tiled=True,
        ).astype(jnp.float32)
    return (grad_queries, pair_terms.transpose(1, 0, 2))


def layer_forward(hidden_in, doc_own, memory, memory_docs, weights, is_decoder):
    (
        qkv_weight,
        out_weight,
        in_weight,
        down_weight,
        gains_pair,
        query_weight,
        pair_weight,
        cross_weight,
        cross_gains,
    ) = weights
    model_width = hidden_in.shape[-1]
    mixed = matmul(hidden_in, qkv_weight).astype(jnp.bfloat16)
    attended, self_lse = attend(
        mixed[..., :model_width],
        mixed[..., model_width : 2 * model_width],
        mixed[..., 2 * model_width :],
        doc_own,
        doc_own,
        is_decoder,
        False,
    )
    attended = attended.astype(jnp.bfloat16)
    first, first_unit, first_inv = normalize(
        hidden_in.astype(jnp.float32) + matmul(attended, out_weight), gains_pair[0]
    )
    first_low = first.astype(jnp.bfloat16)
    cross_queries = matmul(first_low, query_weight).astype(jnp.bfloat16)
    pair = matmul(memory, pair_weight).astype(jnp.bfloat16)
    cross_att, cross_lse = attend(
        cross_queries,
        pair[..., :model_width],
        pair[..., model_width:],
        doc_own,
        memory_docs,
        False,
        True,
    )
    cross_att = cross_att.astype(jnp.bfloat16)
    second_cross, second_unit, second_inv = normalize(
        first + matmul(cross_att, cross_weight), cross_gains
    )
    second = jnp.where(is_decoder, second_cross, first)
    second_low = second.astype(jnp.bfloat16)
    upward = matmul(second_low, in_weight)
    active = jax.nn.silu(upward).astype(jnp.bfloat16)
    result, third_unit, third_inv = normalize(second + matmul(active, down_weight), gains_pair[1])
    saved = {
        "mixed": mixed,
        "attended": attended,
        "self_lse": self_lse,
        "first_unit": first_unit,
        "first_inv": first_inv,
        "first_low": first_low,
        "cross_queries": cross_queries,
        "pair": pair,
        "cross_att": cross_att,
        "cross_lse": cross_lse,
        "second_unit": second_unit,
        "second_inv": second_inv,
        "second_low": second_low,
        "upward": upward,
        "active": active,
        "third_unit": third_unit,
        "third_inv": third_inv,
    }
    return (result, saved)


def layer_backward(
    grad_result, saved, hidden_in, doc_own, memory, memory_docs, weights, is_decoder
):
    (
        qkv_weight,
        out_weight,
        in_weight,
        down_weight,
        gains_pair,
        query_weight,
        pair_weight,
        cross_weight,
        cross_gains,
    ) = weights
    model_width = hidden_in.shape[-1]
    grad_third, grad_gain_late = normalize_back(
        grad_result, saved["third_unit"], gains_pair[1], saved["third_inv"]
    )
    down_grad = grad_third.astype(jnp.bfloat16)
    grad_down_w = contract(saved["active"], down_grad)
    grad_active = matmul_back(down_grad, down_weight).astype(jnp.bfloat16)
    sigmoid_up = jax.nn.sigmoid(saved["upward"])
    grad_upward = (
        grad_active.astype(jnp.float32)
        * (sigmoid_up + saved["upward"] * sigmoid_up * (1.0 - sigmoid_up))
    ).astype(jnp.bfloat16)
    grad_in_w = contract(saved["second_low"], grad_upward)
    grad_second = grad_third + matmul_back(grad_upward, in_weight)
    grad_cross_sum, grad_cross_gain = normalize_back(
        grad_second, saved["second_unit"], cross_gains, saved["second_inv"]
    )
    decoder_flag = is_decoder.astype(jnp.float32)
    grad_cross_sum = grad_cross_sum * decoder_flag
    grad_cross_gain = grad_cross_gain * decoder_flag
    cross_branch = grad_cross_sum.astype(jnp.bfloat16)
    grad_cross_w = contract(saved["cross_att"], cross_branch)
    grad_cross_att = matmul_back(cross_branch, cross_weight).astype(jnp.bfloat16)
    pair = saved["pair"]
    grad_cross_q, grad_pair = attend_back(
        saved["cross_queries"],
        pair[..., :model_width],
        pair[..., model_width:],
        doc_own,
        memory_docs,
        False,
        saved["cross_lse"],
        grad_cross_att,
        True,
    )
    grad_cross_q = grad_cross_q.astype(jnp.bfloat16)
    grad_pair = grad_pair.astype(jnp.bfloat16)
    grad_query_w = contract(saved["first_low"], grad_cross_q)
    grad_pair_w = contract(memory, grad_pair)
    grad_memory = matmul_back(grad_pair, pair_weight)
    grad_first = jnp.where(
        is_decoder, grad_cross_sum + matmul_back(grad_cross_q, query_weight), grad_second
    )
    grad_first_sum, grad_gain_early = normalize_back(
        grad_first, saved["first_unit"], gains_pair[0], saved["first_inv"]
    )
    self_branch = grad_first_sum.astype(jnp.bfloat16)
    grad_out_w = contract(saved["attended"], self_branch)
    grad_attended = matmul_back(self_branch, out_weight).astype(jnp.bfloat16)
    mixed = saved["mixed"]
    grad_queries, grad_pair_self = attend_back(
        mixed[..., :model_width],
        mixed[..., model_width : 2 * model_width],
        mixed[..., 2 * model_width :],
        doc_own,
        doc_own,
        is_decoder,
        saved["self_lse"],
        grad_attended,
        False,
    )
    grad_mixed = jnp.concatenate([grad_queries, grad_pair_self], axis=-1).astype(jnp.bfloat16)
    grad_qkv_w = contract(hidden_in, grad_mixed)
    grad_hidden = grad_first_sum + matmul_back(grad_mixed, qkv_weight)
    layer_grads = (
        grad_qkv_w,
        grad_out_w,
        grad_in_w,
        grad_down_w,
        jnp.stack([grad_gain_early, grad_gain_late]),
        grad_query_w,
        grad_pair_w,
        grad_cross_w,
        grad_cross_gain,
    )
    return (grad_hidden, grad_memory, layer_grads)


def any_rows(
    layer_input,
    segment_ids,
    attn_qkv,
    attn_out,
    ffn_in,
    ffn_out,
    norm_gain,
    cross_query,
    cross_pair,
    cross_out,
    cross_gain,
    out_cotangent,
):
    micro_count = layer_input.shape[1]
    section_index = lax.axis_index("section")
    is_decoder = section_index == 1
    weights = (
        attn_qkv[0],
        attn_out[0],
        ffn_in[0],
        ffn_out[0],
        norm_gain[0],
        cross_query,
        cross_pair,
        cross_out,
        cross_gain,
    )
    inputs_all = layer_input[0]
    docs_all = segment_ids[0]
    slot_ids = jnp.arange(micro_count)
    received = (jnp.zeros_like(inputs_all[0]), jnp.zeros_like(docs_all[0]))
    results = jnp.zeros_like(inputs_all)
    memories = []
    memory_doc_list = []
    for step_index in range(micro_count + 1):
        batch_index = step_index - section_index
        is_valid = (batch_index >= 0) & (batch_index < micro_count)
        chosen = jnp.clip(batch_index, 0, micro_count - 1)
        hidden_in = lax.dynamic_index_in_dim(inputs_all, chosen, 0, keepdims=False)
        doc_own = lax.dynamic_index_in_dim(docs_all, chosen, 0, keepdims=False)
        memory = received[0]
        memory_docs = jnp.where(is_valid & is_decoder, received[1], doc_own)
        memories.append(memory)
        memory_doc_list.append(memory_docs)
        result, saved = layer_forward(hidden_in, doc_own, memory, memory_docs, weights, is_decoder)
        low_result = result.astype(jnp.bfloat16)
        writing = (slot_ids == chosen) & is_valid
        results = jnp.where(writing[:, None, None, None], low_result[None], results)
        if step_index < micro_count:
            received = from_behind((low_result, doc_own), "section", 1)
    memory_stack = jnp.stack(memories)
    memory_doc_stack = jnp.stack(memory_doc_list)
    totals = tuple((jnp.zeros(weight.shape, jnp.float32) for weight in weights))
    input_grads = jnp.zeros(inputs_all.shape, jnp.float32)
    returned = jnp.zeros(inputs_all.shape[1:], jnp.float32)
    for step_index in range(micro_count + 1):
        batch_index = micro_count - step_index - section_index
        is_valid = (batch_index >= 0) & (batch_index < micro_count)
        chosen = jnp.clip(batch_index, 0, micro_count - 1)
        forward_step = jnp.clip(batch_index + section_index, 0, micro_count)
        hidden_in = lax.dynamic_index_in_dim(inputs_all, chosen, 0, keepdims=False)
        doc_own = lax.dynamic_index_in_dim(docs_all, chosen, 0, keepdims=False)
        memory = lax.dynamic_index_in_dim(memory_stack, forward_step, 0, keepdims=False)
        memory_docs = lax.dynamic_index_in_dim(memory_doc_stack, forward_step, 0, keepdims=False)
        discarded, saved = layer_forward(
            hidden_in, doc_own, memory, memory_docs, weights, is_decoder
        )
        cotangent = jnp.where(
            is_decoder,
            lax.dynamic_index_in_dim(out_cotangent, chosen, 0, keepdims=False).astype(jnp.float32),
            returned,
        )
        grad_hidden, grad_memory, layer_grads = layer_backward(
            cotangent, saved, hidden_in, doc_own, memory, memory_docs, weights, is_decoder
        )
        valid_flag = is_valid.astype(jnp.float32)
        totals = tuple(
            (running + valid_flag * fresh for running, fresh in zip(totals, layer_grads))
        )
        writing = (slot_ids == chosen) & is_valid
        input_grads = jnp.where(writing[:, None, None, None], grad_hidden[None], input_grads)
        if step_index < micro_count:
            returned = from_behind(grad_memory.astype(jnp.bfloat16), "section", -1).astype(
                grad_memory.dtype
            )
    group_sums = lax.psum(
        (
            totals[0],
            totals[1],
            totals[2],
            totals[3],
            totals[4],
            totals[5],
            totals[6],
            totals[7],
            totals[8],
        ),
        ("seq", "dp"),
    )
    section_sums = group_sums[:5]
    cross_sums = (
        from_root(group_sums[5].astype(jnp.bfloat16), "section", 1).astype(jnp.float32),
        from_root(group_sums[6].astype(jnp.bfloat16), "section", 1).astype(jnp.float32),
        from_root(group_sums[7].astype(jnp.bfloat16), "section", 1).astype(jnp.float32),
        from_root(group_sums[8].astype(jnp.bfloat16), "section", 1).astype(jnp.float32),
    )
    return (
        results[None],
        input_grads[None],
        section_sums[0][None],
        section_sums[1][None],
        section_sums[2][None],
        section_sums[3][None],
        section_sums[4][None],
        cross_sums[0],
        cross_sums[1],
        cross_sums[2],
        cross_sums[3],
    )


def split_rows(
    layer_input,
    segment_ids,
    attn_qkv,
    attn_out,
    ffn_in,
    ffn_out,
    norm_gain,
    cross_query,
    cross_pair,
    cross_out,
    cross_gain,
    out_cotangent,
):
    micros = layer_input.shape[1]
    length, width = layer_input.shape[3:]
    hidden = ffn_in.shape[-1]
    q_tiles = length // TILE
    group = lax.axis_size("dp") // 2
    axes = ("section", "seq", "dp")
    decoder = lax.axis_index("section") == 1
    flag = decoder.astype(jnp.int32)
    x = lax.axis_index("seq")
    core = lax.rem(lax.axis_index("dp"), 2)
    z = lax.axis_index("dp") // 2
    places = [(t, i, k, c) for t in range(2) for i in range(2) for k in range(group) for c in range(2)]

    def number(t, i, k, c):
        return ((t * 2 + i) * group + k) * 2 + c

    def send(values, target, section=None):
        route = [
            (number(*place), number(*target(*place)))
            for place in places
            if section in (None, place[0]) and target(*place)
        ]
        return lax.ppermute(values, axes, route)

    def to_core(t, i, k, c):
        return (t, i, k, 1 - c)

    def to_x(t, i, k, c):
        return (t, 1 - i, k, c)

    def to_row(t, i, k, c):
        return (t, c, k, i)

    def to_decoder(t, i, k, c):
        return (1, i, k, c) if t == 0 else None

    def to_encoder(t, i, k, c):
        return (0, i, k, c) if t == 1 else None

    def fence(values, *before):
        return lax.optimization_barrier((values,) + before)[0]

    def exchange(values):
        return send(values, to_core)

    low = ((length, width), bf16)
    wide = ((length, width), f32)
    marked = ((length + 16, width), bf16)
    both = ((2 * length, width), bf16)
    keys_all = ((2 * length, 2 * width), bf16)
    mixing = ((width, 3 * width), bf16)
    inner = ((length, hidden), bf16)
    lse = ((q_tiles, 8, 2 * TILE), f32)
    stat = ((length, LANES), f32)
    square = ((width, width), bf16)
    rising = ((width, hidden), bf16)
    falling = ((hidden, width), bf16)
    gain_rows = ((8, width), f32)

    meta = jnp.stack([flag, core, x, z]).astype(jnp.int32)
    numbers = segment_ids[0, :, 0].astype(bf16)
    padding = jnp.zeros((15, width), bf16)
    with_numbers = [
        jnp.concatenate([layer_input[0, micro, 0], numbers[micro][None], padding])
        for micro in range(micros)
    ]
    own = [send(with_numbers[0], to_row)]
    for micro in range(1, micros):
        own.append(send(fence(with_numbers[micro], own[-1]), to_row))
    other = [exchange(part) for part in own]

    plain = dict(meta=meta)
    small = dict(gains=norm_gain[0])
    forward, memories, memories_other = [], [], []
    for micro in range(micros):
        call = launch(
            self_forward,
            micro,
            None,
            plain,
            small,
            dict(
                x_own_h=own[micro],
                x_other_h=other[micro],
                w_mixed_h=attn_qkv[0],
                w_out_h=attn_out[0],
                w_in_h=ffn_in[0],
                w_down_h=ffn_out[0],
            ),
            dict(
                q_o=low,
                kv_o=keys_all,
                att_o=low,
                lse_o=lse,
                unit1_o=wide,
                inv1_o=stat,
                first_low_o=low,
                memory_o=marked,
                ffn_low_o=low,
                act_o=inner,
                slope_o=inner,
                unit2_o=wide,
                inv2_o=stat,
            ),
            dict(
                **attention_scratch(length, width),
                **forward_scratch(length, width),
                x=both,
                w_mixed=mixing,
                w_out=square,
                w_in=rising,
                w_down=falling,
                unit1=wide,
                inv1=stat,
                first_low=low,
                memory=marked,
                act=inner,
                slope=inner,
                unit2=wide,
                inv2=stat,
                sum=wide,
            ),
            28,
            26,
            after=(forward[0].lse_o,) if micro else (),
        )
        forward.append(call)
        memories.append(send(call.memory_o, to_decoder))

    for micro in range(micros):
        memories_other.append(exchange(fence(memories[micro], forward[-1].lse_o)))
    cotangent = send(fence(out_cotangent[:, 0], forward[0].lse_o), to_row)

    cross, grads_memory, made = [], [], []
    after = (forward[-1].lse_o,)
    for micro in range(micros):
        done = forward[micro]
        call = launch(
            cross_both_ways,
            micro,
            1,
            plain,
            dict(**small, cross_gain=cross_gain[None]),
            dict(
                x_own_h=own[micro],
                memory_own_h=memories[micro],
                memory_other_h=memories_other[micro],
                w_pair_h=cross_pair,
                first_low_h=done.first_low_o,
                unit1_h=done.unit1_o,
                w_query_h=cross_query,
                w_cross_h=cross_out,
                w_in_h=ffn_in[0],
                w_down_h=ffn_out[0],
                cot_h=cotangent,
            ),
            dict(
                att_o=low,
                ffn_low_o=low,
                act_o=inner,
                decoded_o=low,
                down_grad_o=low,
                up_grad_o=inner,
                gain_grads_o=gain_rows,
                branch_o=low,
                dq_low_o=low,
                dkv_o=keys_all,
                part_own_o=wide,
                part_other_o=low,
                grad_first_o=wide,
            ),
            dict(
                **attention_scratch(length, width),
                **forward_scratch(length, width),
                **backward_scratch(length, width),
                x=both,
                w_pair=((width, 2 * width), bf16),
                first_low=low,
                unit1=wide,
                w_query=square,
                w_cross=square,
                w_in=rising,
                w_down=falling,
                cot=low,
                unit2=wide,
                inv2=stat,
                second_low=low,
                act=inner,
                slope=inner,
                sum=wide,
                decoded=low,
                keep=wide,
                down_grad=low,
                up_grad=inner,
                gain_grads=gain_rows,
                branch=low,
                part_own=wide,
            ),
            36,
            44,
            dict(act_o=done.act_o, ffn_low_o=done.ffn_low_o),
            after,
        )
        cross.append(call)
        away = call.part_other_o
        if micro:
            away = fence(away, grads_memory[-1])
        total = call.part_own_o + exchange(away).astype(f32)
        made.append(total.astype(bf16))
        after = (made[micro],)
        grads_memory.append(send(made[micro], to_encoder))

    def backward_feed(micro, after):
        done, late = forward[micro], cross[micro]
        return launch(
            feed_backward_alone,
            micro,
            0,
            plain,
            dict(gains=norm_gain[0]),
            dict(
                grad_memory_h=grads_memory[micro],
                unit2_h=done.unit2_o,
                inv2_h=done.inv2_o,
                slope_h=done.slope_o,
                w_in_h=ffn_in[0],
                w_down_h=ffn_out[0],
            ),
            dict(gain_late_o=gain_rows, down_grad_o=low, up_grad_o=inner, grad_first_o=wide),
            dict(
                cot=low,
                unit2=wide,
                inv2=stat,
                slope=inner,
                w_in=rising,
                w_down=falling,
                gain_grads=gain_rows,
                keep=wide,
                down_grad=low,
                up_grad=inner,
                sum=wide,
            ),
            12,
            10,
            dict(
                down_grad_o=late.down_grad_o, up_grad_o=late.up_grad_o, grad_first_o=late.grad_first_o
            ),
            after,
        )

    def backward_self(micro, side, grad_first, previous=None, after=(), halfway=None):
        done = forward[micro]
        heads = width // LANES
        given = dict(
            x_own_h=own[micro],
            x_other_h=other[micro],
            q_h=done.q_o,
            kv_h=done.kv_o,
            att_h=done.att_o,
            lse_h=done.lse_o,
        )
        ahead = dict(
            grad_first_h=grad_first,
            unit1_h=done.unit1_o,
            inv1_h=done.inv1_o,
            w_out_h=attn_out[0],
        )
        makes = dict(dq_low_o=low, dkv_o=keys_all)
        makes_first = dict(gain_early_o=gain_rows, branch_o=low)
        makes_last = dict(part_own_o=wide, part_other_o=low)
        scratch = dict(
            **attention_scratch(length, width),
            **backward_scratch(length, width),
            w_out=square,
            w_mixed=mixing,
            unit1=wide,
            inv1=stat,
            keep=wide,
            branch=low,
            grad_att=low,
            gain_grads=gain_rows,
        )

        def part(first, last, large, outs, work, previous, after):
            return launch(
                self_backward,
                (micro, first, last),
                side,
                plain,
                small,
                dict(**given, **large),
                dict(**makes, **outs),
                scratch,
                28,
                work,
                previous,
                after,
            )

        if halfway is None:
            large = dict(**ahead, w_mixed_h=attn_qkv[0])
            outs = dict(**makes_first, **makes_last)
            return part(0, heads, large, outs, 22, previous, after)
        outs = dict(**makes_first, grad_sum_o=wide, grad_att_o=low)
        one = part(0, heads // 2, ahead, outs, 12, None, after)
        large = dict(
            w_mixed_h=attn_qkv[0],
            grad_sum_h=one.grad_sum_o,
            grad_att_h=one.grad_att_o,
            dq_h=one.dq_low_o,
            dkv_h=one.dkv_o,
        )
        two = part(heads // 2, heads, large, makes_last, 12, None, halfway(one))
        return types.SimpleNamespace(**{**vars(one), **vars(two)})

    def weight_grads(plan, arrays, scratch, after=(), kernel=contract_blocks, outs=None):
        blocks = ((2, width, width), bf16)
        call = launch(
            kernel,
            plan,
            None,
            plain,
            dict(),
            arrays,
            outs or dict(sent_o=blocks, kept_o=blocks),
            dict(**scratch, blocks=((4, width, width), bf16)),
            36,
            8,
            after=after,
        )
        return call.all_o if outs else (call.sent_o, call.kept_o)

    def first_sums(halves):
        sent, kept = halves
        got = exchange(sent)

        def block(side):
            return sum(
                lax.dynamic_index_in_dim(part, side, 0, keepdims=False).astype(f32)
                for part in (kept, got)
            )

        return block(1 - x).astype(bf16), block(x)

    def middle_sums(sums):
        away, total = sums
        return (total + send(away, to_x).astype(f32)).astype(bf16)

    def last_sums(total, *later):
        shares = total.reshape(group, width // group, width)

        def share(step):
            return lax.dynamic_index_in_dim(shares, lax.rem(z + step, group), 0, keepdims=False)

        parts = [share(0)]
        for step in range(1, group):
            parts.append(send(share(step), along_z(step)))
        if later:
            parts = [fence(part, *later) for part in parts]
        return sum(part.astype(f32) for part in parts).astype(bf16)

    def along_z(step):
        return lambda t, i, k, c: (t, i, (k + step) % group, c)

    def gather_z(share):
        return jnp.stack([share] + [send(share, along_z(step)) for step in range(1, group)])

    def gain_block(rows):
        filled = jnp.concatenate([jnp.stack(rows), jnp.zeros((16 - len(rows), width), f32)])
        return filled.astype(bf16)

    def spread(targets, own, own_x, outs, parts):
        return launch(
            spread_pieces,
            targets,
            None,
            plain,
            dict(),
            dict(own_h=own, own_x_h=own_x, other_h=exchange(own), other_x_h=exchange(own_x)),
            outs,
            dict(
                pieces=((4,) + own.shape, bf16),
                wide=((4 * group * parts, width // group, width), f32),
                gain_grads=((16, width), f32),
            ),
            8 + 4 * group * parts,
            5,
        )

    tokens, all_tokens = micros * length, 2 * micros * length
    turn, turn_all = ((width, tokens), bf16), ((width, all_tokens), bf16)
    narrow, narrow_all = ((tokens, width), bf16), ((all_tokens, width), bf16)
    pair_all = ((all_tokens, 2 * width), bf16)
    deep = ((tokens, hidden), bf16)

    def part_of(buffer, *sources):
        return lambda column: (buffer, sources, column)

    def key_rows(buffer, sources):
        first, second = pl.ds(0, length), pl.ds(length, length)
        return part_of(buffer, *[source.at[rows] for rows in (first, second) for source in sources])

    def cross_plan(r):
        rows = pl.ds(0, length)
        low_part = part_of(r.low, r.low0_h, r.low1_h)
        att_part = part_of(r.att, r.att0_h, r.att1_h)
        dq_part = part_of(r.dq, r.dq0_h, r.dq1_h)
        branch_part = part_of(r.branch, r.branch0_h, r.branch1_h)
        sources = (r.mem0_h, r.mem1_h, r.mem2_h, r.mem3_h)
        mem_part = part_of(r.mem, *[source.at[rows] for source in sources])
        pair_part = key_rows(r.pair, (r.pair0_h, r.pair1_h))
        return [
            (r.turn, low_part(0), dq_part(0)),
            (r.turn_att, att_part(0), branch_part(0)),
            (r.turn_all, mem_part(0), pair_part(0)),
            (r.turn_all, mem_part(0), pair_part(1)),
        ]

    def rising_plan(r):
        low_part = part_of(r.low, r.low0_h, r.low1_h)
        up_part = part_of(r.up, r.up0_h, r.up1_h)
        return [(r.turn, low_part(0), up_part(block)) for block in range(4)]

    def falling_plan(r):
        act_part = part_of(r.act, r.act0_h, r.act1_h)
        down_part = part_of(r.down, r.down0_h, r.down1_h)
        return [(r.turn, act_part(block), down_part(0)) for block in range(4)]

    def self_plan(r):
        rows = pl.ds(0, length)
        sources = (r.x0_h, r.x1_h, r.x2_h, r.x3_h)
        x_part = part_of(r.x, *[source.at[rows] for source in sources])
        dq_part = part_of(r.dq, r.dq0_h, r.dq1_h)
        pair_part = key_rows(r.pair, (r.pair0_h, r.pair1_h))
        att_part = part_of(r.att, r.att0_h, r.att1_h)
        branch_part = part_of(r.branch, r.branch0_h, r.branch1_h)
        return [
            (r.turn_all, x_part(0), dq_part(0)),
            (r.turn_all, x_part(0), pair_part(0)),
            (r.turn_all, x_part(0), pair_part(1)),
            (r.turn, att_part(0), branch_part(0)),
        ]

    last = micros - 1
    feeds, ends = [None] * micros, [None] * micros
    cross_local = weight_grads(
        cross_plan,
        dict(
            low0_h=forward[0].first_low_o,
            low1_h=forward[1].first_low_o,
            dq0_h=cross[0].dq_low_o,
            dq1_h=cross[1].dq_low_o,
            att0_h=cross[0].att_o,
            att1_h=cross[1].att_o,
            branch0_h=cross[0].branch_o,
            branch1_h=cross[1].branch_o,
            mem0_h=memories[0],
            mem1_h=memories[1],
            mem2_h=memories_other[0],
            mem3_h=memories_other[1],
            pair0_h=cross[0].dkv_o,
            pair1_h=cross[1].dkv_o,
            gain0_h=cross[0].gain_grads_o,
            gain1_h=cross[1].gain_grads_o,
        ),
        dict(
            low=narrow,
            dq=narrow,
            att=narrow,
            branch=narrow,
            mem=narrow_all,
            pair=pair_all,
            turn=turn,
            turn_att=turn,
            turn_all=turn_all,
            gain0=gain_rows,
            gain1=gain_rows,
            extra=((32, width), bf16),
        ),
        (made[last],),
        contract_cross,
        dict(all_o=((4 * width + 32, width), bf16)),
    )
    cross_sums = lax.psum(cross_local, axes[1:])
    results = jnp.stack(
        [
            jnp.where(decoder, call.decoded_o, done.memory_o[:length])
            for call, done in zip(cross, forward)
        ]
    )
    results = send(results, to_row)
    latest = made[last]

    def part_sum(micro):
        end = ends[micro]
        total = (end.part_own_o + exchange(end.part_other_o).astype(f32)).astype(bf16)
        return total, send(total, to_row)

    steps = []
    for micro in range(last):
        feeds[micro] = backward_feed(micro, (latest,))
        first = feeds[micro].grad_first_o
        ends[micro] = backward_self(micro, 0, first)
        ends[micro] = backward_self(micro, 1, first, vars(ends[micro]), (cross_local, grads_memory[last]))
        steps.append(part_sum(micro))
        latest = ends[micro].gain_early_o
    feeds[last] = backward_feed(last, (latest,))

    rising_halves = weight_grads(
        rising_plan,
        dict(
            low0_h=cross[0].ffn_low_o,
            low1_h=cross[1].ffn_low_o,
            up0_h=feeds[0].up_grad_o,
            up1_h=feeds[1].up_grad_o,
        ),
        dict(low=narrow, up=deep, turn=turn),
        (results,) + tuple(step[0] for step in steps),
    )
    rising_sums = first_sums(rising_halves)
    falling_halves = weight_grads(
        falling_plan,
        dict(
            act0_h=cross[0].act_o,
            act1_h=cross[1].act_o,
            down0_h=feeds[0].down_grad_o,
            down1_h=feeds[1].down_grad_o,
        ),
        dict(act=deep, down=narrow, turn=turn),
        (rising_sums[0],) + tuple(step[1] for step in steps),
    )
    falling_sums = first_sums(falling_halves)
    rising_total, falling_total = middle_sums(rising_sums), middle_sums(falling_sums)
    shares = []

    def halfway(one):
        shares.append(last_sums(rising_total, one.gain_early_o))
        return (shares[0], falling_total)

    ends[last] = backward_self(
        last,
        None,
        feeds[last].grad_first_o,
        None,
        (rising_total, falling_sums[0]),
        halfway,
    )
    rising_share, falling_share = shares[0], last_sums(falling_total, ends[last].part_own_o)

    self_halves = weight_grads(
        self_plan,
        dict(
            x0_h=own[0],
            x1_h=own[1],
            x2_h=other[0],
            x3_h=other[1],
            dq0_h=ends[0].dq_low_o,
            dq1_h=ends[1].dq_low_o,
            pair0_h=ends[0].dkv_o,
            pair1_h=ends[1].dkv_o,
            att0_h=forward[0].att_o,
            att1_h=forward[1].att_o,
            branch0_h=ends[0].branch_o,
            branch1_h=ends[1].branch_o,
        ),
        dict(
            x=narrow_all,
            dq=narrow,
            pair=pair_all,
            att=narrow,
            branch=narrow,
            turn=turn,
            turn_all=turn_all,
        ),
        (falling_share,),
    )
    away, total = first_sums(self_halves)
    self_total = middle_sums((away, total))
    feed_own = gather_z(jnp.concatenate([rising_share, falling_share]))
    self_share = last_sums(self_total)
    feed_own_x = send(fence(feed_own, self_total), to_x)
    steps.append(part_sum(last))
    early = sum(end.gain_early_o[0] for end in ends)
    late = jnp.where(
        decoder,
        sum(call.gain_grads_o[0] for call in cross),
        sum(call.gain_late_o[0] for call in feeds),
    )
    self_own = gather_z(jnp.concatenate([self_share, gain_block([early, late])]))
    self_own_x = send(fence(self_own, feed_own_x), to_x)

    def columns(block):
        return pl.ds(block * width, width)

    def feed_targets(r, block, row, rows):
        return [
            r.up_o.at[pl.ds(row, rows), columns(block)],
            r.down_o.at[pl.ds(block * width + row, rows)],
        ]

    def self_targets(r, block, row, rows):
        if block == 3:
            return [r.out_o.at[pl.ds(row, rows)]]
        return [r.mixed_o.at[pl.ds(row, rows), columns(block)]]

    square_out, gains_out = ((width, width), f32), ((16, width), f32)
    feed_grads = spread(
        feed_targets,
        feed_own,
        feed_own_x,
        dict(up_o=((width, hidden), f32), down_o=((hidden, width), f32)),
        2,
    )
    self_grads = spread(
        self_targets,
        self_own,
        self_own_x,
        dict(mixed_o=((width, 3 * width), f32), out_o=square_out, gains_o=gains_out),
        1,
    )

    grad_input = jnp.stack([step[1] for step in steps])
    half_rows = cross_sums.shape[0] // 2
    cross_half = send(
        lax.dynamic_slice_in_dim(
            fence(cross_sums, self_halves[0]), core * half_rows, half_rows
        ),
        to_encoder,
    )
    cross_other = exchange(cross_half)
    halves = [
        jnp.where(core == 0, cross_half, cross_other),
        jnp.where(core == 0, cross_other, cross_half),
    ]
    cross_sums = jnp.where(decoder, cross_sums, jnp.concatenate(halves))
    cross_parts = [
        cross_sums[block * width : (block + 1) * width].astype(f32) for block in range(4)
    ]
    return (
        results[None, :, None],
        grad_input.astype(f32)[None, :, None],
        self_grads.mixed_o[None],
        self_grads.out_o[None],
        feed_grads.up_o[None],
        feed_grads.down_o[None],
        self_grads.gains_o[None, :2],
        cross_parts[0],
        jnp.concatenate(cross_parts[2:], axis=1),
        cross_parts[1],
        cross_sums[4 * width].astype(f32),
    )


def shards(*arrays):
    layer_input = arrays[0]
    micros, rows, length = layer_input.shape[1:4]
    simple = (
        lax.axis_size("section") == 2
        and lax.axis_size("seq") == 2
        and lax.axis_size("dp") in (4, 8, 16)
        and (micros, rows) == (2, 1)
        and length == layer_input.shape[-1] == CHUNK
        and arrays[4].shape[-1] == 4 * CHUNK
    )
    return split_rows(*arrays) if simple else any_rows(*arrays)


def solution(mesh):
    in_specs = (
        P("section", None, "dp", "seq", None),
        P("section", None, "dp", "seq"),
        P("section", None, None),
        P("section", None, None),
        P("section", None, None),
        P("section", None, None),
        P("section", None, None),
        P(),
        P(),
        P(),
        P(),
        P(None, "dp", "seq", None),
    )
    out_specs = (
        P("section", None, "dp", "seq", None),
        P("section", None, "dp", "seq", None),
        P("section", None, None),
        P("section", None, None),
        P("section", None, None),
        P("section", None, None),
        P("section", None, None),
        P(),
        P(),
        P(),
        P(),
    )
    return jax.shard_map(shards, mesh=mesh, in_specs=in_specs, out_specs=out_specs, check_vma=False)
```

```python
import types

import jax
import jax.numpy as jnp
from jax import lax
from jax.experimental import pallas as pl
from jax.experimental.pallas import tpu as pltpu
from jax.sharding import PartitionSpec as P

HEADS = 8
TILE = 256
LANES = 128
CHUNK = 512

f32 = jnp.float32
bf16 = jnp.bfloat16
negative_big = -1e30
epsilon = 1e-05


def dot(left, right):
    return lax.dot_general(left, right, (((1,), (0,)), ((), ())), preferred_element_type=f32)


def dot_nt(left, right):
    return lax.dot_general(left, right, (((1,), (1,)), ((), ())), preferred_element_type=f32)


def dot_tn(left, right):
    return lax.dot_general(left, right, (((0,), (0,)), ((), ())), preferred_element_type=f32)


def standardize(values):
    center = values - jnp.mean(values, axis=-1, keepdims=True)
    inverse = lax.rsqrt(jnp.mean(center * center, axis=-1, keepdims=True) + epsilon)
    return center * inverse, inverse


def standardize_back(grad_out, standard, gain_row, inverse):
    scaled = grad_out * gain_row
    grad_in = inverse * (
        scaled
        - jnp.mean(scaled, axis=-1, keepdims=True)
        - standard * jnp.mean(scaled * standard, axis=-1, keepdims=True)
    )
    return grad_in, jnp.sum(grad_out * standard, axis=0, keepdims=True)


class Copies:
    def __init__(self, sems):
        self.sems = sems
        self.used = 0

    def start(self, source, target):
        copy = pltpu.make_async_copy(source, target, self.sems.at[self.used])
        self.used += 1
        copy.start()
        return copy


def wait_all(copies):
    for copy in copies:
        copy.wait()


def spread_pairs(target, source, factor, pairs):
    tiles = target.shape[1]
    half = lax.broadcasted_iota(jnp.int32, (TILE, LANES), 1) < LANES // 2
    first = jnp.where(half, factor, 0.0).astype(bf16)
    second = jnp.where(half, 0.0, factor).astype(bf16)
    for tile in range(tiles):
        for pair in pairs:
            block = source[tile * TILE : (tile + 1) * TILE, pair * LANES : (pair + 1) * LANES]
            target[pair, tile, :TILE, :] = block * first
            target[pair, tile, TILE:, :] = block * second


def turn_tiles(target, source, column, pairs):
    low, high = pairs[0] * LANES, (pairs[-1] + 1) * LANES
    for tile in range(target.shape[0]):
        block = source[tile * TILE : (tile + 1) * TILE, column + low : column + high]
        target[tile, low:high, :] = jnp.transpose(block)


def place_documents(r, copies):
    wait_all(copies)
    q_tiles = r.qd.shape[0]
    for part in range(3):
        row = r.docs[part].astype(f32)[0:1, :]
        for tile in range(q_tiles):
            piece = row[:, tile * TILE : (tile + 1) * TILE]
            slot = part * q_tiles + tile
            r.bounds[0, slot] = jnp.min(piece).astype(jnp.int32)
            r.bounds[1, slot] = jnp.max(piece).astype(jnp.int32)
            if part == 0:
                r.qd[tile] = jnp.broadcast_to(piece, (8, TILE))
        if part > 0:
            for start in range(0, row.shape[1], LANES):
                block = jnp.broadcast_to(row[:, start : start + LANES], (LANES, LANES))
                place = (part - 1) * row.shape[1] + start
                r.kdc[place : place + LANES, :] = jnp.transpose(block)


def load_documents(r, move, queries, own, other):
    rows = pl.ds(r.docs.shape[2], r.docs.shape[1])
    return [
        move.start(source.at[rows], r.docs.at[part])
        for part, source in enumerate((queries, own, other))
    ]


def tile_place(r, core, causal, q_tile, k_tile):
    q_tiles = r.qd.shape[0]
    length = q_tiles * TILE
    owner = jnp.where(k_tile < q_tiles, core, 1 - core)
    k_start = owner * length + lax.rem(k_tile, q_tiles) * TILE
    ahead = core * length + q_tile * TILE - k_start
    ahead = jnp.where(causal == 1, ahead, 2 * length * TILE)
    q_low, q_high = r.bounds[0, q_tile], r.bounds[1, q_tile]
    k_low, k_high = r.bounds[0, q_tiles + k_tile], r.bounds[1, q_tiles + k_tile]
    active = (q_low <= k_high) & (k_low <= q_high) & (ahead > -TILE)
    return active, ahead


def fill_bias(r, q_tile, k_tile, ahead):
    keys = r.kdc[pl.ds(pl.multiple_of(k_tile * TILE, TILE), TILE), :]
    shift = lax.broadcasted_iota(jnp.int32, (TILE, LANES), 0) - lax.broadcasted_iota(
        jnp.int32, (TILE, LANES), 1
    )
    queries = r.qd[q_tile]
    for start in range(0, TILE, LANES):
        same = keys == queries[0:1, start : start + LANES]
        allowed = same & (shift - start <= ahead)
        r.bias[:, start : start + LANES] = jnp.where(allowed, 0.0, negative_big)


def attention_forward(r, core, causal):
    pairs, q_tiles = r.qm.shape[:2]
    k_tiles = r.vt.shape[0]

    def one_query_tile(q_tile, carry):
        r.top[...] = jnp.full(r.top.shape, negative_big, f32)
        r.total[...] = jnp.zeros(r.total.shape, f32)
        r.turned[...] = jnp.zeros(r.turned.shape, f32)

        def one_key_tile(k_tile, inner):
            active, ahead = tile_place(r, core, causal, q_tile, k_tile)

            @pl.when(active)
            def _():
                fill_bias(r, q_tile, k_tile, ahead)
                rows = pl.ds(pl.multiple_of(k_tile * TILE, TILE), TILE)

                def raw(pair):
                    keys = r.kv[rows, pair * LANES : (pair + 1) * LANES]
                    return dot_nt(keys, r.qm[pair, q_tile])

                raw_next = raw(0)
                for pair in range(pairs):
                    bias = r.bias[...]
                    scores = raw_next + jnp.concatenate([bias, bias], axis=1)
                    if pair + 1 < pairs:
                        raw_next = raw(pair + 1)
                    old_top = r.top[pair : pair + 1, :]
                    new_top = jnp.maximum(old_top, jnp.max(scores, axis=0, keepdims=True))
                    weights = jnp.exp(scores - new_top)
                    shrink = jnp.exp(old_top - new_top)
                    r.top[pair : pair + 1, :] = new_top
                    r.total[pair : pair + 1, :] = r.total[
                        pair : pair + 1, :
                    ] * shrink + jnp.sum(weights, axis=0, keepdims=True)
                    low = weights.astype(bf16)
                    for side in range(2):
                        span = slice(side * TILE, (side + 1) * TILE)
                        head = slice((2 * pair + side) * 64, (2 * pair + side + 1) * 64)
                        r.turned[head, :] = r.turned[head, :] * shrink[:, span] + dot(
                            r.vt[k_tile, head, :], low[:, span]
                        )

            return inner

        lax.fori_loop(0, k_tiles, one_key_tile, 0)
        for pair in range(pairs):
            total = r.total[pair : pair + 1, :]
            r.lse[q_tile, pair : pair + 1, :] = r.top[pair : pair + 1, :] + jnp.log(total)
            share = 1.0 / total
            for side in range(2):
                span = slice(side * TILE, (side + 1) * TILE)
                head = slice((2 * pair + side) * 64, (2 * pair + side + 1) * 64)
                r.turned[head, :] = r.turned[head, :] * share[:, span]
        rows = pl.ds(pl.multiple_of(q_tile * TILE, TILE), TILE)
        r.att[rows, :] = jnp.transpose(r.turned[...]).astype(bf16)
        return carry

    lax.fori_loop(0, q_tiles, one_query_tile, 0)


def row_products(r, grad_att, pairs):
    low, high = pairs[0] * LANES, (pairs[-1] + 1) * LANES
    for tile in range(r.qm.shape[1]):
        rows = slice(tile * TILE, (tile + 1) * TILE)
        product = jnp.transpose(
            grad_att[rows, low:high].astype(f32) * r.att[rows, low:high].astype(f32)
        )
        for pair in pairs:
            for side in range(2):
                head = (2 * pair + side) * 64 - low
                r.delta[tile, pair : pair + 1, side * TILE : (side + 1) * TILE] = jnp.sum(
                    product[head : head + 64, :], axis=0, keepdims=True
                )


def attention_backward(r, core, causal, pairs):
    q_tiles, k_tiles = r.qm.shape[1], r.kt.shape[0]
    width = r.kt.shape[1]
    low, high = pairs[0] * LANES, (pairs[-1] + 1) * LANES
    for start in (0, width):
        r.dkv[:, start + low : start + high] = jnp.zeros((r.dkv.shape[0], high - low), f32)

    def one_query_tile(q_tile, carry):
        r.turned[low:high, :] = jnp.zeros((high - low, TILE), f32)

        def one_key_tile(k_tile, inner):
            active, ahead = tile_place(r, core, causal, q_tile, k_tile)

            @pl.when(active)
            def _():
                fill_bias(r, q_tile, k_tile, ahead)
                rows = pl.ds(pl.multiple_of(k_tile * TILE, TILE), TILE)

                def raw(pair):
                    lanes = slice(pair * LANES, (pair + 1) * LANES)
                    lanes_v = slice(width + pair * LANES, width + (pair + 1) * LANES)
                    return (
                        dot_nt(r.kv[rows, lanes], r.qm[pair, q_tile]),
                        dot_nt(r.kv[rows, lanes_v], r.gm[pair, q_tile]),
                    )

                raw_next = raw(pairs[0])
                for pair in pairs:
                    bias = r.bias[...]
                    scores, grad_probs = raw_next
                    scores = scores + jnp.concatenate([bias, bias], axis=1)
                    if pair < pairs[-1]:
                        raw_next = raw(pair + 1)
                    probs = jnp.exp(scores - r.lse[q_tile, pair : pair + 1, :])
                    grad_scores = probs * (grad_probs - r.delta[q_tile, pair : pair + 1, :])
                    probs_low = probs.astype(bf16)
                    grad_low = grad_scores.astype(bf16)
                    lanes = slice(pair * LANES, (pair + 1) * LANES)
                    lanes_v = slice(width + pair * LANES, width + (pair + 1) * LANES)
                    r.dkv[rows, lanes] += dot(grad_low, r.qm[pair, q_tile])
                    r.dkv[rows, lanes_v] += dot(probs_low, r.gm[pair, q_tile])
                    for side in range(2):
                        span = slice(side * TILE, (side + 1) * TILE)
                        head = slice((2 * pair + side) * 64, (2 * pair + side + 1) * 64)
                        r.turned[head, :] += dot(r.kt[k_tile, head, :], grad_low[:, span])

            return inner

        lax.fori_loop(0, k_tiles, one_key_tile, 0)
        rows = pl.ds(pl.multiple_of(q_tile * TILE, TILE), TILE)
        r.dq[rows, low:high] = jnp.transpose(r.turned[low:high, :]) * (64**-0.5)
        return carry

    lax.fori_loop(0, q_tiles, one_query_tile, 0)


def feed_forward(r, low):
    r.sum[...] = jnp.zeros(r.sum.shape, f32)

    def one_chunk(chunk, carry):
        span = pl.ds(pl.multiple_of(chunk * CHUNK, CHUNK), CHUNK)
        upward = dot(low[...], r.w_in[:, span])
        gate = jax.nn.sigmoid(upward)
        active = (upward * gate).astype(bf16)
        r.act[:, span] = active
        r.slope[:, span] = (gate + upward * gate * (1.0 - gate)).astype(r.slope.dtype)
        r.sum[...] += dot(active, r.w_down[span, :])
        return carry

    lax.fori_loop(0, r.w_in.shape[1] // CHUNK, one_chunk, 0)


def feed_backward(r):
    r.sum[...] = jnp.zeros(r.sum.shape, f32)

    def one_chunk(chunk, carry):
        span = pl.ds(pl.multiple_of(chunk * CHUNK, CHUNK), CHUNK)
        grad_active = dot_nt(r.down_grad[...], r.w_down[span, :]).astype(bf16)
        grad_up = (grad_active.astype(f32) * r.slope[:, span].astype(f32)).astype(bf16)
        r.up_grad[:, span] = grad_up
        r.sum[...] += dot_nt(grad_up, r.w_in[:, span])
        return carry

    lax.fori_loop(0, r.w_in.shape[1] // CHUNK, one_chunk, 0)


def self_forward(r):
    length, width = r.unit1.shape
    decoder, core = r.meta[0], r.meta[1]
    move = Copies(r.sems)
    whole = pl.ds(0, length)
    documents = load_documents(r, move, r.x_own_h, r.x_own_h, r.x_other_h)
    early = [
        move.start(r.x_own_h.at[whole], r.x.at[whole]),
        move.start(r.x_other_h.at[whole], r.x.at[pl.ds(length, length)]),
        move.start(r.w_mixed_h, r.w_mixed),
    ]
    later = [
        move.start(r.w_out_h, r.w_out),
        move.start(r.w_in_h, r.w_in),
        move.start(r.w_down_h, r.w_down),
    ]
    place_documents(r, documents)
    wait_all(early)
    r.q[...] = dot(r.x[:length, :], r.w_mixed[:, :width]).astype(bf16)
    r.kv[...] = dot(r.x[...], r.w_mixed[:, width:]).astype(bf16)
    outs = [move.start(r.q, r.q_o), move.start(r.kv, r.kv_o)]
    pairs = range(width // LANES)
    spread_pairs(r.qm, r.q, 64**-0.5, pairs)
    turn_tiles(r.vt, r.kv, width, pairs)
    attention_forward(r, core, decoder)
    wait_all(later)
    outs += [move.start(r.att, r.att_o), move.start(r.lse, r.lse_o)]
    unit, inverse = standardize(r.x[:length, :].astype(f32) + dot(r.att[...], r.w_out[...]))
    r.unit1[...] = unit
    r.inv1[...] = jnp.broadcast_to(inverse, r.inv1.shape)
    r.first_low[...] = (unit * r.gains[0:1, :]).astype(bf16)
    outs += [
        move.start(r.unit1, r.unit1_o),
        move.start(r.inv1, r.inv1_o),
        move.start(r.first_low, r.first_low_o),
    ]

    @pl.when(decoder == 0)
    def _():
        feed_forward(r, r.first_low)
        late = [
            move.start(r.first_low, r.ffn_low_o),
            move.start(r.act, r.act_o),
            move.start(r.slope, r.slope_o),
        ]
        unit2, inverse2 = standardize(r.unit1[...] * r.gains[0:1, :] + r.sum[...])
        r.memory[:length, :] = (unit2 * r.gains[1:2, :]).astype(bf16)
        r.memory[length:, :] = r.docs[0]
        late += [move.start(r.memory, r.memory_o)]
        r.unit2[...] = unit2
        r.inv2[...] = jnp.broadcast_to(inverse2, r.inv2.shape)
        late += [move.start(r.unit2, r.unit2_o), move.start(r.inv2, r.inv2_o)]
        wait_all(late)

    wait_all(outs)


def cross_both_ways(r):
    length, width = r.unit1_h.shape
    core = r.meta[1]
    move = Copies(r.sems)
    whole = pl.ds(0, length)
    documents = load_documents(r, move, r.x_own_h, r.memory_own_h, r.memory_other_h)
    moves = [
        move.start(r.memory_own_h.at[whole], r.x.at[whole]),
        move.start(r.memory_other_h.at[whole], r.x.at[pl.ds(length, length)]),
        move.start(r.w_pair_h, r.w_pair),
        move.start(r.first_low_h, r.first_low),
        move.start(r.w_query_h, r.w_query),
    ]
    later = [
        move.start(r.unit1_h, r.unit1),
        move.start(r.w_cross_h, r.w_cross),
        move.start(r.w_in_h, r.w_in),
        move.start(r.w_down_h, r.w_down),
        move.start(r.cot_h.at[r.micro], r.cot),
    ]
    place_documents(r, documents)
    wait_all(moves)
    r.kv[...] = dot(r.x[...], r.w_pair[...]).astype(bf16)
    r.q[...] = dot(r.first_low[...], r.w_query[...]).astype(bf16)
    pairs = range(width // LANES)
    spread_pairs(r.qm, r.q, 64**-0.5, pairs)
    turn_tiles(r.vt, r.kv, width, pairs)
    turn_tiles(r.kt, r.kv, 0, pairs)
    attention_forward(r, core, 0)
    outs = [move.start(r.att, r.att_o)]
    wait_all(later)
    first = r.unit1[...] * r.gains[0:1, :]
    unit, inverse = standardize(first + dot(r.att[...], r.w_cross[...]))
    r.unit2[...] = unit
    r.inv2[...] = jnp.broadcast_to(inverse, r.inv2.shape)
    r.second_low[...] = (unit * r.cross_gain[...]).astype(bf16)
    outs += [move.start(r.second_low, r.ffn_low_o)]
    feed_forward(r, r.second_low)
    outs += [move.start(r.act, r.act_o)]
    unit3, inverse3 = standardize(r.unit2[...] * r.cross_gain[...] + r.sum[...])
    r.decoded[...] = (unit3 * r.gains[1:2, :]).astype(bf16)
    outs += [move.start(r.decoded, r.decoded_o)]
    grad_third, gain_late = standardize_back(
        r.cot[...].astype(f32), unit3, r.gains[1:2, :], inverse3
    )
    r.keep[...] = grad_third
    r.down_grad[...] = grad_third.astype(bf16)
    outs += [move.start(r.down_grad, r.down_grad_o)]
    feed_backward(r)
    outs += [move.start(r.up_grad, r.up_grad_o)]
    grad_sum, gain_cross = standardize_back(
        r.keep[...] + r.sum[...], r.unit2[...], r.cross_gain[...], r.inv2[:, 0:1]
    )
    r.gain_grads[...] = jnp.zeros(r.gain_grads.shape, f32)
    r.gain_grads[0:1, :] = gain_late
    r.gain_grads[1:2, :] = gain_cross
    r.keep[...] = grad_sum
    r.branch[...] = grad_sum.astype(bf16)
    outs += [move.start(r.gain_grads, r.gain_grads_o), move.start(r.branch, r.branch_o)]
    r.q[...] = dot_nt(r.branch[...], r.w_cross[...]).astype(bf16)
    spread_pairs(r.gm, r.q, 1.0, pairs)
    row_products(r, r.q, pairs)
    attention_backward(r, core, 0, pairs)
    r.dq_low[...] = r.dq[...].astype(bf16)
    r.keep[...] += dot_nt(r.dq_low[...], r.w_query[...])
    outs += [move.start(r.dq_low, r.dq_low_o), move.start(r.keep, r.grad_first_o)]
    r.dkv_low[...] = r.dkv[...].astype(bf16)
    outs += [move.start(r.dkv_low, r.dkv_o)]
    part = dot_nt(r.dkv_low[...], r.w_pair[...])
    r.part_other[...] = part[length:, :].astype(bf16)
    r.part_own[...] = part[:length, :]
    outs += [move.start(r.part_other, r.part_other_o), move.start(r.part_own, r.part_own_o)]
    wait_all(outs)


def feed_backward_alone(r):
    move = Copies(r.sems)
    early = [
        move.start(r.grad_memory_h, r.cot),
        move.start(r.unit2_h, r.unit2),
        move.start(r.inv2_h, r.inv2),
    ]
    later = [
        move.start(r.w_down_h, r.w_down),
        move.start(r.slope_h, r.slope),
        move.start(r.w_in_h, r.w_in),
    ]
    wait_all(early)
    grad_third, gain_late = standardize_back(
        r.cot[...].astype(f32), r.unit2[...], r.gains[1:2, :], r.inv2[:, 0:1]
    )
    r.gain_grads[...] = jnp.broadcast_to(gain_late, r.gain_grads.shape)
    r.keep[...] = grad_third
    r.down_grad[...] = grad_third.astype(bf16)
    outs = [move.start(r.down_grad, r.down_grad_o), move.start(r.gain_grads, r.gain_late_o)]
    wait_all(later)
    feed_backward(r)
    outs += [move.start(r.up_grad, r.up_grad_o)]
    r.keep[...] += r.sum[...]
    outs += [move.start(r.keep, r.grad_first_o)]
    wait_all(outs)


def self_backward(r, plan):
    r.micro, first, last = plan
    length, width = r.att_h.shape
    decoder, core = r.meta[0], r.meta[1]
    pairs = range(first, last)
    low, high = first * LANES, last * LANES
    move = Copies(r.sems)
    later = [
        move.start(r.q_h, r.q),
        move.start(r.kv_h, r.kv),
        move.start(r.att_h, r.att),
        move.start(r.lse_h, r.lse),
    ]
    if first == 0:
        early = [
            move.start(r.grad_first_h, r.keep),
            move.start(r.unit1_h, r.unit1),
            move.start(r.inv1_h, r.inv1),
            move.start(r.w_out_h, r.w_out),
        ]
    else:
        early = [move.start(r.grad_att_h, r.grad_att)]
    outs = []
    place_documents(r, load_documents(r, move, r.x_own_h, r.x_own_h, r.x_other_h))
    wait_all(early)
    if first == 0:
        grad_sum, gain_early = standardize_back(
            r.keep[...], r.unit1[...], r.gains[0:1, :], r.inv1[:, 0:1]
        )
        r.gain_grads[...] = jnp.broadcast_to(gain_early, r.gain_grads.shape)
        r.keep[...] = grad_sum
        r.branch[...] = grad_sum.astype(bf16)
        r.grad_att[...] = dot_nt(r.branch[...], r.w_out[...]).astype(bf16)
        outs += [move.start(r.gain_grads, r.gain_early_o), move.start(r.branch, r.branch_o)]
        if last < width // LANES:
            outs += [move.start(r.keep, r.grad_sum_o), move.start(r.grad_att, r.grad_att_o)]
    wait_all(later)
    if last == width // LANES:
        ends = [move.start(r.w_mixed_h, r.w_mixed)]
        if first > 0:
            ends += [
                move.start(r.grad_sum_h, r.keep),
                move.start(r.dq_h.at[:, pl.ds(0, low)], r.dq_low.at[:, pl.ds(0, low)]),
                move.start(r.dkv_h.at[:, pl.ds(0, low)], r.dkv_low.at[:, pl.ds(0, low)]),
                move.start(
                    r.dkv_h.at[:, pl.ds(width, low)], r.dkv_low.at[:, pl.ds(width, low)]
                ),
            ]
    spread_pairs(r.qm, r.q, 64**-0.5, pairs)
    turn_tiles(r.kt, r.kv, 0, pairs)
    spread_pairs(r.gm, r.grad_att, 1.0, pairs)
    row_products(r, r.grad_att, pairs)
    attention_backward(r, core, decoder, pairs)
    r.dq_low[:, low:high] = r.dq[:, low:high].astype(bf16)
    for start in (0, width):
        span = slice(start + low, start + high)
        r.dkv_low[:, span] = r.dkv[:, span].astype(bf16)
    if last == width // LANES:
        wait_all(ends)
        outs += [move.start(r.dq_low, r.dq_low_o), move.start(r.dkv_low, r.dkv_o)]
        r.keep[...] += dot_nt(r.dq_low[...], r.w_mixed[:, :width])
        part = dot_nt(r.dkv_low[...], r.w_mixed[:, width:])
        r.part_other[...] = part[length:, :].astype(bf16)
        r.keep[...] += part[:length, :]
        outs += [move.start(r.part_other, r.part_other_o), move.start(r.keep, r.part_own_o)]
    else:
        outs.append(move.start(r.dq_low.at[:, pl.ds(low, high - low)], r.dq_low_o.at[:, pl.ds(low, high - low)]))
        for start in (0, width):
            span = pl.ds(start + low, high - low)
            outs.append(move.start(r.dkv_low.at[:, span], r.dkv_o.at[:, span]))
    wait_all(outs)


def contract_blocks(r, plan):
    for core in range(2):

        @pl.when(r.meta[1] == core)
        def _(core=core):
            targets = [None] * 4
            for half in range(2):
                target = r.kept_o if half == core else r.sent_o
                targets[2 * half], targets[2 * half + 1] = target.at[0], target.at[1]
            order = (0, 1, 2, 3) if core else (2, 3, 0, 1)
            contract_in_order(r, plan(r), order, targets, Copies(r.sems))


def contract_in_order(r, blocks, order, targets, move):
    loads = dict()
    for slot in order:
        for buffer, sources, at in blocks[slot][1:]:
            if (id(buffer), at) not in loads:
                span = pl.ds(at * CHUNK, CHUNK)
                row = 0
                copies = []
                for source in sources:
                    rows = pl.ds(row, source.shape[0])
                    copies.append(move.start(source.at[:, span], buffer.at[rows, span]))
                    row += source.shape[0]
                loads[id(buffer), at] = copies
    outs = []
    held = dict()
    for slot in order:
        turn, (left, _, left_at), (right, _, right_at) = blocks[slot]
        wait_all(loads.pop((id(left), left_at), ()))
        wait_all(loads.pop((id(right), right_at), ()))
        if held.get(id(turn)) != left_at:
            for row in range(0, left.shape[0], CHUNK):
                block = left[row : row + CHUNK, left_at * CHUNK : (left_at + 1) * CHUNK]
                turn[:, row : row + CHUNK] = jnp.transpose(block)
            held[id(turn)] = left_at
        block = right[:, right_at * CHUNK : (right_at + 1) * CHUNK]
        r.blocks[slot] = dot(turn[:, : right.shape[0]], block).astype(bf16)
        outs.append(move.start(r.blocks.at[slot], targets[slot]))
    wait_all(outs)


def spread_pieces(r, targets):
    z = r.meta[3]
    group, height = r.own_h.shape[:2]
    rows = r.own_h.shape[2] // group
    for core in range(2):
        for x in range(2):

            @pl.when((r.meta[1] == core) & (r.meta[2] == x))
            def _(core=core, x=x):
                move = Copies(r.sems)
                parts = [
                    (r.own_h, core, x),
                    (r.own_x_h, core, 1 - x),
                    (r.other_h, 1 - core, x),
                    (r.other_x_h, 1 - core, 1 - x),
                ]
                loads = [
                    move.start(source, r.pieces.at[place])
                    for place, (source, _, _) in enumerate(parts)
                ]
                outs = []
                slot = 0
                gains = None
                for place, (_, half, side) in enumerate(parts):
                    loads[place].wait()
                    for step in range(group):
                        row = pl.multiple_of(lax.rem(z + (group - step), group) * rows, rows)
                        start = 0
                        for target in targets(r, 2 * half + side, row, rows):
                            r.wide[slot] = r.pieces[place, step, start : start + rows].astype(f32)
                            outs.append(move.start(r.wide.at[slot], target))
                            slot += 1
                            start += rows
                        if start < height:
                            extra = r.pieces[place, step, start:height].astype(f32)
                            gains = extra if gains is None else gains + extra
                if gains is not None:
                    r.gain_grads[...] = gains
                    outs.append(move.start(r.gain_grads, r.gains_o))
                wait_all(outs)


def launch(kernel, plan, side, scalars, small, large, outs, scratch, copies, work, previous=None, after=()):
    names = list(scalars) + list(small) + list(large)
    arrays = list(scalars.values()) + list(small.values()) + list(large.values())
    specs = (
        [pl.BlockSpec(memory_space=pltpu.SMEM)] * len(scalars)
        + [pl.BlockSpec(memory_space=pltpu.VMEM)] * len(small)
        + [pl.BlockSpec(memory_space=pl.ANY)] * len(large)
    )
    aliases = dict()
    for position, name in enumerate(outs):
        if previous and name in previous:
            aliases[len(arrays)] = position
            names.append("previous_" + name)
            arrays.append(previous[name])
            specs.append(pl.BlockSpec(memory_space=pl.ANY))
    for array in after:
        names.append("")
        arrays.append(array)
        specs.append(pl.BlockSpec(memory_space=pl.ANY))
    names += list(outs) + list(scratch) + ["sems"]

    def body(*refs):
        r = types.SimpleNamespace(**dict(zip(names, refs)))

        def run():
            if isinstance(plan, int):
                r.micro = plan
                kernel(r)
            else:
                kernel(r, plan)

        if side is None:
            run()
        else:
            pl.when(r.meta[0] == side)(run)

    results = pl.pallas_call(
        body,
        out_shape=[jax.ShapeDtypeStruct(*shape) for shape in outs.values()],
        in_specs=specs,
        out_specs=[pl.BlockSpec(memory_space=pl.ANY)] * len(outs),
        scratch_shapes=[
            pltpu.SMEM(*shape) if shape[1] == jnp.int32 else pltpu.VMEM(*shape)
            for shape in scratch.values()
        ]
        + [pltpu.SemaphoreType.DMA((copies,))],
        input_output_aliases=aliases,
        compiler_params=pltpu.CompilerParams(vmem_limit_bytes=58 * 1024 * 1024),
        cost_estimate=pl.CostEstimate(
            flops=work * 10**9, bytes_accessed=1 << 20, transcendentals=0
        ),
    )(*arrays)
    return types.SimpleNamespace(**dict(zip(outs, results)))


def attention_scratch(length, width):
    pairs, q_tiles, k_tiles = width // LANES, length // TILE, 2 * length // TILE
    return dict(
        q=((length, width), bf16),
        kv=((2 * length, 2 * width), bf16),
        qm=((pairs, q_tiles, 2 * TILE, LANES), bf16),
        kdc=((2 * length, LANES), f32),
        docs=((3, 16, width), bf16),
        qd=((length // TILE, 8, TILE), f32),
        bounds=((2, 3 * length // TILE), jnp.int32),
        bias=((TILE, TILE), f32),
        lse=((q_tiles, 8, 2 * TILE), f32),
        att=((length, width), bf16),
        turned=((width, TILE), f32),
    )


def forward_scratch(length, width):
    k_tiles = 2 * length // TILE
    return dict(
        vt=((k_tiles, width, TILE), bf16),
        top=((8, 2 * TILE), f32),
        total=((8, 2 * TILE), f32),
    )


def backward_scratch(length, width):
    pairs, q_tiles, k_tiles = width // LANES, length // TILE, 2 * length // TILE
    return dict(
        kt=((k_tiles, width, TILE), bf16),
        gm=((pairs, q_tiles, 2 * TILE, LANES), bf16),
        delta=((q_tiles, 8, 2 * TILE), f32),
        dkv=((2 * length, 2 * width), f32),
        dq=((length, width), f32),
        dkv_low=((2 * length, 2 * width), bf16),
        part_other=((length, width), bf16),
        dq_low=((length, width), bf16),
    )


def for_sending(shard):

    def short(part):
        return part.astype(jnp.bfloat16) if part.dtype == jnp.float32 else part

    return jax.tree.map(short, shard)


def from_behind(block, axis, distance):
    devices = range(lax.axis_size(axis))
    route = [(i - distance, i) for i in devices if i - distance in devices]
    return lax.ppermute(block, axis, route)


def from_root(shard, axis, root):
    mine = lax.axis_index(axis) == root
    return lax.psum(jnp.where(mine, shard, jnp.zeros_like(shard)), axis)


def matmul(left_side, right_side):
    return jnp.einsum("rsd,de->rse", left_side, right_side, preferred_element_type=jnp.float32)


def matmul_back(left_side, right_side):
    return jnp.einsum("rse,de->rsd", left_side, right_side, preferred_element_type=jnp.float32)


def contract(left_side, right_side):
    return jnp.einsum("rsd,rse->de", left_side, right_side, preferred_element_type=jnp.float32)


def normalize(values, gain_row):
    center = values - jnp.mean(values, axis=-1, keepdims=True)
    inverse = lax.rsqrt(jnp.mean(center * center, axis=-1, keepdims=True) + epsilon)
    standard = center * inverse
    return (standard * gain_row, standard, inverse)


def normalize_back(grad_out, standard, gain_row, inverse):
    scaled = grad_out * gain_row
    grad_in = inverse * (
        scaled
        - jnp.mean(scaled, axis=-1, keepdims=True)
        - standard * jnp.mean(scaled * standard, axis=-1, keepdims=True)
    )
    return (grad_in, jnp.sum(grad_out * standard, axis=(0, 1)))


def allowed_mask(query_docs, key_docs, query_place, key_place, causal):
    same_doc = query_docs[:, :, None] == key_docs[:, None, :]
    earlier = query_place[:, None] >= key_place[None, :]
    return (same_doc & (earlier | jnp.logical_not(causal)))[:, None]


def attend(queries, keys_local, values_local, query_docs, key_docs, causal, is_cross):
    rows_here, shard_len, model_width = queries.shape
    head_dim = model_width // HEADS
    score_scale = head_dim ** (-0.5)
    query_place = lax.axis_index("seq") * shard_len + jnp.arange(shard_len)
    query_heads = queries.reshape(rows_here, shard_len, HEADS, head_dim)

    def absorb(state_tuple, pieces):
        running_top, running_total, running_sum = state_tuple
        key_piece, value_piece, doc_piece = pieces
        piece_len = key_piece.shape[1]
        raw_scores = jnp.einsum(
            "rqhd,rkhd->rhqk",
            query_heads,
            key_piece.reshape(rows_here, piece_len, HEADS, head_dim),
            preferred_element_type=jnp.float32,
        )
        allowed = allowed_mask(query_docs, doc_piece, query_place, jnp.arange(piece_len), causal)
        scores = jnp.where(allowed, raw_scores * score_scale, negative_big)
        new_top = jnp.maximum(running_top, jnp.max(scores, axis=-1))
        weights = jnp.where(allowed, jnp.exp(scores - new_top[..., None]), 0.0)
        new_total = jnp.sum(weights, axis=-1)
        product = jnp.einsum(
            "rhqk,rkhd->rhqd",
            weights.astype(jnp.bfloat16),
            value_piece.reshape(rows_here, piece_len, HEADS, head_dim),
            preferred_element_type=jnp.float32,
        )
        return (new_top, new_total, product)

    init_state = (
        jnp.full((rows_here, HEADS, shard_len), negative_big, jnp.float32),
        jnp.zeros((rows_here, HEADS, shard_len), jnp.float32),
        jnp.zeros((rows_here, HEADS, shard_len, head_dim), jnp.float32),
    )
    if is_cross:
        final_top, final_total, final_sum = absorb(
            init_state,
            (
                lax.all_gather(keys_local, "seq", axis=1, tiled=True),
                lax.all_gather(values_local, "seq", axis=1, tiled=True),
                lax.all_gather(for_sending(key_docs), "seq", axis=1, tiled=True),
            ),
        )
    else:
        final_top, final_total, final_sum = absorb(
            init_state,
            (
                lax.all_gather(keys_local, "seq", axis=1, tiled=True),
                lax.all_gather(values_local, "seq", axis=1, tiled=True),
                lax.all_gather(key_docs, "seq", axis=1, tiled=True),
            ),
        )
    attended = (
        (final_sum / final_total[..., None])
        .transpose(0, 2, 1, 3)
        .reshape(rows_here, shard_len, model_width)
    )
    return (attended, final_top + jnp.log(final_total))


def attend_back(
    queries,
    keys_local,
    values_local,
    query_docs,
    key_docs,
    causal,
    log_total,
    grad_attended,
    is_cross,
):
    rows_here, shard_len, model_width = queries.shape
    head_dim = model_width // HEADS
    score_scale = head_dim ** (-0.5)
    query_place = lax.axis_index("seq") * shard_len + jnp.arange(shard_len)
    if is_cross:
        keys_full, values_full, docs_full = (
            lax.all_gather(keys_local, "seq", axis=1, tiled=True),
            lax.all_gather(values_local, "seq", axis=1, tiled=True),
            lax.all_gather(for_sending(key_docs), "seq", axis=1, tiled=True).astype(key_docs.dtype),
        )
    else:
        keys_full, values_full, docs_full = (
            lax.all_gather(keys_local, "seq", axis=1, tiled=True),
            lax.all_gather(values_local, "seq", axis=1, tiled=True),
            lax.all_gather(key_docs, "seq", axis=1, tiled=True),
        )
    full_len = keys_full.shape[1]
    query_heads = queries.reshape(rows_here, shard_len, HEADS, head_dim)
    key_heads = keys_full.reshape(rows_here, full_len, HEADS, head_dim)
    value_heads = values_full.reshape(rows_here, full_len, HEADS, head_dim)
    grad_heads = grad_attended.reshape(rows_here, shard_len, HEADS, head_dim)
    raw_scores = jnp.einsum(
        "rqhd,rkhd->rhqk", query_heads, key_heads, preferred_element_type=jnp.float32
    )
    allowed = allowed_mask(query_docs, docs_full, query_place, jnp.arange(full_len), causal)
    shifted = jnp.where(allowed, raw_scores * score_scale - log_total[..., None], negative_big)
    probs = jnp.where(allowed, jnp.exp(shifted), 0.0)
    grad_probs = jnp.einsum(
        "rqhd,rkhd->rhqk", grad_heads, value_heads, preferred_element_type=jnp.float32
    )
    delta = jnp.sum(probs * grad_probs, axis=-1)
    grad_scores = (probs * (grad_probs - delta[..., None]) * score_scale).astype(jnp.bfloat16)
    grad_queries = jnp.einsum(
        "rhqk,rkhd->rqhd", grad_scores, key_heads, preferred_element_type=jnp.float32
    ).reshape(rows_here, shard_len, model_width)
    probs_low = probs.astype(jnp.bfloat16)

    def key_terms(span):
        grad_keys = jnp.einsum(
            "rhqk,rqhd->krhd", grad_scores, query_heads, preferred_element_type=jnp.float32
        )
        grad_values = jnp.einsum(
            "rhqk,rqhd->krhd", probs_low, grad_heads, preferred_element_type=jnp.float32
        )
        return jnp.concatenate(
            [
                grad_keys.reshape(span, rows_here, model_width),
                grad_values.reshape(span, rows_here, model_width),
            ],
            axis=-1,
        )

    if is_cross:
        pair_terms = lax.psum_scatter(
            key_terms(shard_len * lax.axis_size("seq")).astype(jnp.bfloat16),
            "seq",
            scatter_dimension=0,
            tiled=True,
        ).astype(jnp.float32)
    else:
        pair_terms = lax.psum_scatter(
            key_terms(shard_len * lax.axis_size("seq")).astype(jnp.bfloat16),
            "seq",
            scatter_dimension=0,
            tiled=True,
        ).astype(jnp.float32)
    return (grad_queries, pair_terms.transpose(1, 0, 2))


def layer_forward(hidden_in, doc_own, memory, memory_docs, weights, is_decoder):
    (
        qkv_weight,
        out_weight,
        in_weight,
        down_weight,
        gains_pair,
        query_weight,
        pair_weight,
        cross_weight,
        cross_gains,
    ) = weights
    model_width = hidden_in.shape[-1]
    mixed = matmul(hidden_in, qkv_weight).astype(jnp.bfloat16)
    attended, self_lse = attend(
        mixed[..., :model_width],
        mixed[..., model_width : 2 * model_width],
        mixed[..., 2 * model_width :],
        doc_own,
        doc_own,
        is_decoder,
        False,
    )
    attended = attended.astype(jnp.bfloat16)
    first, first_unit, first_inv = normalize(
        hidden_in.astype(jnp.float32) + matmul(attended, out_weight), gains_pair[0]
    )
    first_low = first.astype(jnp.bfloat16)
    cross_queries = matmul(first_low, query_weight).astype(jnp.bfloat16)
    pair = matmul(memory, pair_weight).astype(jnp.bfloat16)
    cross_att, cross_lse = attend(
        cross_queries,
        pair[..., :model_width],
        pair[..., model_width:],
        doc_own,
        memory_docs,
        False,
        True,
    )
    cross_att = cross_att.astype(jnp.bfloat16)
    second_cross, second_unit, second_inv = normalize(
        first + matmul(cross_att, cross_weight), cross_gains
    )
    second = jnp.where(is_decoder, second_cross, first)
    second_low = second.astype(jnp.bfloat16)
    upward = matmul(second_low, in_weight)
    active = jax.nn.silu(upward).astype(jnp.bfloat16)
    result, third_unit, third_inv = normalize(second + matmul(active, down_weight), gains_pair[1])
    saved = {
        "mixed": mixed,
        "attended": attended,
        "self_lse": self_lse,
        "first_unit": first_unit,
        "first_inv": first_inv,
        "first_low": first_low,
        "cross_queries": cross_queries,
        "pair": pair,
        "cross_att": cross_att,
        "cross_lse": cross_lse,
        "second_unit": second_unit,
        "second_inv": second_inv,
        "second_low": second_low,
        "upward": upward,
        "active": active,
        "third_unit": third_unit,
        "third_inv": third_inv,
    }
    return (result, saved)


def layer_backward(
    grad_result, saved, hidden_in, doc_own, memory, memory_docs, weights, is_decoder
):
    (
        qkv_weight,
        out_weight,
        in_weight,
        down_weight,
        gains_pair,
        query_weight,
        pair_weight,
        cross_weight,
        cross_gains,
    ) = weights
    model_width = hidden_in.shape[-1]
    grad_third, grad_gain_late = normalize_back(
        grad_result, saved["third_unit"], gains_pair[1], saved["third_inv"]
    )
    down_grad = grad_third.astype(jnp.bfloat16)
    grad_down_w = contract(saved["active"], down_grad)
    grad_active = matmul_back(down_grad, down_weight).astype(jnp.bfloat16)
    sigmoid_up = jax.nn.sigmoid(saved["upward"])
    grad_upward = (
        grad_active.astype(jnp.float32)
        * (sigmoid_up + saved["upward"] * sigmoid_up * (1.0 - sigmoid_up))
    ).astype(jnp.bfloat16)
    grad_in_w = contract(saved["second_low"], grad_upward)
    grad_second = grad_third + matmul_back(grad_upward, in_weight)
    grad_cross_sum, grad_cross_gain = normalize_back(
        grad_second, saved["second_unit"], cross_gains, saved["second_inv"]
    )
    decoder_flag = is_decoder.astype(jnp.float32)
    grad_cross_sum = grad_cross_sum * decoder_flag
    grad_cross_gain = grad_cross_gain * decoder_flag
    cross_branch = grad_cross_sum.astype(jnp.bfloat16)
    grad_cross_w = contract(saved["cross_att"], cross_branch)
    grad_cross_att = matmul_back(cross_branch, cross_weight).astype(jnp.bfloat16)
    pair = saved["pair"]
    grad_cross_q, grad_pair = attend_back(
        saved["cross_queries"],
        pair[..., :model_width],
        pair[..., model_width:],
        doc_own,
        memory_docs,
        False,
        saved["cross_lse"],
        grad_cross_att,
        True,
    )
    grad_cross_q = grad_cross_q.astype(jnp.bfloat16)
    grad_pair = grad_pair.astype(jnp.bfloat16)
    grad_query_w = contract(saved["first_low"], grad_cross_q)
    grad_pair_w = contract(memory, grad_pair)
    grad_memory = matmul_back(grad_pair, pair_weight)
    grad_first = jnp.where(
        is_decoder, grad_cross_sum + matmul_back(grad_cross_q, query_weight), grad_second
    )
    grad_first_sum, grad_gain_early = normalize_back(
        grad_first, saved["first_unit"], gains_pair[0], saved["first_inv"]
    )
    self_branch = grad_first_sum.astype(jnp.bfloat16)
    grad_out_w = contract(saved["attended"], self_branch)
    grad_attended = matmul_back(self_branch, out_weight).astype(jnp.bfloat16)
    mixed = saved["mixed"]
    grad_queries, grad_pair_self = attend_back(
        mixed[..., :model_width],
        mixed[..., model_width : 2 * model_width],
        mixed[..., 2 * model_width :],
        doc_own,
        doc_own,
        is_decoder,
        saved["self_lse"],
        grad_attended,
        False,
    )
    grad_mixed = jnp.concatenate([grad_queries, grad_pair_self], axis=-1).astype(jnp.bfloat16)
    grad_qkv_w = contract(hidden_in, grad_mixed)
    grad_hidden = grad_first_sum + matmul_back(grad_mixed, qkv_weight)
    layer_grads = (
        grad_qkv_w,
        grad_out_w,
        grad_in_w,
        grad_down_w,
        jnp.stack([grad_gain_early, grad_gain_late]),
        grad_query_w,
        grad_pair_w,
        grad_cross_w,
        grad_cross_gain,
    )
    return (grad_hidden, grad_memory, layer_grads)


def any_rows(
    layer_input,
    segment_ids,
    attn_qkv,
    attn_out,
    ffn_in,
    ffn_out,
    norm_gain,
    cross_query,
    cross_pair,
    cross_out,
    cross_gain,
    out_cotangent,
):
    micro_count = layer_input.shape[1]
    section_index = lax.axis_index("section")
    is_decoder = section_index == 1
    weights = (
        attn_qkv[0],
        attn_out[0],
        ffn_in[0],
        ffn_out[0],
        norm_gain[0],
        cross_query,
        cross_pair,
        cross_out,
        cross_gain,
    )
    inputs_all = layer_input[0]
    docs_all = segment_ids[0]
    slot_ids = jnp.arange(micro_count)
    received = (jnp.zeros_like(inputs_all[0]), jnp.zeros_like(docs_all[0]))
    results = jnp.zeros_like(inputs_all)
    memories = []
    memory_doc_list = []
    for step_index in range(micro_count + 1):
        batch_index = step_index - section_index
        is_valid = (batch_index >= 0) & (batch_index < micro_count)
        chosen = jnp.clip(batch_index, 0, micro_count - 1)
        hidden_in = lax.dynamic_index_in_dim(inputs_all, chosen, 0, keepdims=False)
        doc_own = lax.dynamic_index_in_dim(docs_all, chosen, 0, keepdims=False)
        memory = received[0]
        memory_docs = jnp.where(is_valid & is_decoder, received[1], doc_own)
        memories.append(memory)
        memory_doc_list.append(memory_docs)
        result, saved = layer_forward(hidden_in, doc_own, memory, memory_docs, weights, is_decoder)
        low_result = result.astype(jnp.bfloat16)
        writing = (slot_ids == chosen) & is_valid
        results = jnp.where(writing[:, None, None, None], low_result[None], results)
        if step_index < micro_count:
            received = from_behind((low_result, doc_own), "section", 1)
    memory_stack = jnp.stack(memories)
    memory_doc_stack = jnp.stack(memory_doc_list)
    totals = tuple((jnp.zeros(weight.shape, jnp.float32) for weight in weights))
    input_grads = jnp.zeros(inputs_all.shape, jnp.float32)
    returned = jnp.zeros(inputs_all.shape[1:], jnp.float32)
    for step_index in range(micro_count + 1):
        batch_index = micro_count - step_index - section_index
        is_valid = (batch_index >= 0) & (batch_index < micro_count)
        chosen = jnp.clip(batch_index, 0, micro_count - 1)
        forward_step = jnp.clip(batch_index + section_index, 0, micro_count)
        hidden_in = lax.dynamic_index_in_dim(inputs_all, chosen, 0, keepdims=False)
        doc_own = lax.dynamic_index_in_dim(docs_all, chosen, 0, keepdims=False)
        memory = lax.dynamic_index_in_dim(memory_stack, forward_step, 0, keepdims=False)
        memory_docs = lax.dynamic_index_in_dim(memory_doc_stack, forward_step, 0, keepdims=False)
        discarded, saved = layer_forward(
            hidden_in, doc_own, memory, memory_docs, weights, is_decoder
        )
        cotangent = jnp.where(
            is_decoder,
            lax.dynamic_index_in_dim(out_cotangent, chosen, 0, keepdims=False).astype(jnp.float32),
            returned,
        )
        grad_hidden, grad_memory, layer_grads = layer_backward(
            cotangent, saved, hidden_in, doc_own, memory, memory_docs, weights, is_decoder
        )
        valid_flag = is_valid.astype(jnp.float32)
        totals = tuple(
            (running + valid_flag * fresh for running, fresh in zip(totals, layer_grads))
        )
        writing = (slot_ids == chosen) & is_valid
        input_grads = jnp.where(writing[:, None, None, None], grad_hidden[None], input_grads)
        if step_index < micro_count:
            returned = from_behind(grad_memory.astype(jnp.bfloat16), "section", -1).astype(
                grad_memory.dtype
            )
    group_sums = lax.psum(
        (
            totals[0],
            totals[1],
            totals[2],
            totals[3],
            totals[4],
            totals[5],
            totals[6],
            totals[7],
            totals[8],
        ),
        ("seq", "dp"),
    )
    section_sums = group_sums[:5]
    cross_sums = (
        from_root(group_sums[5].astype(jnp.bfloat16), "section", 1).astype(jnp.float32),
        from_root(group_sums[6].astype(jnp.bfloat16), "section", 1).astype(jnp.float32),
        from_root(group_sums[7].astype(jnp.bfloat16), "section", 1).astype(jnp.float32),
        from_root(group_sums[8].astype(jnp.bfloat16), "section", 1).astype(jnp.float32),
    )
    return (
        results[None],
        input_grads[None],
        section_sums[0][None],
        section_sums[1][None],
        section_sums[2][None],
        section_sums[3][None],
        section_sums[4][None],
        cross_sums[0],
        cross_sums[1],
        cross_sums[2],
        cross_sums[3],
    )


def split_rows(
    layer_input,
    segment_ids,
    attn_qkv,
    attn_out,
    ffn_in,
    ffn_out,
    norm_gain,
    cross_query,
    cross_pair,
    cross_out,
    cross_gain,
    out_cotangent,
):
    micros = layer_input.shape[1]
    length, width = layer_input.shape[3:]
    hidden = ffn_in.shape[-1]
    q_tiles = length // TILE
    group = lax.axis_size("dp") // 2
    axes = ("section", "seq", "dp")
    decoder = lax.axis_index("section") == 1
    flag = decoder.astype(jnp.int32)
    x = lax.axis_index("seq")
    core = lax.rem(lax.axis_index("dp"), 2)
    z = lax.axis_index("dp") // 2
    places = [(t, i, k, c) for t in range(2) for i in range(2) for k in range(group) for c in range(2)]

    def number(t, i, k, c):
        return ((t * 2 + i) * group + k) * 2 + c

    def send(values, target, section=None):
        route = [
            (number(*place), number(*target(*place)))
            for place in places
            if section in (None, place[0]) and target(*place)
        ]
        return lax.ppermute(values, axes, route)

    def to_core(t, i, k, c):
        return (t, i, k, 1 - c)

    def to_x(t, i, k, c):
        return (t, 1 - i, k, c)

    def to_row(t, i, k, c):
        return (t, c, k, i)

    def to_decoder(t, i, k, c):
        return (1, i, k, c) if t == 0 else None

    def to_encoder(t, i, k, c):
        return (0, i, k, c) if t == 1 else None

    def fence(values, *before):
        return lax.optimization_barrier((values,) + before)[0]

    def exchange(values):
        return send(values, to_core)

    low = ((length, width), bf16)
    wide = ((length, width), f32)
    marked = ((length + 16, width), bf16)
    both = ((2 * length, width), bf16)
    keys_all = ((2 * length, 2 * width), bf16)
    mixing = ((width, 3 * width), bf16)
    inner = ((length, hidden), bf16)
    lse = ((q_tiles, 8, 2 * TILE), f32)
    stat = ((length, LANES), f32)
    square = ((width, width), bf16)
    rising = ((width, hidden), bf16)
    falling = ((hidden, width), bf16)
    gain_rows = ((8, width), f32)

    meta = jnp.stack([flag, core, x, z]).astype(jnp.int32)
    numbers = segment_ids[0, :, 0].astype(bf16)
    padding = jnp.zeros((15, width), bf16)
    with_numbers = [
        jnp.concatenate([layer_input[0, micro, 0], numbers[micro][None], padding])
        for micro in range(micros)
    ]
    own = [send(with_numbers[0], to_row)]
    for micro in range(1, micros):
        own.append(send(fence(with_numbers[micro], own[-1]), to_row))
    other = [exchange(part) for part in own]

    plain = dict(meta=meta)
    small = dict(gains=norm_gain[0])
    forward, memories, memories_other = [], [], []
    for micro in range(micros):
        call = launch(
            self_forward,
            micro,
            None,
            plain,
            small,
            dict(
                x_own_h=own[micro],
                x_other_h=other[micro],
                w_mixed_h=attn_qkv[0],
                w_out_h=attn_out[0],
                w_in_h=ffn_in[0],
                w_down_h=ffn_out[0],
            ),
            dict(
                q_o=low,
                kv_o=keys_all,
                att_o=low,
                lse_o=lse,
                unit1_o=wide,
                inv1_o=stat,
                first_low_o=low,
                memory_o=marked,
                ffn_low_o=low,
                act_o=inner,
                slope_o=inner,
                unit2_o=wide,
                inv2_o=stat,
            ),
            dict(
                **attention_scratch(length, width),
                **forward_scratch(length, width),
                x=both,
                w_mixed=mixing,
                w_out=square,
                w_in=rising,
                w_down=falling,
                unit1=wide,
                inv1=stat,
                first_low=low,
                memory=marked,
                act=inner,
                slope=inner,
                unit2=wide,
                inv2=stat,
                sum=wide,
            ),
            28,
            26,
            after=(forward[0].lse_o,) if micro else (),
        )
        forward.append(call)
        memories.append(send(call.memory_o, to_decoder))

    for micro in range(micros):
        memories_other.append(exchange(fence(memories[micro], forward[-1].lse_o)))
    cotangent = send(fence(out_cotangent[:, 0], forward[0].lse_o), to_row)

    cross, grads_memory, made = [], [], []
    after = (forward[-1].lse_o,)
    for micro in range(micros):
        done = forward[micro]
        call = launch(
            cross_both_ways,
            micro,
            1,
            plain,
            dict(**small, cross_gain=cross_gain[None]),
            dict(
                x_own_h=own[micro],
                memory_own_h=memories[micro],
                memory_other_h=memories_other[micro],
                w_pair_h=cross_pair,
                first_low_h=done.first_low_o,
                unit1_h=done.unit1_o,
                w_query_h=cross_query,
                w_cross_h=cross_out,
                w_in_h=ffn_in[0],
                w_down_h=ffn_out[0],
                cot_h=cotangent,
            ),
            dict(
                att_o=low,
                ffn_low_o=low,
                act_o=inner,
                decoded_o=low,
                down_grad_o=low,
                up_grad_o=inner,
                gain_grads_o=gain_rows,
                branch_o=low,
                dq_low_o=low,
                dkv_o=keys_all,
                part_own_o=wide,
                part_other_o=low,
                grad_first_o=wide,
            ),
            dict(
                **attention_scratch(length, width),
                **forward_scratch(length, width),
                **backward_scratch(length, width),
                x=both,
                w_pair=((width, 2 * width), bf16),
                first_low=low,
                unit1=wide,
                w_query=square,
                w_cross=square,
                w_in=rising,
                w_down=falling,
                cot=low,
                unit2=wide,
                inv2=stat,
                second_low=low,
                act=inner,
                slope=inner,
                sum=wide,
                decoded=low,
                keep=wide,
                down_grad=low,
                up_grad=inner,
                gain_grads=gain_rows,
                branch=low,
                part_own=wide,
            ),
            36,
            44,
            dict(act_o=done.act_o, ffn_low_o=done.ffn_low_o),
            after,
        )
        cross.append(call)
        away = call.part_other_o
        if micro:
            away = fence(away, grads_memory[-1])
        total = call.part_own_o + exchange(away).astype(f32)
        made.append(total.astype(bf16))
        after = (made[micro],)
        grads_memory.append(send(made[micro], to_encoder))

    def backward_feed(micro, after):
        done, late = forward[micro], cross[micro]
        return launch(
            feed_backward_alone,
            micro,
            0,
            plain,
            dict(gains=norm_gain[0]),
            dict(
                grad_memory_h=grads_memory[micro],
                unit2_h=done.unit2_o,
                inv2_h=done.inv2_o,
                slope_h=done.slope_o,
                w_in_h=ffn_in[0],
                w_down_h=ffn_out[0],
            ),
            dict(gain_late_o=gain_rows, down_grad_o=low, up_grad_o=inner, grad_first_o=wide),
            dict(
                cot=low,
                unit2=wide,
                inv2=stat,
                slope=inner,
                w_in=rising,
                w_down=falling,
                gain_grads=gain_rows,
                keep=wide,
                down_grad=low,
                up_grad=inner,
                sum=wide,
            ),
            12,
            10,
            dict(
                down_grad_o=late.down_grad_o, up_grad_o=late.up_grad_o, grad_first_o=late.grad_first_o
            ),
            after,
        )

    def backward_self(micro, side, grad_first, previous=None, after=(), halfway=None):
        done = forward[micro]
        heads = width // LANES
        given = dict(
            x_own_h=own[micro],
            x_other_h=other[micro],
            q_h=done.q_o,
            kv_h=done.kv_o,
            att_h=done.att_o,
            lse_h=done.lse_o,
        )
        ahead = dict(
            grad_first_h=grad_first,
            unit1_h=done.unit1_o,
            inv1_h=done.inv1_o,
            w_out_h=attn_out[0],
        )
        makes = dict(dq_low_o=low, dkv_o=keys_all)
        makes_first = dict(gain_early_o=gain_rows, branch_o=low)
        makes_last = dict(part_own_o=wide, part_other_o=low)
        scratch = dict(
            **attention_scratch(length, width),
            **backward_scratch(length, width),
            w_out=square,
            w_mixed=mixing,
            unit1=wide,
            inv1=stat,
            keep=wide,
            branch=low,
            grad_att=low,
            gain_grads=gain_rows,
        )

        def part(first, last, large, outs, work, previous, after):
            return launch(
                self_backward,
                (micro, first, last),
                side,
                plain,
                small,
                dict(**given, **large),
                dict(**makes, **outs),
                scratch,
                28,
                work,
                previous,
                after,
            )

        if halfway is None:
            large = dict(**ahead, w_mixed_h=attn_qkv[0])
            outs = dict(**makes_first, **makes_last)
            return part(0, heads, large, outs, 22, previous, after)
        outs = dict(**makes_first, grad_sum_o=wide, grad_att_o=low)
        one = part(0, heads // 2, ahead, outs, 12, None, after)
        large = dict(
            w_mixed_h=attn_qkv[0],
            grad_sum_h=one.grad_sum_o,
            grad_att_h=one.grad_att_o,
            dq_h=one.dq_low_o,
            dkv_h=one.dkv_o,
        )
        two = part(heads // 2, heads, large, makes_last, 12, None, halfway(one))
        return types.SimpleNamespace(**{**vars(one), **vars(two)})

    def weight_grads(plan, side, arrays, scratch, after=()):
        blocks = ((2, width, width), bf16)
        call = launch(
            contract_blocks,
            plan,
            side,
            plain,
            dict(),
            arrays,
            dict(sent_o=blocks, kept_o=blocks),
            dict(**scratch, blocks=((4, width, width), bf16)),
            36,
            8,
            after=after,
        )
        return call.sent_o, call.kept_o

    def first_sums(halves, section=None):
        sent, kept = halves
        got = send(sent, to_core, section)

        def block(side):
            return sum(
                lax.dynamic_index_in_dim(part, side, 0, keepdims=False).astype(f32)
                for part in (kept, got)
            )

        return block(1 - x).astype(bf16), block(x)

    def middle_sums(sums, section=None):
        away, total = sums
        return (total + send(away, to_x, section).astype(f32)).astype(bf16)

    def last_sums(total, later=(), section=None):
        shares = total.reshape(group, width // group, width)

        def share(step):
            return lax.dynamic_index_in_dim(shares, lax.rem(z + step, group), 0, keepdims=False)

        parts = [share(0)]
        for step in range(1, group):
            parts.append(send(share(step), along_z(step), section))
        if later:
            parts = [fence(part, *later) for part in parts]
        return sum(part.astype(f32) for part in parts).astype(bf16)

    def along_z(step):
        return lambda t, i, k, c: (t, i, (k + step) % group, c)

    def gather_z(share):
        return [share] + [send(share, along_z(step)) for step in range(1, group)]

    def gain_block(rows):
        filled = jnp.concatenate([jnp.stack(rows), jnp.zeros((16 - len(rows), width), f32)])
        return filled.astype(bf16)

    def spread(targets, own, own_x, outs, parts):
        return launch(
            spread_pieces,
            targets,
            None,
            plain,
            dict(),
            dict(own_h=own, own_x_h=own_x, other_h=exchange(own), other_x_h=exchange(own_x)),
            outs,
            dict(
                pieces=((4,) + own.shape, bf16),
                wide=((4 * group * parts, width // group, width), f32),
                gain_grads=((16, width), f32),
            ),
            8 + 4 * group * parts,
            5,
        )

    tokens, all_tokens = micros * length, 2 * micros * length
    turn, turn_all = ((width, tokens), bf16), ((width, all_tokens), bf16)
    narrow, narrow_all = ((tokens, width), bf16), ((all_tokens, width), bf16)
    pair_all = ((all_tokens, 2 * width), bf16)
    deep = ((tokens, hidden), bf16)

    def part_of(buffer, *sources):
        return lambda column: (buffer, sources, column)

    def key_rows(buffer, sources):
        first, second = pl.ds(0, length), pl.ds(length, length)
        return part_of(buffer, *[source.at[rows] for rows in (first, second) for source in sources])

    def cross_plan(r):
        rows = pl.ds(0, length)
        low_part = part_of(r.low, r.low0_h, r.low1_h)
        att_part = part_of(r.att, r.att0_h, r.att1_h)
        dq_part = part_of(r.dq, r.dq0_h, r.dq1_h)
        branch_part = part_of(r.branch, r.branch0_h, r.branch1_h)
        sources = (r.mem0_h, r.mem1_h, r.mem2_h, r.mem3_h)
        mem_part = part_of(r.mem, *[source.at[rows] for source in sources])
        pair_part = key_rows(r.pair, (r.pair0_h, r.pair1_h))
        return [
            (r.turn, low_part(0), dq_part(0)),
            (r.turn_att, att_part(0), branch_part(0)),
            (r.turn_all, mem_part(0), pair_part(0)),
            (r.turn_all, mem_part(0), pair_part(1)),
        ]

    def rising_plan(r):
        low_part = part_of(r.low, r.low0_h, r.low1_h)
        up_part = part_of(r.up, r.up0_h, r.up1_h)
        return [(r.turn, low_part(0), up_part(block)) for block in range(4)]

    def falling_plan(r):
        act_part = part_of(r.act, r.act0_h, r.act1_h)
        down_part = part_of(r.down, r.down0_h, r.down1_h)
        return [(r.turn, act_part(block), down_part(0)) for block in range(4)]

    def self_plan(r):
        rows = pl.ds(0, length)
        sources = (r.x0_h, r.x1_h, r.x2_h, r.x3_h)
        x_part = part_of(r.x, *[source.at[rows] for source in sources])
        dq_part = part_of(r.dq, r.dq0_h, r.dq1_h)
        pair_part = key_rows(r.pair, (r.pair0_h, r.pair1_h))
        att_part = part_of(r.att, r.att0_h, r.att1_h)
        branch_part = part_of(r.branch, r.branch0_h, r.branch1_h)
        return [
            (r.turn_all, x_part(0), dq_part(0)),
            (r.turn_all, x_part(0), pair_part(0)),
            (r.turn_all, x_part(0), pair_part(1)),
            (r.turn, att_part(0), branch_part(0)),
        ]

    last = micros - 1
    feeds, ends = [None] * micros, [None] * micros
    cross_halves = weight_grads(
        cross_plan,
        1,
        dict(
            low0_h=forward[0].first_low_o,
            low1_h=forward[1].first_low_o,
            dq0_h=cross[0].dq_low_o,
            dq1_h=cross[1].dq_low_o,
            att0_h=cross[0].att_o,
            att1_h=cross[1].att_o,
            branch0_h=cross[0].branch_o,
            branch1_h=cross[1].branch_o,
            mem0_h=memories[0],
            mem1_h=memories[1],
            mem2_h=memories_other[0],
            mem3_h=memories_other[1],
            pair0_h=cross[0].dkv_o,
            pair1_h=cross[1].dkv_o,
        ),
        dict(
            low=narrow,
            dq=narrow,
            att=narrow,
            branch=narrow,
            mem=narrow_all,
            pair=pair_all,
            turn=turn,
            turn_att=turn,
            turn_all=turn_all,
        ),
        (made[last],),
    )
    cross_sums = first_sums(cross_halves, 1)
    results = jnp.stack(
        [
            jnp.where(decoder, call.decoded_o, done.memory_o[:length])
            for call, done in zip(cross, forward)
        ]
    )
    results = send(results, to_row)
    latest = made[last]

    def part_sum(micro, *before):
        end = ends[micro]
        away = fence(end.part_other_o, *before)
        total = (end.part_own_o + exchange(away).astype(f32)).astype(bf16)
        return total, send(total, to_row)

    steps = []
    for micro in range(last):
        feeds[micro] = backward_feed(micro, (latest,))
        first = feeds[micro].grad_first_o
        ends[micro] = backward_self(micro, 0, first)
        ends[micro] = backward_self(micro, 1, first, vars(ends[micro]), (cross_sums[0], grads_memory[last]))
        cross_total = middle_sums(cross_sums, 1)
        steps.append(part_sum(micro, cross_total))
        latest = ends[micro].gain_early_o
    feeds[last] = backward_feed(last, (latest,))

    rising_halves = weight_grads(
        rising_plan,
        None,
        dict(
            low0_h=cross[0].ffn_low_o,
            low1_h=cross[1].ffn_low_o,
            up0_h=feeds[0].up_grad_o,
            up1_h=feeds[1].up_grad_o,
        ),
        dict(low=narrow, up=deep, turn=turn),
        (results,) + tuple(step[0] for step in steps),
    )
    cross_share = last_sums(cross_total, (rising_halves[0],), 1)
    third = sum(call.gain_grads_o[1] for call in cross)
    cross_share = jnp.concatenate([cross_share, gain_block([third])])
    rising_sums = first_sums((fence(rising_halves[0], cross_share), rising_halves[1]))
    rising_total = middle_sums(rising_sums)
    falling_halves = weight_grads(
        falling_plan,
        None,
        dict(
            act0_h=cross[0].act_o,
            act1_h=cross[1].act_o,
            down0_h=feeds[0].down_grad_o,
            down1_h=feeds[1].down_grad_o,
        ),
        dict(act=deep, down=narrow, turn=turn),
        (rising_sums[0],) + tuple(step[1] for step in steps),
    )
    cross_sent = send(cross_share, to_encoder)
    falling_sent = fence(falling_halves[0], rising_total)
    falling_sums = first_sums((falling_sent, falling_halves[1]))
    falling_total = middle_sums(falling_sums)
    shares = []

    def halfway(one):
        shares.append(last_sums(rising_total, (one.gain_early_o,)))
        shares.append(jnp.where(decoder, cross_share, fence(cross_sent, one.gain_early_o)))
        return (*shares, falling_total)

    ends[last] = backward_self(
        last,
        None,
        feeds[last].grad_first_o,
        None,
        (falling_sums[0],),
        halfway,
    )
    one_own = gather_z(jnp.concatenate(shares))
    steps.append(part_sum(last, one_own[1], one_own[-1]))

    self_halves = weight_grads(
        self_plan,
        None,
        dict(
            x0_h=own[0],
            x1_h=own[1],
            x2_h=other[0],
            x3_h=other[1],
            dq0_h=ends[0].dq_low_o,
            dq1_h=ends[1].dq_low_o,
            pair0_h=ends[0].dkv_o,
            pair1_h=ends[1].dkv_o,
            att0_h=forward[0].att_o,
            att1_h=forward[1].att_o,
            branch0_h=ends[0].branch_o,
            branch1_h=ends[1].branch_o,
        ),
        dict(
            x=narrow_all,
            dq=narrow,
            pair=pair_all,
            att=narrow,
            branch=narrow,
            turn=turn,
            turn_all=turn_all,
        ),
        (one_own[1], one_own[-1], steps[last][0]),
    )
    away, total = first_sums((fence(self_halves[0], *one_own[1:]), self_halves[1]))
    one_own = jnp.stack(one_own)
    self_total = middle_sums((fence(away, one_own, steps[last][1]), total))
    falling_share = last_sums(fence(falling_total, one_own))
    self_share = last_sums(self_total)
    one_own_x = send(fence(one_own, self_total), to_x)

    early = sum(end.gain_early_o[0] for end in ends)
    late = jnp.where(
        decoder,
        sum(call.gain_grads_o[0] for call in cross),
        sum(call.gain_late_o[0] for call in feeds),
    )
    two_own = jnp.stack(
        gather_z(jnp.concatenate([falling_share, self_share, gain_block([early, late])]))
    )
    two_own_x = send(fence(two_own, one_own_x), to_x)

    def columns(block):
        return pl.ds(block * width, width)

    def one_targets(r, block, row, rows):
        lines = pl.ds(row, rows)
        rising = r.up_o.at[lines, columns(block)]
        if block >= 2:
            return [rising, r.pair_o.at[lines, columns(block - 2)]]
        return [rising, (r.out_o if block else r.query_o).at[lines]]

    def two_targets(r, block, row, rows):
        falling = r.down_o.at[pl.ds(block * width + row, rows)]
        lines = pl.ds(row, rows)
        if block == 3:
            return [falling, r.out_o.at[lines]]
        return [falling, r.mixed_o.at[lines, columns(block)]]

    square_out, gains_out = ((width, width), f32), ((16, width), f32)
    one_grads = spread(
        one_targets,
        one_own,
        one_own_x,
        dict(
            up_o=((width, hidden), f32),
            query_o=square_out,
            pair_o=((width, 2 * width), f32),
            out_o=square_out,
            gains_o=gains_out,
        ),
        2,
    )
    two_grads = spread(
        two_targets,
        two_own,
        two_own_x,
        dict(
            down_o=((hidden, width), f32),
            mixed_o=((width, 3 * width), f32),
            out_o=square_out,
            gains_o=gains_out,
        ),
        2,
    )

    grad_input = jnp.stack([step[1] for step in steps])
    return (
        results[None, :, None],
        grad_input.astype(f32)[None, :, None],
        two_grads.mixed_o[None],
        two_grads.out_o[None],
        one_grads.up_o[None],
        two_grads.down_o[None],
        two_grads.gains_o[None, :2],
        one_grads.query_o,
        one_grads.pair_o,
        one_grads.out_o,
        one_grads.gains_o[0],
    )


def shards(*arrays):
    layer_input = arrays[0]
    micros, rows, length = layer_input.shape[1:4]
    simple = (
        lax.axis_size("section") == 2
        and lax.axis_size("seq") == 2
        and lax.axis_size("dp") in (4, 8, 16)
        and (micros, rows) == (2, 1)
        and length == layer_input.shape[-1] == CHUNK
        and arrays[4].shape[-1] == 4 * CHUNK
    )
    return split_rows(*arrays) if simple else any_rows(*arrays)


def solution(mesh):
    in_specs = (
        P("section", None, "dp", "seq", None),
        P("section", None, "dp", "seq"),
        P("section", None, None),
        P("section", None, None),
        P("section", None, None),
        P("section", None, None),
        P("section", None, None),
        P(),
        P(),
        P(),
        P(),
        P(None, "dp", "seq", None),
    )
    out_specs = (
        P("section", None, "dp", "seq", None),
        P("section", None, "dp", "seq", None),
        P("section", None, None),
        P("section", None, None),
        P("section", None, None),
        P("section", None, None),
        P("section", None, None),
        P(),
        P(),
        P(),
        P(),
    )
    return jax.shard_map(shards, mesh=mesh, in_specs=in_specs, out_specs=out_specs, check_vma=False)
```

```python
import types

import jax
import jax.numpy as jnp
from jax import lax
from jax.experimental import pallas as pl
from jax.experimental.pallas import tpu as pltpu
from jax.sharding import PartitionSpec as P

HEADS = 8
TILE = 256
LANES = 128
CHUNK = 512

f32 = jnp.float32
bf16 = jnp.bfloat16
negative_big = -1e30
epsilon = 1e-05


def dot(left, right):
    return lax.dot_general(left, right, (((1,), (0,)), ((), ())), preferred_element_type=f32)


def dot_nt(left, right):
    return lax.dot_general(left, right, (((1,), (1,)), ((), ())), preferred_element_type=f32)


def dot_tn(left, right):
    return lax.dot_general(left, right, (((0,), (0,)), ((), ())), preferred_element_type=f32)


def standardize(values):
    center = values - jnp.mean(values, axis=-1, keepdims=True)
    inverse = lax.rsqrt(jnp.mean(center * center, axis=-1, keepdims=True) + epsilon)
    return center * inverse, inverse


def standardize_back(grad_out, standard, gain_row, inverse):
    scaled = grad_out * gain_row
    grad_in = inverse * (
        scaled
        - jnp.mean(scaled, axis=-1, keepdims=True)
        - standard * jnp.mean(scaled * standard, axis=-1, keepdims=True)
    )
    return grad_in, jnp.sum(grad_out * standard, axis=0, keepdims=True)


class Copies:
    def __init__(self, sems):
        self.sems = sems
        self.used = 0

    def start(self, source, target):
        copy = pltpu.make_async_copy(source, target, self.sems.at[self.used])
        self.used += 1
        copy.start()
        return copy


def wait_all(copies):
    for copy in copies:
        copy.wait()


def spread_pairs(target, source, factor, pairs):
    tiles = target.shape[1]
    half = lax.broadcasted_iota(jnp.int32, (TILE, LANES), 1) < LANES // 2
    first = jnp.where(half, factor, 0.0).astype(bf16)
    second = jnp.where(half, 0.0, factor).astype(bf16)
    for tile in range(tiles):
        for pair in pairs:
            block = source[tile * TILE : (tile + 1) * TILE, pair * LANES : (pair + 1) * LANES]
            target[pair, tile, :TILE, :] = block * first
            target[pair, tile, TILE:, :] = block * second


def turn_tiles(target, source, column, pairs):
    low, high = pairs[0] * LANES, (pairs[-1] + 1) * LANES
    for tile in range(target.shape[0]):
        block = source[tile * TILE : (tile + 1) * TILE, column + low : column + high]
        target[tile, low:high, :] = jnp.transpose(block)


def place_documents(r, copies):
    wait_all(copies)
    q_tiles = r.qd.shape[0]
    for part in range(3):
        row = r.docs[part].astype(f32)[0:1, :]
        for tile in range(q_tiles):
            piece = row[:, tile * TILE : (tile + 1) * TILE]
            slot = part * q_tiles + tile
            r.bounds[0, slot] = jnp.min(piece).astype(jnp.int32)
            r.bounds[1, slot] = jnp.max(piece).astype(jnp.int32)
            if part == 0:
                r.qd[tile] = jnp.broadcast_to(piece, (8, TILE))
        if part > 0:
            for start in range(0, row.shape[1], LANES):
                block = jnp.broadcast_to(row[:, start : start + LANES], (LANES, LANES))
                place = (part - 1) * row.shape[1] + start
                r.kdc[place : place + LANES, :] = jnp.transpose(block)


def load_documents(r, move, queries, own, other):
    rows = pl.ds(r.docs.shape[2], r.docs.shape[1])
    return [
        move.start(source.at[rows], r.docs.at[part])
        for part, source in enumerate((queries, own, other))
    ]


def tile_place(r, core, causal, q_tile, k_tile):
    q_tiles = r.qd.shape[0]
    length = q_tiles * TILE
    owner = jnp.where(k_tile < q_tiles, core, 1 - core)
    k_start = owner * length + lax.rem(k_tile, q_tiles) * TILE
    ahead = core * length + q_tile * TILE - k_start
    ahead = jnp.where(causal == 1, ahead, 2 * length * TILE)
    q_low, q_high = r.bounds[0, q_tile], r.bounds[1, q_tile]
    k_low, k_high = r.bounds[0, q_tiles + k_tile], r.bounds[1, q_tiles + k_tile]
    active = (q_low <= k_high) & (k_low <= q_high) & (ahead > -TILE)
    whole = (q_low == k_high) & (k_low == q_high) & (ahead >= TILE)
    return active, whole, ahead


def each_tile(place, body):
    active, whole, ahead = place
    pl.when(active & jnp.logical_not(whole))(lambda: body(ahead))
    pl.when(whole)(lambda: body(None))


def fill_bias(r, q_tile, k_tile, ahead):
    keys = r.kdc[pl.ds(pl.multiple_of(k_tile * TILE, TILE), TILE), :]
    shift = lax.broadcasted_iota(jnp.int32, (TILE, LANES), 0) - lax.broadcasted_iota(
        jnp.int32, (TILE, LANES), 1
    )
    queries = r.qd[q_tile]
    for start in range(0, TILE, LANES):
        same = keys == queries[0:1, start : start + LANES]
        allowed = same & (shift - start <= ahead)
        r.bias[:, start : start + LANES] = jnp.where(allowed, 0.0, negative_big)


def attention_forward(r, core, causal):
    pairs, q_tiles = r.qm.shape[:2]
    k_tiles = r.vt.shape[0]

    def one_query_tile(q_tile, carry):
        r.top[...] = jnp.full(r.top.shape, negative_big, f32)
        r.total[...] = jnp.zeros(r.total.shape, f32)
        r.turned[...] = jnp.zeros(r.turned.shape, f32)

        def one_key_tile(k_tile, inner):
            def one_tile(ahead):
                if ahead is not None:
                    fill_bias(r, q_tile, k_tile, ahead)
                rows = pl.ds(pl.multiple_of(k_tile * TILE, TILE), TILE)

                def raw(pair):
                    keys = r.kv[rows, pair * LANES : (pair + 1) * LANES]
                    return dot_nt(keys, r.qm[pair, q_tile])

                raw_next = raw(0)
                for pair in range(pairs):
                    scores = raw_next
                    if ahead is not None:
                        bias = r.bias[...]
                        scores = scores + jnp.concatenate([bias, bias], axis=1)
                    if pair + 1 < pairs:
                        raw_next = raw(pair + 1)
                    old_top = r.top[pair : pair + 1, :]
                    new_top = jnp.maximum(old_top, jnp.max(scores, axis=0, keepdims=True))
                    weights = jnp.exp(scores - new_top)
                    shrink = jnp.exp(old_top - new_top)
                    r.top[pair : pair + 1, :] = new_top
                    r.total[pair : pair + 1, :] = r.total[
                        pair : pair + 1, :
                    ] * shrink + jnp.sum(weights, axis=0, keepdims=True)
                    low = weights.astype(bf16)
                    for side in range(2):
                        span = slice(side * TILE, (side + 1) * TILE)
                        head = slice((2 * pair + side) * 64, (2 * pair + side + 1) * 64)
                        r.turned[head, :] = r.turned[head, :] * shrink[:, span] + dot(
                            r.vt[k_tile, head, :], low[:, span]
                        )

            each_tile(tile_place(r, core, causal, q_tile, k_tile), one_tile)
            return inner

        lax.fori_loop(0, k_tiles, one_key_tile, 0)
        for pair in range(pairs):
            total = r.total[pair : pair + 1, :]
            r.lse[q_tile, pair : pair + 1, :] = r.top[pair : pair + 1, :] + jnp.log(total)
            share = 1.0 / total
            for side in range(2):
                span = slice(side * TILE, (side + 1) * TILE)
                head = slice((2 * pair + side) * 64, (2 * pair + side + 1) * 64)
                r.turned[head, :] = r.turned[head, :] * share[:, span]
        rows = pl.ds(pl.multiple_of(q_tile * TILE, TILE), TILE)
        r.att[rows, :] = jnp.transpose(r.turned[...]).astype(bf16)
        return carry

    lax.fori_loop(0, q_tiles, one_query_tile, 0)


def row_products(r, grad_att, pairs):
    low, high = pairs[0] * LANES, (pairs[-1] + 1) * LANES
    for tile in range(r.qm.shape[1]):
        rows = slice(tile * TILE, (tile + 1) * TILE)
        product = jnp.transpose(
            grad_att[rows, low:high].astype(f32) * r.att[rows, low:high].astype(f32)
        )
        for pair in pairs:
            for side in range(2):
                head = (2 * pair + side) * 64 - low
                r.delta[tile, pair : pair + 1, side * TILE : (side + 1) * TILE] = jnp.sum(
                    product[head : head + 64, :], axis=0, keepdims=True
                )


def attention_backward(r, core, causal, pairs):
    q_tiles, k_tiles = r.qm.shape[1], r.kt.shape[0]
    width = r.kt.shape[1]
    low, high = pairs[0] * LANES, (pairs[-1] + 1) * LANES
    for start in (0, width):
        r.dkv[:, start + low : start + high] = jnp.zeros((r.dkv.shape[0], high - low), f32)

    def one_query_tile(q_tile, carry):
        r.turned[low:high, :] = jnp.zeros((high - low, TILE), f32)

        def one_key_tile(k_tile, inner):
            def one_tile(ahead):
                if ahead is not None:
                    fill_bias(r, q_tile, k_tile, ahead)
                rows = pl.ds(pl.multiple_of(k_tile * TILE, TILE), TILE)

                def raw(pair):
                    lanes = slice(pair * LANES, (pair + 1) * LANES)
                    lanes_v = slice(width + pair * LANES, width + (pair + 1) * LANES)
                    return (
                        dot_nt(r.kv[rows, lanes], r.qm[pair, q_tile]),
                        dot_nt(r.kv[rows, lanes_v], r.gm[pair, q_tile]),
                    )

                raw_next = raw(pairs[0])
                for pair in pairs:
                    scores, grad_probs = raw_next
                    if ahead is not None:
                        bias = r.bias[...]
                        scores = scores + jnp.concatenate([bias, bias], axis=1)
                    if pair < pairs[-1]:
                        raw_next = raw(pair + 1)
                    probs = jnp.exp(scores - r.lse[q_tile, pair : pair + 1, :])
                    grad_scores = probs * (grad_probs - r.delta[q_tile, pair : pair + 1, :])
                    probs_low = probs.astype(bf16)
                    grad_low = grad_scores.astype(bf16)
                    lanes = slice(pair * LANES, (pair + 1) * LANES)
                    lanes_v = slice(width + pair * LANES, width + (pair + 1) * LANES)
                    r.dkv[rows, lanes] += dot(grad_low, r.qm[pair, q_tile])
                    r.dkv[rows, lanes_v] += dot(probs_low, r.gm[pair, q_tile])
                    for side in range(2):
                        span = slice(side * TILE, (side + 1) * TILE)
                        head = slice((2 * pair + side) * 64, (2 * pair + side + 1) * 64)
                        r.turned[head, :] += dot(r.kt[k_tile, head, :], grad_low[:, span])

            each_tile(tile_place(r, core, causal, q_tile, k_tile), one_tile)
            return inner

        lax.fori_loop(0, k_tiles, one_key_tile, 0)
        rows = pl.ds(pl.multiple_of(q_tile * TILE, TILE), TILE)
        r.dq[rows, low:high] = jnp.transpose(r.turned[low:high, :]) * (64**-0.5)
        return carry

    lax.fori_loop(0, q_tiles, one_query_tile, 0)


def feed_forward(r, low):
    chunks = [slice(at, at + CHUNK) for at in range(0, r.w_in.shape[1], CHUNK)]
    upward_next = dot(low[...], r.w_in[:, chunks[0]])
    for place, span in enumerate(chunks):
        upward = upward_next
        if place + 1 < len(chunks):
            upward_next = dot(low[...], r.w_in[:, chunks[place + 1]])
        gate = jax.nn.sigmoid(upward)
        active = (upward * gate).astype(bf16)
        r.act[:, span] = active
        r.slope[:, span] = (gate + upward * gate * (1.0 - gate)).astype(r.slope.dtype)
        part = dot(active, r.w_down[span, :])
        if place:
            r.sum[...] += part
        else:
            r.sum[...] = part


def feed_backward(r):
    chunks = [slice(at, at + CHUNK) for at in range(0, r.w_in.shape[1], CHUNK)]
    active_next = dot_nt(r.down_grad[...], r.w_down[chunks[0], :])
    for place, span in enumerate(chunks):
        grad_active = active_next.astype(bf16)
        if place + 1 < len(chunks):
            active_next = dot_nt(r.down_grad[...], r.w_down[chunks[place + 1], :])
        grad_up = (grad_active.astype(f32) * r.slope[:, span].astype(f32)).astype(bf16)
        r.up_grad[:, span] = grad_up
        part = dot_nt(grad_up, r.w_in[:, span])
        if place:
            r.sum[...] += part
        else:
            r.sum[...] = part


def self_forward(r):
    length, width = r.unit1.shape
    decoder, core = r.meta[0], r.meta[1]
    move = Copies(r.sems)
    whole = pl.ds(0, length)
    documents = load_documents(r, move, r.x_own_h, r.x_own_h, r.x_other_h)
    early = [
        move.start(r.x_own_h.at[whole], r.x.at[whole]),
        move.start(r.x_other_h.at[whole], r.x.at[pl.ds(length, length)]),
        move.start(r.w_mixed_h, r.w_mixed),
    ]
    later = [
        move.start(r.w_out_h, r.w_out),
        move.start(r.w_in_h, r.w_in),
        move.start(r.w_down_h, r.w_down),
    ]
    place_documents(r, documents)
    wait_all(early)
    r.q[...] = dot(r.x[:length, :], r.w_mixed[:, :width]).astype(bf16)
    r.kv[...] = dot(r.x[...], r.w_mixed[:, width:]).astype(bf16)
    outs = [move.start(r.q, r.q_o), move.start(r.kv, r.kv_o)]
    pairs = range(width // LANES)
    spread_pairs(r.qm, r.q, 64**-0.5, pairs)
    turn_tiles(r.vt, r.kv, width, pairs)
    attention_forward(r, core, decoder)
    wait_all(later)
    outs += [move.start(r.att, r.att_o), move.start(r.lse, r.lse_o)]
    unit, inverse = standardize(r.x[:length, :].astype(f32) + dot(r.att[...], r.w_out[...]))
    r.unit1[...] = unit
    r.inv1[...] = jnp.broadcast_to(inverse, r.inv1.shape)
    r.first_low[...] = (unit * r.gains[0:1, :]).astype(bf16)
    outs += [
        move.start(r.unit1, r.unit1_o),
        move.start(r.inv1, r.inv1_o),
        move.start(r.first_low, r.first_low_o),
    ]

    @pl.when(decoder == 0)
    def _():
        feed_forward(r, r.first_low)
        late = [
            move.start(r.first_low, r.ffn_low_o),
            move.start(r.act, r.act_o),
            move.start(r.slope, r.slope_o),
        ]
        unit2, inverse2 = standardize(r.unit1[...] * r.gains[0:1, :] + r.sum[...])
        r.memory[:length, :] = (unit2 * r.gains[1:2, :]).astype(bf16)
        r.memory[length:, :] = r.docs[0]
        late += [move.start(r.memory, r.memory_o)]
        r.unit2[...] = unit2
        r.inv2[...] = jnp.broadcast_to(inverse2, r.inv2.shape)
        late += [move.start(r.unit2, r.unit2_o), move.start(r.inv2, r.inv2_o)]
        wait_all(late)

    wait_all(outs)


def cross_both_ways(r):
    length, width = r.unit1_h.shape
    core = r.meta[1]
    move = Copies(r.sems)
    whole = pl.ds(0, length)
    documents = load_documents(r, move, r.x_own_h, r.memory_own_h, r.memory_other_h)
    moves = [
        move.start(r.memory_own_h.at[whole], r.x.at[whole]),
        move.start(r.memory_other_h.at[whole], r.x.at[pl.ds(length, length)]),
        move.start(r.w_pair_h, r.w_pair),
        move.start(r.first_low_h, r.first_low),
        move.start(r.w_query_h, r.w_query),
    ]
    later = [
        move.start(r.unit1_h, r.unit1),
        move.start(r.w_cross_h, r.w_cross),
        move.start(r.w_in_h, r.w_in),
        move.start(r.w_down_h, r.w_down),
        move.start(r.cot_h.at[r.micro], r.cot),
    ]
    place_documents(r, documents)
    wait_all(moves)
    r.kv[...] = dot(r.x[...], r.w_pair[...]).astype(bf16)
    r.q[...] = dot(r.first_low[...], r.w_query[...]).astype(bf16)
    pairs = range(width // LANES)
    spread_pairs(r.qm, r.q, 64**-0.5, pairs)
    turn_tiles(r.vt, r.kv, width, pairs)
    turn_tiles(r.kt, r.kv, 0, pairs)
    attention_forward(r, core, 0)
    outs = [move.start(r.att, r.att_o)]
    wait_all(later)
    first = r.unit1[...] * r.gains[0:1, :]
    unit, inverse = standardize(first + dot(r.att[...], r.w_cross[...]))
    r.unit2[...] = unit
    r.inv2[...] = jnp.broadcast_to(inverse, r.inv2.shape)
    r.second_low[...] = (unit * r.cross_gain[...]).astype(bf16)
    outs += [move.start(r.second_low, r.ffn_low_o)]
    feed_forward(r, r.second_low)
    outs += [move.start(r.act, r.act_o)]
    unit3, inverse3 = standardize(r.unit2[...] * r.cross_gain[...] + r.sum[...])
    r.decoded[...] = (unit3 * r.gains[1:2, :]).astype(bf16)
    outs += [move.start(r.decoded, r.decoded_o)]
    grad_third, gain_late = standardize_back(
        r.cot[...].astype(f32), unit3, r.gains[1:2, :], inverse3
    )
    r.keep[...] = grad_third
    r.down_grad[...] = grad_third.astype(bf16)
    outs += [move.start(r.down_grad, r.down_grad_o)]
    feed_backward(r)
    outs += [move.start(r.up_grad, r.up_grad_o)]
    grad_sum, gain_cross = standardize_back(
        r.keep[...] + r.sum[...], r.unit2[...], r.cross_gain[...], r.inv2[:, 0:1]
    )
    r.gain_grads[...] = jnp.zeros(r.gain_grads.shape, f32)
    r.gain_grads[0:1, :] = gain_late
    r.gain_grads[1:2, :] = gain_cross
    r.keep[...] = grad_sum
    r.branch[...] = grad_sum.astype(bf16)
    outs += [move.start(r.gain_grads, r.gain_grads_o), move.start(r.branch, r.branch_o)]
    r.q[...] = dot_nt(r.branch[...], r.w_cross[...]).astype(bf16)
    spread_pairs(r.gm, r.q, 1.0, pairs)
    row_products(r, r.q, pairs)
    attention_backward(r, core, 0, pairs)
    r.dq_low[...] = r.dq[...].astype(bf16)
    r.keep[...] += dot_nt(r.dq_low[...], r.w_query[...])
    outs += [move.start(r.dq_low, r.dq_low_o), move.start(r.keep, r.grad_first_o)]
    r.dkv_low[...] = r.dkv[...].astype(bf16)
    outs += [move.start(r.dkv_low, r.dkv_o)]
    part = dot_nt(r.dkv_low[...], r.w_pair[...])
    r.part_other[...] = part[length:, :].astype(bf16)
    r.part_own[...] = part[:length, :]
    outs += [move.start(r.part_other, r.part_other_o), move.start(r.part_own, r.part_own_o)]
    wait_all(outs)


def feed_backward_alone(r):
    move = Copies(r.sems)
    early = [
        move.start(r.grad_memory_h, r.cot),
        move.start(r.unit2_h, r.unit2),
        move.start(r.inv2_h, r.inv2),
    ]
    later = [
        move.start(r.w_down_h, r.w_down),
        move.start(r.slope_h, r.slope),
        move.start(r.w_in_h, r.w_in),
    ]
    wait_all(early)
    grad_third, gain_late = standardize_back(
        r.cot[...].astype(f32), r.unit2[...], r.gains[1:2, :], r.inv2[:, 0:1]
    )
    r.gain_grads[...] = jnp.broadcast_to(gain_late, r.gain_grads.shape)
    r.keep[...] = grad_third
    r.down_grad[...] = grad_third.astype(bf16)
    outs = [move.start(r.down_grad, r.down_grad_o), move.start(r.gain_grads, r.gain_late_o)]
    wait_all(later)
    feed_backward(r)
    outs += [move.start(r.up_grad, r.up_grad_o)]
    r.keep[...] += r.sum[...]
    outs += [move.start(r.keep, r.grad_first_o)]
    wait_all(outs)


def self_backward(r, plan):
    r.micro, first, last = plan
    length, width = r.att_h.shape
    decoder, core = r.meta[0], r.meta[1]
    pairs = range(first, last)
    low, high = first * LANES, last * LANES
    move = Copies(r.sems)
    later = [
        move.start(r.q_h, r.q),
        move.start(r.kv_h, r.kv),
        move.start(r.att_h, r.att),
        move.start(r.lse_h, r.lse),
    ]
    if first == 0:
        early = [
            move.start(r.grad_first_h, r.keep),
            move.start(r.unit1_h, r.unit1),
            move.start(r.inv1_h, r.inv1),
            move.start(r.w_out_h, r.w_out),
        ]
    else:
        early = [move.start(r.grad_att_h, r.grad_att)]
    outs = []
    place_documents(r, load_documents(r, move, r.x_own_h, r.x_own_h, r.x_other_h))
    wait_all(early)
    if first == 0:
        grad_sum, gain_early = standardize_back(
            r.keep[...], r.unit1[...], r.gains[0:1, :], r.inv1[:, 0:1]
        )
        r.gain_grads[...] = jnp.broadcast_to(gain_early, r.gain_grads.shape)
        r.keep[...] = grad_sum
        r.branch[...] = grad_sum.astype(bf16)
        r.grad_att[...] = dot_nt(r.branch[...], r.w_out[...]).astype(bf16)
        outs += [move.start(r.gain_grads, r.gain_early_o), move.start(r.branch, r.branch_o)]
        if last < width // LANES:
            outs += [move.start(r.keep, r.grad_sum_o), move.start(r.grad_att, r.grad_att_o)]
    wait_all(later)
    if last == width // LANES:
        ends = [move.start(r.w_mixed_h, r.w_mixed)]
        if first > 0:
            ends += [
                move.start(r.grad_sum_h, r.keep),
                move.start(r.dq_h.at[:, pl.ds(0, low)], r.dq_low.at[:, pl.ds(0, low)]),
                move.start(r.dkv_h.at[:, pl.ds(0, low)], r.dkv_low.at[:, pl.ds(0, low)]),
                move.start(
                    r.dkv_h.at[:, pl.ds(width, low)], r.dkv_low.at[:, pl.ds(width, low)]
                ),
            ]
    spread_pairs(r.qm, r.q, 64**-0.5, pairs)
    turn_tiles(r.kt, r.kv, 0, pairs)
    spread_pairs(r.gm, r.grad_att, 1.0, pairs)
    row_products(r, r.grad_att, pairs)
    attention_backward(r, core, decoder, pairs)
    r.dq_low[:, low:high] = r.dq[:, low:high].astype(bf16)
    for start in (0, width):
        span = slice(start + low, start + high)
        r.dkv_low[:, span] = r.dkv[:, span].astype(bf16)
    if last == width // LANES:
        wait_all(ends)
        outs += [move.start(r.dq_low, r.dq_low_o), move.start(r.dkv_low, r.dkv_o)]
        r.keep[...] += dot_nt(r.dq_low[...], r.w_mixed[:, :width])
        part = dot_nt(r.dkv_low[...], r.w_mixed[:, width:])
        r.part_other[...] = part[length:, :].astype(bf16)
        r.keep[...] += part[:length, :]
        outs += [move.start(r.part_other, r.part_other_o), move.start(r.keep, r.part_own_o)]
    else:
        outs.append(move.start(r.dq_low.at[:, pl.ds(low, high - low)], r.dq_low_o.at[:, pl.ds(low, high - low)]))
        for start in (0, width):
            span = pl.ds(start + low, high - low)
            outs.append(move.start(r.dkv_low.at[:, span], r.dkv_o.at[:, span]))
    wait_all(outs)


def contract_blocks(r, plan):
    for core in range(2):

        @pl.when(r.meta[1] == core)
        def _(core=core):
            targets = [None] * 4
            for half in range(2):
                target = r.kept_o if half == core else r.sent_o
                targets[2 * half], targets[2 * half + 1] = target.at[0], target.at[1]
            order = (0, 1, 2, 3) if core else (2, 3, 0, 1)
            contract_in_order(r, plan(r), order, targets, Copies(r.sems))


def contract_in_order(r, blocks, order, targets, move):
    loads = dict()
    for slot in order:
        for buffer, sources, at in blocks[slot][1:]:
            if (id(buffer), at) not in loads:
                span = pl.ds(at * CHUNK, CHUNK)
                row = 0
                copies = []
                for source in sources:
                    rows = pl.ds(row, source.shape[0])
                    copies.append(move.start(source.at[:, span], buffer.at[rows, span]))
                    row += source.shape[0]
                loads[id(buffer), at] = copies
    outs = []
    held = dict()
    for slot in order:
        turn, (left, _, left_at), (right, _, right_at) = blocks[slot]
        wait_all(loads.pop((id(left), left_at), ()))
        wait_all(loads.pop((id(right), right_at), ()))
        if held.get(id(turn)) != left_at:
            for row in range(0, left.shape[0], CHUNK):
                block = left[row : row + CHUNK, left_at * CHUNK : (left_at + 1) * CHUNK]
                turn[:, row : row + CHUNK] = jnp.transpose(block)
            held[id(turn)] = left_at
        block = right[:, right_at * CHUNK : (right_at + 1) * CHUNK]
        r.blocks[slot] = dot(turn[:, : right.shape[0]], block).astype(bf16)
        outs.append(move.start(r.blocks.at[slot], targets[slot]))
    wait_all(outs)


def spread_pieces(r, targets):
    z = r.meta[3]
    group, height = r.own_h.shape[:2]
    rows = r.own_h.shape[2] // group
    for core in range(2):
        for x in range(2):

            @pl.when((r.meta[1] == core) & (r.meta[2] == x))
            def _(core=core, x=x):
                move = Copies(r.sems)
                parts = [
                    (r.own_h, core, x),
                    (r.own_x_h, core, 1 - x),
                    (r.other_h, 1 - core, x),
                    (r.other_x_h, 1 - core, 1 - x),
                ]
                loads = [
                    move.start(source, r.pieces.at[place])
                    for place, (source, _, _) in enumerate(parts)
                ]
                outs = []
                slot = 0
                gains = None
                for place, (_, half, side) in enumerate(parts):
                    loads[place].wait()
                    for step in range(group):
                        row = pl.multiple_of(lax.rem(z + (group - step), group) * rows, rows)
                        start = 0
                        for target in targets(r, 2 * half + side, row, rows):
                            r.wide[slot] = r.pieces[place, step, start : start + rows].astype(f32)
                            outs.append(move.start(r.wide.at[slot], target))
                            slot += 1
                            start += rows
                        if start < height:
                            extra = r.pieces[place, step, start:height].astype(f32)
                            gains = extra if gains is None else gains + extra
                r.gains_o[...] = gains[: r.gains_o.shape[0], :]
                wait_all(outs)


def launch(kernel, plan, side, scalars, small, large, outs, scratch, copies, work, previous=None, after=()):
    names = list(scalars) + list(small) + list(large)
    arrays = list(scalars.values()) + list(small.values()) + list(large.values())
    specs = (
        [pl.BlockSpec(memory_space=pltpu.SMEM)] * len(scalars)
        + [pl.BlockSpec(memory_space=pltpu.VMEM)] * len(small)
        + [pl.BlockSpec(memory_space=pl.ANY)] * len(large)
    )
    aliases = dict()
    for position, name in enumerate(outs):
        if previous and name in previous:
            aliases[len(arrays)] = position
            names.append("previous_" + name)
            arrays.append(previous[name])
            specs.append(pl.BlockSpec(memory_space=pl.ANY))
    for array in after:
        names.append("")
        arrays.append(array)
        specs.append(pl.BlockSpec(memory_space=pl.ANY))
    names += list(outs) + list(scratch) + ["sems"]

    def body(*refs):
        r = types.SimpleNamespace(**dict(zip(names, refs)))

        def run():
            if isinstance(plan, int):
                r.micro = plan
                kernel(r)
            else:
                kernel(r, plan)

        if side is None:
            run()
        else:
            pl.when(r.meta[0] == side)(run)

    results = pl.pallas_call(
        body,
        out_shape=[jax.ShapeDtypeStruct(*shape) for shape in outs.values()],
        in_specs=specs,
        out_specs=[
            pl.BlockSpec(memory_space=pltpu.VMEM if shape[0][0] < 8 else pl.ANY)
            for shape in outs.values()
        ],
        scratch_shapes=[
            pltpu.SMEM(*shape) if shape[1] == jnp.int32 else pltpu.VMEM(*shape)
            for shape in scratch.values()
        ]
        + [pltpu.SemaphoreType.DMA((copies,))],
        input_output_aliases=aliases,
        compiler_params=pltpu.CompilerParams(vmem_limit_bytes=58 * 1024 * 1024),
        cost_estimate=pl.CostEstimate(
            flops=work * 10**9, bytes_accessed=1 << 20, transcendentals=0
        ),
    )(*arrays)
    return types.SimpleNamespace(**dict(zip(outs, results)))


def attention_scratch(length, width):
    pairs, q_tiles, k_tiles = width // LANES, length // TILE, 2 * length // TILE
    return dict(
        q=((length, width), bf16),
        kv=((2 * length, 2 * width), bf16),
        qm=((pairs, q_tiles, 2 * TILE, LANES), bf16),
        kdc=((2 * length, LANES), f32),
        docs=((3, 16, width), bf16),
        qd=((length // TILE, 8, TILE), f32),
        bounds=((2, 3 * length // TILE), jnp.int32),
        bias=((TILE, TILE), f32),
        lse=((q_tiles, 8, 2 * TILE), f32),
        att=((length, width), bf16),
        turned=((width, TILE), f32),
    )


def forward_scratch(length, width):
    k_tiles = 2 * length // TILE
    return dict(
        vt=((k_tiles, width, TILE), bf16),
        top=((8, 2 * TILE), f32),
        total=((8, 2 * TILE), f32),
    )


def backward_scratch(length, width):
    pairs, q_tiles, k_tiles = width // LANES, length // TILE, 2 * length // TILE
    return dict(
        kt=((k_tiles, width, TILE), bf16),
        gm=((pairs, q_tiles, 2 * TILE, LANES), bf16),
        delta=((q_tiles, 8, 2 * TILE), f32),
        dkv=((2 * length, 2 * width), f32),
        dq=((length, width), f32),
        dkv_low=((2 * length, 2 * width), bf16),
        part_other=((length, width), bf16),
        dq_low=((length, width), bf16),
    )


def for_sending(shard):

    def short(part):
        return part.astype(jnp.bfloat16) if part.dtype == jnp.float32 else part

    return jax.tree.map(short, shard)


def from_behind(block, axis, distance):
    devices = range(lax.axis_size(axis))
    route = [(i - distance, i) for i in devices if i - distance in devices]
    return lax.ppermute(block, axis, route)


def from_root(shard, axis, root):
    mine = lax.axis_index(axis) == root
    return lax.psum(jnp.where(mine, shard, jnp.zeros_like(shard)), axis)


def matmul(left_side, right_side):
    return jnp.einsum("rsd,de->rse", left_side, right_side, preferred_element_type=jnp.float32)


def matmul_back(left_side, right_side):
    return jnp.einsum("rse,de->rsd", left_side, right_side, preferred_element_type=jnp.float32)


def contract(left_side, right_side):
    return jnp.einsum("rsd,rse->de", left_side, right_side, preferred_element_type=jnp.float32)


def normalize(values, gain_row):
    center = values - jnp.mean(values, axis=-1, keepdims=True)
    inverse = lax.rsqrt(jnp.mean(center * center, axis=-1, keepdims=True) + epsilon)
    standard = center * inverse
    return (standard * gain_row, standard, inverse)


def normalize_back(grad_out, standard, gain_row, inverse):
    scaled = grad_out * gain_row
    grad_in = inverse * (
        scaled
        - jnp.mean(scaled, axis=-1, keepdims=True)
        - standard * jnp.mean(scaled * standard, axis=-1, keepdims=True)
    )
    return (grad_in, jnp.sum(grad_out * standard, axis=(0, 1)))


def allowed_mask(query_docs, key_docs, query_place, key_place, causal):
    same_doc = query_docs[:, :, None] == key_docs[:, None, :]
    earlier = query_place[:, None] >= key_place[None, :]
    return (same_doc & (earlier | jnp.logical_not(causal)))[:, None]


def attend(queries, keys_local, values_local, query_docs, key_docs, causal, is_cross):
    rows_here, shard_len, model_width = queries.shape
    head_dim = model_width // HEADS
    score_scale = head_dim ** (-0.5)
    query_place = lax.axis_index("seq") * shard_len + jnp.arange(shard_len)
    query_heads = queries.reshape(rows_here, shard_len, HEADS, head_dim)

    def absorb(state_tuple, pieces):
        running_top, running_total, running_sum = state_tuple
        key_piece, value_piece, doc_piece = pieces
        piece_len = key_piece.shape[1]
        raw_scores = jnp.einsum(
            "rqhd,rkhd->rhqk",
            query_heads,
            key_piece.reshape(rows_here, piece_len, HEADS, head_dim),
            preferred_element_type=jnp.float32,
        )
        allowed = allowed_mask(query_docs, doc_piece, query_place, jnp.arange(piece_len), causal)
        scores = jnp.where(allowed, raw_scores * score_scale, negative_big)
        new_top = jnp.maximum(running_top, jnp.max(scores, axis=-1))
        weights = jnp.where(allowed, jnp.exp(scores - new_top[..., None]), 0.0)
        new_total = jnp.sum(weights, axis=-1)
        product = jnp.einsum(
            "rhqk,rkhd->rhqd",
            weights.astype(jnp.bfloat16),
            value_piece.reshape(rows_here, piece_len, HEADS, head_dim),
            preferred_element_type=jnp.float32,
        )
        return (new_top, new_total, product)

    init_state = (
        jnp.full((rows_here, HEADS, shard_len), negative_big, jnp.float32),
        jnp.zeros((rows_here, HEADS, shard_len), jnp.float32),
        jnp.zeros((rows_here, HEADS, shard_len, head_dim), jnp.float32),
    )
    if is_cross:
        final_top, final_total, final_sum = absorb(
            init_state,
            (
                lax.all_gather(keys_local, "seq", axis=1, tiled=True),
                lax.all_gather(values_local, "seq", axis=1, tiled=True),
                lax.all_gather(for_sending(key_docs), "seq", axis=1, tiled=True),
            ),
        )
    else:
        final_top, final_total, final_sum = absorb(
            init_state,
            (
                lax.all_gather(keys_local, "seq", axis=1, tiled=True),
                lax.all_gather(values_local, "seq", axis=1, tiled=True),
                lax.all_gather(key_docs, "seq", axis=1, tiled=True),
            ),
        )
    attended = (
        (final_sum / final_total[..., None])
        .transpose(0, 2, 1, 3)
        .reshape(rows_here, shard_len, model_width)
    )
    return (attended, final_top + jnp.log(final_total))


def attend_back(
    queries,
    keys_local,
    values_local,
    query_docs,
    key_docs,
    causal,
    log_total,
    grad_attended,
    is_cross,
):
    rows_here, shard_len, model_width = queries.shape
    head_dim = model_width // HEADS
    score_scale = head_dim ** (-0.5)
    query_place = lax.axis_index("seq") * shard_len + jnp.arange(shard_len)
    if is_cross:
        keys_full, values_full, docs_full = (
            lax.all_gather(keys_local, "seq", axis=1, tiled=True),
            lax.all_gather(values_local, "seq", axis=1, tiled=True),
            lax.all_gather(for_sending(key_docs), "seq", axis=1, tiled=True).astype(key_docs.dtype),
        )
    else:
        keys_full, values_full, docs_full = (
            lax.all_gather(keys_local, "seq", axis=1, tiled=True),
            lax.all_gather(values_local, "seq", axis=1, tiled=True),
            lax.all_gather(key_docs, "seq", axis=1, tiled=True),
        )
    full_len = keys_full.shape[1]
    query_heads = queries.reshape(rows_here, shard_len, HEADS, head_dim)
    key_heads = keys_full.reshape(rows_here, full_len, HEADS, head_dim)
    value_heads = values_full.reshape(rows_here, full_len, HEADS, head_dim)
    grad_heads = grad_attended.reshape(rows_here, shard_len, HEADS, head_dim)
    raw_scores = jnp.einsum(
        "rqhd,rkhd->rhqk", query_heads, key_heads, preferred_element_type=jnp.float32
    )
    allowed = allowed_mask(query_docs, docs_full, query_place, jnp.arange(full_len), causal)
    shifted = jnp.where(allowed, raw_scores * score_scale - log_total[..., None], negative_big)
    probs = jnp.where(allowed, jnp.exp(shifted), 0.0)
    grad_probs = jnp.einsum(
        "rqhd,rkhd->rhqk", grad_heads, value_heads, preferred_element_type=jnp.float32
    )
    delta = jnp.sum(probs * grad_probs, axis=-1)
    grad_scores = (probs * (grad_probs - delta[..., None]) * score_scale).astype(jnp.bfloat16)
    grad_queries = jnp.einsum(
        "rhqk,rkhd->rqhd", grad_scores, key_heads, preferred_element_type=jnp.float32
    ).reshape(rows_here, shard_len, model_width)
    probs_low = probs.astype(jnp.bfloat16)

    def key_terms(span):
        grad_keys = jnp.einsum(
            "rhqk,rqhd->krhd", grad_scores, query_heads, preferred_element_type=jnp.float32
        )
        grad_values = jnp.einsum(
            "rhqk,rqhd->krhd", probs_low, grad_heads, preferred_element_type=jnp.float32
        )
        return jnp.concatenate(
            [
                grad_keys.reshape(span, rows_here, model_width),
                grad_values.reshape(span, rows_here, model_width),
            ],
            axis=-1,
        )

    if is_cross:
        pair_terms = lax.psum_scatter(
            key_terms(shard_len * lax.axis_size("seq")).astype(jnp.bfloat16),
            "seq",
            scatter_dimension=0,
            tiled=True,
        ).astype(jnp.float32)
    else:
        pair_terms = lax.psum_scatter(
            key_terms(shard_len * lax.axis_size("seq")).astype(jnp.bfloat16),
            "seq",
            scatter_dimension=0,
            tiled=True,
        ).astype(jnp.float32)
    return (grad_queries, pair_terms.transpose(1, 0, 2))


def layer_forward(hidden_in, doc_own, memory, memory_docs, weights, is_decoder):
    (
        qkv_weight,
        out_weight,
        in_weight,
        down_weight,
        gains_pair,
        query_weight,
        pair_weight,
        cross_weight,
        cross_gains,
    ) = weights
    model_width = hidden_in.shape[-1]
    mixed = matmul(hidden_in, qkv_weight).astype(jnp.bfloat16)
    attended, self_lse = attend(
        mixed[..., :model_width],
        mixed[..., model_width : 2 * model_width],
        mixed[..., 2 * model_width :],
        doc_own,
        doc_own,
        is_decoder,
        False,
    )
    attended = attended.astype(jnp.bfloat16)
    first, first_unit, first_inv = normalize(
        hidden_in.astype(jnp.float32) + matmul(attended, out_weight), gains_pair[0]
    )
    first_low = first.astype(jnp.bfloat16)
    cross_queries = matmul(first_low, query_weight).astype(jnp.bfloat16)
    pair = matmul(memory, pair_weight).astype(jnp.bfloat16)
    cross_att, cross_lse = attend(
        cross_queries,
        pair[..., :model_width],
        pair[..., model_width:],
        doc_own,
        memory_docs,
        False,
        True,
    )
    cross_att = cross_att.astype(jnp.bfloat16)
    second_cross, second_unit, second_inv = normalize(
        first + matmul(cross_att, cross_weight), cross_gains
    )
    second = jnp.where(is_decoder, second_cross, first)
    second_low = second.astype(jnp.bfloat16)
    upward = matmul(second_low, in_weight)
    active = jax.nn.silu(upward).astype(jnp.bfloat16)
    result, third_unit, third_inv = normalize(second + matmul(active, down_weight), gains_pair[1])
    saved = {
        "mixed": mixed,
        "attended": attended,
        "self_lse": self_lse,
        "first_unit": first_unit,
        "first_inv": first_inv,
        "first_low": first_low,
        "cross_queries": cross_queries,
        "pair": pair,
        "cross_att": cross_att,
        "cross_lse": cross_lse,
        "second_unit": second_unit,
        "second_inv": second_inv,
        "second_low": second_low,
        "upward": upward,
        "active": active,
        "third_unit": third_unit,
        "third_inv": third_inv,
    }
    return (result, saved)


def layer_backward(
    grad_result, saved, hidden_in, doc_own, memory, memory_docs, weights, is_decoder
):
    (
        qkv_weight,
        out_weight,
        in_weight,
        down_weight,
        gains_pair,
        query_weight,
        pair_weight,
        cross_weight,
        cross_gains,
    ) = weights
    model_width = hidden_in.shape[-1]
    grad_third, grad_gain_late = normalize_back(
        grad_result, saved["third_unit"], gains_pair[1], saved["third_inv"]
    )
    down_grad = grad_third.astype(jnp.bfloat16)
    grad_down_w = contract(saved["active"], down_grad)
    grad_active = matmul_back(down_grad, down_weight).astype(jnp.bfloat16)
    sigmoid_up = jax.nn.sigmoid(saved["upward"])
    grad_upward = (
        grad_active.astype(jnp.float32)
        * (sigmoid_up + saved["upward"] * sigmoid_up * (1.0 - sigmoid_up))
    ).astype(jnp.bfloat16)
    grad_in_w = contract(saved["second_low"], grad_upward)
    grad_second = grad_third + matmul_back(grad_upward, in_weight)
    grad_cross_sum, grad_cross_gain = normalize_back(
        grad_second, saved["second_unit"], cross_gains, saved["second_inv"]
    )
    decoder_flag = is_decoder.astype(jnp.float32)
    grad_cross_sum = grad_cross_sum * decoder_flag
    grad_cross_gain = grad_cross_gain * decoder_flag
    cross_branch = grad_cross_sum.astype(jnp.bfloat16)
    grad_cross_w = contract(saved["cross_att"], cross_branch)
    grad_cross_att = matmul_back(cross_branch, cross_weight).astype(jnp.bfloat16)
    pair = saved["pair"]
    grad_cross_q, grad_pair = attend_back(
        saved["cross_queries"],
        pair[..., :model_width],
        pair[..., model_width:],
        doc_own,
        memory_docs,
        False,
        saved["cross_lse"],
        grad_cross_att,
        True,
    )
    grad_cross_q = grad_cross_q.astype(jnp.bfloat16)
    grad_pair = grad_pair.astype(jnp.bfloat16)
    grad_query_w = contract(saved["first_low"], grad_cross_q)
    grad_pair_w = contract(memory, grad_pair)
    grad_memory = matmul_back(grad_pair, pair_weight)
    grad_first = jnp.where(
        is_decoder, grad_cross_sum + matmul_back(grad_cross_q, query_weight), grad_second
    )
    grad_first_sum, grad_gain_early = normalize_back(
        grad_first, saved["first_unit"], gains_pair[0], saved["first_inv"]
    )
    self_branch = grad_first_sum.astype(jnp.bfloat16)
    grad_out_w = contract(saved["attended"], self_branch)
    grad_attended = matmul_back(self_branch, out_weight).astype(jnp.bfloat16)
    mixed = saved["mixed"]
    grad_queries, grad_pair_self = attend_back(
        mixed[..., :model_width],
        mixed[..., model_width : 2 * model_width],
        mixed[..., 2 * model_width :],
        doc_own,
        doc_own,
        is_decoder,
        saved["self_lse"],
        grad_attended,
        False,
    )
    grad_mixed = jnp.concatenate([grad_queries, grad_pair_self], axis=-1).astype(jnp.bfloat16)
    grad_qkv_w = contract(hidden_in, grad_mixed)
    grad_hidden = grad_first_sum + matmul_back(grad_mixed, qkv_weight)
    layer_grads = (
        grad_qkv_w,
        grad_out_w,
        grad_in_w,
        grad_down_w,
        jnp.stack([grad_gain_early, grad_gain_late]),
        grad_query_w,
        grad_pair_w,
        grad_cross_w,
        grad_cross_gain,
    )
    return (grad_hidden, grad_memory, layer_grads)


def any_rows(
    layer_input,
    segment_ids,
    attn_qkv,
    attn_out,
    ffn_in,
    ffn_out,
    norm_gain,
    cross_query,
    cross_pair,
    cross_out,
    cross_gain,
    out_cotangent,
):
    micro_count = layer_input.shape[1]
    section_index = lax.axis_index("section")
    is_decoder = section_index == 1
    weights = (
        attn_qkv[0],
        attn_out[0],
        ffn_in[0],
        ffn_out[0],
        norm_gain[0],
        cross_query,
        cross_pair,
        cross_out,
        cross_gain,
    )
    inputs_all = layer_input[0]
    docs_all = segment_ids[0]
    slot_ids = jnp.arange(micro_count)
    received = (jnp.zeros_like(inputs_all[0]), jnp.zeros_like(docs_all[0]))
    results = jnp.zeros_like(inputs_all)
    memories = []
    memory_doc_list = []
    for step_index in range(micro_count + 1):
        batch_index = step_index - section_index
        is_valid = (batch_index >= 0) & (batch_index < micro_count)
        chosen = jnp.clip(batch_index, 0, micro_count - 1)
        hidden_in = lax.dynamic_index_in_dim(inputs_all, chosen, 0, keepdims=False)
        doc_own = lax.dynamic_index_in_dim(docs_all, chosen, 0, keepdims=False)
        memory = received[0]
        memory_docs = jnp.where(is_valid & is_decoder, received[1], doc_own)
        memories.append(memory)
        memory_doc_list.append(memory_docs)
        result, saved = layer_forward(hidden_in, doc_own, memory, memory_docs, weights, is_decoder)
        low_result = result.astype(jnp.bfloat16)
        writing = (slot_ids == chosen) & is_valid
        results = jnp.where(writing[:, None, None, None], low_result[None], results)
        if step_index < micro_count:
            received = from_behind((low_result, doc_own), "section", 1)
    memory_stack = jnp.stack(memories)
    memory_doc_stack = jnp.stack(memory_doc_list)
    totals = tuple((jnp.zeros(weight.shape, jnp.float32) for weight in weights))
    input_grads = jnp.zeros(inputs_all.shape, jnp.float32)
    returned = jnp.zeros(inputs_all.shape[1:], jnp.float32)
    for step_index in range(micro_count + 1):
        batch_index = micro_count - step_index - section_index
        is_valid = (batch_index >= 0) & (batch_index < micro_count)
        chosen = jnp.clip(batch_index, 0, micro_count - 1)
        forward_step = jnp.clip(batch_index + section_index, 0, micro_count)
        hidden_in = lax.dynamic_index_in_dim(inputs_all, chosen, 0, keepdims=False)
        doc_own = lax.dynamic_index_in_dim(docs_all, chosen, 0, keepdims=False)
        memory = lax.dynamic_index_in_dim(memory_stack, forward_step, 0, keepdims=False)
        memory_docs = lax.dynamic_index_in_dim(memory_doc_stack, forward_step, 0, keepdims=False)
        discarded, saved = layer_forward(
            hidden_in, doc_own, memory, memory_docs, weights, is_decoder
        )
        cotangent = jnp.where(
            is_decoder,
            lax.dynamic_index_in_dim(out_cotangent, chosen, 0, keepdims=False).astype(jnp.float32),
            returned,
        )
        grad_hidden, grad_memory, layer_grads = layer_backward(
            cotangent, saved, hidden_in, doc_own, memory, memory_docs, weights, is_decoder
        )
        valid_flag = is_valid.astype(jnp.float32)
        totals = tuple(
            (running + valid_flag * fresh for running, fresh in zip(totals, layer_grads))
        )
        writing = (slot_ids == chosen) & is_valid
        input_grads = jnp.where(writing[:, None, None, None], grad_hidden[None], input_grads)
        if step_index < micro_count:
            returned = from_behind(grad_memory.astype(jnp.bfloat16), "section", -1).astype(
                grad_memory.dtype
            )
    group_sums = lax.psum(
        (
            totals[0],
            totals[1],
            totals[2],
            totals[3],
            totals[4],
            totals[5],
            totals[6],
            totals[7],
            totals[8],
        ),
        ("seq", "dp"),
    )
    section_sums = group_sums[:5]
    cross_sums = (
        from_root(group_sums[5].astype(jnp.bfloat16), "section", 1).astype(jnp.float32),
        from_root(group_sums[6].astype(jnp.bfloat16), "section", 1).astype(jnp.float32),
        from_root(group_sums[7].astype(jnp.bfloat16), "section", 1).astype(jnp.float32),
        from_root(group_sums[8].astype(jnp.bfloat16), "section", 1).astype(jnp.float32),
    )
    return (
        results[None],
        input_grads[None],
        section_sums[0][None],
        section_sums[1][None],
        section_sums[2][None],
        section_sums[3][None],
        section_sums[4][None],
        cross_sums[0],
        cross_sums[1],
        cross_sums[2],
        cross_sums[3],
    )


def split_rows(
    layer_input,
    segment_ids,
    attn_qkv,
    attn_out,
    ffn_in,
    ffn_out,
    norm_gain,
    cross_query,
    cross_pair,
    cross_out,
    cross_gain,
    out_cotangent,
):
    micros = layer_input.shape[1]
    length, width = layer_input.shape[3:]
    hidden = ffn_in.shape[-1]
    q_tiles = length // TILE
    group = lax.axis_size("dp") // 2
    axes = ("section", "seq", "dp")
    decoder = lax.axis_index("section") == 1
    flag = decoder.astype(jnp.int32)
    x = lax.axis_index("seq")
    core = lax.rem(lax.axis_index("dp"), 2)
    z = lax.axis_index("dp") // 2
    places = [(t, i, k, c) for t in range(2) for i in range(2) for k in range(group) for c in range(2)]

    def number(t, i, k, c):
        return ((t * 2 + i) * group + k) * 2 + c

    def send(values, target, section=None):
        route = [
            (number(*place), number(*target(*place)))
            for place in places
            if section in (None, place[0]) and target(*place)
        ]
        return lax.ppermute(values, axes, route)

    def to_core(t, i, k, c):
        return (t, i, k, 1 - c)

    def to_x(t, i, k, c):
        return (t, 1 - i, k, c)

    def to_row(t, i, k, c):
        return (t, c, k, i)

    def to_decoder(t, i, k, c):
        return (1, i, k, c) if t == 0 else None

    def to_encoder(t, i, k, c):
        return (0, i, k, c) if t == 1 else None

    def fence(values, *before):
        return lax.optimization_barrier((values,) + before)[0]

    def exchange(values):
        return send(values, to_core)

    low = ((length, width), bf16)
    wide = ((length, width), f32)
    marked = ((length + 16, width), bf16)
    both = ((2 * length, width), bf16)
    keys_all = ((2 * length, 2 * width), bf16)
    mixing = ((width, 3 * width), bf16)
    inner = ((length, hidden), bf16)
    lse = ((q_tiles, 8, 2 * TILE), f32)
    stat = ((length, LANES), f32)
    square = ((width, width), bf16)
    rising = ((width, hidden), bf16)
    falling = ((hidden, width), bf16)
    gain_rows = ((8, width), f32)

    meta = jnp.stack([flag, core, x, z]).astype(jnp.int32)
    numbers = segment_ids[0, :, 0].astype(bf16)
    padding = jnp.zeros((15, width), bf16)
    with_numbers = [
        jnp.concatenate([layer_input[0, micro, 0], numbers[micro][None], padding])
        for micro in range(micros)
    ]
    own = [send(with_numbers[0], to_row)]
    for micro in range(1, micros):
        own.append(send(fence(with_numbers[micro], own[-1]), to_row))
    other = [exchange(own[0])]

    plain = dict(meta=meta)
    small = dict(gains=norm_gain[0])
    forward, memories, memories_other = [], [], []
    for micro in range(micros):
        call = launch(
            self_forward,
            micro,
            None,
            plain,
            small,
            dict(
                x_own_h=own[micro],
                x_other_h=other[micro],
                w_mixed_h=attn_qkv[0],
                w_out_h=attn_out[0],
                w_in_h=ffn_in[0],
                w_down_h=ffn_out[0],
            ),
            dict(
                q_o=low,
                kv_o=keys_all,
                att_o=low,
                lse_o=lse,
                unit1_o=wide,
                inv1_o=stat,
                first_low_o=low,
                memory_o=marked,
                ffn_low_o=low,
                act_o=inner,
                slope_o=inner,
                unit2_o=wide,
                inv2_o=stat,
            ),
            dict(
                **attention_scratch(length, width),
                **forward_scratch(length, width),
                x=both,
                w_mixed=mixing,
                w_out=square,
                w_in=rising,
                w_down=falling,
                unit1=wide,
                inv1=stat,
                first_low=low,
                memory=marked,
                act=inner,
                slope=inner,
                unit2=wide,
                inv2=stat,
                sum=wide,
            ),
            28,
            26,
            after=(forward[0].lse_o,) if micro else (),
        )
        forward.append(call)
        memories.append(send(call.memory_o, to_decoder))
        if micro + 1 < micros:
            other.append(exchange(fence(own[micro + 1], call.lse_o)))

    for micro in range(micros):
        memories_other.append(exchange(fence(memories[micro], forward[-1].lse_o)))
    cotangent = send(fence(out_cotangent[:, 0], forward[0].lse_o), to_row)

    cross, grads_memory, made = [], [], []
    after = (forward[-1].lse_o,)
    for micro in range(micros):
        done = forward[micro]
        call = launch(
            cross_both_ways,
            micro,
            1,
            plain,
            dict(**small, cross_gain=cross_gain[None]),
            dict(
                x_own_h=own[micro],
                memory_own_h=memories[micro],
                memory_other_h=memories_other[micro],
                w_pair_h=cross_pair,
                first_low_h=done.first_low_o,
                unit1_h=done.unit1_o,
                w_query_h=cross_query,
                w_cross_h=cross_out,
                w_in_h=ffn_in[0],
                w_down_h=ffn_out[0],
                cot_h=cotangent,
            ),
            dict(
                att_o=low,
                ffn_low_o=low,
                act_o=inner,
                decoded_o=low,
                down_grad_o=low,
                up_grad_o=inner,
                gain_grads_o=gain_rows,
                branch_o=low,
                dq_low_o=low,
                dkv_o=keys_all,
                part_own_o=wide,
                part_other_o=low,
                grad_first_o=wide,
            ),
            dict(
                **attention_scratch(length, width),
                **forward_scratch(length, width),
                **backward_scratch(length, width),
                x=both,
                w_pair=((width, 2 * width), bf16),
                first_low=low,
                unit1=wide,
                w_query=square,
                w_cross=square,
                w_in=rising,
                w_down=falling,
                cot=low,
                unit2=wide,
                inv2=stat,
                second_low=low,
                act=inner,
                slope=inner,
                sum=wide,
                decoded=low,
                keep=wide,
                down_grad=low,
                up_grad=inner,
                gain_grads=gain_rows,
                branch=low,
                part_own=wide,
            ),
            36,
            44,
            dict(act_o=done.act_o, ffn_low_o=done.ffn_low_o),
            after,
        )
        cross.append(call)
        away = call.part_other_o
        if micro:
            away = fence(away, grads_memory[-1])
        total = call.part_own_o + exchange(away).astype(f32)
        made.append(total.astype(bf16))
        after = (made[micro],)
        grads_memory.append(send(made[micro], to_encoder))

    def backward_feed(micro, after):
        done, late = forward[micro], cross[micro]
        return launch(
            feed_backward_alone,
            micro,
            0,
            plain,
            dict(gains=norm_gain[0]),
            dict(
                grad_memory_h=grads_memory[micro],
                unit2_h=done.unit2_o,
                inv2_h=done.inv2_o,
                slope_h=done.slope_o,
                w_in_h=ffn_in[0],
                w_down_h=ffn_out[0],
            ),
            dict(gain_late_o=gain_rows, down_grad_o=low, up_grad_o=inner, grad_first_o=wide),
            dict(
                cot=low,
                unit2=wide,
                inv2=stat,
                slope=inner,
                w_in=rising,
                w_down=falling,
                gain_grads=gain_rows,
                keep=wide,
                down_grad=low,
                up_grad=inner,
                sum=wide,
            ),
            12,
            10,
            dict(
                down_grad_o=late.down_grad_o, up_grad_o=late.up_grad_o, grad_first_o=late.grad_first_o
            ),
            after,
        )

    def backward_self(micro, side, grad_first, previous=None, after=(), halfway=None):
        done = forward[micro]
        heads = width // LANES
        given = dict(
            x_own_h=own[micro],
            x_other_h=other[micro],
            q_h=done.q_o,
            kv_h=done.kv_o,
            att_h=done.att_o,
            lse_h=done.lse_o,
        )
        ahead = dict(
            grad_first_h=grad_first,
            unit1_h=done.unit1_o,
            inv1_h=done.inv1_o,
            w_out_h=attn_out[0],
        )
        makes = dict(dq_low_o=low, dkv_o=keys_all)
        makes_first = dict(gain_early_o=gain_rows, branch_o=low)
        makes_last = dict(part_own_o=wide, part_other_o=low)
        scratch = dict(
            **attention_scratch(length, width),
            **backward_scratch(length, width),
            w_out=square,
            w_mixed=mixing,
            unit1=wide,
            inv1=stat,
            keep=wide,
            branch=low,
            grad_att=low,
            gain_grads=gain_rows,
        )

        def part(first, last, large, outs, work, previous, after):
            return launch(
                self_backward,
                (micro, first, last),
                side,
                plain,
                small,
                dict(**given, **large),
                dict(**makes, **outs),
                scratch,
                28,
                work,
                previous,
                after,
            )

        if halfway is None:
            large = dict(**ahead, w_mixed_h=attn_qkv[0])
            outs = dict(**makes_first, **makes_last)
            return part(0, heads, large, outs, 22, previous, after)
        outs = dict(**makes_first, grad_sum_o=wide, grad_att_o=low)
        one = part(0, heads // 2, ahead, outs, 12, None, after)
        large = dict(
            w_mixed_h=attn_qkv[0],
            grad_sum_h=one.grad_sum_o,
            grad_att_h=one.grad_att_o,
            dq_h=one.dq_low_o,
            dkv_h=one.dkv_o,
        )
        two = part(heads // 2, heads, large, makes_last, 12, None, halfway(one))
        return types.SimpleNamespace(**{**vars(one), **vars(two)})

    def weight_grads(plan, side, arrays, scratch, after=()):
        blocks = ((2, width, width), bf16)
        call = launch(
            contract_blocks,
            plan,
            side,
            plain,
            dict(),
            arrays,
            dict(sent_o=blocks, kept_o=blocks),
            dict(**scratch, blocks=((4, width, width), bf16)),
            36,
            8,
            after=after,
        )
        return call.sent_o, call.kept_o

    def first_sums(halves, section=None):
        sent, kept = halves
        got = send(sent, to_core, section)

        def block(side):
            return sum(
                lax.dynamic_index_in_dim(part, side, 0, keepdims=False).astype(f32)
                for part in (kept, got)
            )

        return block(1 - x).astype(bf16), block(x)

    def middle_sums(sums, section=None):
        away, total = sums
        return (total + send(away, to_x, section).astype(f32)).astype(bf16)

    def last_sums(total, later=(), section=None):
        shares = total.reshape(group, width // group, width)

        def share(step):
            return lax.dynamic_index_in_dim(shares, lax.rem(z + step, group), 0, keepdims=False)

        parts = [share(0)]
        for step in range(1, group):
            parts.append(send(share(step), along_z(step), section))
        if later:
            parts = [fence(part, *later) for part in parts]
        return sum(part.astype(f32) for part in parts).astype(bf16)

    def along_z(step):
        return lambda t, i, k, c: (t, i, (k + step) % group, c)

    def gather_z(share):
        return [share] + [send(share, along_z(step)) for step in range(1, group)]

    def gain_block(rows):
        filled = jnp.concatenate([jnp.stack(rows), jnp.zeros((16 - len(rows), width), f32)])
        return filled.astype(bf16)

    def spread(targets, own, own_x, outs, parts):
        return launch(
            spread_pieces,
            targets,
            None,
            plain,
            dict(),
            dict(own_h=own, own_x_h=own_x, other_h=exchange(own), other_x_h=exchange(own_x)),
            outs,
            dict(
                pieces=((4,) + own.shape, bf16),
                wide=((4 * group * parts, width // group, width), f32),
            ),
            8 + 4 * group * parts,
            5,
        )

    tokens, all_tokens = micros * length, 2 * micros * length
    turn, turn_all = ((width, tokens), bf16), ((width, all_tokens), bf16)
    narrow, narrow_all = ((tokens, width), bf16), ((all_tokens, width), bf16)
    pair_all = ((all_tokens, 2 * width), bf16)
    deep = ((tokens, hidden), bf16)

    def part_of(buffer, *sources):
        return lambda column: (buffer, sources, column)

    def key_rows(buffer, sources):
        first, second = pl.ds(0, length), pl.ds(length, length)
        return part_of(buffer, *[source.at[rows] for rows in (first, second) for source in sources])

    def cross_plan(r):
        rows = pl.ds(0, length)
        low_part = part_of(r.low, r.low0_h, r.low1_h)
        att_part = part_of(r.att, r.att0_h, r.att1_h)
        dq_part = part_of(r.dq, r.dq0_h, r.dq1_h)
        branch_part = part_of(r.branch, r.branch0_h, r.branch1_h)
        sources = (r.mem0_h, r.mem1_h, r.mem2_h, r.mem3_h)
        mem_part = part_of(r.mem, *[source.at[rows] for source in sources])
        pair_part = key_rows(r.pair, (r.pair0_h, r.pair1_h))
        return [
            (r.turn, low_part(0), dq_part(0)),
            (r.turn_att, att_part(0), branch_part(0)),
            (r.turn_all, mem_part(0), pair_part(0)),
            (r.turn_all, mem_part(0), pair_part(1)),
        ]

    def rising_plan(r):
        low_part = part_of(r.low, r.low0_h, r.low1_h)
        up_part = part_of(r.up, r.up0_h, r.up1_h)
        return [(r.turn, low_part(0), up_part(block)) for block in range(4)]

    def falling_plan(r):
        act_part = part_of(r.act, r.act0_h, r.act1_h)
        down_part = part_of(r.down, r.down0_h, r.down1_h)
        return [(r.turn, act_part(block), down_part(0)) for block in range(4)]

    def self_plan(r):
        rows = pl.ds(0, length)
        sources = (r.x0_h, r.x1_h, r.x2_h, r.x3_h)
        x_part = part_of(r.x, *[source.at[rows] for source in sources])
        dq_part = part_of(r.dq, r.dq0_h, r.dq1_h)
        pair_part = key_rows(r.pair, (r.pair0_h, r.pair1_h))
        att_part = part_of(r.att, r.att0_h, r.att1_h)
        branch_part = part_of(r.branch, r.branch0_h, r.branch1_h)
        return [
            (r.turn_all, x_part(0), dq_part(0)),
            (r.turn_all, x_part(0), pair_part(0)),
            (r.turn_all, x_part(0), pair_part(1)),
            (r.turn, att_part(0), branch_part(0)),
        ]

    last = micros - 1
    feeds, ends = [None] * micros, [None] * micros
    cross_halves = weight_grads(
        cross_plan,
        1,
        dict(
            low0_h=forward[0].first_low_o,
            low1_h=forward[1].first_low_o,
            dq0_h=cross[0].dq_low_o,
            dq1_h=cross[1].dq_low_o,
            att0_h=cross[0].att_o,
            att1_h=cross[1].att_o,
            branch0_h=cross[0].branch_o,
            branch1_h=cross[1].branch_o,
            mem0_h=memories[0],
            mem1_h=memories[1],
            mem2_h=memories_other[0],
            mem3_h=memories_other[1],
            pair0_h=cross[0].dkv_o,
            pair1_h=cross[1].dkv_o,
        ),
        dict(
            low=narrow,
            dq=narrow,
            att=narrow,
            branch=narrow,
            mem=narrow_all,
            pair=pair_all,
            turn=turn,
            turn_att=turn,
            turn_all=turn_all,
        ),
        (made[last],),
    )
    cross_sums = first_sums(cross_halves, 1)
    results = jnp.stack(
        [
            jnp.where(decoder, call.decoded_o, done.memory_o[:length])
            for call, done in zip(cross, forward)
        ]
    )
    results = send(results, to_row)
    latest = made[last]

    def part_sum(micro, *before):
        end = ends[micro]
        away = fence(end.part_other_o, *before)
        total = (end.part_own_o + exchange(away).astype(f32)).astype(bf16)
        return total, send(total, to_row)

    steps = []
    for micro in range(last):
        feeds[micro] = backward_feed(micro, (latest,))
        first = feeds[micro].grad_first_o
        ends[micro] = backward_self(micro, 0, first)
        ends[micro] = backward_self(micro, 1, first, vars(ends[micro]), (cross_sums[0], grads_memory[last]))
        cross_total = middle_sums(cross_sums, 1)
        steps.append(part_sum(micro, cross_total))
        latest = ends[micro].gain_early_o
    feeds[last] = backward_feed(last, (latest,))

    rising_halves = weight_grads(
        rising_plan,
        None,
        dict(
            low0_h=cross[0].ffn_low_o,
            low1_h=cross[1].ffn_low_o,
            up0_h=feeds[0].up_grad_o,
            up1_h=feeds[1].up_grad_o,
        ),
        dict(low=narrow, up=deep, turn=turn),
        (results,) + tuple(step[0] for step in steps),
    )
    cross_share = last_sums(cross_total, (rising_halves[0],), 1)
    third = sum(call.gain_grads_o[1] for call in cross)
    cross_share = jnp.concatenate([cross_share, gain_block([third])])
    rising_sums = first_sums((fence(rising_halves[0], cross_share), rising_halves[1]))
    rising_total = middle_sums(rising_sums)
    falling_halves = weight_grads(
        falling_plan,
        None,
        dict(
            act0_h=cross[0].act_o,
            act1_h=cross[1].act_o,
            down0_h=feeds[0].down_grad_o,
            down1_h=feeds[1].down_grad_o,
        ),
        dict(act=deep, down=narrow, turn=turn),
        (rising_sums[0],) + tuple(step[1] for step in steps),
    )
    cross_sent = send(cross_share, to_encoder)
    falling_sent = fence(falling_halves[0], rising_total)
    falling_sums = first_sums((falling_sent, falling_halves[1]))
    falling_total = middle_sums(falling_sums)
    shares = []

    def halfway(one):
        shares.append(last_sums(rising_total, (one.gain_early_o,)))
        shares.append(jnp.where(decoder, cross_share, fence(cross_sent, one.gain_early_o)))
        return (*shares, falling_total)

    ends[last] = backward_self(
        last,
        None,
        feeds[last].grad_first_o,
        None,
        (falling_sums[0],),
        halfway,
    )
    falling_share = last_sums(falling_total, (ends[last].gain_early_o, ends[last].part_own_o))
    one_own = gather_z(jnp.concatenate([shares[0], falling_share, shares[1]]))
    steps.append(part_sum(last, falling_share))

    self_halves = weight_grads(
        self_plan,
        None,
        dict(
            x0_h=own[0],
            x1_h=own[1],
            x2_h=other[0],
            x3_h=other[1],
            dq0_h=ends[0].dq_low_o,
            dq1_h=ends[1].dq_low_o,
            pair0_h=ends[0].dkv_o,
            pair1_h=ends[1].dkv_o,
            att0_h=forward[0].att_o,
            att1_h=forward[1].att_o,
            branch0_h=ends[0].branch_o,
            branch1_h=ends[1].branch_o,
        ),
        dict(
            x=narrow_all,
            dq=narrow,
            pair=pair_all,
            att=narrow,
            branch=narrow,
            turn=turn,
            turn_all=turn_all,
        ),
        (steps[last][0],),
    )
    away, total = first_sums(
        (fence(self_halves[0], one_own[1], one_own[-1], steps[last][1]), self_halves[1])
    )
    one_own = jnp.stack(one_own)
    self_total = middle_sums((away, total))
    self_share = last_sums(self_total)
    one_own_x = send(fence(one_own, self_total), to_x)

    early = sum(end.gain_early_o[0] for end in ends)
    late = jnp.where(
        decoder,
        sum(call.gain_grads_o[0] for call in cross),
        sum(call.gain_late_o[0] for call in feeds),
    )
    two_own = jnp.stack(
        gather_z(jnp.concatenate([self_share, gain_block([early, late])]))
    )
    two_own_x = send(fence(two_own, one_own_x), to_x)

    def columns(block):
        return pl.ds(block * width, width)

    def one_targets(r, block, row, rows):
        lines = pl.ds(row, rows)
        feed = [r.up_o.at[lines, columns(block)], r.down_o.at[pl.ds(block * width + row, rows)]]
        if block >= 2:
            return feed + [r.pair_o.at[lines, columns(block - 2)]]
        return feed + [(r.out_o if block else r.query_o).at[lines]]

    def two_targets(r, block, row, rows):
        lines = pl.ds(row, rows)
        return [r.out_o.at[lines] if block == 3 else r.mixed_o.at[lines, columns(block)]]

    square_out = ((width, width), f32)
    one_own_x = fence(one_own_x, two_own)
    one_grads = spread(
        one_targets,
        one_own,
        one_own_x,
        dict(
            up_o=((width, hidden), f32),
            query_o=square_out,
            pair_o=((width, 2 * width), f32),
            down_o=((hidden, width), f32),
            out_o=square_out,
            gains_o=((1, width), f32),
        ),
        3,
    )
    two_own_x = fence(two_own_x, one_grads.gains_o)
    two_grads = spread(
        two_targets,
        two_own,
        two_own_x,
        dict(
            mixed_o=((width, 3 * width), f32),
            out_o=square_out,
            gains_o=((2, width), f32),
        ),
        1,
    )

    grad_input = jnp.stack([step[1] for step in steps])
    return (
        results[None, :, None],
        grad_input.astype(f32)[None, :, None],
        two_grads.mixed_o[None],
        two_grads.out_o[None],
        one_grads.up_o[None],
        one_grads.down_o[None],
        two_grads.gains_o[None],
        one_grads.query_o,
        one_grads.pair_o,
        one_grads.out_o,
        one_grads.gains_o[0],
    )


def shards(*arrays):
    layer_input = arrays[0]
    micros, rows, length = layer_input.shape[1:4]
    simple = (
        lax.axis_size("section") == 2
        and lax.axis_size("seq") == 2
        and lax.axis_size("dp") in (4, 8, 16)
        and (micros, rows) == (2, 1)
        and length == layer_input.shape[-1] == CHUNK
        and arrays[4].shape[-1] == 4 * CHUNK
    )
    return split_rows(*arrays) if simple else any_rows(*arrays)


def solution(mesh):
    in_specs = (
        P("section", None, "dp", "seq", None),
        P("section", None, "dp", "seq"),
        P("section", None, None),
        P("section", None, None),
        P("section", None, None),
        P("section", None, None),
        P("section", None, None),
        P(),
        P(),
        P(),
        P(),
        P(None, "dp", "seq", None),
    )
    out_specs = (
        P("section", None, "dp", "seq", None),
        P("section", None, "dp", "seq", None),
        P("section", None, None),
        P("section", None, None),
        P("section", None, None),
        P("section", None, None),
        P("section", None, None),
        P(),
        P(),
        P(),
        P(),
    )
    return jax.shard_map(shards, mesh=mesh, in_specs=in_specs, out_specs=out_specs, check_vma=False)
```

```python
import types

import jax
import jax.numpy as jnp
from jax import lax
from jax.experimental import pallas as pl
from jax.experimental.pallas import tpu as pltpu
from jax.sharding import PartitionSpec as P

HEADS = 8
TILE = 256
LANES = 128
CHUNK = 512

f32 = jnp.float32
bf16 = jnp.bfloat16
negative_big = -1e30
epsilon = 1e-05


def dot(left, right):
    return lax.dot_general(left, right, (((1,), (0,)), ((), ())), preferred_element_type=f32)


def dot_nt(left, right):
    return lax.dot_general(left, right, (((1,), (1,)), ((), ())), preferred_element_type=f32)


def dot_tn(left, right):
    return lax.dot_general(left, right, (((0,), (0,)), ((), ())), preferred_element_type=f32)


def standardize(values):
    center = values - jnp.mean(values, axis=-1, keepdims=True)
    inverse = lax.rsqrt(jnp.mean(center * center, axis=-1, keepdims=True) + epsilon)
    return center * inverse, inverse


def standardize_back(grad_out, standard, gain_row, inverse):
    scaled = grad_out * gain_row
    grad_in = inverse * (
        scaled
        - jnp.mean(scaled, axis=-1, keepdims=True)
        - standard * jnp.mean(scaled * standard, axis=-1, keepdims=True)
    )
    return grad_in, jnp.sum(grad_out * standard, axis=0, keepdims=True)


class Copies:
    def __init__(self, sems):
        self.sems = sems
        self.used = 0

    def start(self, source, target):
        copy = pltpu.make_async_copy(source, target, self.sems.at[self.used])
        self.used += 1
        copy.start()
        return copy


def wait_all(copies):
    for copy in copies:
        copy.wait()


def spread_pairs(target, source, factor, pairs):
    tiles = target.shape[1]
    half = lax.broadcasted_iota(jnp.int32, (TILE, LANES), 1) < LANES // 2
    first = jnp.where(half, factor, 0.0).astype(bf16)
    second = jnp.where(half, 0.0, factor).astype(bf16)
    for tile in range(tiles):
        for pair in pairs:
            block = source[tile * TILE : (tile + 1) * TILE, pair * LANES : (pair + 1) * LANES]
            target[pair, tile, :TILE, :] = block * first
            target[pair, tile, TILE:, :] = block * second


def turn_tiles(target, source, column, pairs):
    low, high = pairs[0] * LANES, (pairs[-1] + 1) * LANES
    for tile in range(target.shape[0]):
        block = source[tile * TILE : (tile + 1) * TILE, column + low : column + high]
        target[tile, low:high, :] = jnp.transpose(block)


def place_documents(r, copies):
    wait_all(copies)
    q_tiles = r.qd.shape[0]
    for part in range(3):
        row = r.docs[part].astype(f32)[0:1, :]
        for tile in range(q_tiles):
            piece = row[:, tile * TILE : (tile + 1) * TILE]
            slot = part * q_tiles + tile
            r.bounds[0, slot] = jnp.min(piece).astype(jnp.int32)
            r.bounds[1, slot] = jnp.max(piece).astype(jnp.int32)
            if part == 0:
                r.qd[tile] = jnp.broadcast_to(piece, (8, TILE))
        if part > 0:
            for start in range(0, row.shape[1], LANES):
                block = jnp.broadcast_to(row[:, start : start + LANES], (LANES, LANES))
                place = (part - 1) * row.shape[1] + start
                r.kdc[place : place + LANES, :] = jnp.transpose(block)


def load_documents(r, move, queries, own, other):
    rows = pl.ds(r.docs.shape[2], r.docs.shape[1])
    return [
        move.start(source.at[rows], r.docs.at[part])
        for part, source in enumerate((queries, own, other))
    ]


def tile_place(r, core, causal, q_tile, k_tile):
    q_tiles = r.qd.shape[0]
    length = q_tiles * TILE
    owner = jnp.where(k_tile < q_tiles, core, 1 - core)
    k_start = owner * length + lax.rem(k_tile, q_tiles) * TILE
    ahead = core * length + q_tile * TILE - k_start
    ahead = jnp.where(causal == 1, ahead, 2 * length * TILE)
    q_low, q_high = r.bounds[0, q_tile], r.bounds[1, q_tile]
    k_low, k_high = r.bounds[0, q_tiles + k_tile], r.bounds[1, q_tiles + k_tile]
    active = (q_low <= k_high) & (k_low <= q_high) & (ahead > -TILE)
    whole = (q_low == k_high) & (k_low == q_high) & (ahead >= TILE)
    return active, whole, ahead


def each_tile(place, body):
    active, whole, ahead = place
    pl.when(active & jnp.logical_not(whole))(lambda: body(ahead))
    pl.when(whole)(lambda: body(None))


def fill_bias(r, q_tile, k_tile, ahead):
    keys = r.kdc[pl.ds(pl.multiple_of(k_tile * TILE, TILE), TILE), :]
    shift = lax.broadcasted_iota(jnp.int32, (TILE, LANES), 0) - lax.broadcasted_iota(
        jnp.int32, (TILE, LANES), 1
    )
    queries = r.qd[q_tile]
    for start in range(0, TILE, LANES):
        same = keys == queries[0:1, start : start + LANES]
        allowed = same & (shift - start <= ahead)
        r.bias[:, start : start + LANES] = jnp.where(allowed, 0.0, negative_big)


def attention_forward(r, core, causal):
    pairs, q_tiles = r.qm.shape[:2]
    k_tiles = r.vt.shape[0]

    def one_query_tile(q_tile, carry):
        r.top[...] = jnp.full(r.top.shape, negative_big, f32)
        r.total[...] = jnp.zeros(r.total.shape, f32)
        r.turned[...] = jnp.zeros(r.turned.shape, f32)

        def one_key_tile(k_tile, inner):
            def one_tile(ahead):
                if ahead is not None:
                    fill_bias(r, q_tile, k_tile, ahead)
                rows = pl.ds(pl.multiple_of(k_tile * TILE, TILE), TILE)

                def raw(pair):
                    keys = r.kv[rows, pair * LANES : (pair + 1) * LANES]
                    return dot_nt(keys, r.qm[pair, q_tile])

                raw_next = raw(0)
                for pair in range(pairs):
                    scores = raw_next
                    if ahead is not None:
                        bias = r.bias[...]
                        scores = scores + jnp.concatenate([bias, bias], axis=1)
                    if pair + 1 < pairs:
                        raw_next = raw(pair + 1)
                    old_top = r.top[pair : pair + 1, :]
                    new_top = jnp.maximum(old_top, jnp.max(scores, axis=0, keepdims=True))
                    weights = jnp.exp(scores - new_top)
                    shrink = jnp.exp(old_top - new_top)
                    r.top[pair : pair + 1, :] = new_top
                    r.total[pair : pair + 1, :] = r.total[
                        pair : pair + 1, :
                    ] * shrink + jnp.sum(weights, axis=0, keepdims=True)
                    low = weights.astype(bf16)
                    for side in range(2):
                        span = slice(side * TILE, (side + 1) * TILE)
                        head = slice((2 * pair + side) * 64, (2 * pair + side + 1) * 64)
                        r.turned[head, :] = r.turned[head, :] * shrink[:, span] + dot(
                            r.vt[k_tile, head, :], low[:, span]
                        )

            each_tile(tile_place(r, core, causal, q_tile, k_tile), one_tile)
            return inner

        lax.fori_loop(0, k_tiles, one_key_tile, 0)
        for pair in range(pairs):
            total = r.total[pair : pair + 1, :]
            r.lse[q_tile, pair : pair + 1, :] = r.top[pair : pair + 1, :] + jnp.log(total)
            share = 1.0 / total
            for side in range(2):
                span = slice(side * TILE, (side + 1) * TILE)
                head = slice((2 * pair + side) * 64, (2 * pair + side + 1) * 64)
                r.turned[head, :] = r.turned[head, :] * share[:, span]
        rows = pl.ds(pl.multiple_of(q_tile * TILE, TILE), TILE)
        r.att[rows, :] = jnp.transpose(r.turned[...]).astype(bf16)
        return carry

    lax.fori_loop(0, q_tiles, one_query_tile, 0)


def row_products(r, grad_att, pairs):
    low, high = pairs[0] * LANES, (pairs[-1] + 1) * LANES
    for tile in range(r.qm.shape[1]):
        rows = slice(tile * TILE, (tile + 1) * TILE)
        product = jnp.transpose(
            grad_att[rows, low:high].astype(f32) * r.att[rows, low:high].astype(f32)
        )
        for pair in pairs:
            for side in range(2):
                head = (2 * pair + side) * 64 - low
                r.delta[tile, pair : pair + 1, side * TILE : (side + 1) * TILE] = jnp.sum(
                    product[head : head + 64, :], axis=0, keepdims=True
                )


def attention_backward(r, core, causal, pairs):
    q_tiles, k_tiles = r.qm.shape[1], r.kt.shape[0]
    width = r.kt.shape[1]
    low, high = pairs[0] * LANES, (pairs[-1] + 1) * LANES
    for start in (0, width):
        r.dkv[:, start + low : start + high] = jnp.zeros((r.dkv.shape[0], high - low), f32)

    def one_query_tile(q_tile, carry):
        r.turned[low:high, :] = jnp.zeros((high - low, TILE), f32)

        def one_key_tile(k_tile, inner):
            def one_tile(ahead):
                if ahead is not None:
                    fill_bias(r, q_tile, k_tile, ahead)
                rows = pl.ds(pl.multiple_of(k_tile * TILE, TILE), TILE)

                def raw(pair):
                    lanes = slice(pair * LANES, (pair + 1) * LANES)
                    lanes_v = slice(width + pair * LANES, width + (pair + 1) * LANES)
                    return (
                        dot_nt(r.kv[rows, lanes], r.qm[pair, q_tile]),
                        dot_nt(r.kv[rows, lanes_v], r.gm[pair, q_tile]),
                    )

                raw_next = raw(pairs[0])
                for pair in pairs:
                    scores, grad_probs = raw_next
                    if ahead is not None:
                        bias = r.bias[...]
                        scores = scores + jnp.concatenate([bias, bias], axis=1)
                    if pair < pairs[-1]:
                        raw_next = raw(pair + 1)
                    probs = jnp.exp(scores - r.lse[q_tile, pair : pair + 1, :])
                    grad_scores = probs * (grad_probs - r.delta[q_tile, pair : pair + 1, :])
                    probs_low = probs.astype(bf16)
                    grad_low = grad_scores.astype(bf16)
                    lanes = slice(pair * LANES, (pair + 1) * LANES)
                    lanes_v = slice(width + pair * LANES, width + (pair + 1) * LANES)
                    r.dkv[rows, lanes] += dot(grad_low, r.qm[pair, q_tile])
                    r.dkv[rows, lanes_v] += dot(probs_low, r.gm[pair, q_tile])
                    for side in range(2):
                        span = slice(side * TILE, (side + 1) * TILE)
                        head = slice((2 * pair + side) * 64, (2 * pair + side + 1) * 64)
                        r.turned[head, :] += dot(r.kt[k_tile, head, :], grad_low[:, span])

            each_tile(tile_place(r, core, causal, q_tile, k_tile), one_tile)
            return inner

        lax.fori_loop(0, k_tiles, one_key_tile, 0)
        rows = pl.ds(pl.multiple_of(q_tile * TILE, TILE), TILE)
        r.dq[rows, low:high] = jnp.transpose(r.turned[low:high, :]) * (64**-0.5)
        return carry

    lax.fori_loop(0, q_tiles, one_query_tile, 0)


def feed_forward(r, low):
    chunks = [slice(at, at + CHUNK) for at in range(0, r.w_in.shape[1], CHUNK)]
    upward_next = dot(low[...], r.w_in[:, chunks[0]])
    for place, span in enumerate(chunks):
        upward = upward_next
        if place + 1 < len(chunks):
            upward_next = dot(low[...], r.w_in[:, chunks[place + 1]])
        gate = jax.nn.sigmoid(upward)
        active = (upward * gate).astype(bf16)
        r.act[:, span] = active
        r.slope[:, span] = (gate + upward * gate * (1.0 - gate)).astype(r.slope.dtype)
        part = dot(active, r.w_down[span, :])
        if place:
            r.sum[...] += part
        else:
            r.sum[...] = part


def feed_backward(r):
    chunks = [slice(at, at + CHUNK) for at in range(0, r.w_in.shape[1], CHUNK)]
    active_next = dot_nt(r.down_grad[...], r.w_down[chunks[0], :])
    for place, span in enumerate(chunks):
        grad_active = active_next.astype(bf16)
        if place + 1 < len(chunks):
            active_next = dot_nt(r.down_grad[...], r.w_down[chunks[place + 1], :])
        grad_up = (grad_active.astype(f32) * r.slope[:, span].astype(f32)).astype(bf16)
        r.up_grad[:, span] = grad_up
        part = dot_nt(grad_up, r.w_in[:, span])
        if place:
            r.sum[...] += part
        else:
            r.sum[...] = part


def self_forward(r):
    length, width = r.unit1.shape
    decoder, core = r.meta[0], r.meta[1]
    move = Copies(r.sems)
    whole = pl.ds(0, length)
    documents = load_documents(r, move, r.x_own_h, r.x_own_h, r.x_other_h)
    early = [
        move.start(r.x_own_h.at[whole], r.x.at[whole]),
        move.start(r.x_other_h.at[whole], r.x.at[pl.ds(length, length)]),
        move.start(r.w_mixed_h, r.w_mixed),
    ]
    later = [
        move.start(r.w_out_h, r.w_out),
        move.start(r.w_in_h, r.w_in),
        move.start(r.w_down_h, r.w_down),
    ]
    place_documents(r, documents)
    wait_all(early)
    r.q[...] = dot(r.x[:length, :], r.w_mixed[:, :width]).astype(bf16)
    r.kv[...] = dot(r.x[...], r.w_mixed[:, width:]).astype(bf16)
    outs = [move.start(r.q, r.q_o), move.start(r.kv, r.kv_o)]
    pairs = range(width // LANES)
    spread_pairs(r.qm, r.q, 64**-0.5, pairs)
    turn_tiles(r.vt, r.kv, width, pairs)
    attention_forward(r, core, decoder)
    wait_all(later)
    outs += [move.start(r.att, r.att_o), move.start(r.lse, r.lse_o)]
    unit, inverse = standardize(r.x[:length, :].astype(f32) + dot(r.att[...], r.w_out[...]))
    r.unit1[...] = unit
    r.inv1[...] = jnp.broadcast_to(inverse, r.inv1.shape)
    r.first_low[...] = (unit * r.gains[0:1, :]).astype(bf16)
    outs += [
        move.start(r.unit1, r.unit1_o),
        move.start(r.inv1, r.inv1_o),
        move.start(r.first_low, r.first_low_o),
    ]

    @pl.when(decoder == 0)
    def _():
        feed_forward(r, r.first_low)
        late = [
            move.start(r.first_low, r.ffn_low_o),
            move.start(r.act, r.act_o),
            move.start(r.slope, r.slope_o),
        ]
        unit2, inverse2 = standardize(r.unit1[...] * r.gains[0:1, :] + r.sum[...])
        r.memory[:length, :] = (unit2 * r.gains[1:2, :]).astype(bf16)
        r.memory[length:, :] = r.docs[0]
        late += [move.start(r.memory, r.memory_o)]
        r.unit2[...] = unit2
        r.inv2[...] = jnp.broadcast_to(inverse2, r.inv2.shape)
        late += [move.start(r.unit2, r.unit2_o), move.start(r.inv2, r.inv2_o)]
        wait_all(late)

    wait_all(outs)


def cross_both_ways(r):
    length, width = r.unit1_h.shape
    core = r.meta[1]
    move = Copies(r.sems)
    whole = pl.ds(0, length)
    documents = load_documents(r, move, r.x_own_h, r.memory_own_h, r.memory_other_h)
    moves = [
        move.start(r.memory_own_h.at[whole], r.x.at[whole]),
        move.start(r.memory_other_h.at[whole], r.x.at[pl.ds(length, length)]),
        move.start(r.w_pair_h, r.w_pair),
        move.start(r.first_low_h, r.first_low),
        move.start(r.w_query_h, r.w_query),
    ]
    later = [
        move.start(r.unit1_h, r.unit1),
        move.start(r.w_cross_h, r.w_cross),
        move.start(r.w_in_h, r.w_in),
        move.start(r.w_down_h, r.w_down),
        move.start(r.cot_h.at[r.micro], r.cot),
    ]
    place_documents(r, documents)
    wait_all(moves)
    r.kv[...] = dot(r.x[...], r.w_pair[...]).astype(bf16)
    r.q[...] = dot(r.first_low[...], r.w_query[...]).astype(bf16)
    pairs = range(width // LANES)
    spread_pairs(r.qm, r.q, 64**-0.5, pairs)
    turn_tiles(r.vt, r.kv, width, pairs)
    turn_tiles(r.kt, r.kv, 0, pairs)
    attention_forward(r, core, 0)
    outs = [move.start(r.att, r.att_o)]
    wait_all(later)
    first = r.unit1[...] * r.gains[0:1, :]
    unit, inverse = standardize(first + dot(r.att[...], r.w_cross[...]))
    r.unit2[...] = unit
    r.inv2[...] = jnp.broadcast_to(inverse, r.inv2.shape)
    r.second_low[...] = (unit * r.cross_gain[...]).astype(bf16)
    outs += [move.start(r.second_low, r.ffn_low_o)]
    feed_forward(r, r.second_low)
    outs += [move.start(r.act, r.act_o)]
    unit3, inverse3 = standardize(r.unit2[...] * r.cross_gain[...] + r.sum[...])
    r.decoded[...] = (unit3 * r.gains[1:2, :]).astype(bf16)
    outs += [move.start(r.decoded, r.decoded_o)]
    grad_third, gain_late = standardize_back(
        r.cot[...].astype(f32), unit3, r.gains[1:2, :], inverse3
    )
    r.keep[...] = grad_third
    r.down_grad[...] = grad_third.astype(bf16)
    outs += [move.start(r.down_grad, r.down_grad_o)]
    feed_backward(r)
    outs += [move.start(r.up_grad, r.up_grad_o)]
    grad_sum, gain_cross = standardize_back(
        r.keep[...] + r.sum[...], r.unit2[...], r.cross_gain[...], r.inv2[:, 0:1]
    )
    r.gain_grads[...] = jnp.zeros(r.gain_grads.shape, f32)
    r.gain_grads[0:1, :] = gain_late
    r.gain_grads[1:2, :] = gain_cross
    r.keep[...] = grad_sum
    r.branch[...] = grad_sum.astype(bf16)
    outs += [move.start(r.gain_grads, r.gain_grads_o), move.start(r.branch, r.branch_o)]
    r.q[...] = dot_nt(r.branch[...], r.w_cross[...]).astype(bf16)
    spread_pairs(r.gm, r.q, 1.0, pairs)
    row_products(r, r.q, pairs)
    attention_backward(r, core, 0, pairs)
    r.dq_low[...] = r.dq[...].astype(bf16)
    r.keep[...] += dot_nt(r.dq_low[...], r.w_query[...])
    outs += [move.start(r.dq_low, r.dq_low_o), move.start(r.keep, r.grad_first_o)]
    r.dkv_low[...] = r.dkv[...].astype(bf16)
    outs += [move.start(r.dkv_low, r.dkv_o)]
    part = dot_nt(r.dkv_low[...], r.w_pair[...])
    r.part_other[...] = part[length:, :].astype(bf16)
    r.part_own[...] = part[:length, :]
    outs += [move.start(r.part_other, r.part_other_o), move.start(r.part_own, r.part_own_o)]
    wait_all(outs)


def feed_backward_alone(r):
    move = Copies(r.sems)
    early = [
        move.start(r.grad_memory_h, r.cot),
        move.start(r.unit2_h, r.unit2),
        move.start(r.inv2_h, r.inv2),
    ]
    later = [
        move.start(r.w_down_h, r.w_down),
        move.start(r.slope_h, r.slope),
        move.start(r.w_in_h, r.w_in),
    ]
    wait_all(early)
    grad_third, gain_late = standardize_back(
        r.cot[...].astype(f32), r.unit2[...], r.gains[1:2, :], r.inv2[:, 0:1]
    )
    r.gain_grads[...] = jnp.broadcast_to(gain_late, r.gain_grads.shape)
    r.keep[...] = grad_third
    r.down_grad[...] = grad_third.astype(bf16)
    outs = [move.start(r.down_grad, r.down_grad_o), move.start(r.gain_grads, r.gain_late_o)]
    wait_all(later)
    feed_backward(r)
    outs += [move.start(r.up_grad, r.up_grad_o)]
    r.keep[...] += r.sum[...]
    outs += [move.start(r.keep, r.grad_first_o)]
    wait_all(outs)


def self_backward(r, plan):
    r.micro, first, last = plan
    length, width = r.att_h.shape
    decoder, core = r.meta[0], r.meta[1]
    pairs = range(first, last)
    low, high = first * LANES, last * LANES
    move = Copies(r.sems)
    later = [
        move.start(r.q_h, r.q),
        move.start(r.kv_h, r.kv),
        move.start(r.att_h, r.att),
        move.start(r.lse_h, r.lse),
    ]
    if first == 0:
        early = [
            move.start(r.grad_first_h, r.keep),
            move.start(r.unit1_h, r.unit1),
            move.start(r.inv1_h, r.inv1),
            move.start(r.w_out_h, r.w_out),
        ]
    else:
        early = [move.start(r.grad_att_h, r.grad_att)]
    outs = []
    place_documents(r, load_documents(r, move, r.x_own_h, r.x_own_h, r.x_other_h))
    wait_all(early)
    if first == 0:
        grad_sum, gain_early = standardize_back(
            r.keep[...], r.unit1[...], r.gains[0:1, :], r.inv1[:, 0:1]
        )
        r.gain_grads[...] = jnp.broadcast_to(gain_early, r.gain_grads.shape)
        r.keep[...] = grad_sum
        r.branch[...] = grad_sum.astype(bf16)
        r.grad_att[...] = dot_nt(r.branch[...], r.w_out[...]).astype(bf16)
        outs += [move.start(r.gain_grads, r.gain_early_o), move.start(r.branch, r.branch_o)]
        if last < width // LANES:
            outs += [move.start(r.keep, r.grad_sum_o), move.start(r.grad_att, r.grad_att_o)]
    wait_all(later)
    if last == width // LANES:
        ends = [move.start(r.w_mixed_h, r.w_mixed)]
        if first > 0:
            ends += [
                move.start(r.grad_sum_h, r.keep),
                move.start(r.dq_h.at[:, pl.ds(0, low)], r.dq_low.at[:, pl.ds(0, low)]),
                move.start(r.dkv_h.at[:, pl.ds(0, low)], r.dkv_low.at[:, pl.ds(0, low)]),
                move.start(
                    r.dkv_h.at[:, pl.ds(width, low)], r.dkv_low.at[:, pl.ds(width, low)]
                ),
            ]
    spread_pairs(r.qm, r.q, 64**-0.5, pairs)
    turn_tiles(r.kt, r.kv, 0, pairs)
    spread_pairs(r.gm, r.grad_att, 1.0, pairs)
    row_products(r, r.grad_att, pairs)
    attention_backward(r, core, decoder, pairs)
    r.dq_low[:, low:high] = r.dq[:, low:high].astype(bf16)
    for start in (0, width):
        span = slice(start + low, start + high)
        r.dkv_low[:, span] = r.dkv[:, span].astype(bf16)
    if last == width // LANES:
        wait_all(ends)
        outs += [move.start(r.dq_low, r.dq_low_o), move.start(r.dkv_low, r.dkv_o)]
        r.keep[...] += dot_nt(r.dq_low[...], r.w_mixed[:, :width])
        part = dot_nt(r.dkv_low[...], r.w_mixed[:, width:])
        r.part_other[...] = part[length:, :].astype(bf16)
        r.keep[...] += part[:length, :]
        outs += [move.start(r.part_other, r.part_other_o), move.start(r.keep, r.part_own_o)]
    else:
        outs.append(move.start(r.dq_low.at[:, pl.ds(low, high - low)], r.dq_low_o.at[:, pl.ds(low, high - low)]))
        for start in (0, width):
            span = pl.ds(start + low, high - low)
            outs.append(move.start(r.dkv_low.at[:, span], r.dkv_o.at[:, span]))
    wait_all(outs)


def contract_blocks(r, plan):
    for core in range(2):

        @pl.when(r.meta[1] == core)
        def _(core=core):
            targets = [None] * 4
            for half in range(2):
                target = r.kept_o if half == core else r.sent_o
                targets[2 * half], targets[2 * half + 1] = target.at[0], target.at[1]
            order = (0, 1, 2, 3) if core else (2, 3, 0, 1)
            contract_in_order(r, plan(r), order, targets, Copies(r.sems))


def contract_in_order(r, blocks, order, targets, move):
    loads = dict()
    for slot in order:
        for buffer, sources, at in blocks[slot][1:]:
            span = pl.ds(at * CHUNK, CHUNK)
            if buffer.shape[1] == 4 * CHUNK:
                at, span = 0, pl.ds(0, 4 * CHUNK)
            if (id(buffer), at) not in loads:
                row = 0
                copies = []
                for source in sources:
                    rows = pl.ds(row, source.shape[0])
                    copies.append(move.start(source.at[:, span], buffer.at[rows, span]))
                    row += source.shape[0]
                loads[id(buffer), at] = copies
    outs = []
    held = dict()
    for slot in order:
        turn, (left, _, left_at), (right, _, right_at) = blocks[slot]
        for buffer, at in ((left, left_at), (right, right_at)):
            at = 0 if buffer.shape[1] == 4 * CHUNK else at
            wait_all(loads.pop((id(buffer), at), ()))
        if held.get(id(turn)) != left_at:
            for row in range(0, left.shape[0], CHUNK):
                block = left[row : row + CHUNK, left_at * CHUNK : (left_at + 1) * CHUNK]
                turn[:, row : row + CHUNK] = jnp.transpose(block)
            held[id(turn)] = left_at
        block = right[:, right_at * CHUNK : (right_at + 1) * CHUNK]
        r.blocks[slot] = dot(turn[:, : right.shape[0]], block).astype(bf16)
        outs.append(move.start(r.blocks.at[slot], targets[slot]))
    wait_all(outs)


def spread_pieces(r, targets):
    z = r.meta[3]
    group, height = r.own_h.shape[:2]
    rows = r.own_h.shape[2] // group
    for core in range(2):
        for x in range(2):

            @pl.when((r.meta[1] == core) & (r.meta[2] == x))
            def _(core=core, x=x):
                move = Copies(r.sems)
                parts = [
                    (r.own_h, core, x),
                    (r.own_x_h, core, 1 - x),
                    (r.other_h, 1 - core, x),
                    (r.other_x_h, 1 - core, 1 - x),
                ]
                loads = [
                    move.start(source, r.pieces.at[place])
                    for place, (source, _, _) in enumerate(parts)
                ]
                outs = []
                slot = 0
                gains = []
                for place, (_, half, side) in enumerate(parts):
                    loads[place].wait()
                    for step in range(group):
                        row = pl.multiple_of(lax.rem(z + (group - step), group) * rows, rows)
                        start = 0
                        for target in targets(r, 2 * half + side, row, rows):
                            r.wide[slot] = r.pieces[place, step, start : start + rows].astype(f32)
                            outs.append(move.start(r.wide.at[slot], target))
                            slot += 1
                            start += rows
                        if start < height:
                            gains.append(r.pieces[place, step, start:height].astype(f32))
                if gains:
                    gains = sum(gains)
                    r.gains_o[0:2, :] = gains[16:18, :]
                    r.gains_o[2:3, :] = gains[0:1, :]
                wait_all(outs)


def launch(kernel, plan, side, scalars, small, large, outs, scratch, copies, work, previous=None, after=()):
    names = list(scalars) + list(small) + list(large)
    arrays = list(scalars.values()) + list(small.values()) + list(large.values())
    specs = (
        [pl.BlockSpec(memory_space=pltpu.SMEM)] * len(scalars)
        + [pl.BlockSpec(memory_space=pltpu.VMEM)] * len(small)
        + [pl.BlockSpec(memory_space=pl.ANY)] * len(large)
    )
    aliases = dict()
    for position, name in enumerate(outs):
        if previous and name in previous:
            aliases[len(arrays)] = position
            names.append("previous_" + name)
            arrays.append(previous[name])
            specs.append(pl.BlockSpec(memory_space=pl.ANY))
    for array in after:
        names.append("")
        arrays.append(array)
        specs.append(pl.BlockSpec(memory_space=pl.ANY))
    names += list(outs) + list(scratch) + ["sems"]

    def body(*refs):
        r = types.SimpleNamespace(**dict(zip(names, refs)))

        def run():
            if isinstance(plan, int):
                r.micro = plan
                kernel(r)
            else:
                kernel(r, plan)

        if side is None:
            run()
        else:
            pl.when(r.meta[0] == side)(run)

    results = pl.pallas_call(
        body,
        out_shape=[jax.ShapeDtypeStruct(*shape) for shape in outs.values()],
        in_specs=specs,
        out_specs=[
            pl.BlockSpec(memory_space=pltpu.VMEM if shape[0][0] < 8 else pl.ANY)
            for shape in outs.values()
        ],
        scratch_shapes=[
            pltpu.SMEM(*shape) if shape[1] == jnp.int32 else pltpu.VMEM(*shape)
            for shape in scratch.values()
        ]
        + [pltpu.SemaphoreType.DMA((copies,))],
        input_output_aliases=aliases,
        compiler_params=pltpu.CompilerParams(vmem_limit_bytes=58 * 1024 * 1024),
        cost_estimate=pl.CostEstimate(
            flops=work * 10**9, bytes_accessed=1 << 20, transcendentals=0
        ),
    )(*arrays)
    return types.SimpleNamespace(**dict(zip(outs, results)))


def attention_scratch(length, width):
    pairs, q_tiles, k_tiles = width // LANES, length // TILE, 2 * length // TILE
    return dict(
        q=((length, width), bf16),
        kv=((2 * length, 2 * width), bf16),
        qm=((pairs, q_tiles, 2 * TILE, LANES), bf16),
        kdc=((2 * length, LANES), f32),
        docs=((3, 16, width), bf16),
        qd=((length // TILE, 8, TILE), f32),
        bounds=((2, 3 * length // TILE), jnp.int32),
        bias=((TILE, TILE), f32),
        lse=((q_tiles, 8, 2 * TILE), f32),
        att=((length, width), bf16),
        turned=((width, TILE), f32),
    )


def forward_scratch(length, width):
    k_tiles = 2 * length // TILE
    return dict(
        vt=((k_tiles, width, TILE), bf16),
        top=((8, 2 * TILE), f32),
        total=((8, 2 * TILE), f32),
    )


def backward_scratch(length, width):
    pairs, q_tiles, k_tiles = width // LANES, length // TILE, 2 * length // TILE
    return dict(
        kt=((k_tiles, width, TILE), bf16),
        gm=((pairs, q_tiles, 2 * TILE, LANES), bf16),
        delta=((q_tiles, 8, 2 * TILE), f32),
        dkv=((2 * length, 2 * width), f32),
        dq=((length, width), f32),
        dkv_low=((2 * length, 2 * width), bf16),
        part_other=((length, width), bf16),
        dq_low=((length, width), bf16),
    )


def for_sending(shard):

    def short(part):
        return part.astype(jnp.bfloat16) if part.dtype == jnp.float32 else part

    return jax.tree.map(short, shard)


def from_behind(block, axis, distance):
    devices = range(lax.axis_size(axis))
    route = [(i - distance, i) for i in devices if i - distance in devices]
    return lax.ppermute(block, axis, route)


def from_root(shard, axis, root):
    mine = lax.axis_index(axis) == root
    return lax.psum(jnp.where(mine, shard, jnp.zeros_like(shard)), axis)


def matmul(left_side, right_side):
    return jnp.einsum("rsd,de->rse", left_side, right_side, preferred_element_type=jnp.float32)


def matmul_back(left_side, right_side):
    return jnp.einsum("rse,de->rsd", left_side, right_side, preferred_element_type=jnp.float32)


def contract(left_side, right_side):
    return jnp.einsum("rsd,rse->de", left_side, right_side, preferred_element_type=jnp.float32)


def normalize(values, gain_row):
    center = values - jnp.mean(values, axis=-1, keepdims=True)
    inverse = lax.rsqrt(jnp.mean(center * center, axis=-1, keepdims=True) + epsilon)
    standard = center * inverse
    return (standard * gain_row, standard, inverse)


def normalize_back(grad_out, standard, gain_row, inverse):
    scaled = grad_out * gain_row
    grad_in = inverse * (
        scaled
        - jnp.mean(scaled, axis=-1, keepdims=True)
        - standard * jnp.mean(scaled * standard, axis=-1, keepdims=True)
    )
    return (grad_in, jnp.sum(grad_out * standard, axis=(0, 1)))


def allowed_mask(query_docs, key_docs, query_place, key_place, causal):
    same_doc = query_docs[:, :, None] == key_docs[:, None, :]
    earlier = query_place[:, None] >= key_place[None, :]
    return (same_doc & (earlier | jnp.logical_not(causal)))[:, None]


def attend(queries, keys_local, values_local, query_docs, key_docs, causal, is_cross):
    rows_here, shard_len, model_width = queries.shape
    head_dim = model_width // HEADS
    score_scale = head_dim ** (-0.5)
    query_place = lax.axis_index("seq") * shard_len + jnp.arange(shard_len)
    query_heads = queries.reshape(rows_here, shard_len, HEADS, head_dim)

    def absorb(state_tuple, pieces):
        running_top, running_total, running_sum = state_tuple
        key_piece, value_piece, doc_piece = pieces
        piece_len = key_piece.shape[1]
        raw_scores = jnp.einsum(
            "rqhd,rkhd->rhqk",
            query_heads,
            key_piece.reshape(rows_here, piece_len, HEADS, head_dim),
            preferred_element_type=jnp.float32,
        )
        allowed = allowed_mask(query_docs, doc_piece, query_place, jnp.arange(piece_len), causal)
        scores = jnp.where(allowed, raw_scores * score_scale, negative_big)
        new_top = jnp.maximum(running_top, jnp.max(scores, axis=-1))
        weights = jnp.where(allowed, jnp.exp(scores - new_top[..., None]), 0.0)
        new_total = jnp.sum(weights, axis=-1)
        product = jnp.einsum(
            "rhqk,rkhd->rhqd",
            weights.astype(jnp.bfloat16),
            value_piece.reshape(rows_here, piece_len, HEADS, head_dim),
            preferred_element_type=jnp.float32,
        )
        return (new_top, new_total, product)

    init_state = (
        jnp.full((rows_here, HEADS, shard_len), negative_big, jnp.float32),
        jnp.zeros((rows_here, HEADS, shard_len), jnp.float32),
        jnp.zeros((rows_here, HEADS, shard_len, head_dim), jnp.float32),
    )
    if is_cross:
        final_top, final_total, final_sum = absorb(
            init_state,
            (
                lax.all_gather(keys_local, "seq", axis=1, tiled=True),
                lax.all_gather(values_local, "seq", axis=1, tiled=True),
                lax.all_gather(for_sending(key_docs), "seq", axis=1, tiled=True),
            ),
        )
    else:
        final_top, final_total, final_sum = absorb(
            init_state,
            (
                lax.all_gather(keys_local, "seq", axis=1, tiled=True),
                lax.all_gather(values_local, "seq", axis=1, tiled=True),
                lax.all_gather(key_docs, "seq", axis=1, tiled=True),
            ),
        )
    attended = (
        (final_sum / final_total[..., None])
        .transpose(0, 2, 1, 3)
        .reshape(rows_here, shard_len, model_width)
    )
    return (attended, final_top + jnp.log(final_total))


def attend_back(
    queries,
    keys_local,
    values_local,
    query_docs,
    key_docs,
    causal,
    log_total,
    grad_attended,
    is_cross,
):
    rows_here, shard_len, model_width = queries.shape
    head_dim = model_width // HEADS
    score_scale = head_dim ** (-0.5)
    query_place = lax.axis_index("seq") * shard_len + jnp.arange(shard_len)
    if is_cross:
        keys_full, values_full, docs_full = (
            lax.all_gather(keys_local, "seq", axis=1, tiled=True),
            lax.all_gather(values_local, "seq", axis=1, tiled=True),
            lax.all_gather(for_sending(key_docs), "seq", axis=1, tiled=True).astype(key_docs.dtype),
        )
    else:
        keys_full, values_full, docs_full = (
            lax.all_gather(keys_local, "seq", axis=1, tiled=True),
            lax.all_gather(values_local, "seq", axis=1, tiled=True),
            lax.all_gather(key_docs, "seq", axis=1, tiled=True),
        )
    full_len = keys_full.shape[1]
    query_heads = queries.reshape(rows_here, shard_len, HEADS, head_dim)
    key_heads = keys_full.reshape(rows_here, full_len, HEADS, head_dim)
    value_heads = values_full.reshape(rows_here, full_len, HEADS, head_dim)
    grad_heads = grad_attended.reshape(rows_here, shard_len, HEADS, head_dim)
    raw_scores = jnp.einsum(
        "rqhd,rkhd->rhqk", query_heads, key_heads, preferred_element_type=jnp.float32
    )
    allowed = allowed_mask(query_docs, docs_full, query_place, jnp.arange(full_len), causal)
    shifted = jnp.where(allowed, raw_scores * score_scale - log_total[..., None], negative_big)
    probs = jnp.where(allowed, jnp.exp(shifted), 0.0)
    grad_probs = jnp.einsum(
        "rqhd,rkhd->rhqk", grad_heads, value_heads, preferred_element_type=jnp.float32
    )
    delta = jnp.sum(probs * grad_probs, axis=-1)
    grad_scores = (probs * (grad_probs - delta[..., None]) * score_scale).astype(jnp.bfloat16)
    grad_queries = jnp.einsum(
        "rhqk,rkhd->rqhd", grad_scores, key_heads, preferred_element_type=jnp.float32
    ).reshape(rows_here, shard_len, model_width)
    probs_low = probs.astype(jnp.bfloat16)

    def key_terms(span):
        grad_keys = jnp.einsum(
            "rhqk,rqhd->krhd", grad_scores, query_heads, preferred_element_type=jnp.float32
        )
        grad_values = jnp.einsum(
            "rhqk,rqhd->krhd", probs_low, grad_heads, preferred_element_type=jnp.float32
        )
        return jnp.concatenate(
            [
                grad_keys.reshape(span, rows_here, model_width),
                grad_values.reshape(span, rows_here, model_width),
            ],
            axis=-1,
        )

    if is_cross:
        pair_terms = lax.psum_scatter(
            key_terms(shard_len * lax.axis_size("seq")).astype(jnp.bfloat16),
            "seq",
            scatter_dimension=0,
            tiled=True,
        ).astype(jnp.float32)
    else:
        pair_terms = lax.psum_scatter(
            key_terms(shard_len * lax.axis_size("seq")).astype(jnp.bfloat16),
            "seq",
            scatter_dimension=0,
            tiled=True,
        ).astype(jnp.float32)
    return (grad_queries, pair_terms.transpose(1, 0, 2))


def layer_forward(hidden_in, doc_own, memory, memory_docs, weights, is_decoder):
    (
        qkv_weight,
        out_weight,
        in_weight,
        down_weight,
        gains_pair,
        query_weight,
        pair_weight,
        cross_weight,
        cross_gains,
    ) = weights
    model_width = hidden_in.shape[-1]
    mixed = matmul(hidden_in, qkv_weight).astype(jnp.bfloat16)
    attended, self_lse = attend(
        mixed[..., :model_width],
        mixed[..., model_width : 2 * model_width],
        mixed[..., 2 * model_width :],
        doc_own,
        doc_own,
        is_decoder,
        False,
    )
    attended = attended.astype(jnp.bfloat16)
    first, first_unit, first_inv = normalize(
        hidden_in.astype(jnp.float32) + matmul(attended, out_weight), gains_pair[0]
    )
    first_low = first.astype(jnp.bfloat16)
    cross_queries = matmul(first_low, query_weight).astype(jnp.bfloat16)
    pair = matmul(memory, pair_weight).astype(jnp.bfloat16)
    cross_att, cross_lse = attend(
        cross_queries,
        pair[..., :model_width],
        pair[..., model_width:],
        doc_own,
        memory_docs,
        False,
        True,
    )
    cross_att = cross_att.astype(jnp.bfloat16)
    second_cross, second_unit, second_inv = normalize(
        first + matmul(cross_att, cross_weight), cross_gains
    )
    second = jnp.where(is_decoder, second_cross, first)
    second_low = second.astype(jnp.bfloat16)
    upward = matmul(second_low, in_weight)
    active = jax.nn.silu(upward).astype(jnp.bfloat16)
    result, third_unit, third_inv = normalize(second + matmul(active, down_weight), gains_pair[1])
    saved = {
        "mixed": mixed,
        "attended": attended,
        "self_lse": self_lse,
        "first_unit": first_unit,
        "first_inv": first_inv,
        "first_low": first_low,
        "cross_queries": cross_queries,
        "pair": pair,
        "cross_att": cross_att,
        "cross_lse": cross_lse,
        "second_unit": second_unit,
        "second_inv": second_inv,
        "second_low": second_low,
        "upward": upward,
        "active": active,
        "third_unit": third_unit,
        "third_inv": third_inv,
    }
    return (result, saved)


def layer_backward(
    grad_result, saved, hidden_in, doc_own, memory, memory_docs, weights, is_decoder
):
    (
        qkv_weight,
        out_weight,
        in_weight,
        down_weight,
        gains_pair,
        query_weight,
        pair_weight,
        cross_weight,
        cross_gains,
    ) = weights
    model_width = hidden_in.shape[-1]
    grad_third, grad_gain_late = normalize_back(
        grad_result, saved["third_unit"], gains_pair[1], saved["third_inv"]
    )
    down_grad = grad_third.astype(jnp.bfloat16)
    grad_down_w = contract(saved["active"], down_grad)
    grad_active = matmul_back(down_grad, down_weight).astype(jnp.bfloat16)
    sigmoid_up = jax.nn.sigmoid(saved["upward"])
    grad_upward = (
        grad_active.astype(jnp.float32)
        * (sigmoid_up + saved["upward"] * sigmoid_up * (1.0 - sigmoid_up))
    ).astype(jnp.bfloat16)
    grad_in_w = contract(saved["second_low"], grad_upward)
    grad_second = grad_third + matmul_back(grad_upward, in_weight)
    grad_cross_sum, grad_cross_gain = normalize_back(
        grad_second, saved["second_unit"], cross_gains, saved["second_inv"]
    )
    decoder_flag = is_decoder.astype(jnp.float32)
    grad_cross_sum = grad_cross_sum * decoder_flag
    grad_cross_gain = grad_cross_gain * decoder_flag
    cross_branch = grad_cross_sum.astype(jnp.bfloat16)
    grad_cross_w = contract(saved["cross_att"], cross_branch)
    grad_cross_att = matmul_back(cross_branch, cross_weight).astype(jnp.bfloat16)
    pair = saved["pair"]
    grad_cross_q, grad_pair = attend_back(
        saved["cross_queries"],
        pair[..., :model_width],
        pair[..., model_width:],
        doc_own,
        memory_docs,
        False,
        saved["cross_lse"],
        grad_cross_att,
        True,
    )
    grad_cross_q = grad_cross_q.astype(jnp.bfloat16)
    grad_pair = grad_pair.astype(jnp.bfloat16)
    grad_query_w = contract(saved["first_low"], grad_cross_q)
    grad_pair_w = contract(memory, grad_pair)
    grad_memory = matmul_back(grad_pair, pair_weight)
    grad_first = jnp.where(
        is_decoder, grad_cross_sum + matmul_back(grad_cross_q, query_weight), grad_second
    )
    grad_first_sum, grad_gain_early = normalize_back(
        grad_first, saved["first_unit"], gains_pair[0], saved["first_inv"]
    )
    self_branch = grad_first_sum.astype(jnp.bfloat16)
    grad_out_w = contract(saved["attended"], self_branch)
    grad_attended = matmul_back(self_branch, out_weight).astype(jnp.bfloat16)
    mixed = saved["mixed"]
    grad_queries, grad_pair_self = attend_back(
        mixed[..., :model_width],
        mixed[..., model_width : 2 * model_width],
        mixed[..., 2 * model_width :],
        doc_own,
        doc_own,
        is_decoder,
        saved["self_lse"],
        grad_attended,
        False,
    )
    grad_mixed = jnp.concatenate([grad_queries, grad_pair_self], axis=-1).astype(jnp.bfloat16)
    grad_qkv_w = contract(hidden_in, grad_mixed)
    grad_hidden = grad_first_sum + matmul_back(grad_mixed, qkv_weight)
    layer_grads = (
        grad_qkv_w,
        grad_out_w,
        grad_in_w,
        grad_down_w,
        jnp.stack([grad_gain_early, grad_gain_late]),
        grad_query_w,
        grad_pair_w,
        grad_cross_w,
        grad_cross_gain,
    )
    return (grad_hidden, grad_memory, layer_grads)


def any_rows(
    layer_input,
    segment_ids,
    attn_qkv,
    attn_out,
    ffn_in,
    ffn_out,
    norm_gain,
    cross_query,
    cross_pair,
    cross_out,
    cross_gain,
    out_cotangent,
):
    micro_count = layer_input.shape[1]
    section_index = lax.axis_index("section")
    is_decoder = section_index == 1
    weights = (
        attn_qkv[0],
        attn_out[0],
        ffn_in[0],
        ffn_out[0],
        norm_gain[0],
        cross_query,
        cross_pair,
        cross_out,
        cross_gain,
    )
    inputs_all = layer_input[0]
    docs_all = segment_ids[0]
    slot_ids = jnp.arange(micro_count)
    received = (jnp.zeros_like(inputs_all[0]), jnp.zeros_like(docs_all[0]))
    results = jnp.zeros_like(inputs_all)
    memories = []
    memory_doc_list = []
    for step_index in range(micro_count + 1):
        batch_index = step_index - section_index
        is_valid = (batch_index >= 0) & (batch_index < micro_count)
        chosen = jnp.clip(batch_index, 0, micro_count - 1)
        hidden_in = lax.dynamic_index_in_dim(inputs_all, chosen, 0, keepdims=False)
        doc_own = lax.dynamic_index_in_dim(docs_all, chosen, 0, keepdims=False)
        memory = received[0]
        memory_docs = jnp.where(is_valid & is_decoder, received[1], doc_own)
        memories.append(memory)
        memory_doc_list.append(memory_docs)
        result, saved = layer_forward(hidden_in, doc_own, memory, memory_docs, weights, is_decoder)
        low_result = result.astype(jnp.bfloat16)
        writing = (slot_ids == chosen) & is_valid
        results = jnp.where(writing[:, None, None, None], low_result[None], results)
        if step_index < micro_count:
            received = from_behind((low_result, doc_own), "section", 1)
    memory_stack = jnp.stack(memories)
    memory_doc_stack = jnp.stack(memory_doc_list)
    totals = tuple((jnp.zeros(weight.shape, jnp.float32) for weight in weights))
    input_grads = jnp.zeros(inputs_all.shape, jnp.float32)
    returned = jnp.zeros(inputs_all.shape[1:], jnp.float32)
    for step_index in range(micro_count + 1):
        batch_index = micro_count - step_index - section_index
        is_valid = (batch_index >= 0) & (batch_index < micro_count)
        chosen = jnp.clip(batch_index, 0, micro_count - 1)
        forward_step = jnp.clip(batch_index + section_index, 0, micro_count)
        hidden_in = lax.dynamic_index_in_dim(inputs_all, chosen, 0, keepdims=False)
        doc_own = lax.dynamic_index_in_dim(docs_all, chosen, 0, keepdims=False)
        memory = lax.dynamic_index_in_dim(memory_stack, forward_step, 0, keepdims=False)
        memory_docs = lax.dynamic_index_in_dim(memory_doc_stack, forward_step, 0, keepdims=False)
        discarded, saved = layer_forward(
            hidden_in, doc_own, memory, memory_docs, weights, is_decoder
        )
        cotangent = jnp.where(
            is_decoder,
            lax.dynamic_index_in_dim(out_cotangent, chosen, 0, keepdims=False).astype(jnp.float32),
            returned,
        )
        grad_hidden, grad_memory, layer_grads = layer_backward(
            cotangent, saved, hidden_in, doc_own, memory, memory_docs, weights, is_decoder
        )
        valid_flag = is_valid.astype(jnp.float32)
        totals = tuple(
            (running + valid_flag * fresh for running, fresh in zip(totals, layer_grads))
        )
        writing = (slot_ids == chosen) & is_valid
        input_grads = jnp.where(writing[:, None, None, None], grad_hidden[None], input_grads)
        if step_index < micro_count:
            returned = from_behind(grad_memory.astype(jnp.bfloat16), "section", -1).astype(
                grad_memory.dtype
            )
    group_sums = lax.psum(
        (
            totals[0],
            totals[1],
            totals[2],
            totals[3],
            totals[4],
            totals[5],
            totals[6],
            totals[7],
            totals[8],
        ),
        ("seq", "dp"),
    )
    section_sums = group_sums[:5]
    cross_sums = (
        from_root(group_sums[5].astype(jnp.bfloat16), "section", 1).astype(jnp.float32),
        from_root(group_sums[6].astype(jnp.bfloat16), "section", 1).astype(jnp.float32),
        from_root(group_sums[7].astype(jnp.bfloat16), "section", 1).astype(jnp.float32),
        from_root(group_sums[8].astype(jnp.bfloat16), "section", 1).astype(jnp.float32),
    )
    return (
        results[None],
        input_grads[None],
        section_sums[0][None],
        section_sums[1][None],
        section_sums[2][None],
        section_sums[3][None],
        section_sums[4][None],
        cross_sums[0],
        cross_sums[1],
        cross_sums[2],
        cross_sums[3],
    )


def split_rows(
    layer_input,
    segment_ids,
    attn_qkv,
    attn_out,
    ffn_in,
    ffn_out,
    norm_gain,
    cross_query,
    cross_pair,
    cross_out,
    cross_gain,
    out_cotangent,
):
    micros = layer_input.shape[1]
    length, width = layer_input.shape[3:]
    hidden = ffn_in.shape[-1]
    q_tiles = length // TILE
    group = lax.axis_size("dp") // 2
    axes = ("section", "seq", "dp")
    decoder = lax.axis_index("section") == 1
    flag = decoder.astype(jnp.int32)
    x = lax.axis_index("seq")
    core = lax.rem(lax.axis_index("dp"), 2)
    z = lax.axis_index("dp") // 2
    places = [(t, i, k, c) for t in range(2) for i in range(2) for k in range(group) for c in range(2)]

    def number(t, i, k, c):
        return ((t * 2 + i) * group + k) * 2 + c

    def send(values, target, section=None):
        route = [
            (number(*place), number(*target(*place)))
            for place in places
            if section in (None, place[0]) and target(*place)
        ]
        return lax.ppermute(values, axes, route)

    def to_core(t, i, k, c):
        return (t, i, k, 1 - c)

    def to_x(t, i, k, c):
        return (t, 1 - i, k, c)

    def to_row(t, i, k, c):
        return (t, c, k, i)

    def to_decoder(t, i, k, c):
        return (1, i, k, c) if t == 0 else None

    def to_encoder(t, i, k, c):
        return (0, i, k, c) if t == 1 else None

    def fence(values, *before):
        return lax.optimization_barrier((values,) + before)[0]

    def exchange(values):
        return send(values, to_core)

    low = ((length, width), bf16)
    wide = ((length, width), f32)
    marked = ((length + 16, width), bf16)
    both = ((2 * length, width), bf16)
    keys_all = ((2 * length, 2 * width), bf16)
    mixing = ((width, 3 * width), bf16)
    inner = ((length, hidden), bf16)
    lse = ((q_tiles, 8, 2 * TILE), f32)
    stat = ((length, LANES), f32)
    square = ((width, width), bf16)
    rising = ((width, hidden), bf16)
    falling = ((hidden, width), bf16)
    gain_rows = ((8, width), f32)

    meta = jnp.stack([flag, core, x, z]).astype(jnp.int32)
    numbers = segment_ids[0, :, 0].astype(bf16)
    padding = jnp.zeros((15, width), bf16)
    with_numbers = [
        jnp.concatenate([layer_input[0, micro, 0], numbers[micro][None], padding])
        for micro in range(micros)
    ]
    own = [send(with_numbers[0], to_row)]
    for micro in range(1, micros):
        own.append(send(fence(with_numbers[micro], own[-1]), to_row))
    other = [exchange(own[0])]

    plain = dict(meta=meta)
    small = dict(gains=norm_gain[0])
    forward, memories, memories_other = [], [], []
    for micro in range(micros):
        call = launch(
            self_forward,
            micro,
            None,
            plain,
            small,
            dict(
                x_own_h=own[micro],
                x_other_h=other[micro],
                w_mixed_h=attn_qkv[0],
                w_out_h=attn_out[0],
                w_in_h=ffn_in[0],
                w_down_h=ffn_out[0],
            ),
            dict(
                q_o=low,
                kv_o=keys_all,
                att_o=low,
                lse_o=lse,
                unit1_o=wide,
                inv1_o=stat,
                first_low_o=low,
                memory_o=marked,
                ffn_low_o=low,
                act_o=inner,
                slope_o=inner,
                unit2_o=wide,
                inv2_o=stat,
            ),
            dict(
                **attention_scratch(length, width),
                **forward_scratch(length, width),
                x=both,
                w_mixed=mixing,
                w_out=square,
                w_in=rising,
                w_down=falling,
                unit1=wide,
                inv1=stat,
                first_low=low,
                memory=marked,
                act=inner,
                slope=inner,
                unit2=wide,
                inv2=stat,
                sum=wide,
            ),
            28,
            26,
            after=(forward[0].lse_o,) if micro else (),
        )
        forward.append(call)
        memories.append(send(call.memory_o, to_decoder))
        if micro + 1 < micros:
            other.append(exchange(fence(own[micro + 1], call.lse_o)))

    for micro in range(micros):
        memories_other.append(exchange(fence(memories[micro], forward[-1].lse_o)))
    cotangent = send(fence(out_cotangent[:, 0], forward[0].lse_o), to_row)

    cross, grads_memory, made = [], [], []
    after = (forward[-1].lse_o,)
    for micro in range(micros):
        done = forward[micro]
        call = launch(
            cross_both_ways,
            micro,
            1,
            plain,
            dict(**small, cross_gain=cross_gain[None]),
            dict(
                x_own_h=own[micro],
                memory_own_h=memories[micro],
                memory_other_h=memories_other[micro],
                w_pair_h=cross_pair,
                first_low_h=done.first_low_o,
                unit1_h=done.unit1_o,
                w_query_h=cross_query,
                w_cross_h=cross_out,
                w_in_h=ffn_in[0],
                w_down_h=ffn_out[0],
                cot_h=cotangent,
            ),
            dict(
                att_o=low,
                ffn_low_o=low,
                act_o=inner,
                decoded_o=low,
                down_grad_o=low,
                up_grad_o=inner,
                gain_grads_o=gain_rows,
                branch_o=low,
                dq_low_o=low,
                dkv_o=keys_all,
                part_own_o=wide,
                part_other_o=low,
                grad_first_o=wide,
            ),
            dict(
                **attention_scratch(length, width),
                **forward_scratch(length, width),
                **backward_scratch(length, width),
                x=both,
                w_pair=((width, 2 * width), bf16),
                first_low=low,
                unit1=wide,
                w_query=square,
                w_cross=square,
                w_in=rising,
                w_down=falling,
                cot=low,
                unit2=wide,
                inv2=stat,
                second_low=low,
                act=inner,
                slope=inner,
                sum=wide,
                decoded=low,
                keep=wide,
                down_grad=low,
                up_grad=inner,
                gain_grads=gain_rows,
                branch=low,
                part_own=wide,
            ),
            36,
            44,
            dict(act_o=done.act_o, ffn_low_o=done.ffn_low_o),
            after,
        )
        cross.append(call)
        away = call.part_other_o
        if micro:
            away = fence(away, grads_memory[-1])
        total = call.part_own_o + exchange(away).astype(f32)
        made.append(total.astype(bf16))
        after = (made[micro],)
        grads_memory.append(send(made[micro], to_encoder))

    def backward_feed(micro, after):
        done, late = forward[micro], cross[micro]
        return launch(
            feed_backward_alone,
            micro,
            0,
            plain,
            dict(gains=norm_gain[0]),
            dict(
                grad_memory_h=grads_memory[micro],
                unit2_h=done.unit2_o,
                inv2_h=done.inv2_o,
                slope_h=done.slope_o,
                w_in_h=ffn_in[0],
                w_down_h=ffn_out[0],
            ),
            dict(gain_late_o=gain_rows, down_grad_o=low, up_grad_o=inner, grad_first_o=wide),
            dict(
                cot=low,
                unit2=wide,
                inv2=stat,
                slope=inner,
                w_in=rising,
                w_down=falling,
                gain_grads=gain_rows,
                keep=wide,
                down_grad=low,
                up_grad=inner,
                sum=wide,
            ),
            12,
            10,
            dict(
                down_grad_o=late.down_grad_o, up_grad_o=late.up_grad_o, grad_first_o=late.grad_first_o
            ),
            after,
        )

    def backward_self(micro, side, grad_first, previous=None, after=(), halfway=None):
        done = forward[micro]
        heads = width // LANES
        given = dict(
            x_own_h=own[micro],
            x_other_h=other[micro],
            q_h=done.q_o,
            kv_h=done.kv_o,
            att_h=done.att_o,
            lse_h=done.lse_o,
        )
        ahead = dict(
            grad_first_h=grad_first,
            unit1_h=done.unit1_o,
            inv1_h=done.inv1_o,
            w_out_h=attn_out[0],
        )
        makes = dict(dq_low_o=low, dkv_o=keys_all)
        makes_first = dict(gain_early_o=gain_rows, branch_o=low)
        makes_last = dict(part_own_o=wide, part_other_o=low)
        scratch = dict(
            **attention_scratch(length, width),
            **backward_scratch(length, width),
            w_out=square,
            w_mixed=mixing,
            unit1=wide,
            inv1=stat,
            keep=wide,
            branch=low,
            grad_att=low,
            gain_grads=gain_rows,
        )

        def part(first, last, large, outs, work, previous, after):
            return launch(
                self_backward,
                (micro, first, last),
                side,
                plain,
                small,
                dict(**given, **large),
                dict(**makes, **outs),
                scratch,
                28,
                work,
                previous,
                after,
            )

        if halfway is None:
            large = dict(**ahead, w_mixed_h=attn_qkv[0])
            outs = dict(**makes_first, **makes_last)
            return part(0, heads, large, outs, 22, previous, after)
        outs = dict(**makes_first, grad_sum_o=wide, grad_att_o=low)
        one = part(0, heads // 2, ahead, outs, 12, None, after)
        large = dict(
            w_mixed_h=attn_qkv[0],
            grad_sum_h=one.grad_sum_o,
            grad_att_h=one.grad_att_o,
            dq_h=one.dq_low_o,
            dkv_h=one.dkv_o,
        )
        two = part(heads // 2, heads, large, makes_last, 12, None, halfway(one))
        return types.SimpleNamespace(**{**vars(one), **vars(two)})

    def weight_grads(plan, side, arrays, scratch, after=()):
        blocks = ((2, width, width), bf16)
        call = launch(
            contract_blocks,
            plan,
            side,
            plain,
            dict(),
            arrays,
            dict(sent_o=blocks, kept_o=blocks),
            dict(**scratch, blocks=((4, width, width), bf16)),
            36,
            8,
            after=after,
        )
        return call.sent_o, call.kept_o

    def first_sums(halves, section=None):
        sent, kept = halves
        got = send(sent, to_core, section)

        def block(side):
            return sum(
                lax.dynamic_index_in_dim(part, side, 0, keepdims=False).astype(f32)
                for part in (kept, got)
            )

        return block(1 - x).astype(bf16), block(x)

    def middle_sums(sums, section=None):
        away, total = sums
        return (total + send(away, to_x, section).astype(f32)).astype(bf16)

    def last_sums(total, later=(), section=None):
        shares = total.reshape(group, width // group, width)

        def share(step):
            return lax.dynamic_index_in_dim(shares, lax.rem(z + step, group), 0, keepdims=False)

        parts = [share(0)]
        for step in range(1, group):
            parts.append(send(share(step), along_z(step), section))
        if later:
            parts = [fence(part, *later) for part in parts]
        return sum(part.astype(f32) for part in parts).astype(bf16)

    def along_z(step):
        return lambda t, i, k, c: (t, i, (k + step) % group, c)

    def gather_z(share):
        return [share] + [send(share, along_z(step)) for step in range(1, group)]

    def gain_block(rows):
        filled = jnp.concatenate([jnp.stack(rows), jnp.zeros((16 - len(rows), width), f32)])
        return filled.astype(bf16)

    def spread(targets, own, own_x, outs, parts):
        return launch(
            spread_pieces,
            targets,
            None,
            plain,
            dict(),
            dict(own_h=own, own_x_h=own_x, other_h=exchange(own), other_x_h=exchange(own_x)),
            outs,
            dict(
                pieces=((4,) + own.shape, bf16),
                wide=((4 * group * parts, width // group, width), f32),
            ),
            8 + 4 * group * parts,
            5,
        )

    tokens, all_tokens = micros * length, 2 * micros * length
    turn, turn_all = ((width, tokens), bf16), ((width, all_tokens), bf16)
    narrow, narrow_all = ((tokens, width), bf16), ((all_tokens, width), bf16)
    pair_all = ((all_tokens, 2 * width), bf16)
    deep = ((tokens, hidden), bf16)

    def part_of(buffer, *sources):
        return lambda column: (buffer, sources, column)

    def key_rows(buffer, sources):
        first, second = pl.ds(0, length), pl.ds(length, length)
        return part_of(buffer, *[source.at[rows] for rows in (first, second) for source in sources])

    def cross_plan(r):
        rows = pl.ds(0, length)
        low_part = part_of(r.low, r.low0_h, r.low1_h)
        att_part = part_of(r.att, r.att0_h, r.att1_h)
        dq_part = part_of(r.dq, r.dq0_h, r.dq1_h)
        branch_part = part_of(r.branch, r.branch0_h, r.branch1_h)
        sources = (r.mem0_h, r.mem1_h, r.mem2_h, r.mem3_h)
        mem_part = part_of(r.mem, *[source.at[rows] for source in sources])
        pair_part = key_rows(r.pair, (r.pair0_h, r.pair1_h))
        return [
            (r.turn, low_part(0), dq_part(0)),
            (r.turn_att, att_part(0), branch_part(0)),
            (r.turn_all, mem_part(0), pair_part(0)),
            (r.turn_all, mem_part(0), pair_part(1)),
        ]

    def rising_plan(r):
        low_part = part_of(r.low, r.low0_h, r.low1_h)
        up_part = part_of(r.up, r.up0_h, r.up1_h)
        return [(r.turn, low_part(0), up_part(block)) for block in range(4)]

    def falling_plan(r):
        act_part = part_of(r.act, r.act0_h, r.act1_h)
        down_part = part_of(r.down, r.down0_h, r.down1_h)
        return [(r.turn, act_part(block), down_part(0)) for block in range(4)]

    def self_plan(r):
        rows = pl.ds(0, length)
        sources = (r.x0_h, r.x1_h, r.x2_h, r.x3_h)
        x_part = part_of(r.x, *[source.at[rows] for source in sources])
        dq_part = part_of(r.dq, r.dq0_h, r.dq1_h)
        pair_part = key_rows(r.pair, (r.pair0_h, r.pair1_h))
        att_part = part_of(r.att, r.att0_h, r.att1_h)
        branch_part = part_of(r.branch, r.branch0_h, r.branch1_h)
        return [
            (r.turn_all, x_part(0), dq_part(0)),
            (r.turn_all, x_part(0), pair_part(0)),
            (r.turn_all, x_part(0), pair_part(1)),
            (r.turn, att_part(0), branch_part(0)),
        ]

    last = micros - 1
    feeds, ends = [None] * micros, [None] * micros
    results = jnp.stack(
        [
            jnp.where(decoder, call.decoded_o, done.memory_o[:length])
            for call, done in zip(cross, forward)
        ]
    )
    results = send(results, to_row)
    latest = made[last]

    def part_sum(micro, *before):
        end = ends[micro]
        away = fence(end.part_other_o, *before)
        total = (end.part_own_o + exchange(away).astype(f32)).astype(bf16)
        return total, send(total, to_row)

    steps = []
    for micro in range(last):
        feeds[micro] = backward_feed(micro, (latest,))
        first = feeds[micro].grad_first_o
        ends[micro] = backward_self(micro, 0, first)
        ends[micro] = backward_self(micro, 1, first, vars(ends[micro]), (made[last],))
        steps.append(part_sum(micro, grads_memory[last]))
        latest = ends[micro].gain_early_o
    feeds[last] = backward_feed(last, (latest,))

    rising_halves = weight_grads(
        rising_plan,
        None,
        dict(
            low0_h=cross[0].ffn_low_o,
            low1_h=cross[1].ffn_low_o,
            up0_h=feeds[0].up_grad_o,
            up1_h=feeds[1].up_grad_o,
        ),
        dict(low=narrow, up=deep, turn=turn),
        (results,) + tuple(step[0] for step in steps),
    )
    rising_sums = first_sums(rising_halves)
    rising_total = middle_sums(rising_sums)
    falling_halves = weight_grads(
        falling_plan,
        None,
        dict(
            act0_h=cross[0].act_o,
            act1_h=cross[1].act_o,
            down0_h=feeds[0].down_grad_o,
            down1_h=feeds[1].down_grad_o,
        ),
        dict(act=deep, down=narrow, turn=turn),
        (rising_sums[0],) + tuple(step[1] for step in steps),
    )
    cross_halves = weight_grads(
        cross_plan,
        1,
        dict(
            low0_h=forward[0].first_low_o,
            low1_h=forward[1].first_low_o,
            dq0_h=cross[0].dq_low_o,
            dq1_h=cross[1].dq_low_o,
            att0_h=cross[0].att_o,
            att1_h=cross[1].att_o,
            branch0_h=cross[0].branch_o,
            branch1_h=cross[1].branch_o,
            mem0_h=memories[0],
            mem1_h=memories[1],
            mem2_h=memories_other[0],
            mem3_h=memories_other[1],
            pair0_h=cross[0].dkv_o,
            pair1_h=cross[1].dkv_o,
        ),
        dict(
            low=narrow,
            dq=narrow,
            att=narrow,
            branch=narrow,
            mem=narrow_all,
            pair=pair_all,
            turn=turn,
            turn_att=turn,
            turn_all=turn_all,
        ),
        (falling_halves[0],),
    )
    falling_sent = fence(falling_halves[0], rising_total, cross_halves[0])
    falling_sums = first_sums((falling_sent, falling_halves[1]))
    cross_sums = first_sums(cross_halves, 1)
    falling_total = middle_sums(falling_sums)
    shares = []

    def halfway(one):
        shares.append(last_sums(rising_total, (one.gain_early_o,)))
        shares.append(middle_sums((fence(cross_sums[0], one.gain_early_o), cross_sums[1]), 1))
        return (shares[0], falling_total)

    ends[last] = backward_self(
        last,
        None,
        feeds[last].grad_first_o,
        None,
        (falling_sums[0], cross_sums[0]),
        halfway,
    )
    rising_share, cross_total = shares
    falling_share = last_sums(falling_total, (ends[last].gain_early_o, ends[last].part_own_o))
    steps.append(part_sum(last, falling_share, cross_total))
    one_own = gather_z(jnp.concatenate([rising_share, falling_share]))

    self_halves = weight_grads(
        self_plan,
        None,
        dict(
            x0_h=own[0],
            x1_h=own[1],
            x2_h=other[0],
            x3_h=other[1],
            dq0_h=ends[0].dq_low_o,
            dq1_h=ends[1].dq_low_o,
            pair0_h=ends[0].dkv_o,
            pair1_h=ends[1].dkv_o,
            att0_h=forward[0].att_o,
            att1_h=forward[1].att_o,
            branch0_h=ends[0].branch_o,
            branch1_h=ends[1].branch_o,
        ),
        dict(
            x=narrow_all,
            dq=narrow,
            pair=pair_all,
            att=narrow,
            branch=narrow,
            turn=turn,
            turn_all=turn_all,
        ),
        (steps[last][0],),
    )
    cross_share = last_sums(cross_total, (self_halves[0],), 1)
    away, total = first_sums(
        (fence(self_halves[0], cross_share, steps[last][1]), self_halves[1])
    )
    one_own = jnp.stack(one_own)
    self_total = middle_sums((away, total))
    third = sum(call.gain_grads_o[1] for call in cross)
    cross_share = jnp.concatenate([cross_share, gain_block([third])])
    cross_share = jnp.where(decoder, cross_share, send(cross_share, to_encoder))
    self_share = last_sums(self_total)
    one_own_x = send(fence(one_own, self_total), to_x)

    early = sum(end.gain_early_o[0] for end in ends)
    late = jnp.where(
        decoder,
        sum(call.gain_grads_o[0] for call in cross),
        sum(call.gain_late_o[0] for call in feeds),
    )
    two_own = jnp.stack(
        gather_z(jnp.concatenate([self_share, cross_share, gain_block([early, late])]))
    )
    two_own_x = send(fence(two_own, one_own_x), to_x)

    def columns(block):
        return pl.ds(block * width, width)

    def one_targets(r, block, row, rows):
        lines = pl.ds(row, rows)
        return [r.up_o.at[lines, columns(block)], r.down_o.at[pl.ds(block * width + row, rows)]]

    def two_targets(r, block, row, rows):
        lines = pl.ds(row, rows)
        own = r.out_o.at[lines] if block == 3 else r.mixed_o.at[lines, columns(block)]
        if block >= 2:
            return [own, r.pair_o.at[lines, columns(block - 2)]]
        return [own, (r.cross_o if block else r.query_o).at[lines]]

    square_out = ((width, width), f32)
    one_own_x = fence(one_own_x, two_own)
    one_grads = spread(
        one_targets,
        one_own,
        one_own_x,
        dict(up_o=((width, hidden), f32), down_o=((hidden, width), f32)),
        2,
    )
    two_own_x = fence(two_own_x, one_grads.up_o)
    two_grads = spread(
        two_targets,
        two_own,
        two_own_x,
        dict(
            mixed_o=((width, 3 * width), f32),
            out_o=square_out,
            query_o=square_out,
            pair_o=((width, 2 * width), f32),
            cross_o=square_out,
            gains_o=((3, width), f32),
        ),
        2,
    )

    grad_input = jnp.stack([step[1] for step in steps])
    return (
        results[None, :, None],
        grad_input.astype(f32)[None, :, None],
        two_grads.mixed_o[None],
        two_grads.out_o[None],
        one_grads.up_o[None],
        one_grads.down_o[None],
        two_grads.gains_o[None, :2],
        two_grads.query_o,
        two_grads.pair_o,
        two_grads.cross_o,
        two_grads.gains_o[2],
    )


def shards(*arrays):
    layer_input = arrays[0]
    micros, rows, length = layer_input.shape[1:4]
    simple = (
        lax.axis_size("section") == 2
        and lax.axis_size("seq") == 2
        and lax.axis_size("dp") in (4, 8, 16)
        and (micros, rows) == (2, 1)
        and length == layer_input.shape[-1] == CHUNK
        and arrays[4].shape[-1] == 4 * CHUNK
    )
    return split_rows(*arrays) if simple else any_rows(*arrays)


def solution(mesh):
    in_specs = (
        P("section", None, "dp", "seq", None),
        P("section", None, "dp", "seq"),
        P("section", None, None),
        P("section", None, None),
        P("section", None, None),
        P("section", None, None),
        P("section", None, None),
        P(),
        P(),
        P(),
        P(),
        P(None, "dp", "seq", None),
    )
    out_specs = (
        P("section", None, "dp", "seq", None),
        P("section", None, "dp", "seq", None),
        P("section", None, None),
        P("section", None, None),
        P("section", None, None),
        P("section", None, None),
        P("section", None, None),
        P(),
        P(),
        P(),
        P(),
    )
    return jax.shard_map(shards, mesh=mesh, in_specs=in_specs, out_specs=out_specs, check_vma=False)
```

```python
import types

import jax
import jax.numpy as jnp
from jax import lax
from jax.experimental import pallas as pl
from jax.experimental.pallas import tpu as pltpu
from jax.sharding import PartitionSpec as P

HEADS = 8
TILE = 256
LANES = 128
CHUNK = 512

f32 = jnp.float32
bf16 = jnp.bfloat16
negative_big = -1e30
epsilon = 1e-05


def dot(left, right):
    return lax.dot_general(left, right, (((1,), (0,)), ((), ())), preferred_element_type=f32)


def dot_nt(left, right):
    return lax.dot_general(left, right, (((1,), (1,)), ((), ())), preferred_element_type=f32)


def dot_tn(left, right):
    return lax.dot_general(left, right, (((0,), (0,)), ((), ())), preferred_element_type=f32)


def standardize(values):
    center = values - jnp.mean(values, axis=-1, keepdims=True)
    inverse = lax.rsqrt(jnp.mean(center * center, axis=-1, keepdims=True) + epsilon)
    return center * inverse, inverse


def standardize_back(grad_out, standard, gain_row, inverse):
    scaled = grad_out * gain_row
    grad_in = inverse * (
        scaled
        - jnp.mean(scaled, axis=-1, keepdims=True)
        - standard * jnp.mean(scaled * standard, axis=-1, keepdims=True)
    )
    return grad_in, jnp.sum(grad_out * standard, axis=0, keepdims=True)


class Copies:
    def __init__(self, sems):
        self.sems = sems
        self.used = 0

    def start(self, source, target):
        copy = pltpu.make_async_copy(source, target, self.sems.at[self.used])
        self.used += 1
        copy.start()
        return copy


def wait_all(copies):
    for copy in copies:
        copy.wait()


def spread_pairs(target, source, factor, pairs):
    tiles = target.shape[1]
    half = lax.broadcasted_iota(jnp.int32, (TILE, LANES), 1) < LANES // 2
    first = jnp.where(half, factor, 0.0).astype(bf16)
    second = jnp.where(half, 0.0, factor).astype(bf16)
    for tile in range(tiles):
        for pair in pairs:
            block = source[tile * TILE : (tile + 1) * TILE, pair * LANES : (pair + 1) * LANES]
            target[pair, tile, :TILE, :] = block * first
            target[pair, tile, TILE:, :] = block * second


def turn_tiles(target, source, column, pairs):
    low, high = pairs[0] * LANES, (pairs[-1] + 1) * LANES
    for tile in range(target.shape[0]):
        block = source[tile * TILE : (tile + 1) * TILE, column + low : column + high]
        target[tile, low:high, :] = jnp.transpose(block)


def place_documents(r, copies):
    wait_all(copies)
    q_tiles = r.qd.shape[0]
    for part in range(3):
        row = r.docs[part].astype(f32)[0:1, :]
        for tile in range(q_tiles):
            piece = row[:, tile * TILE : (tile + 1) * TILE]
            slot = part * q_tiles + tile
            r.bounds[0, slot] = jnp.min(piece).astype(jnp.int32)
            r.bounds[1, slot] = jnp.max(piece).astype(jnp.int32)
            if part == 0:
                r.qd[tile] = jnp.broadcast_to(piece, (8, TILE))
        if part > 0:
            for start in range(0, row.shape[1], LANES):
                block = jnp.broadcast_to(row[:, start : start + LANES], (LANES, LANES))
                place = (part - 1) * row.shape[1] + start
                r.kdc[place : place + LANES, :] = jnp.transpose(block)


def load_documents(r, move, queries, own, other):
    rows = pl.ds(r.docs.shape[2], r.docs.shape[1])
    return [
        move.start(source.at[rows], r.docs.at[part])
        for part, source in enumerate((queries, own, other))
    ]


def tile_place(r, core, causal, q_tile, k_tile):
    q_tiles = r.qd.shape[0]
    length = q_tiles * TILE
    owner = jnp.where(k_tile < q_tiles, core, 1 - core)
    k_start = owner * length + lax.rem(k_tile, q_tiles) * TILE
    ahead = core * length + q_tile * TILE - k_start
    ahead = jnp.where(causal == 1, ahead, 2 * length * TILE)
    q_low, q_high = r.bounds[0, q_tile], r.bounds[1, q_tile]
    k_low, k_high = r.bounds[0, q_tiles + k_tile], r.bounds[1, q_tiles + k_tile]
    active = (q_low <= k_high) & (k_low <= q_high) & (ahead > -TILE)
    whole = (q_low == k_high) & (k_low == q_high) & (ahead >= TILE)
    return active, whole, ahead


def each_tile(place, body):
    active, whole, ahead = place
    pl.when(active & jnp.logical_not(whole))(lambda: body(ahead))
    pl.when(whole)(lambda: body(None))


def fill_bias(r, q_tile, k_tile, ahead):
    keys = r.kdc[pl.ds(pl.multiple_of(k_tile * TILE, TILE), TILE), :]
    shift = lax.broadcasted_iota(jnp.int32, (TILE, LANES), 0) - lax.broadcasted_iota(
        jnp.int32, (TILE, LANES), 1
    )
    queries = r.qd[q_tile]
    for start in range(0, TILE, LANES):
        same = keys == queries[0:1, start : start + LANES]
        allowed = same & (shift - start <= ahead)
        r.bias[:, start : start + LANES] = jnp.where(allowed, 0.0, negative_big)


def attention_forward(r, core, causal):
    pairs, q_tiles = r.qm.shape[:2]
    k_tiles = r.vt.shape[0]

    def one_query_tile(q_tile, carry):
        r.top[...] = jnp.full(r.top.shape, negative_big, f32)
        r.total[...] = jnp.zeros(r.total.shape, f32)
        r.turned[...] = jnp.zeros(r.turned.shape, f32)

        def one_key_tile(k_tile, inner):
            def one_tile(ahead):
                if ahead is not None:
                    fill_bias(r, q_tile, k_tile, ahead)
                rows = pl.ds(pl.multiple_of(k_tile * TILE, TILE), TILE)

                def raw(pair):
                    keys = r.kv[rows, pair * LANES : (pair + 1) * LANES]
                    return dot_nt(keys, r.qm[pair, q_tile])

                raw_next = raw(0)
                for pair in range(pairs):
                    scores = raw_next
                    if ahead is not None:
                        bias = r.bias[...]
                        scores = scores + jnp.concatenate([bias, bias], axis=1)
                    if pair + 1 < pairs:
                        raw_next = raw(pair + 1)
                    old_top = r.top[pair : pair + 1, :]
                    new_top = jnp.maximum(old_top, jnp.max(scores, axis=0, keepdims=True))
                    weights = jnp.exp(scores - new_top)
                    shrink = jnp.exp(old_top - new_top)
                    r.top[pair : pair + 1, :] = new_top
                    r.total[pair : pair + 1, :] = r.total[
                        pair : pair + 1, :
                    ] * shrink + jnp.sum(weights, axis=0, keepdims=True)
                    low = weights.astype(bf16)
                    for side in range(2):
                        span = slice(side * TILE, (side + 1) * TILE)
                        head = slice((2 * pair + side) * 64, (2 * pair + side + 1) * 64)
                        r.turned[head, :] = r.turned[head, :] * shrink[:, span] + dot(
                            r.vt[k_tile, head, :], low[:, span]
                        )

            each_tile(tile_place(r, core, causal, q_tile, k_tile), one_tile)
            return inner

        lax.fori_loop(0, k_tiles, one_key_tile, 0)
        for pair in range(pairs):
            total = r.total[pair : pair + 1, :]
            r.lse[q_tile, pair : pair + 1, :] = r.top[pair : pair + 1, :] + jnp.log(total)
            share = 1.0 / total
            for side in range(2):
                span = slice(side * TILE, (side + 1) * TILE)
                head = slice((2 * pair + side) * 64, (2 * pair + side + 1) * 64)
                r.turned[head, :] = r.turned[head, :] * share[:, span]
        rows = pl.ds(pl.multiple_of(q_tile * TILE, TILE), TILE)
        r.att[rows, :] = jnp.transpose(r.turned[...]).astype(bf16)
        return carry

    lax.fori_loop(0, q_tiles, one_query_tile, 0)


def row_products(r, grad_att, pairs):
    low, high = pairs[0] * LANES, (pairs[-1] + 1) * LANES
    for tile in range(r.qm.shape[1]):
        rows = slice(tile * TILE, (tile + 1) * TILE)
        product = jnp.transpose(
            grad_att[rows, low:high].astype(f32) * r.att[rows, low:high].astype(f32)
        )
        for pair in pairs:
            for side in range(2):
                head = (2 * pair + side) * 64 - low
                r.delta[tile, pair : pair + 1, side * TILE : (side + 1) * TILE] = jnp.sum(
                    product[head : head + 64, :], axis=0, keepdims=True
                )


def attention_backward(r, core, causal, pairs):
    q_tiles, k_tiles = r.qm.shape[1], r.kt.shape[0]
    width = r.kt.shape[1]
    low, high = pairs[0] * LANES, (pairs[-1] + 1) * LANES
    for start in (0, width):
        r.dkv[:, start + low : start + high] = jnp.zeros((r.dkv.shape[0], high - low), f32)

    def one_query_tile(q_tile, carry):
        r.turned[low:high, :] = jnp.zeros((high - low, TILE), f32)

        def one_key_tile(k_tile, inner):
            def one_tile(ahead):
                if ahead is not None:
                    fill_bias(r, q_tile, k_tile, ahead)
                rows = pl.ds(pl.multiple_of(k_tile * TILE, TILE), TILE)

                def raw(pair):
                    lanes = slice(pair * LANES, (pair + 1) * LANES)
                    lanes_v = slice(width + pair * LANES, width + (pair + 1) * LANES)
                    return (
                        dot_nt(r.kv[rows, lanes], r.qm[pair, q_tile]),
                        dot_nt(r.kv[rows, lanes_v], r.gm[pair, q_tile]),
                    )

                raw_next = raw(pairs[0])
                for pair in pairs:
                    scores, grad_probs = raw_next
                    if ahead is not None:
                        bias = r.bias[...]
                        scores = scores + jnp.concatenate([bias, bias], axis=1)
                    if pair < pairs[-1]:
                        raw_next = raw(pair + 1)
                    probs = jnp.exp(scores - r.lse[q_tile, pair : pair + 1, :])
                    grad_scores = probs * (grad_probs - r.delta[q_tile, pair : pair + 1, :])
                    probs_low = probs.astype(bf16)
                    grad_low = grad_scores.astype(bf16)
                    lanes = slice(pair * LANES, (pair + 1) * LANES)
                    lanes_v = slice(width + pair * LANES, width + (pair + 1) * LANES)
                    r.dkv[rows, lanes] += dot(grad_low, r.qm[pair, q_tile])
                    r.dkv[rows, lanes_v] += dot(probs_low, r.gm[pair, q_tile])
                    for side in range(2):
                        span = slice(side * TILE, (side + 1) * TILE)
                        head = slice((2 * pair + side) * 64, (2 * pair + side + 1) * 64)
                        r.turned[head, :] += dot(r.kt[k_tile, head, :], grad_low[:, span])

            each_tile(tile_place(r, core, causal, q_tile, k_tile), one_tile)
            return inner

        lax.fori_loop(0, k_tiles, one_key_tile, 0)
        rows = pl.ds(pl.multiple_of(q_tile * TILE, TILE), TILE)
        r.dq[rows, low:high] = jnp.transpose(r.turned[low:high, :]) * (64**-0.5)
        return carry

    lax.fori_loop(0, q_tiles, one_query_tile, 0)


def feed_forward(r, low):
    chunks = [slice(at, at + CHUNK) for at in range(0, r.w_in.shape[1], CHUNK)]
    upward_next = dot(low[...], r.w_in[:, chunks[0]])
    for place, span in enumerate(chunks):
        upward = upward_next
        if place + 1 < len(chunks):
            upward_next = dot(low[...], r.w_in[:, chunks[place + 1]])
        gate = jax.nn.sigmoid(upward)
        active = (upward * gate).astype(bf16)
        r.act[:, span] = active
        r.slope[:, span] = (gate + upward * gate * (1.0 - gate)).astype(r.slope.dtype)
        part = dot(active, r.w_down[span, :])
        if place:
            r.sum[...] += part
        else:
            r.sum[...] = part


def feed_backward(r):
    chunks = [slice(at, at + CHUNK) for at in range(0, r.w_in.shape[1], CHUNK)]
    active_next = dot_nt(r.down_grad[...], r.w_down[chunks[0], :])
    for place, span in enumerate(chunks):
        grad_active = active_next.astype(bf16)
        if place + 1 < len(chunks):
            active_next = dot_nt(r.down_grad[...], r.w_down[chunks[place + 1], :])
        grad_up = (grad_active.astype(f32) * r.slope[:, span].astype(f32)).astype(bf16)
        r.up_grad[:, span] = grad_up
        part = dot_nt(grad_up, r.w_in[:, span])
        if place:
            r.sum[...] += part
        else:
            r.sum[...] = part


def self_forward(r):
    length, width = r.unit1.shape
    decoder, core = r.meta[0], r.meta[1]
    move = Copies(r.sems)
    whole = pl.ds(0, length)
    documents = load_documents(r, move, r.x_own_h, r.x_own_h, r.x_other_h)
    early = [
        move.start(r.x_own_h.at[whole], r.x.at[whole]),
        move.start(r.x_other_h.at[whole], r.x.at[pl.ds(length, length)]),
        move.start(r.w_mixed_h, r.w_mixed),
    ]
    later = [
        move.start(r.w_out_h, r.w_out),
        move.start(r.w_in_h, r.w_in),
        move.start(r.w_down_h, r.w_down),
    ]
    place_documents(r, documents)
    wait_all(early)
    r.q[...] = dot(r.x[:length, :], r.w_mixed[:, :width]).astype(bf16)
    r.kv[...] = dot(r.x[...], r.w_mixed[:, width:]).astype(bf16)
    outs = [move.start(r.q, r.q_o), move.start(r.kv, r.kv_o)]
    pairs = range(width // LANES)
    spread_pairs(r.qm, r.q, 64**-0.5, pairs)
    turn_tiles(r.vt, r.kv, width, pairs)
    attention_forward(r, core, decoder)
    wait_all(later)
    outs += [move.start(r.att, r.att_o), move.start(r.lse, r.lse_o)]
    unit, inverse = standardize(r.x[:length, :].astype(f32) + dot(r.att[...], r.w_out[...]))
    r.unit1[...] = unit
    r.inv1[...] = jnp.broadcast_to(inverse, r.inv1.shape)
    r.first_low[...] = (unit * r.gains[0:1, :]).astype(bf16)
    outs += [
        move.start(r.unit1, r.unit1_o),
        move.start(r.inv1, r.inv1_o),
        move.start(r.first_low, r.first_low_o),
    ]

    @pl.when(decoder == 0)
    def _():
        feed_forward(r, r.first_low)
        late = [
            move.start(r.first_low, r.ffn_low_o),
            move.start(r.act, r.act_o),
            move.start(r.slope, r.slope_o),
        ]
        unit2, inverse2 = standardize(r.unit1[...] * r.gains[0:1, :] + r.sum[...])
        r.memory[:length, :] = (unit2 * r.gains[1:2, :]).astype(bf16)
        r.memory[length:, :] = r.docs[0]
        late += [move.start(r.memory, r.memory_o)]
        r.unit2[...] = unit2
        r.inv2[...] = jnp.broadcast_to(inverse2, r.inv2.shape)
        late += [move.start(r.unit2, r.unit2_o), move.start(r.inv2, r.inv2_o)]
        wait_all(late)

    wait_all(outs)


def cross_both_ways(r):
    length, width = r.unit1_h.shape
    core = r.meta[1]
    move = Copies(r.sems)
    whole = pl.ds(0, length)
    documents = load_documents(r, move, r.x_own_h, r.memory_own_h, r.memory_other_h)
    moves = [
        move.start(r.memory_own_h.at[whole], r.x.at[whole]),
        move.start(r.memory_other_h.at[whole], r.x.at[pl.ds(length, length)]),
        move.start(r.w_pair_h, r.w_pair),
        move.start(r.first_low_h, r.first_low),
        move.start(r.w_query_h, r.w_query),
    ]
    later = [
        move.start(r.unit1_h, r.unit1),
        move.start(r.w_cross_h, r.w_cross),
        move.start(r.w_in_h, r.w_in),
        move.start(r.w_down_h, r.w_down),
        move.start(r.cot_h.at[r.micro], r.cot),
    ]
    place_documents(r, documents)
    wait_all(moves)
    r.kv[...] = dot(r.x[...], r.w_pair[...]).astype(bf16)
    r.q[...] = dot(r.first_low[...], r.w_query[...]).astype(bf16)
    pairs = range(width // LANES)
    spread_pairs(r.qm, r.q, 64**-0.5, pairs)
    turn_tiles(r.vt, r.kv, width, pairs)
    turn_tiles(r.kt, r.kv, 0, pairs)
    attention_forward(r, core, 0)
    outs = [move.start(r.att, r.att_o)]
    wait_all(later)
    first = r.unit1[...] * r.gains[0:1, :]
    unit, inverse = standardize(first + dot(r.att[...], r.w_cross[...]))
    r.unit2[...] = unit
    r.inv2[...] = jnp.broadcast_to(inverse, r.inv2.shape)
    r.second_low[...] = (unit * r.cross_gain[...]).astype(bf16)
    outs += [move.start(r.second_low, r.ffn_low_o)]
    feed_forward(r, r.second_low)
    outs += [move.start(r.act, r.act_o)]
    unit3, inverse3 = standardize(r.unit2[...] * r.cross_gain[...] + r.sum[...])
    r.decoded[...] = (unit3 * r.gains[1:2, :]).astype(bf16)
    outs += [move.start(r.decoded, r.decoded_o)]
    grad_third, gain_late = standardize_back(
        r.cot[...].astype(f32), unit3, r.gains[1:2, :], inverse3
    )
    r.keep[...] = grad_third
    r.down_grad[...] = grad_third.astype(bf16)
    outs += [move.start(r.down_grad, r.down_grad_o)]
    feed_backward(r)
    outs += [move.start(r.up_grad, r.up_grad_o)]
    grad_sum, gain_cross = standardize_back(
        r.keep[...] + r.sum[...], r.unit2[...], r.cross_gain[...], r.inv2[:, 0:1]
    )
    r.gain_grads[...] = jnp.zeros(r.gain_grads.shape, f32)
    r.gain_grads[0:1, :] = gain_late
    r.gain_grads[1:2, :] = gain_cross
    r.keep[...] = grad_sum
    r.branch[...] = grad_sum.astype(bf16)
    outs += [move.start(r.gain_grads, r.gain_grads_o), move.start(r.branch, r.branch_o)]
    r.q[...] = dot_nt(r.branch[...], r.w_cross[...]).astype(bf16)
    spread_pairs(r.gm, r.q, 1.0, pairs)
    row_products(r, r.q, pairs)
    attention_backward(r, core, 0, pairs)
    r.dq_low[...] = r.dq[...].astype(bf16)
    r.keep[...] += dot_nt(r.dq_low[...], r.w_query[...])
    outs += [move.start(r.dq_low, r.dq_low_o), move.start(r.keep, r.grad_first_o)]
    r.dkv_low[...] = r.dkv[...].astype(bf16)
    outs += [move.start(r.dkv_low, r.dkv_o)]
    part = dot_nt(r.dkv_low[...], r.w_pair[...])
    r.part_other[...] = part[length:, :].astype(bf16)
    r.part_own[...] = part[:length, :]
    outs += [move.start(r.part_other, r.part_other_o), move.start(r.part_own, r.part_own_o)]
    wait_all(outs)


def feed_backward_alone(r):
    move = Copies(r.sems)
    early = [
        move.start(r.grad_memory_h, r.cot),
        move.start(r.unit2_h, r.unit2),
        move.start(r.inv2_h, r.inv2),
    ]
    later = [
        move.start(r.w_down_h, r.w_down),
        move.start(r.slope_h, r.slope),
        move.start(r.w_in_h, r.w_in),
    ]
    wait_all(early)
    grad_third, gain_late = standardize_back(
        r.cot[...].astype(f32), r.unit2[...], r.gains[1:2, :], r.inv2[:, 0:1]
    )
    r.gain_grads[...] = jnp.broadcast_to(gain_late, r.gain_grads.shape)
    r.keep[...] = grad_third
    r.down_grad[...] = grad_third.astype(bf16)
    outs = [move.start(r.down_grad, r.down_grad_o), move.start(r.gain_grads, r.gain_late_o)]
    wait_all(later)
    feed_backward(r)
    outs += [move.start(r.up_grad, r.up_grad_o)]
    r.keep[...] += r.sum[...]
    outs += [move.start(r.keep, r.grad_first_o)]
    wait_all(outs)


def self_backward(r, plan):
    r.micro, first, last = plan
    length, width = r.att_h.shape
    decoder, core = r.meta[0], r.meta[1]
    pairs = range(first, last)
    low, high = first * LANES, last * LANES
    move = Copies(r.sems)
    later = [
        move.start(r.q_h, r.q),
        move.start(r.kv_h, r.kv),
        move.start(r.att_h, r.att),
        move.start(r.lse_h, r.lse),
    ]
    if first == 0:
        early = [
            move.start(r.grad_first_h, r.keep),
            move.start(r.unit1_h, r.unit1),
            move.start(r.inv1_h, r.inv1),
            move.start(r.w_out_h, r.w_out),
        ]
    else:
        early = [move.start(r.grad_att_h, r.grad_att)]
    outs = []
    place_documents(r, load_documents(r, move, r.x_own_h, r.x_own_h, r.x_other_h))
    wait_all(early)
    if first == 0:
        grad_sum, gain_early = standardize_back(
            r.keep[...], r.unit1[...], r.gains[0:1, :], r.inv1[:, 0:1]
        )
        r.gain_grads[...] = jnp.broadcast_to(gain_early, r.gain_grads.shape)
        r.keep[...] = grad_sum
        r.branch[...] = grad_sum.astype(bf16)
        r.grad_att[...] = dot_nt(r.branch[...], r.w_out[...]).astype(bf16)
        outs += [move.start(r.gain_grads, r.gain_early_o), move.start(r.branch, r.branch_o)]
        if last < width // LANES:
            outs += [move.start(r.keep, r.grad_sum_o), move.start(r.grad_att, r.grad_att_o)]
    wait_all(later)
    if last == width // LANES:
        ends = [move.start(r.w_mixed_h, r.w_mixed)]
        if first > 0:
            ends += [
                move.start(r.grad_sum_h, r.keep),
                move.start(r.dq_h.at[:, pl.ds(0, low)], r.dq_low.at[:, pl.ds(0, low)]),
                move.start(r.dkv_h.at[:, pl.ds(0, low)], r.dkv_low.at[:, pl.ds(0, low)]),
                move.start(
                    r.dkv_h.at[:, pl.ds(width, low)], r.dkv_low.at[:, pl.ds(width, low)]
                ),
            ]
    spread_pairs(r.qm, r.q, 64**-0.5, pairs)
    turn_tiles(r.kt, r.kv, 0, pairs)
    spread_pairs(r.gm, r.grad_att, 1.0, pairs)
    row_products(r, r.grad_att, pairs)
    attention_backward(r, core, decoder, pairs)
    r.dq_low[:, low:high] = r.dq[:, low:high].astype(bf16)
    for start in (0, width):
        span = slice(start + low, start + high)
        r.dkv_low[:, span] = r.dkv[:, span].astype(bf16)
    if last == width // LANES:
        wait_all(ends)
        outs += [move.start(r.dq_low, r.dq_low_o), move.start(r.dkv_low, r.dkv_o)]
        r.keep[...] += dot_nt(r.dq_low[...], r.w_mixed[:, :width])
        part = dot_nt(r.dkv_low[...], r.w_mixed[:, width:])
        r.part_other[...] = part[length:, :].astype(bf16)
        r.keep[...] += part[:length, :]
        outs += [move.start(r.part_other, r.part_other_o), move.start(r.keep, r.part_own_o)]
    else:
        outs.append(move.start(r.dq_low.at[:, pl.ds(low, high - low)], r.dq_low_o.at[:, pl.ds(low, high - low)]))
        for start in (0, width):
            span = pl.ds(start + low, high - low)
            outs.append(move.start(r.dkv_low.at[:, span], r.dkv_o.at[:, span]))
    wait_all(outs)


def contract_blocks(r, plan):
    for core in range(2):

        @pl.when(r.meta[1] == core)
        def _(core=core):
            targets = [None] * 4
            for half in range(2):
                target = r.kept_o if half == core else r.sent_o
                targets[2 * half], targets[2 * half + 1] = target.at[0], target.at[1]
            order = (0, 1, 2, 3) if core else (2, 3, 0, 1)
            contract_in_order(r, plan(r), order, targets, Copies(r.sems))


def contract_in_order(r, blocks, order, targets, move):
    loads = dict()
    for slot in order:
        for buffer, sources, at in blocks[slot][1:]:
            span = pl.ds(at * CHUNK, CHUNK)
            if buffer.shape[1] == 4 * CHUNK:
                at, span = 0, pl.ds(0, 4 * CHUNK)
            if (id(buffer), at) not in loads:
                row = 0
                copies = []
                for source in sources:
                    rows = pl.ds(row, source.shape[0])
                    copies.append(move.start(source.at[:, span], buffer.at[rows, span]))
                    row += source.shape[0]
                loads[id(buffer), at] = copies
    outs = []
    held = dict()
    for slot in order:
        turn, (left, _, left_at), (right, _, right_at) = blocks[slot]
        for buffer, at in ((left, left_at), (right, right_at)):
            at = 0 if buffer.shape[1] == 4 * CHUNK else at
            wait_all(loads.pop((id(buffer), at), ()))
        if held.get(id(turn)) != left_at:
            for row in range(0, left.shape[0], CHUNK):
                block = left[row : row + CHUNK, left_at * CHUNK : (left_at + 1) * CHUNK]
                turn[:, row : row + CHUNK] = jnp.transpose(block)
            held[id(turn)] = left_at
        block = right[:, right_at * CHUNK : (right_at + 1) * CHUNK]
        r.blocks[slot] = dot(turn[:, : right.shape[0]], block).astype(bf16)
        outs.append(move.start(r.blocks.at[slot], targets[slot]))
    wait_all(outs)


def spread_pieces(r, targets):
    z = r.meta[3]
    group, height = r.own_h.shape[:2]
    rows = r.own_h.shape[2] // group
    for core in range(2):
        for x in range(2):

            @pl.when((r.meta[1] == core) & (r.meta[2] == x))
            def _(core=core, x=x):
                move = Copies(r.sems)
                parts = [
                    (r.own_h, core, x),
                    (r.own_x_h, core, 1 - x),
                    (r.other_h, 1 - core, x),
                    (r.other_x_h, 1 - core, 1 - x),
                ]
                loads = [
                    move.start(source, r.pieces.at[place])
                    for place, (source, _, _) in enumerate(parts)
                ]
                outs = []
                slot = 0
                gains = []
                for place, (_, half, side) in enumerate(parts):
                    loads[place].wait()
                    for step in range(group):
                        row = pl.multiple_of(lax.rem(z + (group - step), group) * rows, rows)
                        start = 0
                        for target in targets(r, 2 * half + side, row, rows):
                            r.wide[slot] = r.pieces[place, step, start : start + rows].astype(f32)
                            outs.append(move.start(r.wide.at[slot], target))
                            slot += 1
                            start += rows
                        if start < height:
                            gains.append(r.pieces[place, step, start:height].astype(f32))
                if gains:
                    r.gains_o[...] = sum(gains)[: r.gains_o.shape[0], :]
                wait_all(outs)


def launch(kernel, plan, side, scalars, small, large, outs, scratch, copies, work, previous=None, after=()):
    names = list(scalars) + list(small) + list(large)
    arrays = list(scalars.values()) + list(small.values()) + list(large.values())
    specs = (
        [pl.BlockSpec(memory_space=pltpu.SMEM)] * len(scalars)
        + [pl.BlockSpec(memory_space=pltpu.VMEM)] * len(small)
        + [pl.BlockSpec(memory_space=pl.ANY)] * len(large)
    )
    aliases = dict()
    for position, name in enumerate(outs):
        if previous and name in previous:
            aliases[len(arrays)] = position
            names.append("previous_" + name)
            arrays.append(previous[name])
            specs.append(pl.BlockSpec(memory_space=pl.ANY))
    for array in after:
        names.append("")
        arrays.append(array)
        specs.append(pl.BlockSpec(memory_space=pl.ANY))
    names += list(outs) + list(scratch) + ["sems"]

    def body(*refs):
        r = types.SimpleNamespace(**dict(zip(names, refs)))

        def run():
            if isinstance(plan, int):
                r.micro = plan
                kernel(r)
            else:
                kernel(r, plan)

        if side is None:
            run()
        else:
            pl.when(r.meta[0] == side)(run)

    results = pl.pallas_call(
        body,
        out_shape=[jax.ShapeDtypeStruct(*shape) for shape in outs.values()],
        in_specs=specs,
        out_specs=[
            pl.BlockSpec(memory_space=pltpu.VMEM if shape[0][0] < 8 else pl.ANY)
            for shape in outs.values()
        ],
        scratch_shapes=[
            pltpu.SMEM(*shape) if shape[1] == jnp.int32 else pltpu.VMEM(*shape)
            for shape in scratch.values()
        ]
        + [pltpu.SemaphoreType.DMA((copies,))],
        input_output_aliases=aliases,
        compiler_params=pltpu.CompilerParams(vmem_limit_bytes=58 * 1024 * 1024),
        cost_estimate=pl.CostEstimate(
            flops=work * 10**9, bytes_accessed=1 << 20, transcendentals=0
        ),
    )(*arrays)
    return types.SimpleNamespace(**dict(zip(outs, results)))


def attention_scratch(length, width):
    pairs, q_tiles, k_tiles = width // LANES, length // TILE, 2 * length // TILE
    return dict(
        q=((length, width), bf16),
        kv=((2 * length, 2 * width), bf16),
        qm=((pairs, q_tiles, 2 * TILE, LANES), bf16),
        kdc=((2 * length, LANES), f32),
        docs=((3, 16, width), bf16),
        qd=((length // TILE, 8, TILE), f32),
        bounds=((2, 3 * length // TILE), jnp.int32),
        bias=((TILE, TILE), f32),
        lse=((q_tiles, 8, 2 * TILE), f32),
        att=((length, width), bf16),
        turned=((width, TILE), f32),
    )


def forward_scratch(length, width):
    k_tiles = 2 * length // TILE
    return dict(
        vt=((k_tiles, width, TILE), bf16),
        top=((8, 2 * TILE), f32),
        total=((8, 2 * TILE), f32),
    )


def backward_scratch(length, width):
    pairs, q_tiles, k_tiles = width // LANES, length // TILE, 2 * length // TILE
    return dict(
        kt=((k_tiles, width, TILE), bf16),
        gm=((pairs, q_tiles, 2 * TILE, LANES), bf16),
        delta=((q_tiles, 8, 2 * TILE), f32),
        dkv=((2 * length, 2 * width), f32),
        dq=((length, width), f32),
        dkv_low=((2 * length, 2 * width), bf16),
        part_other=((length, width), bf16),
        dq_low=((length, width), bf16),
    )


def for_sending(shard):

    def short(part):
        return part.astype(jnp.bfloat16) if part.dtype == jnp.float32 else part

    return jax.tree.map(short, shard)


def from_behind(block, axis, distance):
    devices = range(lax.axis_size(axis))
    route = [(i - distance, i) for i in devices if i - distance in devices]
    return lax.ppermute(block, axis, route)


def from_root(shard, axis, root):
    mine = lax.axis_index(axis) == root
    return lax.psum(jnp.where(mine, shard, jnp.zeros_like(shard)), axis)


def matmul(left_side, right_side):
    return jnp.einsum("rsd,de->rse", left_side, right_side, preferred_element_type=jnp.float32)


def matmul_back(left_side, right_side):
    return jnp.einsum("rse,de->rsd", left_side, right_side, preferred_element_type=jnp.float32)


def contract(left_side, right_side):
    return jnp.einsum("rsd,rse->de", left_side, right_side, preferred_element_type=jnp.float32)


def normalize(values, gain_row):
    center = values - jnp.mean(values, axis=-1, keepdims=True)
    inverse = lax.rsqrt(jnp.mean(center * center, axis=-1, keepdims=True) + epsilon)
    standard = center * inverse
    return (standard * gain_row, standard, inverse)


def normalize_back(grad_out, standard, gain_row, inverse):
    scaled = grad_out * gain_row
    grad_in = inverse * (
        scaled
        - jnp.mean(scaled, axis=-1, keepdims=True)
        - standard * jnp.mean(scaled * standard, axis=-1, keepdims=True)
    )
    return (grad_in, jnp.sum(grad_out * standard, axis=(0, 1)))


def allowed_mask(query_docs, key_docs, query_place, key_place, causal):
    same_doc = query_docs[:, :, None] == key_docs[:, None, :]
    earlier = query_place[:, None] >= key_place[None, :]
    return (same_doc & (earlier | jnp.logical_not(causal)))[:, None]


def attend(queries, keys_local, values_local, query_docs, key_docs, causal, is_cross):
    rows_here, shard_len, model_width = queries.shape
    head_dim = model_width // HEADS
    score_scale = head_dim ** (-0.5)
    query_place = lax.axis_index("seq") * shard_len + jnp.arange(shard_len)
    query_heads = queries.reshape(rows_here, shard_len, HEADS, head_dim)

    def absorb(state_tuple, pieces):
        running_top, running_total, running_sum = state_tuple
        key_piece, value_piece, doc_piece = pieces
        piece_len = key_piece.shape[1]
        raw_scores = jnp.einsum(
            "rqhd,rkhd->rhqk",
            query_heads,
            key_piece.reshape(rows_here, piece_len, HEADS, head_dim),
            preferred_element_type=jnp.float32,
        )
        allowed = allowed_mask(query_docs, doc_piece, query_place, jnp.arange(piece_len), causal)
        scores = jnp.where(allowed, raw_scores * score_scale, negative_big)
        new_top = jnp.maximum(running_top, jnp.max(scores, axis=-1))
        weights = jnp.where(allowed, jnp.exp(scores - new_top[..., None]), 0.0)
        new_total = jnp.sum(weights, axis=-1)
        product = jnp.einsum(
            "rhqk,rkhd->rhqd",
            weights.astype(jnp.bfloat16),
            value_piece.reshape(rows_here, piece_len, HEADS, head_dim),
            preferred_element_type=jnp.float32,
        )
        return (new_top, new_total, product)

    init_state = (
        jnp.full((rows_here, HEADS, shard_len), negative_big, jnp.float32),
        jnp.zeros((rows_here, HEADS, shard_len), jnp.float32),
        jnp.zeros((rows_here, HEADS, shard_len, head_dim), jnp.float32),
    )
    if is_cross:
        final_top, final_total, final_sum = absorb(
            init_state,
            (
                lax.all_gather(keys_local, "seq", axis=1, tiled=True),
                lax.all_gather(values_local, "seq", axis=1, tiled=True),
                lax.all_gather(for_sending(key_docs), "seq", axis=1, tiled=True),
            ),
        )
    else:
        final_top, final_total, final_sum = absorb(
            init_state,
            (
                lax.all_gather(keys_local, "seq", axis=1, tiled=True),
                lax.all_gather(values_local, "seq", axis=1, tiled=True),
                lax.all_gather(key_docs, "seq", axis=1, tiled=True),
            ),
        )
    attended = (
        (final_sum / final_total[..., None])
        .transpose(0, 2, 1, 3)
        .reshape(rows_here, shard_len, model_width)
    )
    return (attended, final_top + jnp.log(final_total))


def attend_back(
    queries,
    keys_local,
    values_local,
    query_docs,
    key_docs,
    causal,
    log_total,
    grad_attended,
    is_cross,
):
    rows_here, shard_len, model_width = queries.shape
    head_dim = model_width // HEADS
    score_scale = head_dim ** (-0.5)
    query_place = lax.axis_index("seq") * shard_len + jnp.arange(shard_len)
    if is_cross:
        keys_full, values_full, docs_full = (
            lax.all_gather(keys_local, "seq", axis=1, tiled=True),
            lax.all_gather(values_local, "seq", axis=1, tiled=True),
            lax.all_gather(for_sending(key_docs), "seq", axis=1, tiled=True).astype(key_docs.dtype),
        )
    else:
        keys_full, values_full, docs_full = (
            lax.all_gather(keys_local, "seq", axis=1, tiled=True),
            lax.all_gather(values_local, "seq", axis=1, tiled=True),
            lax.all_gather(key_docs, "seq", axis=1, tiled=True),
        )
    full_len = keys_full.shape[1]
    query_heads = queries.reshape(rows_here, shard_len, HEADS, head_dim)
    key_heads = keys_full.reshape(rows_here, full_len, HEADS, head_dim)
    value_heads = values_full.reshape(rows_here, full_len, HEADS, head_dim)
    grad_heads = grad_attended.reshape(rows_here, shard_len, HEADS, head_dim)
    raw_scores = jnp.einsum(
        "rqhd,rkhd->rhqk", query_heads, key_heads, preferred_element_type=jnp.float32
    )
    allowed = allowed_mask(query_docs, docs_full, query_place, jnp.arange(full_len), causal)
    shifted = jnp.where(allowed, raw_scores * score_scale - log_total[..., None], negative_big)
    probs = jnp.where(allowed, jnp.exp(shifted), 0.0)
    grad_probs = jnp.einsum(
        "rqhd,rkhd->rhqk", grad_heads, value_heads, preferred_element_type=jnp.float32
    )
    delta = jnp.sum(probs * grad_probs, axis=-1)
    grad_scores = (probs * (grad_probs - delta[..., None]) * score_scale).astype(jnp.bfloat16)
    grad_queries = jnp.einsum(
        "rhqk,rkhd->rqhd", grad_scores, key_heads, preferred_element_type=jnp.float32
    ).reshape(rows_here, shard_len, model_width)
    probs_low = probs.astype(jnp.bfloat16)

    def key_terms(span):
        grad_keys = jnp.einsum(
            "rhqk,rqhd->krhd", grad_scores, query_heads, preferred_element_type=jnp.float32
        )
        grad_values = jnp.einsum(
            "rhqk,rqhd->krhd", probs_low, grad_heads, preferred_element_type=jnp.float32
        )
        return jnp.concatenate(
            [
                grad_keys.reshape(span, rows_here, model_width),
                grad_values.reshape(span, rows_here, model_width),
            ],
            axis=-1,
        )

    if is_cross:
        pair_terms = lax.psum_scatter(
            key_terms(shard_len * lax.axis_size("seq")).astype(jnp.bfloat16),
            "seq",
            scatter_dimension=0,
            tiled=True,
        ).astype(jnp.float32)
    else:
        pair_terms = lax.psum_scatter(
            key_terms(shard_len * lax.axis_size("seq")).astype(jnp.bfloat16),
            "seq",
            scatter_dimension=0,
            tiled=True,
        ).astype(jnp.float32)
    return (grad_queries, pair_terms.transpose(1, 0, 2))


def layer_forward(hidden_in, doc_own, memory, memory_docs, weights, is_decoder):
    (
        qkv_weight,
        out_weight,
        in_weight,
        down_weight,
        gains_pair,
        query_weight,
        pair_weight,
        cross_weight,
        cross_gains,
    ) = weights
    model_width = hidden_in.shape[-1]
    mixed = matmul(hidden_in, qkv_weight).astype(jnp.bfloat16)
    attended, self_lse = attend(
        mixed[..., :model_width],
        mixed[..., model_width : 2 * model_width],
        mixed[..., 2 * model_width :],
        doc_own,
        doc_own,
        is_decoder,
        False,
    )
    attended = attended.astype(jnp.bfloat16)
    first, first_unit, first_inv = normalize(
        hidden_in.astype(jnp.float32) + matmul(attended, out_weight), gains_pair[0]
    )
    first_low = first.astype(jnp.bfloat16)
    cross_queries = matmul(first_low, query_weight).astype(jnp.bfloat16)
    pair = matmul(memory, pair_weight).astype(jnp.bfloat16)
    cross_att, cross_lse = attend(
        cross_queries,
        pair[..., :model_width],
        pair[..., model_width:],
        doc_own,
        memory_docs,
        False,
        True,
    )
    cross_att = cross_att.astype(jnp.bfloat16)
    second_cross, second_unit, second_inv = normalize(
        first + matmul(cross_att, cross_weight), cross_gains
    )
    second = jnp.where(is_decoder, second_cross, first)
    second_low = second.astype(jnp.bfloat16)
    upward = matmul(second_low, in_weight)
    active = jax.nn.silu(upward).astype(jnp.bfloat16)
    result, third_unit, third_inv = normalize(second + matmul(active, down_weight), gains_pair[1])
    saved = {
        "mixed": mixed,
        "attended": attended,
        "self_lse": self_lse,
        "first_unit": first_unit,
        "first_inv": first_inv,
        "first_low": first_low,
        "cross_queries": cross_queries,
        "pair": pair,
        "cross_att": cross_att,
        "cross_lse": cross_lse,
        "second_unit": second_unit,
        "second_inv": second_inv,
        "second_low": second_low,
        "upward": upward,
        "active": active,
        "third_unit": third_unit,
        "third_inv": third_inv,
    }
    return (result, saved)


def layer_backward(
    grad_result, saved, hidden_in, doc_own, memory, memory_docs, weights, is_decoder
):
    (
        qkv_weight,
        out_weight,
        in_weight,
        down_weight,
        gains_pair,
        query_weight,
        pair_weight,
        cross_weight,
        cross_gains,
    ) = weights
    model_width = hidden_in.shape[-1]
    grad_third, grad_gain_late = normalize_back(
        grad_result, saved["third_unit"], gains_pair[1], saved["third_inv"]
    )
    down_grad = grad_third.astype(jnp.bfloat16)
    grad_down_w = contract(saved["active"], down_grad)
    grad_active = matmul_back(down_grad, down_weight).astype(jnp.bfloat16)
    sigmoid_up = jax.nn.sigmoid(saved["upward"])
    grad_upward = (
        grad_active.astype(jnp.float32)
        * (sigmoid_up + saved["upward"] * sigmoid_up * (1.0 - sigmoid_up))
    ).astype(jnp.bfloat16)
    grad_in_w = contract(saved["second_low"], grad_upward)
    grad_second = grad_third + matmul_back(grad_upward, in_weight)
    grad_cross_sum, grad_cross_gain = normalize_back(
        grad_second, saved["second_unit"], cross_gains, saved["second_inv"]
    )
    decoder_flag = is_decoder.astype(jnp.float32)
    grad_cross_sum = grad_cross_sum * decoder_flag
    grad_cross_gain = grad_cross_gain * decoder_flag
    cross_branch = grad_cross_sum.astype(jnp.bfloat16)
    grad_cross_w = contract(saved["cross_att"], cross_branch)
    grad_cross_att = matmul_back(cross_branch, cross_weight).astype(jnp.bfloat16)
    pair = saved["pair"]
    grad_cross_q, grad_pair = attend_back(
        saved["cross_queries"],
        pair[..., :model_width],
        pair[..., model_width:],
        doc_own,
        memory_docs,
        False,
        saved["cross_lse"],
        grad_cross_att,
        True,
    )
    grad_cross_q = grad_cross_q.astype(jnp.bfloat16)
    grad_pair = grad_pair.astype(jnp.bfloat16)
    grad_query_w = contract(saved["first_low"], grad_cross_q)
    grad_pair_w = contract(memory, grad_pair)
    grad_memory = matmul_back(grad_pair, pair_weight)
    grad_first = jnp.where(
        is_decoder, grad_cross_sum + matmul_back(grad_cross_q, query_weight), grad_second
    )
    grad_first_sum, grad_gain_early = normalize_back(
        grad_first, saved["first_unit"], gains_pair[0], saved["first_inv"]
    )
    self_branch = grad_first_sum.astype(jnp.bfloat16)
    grad_out_w = contract(saved["attended"], self_branch)
    grad_attended = matmul_back(self_branch, out_weight).astype(jnp.bfloat16)
    mixed = saved["mixed"]
    grad_queries, grad_pair_self = attend_back(
        mixed[..., :model_width],
        mixed[..., model_width : 2 * model_width],
        mixed[..., 2 * model_width :],
        doc_own,
        doc_own,
        is_decoder,
        saved["self_lse"],
        grad_attended,
        False,
    )
    grad_mixed = jnp.concatenate([grad_queries, grad_pair_self], axis=-1).astype(jnp.bfloat16)
    grad_qkv_w = contract(hidden_in, grad_mixed)
    grad_hidden = grad_first_sum + matmul_back(grad_mixed, qkv_weight)
    layer_grads = (
        grad_qkv_w,
        grad_out_w,
        grad_in_w,
        grad_down_w,
        jnp.stack([grad_gain_early, grad_gain_late]),
        grad_query_w,
        grad_pair_w,
        grad_cross_w,
        grad_cross_gain,
    )
    return (grad_hidden, grad_memory, layer_grads)


def any_rows(
    layer_input,
    segment_ids,
    attn_qkv,
    attn_out,
    ffn_in,
    ffn_out,
    norm_gain,
    cross_query,
    cross_pair,
    cross_out,
    cross_gain,
    out_cotangent,
):
    micro_count = layer_input.shape[1]
    section_index = lax.axis_index("section")
    is_decoder = section_index == 1
    weights = (
        attn_qkv[0],
        attn_out[0],
        ffn_in[0],
        ffn_out[0],
        norm_gain[0],
        cross_query,
        cross_pair,
        cross_out,
        cross_gain,
    )
    inputs_all = layer_input[0]
    docs_all = segment_ids[0]
    slot_ids = jnp.arange(micro_count)
    received = (jnp.zeros_like(inputs_all[0]), jnp.zeros_like(docs_all[0]))
    results = jnp.zeros_like(inputs_all)
    memories = []
    memory_doc_list = []
    for step_index in range(micro_count + 1):
        batch_index = step_index - section_index
        is_valid = (batch_index >= 0) & (batch_index < micro_count)
        chosen = jnp.clip(batch_index, 0, micro_count - 1)
        hidden_in = lax.dynamic_index_in_dim(inputs_all, chosen, 0, keepdims=False)
        doc_own = lax.dynamic_index_in_dim(docs_all, chosen, 0, keepdims=False)
        memory = received[0]
        memory_docs = jnp.where(is_valid & is_decoder, received[1], doc_own)
        memories.append(memory)
        memory_doc_list.append(memory_docs)
        result, saved = layer_forward(hidden_in, doc_own, memory, memory_docs, weights, is_decoder)
        low_result = result.astype(jnp.bfloat16)
        writing = (slot_ids == chosen) & is_valid
        results = jnp.where(writing[:, None, None, None], low_result[None], results)
        if step_index < micro_count:
            received = from_behind((low_result, doc_own), "section", 1)
    memory_stack = jnp.stack(memories)
    memory_doc_stack = jnp.stack(memory_doc_list)
    totals = tuple((jnp.zeros(weight.shape, jnp.float32) for weight in weights))
    input_grads = jnp.zeros(inputs_all.shape, jnp.float32)
    returned = jnp.zeros(inputs_all.shape[1:], jnp.float32)
    for step_index in range(micro_count + 1):
        batch_index = micro_count - step_index - section_index
        is_valid = (batch_index >= 0) & (batch_index < micro_count)
        chosen = jnp.clip(batch_index, 0, micro_count - 1)
        forward_step = jnp.clip(batch_index + section_index, 0, micro_count)
        hidden_in = lax.dynamic_index_in_dim(inputs_all, chosen, 0, keepdims=False)
        doc_own = lax.dynamic_index_in_dim(docs_all, chosen, 0, keepdims=False)
        memory = lax.dynamic_index_in_dim(memory_stack, forward_step, 0, keepdims=False)
        memory_docs = lax.dynamic_index_in_dim(memory_doc_stack, forward_step, 0, keepdims=False)
        discarded, saved = layer_forward(
            hidden_in, doc_own, memory, memory_docs, weights, is_decoder
        )
        cotangent = jnp.where(
            is_decoder,
            lax.dynamic_index_in_dim(out_cotangent, chosen, 0, keepdims=False).astype(jnp.float32),
            returned,
        )
        grad_hidden, grad_memory, layer_grads = layer_backward(
            cotangent, saved, hidden_in, doc_own, memory, memory_docs, weights, is_decoder
        )
        valid_flag = is_valid.astype(jnp.float32)
        totals = tuple(
            (running + valid_flag * fresh for running, fresh in zip(totals, layer_grads))
        )
        writing = (slot_ids == chosen) & is_valid
        input_grads = jnp.where(writing[:, None, None, None], grad_hidden[None], input_grads)
        if step_index < micro_count:
            returned = from_behind(grad_memory.astype(jnp.bfloat16), "section", -1).astype(
                grad_memory.dtype
            )
    group_sums = lax.psum(
        (
            totals[0],
            totals[1],
            totals[2],
            totals[3],
            totals[4],
            totals[5],
            totals[6],
            totals[7],
            totals[8],
        ),
        ("seq", "dp"),
    )
    section_sums = group_sums[:5]
    cross_sums = (
        from_root(group_sums[5].astype(jnp.bfloat16), "section", 1).astype(jnp.float32),
        from_root(group_sums[6].astype(jnp.bfloat16), "section", 1).astype(jnp.float32),
        from_root(group_sums[7].astype(jnp.bfloat16), "section", 1).astype(jnp.float32),
        from_root(group_sums[8].astype(jnp.bfloat16), "section", 1).astype(jnp.float32),
    )
    return (
        results[None],
        input_grads[None],
        section_sums[0][None],
        section_sums[1][None],
        section_sums[2][None],
        section_sums[3][None],
        section_sums[4][None],
        cross_sums[0],
        cross_sums[1],
        cross_sums[2],
        cross_sums[3],
    )


def split_rows(
    layer_input,
    segment_ids,
    attn_qkv,
    attn_out,
    ffn_in,
    ffn_out,
    norm_gain,
    cross_query,
    cross_pair,
    cross_out,
    cross_gain,
    out_cotangent,
):
    micros = layer_input.shape[1]
    length, width = layer_input.shape[3:]
    hidden = ffn_in.shape[-1]
    q_tiles = length // TILE
    group = lax.axis_size("dp") // 2
    axes = ("section", "seq", "dp")
    decoder = lax.axis_index("section") == 1
    flag = decoder.astype(jnp.int32)
    x = lax.axis_index("seq")
    core = lax.rem(lax.axis_index("dp"), 2)
    z = lax.axis_index("dp") // 2
    places = [(t, i, k, c) for t in range(2) for i in range(2) for k in range(group) for c in range(2)]

    def number(t, i, k, c):
        return ((t * 2 + i) * group + k) * 2 + c

    def send(values, target, section=None):
        route = [
            (number(*place), number(*target(*place)))
            for place in places
            if section in (None, place[0]) and target(*place)
        ]
        return lax.ppermute(values, axes, route)

    def to_core(t, i, k, c):
        return (t, i, k, 1 - c)

    def to_x(t, i, k, c):
        return (t, 1 - i, k, c)

    def to_row(t, i, k, c):
        return (t, c, k, i)

    def to_decoder(t, i, k, c):
        return (1, i, k, c) if t == 0 else None

    def to_encoder(t, i, k, c):
        return (0, i, k, c) if t == 1 else None

    def fence(values, *before):
        return lax.optimization_barrier((values,) + before)[0]

    def exchange(values):
        return send(values, to_core)

    low = ((length, width), bf16)
    wide = ((length, width), f32)
    marked = ((length + 16, width), bf16)
    both = ((2 * length, width), bf16)
    keys_all = ((2 * length, 2 * width), bf16)
    mixing = ((width, 3 * width), bf16)
    inner = ((length, hidden), bf16)
    lse = ((q_tiles, 8, 2 * TILE), f32)
    stat = ((length, LANES), f32)
    square = ((width, width), bf16)
    rising = ((width, hidden), bf16)
    falling = ((hidden, width), bf16)
    gain_rows = ((8, width), f32)

    meta = jnp.stack([flag, core, x, z]).astype(jnp.int32)
    numbers = segment_ids[0, :, 0].astype(bf16)
    padding = jnp.zeros((15, width), bf16)
    with_numbers = [
        jnp.concatenate([layer_input[0, micro, 0], numbers[micro][None], padding])
        for micro in range(micros)
    ]
    own = [send(with_numbers[0], to_row)]
    for micro in range(1, micros):
        own.append(send(fence(with_numbers[micro], own[-1]), to_row))
    other = [exchange(own[0])]

    plain = dict(meta=meta)
    small = dict(gains=norm_gain[0])
    forward, memories, memories_other = [], [], []
    for micro in range(micros):
        call = launch(
            self_forward,
            micro,
            None,
            plain,
            small,
            dict(
                x_own_h=own[micro],
                x_other_h=other[micro],
                w_mixed_h=attn_qkv[0],
                w_out_h=attn_out[0],
                w_in_h=ffn_in[0],
                w_down_h=ffn_out[0],
            ),
            dict(
                q_o=low,
                kv_o=keys_all,
                att_o=low,
                lse_o=lse,
                unit1_o=wide,
                inv1_o=stat,
                first_low_o=low,
                memory_o=marked,
                ffn_low_o=low,
                act_o=inner,
                slope_o=inner,
                unit2_o=wide,
                inv2_o=stat,
            ),
            dict(
                **attention_scratch(length, width),
                **forward_scratch(length, width),
                x=both,
                w_mixed=mixing,
                w_out=square,
                w_in=rising,
                w_down=falling,
                unit1=wide,
                inv1=stat,
                first_low=low,
                memory=marked,
                act=inner,
                slope=inner,
                unit2=wide,
                inv2=stat,
                sum=wide,
            ),
            28,
            26,
            after=(forward[0].lse_o,) if micro else (),
        )
        forward.append(call)
        memories.append(send(call.memory_o, to_decoder))
        if micro + 1 < micros:
            other.append(exchange(fence(own[micro + 1], call.lse_o)))

    for micro in range(micros):
        memories_other.append(exchange(fence(memories[micro], forward[-1].lse_o)))
    cotangent = send(fence(out_cotangent[:, 0], forward[0].lse_o), to_row)

    cross, grads_memory, made = [], [], []
    after = (forward[-1].lse_o,)
    for micro in range(micros):
        done = forward[micro]
        call = launch(
            cross_both_ways,
            micro,
            1,
            plain,
            dict(**small, cross_gain=cross_gain[None]),
            dict(
                x_own_h=own[micro],
                memory_own_h=memories[micro],
                memory_other_h=memories_other[micro],
                w_pair_h=cross_pair,
                first_low_h=done.first_low_o,
                unit1_h=done.unit1_o,
                w_query_h=cross_query,
                w_cross_h=cross_out,
                w_in_h=ffn_in[0],
                w_down_h=ffn_out[0],
                cot_h=cotangent,
            ),
            dict(
                att_o=low,
                ffn_low_o=low,
                act_o=inner,
                decoded_o=low,
                down_grad_o=low,
                up_grad_o=inner,
                gain_grads_o=gain_rows,
                branch_o=low,
                dq_low_o=low,
                dkv_o=keys_all,
                part_own_o=wide,
                part_other_o=low,
                grad_first_o=wide,
            ),
            dict(
                **attention_scratch(length, width),
                **forward_scratch(length, width),
                **backward_scratch(length, width),
                x=both,
                w_pair=((width, 2 * width), bf16),
                first_low=low,
                unit1=wide,
                w_query=square,
                w_cross=square,
                w_in=rising,
                w_down=falling,
                cot=low,
                unit2=wide,
                inv2=stat,
                second_low=low,
                act=inner,
                slope=inner,
                sum=wide,
                decoded=low,
                keep=wide,
                down_grad=low,
                up_grad=inner,
                gain_grads=gain_rows,
                branch=low,
                part_own=wide,
            ),
            36,
            44,
            dict(act_o=done.act_o, ffn_low_o=done.ffn_low_o),
            after,
        )
        cross.append(call)
        away = call.part_other_o
        if micro:
            away = fence(away, grads_memory[-1])
        total = call.part_own_o + exchange(away).astype(f32)
        made.append(total.astype(bf16))
        after = (made[micro],)
        grads_memory.append(send(made[micro], to_encoder))

    def backward_feed(micro, after):
        done, late = forward[micro], cross[micro]
        return launch(
            feed_backward_alone,
            micro,
            0,
            plain,
            dict(gains=norm_gain[0]),
            dict(
                grad_memory_h=grads_memory[micro],
                unit2_h=done.unit2_o,
                inv2_h=done.inv2_o,
                slope_h=done.slope_o,
                w_in_h=ffn_in[0],
                w_down_h=ffn_out[0],
            ),
            dict(gain_late_o=gain_rows, down_grad_o=low, up_grad_o=inner, grad_first_o=wide),
            dict(
                cot=low,
                unit2=wide,
                inv2=stat,
                slope=inner,
                w_in=rising,
                w_down=falling,
                gain_grads=gain_rows,
                keep=wide,
                down_grad=low,
                up_grad=inner,
                sum=wide,
            ),
            12,
            10,
            dict(
                down_grad_o=late.down_grad_o, up_grad_o=late.up_grad_o, grad_first_o=late.grad_first_o
            ),
            after,
        )

    def backward_self(micro, side, grad_first, previous=None, after=(), halfway=None):
        done = forward[micro]
        heads = width // LANES
        given = dict(
            x_own_h=own[micro],
            x_other_h=other[micro],
            q_h=done.q_o,
            kv_h=done.kv_o,
            att_h=done.att_o,
            lse_h=done.lse_o,
        )
        ahead = dict(
            grad_first_h=grad_first,
            unit1_h=done.unit1_o,
            inv1_h=done.inv1_o,
            w_out_h=attn_out[0],
        )
        makes = dict(dq_low_o=low, dkv_o=keys_all)
        makes_first = dict(gain_early_o=gain_rows, branch_o=low)
        makes_last = dict(part_own_o=wide, part_other_o=low)
        scratch = dict(
            **attention_scratch(length, width),
            **backward_scratch(length, width),
            w_out=square,
            w_mixed=mixing,
            unit1=wide,
            inv1=stat,
            keep=wide,
            branch=low,
            grad_att=low,
            gain_grads=gain_rows,
        )

        def part(first, last, large, outs, work, previous, after):
            return launch(
                self_backward,
                (micro, first, last),
                side,
                plain,
                small,
                dict(**given, **large),
                dict(**makes, **outs),
                scratch,
                28,
                work,
                previous,
                after,
            )

        if halfway is None:
            large = dict(**ahead, w_mixed_h=attn_qkv[0])
            outs = dict(**makes_first, **makes_last)
            return part(0, heads, large, outs, 22, previous, after)
        outs = dict(**makes_first, grad_sum_o=wide, grad_att_o=low)
        one = part(0, heads // 2, ahead, outs, 12, None, after)
        large = dict(
            w_mixed_h=attn_qkv[0],
            grad_sum_h=one.grad_sum_o,
            grad_att_h=one.grad_att_o,
            dq_h=one.dq_low_o,
            dkv_h=one.dkv_o,
        )
        two = part(heads // 2, heads, large, makes_last, 12, None, halfway(one))
        return types.SimpleNamespace(**{**vars(one), **vars(two)})

    def weight_grads(plan, side, arrays, scratch, after=()):
        blocks = ((2, width, width), bf16)
        call = launch(
            contract_blocks,
            plan,
            side,
            plain,
            dict(),
            arrays,
            dict(sent_o=blocks, kept_o=blocks),
            dict(**scratch, blocks=((4, width, width), bf16)),
            36,
            8,
            after=after,
        )
        return call.sent_o, call.kept_o

    def first_sums(halves, section=None):
        sent, kept = halves
        got = send(sent, to_core, section)

        def block(side):
            return sum(
                lax.dynamic_index_in_dim(part, side, 0, keepdims=False).astype(f32)
                for part in (kept, got)
            )

        return block(1 - x).astype(bf16), block(x)

    def middle_sums(sums, section=None):
        away, total = sums
        return (total + send(away, to_x, section).astype(f32)).astype(bf16)

    def last_sums(total, later=(), section=None):
        shares = total.reshape(group, width // group, width)

        def share(step):
            return lax.dynamic_index_in_dim(shares, lax.rem(z + step, group), 0, keepdims=False)

        parts = [share(0)]
        for step in range(1, group):
            parts.append(send(share(step), along_z(step), section))
        if later:
            parts = [fence(part, *later) for part in parts]
        return sum(part.astype(f32) for part in parts).astype(bf16)

    def along_z(step):
        return lambda t, i, k, c: (t, i, (k + step) % group, c)

    def gather_z(share):
        return [share] + [send(share, along_z(step)) for step in range(1, group)]

    def gain_block(rows):
        filled = jnp.concatenate([jnp.stack(rows), jnp.zeros((16 - len(rows), width), f32)])
        return filled.astype(bf16)

    def spread(targets, own, own_x, outs, parts):
        return launch(
            spread_pieces,
            targets,
            None,
            plain,
            dict(),
            dict(own_h=own, own_x_h=own_x, other_h=exchange(own), other_x_h=exchange(own_x)),
            outs,
            dict(
                pieces=((4,) + own.shape, bf16),
                wide=((4 * group * parts, width // group, width), f32),
            ),
            8 + 4 * group * parts,
            5,
        )

    tokens, all_tokens = micros * length, 2 * micros * length
    turn, turn_all = ((width, tokens), bf16), ((width, all_tokens), bf16)
    narrow, narrow_all = ((tokens, width), bf16), ((all_tokens, width), bf16)
    pair_all = ((all_tokens, 2 * width), bf16)
    deep = ((tokens, hidden), bf16)

    def part_of(buffer, *sources):
        return lambda column: (buffer, sources, column)

    def key_rows(buffer, sources):
        first, second = pl.ds(0, length), pl.ds(length, length)
        return part_of(buffer, *[source.at[rows] for rows in (first, second) for source in sources])

    def cross_plan(r):
        rows = pl.ds(0, length)
        low_part = part_of(r.low, r.low0_h, r.low1_h)
        att_part = part_of(r.att, r.att0_h, r.att1_h)
        dq_part = part_of(r.dq, r.dq0_h, r.dq1_h)
        branch_part = part_of(r.branch, r.branch0_h, r.branch1_h)
        sources = (r.mem0_h, r.mem1_h, r.mem2_h, r.mem3_h)
        mem_part = part_of(r.mem, *[source.at[rows] for source in sources])
        pair_part = key_rows(r.pair, (r.pair0_h, r.pair1_h))
        return [
            (r.turn, low_part(0), dq_part(0)),
            (r.turn_att, att_part(0), branch_part(0)),
            (r.turn_all, mem_part(0), pair_part(0)),
            (r.turn_all, mem_part(0), pair_part(1)),
        ]

    def rising_plan(r):
        low_part = part_of(r.low, r.low0_h, r.low1_h)
        up_part = part_of(r.up, r.up0_h, r.up1_h)
        return [(r.turn, low_part(0), up_part(block)) for block in range(4)]

    def falling_plan(r):
        act_part = part_of(r.act, r.act0_h, r.act1_h)
        down_part = part_of(r.down, r.down0_h, r.down1_h)
        return [(r.turn, act_part(block), down_part(0)) for block in range(4)]

    def self_plan(r):
        rows = pl.ds(0, length)
        sources = (r.x0_h, r.x1_h, r.x2_h, r.x3_h)
        x_part = part_of(r.x, *[source.at[rows] for source in sources])
        dq_part = part_of(r.dq, r.dq0_h, r.dq1_h)
        pair_part = key_rows(r.pair, (r.pair0_h, r.pair1_h))
        att_part = part_of(r.att, r.att0_h, r.att1_h)
        branch_part = part_of(r.branch, r.branch0_h, r.branch1_h)
        return [
            (r.turn_all, x_part(0), dq_part(0)),
            (r.turn_all, x_part(0), pair_part(0)),
            (r.turn_all, x_part(0), pair_part(1)),
            (r.turn, att_part(0), branch_part(0)),
        ]

    last = micros - 1
    feeds, ends = [None] * micros, [None] * micros
    results = jnp.stack(
        [
            jnp.where(decoder, call.decoded_o, done.memory_o[:length])
            for call, done in zip(cross, forward)
        ]
    )
    results = send(results, to_row)
    latest = made[last]

    def part_sum(micro, *before):
        end = ends[micro]
        away = fence(end.part_other_o, *before)
        total = (end.part_own_o + exchange(away).astype(f32)).astype(bf16)
        return total, send(total, to_row)

    steps = []
    for micro in range(last):
        feeds[micro] = backward_feed(micro, (latest,))
        first = feeds[micro].grad_first_o
        ends[micro] = backward_self(micro, 0, first)
        ends[micro] = backward_self(micro, 1, first, vars(ends[micro]), (made[last],))
        steps.append(part_sum(micro, grads_memory[last]))
        latest = ends[micro].gain_early_o
    feeds[last] = backward_feed(last, (latest,))

    rising_halves = weight_grads(
        rising_plan,
        None,
        dict(
            low0_h=cross[0].ffn_low_o,
            low1_h=cross[1].ffn_low_o,
            up0_h=feeds[0].up_grad_o,
            up1_h=feeds[1].up_grad_o,
        ),
        dict(low=narrow, up=deep, turn=turn),
        (results,) + tuple(step[0] for step in steps),
    )
    rising_sums = first_sums(rising_halves)
    rising_total = middle_sums(rising_sums)
    falling_halves = weight_grads(
        falling_plan,
        None,
        dict(
            act0_h=cross[0].act_o,
            act1_h=cross[1].act_o,
            down0_h=feeds[0].down_grad_o,
            down1_h=feeds[1].down_grad_o,
        ),
        dict(act=deep, down=narrow, turn=turn),
        (rising_sums[0],) + tuple(step[1] for step in steps),
    )
    cross_halves = weight_grads(
        cross_plan,
        1,
        dict(
            low0_h=forward[0].first_low_o,
            low1_h=forward[1].first_low_o,
            dq0_h=cross[0].dq_low_o,
            dq1_h=cross[1].dq_low_o,
            att0_h=cross[0].att_o,
            att1_h=cross[1].att_o,
            branch0_h=cross[0].branch_o,
            branch1_h=cross[1].branch_o,
            mem0_h=memories[0],
            mem1_h=memories[1],
            mem2_h=memories_other[0],
            mem3_h=memories_other[1],
            pair0_h=cross[0].dkv_o,
            pair1_h=cross[1].dkv_o,
        ),
        dict(
            low=narrow,
            dq=narrow,
            att=narrow,
            branch=narrow,
            mem=narrow_all,
            pair=pair_all,
            turn=turn,
            turn_att=turn,
            turn_all=turn_all,
        ),
        (falling_halves[0],),
    )
    falling_sent = fence(falling_halves[0], rising_total, cross_halves[0])
    falling_sums = first_sums((falling_sent, falling_halves[1]))
    cross_sums = first_sums(cross_halves, 1)
    falling_total = middle_sums(falling_sums)
    shares = []

    def halfway(one):
        shares.append(last_sums(rising_total, (one.gain_early_o,)))
        shares.append(send(fence(cross_sums[0], one.gain_early_o), to_x, 1))
        return (shares[0], falling_total)

    ends[last] = backward_self(
        last,
        None,
        feeds[last].grad_first_o,
        None,
        (falling_sums[0], cross_sums[0]),
        halfway,
    )
    rising_share, cross_arrived = shares
    falling_share = last_sums(falling_total, (ends[last].gain_early_o, ends[last].part_own_o))
    cross_total = cross_sums[1] + fence(cross_arrived, falling_share).astype(f32)
    cross_total = cross_total.astype(bf16)
    steps.append(part_sum(last, cross_total))
    one_own = gather_z(jnp.concatenate([rising_share, falling_share]))

    self_halves = weight_grads(
        self_plan,
        None,
        dict(
            x0_h=own[0],
            x1_h=own[1],
            x2_h=other[0],
            x3_h=other[1],
            dq0_h=ends[0].dq_low_o,
            dq1_h=ends[1].dq_low_o,
            pair0_h=ends[0].dkv_o,
            pair1_h=ends[1].dkv_o,
            att0_h=forward[0].att_o,
            att1_h=forward[1].att_o,
            branch0_h=ends[0].branch_o,
            branch1_h=ends[1].branch_o,
        ),
        dict(
            x=narrow_all,
            dq=narrow,
            pair=pair_all,
            att=narrow,
            branch=narrow,
            turn=turn,
            turn_all=turn_all,
        ),
        (steps[last][0],),
    )
    cross_share = last_sums(cross_total, (self_halves[0],), 1)
    away, total = first_sums(
        (fence(self_halves[0], one_own[1], one_own[-1], steps[last][1]), self_halves[1])
    )
    third = sum(call.gain_grads_o[1] for call in cross)
    cross_share = jnp.concatenate([cross_share, gain_block([third])])
    cross_sent = send(cross_share, to_encoder)
    self_total = (total + fence(send(away, to_x), cross_sent).astype(f32)).astype(bf16)
    self_share = last_sums(self_total)
    one_own = jnp.stack([one_own[0]] + [fence(part, self_total) for part in one_own[1:]])
    one_own_x = send(one_own, to_x)
    cross_share = jnp.where(decoder, cross_share, cross_sent)

    early = sum(end.gain_early_o[0] for end in ends)
    late = jnp.where(
        decoder,
        sum(call.gain_grads_o[0] for call in cross),
        sum(call.gain_late_o[0] for call in feeds),
    )
    two_own = jnp.stack(gather_z(jnp.concatenate([self_share, gain_block([early, late])])))
    two_own_x = send(fence(two_own, one_own_x), to_x)
    three_own = gather_z(fence(cross_share, two_own))

    def columns(block):
        return pl.ds(block * width, width)

    def one_targets(r, block, row, rows):
        lines = pl.ds(row, rows)
        return [r.up_o.at[lines, columns(block)], r.down_o.at[pl.ds(block * width + row, rows)]]

    def two_targets(r, block, row, rows):
        lines = pl.ds(row, rows)
        return [r.out_o.at[lines] if block == 3 else r.mixed_o.at[lines, columns(block)]]

    def three_targets(r, block, row, rows):
        lines = pl.ds(row, rows)
        if block >= 2:
            return [r.pair_o.at[lines, columns(block - 2)]]
        return [(r.out_o if block else r.query_o).at[lines]]

    square_out = ((width, width), f32)
    one_own_x = fence(one_own_x, two_own)
    one_grads = spread(
        one_targets,
        one_own,
        one_own_x,
        dict(up_o=((width, hidden), f32), down_o=((hidden, width), f32)),
        2,
    )
    three_own = [three_own[0]] + [fence(part, one_grads.up_o) for part in three_own[1:]]
    three_own = jnp.stack(three_own)
    three_own_x = send(three_own, to_x)
    two_own_x = fence(two_own_x, one_grads.up_o, three_own)
    two_grads = spread(
        two_targets,
        two_own,
        two_own_x,
        dict(mixed_o=((width, 3 * width), f32), out_o=square_out, gains_o=((2, width), f32)),
        1,
    )
    three_own_x = fence(three_own_x, two_grads.out_o)
    three_grads = spread(
        three_targets,
        three_own,
        three_own_x,
        dict(
            query_o=square_out,
            pair_o=((width, 2 * width), f32),
            out_o=square_out,
            gains_o=((1, width), f32),
        ),
        1,
    )

    grad_input = jnp.stack([step[1] for step in steps])
    return (
        results[None, :, None],
        grad_input.astype(f32)[None, :, None],
        two_grads.mixed_o[None],
        two_grads.out_o[None],
        one_grads.up_o[None],
        one_grads.down_o[None],
        two_grads.gains_o[None],
        three_grads.query_o,
        three_grads.pair_o,
        three_grads.out_o,
        three_grads.gains_o[0],
    )


def shards(*arrays):
    layer_input = arrays[0]
    micros, rows, length = layer_input.shape[1:4]
    simple = (
        lax.axis_size("section") == 2
        and lax.axis_size("seq") == 2
        and lax.axis_size("dp") in (4, 8, 16)
        and (micros, rows) == (2, 1)
        and length == layer_input.shape[-1] == CHUNK
        and arrays[4].shape[-1] == 4 * CHUNK
    )
    return split_rows(*arrays) if simple else any_rows(*arrays)


def solution(mesh):
    in_specs = (
        P("section", None, "dp", "seq", None),
        P("section", None, "dp", "seq"),
        P("section", None, None),
        P("section", None, None),
        P("section", None, None),
        P("section", None, None),
        P("section", None, None),
        P(),
        P(),
        P(),
        P(),
        P(None, "dp", "seq", None),
    )
    out_specs = (
        P("section", None, "dp", "seq", None),
        P("section", None, "dp", "seq", None),
        P("section", None, None),
        P("section", None, None),
        P("section", None, None),
        P("section", None, None),
        P("section", None, None),
        P(),
        P(),
        P(),
        P(),
    )
    return jax.shard_map(shards, mesh=mesh, in_specs=in_specs, out_specs=out_specs, check_vma=False)
```

```python
import types

import jax
import jax.numpy as jnp
from jax import lax
from jax.experimental import pallas as pl
from jax.experimental.pallas import tpu as pltpu
from jax.sharding import PartitionSpec as P

HEADS = 8
TILE = 256
LANES = 128
CHUNK = 512

f32 = jnp.float32
bf16 = jnp.bfloat16
negative_big = -1e30
epsilon = 1e-05


def dot(left, right):
    return lax.dot_general(left, right, (((1,), (0,)), ((), ())), preferred_element_type=f32)


def dot_nt(left, right):
    return lax.dot_general(left, right, (((1,), (1,)), ((), ())), preferred_element_type=f32)


def dot_tn(left, right):
    return lax.dot_general(left, right, (((0,), (0,)), ((), ())), preferred_element_type=f32)


def standardize(values):
    center = values - jnp.mean(values, axis=-1, keepdims=True)
    inverse = lax.rsqrt(jnp.mean(center * center, axis=-1, keepdims=True) + epsilon)
    return center * inverse, inverse


def standardize_back(grad_out, standard, gain_row, inverse):
    scaled = grad_out * gain_row
    grad_in = inverse * (
        scaled
        - jnp.mean(scaled, axis=-1, keepdims=True)
        - standard * jnp.mean(scaled * standard, axis=-1, keepdims=True)
    )
    return grad_in, jnp.sum(grad_out * standard, axis=0, keepdims=True)


class Copies:
    def __init__(self, sems):
        self.sems = sems
        self.used = 0

    def start(self, source, target):
        copy = pltpu.make_async_copy(source, target, self.sems.at[self.used])
        self.used += 1
        copy.start()
        return copy


def wait_all(copies):
    for copy in copies:
        copy.wait()


def spread_pairs(target, source, factor, pairs):
    tiles = target.shape[1]
    half = lax.broadcasted_iota(jnp.int32, (TILE, LANES), 1) < LANES // 2
    first = jnp.where(half, factor, 0.0).astype(bf16)
    second = jnp.where(half, 0.0, factor).astype(bf16)
    for tile in range(tiles):
        for pair in pairs:
            block = source[tile * TILE : (tile + 1) * TILE, pair * LANES : (pair + 1) * LANES]
            target[pair, tile, :TILE, :] = block * first
            target[pair, tile, TILE:, :] = block * second


def turn_tiles(target, source, column, pairs):
    low, high = pairs[0] * LANES, (pairs[-1] + 1) * LANES
    for tile in range(target.shape[0]):
        block = source[tile * TILE : (tile + 1) * TILE, column + low : column + high]
        target[tile, low:high, :] = jnp.transpose(block)


def place_documents(r, copies):
    wait_all(copies)
    q_tiles = r.qd.shape[0]
    for part in range(3):
        row = r.docs[part].astype(f32)[0:1, :]
        for tile in range(q_tiles):
            piece = row[:, tile * TILE : (tile + 1) * TILE]
            slot = part * q_tiles + tile
            r.bounds[0, slot] = jnp.min(piece).astype(jnp.int32)
            r.bounds[1, slot] = jnp.max(piece).astype(jnp.int32)
            if part == 0:
                r.qd[tile] = jnp.broadcast_to(piece, (8, TILE))
        if part > 0:
            for start in range(0, row.shape[1], LANES):
                block = jnp.broadcast_to(row[:, start : start + LANES], (LANES, LANES))
                place = (part - 1) * row.shape[1] + start
                r.kdc[place : place + LANES, :] = jnp.transpose(block)


def load_documents(r, move, queries, own, other):
    rows = pl.ds(r.docs.shape[2], r.docs.shape[1])
    return [
        move.start(source.at[rows], r.docs.at[part])
        for part, source in enumerate((queries, own, other))
    ]


def tile_place(r, core, causal, q_tile, k_tile):
    q_tiles = r.qd.shape[0]
    length = q_tiles * TILE
    owner = jnp.where(k_tile < q_tiles, core, 1 - core)
    k_start = owner * length + lax.rem(k_tile, q_tiles) * TILE
    ahead = core * length + q_tile * TILE - k_start
    ahead = jnp.where(causal == 1, ahead, 2 * length * TILE)
    q_low, q_high = r.bounds[0, q_tile], r.bounds[1, q_tile]
    k_low, k_high = r.bounds[0, q_tiles + k_tile], r.bounds[1, q_tiles + k_tile]
    active = (q_low <= k_high) & (k_low <= q_high) & (ahead > -TILE)
    whole = (q_low == k_high) & (k_low == q_high) & (ahead >= TILE)
    return active, whole, ahead


def each_tile(place, body):
    active, whole, ahead = place
    pl.when(active & jnp.logical_not(whole))(lambda: body(ahead))
    pl.when(whole)(lambda: body(None))


def fill_bias(r, q_tile, k_tile, ahead):
    keys = r.kdc[pl.ds(pl.multiple_of(k_tile * TILE, TILE), TILE), :]
    shift = lax.broadcasted_iota(jnp.int32, (TILE, LANES), 0) - lax.broadcasted_iota(
        jnp.int32, (TILE, LANES), 1
    )
    queries = r.qd[q_tile]
    for start in range(0, TILE, LANES):
        same = keys == queries[0:1, start : start + LANES]
        allowed = same & (shift - start <= ahead)
        r.bias[:, start : start + LANES] = jnp.where(allowed, 0.0, negative_big)


def attention_forward(r, core, causal):
    pairs, q_tiles = r.qm.shape[:2]
    k_tiles = r.vt.shape[0]

    def one_query_tile(q_tile, carry):
        r.top[...] = jnp.full(r.top.shape, negative_big, f32)
        r.total[...] = jnp.zeros(r.total.shape, f32)
        r.turned[...] = jnp.zeros(r.turned.shape, f32)

        def one_key_tile(k_tile, inner):
            def one_tile(ahead):
                if ahead is not None:
                    fill_bias(r, q_tile, k_tile, ahead)
                rows = pl.ds(pl.multiple_of(k_tile * TILE, TILE), TILE)

                def raw(pair):
                    keys = r.kv[rows, pair * LANES : (pair + 1) * LANES]
                    return dot_nt(keys, r.qm[pair, q_tile])

                raw_next = raw(0)
                for pair in range(pairs):
                    scores = raw_next
                    if ahead is not None:
                        bias = r.bias[...]
                        scores = scores + jnp.concatenate([bias, bias], axis=1)
                    if pair + 1 < pairs:
                        raw_next = raw(pair + 1)
                    old_top = r.top[pair : pair + 1, :]
                    new_top = jnp.maximum(old_top, jnp.max(scores, axis=0, keepdims=True))
                    weights = jnp.exp(scores - new_top)
                    shrink = jnp.exp(old_top - new_top)
                    r.top[pair : pair + 1, :] = new_top
                    r.total[pair : pair + 1, :] = r.total[
                        pair : pair + 1, :
                    ] * shrink + jnp.sum(weights, axis=0, keepdims=True)
                    low = weights.astype(bf16)
                    for side in range(2):
                        span = slice(side * TILE, (side + 1) * TILE)
                        head = slice((2 * pair + side) * 64, (2 * pair + side + 1) * 64)
                        r.turned[head, :] = r.turned[head, :] * shrink[:, span] + dot(
                            r.vt[k_tile, head, :], low[:, span]
                        )

            each_tile(tile_place(r, core, causal, q_tile, k_tile), one_tile)
            return inner

        lax.fori_loop(0, k_tiles, one_key_tile, 0)
        for pair in range(pairs):
            total = r.total[pair : pair + 1, :]
            r.lse[q_tile, pair : pair + 1, :] = r.top[pair : pair + 1, :] + jnp.log(total)
            share = 1.0 / total
            for side in range(2):
                span = slice(side * TILE, (side + 1) * TILE)
                head = slice((2 * pair + side) * 64, (2 * pair + side + 1) * 64)
                r.turned[head, :] = r.turned[head, :] * share[:, span]
        rows = pl.ds(pl.multiple_of(q_tile * TILE, TILE), TILE)
        r.att[rows, :] = jnp.transpose(r.turned[...]).astype(bf16)
        return carry

    lax.fori_loop(0, q_tiles, one_query_tile, 0)


def row_products(r, grad_att, pairs):
    low, high = pairs[0] * LANES, (pairs[-1] + 1) * LANES
    for tile in range(r.qm.shape[1]):
        rows = slice(tile * TILE, (tile + 1) * TILE)
        product = jnp.transpose(
            grad_att[rows, low:high].astype(f32) * r.att[rows, low:high].astype(f32)
        )
        for pair in pairs:
            for side in range(2):
                head = (2 * pair + side) * 64 - low
                r.delta[tile, pair : pair + 1, side * TILE : (side + 1) * TILE] = jnp.sum(
                    product[head : head + 64, :], axis=0, keepdims=True
                )


def attention_backward(r, core, causal, pairs):
    q_tiles, k_tiles = r.qm.shape[1], r.kt.shape[0]
    width = r.kt.shape[1]
    low, high = pairs[0] * LANES, (pairs[-1] + 1) * LANES
    for start in (0, width):
        r.dkv[:, start + low : start + high] = jnp.zeros((r.dkv.shape[0], high - low), f32)

    def one_query_tile(q_tile, carry):
        r.turned[low:high, :] = jnp.zeros((high - low, TILE), f32)

        def one_key_tile(k_tile, inner):
            def one_tile(ahead):
                if ahead is not None:
                    fill_bias(r, q_tile, k_tile, ahead)
                rows = pl.ds(pl.multiple_of(k_tile * TILE, TILE), TILE)

                def raw(pair):
                    lanes = slice(pair * LANES, (pair + 1) * LANES)
                    lanes_v = slice(width + pair * LANES, width + (pair + 1) * LANES)
                    return (
                        dot_nt(r.kv[rows, lanes], r.qm[pair, q_tile]),
                        dot_nt(r.kv[rows, lanes_v], r.gm[pair, q_tile]),
                    )

                raw_next = raw(pairs[0])
                for pair in pairs:
                    scores, grad_probs = raw_next
                    if ahead is not None:
                        bias = r.bias[...]
                        scores = scores + jnp.concatenate([bias, bias], axis=1)
                    if pair < pairs[-1]:
                        raw_next = raw(pair + 1)
                    probs = jnp.exp(scores - r.lse[q_tile, pair : pair + 1, :])
                    grad_scores = probs * (grad_probs - r.delta[q_tile, pair : pair + 1, :])
                    probs_low = probs.astype(bf16)
                    grad_low = grad_scores.astype(bf16)
                    lanes = slice(pair * LANES, (pair + 1) * LANES)
                    lanes_v = slice(width + pair * LANES, width + (pair + 1) * LANES)
                    r.dkv[rows, lanes] += dot(grad_low, r.qm[pair, q_tile])
                    r.dkv[rows, lanes_v] += dot(probs_low, r.gm[pair, q_tile])
                    for side in range(2):
                        span = slice(side * TILE, (side + 1) * TILE)
                        head = slice((2 * pair + side) * 64, (2 * pair + side + 1) * 64)
                        r.turned[head, :] += dot(r.kt[k_tile, head, :], grad_low[:, span])

            each_tile(tile_place(r, core, causal, q_tile, k_tile), one_tile)
            return inner

        lax.fori_loop(0, k_tiles, one_key_tile, 0)
        rows = pl.ds(pl.multiple_of(q_tile * TILE, TILE), TILE)
        r.dq[rows, low:high] = jnp.transpose(r.turned[low:high, :]) * (64**-0.5)
        return carry

    lax.fori_loop(0, q_tiles, one_query_tile, 0)


def feed_forward(r, low):
    chunks = [slice(at, at + CHUNK) for at in range(0, r.w_in.shape[1], CHUNK)]
    upward_next = dot(low[...], r.w_in[:, chunks[0]])
    for place, span in enumerate(chunks):
        upward = upward_next
        if place + 1 < len(chunks):
            upward_next = dot(low[...], r.w_in[:, chunks[place + 1]])
        gate = jax.nn.sigmoid(upward)
        active = (upward * gate).astype(bf16)
        r.act[:, span] = active
        r.slope[:, span] = (gate + upward * gate * (1.0 - gate)).astype(r.slope.dtype)
        part = dot(active, r.w_down[span, :])
        if place:
            r.sum[...] += part
        else:
            r.sum[...] = part


def feed_backward(r):
    chunks = [slice(at, at + CHUNK) for at in range(0, r.w_in.shape[1], CHUNK)]
    active_next = dot_nt(r.down_grad[...], r.w_down[chunks[0], :])
    for place, span in enumerate(chunks):
        grad_active = active_next.astype(bf16)
        if place + 1 < len(chunks):
            active_next = dot_nt(r.down_grad[...], r.w_down[chunks[place + 1], :])
        grad_up = (grad_active.astype(f32) * r.slope[:, span].astype(f32)).astype(bf16)
        r.up_grad[:, span] = grad_up
        part = dot_nt(grad_up, r.w_in[:, span])
        if place:
            r.sum[...] += part
        else:
            r.sum[...] = part


def self_forward(r):
    length, width = r.unit1.shape
    decoder, core = r.meta[0], r.meta[1]
    move = Copies(r.sems)
    whole = pl.ds(0, length)
    documents = load_documents(r, move, r.x_own_h, r.x_own_h, r.x_other_h)
    early = [
        move.start(r.x_own_h.at[whole], r.x.at[whole]),
        move.start(r.x_other_h.at[whole], r.x.at[pl.ds(length, length)]),
        move.start(r.w_mixed_h, r.w_mixed),
    ]
    later = [
        move.start(r.w_out_h, r.w_out),
        move.start(r.w_in_h, r.w_in),
        move.start(r.w_down_h, r.w_down),
    ]
    place_documents(r, documents)
    wait_all(early)
    r.q[...] = dot(r.x[:length, :], r.w_mixed[:, :width]).astype(bf16)
    r.kv[...] = dot(r.x[...], r.w_mixed[:, width:]).astype(bf16)
    outs = [move.start(r.q, r.q_o), move.start(r.kv, r.kv_o)]
    pairs = range(width // LANES)
    spread_pairs(r.qm, r.q, 64**-0.5, pairs)
    turn_tiles(r.vt, r.kv, width, pairs)
    attention_forward(r, core, decoder)
    wait_all(later)
    outs += [move.start(r.att, r.att_o), move.start(r.lse, r.lse_o)]
    unit, inverse = standardize(r.x[:length, :].astype(f32) + dot(r.att[...], r.w_out[...]))
    r.unit1[...] = unit
    r.inv1[...] = jnp.broadcast_to(inverse, r.inv1.shape)
    r.first_low[...] = (unit * r.gains[0:1, :]).astype(bf16)
    outs += [
        move.start(r.unit1, r.unit1_o),
        move.start(r.inv1, r.inv1_o),
        move.start(r.first_low, r.first_low_o),
    ]

    @pl.when(decoder == 0)
    def _():
        feed_forward(r, r.first_low)
        late = [
            move.start(r.first_low, r.ffn_low_o),
            move.start(r.act, r.act_o),
            move.start(r.slope, r.slope_o),
        ]
        unit2, inverse2 = standardize(r.unit1[...] * r.gains[0:1, :] + r.sum[...])
        r.memory[:length, :] = (unit2 * r.gains[1:2, :]).astype(bf16)
        r.memory[length:, :] = r.docs[0]
        late += [move.start(r.memory, r.memory_o)]
        r.unit2[...] = unit2
        r.inv2[...] = jnp.broadcast_to(inverse2, r.inv2.shape)
        late += [move.start(r.unit2, r.unit2_o), move.start(r.inv2, r.inv2_o)]
        wait_all(late)

    wait_all(outs)


def cross_both_ways(r):
    length, width = r.unit1_h.shape
    core = r.meta[1]
    move = Copies(r.sems)
    whole = pl.ds(0, length)
    documents = load_documents(r, move, r.x_own_h, r.memory_own_h, r.memory_other_h)
    moves = [
        move.start(r.memory_own_h.at[whole], r.x.at[whole]),
        move.start(r.memory_other_h.at[whole], r.x.at[pl.ds(length, length)]),
        move.start(r.w_pair_h, r.w_pair),
        move.start(r.first_low_h, r.first_low),
        move.start(r.w_query_h, r.w_query),
    ]
    later = [
        move.start(r.unit1_h, r.unit1),
        move.start(r.w_cross_h, r.w_cross),
        move.start(r.w_in_h, r.w_in),
        move.start(r.w_down_h, r.w_down),
        move.start(r.cot_h.at[r.micro], r.cot),
    ]
    place_documents(r, documents)
    wait_all(moves)
    r.kv[...] = dot(r.x[...], r.w_pair[...]).astype(bf16)
    r.q[...] = dot(r.first_low[...], r.w_query[...]).astype(bf16)
    pairs = range(width // LANES)
    spread_pairs(r.qm, r.q, 64**-0.5, pairs)
    turn_tiles(r.vt, r.kv, width, pairs)
    turn_tiles(r.kt, r.kv, 0, pairs)
    attention_forward(r, core, 0)
    outs = [move.start(r.att, r.att_o)]
    wait_all(later)
    first = r.unit1[...] * r.gains[0:1, :]
    unit, inverse = standardize(first + dot(r.att[...], r.w_cross[...]))
    r.unit2[...] = unit
    r.inv2[...] = jnp.broadcast_to(inverse, r.inv2.shape)
    r.second_low[...] = (unit * r.cross_gain[...]).astype(bf16)
    outs += [move.start(r.second_low, r.ffn_low_o)]
    feed_forward(r, r.second_low)
    outs += [move.start(r.act, r.act_o)]
    unit3, inverse3 = standardize(r.unit2[...] * r.cross_gain[...] + r.sum[...])
    r.decoded[...] = (unit3 * r.gains[1:2, :]).astype(bf16)
    outs += [move.start(r.decoded, r.decoded_o)]
    grad_third, gain_late = standardize_back(
        r.cot[...].astype(f32), unit3, r.gains[1:2, :], inverse3
    )
    r.keep[...] = grad_third
    r.down_grad[...] = grad_third.astype(bf16)
    outs += [move.start(r.down_grad, r.down_grad_o)]
    feed_backward(r)
    outs += [move.start(r.up_grad, r.up_grad_o)]
    grad_sum, gain_cross = standardize_back(
        r.keep[...] + r.sum[...], r.unit2[...], r.cross_gain[...], r.inv2[:, 0:1]
    )
    r.gain_grads[...] = jnp.zeros(r.gain_grads.shape, f32)
    r.gain_grads[0:1, :] = gain_late
    r.gain_grads[1:2, :] = gain_cross
    r.keep[...] = grad_sum
    r.branch[...] = grad_sum.astype(bf16)
    outs += [move.start(r.gain_grads, r.gain_grads_o), move.start(r.branch, r.branch_o)]
    r.q[...] = dot_nt(r.branch[...], r.w_cross[...]).astype(bf16)
    spread_pairs(r.gm, r.q, 1.0, pairs)
    row_products(r, r.q, pairs)
    attention_backward(r, core, 0, pairs)
    r.dq_low[...] = r.dq[...].astype(bf16)
    r.keep[...] += dot_nt(r.dq_low[...], r.w_query[...])
    outs += [move.start(r.dq_low, r.dq_low_o), move.start(r.keep, r.grad_first_o)]
    r.dkv_low[...] = r.dkv[...].astype(bf16)
    outs += [move.start(r.dkv_low, r.dkv_o)]
    part = dot_nt(r.dkv_low[...], r.w_pair[...])
    r.part_other[...] = part[length:, :].astype(bf16)
    r.part_own[...] = part[:length, :]
    outs += [move.start(r.part_other, r.part_other_o), move.start(r.part_own, r.part_own_o)]
    wait_all(outs)


def feed_backward_alone(r):
    move = Copies(r.sems)
    early = [
        move.start(r.grad_memory_h, r.cot),
        move.start(r.unit2_h, r.unit2),
        move.start(r.inv2_h, r.inv2),
    ]
    later = [
        move.start(r.w_down_h, r.w_down),
        move.start(r.slope_h, r.slope),
        move.start(r.w_in_h, r.w_in),
    ]
    wait_all(early)
    grad_third, gain_late = standardize_back(
        r.cot[...].astype(f32), r.unit2[...], r.gains[1:2, :], r.inv2[:, 0:1]
    )
    r.gain_grads[...] = jnp.broadcast_to(gain_late, r.gain_grads.shape)
    r.keep[...] = grad_third
    r.down_grad[...] = grad_third.astype(bf16)
    outs = [move.start(r.down_grad, r.down_grad_o), move.start(r.gain_grads, r.gain_late_o)]
    wait_all(later)
    feed_backward(r)
    outs += [move.start(r.up_grad, r.up_grad_o)]
    r.keep[...] += r.sum[...]
    outs += [move.start(r.keep, r.grad_first_o)]
    wait_all(outs)


def self_backward(r, plan):
    r.micro, first, last = plan
    length, width = r.att_h.shape
    decoder, core = r.meta[0], r.meta[1]
    pairs = range(first, last)
    low, high = first * LANES, last * LANES
    move = Copies(r.sems)
    later = [
        move.start(r.q_h, r.q),
        move.start(r.kv_h, r.kv),
        move.start(r.att_h, r.att),
        move.start(r.lse_h, r.lse),
    ]
    if first == 0:
        early = [
            move.start(r.grad_first_h, r.keep),
            move.start(r.unit1_h, r.unit1),
            move.start(r.inv1_h, r.inv1),
            move.start(r.w_out_h, r.w_out),
        ]
    else:
        early = [move.start(r.grad_att_h, r.grad_att)]
    outs = []
    place_documents(r, load_documents(r, move, r.x_own_h, r.x_own_h, r.x_other_h))
    wait_all(early)
    if first == 0:
        grad_sum, gain_early = standardize_back(
            r.keep[...], r.unit1[...], r.gains[0:1, :], r.inv1[:, 0:1]
        )
        r.gain_grads[...] = jnp.broadcast_to(gain_early, r.gain_grads.shape)
        r.keep[...] = grad_sum
        r.branch[...] = grad_sum.astype(bf16)
        r.grad_att[...] = dot_nt(r.branch[...], r.w_out[...]).astype(bf16)
        outs += [move.start(r.gain_grads, r.gain_early_o), move.start(r.branch, r.branch_o)]
        if last < width // LANES:
            outs += [move.start(r.keep, r.grad_sum_o), move.start(r.grad_att, r.grad_att_o)]
    wait_all(later)
    if last == width // LANES:
        ends = [move.start(r.w_mixed_h, r.w_mixed)]
        if first > 0:
            ends += [
                move.start(r.grad_sum_h, r.keep),
                move.start(r.dq_h.at[:, pl.ds(0, low)], r.dq_low.at[:, pl.ds(0, low)]),
                move.start(r.dkv_h.at[:, pl.ds(0, low)], r.dkv_low.at[:, pl.ds(0, low)]),
                move.start(
                    r.dkv_h.at[:, pl.ds(width, low)], r.dkv_low.at[:, pl.ds(width, low)]
                ),
            ]
    spread_pairs(r.qm, r.q, 64**-0.5, pairs)
    turn_tiles(r.kt, r.kv, 0, pairs)
    spread_pairs(r.gm, r.grad_att, 1.0, pairs)
    row_products(r, r.grad_att, pairs)
    attention_backward(r, core, decoder, pairs)
    r.dq_low[:, low:high] = r.dq[:, low:high].astype(bf16)
    for start in (0, width):
        span = slice(start + low, start + high)
        r.dkv_low[:, span] = r.dkv[:, span].astype(bf16)
    if last == width // LANES:
        wait_all(ends)
        outs += [move.start(r.dq_low, r.dq_low_o), move.start(r.dkv_low, r.dkv_o)]
        r.keep[...] += dot_nt(r.dq_low[...], r.w_mixed[:, :width])
        part = dot_nt(r.dkv_low[...], r.w_mixed[:, width:])
        r.part_other[...] = part[length:, :].astype(bf16)
        r.keep[...] += part[:length, :]
        outs += [move.start(r.part_other, r.part_other_o), move.start(r.keep, r.part_own_o)]
    else:
        outs.append(move.start(r.dq_low.at[:, pl.ds(low, high - low)], r.dq_low_o.at[:, pl.ds(low, high - low)]))
        for start in (0, width):
            span = pl.ds(start + low, high - low)
            outs.append(move.start(r.dkv_low.at[:, span], r.dkv_o.at[:, span]))
    wait_all(outs)


def contract_blocks(r, plan):
    for core in range(2):

        @pl.when(r.meta[1] == core)
        def _(core=core):
            targets = [None] * 4
            for half in range(2):
                target = r.kept_o if half == core else r.sent_o
                targets[2 * half], targets[2 * half + 1] = target.at[0], target.at[1]
            order = (0, 1, 2, 3) if core else (2, 3, 0, 1)
            contract_in_order(r, plan(r), order, targets, Copies(r.sems))


def contract_in_order(r, blocks, order, targets, move):
    loads = dict()
    for slot in order:
        for buffer, sources, at in blocks[slot][1:]:
            span = pl.ds(at * CHUNK, CHUNK)
            if buffer.shape[1] == 4 * CHUNK:
                at, span = 0, pl.ds(0, 4 * CHUNK)
            if (id(buffer), at) not in loads:
                row = 0
                copies = []
                for source in sources:
                    rows = pl.ds(row, source.shape[0])
                    copies.append(move.start(source.at[:, span], buffer.at[rows, span]))
                    row += source.shape[0]
                loads[id(buffer), at] = copies
    outs = []
    held = dict()
    for slot in order:
        turn, (left, _, left_at), (right, _, right_at) = blocks[slot]
        for buffer, at in ((left, left_at), (right, right_at)):
            at = 0 if buffer.shape[1] == 4 * CHUNK else at
            wait_all(loads.pop((id(buffer), at), ()))
        if held.get(id(turn)) != left_at:
            for row in range(0, left.shape[0], CHUNK):
                block = left[row : row + CHUNK, left_at * CHUNK : (left_at + 1) * CHUNK]
                turn[:, row : row + CHUNK] = jnp.transpose(block)
            held[id(turn)] = left_at
        block = right[:, right_at * CHUNK : (right_at + 1) * CHUNK]
        r.blocks[slot] = dot(turn[:, : right.shape[0]], block).astype(bf16)
        outs.append(move.start(r.blocks.at[slot], targets[slot]))
    wait_all(outs)


def spread_pieces(r, plan):
    targets, turned = plan
    z = r.meta[3]
    group, height = r.own_h.shape[:2]
    rows = r.own_h.shape[2] // group
    for core in range(2):
        for x in range(2):

            @pl.when((r.meta[1] == core) & (r.meta[2] == x))
            def _(core=core, x=x):
                move = Copies(r.sems)
                parts = [
                    (r.own_h, core, x),
                    (r.own_x_h, core, 1 - x),
                    (r.other_h, 1 - core, x),
                    (r.other_x_h, 1 - core, 1 - x),
                ]
                loads = [
                    move.start(source, r.pieces.at[place])
                    for place, (source, _, _) in enumerate(parts)
                ]
                outs = []
                slot = 0
                gains = []
                for place, (_, half, side) in enumerate(parts):
                    loads[place].wait()
                    for step in range(group):
                        place_z = lax.rem(z + (group - step), group) if turned else step
                        row = pl.multiple_of(place_z * rows, rows) if turned else step * rows
                        start = 0
                        for target in targets(r, 2 * half + side, row, rows):
                            r.wide[slot] = r.pieces[place, step, start : start + rows].astype(f32)
                            outs.append(move.start(r.wide.at[slot], target))
                            slot += 1
                            start += rows
                        if start < height:
                            gains.append(r.pieces[place, step, start:height].astype(f32))
                if gains:
                    r.gains_o[...] = sum(gains)[: r.gains_o.shape[0], :]
                wait_all(outs)


def launch(kernel, plan, side, scalars, small, large, outs, scratch, copies, work, previous=None, after=()):
    names = list(scalars) + list(small) + list(large)
    arrays = list(scalars.values()) + list(small.values()) + list(large.values())
    specs = (
        [pl.BlockSpec(memory_space=pltpu.SMEM)] * len(scalars)
        + [pl.BlockSpec(memory_space=pltpu.VMEM)] * len(small)
        + [pl.BlockSpec(memory_space=pl.ANY)] * len(large)
    )
    aliases = dict()
    for position, name in enumerate(outs):
        if previous and name in previous:
            aliases[len(arrays)] = position
            names.append("previous_" + name)
            arrays.append(previous[name])
            specs.append(pl.BlockSpec(memory_space=pl.ANY))
    for array in after:
        names.append("")
        arrays.append(array)
        specs.append(pl.BlockSpec(memory_space=pl.ANY))
    names += list(outs) + list(scratch) + ["sems"]

    def body(*refs):
        r = types.SimpleNamespace(**dict(zip(names, refs)))

        def run():
            if isinstance(plan, int):
                r.micro = plan
                kernel(r)
            else:
                kernel(r, plan)

        if side is None:
            run()
        else:
            pl.when(r.meta[0] == side)(run)

    results = pl.pallas_call(
        body,
        out_shape=[jax.ShapeDtypeStruct(*shape) for shape in outs.values()],
        in_specs=specs,
        out_specs=[
            pl.BlockSpec(memory_space=pltpu.VMEM if shape[0][0] < 8 else pl.ANY)
            for shape in outs.values()
        ],
        scratch_shapes=[
            pltpu.SMEM(*shape) if shape[1] == jnp.int32 else pltpu.VMEM(*shape)
            for shape in scratch.values()
        ]
        + [pltpu.SemaphoreType.DMA((copies,))],
        input_output_aliases=aliases,
        compiler_params=pltpu.CompilerParams(vmem_limit_bytes=58 * 1024 * 1024),
        cost_estimate=pl.CostEstimate(
            flops=work * 10**9, bytes_accessed=1 << 20, transcendentals=0
        ),
    )(*arrays)
    return types.SimpleNamespace(**dict(zip(outs, results)))


def attention_scratch(length, width):
    pairs, q_tiles, k_tiles = width // LANES, length // TILE, 2 * length // TILE
    return dict(
        q=((length, width), bf16),
        kv=((2 * length, 2 * width), bf16),
        qm=((pairs, q_tiles, 2 * TILE, LANES), bf16),
        kdc=((2 * length, LANES), f32),
        docs=((3, 16, width), bf16),
        qd=((length // TILE, 8, TILE), f32),
        bounds=((2, 3 * length // TILE), jnp.int32),
        bias=((TILE, TILE), f32),
        lse=((q_tiles, 8, 2 * TILE), f32),
        att=((length, width), bf16),
        turned=((width, TILE), f32),
    )


def forward_scratch(length, width):
    k_tiles = 2 * length // TILE
    return dict(
        vt=((k_tiles, width, TILE), bf16),
        top=((8, 2 * TILE), f32),
        total=((8, 2 * TILE), f32),
    )


def backward_scratch(length, width):
    pairs, q_tiles, k_tiles = width // LANES, length // TILE, 2 * length // TILE
    return dict(
        kt=((k_tiles, width, TILE), bf16),
        gm=((pairs, q_tiles, 2 * TILE, LANES), bf16),
        delta=((q_tiles, 8, 2 * TILE), f32),
        dkv=((2 * length, 2 * width), f32),
        dq=((length, width), f32),
        dkv_low=((2 * length, 2 * width), bf16),
        part_other=((length, width), bf16),
        dq_low=((length, width), bf16),
    )


def for_sending(shard):

    def short(part):
        return part.astype(jnp.bfloat16) if part.dtype == jnp.float32 else part

    return jax.tree.map(short, shard)


def from_behind(block, axis, distance):
    devices = range(lax.axis_size(axis))
    route = [(i - distance, i) for i in devices if i - distance in devices]
    return lax.ppermute(block, axis, route)


def from_root(shard, axis, root):
    mine = lax.axis_index(axis) == root
    return lax.psum(jnp.where(mine, shard, jnp.zeros_like(shard)), axis)


def matmul(left_side, right_side):
    return jnp.einsum("rsd,de->rse", left_side, right_side, preferred_element_type=jnp.float32)


def matmul_back(left_side, right_side):
    return jnp.einsum("rse,de->rsd", left_side, right_side, preferred_element_type=jnp.float32)


def contract(left_side, right_side):
    return jnp.einsum("rsd,rse->de", left_side, right_side, preferred_element_type=jnp.float32)


def normalize(values, gain_row):
    center = values - jnp.mean(values, axis=-1, keepdims=True)
    inverse = lax.rsqrt(jnp.mean(center * center, axis=-1, keepdims=True) + epsilon)
    standard = center * inverse
    return (standard * gain_row, standard, inverse)


def normalize_back(grad_out, standard, gain_row, inverse):
    scaled = grad_out * gain_row
    grad_in = inverse * (
        scaled
        - jnp.mean(scaled, axis=-1, keepdims=True)
        - standard * jnp.mean(scaled * standard, axis=-1, keepdims=True)
    )
    return (grad_in, jnp.sum(grad_out * standard, axis=(0, 1)))


def allowed_mask(query_docs, key_docs, query_place, key_place, causal):
    same_doc = query_docs[:, :, None] == key_docs[:, None, :]
    earlier = query_place[:, None] >= key_place[None, :]
    return (same_doc & (earlier | jnp.logical_not(causal)))[:, None]


def attend(queries, keys_local, values_local, query_docs, key_docs, causal, is_cross):
    rows_here, shard_len, model_width = queries.shape
    head_dim = model_width // HEADS
    score_scale = head_dim ** (-0.5)
    query_place = lax.axis_index("seq") * shard_len + jnp.arange(shard_len)
    query_heads = queries.reshape(rows_here, shard_len, HEADS, head_dim)

    def absorb(state_tuple, pieces):
        running_top, running_total, running_sum = state_tuple
        key_piece, value_piece, doc_piece = pieces
        piece_len = key_piece.shape[1]
        raw_scores = jnp.einsum(
            "rqhd,rkhd->rhqk",
            query_heads,
            key_piece.reshape(rows_here, piece_len, HEADS, head_dim),
            preferred_element_type=jnp.float32,
        )
        allowed = allowed_mask(query_docs, doc_piece, query_place, jnp.arange(piece_len), causal)
        scores = jnp.where(allowed, raw_scores * score_scale, negative_big)
        new_top = jnp.maximum(running_top, jnp.max(scores, axis=-1))
        weights = jnp.where(allowed, jnp.exp(scores - new_top[..., None]), 0.0)
        new_total = jnp.sum(weights, axis=-1)
        product = jnp.einsum(
            "rhqk,rkhd->rhqd",
            weights.astype(jnp.bfloat16),
            value_piece.reshape(rows_here, piece_len, HEADS, head_dim),
            preferred_element_type=jnp.float32,
        )
        return (new_top, new_total, product)

    init_state = (
        jnp.full((rows_here, HEADS, shard_len), negative_big, jnp.float32),
        jnp.zeros((rows_here, HEADS, shard_len), jnp.float32),
        jnp.zeros((rows_here, HEADS, shard_len, head_dim), jnp.float32),
    )
    if is_cross:
        final_top, final_total, final_sum = absorb(
            init_state,
            (
                lax.all_gather(keys_local, "seq", axis=1, tiled=True),
                lax.all_gather(values_local, "seq", axis=1, tiled=True),
                lax.all_gather(for_sending(key_docs), "seq", axis=1, tiled=True),
            ),
        )
    else:
        final_top, final_total, final_sum = absorb(
            init_state,
            (
                lax.all_gather(keys_local, "seq", axis=1, tiled=True),
                lax.all_gather(values_local, "seq", axis=1, tiled=True),
                lax.all_gather(key_docs, "seq", axis=1, tiled=True),
            ),
        )
    attended = (
        (final_sum / final_total[..., None])
        .transpose(0, 2, 1, 3)
        .reshape(rows_here, shard_len, model_width)
    )
    return (attended, final_top + jnp.log(final_total))


def attend_back(
    queries,
    keys_local,
    values_local,
    query_docs,
    key_docs,
    causal,
    log_total,
    grad_attended,
    is_cross,
):
    rows_here, shard_len, model_width = queries.shape
    head_dim = model_width // HEADS
    score_scale = head_dim ** (-0.5)
    query_place = lax.axis_index("seq") * shard_len + jnp.arange(shard_len)
    if is_cross:
        keys_full, values_full, docs_full = (
            lax.all_gather(keys_local, "seq", axis=1, tiled=True),
            lax.all_gather(values_local, "seq", axis=1, tiled=True),
            lax.all_gather(for_sending(key_docs), "seq", axis=1, tiled=True).astype(key_docs.dtype),
        )
    else:
        keys_full, values_full, docs_full = (
            lax.all_gather(keys_local, "seq", axis=1, tiled=True),
            lax.all_gather(values_local, "seq", axis=1, tiled=True),
            lax.all_gather(key_docs, "seq", axis=1, tiled=True),
        )
    full_len = keys_full.shape[1]
    query_heads = queries.reshape(rows_here, shard_len, HEADS, head_dim)
    key_heads = keys_full.reshape(rows_here, full_len, HEADS, head_dim)
    value_heads = values_full.reshape(rows_here, full_len, HEADS, head_dim)
    grad_heads = grad_attended.reshape(rows_here, shard_len, HEADS, head_dim)
    raw_scores = jnp.einsum(
        "rqhd,rkhd->rhqk", query_heads, key_heads, preferred_element_type=jnp.float32
    )
    allowed = allowed_mask(query_docs, docs_full, query_place, jnp.arange(full_len), causal)
    shifted = jnp.where(allowed, raw_scores * score_scale - log_total[..., None], negative_big)
    probs = jnp.where(allowed, jnp.exp(shifted), 0.0)
    grad_probs = jnp.einsum(
        "rqhd,rkhd->rhqk", grad_heads, value_heads, preferred_element_type=jnp.float32
    )
    delta = jnp.sum(probs * grad_probs, axis=-1)
    grad_scores = (probs * (grad_probs - delta[..., None]) * score_scale).astype(jnp.bfloat16)
    grad_queries = jnp.einsum(
        "rhqk,rkhd->rqhd", grad_scores, key_heads, preferred_element_type=jnp.float32
    ).reshape(rows_here, shard_len, model_width)
    probs_low = probs.astype(jnp.bfloat16)

    def key_terms(span):
        grad_keys = jnp.einsum(
            "rhqk,rqhd->krhd", grad_scores, query_heads, preferred_element_type=jnp.float32
        )
        grad_values = jnp.einsum(
            "rhqk,rqhd->krhd", probs_low, grad_heads, preferred_element_type=jnp.float32
        )
        return jnp.concatenate(
            [
                grad_keys.reshape(span, rows_here, model_width),
                grad_values.reshape(span, rows_here, model_width),
            ],
            axis=-1,
        )

    if is_cross:
        pair_terms = lax.psum_scatter(
            key_terms(shard_len * lax.axis_size("seq")).astype(jnp.bfloat16),
            "seq",
            scatter_dimension=0,
            tiled=True,
        ).astype(jnp.float32)
    else:
        pair_terms = lax.psum_scatter(
            key_terms(shard_len * lax.axis_size("seq")).astype(jnp.bfloat16),
            "seq",
            scatter_dimension=0,
            tiled=True,
        ).astype(jnp.float32)
    return (grad_queries, pair_terms.transpose(1, 0, 2))


def layer_forward(hidden_in, doc_own, memory, memory_docs, weights, is_decoder):
    (
        qkv_weight,
        out_weight,
        in_weight,
        down_weight,
        gains_pair,
        query_weight,
        pair_weight,
        cross_weight,
        cross_gains,
    ) = weights
    model_width = hidden_in.shape[-1]
    mixed = matmul(hidden_in, qkv_weight).astype(jnp.bfloat16)
    attended, self_lse = attend(
        mixed[..., :model_width],
        mixed[..., model_width : 2 * model_width],
        mixed[..., 2 * model_width :],
        doc_own,
        doc_own,
        is_decoder,
        False,
    )
    attended = attended.astype(jnp.bfloat16)
    first, first_unit, first_inv = normalize(
        hidden_in.astype(jnp.float32) + matmul(attended, out_weight), gains_pair[0]
    )
    first_low = first.astype(jnp.bfloat16)
    cross_queries = matmul(first_low, query_weight).astype(jnp.bfloat16)
    pair = matmul(memory, pair_weight).astype(jnp.bfloat16)
    cross_att, cross_lse = attend(
        cross_queries,
        pair[..., :model_width],
        pair[..., model_width:],
        doc_own,
        memory_docs,
        False,
        True,
    )
    cross_att = cross_att.astype(jnp.bfloat16)
    second_cross, second_unit, second_inv = normalize(
        first + matmul(cross_att, cross_weight), cross_gains
    )
    second = jnp.where(is_decoder, second_cross, first)
    second_low = second.astype(jnp.bfloat16)
    upward = matmul(second_low, in_weight)
    active = jax.nn.silu(upward).astype(jnp.bfloat16)
    result, third_unit, third_inv = normalize(second + matmul(active, down_weight), gains_pair[1])
    saved = {
        "mixed": mixed,
        "attended": attended,
        "self_lse": self_lse,
        "first_unit": first_unit,
        "first_inv": first_inv,
        "first_low": first_low,
        "cross_queries": cross_queries,
        "pair": pair,
        "cross_att": cross_att,
        "cross_lse": cross_lse,
        "second_unit": second_unit,
        "second_inv": second_inv,
        "second_low": second_low,
        "upward": upward,
        "active": active,
        "third_unit": third_unit,
        "third_inv": third_inv,
    }
    return (result, saved)


def layer_backward(
    grad_result, saved, hidden_in, doc_own, memory, memory_docs, weights, is_decoder
):
    (
        qkv_weight,
        out_weight,
        in_weight,
        down_weight,
        gains_pair,
        query_weight,
        pair_weight,
        cross_weight,
        cross_gains,
    ) = weights
    model_width = hidden_in.shape[-1]
    grad_third, grad_gain_late = normalize_back(
        grad_result, saved["third_unit"], gains_pair[1], saved["third_inv"]
    )
    down_grad = grad_third.astype(jnp.bfloat16)
    grad_down_w = contract(saved["active"], down_grad)
    grad_active = matmul_back(down_grad, down_weight).astype(jnp.bfloat16)
    sigmoid_up = jax.nn.sigmoid(saved["upward"])
    grad_upward = (
        grad_active.astype(jnp.float32)
        * (sigmoid_up + saved["upward"] * sigmoid_up * (1.0 - sigmoid_up))
    ).astype(jnp.bfloat16)
    grad_in_w = contract(saved["second_low"], grad_upward)
    grad_second = grad_third + matmul_back(grad_upward, in_weight)
    grad_cross_sum, grad_cross_gain = normalize_back(
        grad_second, saved["second_unit"], cross_gains, saved["second_inv"]
    )
    decoder_flag = is_decoder.astype(jnp.float32)
    grad_cross_sum = grad_cross_sum * decoder_flag
    grad_cross_gain = grad_cross_gain * decoder_flag
    cross_branch = grad_cross_sum.astype(jnp.bfloat16)
    grad_cross_w = contract(saved["cross_att"], cross_branch)
    grad_cross_att = matmul_back(cross_branch, cross_weight).astype(jnp.bfloat16)
    pair = saved["pair"]
    grad_cross_q, grad_pair = attend_back(
        saved["cross_queries"],
        pair[..., :model_width],
        pair[..., model_width:],
        doc_own,
        memory_docs,
        False,
        saved["cross_lse"],
        grad_cross_att,
        True,
    )
    grad_cross_q = grad_cross_q.astype(jnp.bfloat16)
    grad_pair = grad_pair.astype(jnp.bfloat16)
    grad_query_w = contract(saved["first_low"], grad_cross_q)
    grad_pair_w = contract(memory, grad_pair)
    grad_memory = matmul_back(grad_pair, pair_weight)
    grad_first = jnp.where(
        is_decoder, grad_cross_sum + matmul_back(grad_cross_q, query_weight), grad_second
    )
    grad_first_sum, grad_gain_early = normalize_back(
        grad_first, saved["first_unit"], gains_pair[0], saved["first_inv"]
    )
    self_branch = grad_first_sum.astype(jnp.bfloat16)
    grad_out_w = contract(saved["attended"], self_branch)
    grad_attended = matmul_back(self_branch, out_weight).astype(jnp.bfloat16)
    mixed = saved["mixed"]
    grad_queries, grad_pair_self = attend_back(
        mixed[..., :model_width],
        mixed[..., model_width : 2 * model_width],
        mixed[..., 2 * model_width :],
        doc_own,
        doc_own,
        is_decoder,
        saved["self_lse"],
        grad_attended,
        False,
    )
    grad_mixed = jnp.concatenate([grad_queries, grad_pair_self], axis=-1).astype(jnp.bfloat16)
    grad_qkv_w = contract(hidden_in, grad_mixed)
    grad_hidden = grad_first_sum + matmul_back(grad_mixed, qkv_weight)
    layer_grads = (
        grad_qkv_w,
        grad_out_w,
        grad_in_w,
        grad_down_w,
        jnp.stack([grad_gain_early, grad_gain_late]),
        grad_query_w,
        grad_pair_w,
        grad_cross_w,
        grad_cross_gain,
    )
    return (grad_hidden, grad_memory, layer_grads)


def any_rows(
    layer_input,
    segment_ids,
    attn_qkv,
    attn_out,
    ffn_in,
    ffn_out,
    norm_gain,
    cross_query,
    cross_pair,
    cross_out,
    cross_gain,
    out_cotangent,
):
    micro_count = layer_input.shape[1]
    section_index = lax.axis_index("section")
    is_decoder = section_index == 1
    weights = (
        attn_qkv[0],
        attn_out[0],
        ffn_in[0],
        ffn_out[0],
        norm_gain[0],
        cross_query,
        cross_pair,
        cross_out,
        cross_gain,
    )
    inputs_all = layer_input[0]
    docs_all = segment_ids[0]
    slot_ids = jnp.arange(micro_count)
    received = (jnp.zeros_like(inputs_all[0]), jnp.zeros_like(docs_all[0]))
    results = jnp.zeros_like(inputs_all)
    memories = []
    memory_doc_list = []
    for step_index in range(micro_count + 1):
        batch_index = step_index - section_index
        is_valid = (batch_index >= 0) & (batch_index < micro_count)
        chosen = jnp.clip(batch_index, 0, micro_count - 1)
        hidden_in = lax.dynamic_index_in_dim(inputs_all, chosen, 0, keepdims=False)
        doc_own = lax.dynamic_index_in_dim(docs_all, chosen, 0, keepdims=False)
        memory = received[0]
        memory_docs = jnp.where(is_valid & is_decoder, received[1], doc_own)
        memories.append(memory)
        memory_doc_list.append(memory_docs)
        result, saved = layer_forward(hidden_in, doc_own, memory, memory_docs, weights, is_decoder)
        low_result = result.astype(jnp.bfloat16)
        writing = (slot_ids == chosen) & is_valid
        results = jnp.where(writing[:, None, None, None], low_result[None], results)
        if step_index < micro_count:
            received = from_behind((low_result, doc_own), "section", 1)
    memory_stack = jnp.stack(memories)
    memory_doc_stack = jnp.stack(memory_doc_list)
    totals = tuple((jnp.zeros(weight.shape, jnp.float32) for weight in weights))
    input_grads = jnp.zeros(inputs_all.shape, jnp.float32)
    returned = jnp.zeros(inputs_all.shape[1:], jnp.float32)
    for step_index in range(micro_count + 1):
        batch_index = micro_count - step_index - section_index
        is_valid = (batch_index >= 0) & (batch_index < micro_count)
        chosen = jnp.clip(batch_index, 0, micro_count - 1)
        forward_step = jnp.clip(batch_index + section_index, 0, micro_count)
        hidden_in = lax.dynamic_index_in_dim(inputs_all, chosen, 0, keepdims=False)
        doc_own = lax.dynamic_index_in_dim(docs_all, chosen, 0, keepdims=False)
        memory = lax.dynamic_index_in_dim(memory_stack, forward_step, 0, keepdims=False)
        memory_docs = lax.dynamic_index_in_dim(memory_doc_stack, forward_step, 0, keepdims=False)
        discarded, saved = layer_forward(
            hidden_in, doc_own, memory, memory_docs, weights, is_decoder
        )
        cotangent = jnp.where(
            is_decoder,
            lax.dynamic_index_in_dim(out_cotangent, chosen, 0, keepdims=False).astype(jnp.float32),
            returned,
        )
        grad_hidden, grad_memory, layer_grads = layer_backward(
            cotangent, saved, hidden_in, doc_own, memory, memory_docs, weights, is_decoder
        )
        valid_flag = is_valid.astype(jnp.float32)
        totals = tuple(
            (running + valid_flag * fresh for running, fresh in zip(totals, layer_grads))
        )
        writing = (slot_ids == chosen) & is_valid
        input_grads = jnp.where(writing[:, None, None, None], grad_hidden[None], input_grads)
        if step_index < micro_count:
            returned = from_behind(grad_memory.astype(jnp.bfloat16), "section", -1).astype(
                grad_memory.dtype
            )
    group_sums = lax.psum(
        (
            totals[0],
            totals[1],
            totals[2],
            totals[3],
            totals[4],
            totals[5],
            totals[6],
            totals[7],
            totals[8],
        ),
        ("seq", "dp"),
    )
    section_sums = group_sums[:5]
    cross_sums = (
        from_root(group_sums[5].astype(jnp.bfloat16), "section", 1).astype(jnp.float32),
        from_root(group_sums[6].astype(jnp.bfloat16), "section", 1).astype(jnp.float32),
        from_root(group_sums[7].astype(jnp.bfloat16), "section", 1).astype(jnp.float32),
        from_root(group_sums[8].astype(jnp.bfloat16), "section", 1).astype(jnp.float32),
    )
    return (
        results[None],
        input_grads[None],
        section_sums[0][None],
        section_sums[1][None],
        section_sums[2][None],
        section_sums[3][None],
        section_sums[4][None],
        cross_sums[0],
        cross_sums[1],
        cross_sums[2],
        cross_sums[3],
    )


def split_rows(
    layer_input,
    segment_ids,
    attn_qkv,
    attn_out,
    ffn_in,
    ffn_out,
    norm_gain,
    cross_query,
    cross_pair,
    cross_out,
    cross_gain,
    out_cotangent,
):
    micros = layer_input.shape[1]
    length, width = layer_input.shape[3:]
    hidden = ffn_in.shape[-1]
    q_tiles = length // TILE
    group = lax.axis_size("dp") // 2
    axes = ("section", "seq", "dp")
    decoder = lax.axis_index("section") == 1
    flag = decoder.astype(jnp.int32)
    x = lax.axis_index("seq")
    core = lax.rem(lax.axis_index("dp"), 2)
    z = lax.axis_index("dp") // 2
    places = [(t, i, k, c) for t in range(2) for i in range(2) for k in range(group) for c in range(2)]

    def number(t, i, k, c):
        return ((t * 2 + i) * group + k) * 2 + c

    def send(values, target, section=None):
        route = [
            (number(*place), number(*target(*place)))
            for place in places
            if section in (None, place[0]) and target(*place)
        ]
        return lax.ppermute(values, axes, route)

    def to_core(t, i, k, c):
        return (t, i, k, 1 - c)

    def to_x(t, i, k, c):
        return (t, 1 - i, k, c)

    def to_row(t, i, k, c):
        return (t, c, k, i)

    def to_decoder(t, i, k, c):
        return (1, i, k, c) if t == 0 else None

    def to_encoder(t, i, k, c):
        return (0, i, k, c) if t == 1 else None

    def fence(values, *before):
        return lax.optimization_barrier((values,) + before)[0]

    def exchange(values):
        return send(values, to_core)

    low = ((length, width), bf16)
    wide = ((length, width), f32)
    marked = ((length + 16, width), bf16)
    both = ((2 * length, width), bf16)
    keys_all = ((2 * length, 2 * width), bf16)
    mixing = ((width, 3 * width), bf16)
    inner = ((length, hidden), bf16)
    lse = ((q_tiles, 8, 2 * TILE), f32)
    stat = ((length, LANES), f32)
    square = ((width, width), bf16)
    rising = ((width, hidden), bf16)
    falling = ((hidden, width), bf16)
    gain_rows = ((8, width), f32)

    meta = jnp.stack([flag, core, x, z]).astype(jnp.int32)
    numbers = segment_ids[0, :, 0].astype(bf16)
    padding = jnp.zeros((15, width), bf16)
    with_numbers = [
        jnp.concatenate([layer_input[0, micro, 0], numbers[micro][None], padding])
        for micro in range(micros)
    ]
    own = [send(with_numbers[0], to_row)]
    for micro in range(1, micros):
        own.append(send(fence(with_numbers[micro], own[-1]), to_row))
    other = [exchange(own[0])]

    plain = dict(meta=meta)
    small = dict(gains=norm_gain[0])
    forward, memories, memories_other = [], [], []
    for micro in range(micros):
        call = launch(
            self_forward,
            micro,
            None,
            plain,
            small,
            dict(
                x_own_h=own[micro],
                x_other_h=other[micro],
                w_mixed_h=attn_qkv[0],
                w_out_h=attn_out[0],
                w_in_h=ffn_in[0],
                w_down_h=ffn_out[0],
            ),
            dict(
                q_o=low,
                kv_o=keys_all,
                att_o=low,
                lse_o=lse,
                unit1_o=wide,
                inv1_o=stat,
                first_low_o=low,
                memory_o=marked,
                ffn_low_o=low,
                act_o=inner,
                slope_o=inner,
                unit2_o=wide,
                inv2_o=stat,
            ),
            dict(
                **attention_scratch(length, width),
                **forward_scratch(length, width),
                x=both,
                w_mixed=mixing,
                w_out=square,
                w_in=rising,
                w_down=falling,
                unit1=wide,
                inv1=stat,
                first_low=low,
                memory=marked,
                act=inner,
                slope=inner,
                unit2=wide,
                inv2=stat,
                sum=wide,
            ),
            28,
            26,
            after=(forward[0].lse_o,) if micro else (),
        )
        forward.append(call)
        memories.append(send(call.memory_o, to_decoder))
        if micro + 1 < micros:
            other.append(exchange(fence(own[micro + 1], call.lse_o)))

    for micro in range(micros):
        memories_other.append(exchange(fence(memories[micro], forward[-1].lse_o)))
    cotangent = send(fence(out_cotangent[:, 0], forward[0].lse_o), to_row)

    cross, grads_memory, made = [], [], []
    after = (forward[-1].lse_o,)
    for micro in range(micros):
        done = forward[micro]
        call = launch(
            cross_both_ways,
            micro,
            1,
            plain,
            dict(**small, cross_gain=cross_gain[None]),
            dict(
                x_own_h=own[micro],
                memory_own_h=memories[micro],
                memory_other_h=memories_other[micro],
                w_pair_h=cross_pair,
                first_low_h=done.first_low_o,
                unit1_h=done.unit1_o,
                w_query_h=cross_query,
                w_cross_h=cross_out,
                w_in_h=ffn_in[0],
                w_down_h=ffn_out[0],
                cot_h=cotangent,
            ),
            dict(
                att_o=low,
                ffn_low_o=low,
                act_o=inner,
                decoded_o=low,
                down_grad_o=low,
                up_grad_o=inner,
                gain_grads_o=gain_rows,
                branch_o=low,
                dq_low_o=low,
                dkv_o=keys_all,
                part_own_o=wide,
                part_other_o=low,
                grad_first_o=wide,
            ),
            dict(
                **attention_scratch(length, width),
                **forward_scratch(length, width),
                **backward_scratch(length, width),
                x=both,
                w_pair=((width, 2 * width), bf16),
                first_low=low,
                unit1=wide,
                w_query=square,
                w_cross=square,
                w_in=rising,
                w_down=falling,
                cot=low,
                unit2=wide,
                inv2=stat,
                second_low=low,
                act=inner,
                slope=inner,
                sum=wide,
                decoded=low,
                keep=wide,
                down_grad=low,
                up_grad=inner,
                gain_grads=gain_rows,
                branch=low,
                part_own=wide,
            ),
            36,
            44,
            dict(act_o=done.act_o, ffn_low_o=done.ffn_low_o),
            after,
        )
        cross.append(call)
        away = call.part_other_o
        if micro:
            away = fence(away, grads_memory[-1])
        total = call.part_own_o + exchange(away).astype(f32)
        made.append(total.astype(bf16))
        after = (made[micro],)
        grads_memory.append(send(made[micro], to_encoder))

    def backward_feed(micro, after):
        done, late = forward[micro], cross[micro]
        return launch(
            feed_backward_alone,
            micro,
            0,
            plain,
            dict(gains=norm_gain[0]),
            dict(
                grad_memory_h=grads_memory[micro],
                unit2_h=done.unit2_o,
                inv2_h=done.inv2_o,
                slope_h=done.slope_o,
                w_in_h=ffn_in[0],
                w_down_h=ffn_out[0],
            ),
            dict(gain_late_o=gain_rows, down_grad_o=low, up_grad_o=inner, grad_first_o=wide),
            dict(
                cot=low,
                unit2=wide,
                inv2=stat,
                slope=inner,
                w_in=rising,
                w_down=falling,
                gain_grads=gain_rows,
                keep=wide,
                down_grad=low,
                up_grad=inner,
                sum=wide,
            ),
            12,
            10,
            dict(
                down_grad_o=late.down_grad_o, up_grad_o=late.up_grad_o, grad_first_o=late.grad_first_o
            ),
            after,
        )

    def backward_self(micro, side, grad_first, previous=None, after=(), halfway=None):
        done = forward[micro]
        heads = width // LANES
        given = dict(
            x_own_h=own[micro],
            x_other_h=other[micro],
            q_h=done.q_o,
            kv_h=done.kv_o,
            att_h=done.att_o,
            lse_h=done.lse_o,
        )
        ahead = dict(
            grad_first_h=grad_first,
            unit1_h=done.unit1_o,
            inv1_h=done.inv1_o,
            w_out_h=attn_out[0],
        )
        makes = dict(dq_low_o=low, dkv_o=keys_all)
        makes_first = dict(gain_early_o=gain_rows, branch_o=low)
        makes_last = dict(part_own_o=wide, part_other_o=low)
        scratch = dict(
            **attention_scratch(length, width),
            **backward_scratch(length, width),
            w_out=square,
            w_mixed=mixing,
            unit1=wide,
            inv1=stat,
            keep=wide,
            branch=low,
            grad_att=low,
            gain_grads=gain_rows,
        )

        def part(first, last, large, outs, work, previous, after):
            return launch(
                self_backward,
                (micro, first, last),
                side,
                plain,
                small,
                dict(**given, **large),
                dict(**makes, **outs),
                scratch,
                28,
                work,
                previous,
                after,
            )

        if halfway is None:
            large = dict(**ahead, w_mixed_h=attn_qkv[0])
            outs = dict(**makes_first, **makes_last)
            return part(0, heads, large, outs, 22, previous, after)
        outs = dict(**makes_first, grad_sum_o=wide, grad_att_o=low)
        one = part(0, heads // 2, ahead, outs, 12, None, after)
        large = dict(
            w_mixed_h=attn_qkv[0],
            grad_sum_h=one.grad_sum_o,
            grad_att_h=one.grad_att_o,
            dq_h=one.dq_low_o,
            dkv_h=one.dkv_o,
        )
        two = part(heads // 2, heads, large, makes_last, 12, None, halfway(one))
        return types.SimpleNamespace(**{**vars(one), **vars(two)})

    def weight_grads(plan, side, arrays, scratch, after=()):
        blocks = ((2, width, width), bf16)
        call = launch(
            contract_blocks,
            plan,
            side,
            plain,
            dict(),
            arrays,
            dict(sent_o=blocks, kept_o=blocks),
            dict(**scratch, blocks=((4, width, width), bf16)),
            36,
            8,
            after=after,
        )
        return call.sent_o, call.kept_o

    def first_sums(halves, section=None):
        sent, kept = halves
        got = send(sent, to_core, section)

        def block(side):
            return sum(
                lax.dynamic_index_in_dim(part, side, 0, keepdims=False).astype(f32)
                for part in (kept, got)
            )

        return block(1 - x).astype(bf16), block(x)

    def middle_sums(sums, section=None):
        away, total = sums
        return (total + send(away, to_x, section).astype(f32)).astype(bf16)

    def last_sums(total, later=(), section=None):
        shares = total.reshape(group, width // group, width)

        def share(step):
            return lax.dynamic_index_in_dim(shares, lax.rem(z + step, group), 0, keepdims=False)

        parts = [share(0)]
        for step in range(1, group):
            parts.append(send(share(step), along_z(step), section))
        if later:
            parts = [fence(part, *later) for part in parts]
        return sum(part.astype(f32) for part in parts).astype(bf16)

    def along_z(step):
        return lambda t, i, k, c: (t, i, (k + step) % group, c)

    groups = [[2 * k + c for k in range(group)] for c in range(2)]

    def swap_z(blocks):
        return lax.all_to_all(blocks, axes[2], 0, 0, axis_index_groups=groups, tiled=True)

    def sums_z(total):
        parts = swap_z(total.reshape(group, width // group, width))
        return jnp.sum(parts.astype(f32), axis=0).astype(bf16)

    def all_z(share):
        return swap_z(jnp.broadcast_to(share, (group,) + share.shape))

    def gather_z(share):
        return [share] + [send(share, along_z(step)) for step in range(1, group)]

    def gain_block(rows):
        filled = jnp.concatenate([jnp.stack(rows), jnp.zeros((16 - len(rows), width), f32)])
        return filled.astype(bf16)

    def spread(targets, own, own_x, outs, parts, turned=0):
        return launch(
            spread_pieces,
            (targets, turned),
            None,
            plain,
            dict(),
            dict(own_h=own, own_x_h=own_x, other_h=exchange(own), other_x_h=exchange(own_x)),
            outs,
            dict(
                pieces=((4,) + own.shape, bf16),
                wide=((4 * group * parts, width // group, width), f32),
            ),
            8 + 4 * group * parts,
            5,
        )

    tokens, all_tokens = micros * length, 2 * micros * length
    turn, turn_all = ((width, tokens), bf16), ((width, all_tokens), bf16)
    narrow, narrow_all = ((tokens, width), bf16), ((all_tokens, width), bf16)
    pair_all = ((all_tokens, 2 * width), bf16)
    deep = ((tokens, hidden), bf16)

    def part_of(buffer, *sources):
        return lambda column: (buffer, sources, column)

    def key_rows(buffer, sources):
        first, second = pl.ds(0, length), pl.ds(length, length)
        return part_of(buffer, *[source.at[rows] for rows in (first, second) for source in sources])

    def cross_plan(r):
        rows = pl.ds(0, length)
        low_part = part_of(r.low, r.low0_h, r.low1_h)
        att_part = part_of(r.att, r.att0_h, r.att1_h)
        dq_part = part_of(r.dq, r.dq0_h, r.dq1_h)
        branch_part = part_of(r.branch, r.branch0_h, r.branch1_h)
        sources = (r.mem0_h, r.mem1_h, r.mem2_h, r.mem3_h)
        mem_part = part_of(r.mem, *[source.at[rows] for source in sources])
        pair_part = key_rows(r.pair, (r.pair0_h, r.pair1_h))
        return [
            (r.turn, low_part(0), dq_part(0)),
            (r.turn_att, att_part(0), branch_part(0)),
            (r.turn_all, mem_part(0), pair_part(0)),
            (r.turn_all, mem_part(0), pair_part(1)),
        ]

    def rising_plan(r):
        low_part = part_of(r.low, r.low0_h, r.low1_h)
        up_part = part_of(r.up, r.up0_h, r.up1_h)
        return [(r.turn, low_part(0), up_part(block)) for block in range(4)]

    def falling_plan(r):
        act_part = part_of(r.act, r.act0_h, r.act1_h)
        down_part = part_of(r.down, r.down0_h, r.down1_h)
        return [(r.turn, act_part(block), down_part(0)) for block in range(4)]

    def self_plan(r):
        rows = pl.ds(0, length)
        sources = (r.x0_h, r.x1_h, r.x2_h, r.x3_h)
        x_part = part_of(r.x, *[source.at[rows] for source in sources])
        dq_part = part_of(r.dq, r.dq0_h, r.dq1_h)
        pair_part = key_rows(r.pair, (r.pair0_h, r.pair1_h))
        att_part = part_of(r.att, r.att0_h, r.att1_h)
        branch_part = part_of(r.branch, r.branch0_h, r.branch1_h)
        return [
            (r.turn_all, x_part(0), dq_part(0)),
            (r.turn_all, x_part(0), pair_part(0)),
            (r.turn_all, x_part(0), pair_part(1)),
            (r.turn, att_part(0), branch_part(0)),
        ]

    last = micros - 1
    feeds, ends = [None] * micros, [None] * micros
    results = jnp.stack(
        [
            jnp.where(decoder, call.decoded_o, done.memory_o[:length])
            for call, done in zip(cross, forward)
        ]
    )
    results = send(results, to_row)
    latest = made[last]

    def part_sum(micro, *before):
        end = ends[micro]
        away = fence(end.part_other_o, *before)
        total = (end.part_own_o + exchange(away).astype(f32)).astype(bf16)
        return total, send(total, to_row)

    steps = []
    for micro in range(last):
        feeds[micro] = backward_feed(micro, (latest,))
        first = feeds[micro].grad_first_o
        ends[micro] = backward_self(micro, 0, first)
        ends[micro] = backward_self(micro, 1, first, vars(ends[micro]), (made[last],))
        steps.append(part_sum(micro, grads_memory[last]))
        latest = ends[micro].gain_early_o
    feeds[last] = backward_feed(last, (latest,))

    rising_halves = weight_grads(
        rising_plan,
        None,
        dict(
            low0_h=cross[0].ffn_low_o,
            low1_h=cross[1].ffn_low_o,
            up0_h=feeds[0].up_grad_o,
            up1_h=feeds[1].up_grad_o,
        ),
        dict(low=narrow, up=deep, turn=turn),
        (results,) + tuple(step[0] for step in steps),
    )
    rising_sums = first_sums(rising_halves)
    rising_total = middle_sums(rising_sums)
    falling_halves = weight_grads(
        falling_plan,
        None,
        dict(
            act0_h=cross[0].act_o,
            act1_h=cross[1].act_o,
            down0_h=feeds[0].down_grad_o,
            down1_h=feeds[1].down_grad_o,
        ),
        dict(act=deep, down=narrow, turn=turn),
        (rising_sums[0],) + tuple(step[1] for step in steps),
    )
    cross_halves = weight_grads(
        cross_plan,
        1,
        dict(
            low0_h=forward[0].first_low_o,
            low1_h=forward[1].first_low_o,
            dq0_h=cross[0].dq_low_o,
            dq1_h=cross[1].dq_low_o,
            att0_h=cross[0].att_o,
            att1_h=cross[1].att_o,
            branch0_h=cross[0].branch_o,
            branch1_h=cross[1].branch_o,
            mem0_h=memories[0],
            mem1_h=memories[1],
            mem2_h=memories_other[0],
            mem3_h=memories_other[1],
            pair0_h=cross[0].dkv_o,
            pair1_h=cross[1].dkv_o,
        ),
        dict(
            low=narrow,
            dq=narrow,
            att=narrow,
            branch=narrow,
            mem=narrow_all,
            pair=pair_all,
            turn=turn,
            turn_att=turn,
            turn_all=turn_all,
        ),
        (falling_halves[0],),
    )
    falling_sent = fence(falling_halves[0], rising_total, cross_halves[0])
    falling_sums = first_sums((falling_sent, falling_halves[1]))
    cross_sums = first_sums(cross_halves, 1)
    falling_total = middle_sums(falling_sums)
    shares = []

    def halfway(one):
        shares.append(last_sums(rising_total, (one.gain_early_o,)))
        shares.append(send(fence(cross_sums[0], one.gain_early_o), to_x, 1))
        return (shares[0], falling_total)

    ends[last] = backward_self(
        last,
        None,
        feeds[last].grad_first_o,
        None,
        (falling_sums[0], cross_sums[0]),
        halfway,
    )
    rising_share, cross_arrived = shares
    falling_share = last_sums(falling_total, (ends[last].gain_early_o, ends[last].part_own_o))
    cross_total = cross_sums[1] + fence(cross_arrived, falling_share).astype(f32)
    cross_total = cross_total.astype(bf16)
    steps.append(part_sum(last, cross_total))
    one_own = gather_z(jnp.concatenate([rising_share, falling_share]))

    self_halves = weight_grads(
        self_plan,
        None,
        dict(
            x0_h=own[0],
            x1_h=own[1],
            x2_h=other[0],
            x3_h=other[1],
            dq0_h=ends[0].dq_low_o,
            dq1_h=ends[1].dq_low_o,
            pair0_h=ends[0].dkv_o,
            pair1_h=ends[1].dkv_o,
            att0_h=forward[0].att_o,
            att1_h=forward[1].att_o,
            branch0_h=ends[0].branch_o,
            branch1_h=ends[1].branch_o,
        ),
        dict(
            x=narrow_all,
            dq=narrow,
            pair=pair_all,
            att=narrow,
            branch=narrow,
            turn=turn,
            turn_all=turn_all,
        ),
        (steps[last][0],),
    )
    cross_share = last_sums(cross_total, (self_halves[0],), 1)
    away, total = first_sums(
        (fence(self_halves[0], cross_share, one_own[1], one_own[-1], steps[last][1]), self_halves[1])
    )
    third = sum(call.gain_grads_o[1] for call in cross)
    cross_share = jnp.concatenate([cross_share, gain_block([third])])
    cross_sent = send(cross_share, to_encoder)
    self_total = middle_sums((away, total))
    self_share = sums_z(self_total)
    one_own = jnp.stack([one_own[0]] + [fence(part, self_total) for part in one_own[1:]])
    one_own_x = send(one_own, to_x)
    cross_share = jnp.where(decoder, cross_share, fence(cross_sent, self_share))

    early = sum(end.gain_early_o[0] for end in ends)
    late = jnp.where(
        decoder,
        sum(call.gain_grads_o[0] for call in cross),
        sum(call.gain_late_o[0] for call in feeds),
    )
    two_own = all_z(jnp.concatenate([self_share, gain_block([early, late])]))
    two_own_x = send(fence(two_own, one_own_x), to_x)
    three_own = all_z(fence(cross_share, two_own))

    def columns(block):
        return pl.ds(block * width, width)

    def one_targets(r, block, row, rows):
        lines = pl.ds(row, rows)
        return [r.up_o.at[lines, columns(block)], r.down_o.at[pl.ds(block * width + row, rows)]]

    def two_targets(r, block, row, rows):
        lines = pl.ds(row, rows)
        return [r.out_o.at[lines] if block == 3 else r.mixed_o.at[lines, columns(block)]]

    def three_targets(r, block, row, rows):
        lines = pl.ds(row, rows)
        if block >= 2:
            return [r.pair_o.at[lines, columns(block - 2)]]
        return [(r.out_o if block else r.query_o).at[lines]]

    square_out = ((width, width), f32)
    one_own_x = fence(one_own_x, two_own)
    one_grads = spread(
        one_targets,
        one_own,
        one_own_x,
        dict(up_o=((width, hidden), f32), down_o=((hidden, width), f32)),
        2,
        1,
    )
    three_own_x = send(three_own, to_x)
    two_own_x = fence(two_own_x, one_grads.up_o, three_own)
    two_grads = spread(
        two_targets,
        two_own,
        two_own_x,
        dict(mixed_o=((width, 3 * width), f32), out_o=square_out, gains_o=((2, width), f32)),
        1,
    )
    three_own_x = fence(three_own_x, two_grads.out_o)
    three_grads = spread(
        three_targets,
        three_own,
        three_own_x,
        dict(
            query_o=square_out,
            pair_o=((width, 2 * width), f32),
            out_o=square_out,
            gains_o=((1, width), f32),
        ),
        1,
    )

    grad_input = jnp.stack([step[1] for step in steps])
    return (
        results[None, :, None],
        grad_input.astype(f32)[None, :, None],
        two_grads.mixed_o[None],
        two_grads.out_o[None],
        one_grads.up_o[None],
        one_grads.down_o[None],
        two_grads.gains_o[None],
        three_grads.query_o,
        three_grads.pair_o,
        three_grads.out_o,
        three_grads.gains_o[0],
    )


def shards(*arrays):
    layer_input = arrays[0]
    micros, rows, length = layer_input.shape[1:4]
    simple = (
        lax.axis_size("section") == 2
        and lax.axis_size("seq") == 2
        and lax.axis_size("dp") in (4, 8, 16)
        and (micros, rows) == (2, 1)
        and length == layer_input.shape[-1] == CHUNK
        and arrays[4].shape[-1] == 4 * CHUNK
    )
    return split_rows(*arrays) if simple else any_rows(*arrays)


def solution(mesh):
    in_specs = (
        P("section", None, "dp", "seq", None),
        P("section", None, "dp", "seq"),
        P("section", None, None),
        P("section", None, None),
        P("section", None, None),
        P("section", None, None),
        P("section", None, None),
        P(),
        P(),
        P(),
        P(),
        P(None, "dp", "seq", None),
    )
    out_specs = (
        P("section", None, "dp", "seq", None),
        P("section", None, "dp", "seq", None),
        P("section", None, None),
        P("section", None, None),
        P("section", None, None),
        P("section", None, None),
        P("section", None, None),
        P(),
        P(),
        P(),
        P(),
    )
    return jax.shard_map(shards, mesh=mesh, in_specs=in_specs, out_specs=out_specs, check_vma=False)
```

```python
import types

import jax
import jax.numpy as jnp
from jax import lax
from jax.experimental import pallas as pl
from jax.experimental.pallas import tpu as pltpu
from jax.sharding import PartitionSpec as P

HEADS = 8
TILE = 256
LANES = 128
CHUNK = 512

f32 = jnp.float32
bf16 = jnp.bfloat16
negative_big = -1e30
epsilon = 1e-05


def dot(left, right):
    return lax.dot_general(left, right, (((1,), (0,)), ((), ())), preferred_element_type=f32)


def dot_nt(left, right):
    return lax.dot_general(left, right, (((1,), (1,)), ((), ())), preferred_element_type=f32)


def dot_tn(left, right):
    return lax.dot_general(left, right, (((0,), (0,)), ((), ())), preferred_element_type=f32)


def standardize(values):
    center = values - jnp.mean(values, axis=-1, keepdims=True)
    inverse = lax.rsqrt(jnp.mean(center * center, axis=-1, keepdims=True) + epsilon)
    return center * inverse, inverse


def standardize_back(grad_out, standard, gain_row, inverse):
    scaled = grad_out * gain_row
    grad_in = inverse * (
        scaled
        - jnp.mean(scaled, axis=-1, keepdims=True)
        - standard * jnp.mean(scaled * standard, axis=-1, keepdims=True)
    )
    return grad_in, jnp.sum(grad_out * standard, axis=0, keepdims=True)


class Copies:
    def __init__(self, sems):
        self.sems = sems
        self.used = 0

    def start(self, source, target):
        copy = pltpu.make_async_copy(source, target, self.sems.at[self.used])
        self.used += 1
        copy.start()
        return copy


def wait_all(copies):
    for copy in copies:
        copy.wait()


def spread_pairs(target, source, factor, pairs):
    tiles = target.shape[1]
    half = lax.broadcasted_iota(jnp.int32, (TILE, LANES), 1) < LANES // 2
    first = jnp.where(half, factor, 0.0).astype(bf16)
    second = jnp.where(half, 0.0, factor).astype(bf16)
    for tile in range(tiles):
        for pair in pairs:
            block = source[tile * TILE : (tile + 1) * TILE, pair * LANES : (pair + 1) * LANES]
            target[pair, tile, :TILE, :] = block * first
            target[pair, tile, TILE:, :] = block * second


def turn_tiles(target, source, column, pairs):
    low, high = pairs[0] * LANES, (pairs[-1] + 1) * LANES
    for tile in range(target.shape[0]):
        block = source[tile * TILE : (tile + 1) * TILE, column + low : column + high]
        target[tile, low:high, :] = jnp.transpose(block)


def place_documents(r, copies):
    wait_all(copies)
    q_tiles = r.qd.shape[0]
    for part in range(3):
        row = r.docs[part].astype(f32)[0:1, :]
        for tile in range(q_tiles):
            piece = row[:, tile * TILE : (tile + 1) * TILE]
            slot = part * q_tiles + tile
            r.bounds[0, slot] = jnp.min(piece).astype(jnp.int32)
            r.bounds[1, slot] = jnp.max(piece).astype(jnp.int32)
            if part == 0:
                r.qd[tile] = jnp.broadcast_to(piece, (8, TILE))
        if part > 0:
            for start in range(0, row.shape[1], LANES):
                block = jnp.broadcast_to(row[:, start : start + LANES], (LANES, LANES))
                place = (part - 1) * row.shape[1] + start
                r.kdc[place : place + LANES, :] = jnp.transpose(block)


def load_documents(r, move, queries, own, other):
    rows = pl.ds(r.docs.shape[2], r.docs.shape[1])
    return [
        move.start(source.at[rows], r.docs.at[part])
        for part, source in enumerate((queries, own, other))
    ]


def tile_place(r, core, causal, q_tile, k_tile):
    q_tiles = r.qd.shape[0]
    length = q_tiles * TILE
    owner = jnp.where(k_tile < q_tiles, core, 1 - core)
    k_start = owner * length + lax.rem(k_tile, q_tiles) * TILE
    ahead = core * length + q_tile * TILE - k_start
    ahead = jnp.where(causal == 1, ahead, 2 * length * TILE)
    q_low, q_high = r.bounds[0, q_tile], r.bounds[1, q_tile]
    k_low, k_high = r.bounds[0, q_tiles + k_tile], r.bounds[1, q_tiles + k_tile]
    active = (q_low <= k_high) & (k_low <= q_high) & (ahead > -TILE)
    whole = (q_low == k_high) & (k_low == q_high) & (ahead >= TILE)
    return active, whole, ahead


def each_tile(place, body):
    active, whole, ahead = place
    pl.when(active & jnp.logical_not(whole))(lambda: body(ahead))
    pl.when(whole)(lambda: body(None))


def fill_bias(r, q_tile, k_tile, ahead):
    keys = r.kdc[pl.ds(pl.multiple_of(k_tile * TILE, TILE), TILE), :]
    shift = lax.broadcasted_iota(jnp.int32, (TILE, LANES), 0) - lax.broadcasted_iota(
        jnp.int32, (TILE, LANES), 1
    )
    queries = r.qd[q_tile]
    for start in range(0, TILE, LANES):
        same = keys == queries[0:1, start : start + LANES]
        allowed = same & (shift - start <= ahead)
        r.bias[:, start : start + LANES] = jnp.where(allowed, 0.0, negative_big)


def attention_forward(r, core, causal):
    pairs, q_tiles = r.qm.shape[:2]
    k_tiles = r.vt.shape[0]

    def one_query_tile(q_tile, carry):
        r.top[...] = jnp.full(r.top.shape, negative_big, f32)
        r.total[...] = jnp.zeros(r.total.shape, f32)
        r.turned[...] = jnp.zeros(r.turned.shape, f32)

        def one_key_tile(k_tile, inner):
            def one_tile(ahead):
                if ahead is not None:
                    fill_bias(r, q_tile, k_tile, ahead)
                rows = pl.ds(pl.multiple_of(k_tile * TILE, TILE), TILE)

                def raw(pair):
                    keys = r.kv[rows, pair * LANES : (pair + 1) * LANES]
                    return dot_nt(keys, r.qm[pair, q_tile])

                raw_next = raw(0)
                for pair in range(pairs):
                    scores = raw_next
                    if ahead is not None:
                        bias = r.bias[...]
                        scores = scores + jnp.concatenate([bias, bias], axis=1)
                    if pair + 1 < pairs:
                        raw_next = raw(pair + 1)
                    old_top = r.top[pair : pair + 1, :]
                    new_top = jnp.maximum(old_top, jnp.max(scores, axis=0, keepdims=True))
                    weights = jnp.exp(scores - new_top)
                    shrink = jnp.exp(old_top - new_top)
                    r.top[pair : pair + 1, :] = new_top
                    r.total[pair : pair + 1, :] = r.total[
                        pair : pair + 1, :
                    ] * shrink + jnp.sum(weights, axis=0, keepdims=True)
                    low = weights.astype(bf16)
                    for side in range(2):
                        span = slice(side * TILE, (side + 1) * TILE)
                        head = slice((2 * pair + side) * 64, (2 * pair + side + 1) * 64)
                        r.turned[head, :] = r.turned[head, :] * shrink[:, span] + dot(
                            r.vt[k_tile, head, :], low[:, span]
                        )

            each_tile(tile_place(r, core, causal, q_tile, k_tile), one_tile)
            return inner

        lax.fori_loop(0, k_tiles, one_key_tile, 0)
        for pair in range(pairs):
            total = r.total[pair : pair + 1, :]
            r.lse[q_tile, pair : pair + 1, :] = r.top[pair : pair + 1, :] + jnp.log(total)
            share = 1.0 / total
            for side in range(2):
                span = slice(side * TILE, (side + 1) * TILE)
                head = slice((2 * pair + side) * 64, (2 * pair + side + 1) * 64)
                r.turned[head, :] = r.turned[head, :] * share[:, span]
        rows = pl.ds(pl.multiple_of(q_tile * TILE, TILE), TILE)
        r.att[rows, :] = jnp.transpose(r.turned[...]).astype(bf16)
        return carry

    lax.fori_loop(0, q_tiles, one_query_tile, 0)


def row_products(r, grad_att, pairs):
    low, high = pairs[0] * LANES, (pairs[-1] + 1) * LANES
    for tile in range(r.qm.shape[1]):
        rows = slice(tile * TILE, (tile + 1) * TILE)
        product = jnp.transpose(
            grad_att[rows, low:high].astype(f32) * r.att[rows, low:high].astype(f32)
        )
        for pair in pairs:
            for side in range(2):
                head = (2 * pair + side) * 64 - low
                r.delta[tile, pair : pair + 1, side * TILE : (side + 1) * TILE] = jnp.sum(
                    product[head : head + 64, :], axis=0, keepdims=True
                )


def attention_backward(r, core, causal, pairs):
    q_tiles, k_tiles = r.qm.shape[1], r.kt.shape[0]
    width = r.kt.shape[1]
    low, high = pairs[0] * LANES, (pairs[-1] + 1) * LANES
    for start in (0, width):
        r.dkv[:, start + low : start + high] = jnp.zeros((r.dkv.shape[0], high - low), f32)

    def one_query_tile(q_tile, carry):
        r.turned[low:high, :] = jnp.zeros((high - low, TILE), f32)

        def one_key_tile(k_tile, inner):
            def one_tile(ahead):
                if ahead is not None:
                    fill_bias(r, q_tile, k_tile, ahead)
                rows = pl.ds(pl.multiple_of(k_tile * TILE, TILE), TILE)

                def raw(pair):
                    lanes = slice(pair * LANES, (pair + 1) * LANES)
                    lanes_v = slice(width + pair * LANES, width + (pair + 1) * LANES)
                    return (
                        dot_nt(r.kv[rows, lanes], r.qm[pair, q_tile]),
                        dot_nt(r.kv[rows, lanes_v], r.gm[pair, q_tile]),
                    )

                raw_next = raw(pairs[0])
                for pair in pairs:
                    scores, grad_probs = raw_next
                    if ahead is not None:
                        bias = r.bias[...]
                        scores = scores + jnp.concatenate([bias, bias], axis=1)
                    if pair < pairs[-1]:
                        raw_next = raw(pair + 1)
                    probs = jnp.exp(scores - r.lse[q_tile, pair : pair + 1, :])
                    grad_scores = probs * (grad_probs - r.delta[q_tile, pair : pair + 1, :])
                    probs_low = probs.astype(bf16)
                    grad_low = grad_scores.astype(bf16)
                    lanes = slice(pair * LANES, (pair + 1) * LANES)
                    lanes_v = slice(width + pair * LANES, width + (pair + 1) * LANES)
                    r.dkv[rows, lanes] += dot(grad_low, r.qm[pair, q_tile])
                    r.dkv[rows, lanes_v] += dot(probs_low, r.gm[pair, q_tile])
                    for side in range(2):
                        span = slice(side * TILE, (side + 1) * TILE)
                        head = slice((2 * pair + side) * 64, (2 * pair + side + 1) * 64)
                        r.turned[head, :] += dot(r.kt[k_tile, head, :], grad_low[:, span])

            each_tile(tile_place(r, core, causal, q_tile, k_tile), one_tile)
            return inner

        lax.fori_loop(0, k_tiles, one_key_tile, 0)
        rows = pl.ds(pl.multiple_of(q_tile * TILE, TILE), TILE)
        r.dq[rows, low:high] = jnp.transpose(r.turned[low:high, :]) * (64**-0.5)
        return carry

    lax.fori_loop(0, q_tiles, one_query_tile, 0)


def feed_forward(r, low):
    chunks = [slice(at, at + CHUNK) for at in range(0, r.w_in.shape[1], CHUNK)]
    upward_next = dot(low[...], r.w_in[:, chunks[0]])
    for place, span in enumerate(chunks):
        upward = upward_next
        if place + 1 < len(chunks):
            upward_next = dot(low[...], r.w_in[:, chunks[place + 1]])
        gate = jax.nn.sigmoid(upward)
        active = (upward * gate).astype(bf16)
        r.act[:, span] = active
        r.slope[:, span] = (gate + upward * gate * (1.0 - gate)).astype(r.slope.dtype)
        part = dot(active, r.w_down[span, :])
        if place:
            r.sum[...] += part
        else:
            r.sum[...] = part


def feed_backward(r):
    chunks = [slice(at, at + CHUNK) for at in range(0, r.w_in.shape[1], CHUNK)]
    active_next = dot_nt(r.down_grad[...], r.w_down[chunks[0], :])
    for place, span in enumerate(chunks):
        grad_active = active_next.astype(bf16)
        if place + 1 < len(chunks):
            active_next = dot_nt(r.down_grad[...], r.w_down[chunks[place + 1], :])
        grad_up = (grad_active.astype(f32) * r.slope[:, span].astype(f32)).astype(bf16)
        r.up_grad[:, span] = grad_up
        part = dot_nt(grad_up, r.w_in[:, span])
        if place:
            r.sum[...] += part
        else:
            r.sum[...] = part


def self_forward(r):
    length, width = r.unit1.shape
    decoder, core = r.meta[0], r.meta[1]
    move = Copies(r.sems)
    whole = pl.ds(0, length)
    documents = load_documents(r, move, r.x_own_h, r.x_own_h, r.x_other_h)
    early = [
        move.start(r.x_own_h.at[whole], r.x.at[whole]),
        move.start(r.x_other_h.at[whole], r.x.at[pl.ds(length, length)]),
        move.start(r.w_mixed_h, r.w_mixed),
    ]
    later = [
        move.start(r.w_out_h, r.w_out),
        move.start(r.w_in_h, r.w_in),
        move.start(r.w_down_h, r.w_down),
    ]
    place_documents(r, documents)
    wait_all(early)
    r.q[...] = dot(r.x[:length, :], r.w_mixed[:, :width]).astype(bf16)
    r.kv[...] = dot(r.x[...], r.w_mixed[:, width:]).astype(bf16)
    outs = [move.start(r.q, r.q_o), move.start(r.kv, r.kv_o)]
    pairs = range(width // LANES)
    spread_pairs(r.qm, r.q, 64**-0.5, pairs)
    turn_tiles(r.vt, r.kv, width, pairs)
    attention_forward(r, core, decoder)
    wait_all(later)
    outs += [move.start(r.att, r.att_o), move.start(r.lse, r.lse_o)]
    unit, inverse = standardize(r.x[:length, :].astype(f32) + dot(r.att[...], r.w_out[...]))
    r.unit1[...] = unit
    r.inv1[...] = jnp.broadcast_to(inverse, r.inv1.shape)
    r.first_low[...] = (unit * r.gains[0:1, :]).astype(bf16)
    outs += [
        move.start(r.unit1, r.unit1_o),
        move.start(r.inv1, r.inv1_o),
        move.start(r.first_low, r.first_low_o),
    ]

    @pl.when(decoder == 0)
    def _():
        feed_forward(r, r.first_low)
        late = [
            move.start(r.first_low, r.ffn_low_o),
            move.start(r.act, r.act_o),
            move.start(r.slope, r.slope_o),
        ]
        unit2, inverse2 = standardize(r.unit1[...] * r.gains[0:1, :] + r.sum[...])
        r.memory[:length, :] = (unit2 * r.gains[1:2, :]).astype(bf16)
        r.memory[length:, :] = r.docs[0]
        late += [move.start(r.memory, r.memory_o)]
        r.unit2[...] = unit2
        r.inv2[...] = jnp.broadcast_to(inverse2, r.inv2.shape)
        late += [move.start(r.unit2, r.unit2_o), move.start(r.inv2, r.inv2_o)]
        wait_all(late)

    wait_all(outs)


def cross_both_ways(r):
    length, width = r.unit1_h.shape
    core = r.meta[1]
    move = Copies(r.sems)
    whole = pl.ds(0, length)
    documents = load_documents(r, move, r.x_own_h, r.memory_own_h, r.memory_other_h)
    moves = [
        move.start(r.memory_own_h.at[whole], r.x.at[whole]),
        move.start(r.memory_other_h.at[whole], r.x.at[pl.ds(length, length)]),
        move.start(r.w_pair_h, r.w_pair),
        move.start(r.first_low_h, r.first_low),
        move.start(r.w_query_h, r.w_query),
    ]
    later = [
        move.start(r.unit1_h, r.unit1),
        move.start(r.w_cross_h, r.w_cross),
        move.start(r.w_in_h, r.w_in),
        move.start(r.w_down_h, r.w_down),
        move.start(r.cot_h.at[r.micro], r.cot),
    ]
    place_documents(r, documents)
    wait_all(moves)
    r.kv[...] = dot(r.x[...], r.w_pair[...]).astype(bf16)
    r.q[...] = dot(r.first_low[...], r.w_query[...]).astype(bf16)
    pairs = range(width // LANES)
    spread_pairs(r.qm, r.q, 64**-0.5, pairs)
    turn_tiles(r.vt, r.kv, width, pairs)
    turn_tiles(r.kt, r.kv, 0, pairs)
    attention_forward(r, core, 0)
    outs = [move.start(r.att, r.att_o)]
    wait_all(later)
    first = r.unit1[...] * r.gains[0:1, :]
    unit, inverse = standardize(first + dot(r.att[...], r.w_cross[...]))
    r.unit2[...] = unit
    r.inv2[...] = jnp.broadcast_to(inverse, r.inv2.shape)
    r.second_low[...] = (unit * r.cross_gain[...]).astype(bf16)
    outs += [move.start(r.second_low, r.ffn_low_o)]
    feed_forward(r, r.second_low)
    outs += [move.start(r.act, r.act_o)]
    unit3, inverse3 = standardize(r.unit2[...] * r.cross_gain[...] + r.sum[...])
    r.decoded[...] = (unit3 * r.gains[1:2, :]).astype(bf16)
    outs += [move.start(r.decoded, r.decoded_o)]
    grad_third, gain_late = standardize_back(
        r.cot[...].astype(f32), unit3, r.gains[1:2, :], inverse3
    )
    r.keep[...] = grad_third
    r.down_grad[...] = grad_third.astype(bf16)
    outs += [move.start(r.down_grad, r.down_grad_o)]
    feed_backward(r)
    outs += [move.start(r.up_grad, r.up_grad_o)]
    grad_sum, gain_cross = standardize_back(
        r.keep[...] + r.sum[...], r.unit2[...], r.cross_gain[...], r.inv2[:, 0:1]
    )
    r.gain_grads[...] = jnp.zeros(r.gain_grads.shape, f32)
    r.gain_grads[0:1, :] = gain_late
    r.gain_grads[1:2, :] = gain_cross
    r.keep[...] = grad_sum
    r.branch[...] = grad_sum.astype(bf16)
    outs += [move.start(r.gain_grads, r.gain_grads_o), move.start(r.branch, r.branch_o)]
    r.q[...] = dot_nt(r.branch[...], r.w_cross[...]).astype(bf16)
    spread_pairs(r.gm, r.q, 1.0, pairs)
    row_products(r, r.q, pairs)
    attention_backward(r, core, 0, pairs)
    r.dq_low[...] = r.dq[...].astype(bf16)
    r.keep[...] += dot_nt(r.dq_low[...], r.w_query[...])
    outs += [move.start(r.dq_low, r.dq_low_o), move.start(r.keep, r.grad_first_o)]
    r.dkv_low[...] = r.dkv[...].astype(bf16)
    outs += [move.start(r.dkv_low, r.dkv_o)]
    part = dot_nt(r.dkv_low[...], r.w_pair[...])
    r.part_other[...] = part[length:, :].astype(bf16)
    r.part_own[...] = part[:length, :]
    outs += [move.start(r.part_other, r.part_other_o), move.start(r.part_own, r.part_own_o)]
    wait_all(outs)


def feed_backward_alone(r):
    move = Copies(r.sems)
    early = [
        move.start(r.grad_memory_h, r.cot),
        move.start(r.unit2_h, r.unit2),
        move.start(r.inv2_h, r.inv2),
    ]
    later = [
        move.start(r.w_down_h, r.w_down),
        move.start(r.slope_h, r.slope),
        move.start(r.w_in_h, r.w_in),
    ]
    wait_all(early)
    grad_third, gain_late = standardize_back(
        r.cot[...].astype(f32), r.unit2[...], r.gains[1:2, :], r.inv2[:, 0:1]
    )
    r.gain_grads[...] = jnp.broadcast_to(gain_late, r.gain_grads.shape)
    r.keep[...] = grad_third
    r.down_grad[...] = grad_third.astype(bf16)
    outs = [move.start(r.down_grad, r.down_grad_o), move.start(r.gain_grads, r.gain_late_o)]
    wait_all(later)
    feed_backward(r)
    outs += [move.start(r.up_grad, r.up_grad_o)]
    r.keep[...] += r.sum[...]
    outs += [move.start(r.keep, r.grad_first_o)]
    wait_all(outs)


def self_backward(r, plan):
    r.micro, first, last = plan
    length, width = r.att_h.shape
    decoder, core = r.meta[0], r.meta[1]
    pairs = range(first, last)
    low, high = first * LANES, last * LANES
    move = Copies(r.sems)
    later = [
        move.start(r.q_h, r.q),
        move.start(r.kv_h, r.kv),
        move.start(r.att_h, r.att),
        move.start(r.lse_h, r.lse),
    ]
    if first == 0:
        early = [
            move.start(r.grad_first_h, r.keep),
            move.start(r.unit1_h, r.unit1),
            move.start(r.inv1_h, r.inv1),
            move.start(r.w_out_h, r.w_out),
        ]
    else:
        early = [move.start(r.grad_att_h, r.grad_att)]
    outs = []
    place_documents(r, load_documents(r, move, r.x_own_h, r.x_own_h, r.x_other_h))
    wait_all(early)
    if first == 0:
        grad_sum, gain_early = standardize_back(
            r.keep[...], r.unit1[...], r.gains[0:1, :], r.inv1[:, 0:1]
        )
        r.gain_grads[...] = jnp.broadcast_to(gain_early, r.gain_grads.shape)
        r.keep[...] = grad_sum
        r.branch[...] = grad_sum.astype(bf16)
        r.grad_att[...] = dot_nt(r.branch[...], r.w_out[...]).astype(bf16)
        outs += [move.start(r.gain_grads, r.gain_early_o), move.start(r.branch, r.branch_o)]
        if last < width // LANES:
            outs += [move.start(r.keep, r.grad_sum_o), move.start(r.grad_att, r.grad_att_o)]
    wait_all(later)
    if last == width // LANES:
        ends = [move.start(r.w_mixed_h, r.w_mixed)]
        if first > 0:
            ends += [
                move.start(r.grad_sum_h, r.keep),
                move.start(r.dq_h.at[:, pl.ds(0, low)], r.dq_low.at[:, pl.ds(0, low)]),
                move.start(r.dkv_h.at[:, pl.ds(0, low)], r.dkv_low.at[:, pl.ds(0, low)]),
                move.start(
                    r.dkv_h.at[:, pl.ds(width, low)], r.dkv_low.at[:, pl.ds(width, low)]
                ),
            ]
    spread_pairs(r.qm, r.q, 64**-0.5, pairs)
    turn_tiles(r.kt, r.kv, 0, pairs)
    spread_pairs(r.gm, r.grad_att, 1.0, pairs)
    row_products(r, r.grad_att, pairs)
    attention_backward(r, core, decoder, pairs)
    r.dq_low[:, low:high] = r.dq[:, low:high].astype(bf16)
    for start in (0, width):
        span = slice(start + low, start + high)
        r.dkv_low[:, span] = r.dkv[:, span].astype(bf16)
    if last == width // LANES:
        wait_all(ends)
        outs += [move.start(r.dq_low, r.dq_low_o), move.start(r.dkv_low, r.dkv_o)]
        r.keep[...] += dot_nt(r.dq_low[...], r.w_mixed[:, :width])
        part = dot_nt(r.dkv_low[...], r.w_mixed[:, width:])
        r.part_other[...] = part[length:, :].astype(bf16)
        r.keep[...] += part[:length, :]
        outs += [move.start(r.part_other, r.part_other_o), move.start(r.keep, r.part_own_o)]
    else:
        outs.append(move.start(r.dq_low.at[:, pl.ds(low, high - low)], r.dq_low_o.at[:, pl.ds(low, high - low)]))
        for start in (0, width):
            span = pl.ds(start + low, high - low)
            outs.append(move.start(r.dkv_low.at[:, span], r.dkv_o.at[:, span]))
    wait_all(outs)


def contract_blocks(r, plan):
    for core in range(2):

        @pl.when(r.meta[1] == core)
        def _(core=core):
            targets = [None] * 4
            for half in range(2):
                target = r.kept_o if half == core else r.sent_o
                targets[2 * half], targets[2 * half + 1] = target.at[0], target.at[1]
            order = (0, 1, 2, 3) if core else (2, 3, 0, 1)
            contract_in_order(r, plan(r), order, targets, Copies(r.sems))


def contract_in_order(r, blocks, order, targets, move):
    loads = dict()
    for slot in order:
        for buffer, sources, at in blocks[slot][1:]:
            if (id(buffer), at) not in loads:
                span = pl.ds(at * CHUNK, CHUNK)
                row = 0
                copies = []
                for source in sources:
                    rows = pl.ds(row, source.shape[0])
                    copies.append(move.start(source.at[:, span], buffer.at[rows, span]))
                    row += source.shape[0]
                loads[id(buffer), at] = copies
    outs = []
    held = dict()
    for slot in order:
        turn, (left, _, left_at), (right, _, right_at) = blocks[slot]
        wait_all(loads.pop((id(left), left_at), ()))
        wait_all(loads.pop((id(right), right_at), ()))
        if held.get(id(turn)) != left_at:
            for row in range(0, left.shape[0], CHUNK):
                block = left[row : row + CHUNK, left_at * CHUNK : (left_at + 1) * CHUNK]
                turn[:, row : row + CHUNK] = jnp.transpose(block)
            held[id(turn)] = left_at
        block = right[:, right_at * CHUNK : (right_at + 1) * CHUNK]
        r.blocks[slot] = dot(turn[:, : right.shape[0]], block).astype(bf16)
        outs.append(move.start(r.blocks.at[slot], targets[slot]))
    wait_all(outs)


def spread_pieces(r, targets):
    group, height = r.own_h.shape[:2]
    rows = r.own_h.shape[2] // group
    for core in range(2):
        for x in range(2):

            @pl.when((r.meta[1] == core) & (r.meta[2] == x))
            def _(core=core, x=x):
                move = Copies(r.sems)
                parts = [
                    (r.own_h, core, x),
                    (r.own_x_h, core, 1 - x),
                    (r.other_h, 1 - core, x),
                    (r.other_x_h, 1 - core, 1 - x),
                ]
                loads = [
                    move.start(source, r.pieces.at[place])
                    for place, (source, _, _) in enumerate(parts)
                ]
                outs = []
                slot = 0
                gains = None
                for place, (_, half, side) in enumerate(parts):
                    loads[place].wait()
                    for step in range(group):
                        row = step * rows
                        start = 0
                        for target in targets(r, 2 * half + side, row, rows):
                            r.wide[slot] = r.pieces[place, step, start : start + rows].astype(f32)
                            outs.append(move.start(r.wide.at[slot], target))
                            slot += 1
                            start += rows
                        if start < height:
                            extra = r.pieces[place, step, start:height].astype(f32)
                            gains = extra if gains is None else gains + extra
                r.gains_o[...] = gains[: r.gains_o.shape[0], :]
                wait_all(outs)


def launch(kernel, plan, side, scalars, small, large, outs, scratch, copies, work, previous=None, after=()):
    names = list(scalars) + list(small) + list(large)
    arrays = list(scalars.values()) + list(small.values()) + list(large.values())
    specs = (
        [pl.BlockSpec(memory_space=pltpu.SMEM)] * len(scalars)
        + [pl.BlockSpec(memory_space=pltpu.VMEM)] * len(small)
        + [pl.BlockSpec(memory_space=pl.ANY)] * len(large)
    )
    aliases = dict()
    for position, name in enumerate(outs):
        if previous and name in previous:
            aliases[len(arrays)] = position
            names.append("previous_" + name)
            arrays.append(previous[name])
            specs.append(pl.BlockSpec(memory_space=pl.ANY))
    for array in after:
        names.append("")
        arrays.append(array)
        specs.append(pl.BlockSpec(memory_space=pl.ANY))
    names += list(outs) + list(scratch) + ["sems"]

    def body(*refs):
        r = types.SimpleNamespace(**dict(zip(names, refs)))

        def run():
            if isinstance(plan, int):
                r.micro = plan
                kernel(r)
            else:
                kernel(r, plan)

        if side is None:
            run()
        else:
            pl.when(r.meta[0] == side)(run)

    results = pl.pallas_call(
        body,
        out_shape=[jax.ShapeDtypeStruct(*shape) for shape in outs.values()],
        in_specs=specs,
        out_specs=[
            pl.BlockSpec(memory_space=pltpu.VMEM if shape[0][0] < 8 else pl.ANY)
            for shape in outs.values()
        ],
        scratch_shapes=[
            pltpu.SMEM(*shape) if shape[1] == jnp.int32 else pltpu.VMEM(*shape)
            for shape in scratch.values()
        ]
        + [pltpu.SemaphoreType.DMA((copies,))],
        input_output_aliases=aliases,
        compiler_params=pltpu.CompilerParams(vmem_limit_bytes=58 * 1024 * 1024),
        cost_estimate=pl.CostEstimate(
            flops=work * 10**9, bytes_accessed=1 << 20, transcendentals=0
        ),
    )(*arrays)
    return types.SimpleNamespace(**dict(zip(outs, results)))


def attention_scratch(length, width):
    pairs, q_tiles, k_tiles = width // LANES, length // TILE, 2 * length // TILE
    return dict(
        q=((length, width), bf16),
        kv=((2 * length, 2 * width), bf16),
        qm=((pairs, q_tiles, 2 * TILE, LANES), bf16),
        kdc=((2 * length, LANES), f32),
        docs=((3, 16, width), bf16),
        qd=((length // TILE, 8, TILE), f32),
        bounds=((2, 3 * length // TILE), jnp.int32),
        bias=((TILE, TILE), f32),
        lse=((q_tiles, 8, 2 * TILE), f32),
        att=((length, width), bf16),
        turned=((width, TILE), f32),
    )


def forward_scratch(length, width):
    k_tiles = 2 * length // TILE
    return dict(
        vt=((k_tiles, width, TILE), bf16),
        top=((8, 2 * TILE), f32),
        total=((8, 2 * TILE), f32),
    )


def backward_scratch(length, width):
    pairs, q_tiles, k_tiles = width // LANES, length // TILE, 2 * length // TILE
    return dict(
        kt=((k_tiles, width, TILE), bf16),
        gm=((pairs, q_tiles, 2 * TILE, LANES), bf16),
        delta=((q_tiles, 8, 2 * TILE), f32),
        dkv=((2 * length, 2 * width), f32),
        dq=((length, width), f32),
        dkv_low=((2 * length, 2 * width), bf16),
        part_other=((length, width), bf16),
        dq_low=((length, width), bf16),
    )


def for_sending(shard):

    def short(part):
        return part.astype(jnp.bfloat16) if part.dtype == jnp.float32 else part

    return jax.tree.map(short, shard)


def from_behind(block, axis, distance):
    devices = range(lax.axis_size(axis))
    route = [(i - distance, i) for i in devices if i - distance in devices]
    return lax.ppermute(block, axis, route)


def from_root(shard, axis, root):
    mine = lax.axis_index(axis) == root
    return lax.psum(jnp.where(mine, shard, jnp.zeros_like(shard)), axis)


def matmul(left_side, right_side):
    return jnp.einsum("rsd,de->rse", left_side, right_side, preferred_element_type=jnp.float32)


def matmul_back(left_side, right_side):
    return jnp.einsum("rse,de->rsd", left_side, right_side, preferred_element_type=jnp.float32)


def contract(left_side, right_side):
    return jnp.einsum("rsd,rse->de", left_side, right_side, preferred_element_type=jnp.float32)


def normalize(values, gain_row):
    center = values - jnp.mean(values, axis=-1, keepdims=True)
    inverse = lax.rsqrt(jnp.mean(center * center, axis=-1, keepdims=True) + epsilon)
    standard = center * inverse
    return (standard * gain_row, standard, inverse)


def normalize_back(grad_out, standard, gain_row, inverse):
    scaled = grad_out * gain_row
    grad_in = inverse * (
        scaled
        - jnp.mean(scaled, axis=-1, keepdims=True)
        - standard * jnp.mean(scaled * standard, axis=-1, keepdims=True)
    )
    return (grad_in, jnp.sum(grad_out * standard, axis=(0, 1)))


def allowed_mask(query_docs, key_docs, query_place, key_place, causal):
    same_doc = query_docs[:, :, None] == key_docs[:, None, :]
    earlier = query_place[:, None] >= key_place[None, :]
    return (same_doc & (earlier | jnp.logical_not(causal)))[:, None]


def attend(queries, keys_local, values_local, query_docs, key_docs, causal, is_cross):
    rows_here, shard_len, model_width = queries.shape
    head_dim = model_width // HEADS
    score_scale = head_dim ** (-0.5)
    query_place = lax.axis_index("seq") * shard_len + jnp.arange(shard_len)
    query_heads = queries.reshape(rows_here, shard_len, HEADS, head_dim)

    def absorb(state_tuple, pieces):
        running_top, running_total, running_sum = state_tuple
        key_piece, value_piece, doc_piece = pieces
        piece_len = key_piece.shape[1]
        raw_scores = jnp.einsum(
            "rqhd,rkhd->rhqk",
            query_heads,
            key_piece.reshape(rows_here, piece_len, HEADS, head_dim),
            preferred_element_type=jnp.float32,
        )
        allowed = allowed_mask(query_docs, doc_piece, query_place, jnp.arange(piece_len), causal)
        scores = jnp.where(allowed, raw_scores * score_scale, negative_big)
        new_top = jnp.maximum(running_top, jnp.max(scores, axis=-1))
        weights = jnp.where(allowed, jnp.exp(scores - new_top[..., None]), 0.0)
        new_total = jnp.sum(weights, axis=-1)
        product = jnp.einsum(
            "rhqk,rkhd->rhqd",
            weights.astype(jnp.bfloat16),
            value_piece.reshape(rows_here, piece_len, HEADS, head_dim),
            preferred_element_type=jnp.float32,
        )
        return (new_top, new_total, product)

    init_state = (
        jnp.full((rows_here, HEADS, shard_len), negative_big, jnp.float32),
        jnp.zeros((rows_here, HEADS, shard_len), jnp.float32),
        jnp.zeros((rows_here, HEADS, shard_len, head_dim), jnp.float32),
    )
    if is_cross:
        final_top, final_total, final_sum = absorb(
            init_state,
            (
                lax.all_gather(keys_local, "seq", axis=1, tiled=True),
                lax.all_gather(values_local, "seq", axis=1, tiled=True),
                lax.all_gather(for_sending(key_docs), "seq", axis=1, tiled=True),
            ),
        )
    else:
        final_top, final_total, final_sum = absorb(
            init_state,
            (
                lax.all_gather(keys_local, "seq", axis=1, tiled=True),
                lax.all_gather(values_local, "seq", axis=1, tiled=True),
                lax.all_gather(key_docs, "seq", axis=1, tiled=True),
            ),
        )
    attended = (
        (final_sum / final_total[..., None])
        .transpose(0, 2, 1, 3)
        .reshape(rows_here, shard_len, model_width)
    )
    return (attended, final_top + jnp.log(final_total))


def attend_back(
    queries,
    keys_local,
    values_local,
    query_docs,
    key_docs,
    causal,
    log_total,
    grad_attended,
    is_cross,
):
    rows_here, shard_len, model_width = queries.shape
    head_dim = model_width // HEADS
    score_scale = head_dim ** (-0.5)
    query_place = lax.axis_index("seq") * shard_len + jnp.arange(shard_len)
    if is_cross:
        keys_full, values_full, docs_full = (
            lax.all_gather(keys_local, "seq", axis=1, tiled=True),
            lax.all_gather(values_local, "seq", axis=1, tiled=True),
            lax.all_gather(for_sending(key_docs), "seq", axis=1, tiled=True).astype(key_docs.dtype),
        )
    else:
        keys_full, values_full, docs_full = (
            lax.all_gather(keys_local, "seq", axis=1, tiled=True),
            lax.all_gather(values_local, "seq", axis=1, tiled=True),
            lax.all_gather(key_docs, "seq", axis=1, tiled=True),
        )
    full_len = keys_full.shape[1]
    query_heads = queries.reshape(rows_here, shard_len, HEADS, head_dim)
    key_heads = keys_full.reshape(rows_here, full_len, HEADS, head_dim)
    value_heads = values_full.reshape(rows_here, full_len, HEADS, head_dim)
    grad_heads = grad_attended.reshape(rows_here, shard_len, HEADS, head_dim)
    raw_scores = jnp.einsum(
        "rqhd,rkhd->rhqk", query_heads, key_heads, preferred_element_type=jnp.float32
    )
    allowed = allowed_mask(query_docs, docs_full, query_place, jnp.arange(full_len), causal)
    shifted = jnp.where(allowed, raw_scores * score_scale - log_total[..., None], negative_big)
    probs = jnp.where(allowed, jnp.exp(shifted), 0.0)
    grad_probs = jnp.einsum(
        "rqhd,rkhd->rhqk", grad_heads, value_heads, preferred_element_type=jnp.float32
    )
    delta = jnp.sum(probs * grad_probs, axis=-1)
    grad_scores = (probs * (grad_probs - delta[..., None]) * score_scale).astype(jnp.bfloat16)
    grad_queries = jnp.einsum(
        "rhqk,rkhd->rqhd", grad_scores, key_heads, preferred_element_type=jnp.float32
    ).reshape(rows_here, shard_len, model_width)
    probs_low = probs.astype(jnp.bfloat16)

    def key_terms(span):
        grad_keys = jnp.einsum(
            "rhqk,rqhd->krhd", grad_scores, query_heads, preferred_element_type=jnp.float32
        )
        grad_values = jnp.einsum(
            "rhqk,rqhd->krhd", probs_low, grad_heads, preferred_element_type=jnp.float32
        )
        return jnp.concatenate(
            [
                grad_keys.reshape(span, rows_here, model_width),
                grad_values.reshape(span, rows_here, model_width),
            ],
            axis=-1,
        )

    if is_cross:
        pair_terms = lax.psum_scatter(
            key_terms(shard_len * lax.axis_size("seq")).astype(jnp.bfloat16),
            "seq",
            scatter_dimension=0,
            tiled=True,
        ).astype(jnp.float32)
    else:
        pair_terms = lax.psum_scatter(
            key_terms(shard_len * lax.axis_size("seq")).astype(jnp.bfloat16),
            "seq",
            scatter_dimension=0,
            tiled=True,
        ).astype(jnp.float32)
    return (grad_queries, pair_terms.transpose(1, 0, 2))


def layer_forward(hidden_in, doc_own, memory, memory_docs, weights, is_decoder):
    (
        qkv_weight,
        out_weight,
        in_weight,
        down_weight,
        gains_pair,
        query_weight,
        pair_weight,
        cross_weight,
        cross_gains,
    ) = weights
    model_width = hidden_in.shape[-1]
    mixed = matmul(hidden_in, qkv_weight).astype(jnp.bfloat16)
    attended, self_lse = attend(
        mixed[..., :model_width],
        mixed[..., model_width : 2 * model_width],
        mixed[..., 2 * model_width :],
        doc_own,
        doc_own,
        is_decoder,
        False,
    )
    attended = attended.astype(jnp.bfloat16)
    first, first_unit, first_inv = normalize(
        hidden_in.astype(jnp.float32) + matmul(attended, out_weight), gains_pair[0]
    )
    first_low = first.astype(jnp.bfloat16)
    cross_queries = matmul(first_low, query_weight).astype(jnp.bfloat16)
    pair = matmul(memory, pair_weight).astype(jnp.bfloat16)
    cross_att, cross_lse = attend(
        cross_queries,
        pair[..., :model_width],
        pair[..., model_width:],
        doc_own,
        memory_docs,
        False,
        True,
    )
    cross_att = cross_att.astype(jnp.bfloat16)
    second_cross, second_unit, second_inv = normalize(
        first + matmul(cross_att, cross_weight), cross_gains
    )
    second = jnp.where(is_decoder, second_cross, first)
    second_low = second.astype(jnp.bfloat16)
    upward = matmul(second_low, in_weight)
    active = jax.nn.silu(upward).astype(jnp.bfloat16)
    result, third_unit, third_inv = normalize(second + matmul(active, down_weight), gains_pair[1])
    saved = {
        "mixed": mixed,
        "attended": attended,
        "self_lse": self_lse,
        "first_unit": first_unit,
        "first_inv": first_inv,
        "first_low": first_low,
        "cross_queries": cross_queries,
        "pair": pair,
        "cross_att": cross_att,
        "cross_lse": cross_lse,
        "second_unit": second_unit,
        "second_inv": second_inv,
        "second_low": second_low,
        "upward": upward,
        "active": active,
        "third_unit": third_unit,
        "third_inv": third_inv,
    }
    return (result, saved)


def layer_backward(
    grad_result, saved, hidden_in, doc_own, memory, memory_docs, weights, is_decoder
):
    (
        qkv_weight,
        out_weight,
        in_weight,
        down_weight,
        gains_pair,
        query_weight,
        pair_weight,
        cross_weight,
        cross_gains,
    ) = weights
    model_width = hidden_in.shape[-1]
    grad_third, grad_gain_late = normalize_back(
        grad_result, saved["third_unit"], gains_pair[1], saved["third_inv"]
    )
    down_grad = grad_third.astype(jnp.bfloat16)
    grad_down_w = contract(saved["active"], down_grad)
    grad_active = matmul_back(down_grad, down_weight).astype(jnp.bfloat16)
    sigmoid_up = jax.nn.sigmoid(saved["upward"])
    grad_upward = (
        grad_active.astype(jnp.float32)
        * (sigmoid_up + saved["upward"] * sigmoid_up * (1.0 - sigmoid_up))
    ).astype(jnp.bfloat16)
    grad_in_w = contract(saved["second_low"], grad_upward)
    grad_second = grad_third + matmul_back(grad_upward, in_weight)
    grad_cross_sum, grad_cross_gain = normalize_back(
        grad_second, saved["second_unit"], cross_gains, saved["second_inv"]
    )
    decoder_flag = is_decoder.astype(jnp.float32)
    grad_cross_sum = grad_cross_sum * decoder_flag
    grad_cross_gain = grad_cross_gain * decoder_flag
    cross_branch = grad_cross_sum.astype(jnp.bfloat16)
    grad_cross_w = contract(saved["cross_att"], cross_branch)
    grad_cross_att = matmul_back(cross_branch, cross_weight).astype(jnp.bfloat16)
    pair = saved["pair"]
    grad_cross_q, grad_pair = attend_back(
        saved["cross_queries"],
        pair[..., :model_width],
        pair[..., model_width:],
        doc_own,
        memory_docs,
        False,
        saved["cross_lse"],
        grad_cross_att,
        True,
    )
    grad_cross_q = grad_cross_q.astype(jnp.bfloat16)
    grad_pair = grad_pair.astype(jnp.bfloat16)
    grad_query_w = contract(saved["first_low"], grad_cross_q)
    grad_pair_w = contract(memory, grad_pair)
    grad_memory = matmul_back(grad_pair, pair_weight)
    grad_first = jnp.where(
        is_decoder, grad_cross_sum + matmul_back(grad_cross_q, query_weight), grad_second
    )
    grad_first_sum, grad_gain_early = normalize_back(
        grad_first, saved["first_unit"], gains_pair[0], saved["first_inv"]
    )
    self_branch = grad_first_sum.astype(jnp.bfloat16)
    grad_out_w = contract(saved["attended"], self_branch)
    grad_attended = matmul_back(self_branch, out_weight).astype(jnp.bfloat16)
    mixed = saved["mixed"]
    grad_queries, grad_pair_self = attend_back(
        mixed[..., :model_width],
        mixed[..., model_width : 2 * model_width],
        mixed[..., 2 * model_width :],
        doc_own,
        doc_own,
        is_decoder,
        saved["self_lse"],
        grad_attended,
        False,
    )
    grad_mixed = jnp.concatenate([grad_queries, grad_pair_self], axis=-1).astype(jnp.bfloat16)
    grad_qkv_w = contract(hidden_in, grad_mixed)
    grad_hidden = grad_first_sum + matmul_back(grad_mixed, qkv_weight)
    layer_grads = (
        grad_qkv_w,
        grad_out_w,
        grad_in_w,
        grad_down_w,
        jnp.stack([grad_gain_early, grad_gain_late]),
        grad_query_w,
        grad_pair_w,
        grad_cross_w,
        grad_cross_gain,
    )
    return (grad_hidden, grad_memory, layer_grads)


def any_rows(
    layer_input,
    segment_ids,
    attn_qkv,
    attn_out,
    ffn_in,
    ffn_out,
    norm_gain,
    cross_query,
    cross_pair,
    cross_out,
    cross_gain,
    out_cotangent,
):
    micro_count = layer_input.shape[1]
    section_index = lax.axis_index("section")
    is_decoder = section_index == 1
    weights = (
        attn_qkv[0],
        attn_out[0],
        ffn_in[0],
        ffn_out[0],
        norm_gain[0],
        cross_query,
        cross_pair,
        cross_out,
        cross_gain,
    )
    inputs_all = layer_input[0]
    docs_all = segment_ids[0]
    slot_ids = jnp.arange(micro_count)
    received = (jnp.zeros_like(inputs_all[0]), jnp.zeros_like(docs_all[0]))
    results = jnp.zeros_like(inputs_all)
    memories = []
    memory_doc_list = []
    for step_index in range(micro_count + 1):
        batch_index = step_index - section_index
        is_valid = (batch_index >= 0) & (batch_index < micro_count)
        chosen = jnp.clip(batch_index, 0, micro_count - 1)
        hidden_in = lax.dynamic_index_in_dim(inputs_all, chosen, 0, keepdims=False)
        doc_own = lax.dynamic_index_in_dim(docs_all, chosen, 0, keepdims=False)
        memory = received[0]
        memory_docs = jnp.where(is_valid & is_decoder, received[1], doc_own)
        memories.append(memory)
        memory_doc_list.append(memory_docs)
        result, saved = layer_forward(hidden_in, doc_own, memory, memory_docs, weights, is_decoder)
        low_result = result.astype(jnp.bfloat16)
        writing = (slot_ids == chosen) & is_valid
        results = jnp.where(writing[:, None, None, None], low_result[None], results)
        if step_index < micro_count:
            received = from_behind((low_result, doc_own), "section", 1)
    memory_stack = jnp.stack(memories)
    memory_doc_stack = jnp.stack(memory_doc_list)
    totals = tuple((jnp.zeros(weight.shape, jnp.float32) for weight in weights))
    input_grads = jnp.zeros(inputs_all.shape, jnp.float32)
    returned = jnp.zeros(inputs_all.shape[1:], jnp.float32)
    for step_index in range(micro_count + 1):
        batch_index = micro_count - step_index - section_index
        is_valid = (batch_index >= 0) & (batch_index < micro_count)
        chosen = jnp.clip(batch_index, 0, micro_count - 1)
        forward_step = jnp.clip(batch_index + section_index, 0, micro_count)
        hidden_in = lax.dynamic_index_in_dim(inputs_all, chosen, 0, keepdims=False)
        doc_own = lax.dynamic_index_in_dim(docs_all, chosen, 0, keepdims=False)
        memory = lax.dynamic_index_in_dim(memory_stack, forward_step, 0, keepdims=False)
        memory_docs = lax.dynamic_index_in_dim(memory_doc_stack, forward_step, 0, keepdims=False)
        discarded, saved = layer_forward(
            hidden_in, doc_own, memory, memory_docs, weights, is_decoder
        )
        cotangent = jnp.where(
            is_decoder,
            lax.dynamic_index_in_dim(out_cotangent, chosen, 0, keepdims=False).astype(jnp.float32),
            returned,
        )
        grad_hidden, grad_memory, layer_grads = layer_backward(
            cotangent, saved, hidden_in, doc_own, memory, memory_docs, weights, is_decoder
        )
        valid_flag = is_valid.astype(jnp.float32)
        totals = tuple(
            (running + valid_flag * fresh for running, fresh in zip(totals, layer_grads))
        )
        writing = (slot_ids == chosen) & is_valid
        input_grads = jnp.where(writing[:, None, None, None], grad_hidden[None], input_grads)
        if step_index < micro_count:
            returned = from_behind(grad_memory.astype(jnp.bfloat16), "section", -1).astype(
                grad_memory.dtype
            )
    group_sums = lax.psum(
        (
            totals[0],
            totals[1],
            totals[2],
            totals[3],
            totals[4],
            totals[5],
            totals[6],
            totals[7],
            totals[8],
        ),
        ("seq", "dp"),
    )
    section_sums = group_sums[:5]
    cross_sums = (
        from_root(group_sums[5].astype(jnp.bfloat16), "section", 1).astype(jnp.float32),
        from_root(group_sums[6].astype(jnp.bfloat16), "section", 1).astype(jnp.float32),
        from_root(group_sums[7].astype(jnp.bfloat16), "section", 1).astype(jnp.float32),
        from_root(group_sums[8].astype(jnp.bfloat16), "section", 1).astype(jnp.float32),
    )
    return (
        results[None],
        input_grads[None],
        section_sums[0][None],
        section_sums[1][None],
        section_sums[2][None],
        section_sums[3][None],
        section_sums[4][None],
        cross_sums[0],
        cross_sums[1],
        cross_sums[2],
        cross_sums[3],
    )


def split_rows(
    layer_input,
    segment_ids,
    attn_qkv,
    attn_out,
    ffn_in,
    ffn_out,
    norm_gain,
    cross_query,
    cross_pair,
    cross_out,
    cross_gain,
    out_cotangent,
):
    micros = layer_input.shape[1]
    length, width = layer_input.shape[3:]
    hidden = ffn_in.shape[-1]
    q_tiles = length // TILE
    group = lax.axis_size("dp") // 2
    axes = ("section", "seq", "dp")
    decoder = lax.axis_index("section") == 1
    flag = decoder.astype(jnp.int32)
    x = lax.axis_index("seq")
    core = lax.rem(lax.axis_index("dp"), 2)
    z = lax.axis_index("dp") // 2
    places = [(t, i, k, c) for t in range(2) for i in range(2) for k in range(group) for c in range(2)]

    def number(t, i, k, c):
        return ((t * 2 + i) * group + k) * 2 + c

    def send(values, target, section=None):
        route = [
            (number(*place), number(*target(*place)))
            for place in places
            if section in (None, place[0]) and target(*place)
        ]
        return lax.ppermute(values, axes, route)

    def to_core(t, i, k, c):
        return (t, i, k, 1 - c)

    def to_x(t, i, k, c):
        return (t, 1 - i, k, c)

    def to_row(t, i, k, c):
        return (t, c, k, i)

    def to_decoder(t, i, k, c):
        return (1, i, k, c) if t == 0 else None

    def to_encoder(t, i, k, c):
        return (0, i, k, c) if t == 1 else None

    def fence(values, *before):
        return lax.optimization_barrier((values,) + before)[0]

    def exchange(values):
        return send(values, to_core)

    low = ((length, width), bf16)
    wide = ((length, width), f32)
    marked = ((length + 16, width), bf16)
    both = ((2 * length, width), bf16)
    keys_all = ((2 * length, 2 * width), bf16)
    mixing = ((width, 3 * width), bf16)
    inner = ((length, hidden), bf16)
    lse = ((q_tiles, 8, 2 * TILE), f32)
    stat = ((length, LANES), f32)
    square = ((width, width), bf16)
    rising = ((width, hidden), bf16)
    falling = ((hidden, width), bf16)
    gain_rows = ((8, width), f32)

    meta = jnp.stack([flag, core, x, z]).astype(jnp.int32)
    numbers = segment_ids[0, :, 0].astype(bf16)
    padding = jnp.zeros((15, width), bf16)
    with_numbers = [
        jnp.concatenate([layer_input[0, micro, 0], numbers[micro][None], padding])
        for micro in range(micros)
    ]
    own = [send(with_numbers[0], to_row)]
    for micro in range(1, micros):
        own.append(send(fence(with_numbers[micro], own[-1]), to_row))
    other = [exchange(own[0])]

    plain = dict(meta=meta)
    small = dict(gains=norm_gain[0])
    forward, memories, memories_other = [], [], []
    for micro in range(micros):
        call = launch(
            self_forward,
            micro,
            None,
            plain,
            small,
            dict(
                x_own_h=own[micro],
                x_other_h=other[micro],
                w_mixed_h=attn_qkv[0],
                w_out_h=attn_out[0],
                w_in_h=ffn_in[0],
                w_down_h=ffn_out[0],
            ),
            dict(
                q_o=low,
                kv_o=keys_all,
                att_o=low,
                lse_o=lse,
                unit1_o=wide,
                inv1_o=stat,
                first_low_o=low,
                memory_o=marked,
                ffn_low_o=low,
                act_o=inner,
                slope_o=inner,
                unit2_o=wide,
                inv2_o=stat,
            ),
            dict(
                **attention_scratch(length, width),
                **forward_scratch(length, width),
                x=both,
                w_mixed=mixing,
                w_out=square,
                w_in=rising,
                w_down=falling,
                unit1=wide,
                inv1=stat,
                first_low=low,
                memory=marked,
                act=inner,
                slope=inner,
                unit2=wide,
                inv2=stat,
                sum=wide,
            ),
            28,
            26,
            after=(forward[0].lse_o,) if micro else (),
        )
        forward.append(call)
        memories.append(send(call.memory_o, to_decoder))
        if micro + 1 < micros:
            other.append(exchange(fence(own[micro + 1], call.lse_o)))

    for micro in range(micros):
        memories_other.append(exchange(fence(memories[micro], forward[-1].lse_o)))
    cotangent = send(fence(out_cotangent[:, 0], forward[0].lse_o), to_row)

    cross, grads_memory, made = [], [], []
    after = (forward[-1].lse_o,)
    for micro in range(micros):
        done = forward[micro]
        call = launch(
            cross_both_ways,
            micro,
            1,
            plain,
            dict(**small, cross_gain=cross_gain[None]),
            dict(
                x_own_h=own[micro],
                memory_own_h=memories[micro],
                memory_other_h=memories_other[micro],
                w_pair_h=cross_pair,
                first_low_h=done.first_low_o,
                unit1_h=done.unit1_o,
                w_query_h=cross_query,
                w_cross_h=cross_out,
                w_in_h=ffn_in[0],
                w_down_h=ffn_out[0],
                cot_h=cotangent,
            ),
            dict(
                att_o=low,
                ffn_low_o=low,
                act_o=inner,
                decoded_o=low,
                down_grad_o=low,
                up_grad_o=inner,
                gain_grads_o=gain_rows,
                branch_o=low,
                dq_low_o=low,
                dkv_o=keys_all,
                part_own_o=wide,
                part_other_o=low,
                grad_first_o=wide,
            ),
            dict(
                **attention_scratch(length, width),
                **forward_scratch(length, width),
                **backward_scratch(length, width),
                x=both,
                w_pair=((width, 2 * width), bf16),
                first_low=low,
                unit1=wide,
                w_query=square,
                w_cross=square,
                w_in=rising,
                w_down=falling,
                cot=low,
                unit2=wide,
                inv2=stat,
                second_low=low,
                act=inner,
                slope=inner,
                sum=wide,
                decoded=low,
                keep=wide,
                down_grad=low,
                up_grad=inner,
                gain_grads=gain_rows,
                branch=low,
                part_own=wide,
            ),
            36,
            44,
            dict(act_o=done.act_o, ffn_low_o=done.ffn_low_o),
            after,
        )
        cross.append(call)
        away = call.part_other_o
        if micro:
            away = fence(away, grads_memory[-1])
        total = call.part_own_o + exchange(away).astype(f32)
        made.append(total.astype(bf16))
        after = (made[micro],)
        grads_memory.append(send(made[micro], to_encoder))

    def backward_feed(micro, after):
        done, late = forward[micro], cross[micro]
        return launch(
            feed_backward_alone,
            micro,
            0,
            plain,
            dict(gains=norm_gain[0]),
            dict(
                grad_memory_h=grads_memory[micro],
                unit2_h=done.unit2_o,
                inv2_h=done.inv2_o,
                slope_h=done.slope_o,
                w_in_h=ffn_in[0],
                w_down_h=ffn_out[0],
            ),
            dict(gain_late_o=gain_rows, down_grad_o=low, up_grad_o=inner, grad_first_o=wide),
            dict(
                cot=low,
                unit2=wide,
                inv2=stat,
                slope=inner,
                w_in=rising,
                w_down=falling,
                gain_grads=gain_rows,
                keep=wide,
                down_grad=low,
                up_grad=inner,
                sum=wide,
            ),
            12,
            10,
            dict(
                down_grad_o=late.down_grad_o, up_grad_o=late.up_grad_o, grad_first_o=late.grad_first_o
            ),
            after,
        )

    def backward_self(micro, side, grad_first, previous=None, after=(), halfway=None):
        done = forward[micro]
        heads = width // LANES
        given = dict(
            x_own_h=own[micro],
            x_other_h=other[micro],
            q_h=done.q_o,
            kv_h=done.kv_o,
            att_h=done.att_o,
            lse_h=done.lse_o,
        )
        ahead = dict(
            grad_first_h=grad_first,
            unit1_h=done.unit1_o,
            inv1_h=done.inv1_o,
            w_out_h=attn_out[0],
        )
        makes = dict(dq_low_o=low, dkv_o=keys_all)
        makes_first = dict(gain_early_o=gain_rows, branch_o=low)
        makes_last = dict(part_own_o=wide, part_other_o=low)
        scratch = dict(
            **attention_scratch(length, width),
            **backward_scratch(length, width),
            w_out=square,
            w_mixed=mixing,
            unit1=wide,
            inv1=stat,
            keep=wide,
            branch=low,
            grad_att=low,
            gain_grads=gain_rows,
        )

        def part(first, last, large, outs, work, previous, after):
            return launch(
                self_backward,
                (micro, first, last),
                side,
                plain,
                small,
                dict(**given, **large),
                dict(**makes, **outs),
                scratch,
                28,
                work,
                previous,
                after,
            )

        if halfway is None:
            large = dict(**ahead, w_mixed_h=attn_qkv[0])
            outs = dict(**makes_first, **makes_last)
            return part(0, heads, large, outs, 22, previous, after)
        outs = dict(**makes_first, grad_sum_o=wide, grad_att_o=low)
        one = part(0, heads // 2, ahead, outs, 12, None, after)
        large = dict(
            w_mixed_h=attn_qkv[0],
            grad_sum_h=one.grad_sum_o,
            grad_att_h=one.grad_att_o,
            dq_h=one.dq_low_o,
            dkv_h=one.dkv_o,
        )
        two = part(heads // 2, heads, large, makes_last, 12, None, halfway(one))
        return types.SimpleNamespace(**{**vars(one), **vars(two)})

    def weight_grads(plan, side, arrays, scratch, after=()):
        blocks = ((2, width, width), bf16)
        call = launch(
            contract_blocks,
            plan,
            side,
            plain,
            dict(),
            arrays,
            dict(sent_o=blocks, kept_o=blocks),
            dict(**scratch, blocks=((4, width, width), bf16)),
            36,
            8,
            after=after,
        )
        return call.sent_o, call.kept_o

    def first_sums(halves, section=None):
        sent, kept = halves
        got = send(sent, to_core, section)

        def block(side):
            return sum(
                lax.dynamic_index_in_dim(part, side, 0, keepdims=False).astype(f32)
                for part in (kept, got)
            )

        return block(1 - x).astype(bf16), block(x)

    def middle_sums(sums, section=None):
        away, total = sums
        return (total + send(away, to_x, section).astype(f32)).astype(bf16)

    groups = [[2 * k + c for k in range(group)] for c in range(2)]

    def swap_z(blocks):
        return lax.all_to_all(blocks, axes[2], 0, 0, axis_index_groups=groups, tiled=True)

    def last_sums(total, *later):
        parts = swap_z(total.reshape(group, width // group, width))
        if later:
            parts = fence(parts, *later)
        return jnp.sum(parts.astype(f32), axis=0).astype(bf16)

    def gather_z(share):
        return swap_z(jnp.broadcast_to(share, (group,) + share.shape))

    def gain_block(rows):
        filled = jnp.concatenate([jnp.stack(rows), jnp.zeros((16 - len(rows), width), f32)])
        return filled.astype(bf16)

    def spread(targets, own, own_x, outs, parts):
        return launch(
            spread_pieces,
            targets,
            None,
            plain,
            dict(),
            dict(own_h=own, own_x_h=own_x, other_h=exchange(own), other_x_h=exchange(own_x)),
            outs,
            dict(
                pieces=((4,) + own.shape, bf16),
                wide=((4 * group * parts, width // group, width), f32),
            ),
            8 + 4 * group * parts,
            5,
        )

    tokens, all_tokens = micros * length, 2 * micros * length
    turn, turn_all = ((width, tokens), bf16), ((width, all_tokens), bf16)
    narrow, narrow_all = ((tokens, width), bf16), ((all_tokens, width), bf16)
    pair_all = ((all_tokens, 2 * width), bf16)
    deep = ((tokens, hidden), bf16)

    def part_of(buffer, *sources):
        return lambda column: (buffer, sources, column)

    def key_rows(buffer, sources):
        first, second = pl.ds(0, length), pl.ds(length, length)
        return part_of(buffer, *[source.at[rows] for rows in (first, second) for source in sources])

    def cross_plan(r):
        rows = pl.ds(0, length)
        low_part = part_of(r.low, r.low0_h, r.low1_h)
        att_part = part_of(r.att, r.att0_h, r.att1_h)
        dq_part = part_of(r.dq, r.dq0_h, r.dq1_h)
        branch_part = part_of(r.branch, r.branch0_h, r.branch1_h)
        sources = (r.mem0_h, r.mem1_h, r.mem2_h, r.mem3_h)
        mem_part = part_of(r.mem, *[source.at[rows] for source in sources])
        pair_part = key_rows(r.pair, (r.pair0_h, r.pair1_h))
        return [
            (r.turn, low_part(0), dq_part(0)),
            (r.turn_att, att_part(0), branch_part(0)),
            (r.turn_all, mem_part(0), pair_part(0)),
            (r.turn_all, mem_part(0), pair_part(1)),
        ]

    def rising_plan(r):
        low_part = part_of(r.low, r.low0_h, r.low1_h)
        up_part = part_of(r.up, r.up0_h, r.up1_h)
        return [(r.turn, low_part(0), up_part(block)) for block in range(4)]

    def falling_plan(r):
        act_part = part_of(r.act, r.act0_h, r.act1_h)
        down_part = part_of(r.down, r.down0_h, r.down1_h)
        return [(r.turn, act_part(block), down_part(0)) for block in range(4)]

    def self_plan(r):
        rows = pl.ds(0, length)
        sources = (r.x0_h, r.x1_h, r.x2_h, r.x3_h)
        x_part = part_of(r.x, *[source.at[rows] for source in sources])
        dq_part = part_of(r.dq, r.dq0_h, r.dq1_h)
        pair_part = key_rows(r.pair, (r.pair0_h, r.pair1_h))
        att_part = part_of(r.att, r.att0_h, r.att1_h)
        branch_part = part_of(r.branch, r.branch0_h, r.branch1_h)
        return [
            (r.turn_all, x_part(0), dq_part(0)),
            (r.turn_all, x_part(0), pair_part(0)),
            (r.turn_all, x_part(0), pair_part(1)),
            (r.turn, att_part(0), branch_part(0)),
        ]

    last = micros - 1
    feeds, ends = [None] * micros, [None] * micros
    cross_halves = weight_grads(
        cross_plan,
        1,
        dict(
            low0_h=forward[0].first_low_o,
            low1_h=forward[1].first_low_o,
            dq0_h=cross[0].dq_low_o,
            dq1_h=cross[1].dq_low_o,
            att0_h=cross[0].att_o,
            att1_h=cross[1].att_o,
            branch0_h=cross[0].branch_o,
            branch1_h=cross[1].branch_o,
            mem0_h=memories[0],
            mem1_h=memories[1],
            mem2_h=memories_other[0],
            mem3_h=memories_other[1],
            pair0_h=cross[0].dkv_o,
            pair1_h=cross[1].dkv_o,
        ),
        dict(
            low=narrow,
            dq=narrow,
            att=narrow,
            branch=narrow,
            mem=narrow_all,
            pair=pair_all,
            turn=turn,
            turn_att=turn,
            turn_all=turn_all,
        ),
        (made[last],),
    )
    cross_sums = first_sums(cross_halves, 1)
    results = jnp.stack(
        [
            jnp.where(decoder, call.decoded_o, done.memory_o[:length])
            for call, done in zip(cross, forward)
        ]
    )
    results = send(results, to_row)
    latest = made[last]

    def part_sum(micro, *before):
        end = ends[micro]
        away = fence(end.part_other_o, *before)
        total = (end.part_own_o + exchange(away).astype(f32)).astype(bf16)
        return total, send(total, to_row)

    steps = []
    for micro in range(last):
        feeds[micro] = backward_feed(micro, (latest,))
        first = feeds[micro].grad_first_o
        ends[micro] = backward_self(micro, 0, first)
        ends[micro] = backward_self(micro, 1, first, vars(ends[micro]), (cross_sums[0], grads_memory[last]))
        cross_total = middle_sums(cross_sums, 1)
        steps.append(part_sum(micro, cross_total))
        latest = ends[micro].gain_early_o
    feeds[last] = backward_feed(last, (latest,))

    rising_halves = weight_grads(
        rising_plan,
        None,
        dict(
            low0_h=cross[0].ffn_low_o,
            low1_h=cross[1].ffn_low_o,
            up0_h=feeds[0].up_grad_o,
            up1_h=feeds[1].up_grad_o,
        ),
        dict(low=narrow, up=deep, turn=turn),
        (results,) + tuple(step[0] for step in steps),
    )
    cross_share = last_sums(cross_total, rising_halves[0])
    third = sum(call.gain_grads_o[1] for call in cross)
    cross_share = jnp.concatenate([cross_share, gain_block([third])])
    rising_sums = first_sums((fence(rising_halves[0], cross_share), rising_halves[1]))
    rising_total = middle_sums(rising_sums)
    falling_halves = weight_grads(
        falling_plan,
        None,
        dict(
            act0_h=cross[0].act_o,
            act1_h=cross[1].act_o,
            down0_h=feeds[0].down_grad_o,
            down1_h=feeds[1].down_grad_o,
        ),
        dict(act=deep, down=narrow, turn=turn),
        (rising_sums[0],) + tuple(step[1] for step in steps),
    )
    cross_sent = send(cross_share, to_encoder)
    falling_sent = fence(falling_halves[0], rising_total)
    falling_sums = first_sums((falling_sent, falling_halves[1]))
    falling_total = middle_sums(falling_sums)
    shares = []

    def halfway(one):
        shares.append(last_sums(rising_total, one.gain_early_o))
        shares.append(jnp.where(decoder, cross_share, fence(cross_sent, one.gain_early_o)))
        return (*shares, falling_total)

    ends[last] = backward_self(
        last,
        None,
        feeds[last].grad_first_o,
        None,
        (falling_sums[0],),
        halfway,
    )
    falling_share = last_sums(falling_total, ends[last].gain_early_o, ends[last].part_own_o)
    falling_own = gather_z(falling_share)
    steps.append(part_sum(last, falling_share))

    self_halves = weight_grads(
        self_plan,
        None,
        dict(
            x0_h=own[0],
            x1_h=own[1],
            x2_h=other[0],
            x3_h=other[1],
            dq0_h=ends[0].dq_low_o,
            dq1_h=ends[1].dq_low_o,
            pair0_h=ends[0].dkv_o,
            pair1_h=ends[1].dkv_o,
            att0_h=forward[0].att_o,
            att1_h=forward[1].att_o,
            branch0_h=ends[0].branch_o,
            branch1_h=ends[1].branch_o,
        ),
        dict(
            x=narrow_all,
            dq=narrow,
            pair=pair_all,
            att=narrow,
            branch=narrow,
            turn=turn,
            turn_all=turn_all,
        ),
        (steps[last][0],),
    )
    away, total = first_sums(
        (fence(self_halves[0], steps[last][1], falling_own), self_halves[1])
    )
    self_total = middle_sums((away, total))
    one_own = gather_z(fence(jnp.concatenate(shares), self_halves[0]))
    one_own = jnp.concatenate([falling_own, one_own], axis=1)
    self_share = last_sums(self_total)
    one_own_x = send(fence(one_own, self_total), to_x)

    early = sum(end.gain_early_o[0] for end in ends)
    late = jnp.where(
        decoder,
        sum(call.gain_grads_o[0] for call in cross),
        sum(call.gain_late_o[0] for call in feeds),
    )
    two_own = gather_z(jnp.concatenate([self_share, gain_block([early, late])]))
    two_own_x = send(fence(two_own, one_own_x), to_x)

    def columns(block):
        return pl.ds(block * width, width)

    def one_targets(r, block, row, rows):
        lines = pl.ds(row, rows)
        feed = [r.down_o.at[pl.ds(block * width + row, rows)], r.up_o.at[lines, columns(block)]]
        if block >= 2:
            return feed + [r.pair_o.at[lines, columns(block - 2)]]
        return feed + [(r.out_o if block else r.query_o).at[lines]]

    def two_targets(r, block, row, rows):
        lines = pl.ds(row, rows)
        return [r.out_o.at[lines] if block == 3 else r.mixed_o.at[lines, columns(block)]]

    square_out = ((width, width), f32)
    one_own_x = fence(one_own_x, two_own)
    one_grads = spread(
        one_targets,
        one_own,
        one_own_x,
        dict(
            up_o=((width, hidden), f32),
            query_o=square_out,
            pair_o=((width, 2 * width), f32),
            down_o=((hidden, width), f32),
            out_o=square_out,
            gains_o=((1, width), f32),
        ),
        3,
    )
    two_own_x = fence(two_own_x, one_grads.gains_o)
    two_grads = spread(
        two_targets,
        two_own,
        two_own_x,
        dict(
            mixed_o=((width, 3 * width), f32),
            out_o=square_out,
            gains_o=((2, width), f32),
        ),
        1,
    )

    grad_input = jnp.stack([step[1] for step in steps])
    return (
        results[None, :, None],
        grad_input.astype(f32)[None, :, None],
        two_grads.mixed_o[None],
        two_grads.out_o[None],
        one_grads.up_o[None],
        one_grads.down_o[None],
        two_grads.gains_o[None],
        one_grads.query_o,
        one_grads.pair_o,
        one_grads.out_o,
        one_grads.gains_o[0],
    )


def shards(*arrays):
    layer_input = arrays[0]
    micros, rows, length = layer_input.shape[1:4]
    simple = (
        lax.axis_size("section") == 2
        and lax.axis_size("seq") == 2
        and lax.axis_size("dp") in (4, 8, 16)
        and (micros, rows) == (2, 1)
        and length == layer_input.shape[-1] == CHUNK
        and arrays[4].shape[-1] == 4 * CHUNK
    )
    return split_rows(*arrays) if simple else any_rows(*arrays)


def solution(mesh):
    in_specs = (
        P("section", None, "dp", "seq", None),
        P("section", None, "dp", "seq"),
        P("section", None, None),
        P("section", None, None),
        P("section", None, None),
        P("section", None, None),
        P("section", None, None),
        P(),
        P(),
        P(),
        P(),
        P(None, "dp", "seq", None),
    )
    out_specs = (
        P("section", None, "dp", "seq", None),
        P("section", None, "dp", "seq", None),
        P("section", None, None),
        P("section", None, None),
        P("section", None, None),
        P("section", None, None),
        P("section", None, None),
        P(),
        P(),
        P(),
        P(),
    )
    return jax.shard_map(shards, mesh=mesh, in_specs=in_specs, out_specs=out_specs, check_vma=False)
```

```python
import types

import jax
import jax.numpy as jnp
from jax import lax
from jax.experimental import pallas as pl
from jax.experimental.pallas import tpu as pltpu
from jax.sharding import PartitionSpec as P

HEADS = 8
TILE = 256
LANES = 128
CHUNK = 512

f32 = jnp.float32
bf16 = jnp.bfloat16
negative_big = -1e30
epsilon = 1e-05


def dot(left, right):
    return lax.dot_general(left, right, (((1,), (0,)), ((), ())), preferred_element_type=f32)


def dot_nt(left, right):
    return lax.dot_general(left, right, (((1,), (1,)), ((), ())), preferred_element_type=f32)


def dot_tn(left, right):
    return lax.dot_general(left, right, (((0,), (0,)), ((), ())), preferred_element_type=f32)


def standardize(values):
    center = values - jnp.mean(values, axis=-1, keepdims=True)
    inverse = lax.rsqrt(jnp.mean(center * center, axis=-1, keepdims=True) + epsilon)
    return center * inverse, inverse


def standardize_back(grad_out, standard, gain_row, inverse):
    scaled = grad_out * gain_row
    grad_in = inverse * (
        scaled
        - jnp.mean(scaled, axis=-1, keepdims=True)
        - standard * jnp.mean(scaled * standard, axis=-1, keepdims=True)
    )
    return grad_in, jnp.sum(grad_out * standard, axis=0, keepdims=True)


class Copies:
    def __init__(self, sems):
        self.sems = sems
        self.used = 0

    def start(self, source, target):
        copy = pltpu.make_async_copy(source, target, self.sems.at[self.used])
        self.used += 1
        copy.start()
        return copy


def wait_all(copies):
    for copy in copies:
        copy.wait()


def spread_pairs(target, source, factor, pairs):
    tiles = target.shape[1]
    half = lax.broadcasted_iota(jnp.int32, (TILE, LANES), 1) < LANES // 2
    first = jnp.where(half, factor, 0.0).astype(bf16)
    second = jnp.where(half, 0.0, factor).astype(bf16)
    for tile in range(tiles):
        for pair in pairs:
            block = source[tile * TILE : (tile + 1) * TILE, pair * LANES : (pair + 1) * LANES]
            target[pair, tile, :TILE, :] = block * first
            target[pair, tile, TILE:, :] = block * second


def turn_tiles(target, source, column, pairs):
    low, high = pairs[0] * LANES, (pairs[-1] + 1) * LANES
    for tile in range(target.shape[0]):
        block = source[tile * TILE : (tile + 1) * TILE, column + low : column + high]
        target[tile, low:high, :] = jnp.transpose(block)


def place_documents(r, copies):
    wait_all(copies)
    q_tiles = r.qd.shape[0]
    for part in range(3):
        row = r.docs[part].astype(f32)[0:1, :]
        for tile in range(q_tiles):
            piece = row[:, tile * TILE : (tile + 1) * TILE]
            slot = part * q_tiles + tile
            r.bounds[0, slot] = jnp.min(piece).astype(jnp.int32)
            r.bounds[1, slot] = jnp.max(piece).astype(jnp.int32)
            if part == 0:
                r.qd[tile] = jnp.broadcast_to(piece, (8, TILE))
        if part > 0:
            for start in range(0, row.shape[1], LANES):
                block = jnp.broadcast_to(row[:, start : start + LANES], (LANES, LANES))
                place = (part - 1) * row.shape[1] + start
                r.kdc[place : place + LANES, :] = jnp.transpose(block)


def load_documents(r, move, queries, own, other):
    rows = pl.ds(r.docs.shape[2], r.docs.shape[1])
    return [
        move.start(source.at[rows], r.docs.at[part])
        for part, source in enumerate((queries, own, other))
    ]


def tile_place(r, core, causal, q_tile, k_tile):
    q_tiles = r.qd.shape[0]
    length = q_tiles * TILE
    owner = jnp.where(k_tile < q_tiles, core, 1 - core)
    k_start = owner * length + lax.rem(k_tile, q_tiles) * TILE
    ahead = core * length + q_tile * TILE - k_start
    ahead = jnp.where(causal == 1, ahead, 2 * length * TILE)
    q_low, q_high = r.bounds[0, q_tile], r.bounds[1, q_tile]
    k_low, k_high = r.bounds[0, q_tiles + k_tile], r.bounds[1, q_tiles + k_tile]
    active = (q_low <= k_high) & (k_low <= q_high) & (ahead > -TILE)
    whole = (q_low == k_high) & (k_low == q_high) & (ahead >= TILE)
    return active, whole, ahead


def each_tile(place, body):
    active, whole, ahead = place
    pl.when(active & jnp.logical_not(whole))(lambda: body(ahead))
    pl.when(whole)(lambda: body(None))


def fill_bias(r, q_tile, k_tile, ahead):
    keys = r.kdc[pl.ds(pl.multiple_of(k_tile * TILE, TILE), TILE), :]
    shift = lax.broadcasted_iota(jnp.int32, (TILE, LANES), 0) - lax.broadcasted_iota(
        jnp.int32, (TILE, LANES), 1
    )
    queries = r.qd[q_tile]
    for start in range(0, TILE, LANES):
        same = keys == queries[0:1, start : start + LANES]
        allowed = same & (shift - start <= ahead)
        r.bias[:, start : start + LANES] = jnp.where(allowed, 0.0, negative_big)


def attention_forward(r, core, causal):
    pairs, q_tiles = r.qm.shape[:2]
    k_tiles = r.vt.shape[0]

    def one_query_tile(q_tile, carry):
        r.top[...] = jnp.full(r.top.shape, negative_big, f32)
        r.total[...] = jnp.zeros(r.total.shape, f32)
        r.turned[...] = jnp.zeros(r.turned.shape, f32)

        def one_key_tile(k_tile, inner):
            def one_tile(ahead):
                if ahead is not None:
                    fill_bias(r, q_tile, k_tile, ahead)
                rows = pl.ds(pl.multiple_of(k_tile * TILE, TILE), TILE)

                def raw(pair):
                    keys = r.kv[rows, pair * LANES : (pair + 1) * LANES]
                    return dot_nt(keys, r.qm[pair, q_tile])

                raw_next = raw(0)
                for pair in range(pairs):
                    scores = raw_next
                    if ahead is not None:
                        bias = r.bias[...]
                        scores = scores + jnp.concatenate([bias, bias], axis=1)
                    if pair + 1 < pairs:
                        raw_next = raw(pair + 1)
                    old_top = r.top[pair : pair + 1, :]
                    new_top = jnp.maximum(old_top, jnp.max(scores, axis=0, keepdims=True))
                    weights = jnp.exp(scores - new_top)
                    shrink = jnp.exp(old_top - new_top)
                    r.top[pair : pair + 1, :] = new_top
                    r.total[pair : pair + 1, :] = r.total[
                        pair : pair + 1, :
                    ] * shrink + jnp.sum(weights, axis=0, keepdims=True)
                    low = weights.astype(bf16)
                    for side in range(2):
                        span = slice(side * TILE, (side + 1) * TILE)
                        head = slice((2 * pair + side) * 64, (2 * pair + side + 1) * 64)
                        r.turned[head, :] = r.turned[head, :] * shrink[:, span] + dot(
                            r.vt[k_tile, head, :], low[:, span]
                        )

            each_tile(tile_place(r, core, causal, q_tile, k_tile), one_tile)
            return inner

        lax.fori_loop(0, k_tiles, one_key_tile, 0)
        for pair in range(pairs):
            total = r.total[pair : pair + 1, :]
            r.lse[q_tile, pair : pair + 1, :] = r.top[pair : pair + 1, :] + jnp.log(total)
            share = 1.0 / total
            for side in range(2):
                span = slice(side * TILE, (side + 1) * TILE)
                head = slice((2 * pair + side) * 64, (2 * pair + side + 1) * 64)
                r.turned[head, :] = r.turned[head, :] * share[:, span]
        rows = pl.ds(pl.multiple_of(q_tile * TILE, TILE), TILE)
        r.att[rows, :] = jnp.transpose(r.turned[...]).astype(bf16)
        return carry

    lax.fori_loop(0, q_tiles, one_query_tile, 0)


def row_products(r, grad_att, pairs):
    low, high = pairs[0] * LANES, (pairs[-1] + 1) * LANES
    for tile in range(r.qm.shape[1]):
        rows = slice(tile * TILE, (tile + 1) * TILE)
        product = jnp.transpose(
            grad_att[rows, low:high].astype(f32) * r.att[rows, low:high].astype(f32)
        )
        for pair in pairs:
            for side in range(2):
                head = (2 * pair + side) * 64 - low
                r.delta[tile, pair : pair + 1, side * TILE : (side + 1) * TILE] = jnp.sum(
                    product[head : head + 64, :], axis=0, keepdims=True
                )


def attention_backward(r, core, causal, pairs):
    q_tiles, k_tiles = r.qm.shape[1], r.kt.shape[0]
    width = r.kt.shape[1]
    low, high = pairs[0] * LANES, (pairs[-1] + 1) * LANES
    for start in (0, width):
        r.dkv[:, start + low : start + high] = jnp.zeros((r.dkv.shape[0], high - low), f32)

    def one_query_tile(q_tile, carry):
        r.turned[low:high, :] = jnp.zeros((high - low, TILE), f32)

        def one_key_tile(k_tile, inner):
            def one_tile(ahead):
                if ahead is not None:
                    fill_bias(r, q_tile, k_tile, ahead)
                rows = pl.ds(pl.multiple_of(k_tile * TILE, TILE), TILE)

                def raw(pair):
                    lanes = slice(pair * LANES, (pair + 1) * LANES)
                    lanes_v = slice(width + pair * LANES, width + (pair + 1) * LANES)
                    return (
                        dot_nt(r.kv[rows, lanes], r.qm[pair, q_tile]),
                        dot_nt(r.kv[rows, lanes_v], r.gm[pair, q_tile]),
                    )

                raw_next = raw(pairs[0])
                for pair in pairs:
                    scores, grad_probs = raw_next
                    if ahead is not None:
                        bias = r.bias[...]
                        scores = scores + jnp.concatenate([bias, bias], axis=1)
                    if pair < pairs[-1]:
                        raw_next = raw(pair + 1)
                    probs = jnp.exp(scores - r.lse[q_tile, pair : pair + 1, :])
                    grad_scores = probs * (grad_probs - r.delta[q_tile, pair : pair + 1, :])
                    probs_low = probs.astype(bf16)
                    grad_low = grad_scores.astype(bf16)
                    lanes = slice(pair * LANES, (pair + 1) * LANES)
                    lanes_v = slice(width + pair * LANES, width + (pair + 1) * LANES)
                    r.dkv[rows, lanes] += dot(grad_low, r.qm[pair, q_tile])
                    r.dkv[rows, lanes_v] += dot(probs_low, r.gm[pair, q_tile])
                    for side in range(2):
                        span = slice(side * TILE, (side + 1) * TILE)
                        head = slice((2 * pair + side) * 64, (2 * pair + side + 1) * 64)
                        r.turned[head, :] += dot(r.kt[k_tile, head, :], grad_low[:, span])

            each_tile(tile_place(r, core, causal, q_tile, k_tile), one_tile)
            return inner

        lax.fori_loop(0, k_tiles, one_key_tile, 0)
        rows = pl.ds(pl.multiple_of(q_tile * TILE, TILE), TILE)
        r.dq[rows, low:high] = jnp.transpose(r.turned[low:high, :]) * (64**-0.5)
        return carry

    lax.fori_loop(0, q_tiles, one_query_tile, 0)


def feed_forward(r, low):
    chunks = [slice(at, at + CHUNK) for at in range(0, r.w_in.shape[1], CHUNK)]
    upward_next = dot(low[...], r.w_in[:, chunks[0]])
    for place, span in enumerate(chunks):
        upward = upward_next
        if place + 1 < len(chunks):
            upward_next = dot(low[...], r.w_in[:, chunks[place + 1]])
        gate = jax.nn.sigmoid(upward)
        active = (upward * gate).astype(bf16)
        r.act[:, span] = active
        r.slope[:, span] = (gate + upward * gate * (1.0 - gate)).astype(r.slope.dtype)
        part = dot(active, r.w_down[span, :])
        if place:
            r.sum[...] += part
        else:
            r.sum[...] = part


def feed_backward(r):
    chunks = [slice(at, at + CHUNK) for at in range(0, r.w_in.shape[1], CHUNK)]
    active_next = dot_nt(r.down_grad[...], r.w_down[chunks[0], :])
    for place, span in enumerate(chunks):
        grad_active = active_next.astype(bf16)
        if place + 1 < len(chunks):
            active_next = dot_nt(r.down_grad[...], r.w_down[chunks[place + 1], :])
        grad_up = (grad_active.astype(f32) * r.slope[:, span].astype(f32)).astype(bf16)
        r.up_grad[:, span] = grad_up
        part = dot_nt(grad_up, r.w_in[:, span])
        if place:
            r.sum[...] += part
        else:
            r.sum[...] = part


def self_forward(r):
    length, width = r.unit1.shape
    decoder, core = r.meta[0], r.meta[1]
    move = Copies(r.sems)
    whole = pl.ds(0, length)
    documents = load_documents(r, move, r.x_own_h, r.x_own_h, r.x_other_h)
    early = [
        move.start(r.x_own_h.at[whole], r.x.at[whole]),
        move.start(r.x_other_h.at[whole], r.x.at[pl.ds(length, length)]),
        move.start(r.w_mixed_h, r.w_mixed),
    ]
    later = [
        move.start(r.w_out_h, r.w_out),
        move.start(r.w_in_h, r.w_in),
        move.start(r.w_down_h, r.w_down),
    ]
    place_documents(r, documents)
    wait_all(early)
    r.q[...] = dot(r.x[:length, :], r.w_mixed[:, :width]).astype(bf16)
    r.kv[...] = dot(r.x[...], r.w_mixed[:, width:]).astype(bf16)
    outs = [move.start(r.q, r.q_o), move.start(r.kv, r.kv_o)]
    pairs = range(width // LANES)
    spread_pairs(r.qm, r.q, 64**-0.5, pairs)
    turn_tiles(r.vt, r.kv, width, pairs)
    attention_forward(r, core, decoder)
    wait_all(later)
    outs += [move.start(r.att, r.att_o), move.start(r.lse, r.lse_o)]
    unit, inverse = standardize(r.x[:length, :].astype(f32) + dot(r.att[...], r.w_out[...]))
    r.unit1[...] = unit
    r.inv1[...] = jnp.broadcast_to(inverse, r.inv1.shape)
    r.first_low[...] = (unit * r.gains[0:1, :]).astype(bf16)
    outs += [
        move.start(r.unit1, r.unit1_o),
        move.start(r.inv1, r.inv1_o),
        move.start(r.first_low, r.first_low_o),
    ]

    @pl.when(decoder == 0)
    def _():
        feed_forward(r, r.first_low)
        late = [
            move.start(r.first_low, r.ffn_low_o),
            move.start(r.act, r.act_o),
            move.start(r.slope, r.slope_o),
        ]
        unit2, inverse2 = standardize(r.unit1[...] * r.gains[0:1, :] + r.sum[...])
        r.memory[:length, :] = (unit2 * r.gains[1:2, :]).astype(bf16)
        r.memory[length:, :] = r.docs[0]
        late += [move.start(r.memory, r.memory_o)]
        r.unit2[...] = unit2
        r.inv2[...] = jnp.broadcast_to(inverse2, r.inv2.shape)
        late += [move.start(r.unit2, r.unit2_o), move.start(r.inv2, r.inv2_o)]
        wait_all(late)

    wait_all(outs)


def cross_both_ways(r):
    length, width = r.unit1_h.shape
    core = r.meta[1]
    move = Copies(r.sems)
    whole = pl.ds(0, length)
    documents = load_documents(r, move, r.x_own_h, r.memory_own_h, r.memory_other_h)
    moves = [
        move.start(r.memory_own_h.at[whole], r.x.at[whole]),
        move.start(r.memory_other_h.at[whole], r.x.at[pl.ds(length, length)]),
        move.start(r.w_pair_h, r.w_pair),
        move.start(r.first_low_h, r.first_low),
        move.start(r.w_query_h, r.w_query),
    ]
    later = [
        move.start(r.unit1_h, r.unit1),
        move.start(r.w_cross_h, r.w_cross),
        move.start(r.w_in_h, r.w_in),
        move.start(r.w_down_h, r.w_down),
        move.start(r.cot_h.at[r.micro], r.cot),
    ]
    place_documents(r, documents)
    wait_all(moves)
    r.kv[...] = dot(r.x[...], r.w_pair[...]).astype(bf16)
    r.q[...] = dot(r.first_low[...], r.w_query[...]).astype(bf16)
    pairs = range(width // LANES)
    spread_pairs(r.qm, r.q, 64**-0.5, pairs)
    turn_tiles(r.vt, r.kv, width, pairs)
    turn_tiles(r.kt, r.kv, 0, pairs)
    attention_forward(r, core, 0)
    outs = [move.start(r.att, r.att_o)]
    wait_all(later)
    first = r.unit1[...] * r.gains[0:1, :]
    unit, inverse = standardize(first + dot(r.att[...], r.w_cross[...]))
    r.unit2[...] = unit
    r.inv2[...] = jnp.broadcast_to(inverse, r.inv2.shape)
    r.second_low[...] = (unit * r.cross_gain[...]).astype(bf16)
    outs += [move.start(r.second_low, r.ffn_low_o)]
    feed_forward(r, r.second_low)
    outs += [move.start(r.act, r.act_o)]
    unit3, inverse3 = standardize(r.unit2[...] * r.cross_gain[...] + r.sum[...])
    r.decoded[...] = (unit3 * r.gains[1:2, :]).astype(bf16)
    outs += [move.start(r.decoded, r.decoded_o)]
    grad_third, gain_late = standardize_back(
        r.cot[...].astype(f32), unit3, r.gains[1:2, :], inverse3
    )
    r.keep[...] = grad_third
    r.down_grad[...] = grad_third.astype(bf16)
    outs += [move.start(r.down_grad, r.down_grad_o)]
    feed_backward(r)
    outs += [move.start(r.up_grad, r.up_grad_o)]
    grad_sum, gain_cross = standardize_back(
        r.keep[...] + r.sum[...], r.unit2[...], r.cross_gain[...], r.inv2[:, 0:1]
    )
    r.gain_grads[...] = jnp.zeros(r.gain_grads.shape, f32)
    r.gain_grads[0:1, :] = gain_late
    r.gain_grads[1:2, :] = gain_cross
    r.keep[...] = grad_sum
    r.branch[...] = grad_sum.astype(bf16)
    outs += [move.start(r.gain_grads, r.gain_grads_o), move.start(r.branch, r.branch_o)]
    r.q[...] = dot_nt(r.branch[...], r.w_cross[...]).astype(bf16)
    spread_pairs(r.gm, r.q, 1.0, pairs)
    row_products(r, r.q, pairs)
    attention_backward(r, core, 0, pairs)
    r.dq_low[...] = r.dq[...].astype(bf16)
    r.keep[...] += dot_nt(r.dq_low[...], r.w_query[...])
    outs += [move.start(r.dq_low, r.dq_low_o), move.start(r.keep, r.grad_first_o)]
    r.dkv_low[...] = r.dkv[...].astype(bf16)
    outs += [move.start(r.dkv_low, r.dkv_o)]
    part = dot_nt(r.dkv_low[...], r.w_pair[...])
    r.part_other[...] = part[length:, :].astype(bf16)
    r.part_own[...] = part[:length, :]
    outs += [move.start(r.part_other, r.part_other_o), move.start(r.part_own, r.part_own_o)]
    wait_all(outs)


def feed_backward_alone(r):
    move = Copies(r.sems)
    early = [
        move.start(r.grad_memory_h, r.cot),
        move.start(r.unit2_h, r.unit2),
        move.start(r.inv2_h, r.inv2),
    ]
    later = [
        move.start(r.w_down_h, r.w_down),
        move.start(r.slope_h, r.slope),
        move.start(r.w_in_h, r.w_in),
    ]
    wait_all(early)
    grad_third, gain_late = standardize_back(
        r.cot[...].astype(f32), r.unit2[...], r.gains[1:2, :], r.inv2[:, 0:1]
    )
    r.gain_grads[...] = jnp.broadcast_to(gain_late, r.gain_grads.shape)
    r.keep[...] = grad_third
    r.down_grad[...] = grad_third.astype(bf16)
    outs = [move.start(r.down_grad, r.down_grad_o), move.start(r.gain_grads, r.gain_late_o)]
    wait_all(later)
    feed_backward(r)
    outs += [move.start(r.up_grad, r.up_grad_o)]
    r.keep[...] += r.sum[...]
    outs += [move.start(r.keep, r.grad_first_o)]
    wait_all(outs)


def self_backward(r, plan):
    r.micro, first, last = plan
    length, width = r.att_h.shape
    decoder, core = r.meta[0], r.meta[1]
    pairs = range(first, last)
    low, high = first * LANES, last * LANES
    move = Copies(r.sems)
    later = [
        move.start(r.q_h, r.q),
        move.start(r.kv_h, r.kv),
        move.start(r.att_h, r.att),
        move.start(r.lse_h, r.lse),
    ]
    if first == 0:
        early = [
            move.start(r.grad_first_h, r.keep),
            move.start(r.unit1_h, r.unit1),
            move.start(r.inv1_h, r.inv1),
            move.start(r.w_out_h, r.w_out),
        ]
    else:
        early = [move.start(r.grad_att_h, r.grad_att)]
    outs = []
    place_documents(r, load_documents(r, move, r.x_own_h, r.x_own_h, r.x_other_h))
    wait_all(early)
    if first == 0:
        grad_sum, gain_early = standardize_back(
            r.keep[...], r.unit1[...], r.gains[0:1, :], r.inv1[:, 0:1]
        )
        r.gain_grads[...] = jnp.broadcast_to(gain_early, r.gain_grads.shape)
        r.keep[...] = grad_sum
        r.branch[...] = grad_sum.astype(bf16)
        r.grad_att[...] = dot_nt(r.branch[...], r.w_out[...]).astype(bf16)
        outs += [move.start(r.gain_grads, r.gain_early_o), move.start(r.branch, r.branch_o)]
        if last < width // LANES:
            outs += [move.start(r.keep, r.grad_sum_o), move.start(r.grad_att, r.grad_att_o)]
    wait_all(later)
    if last == width // LANES:
        ends = [move.start(r.w_mixed_h, r.w_mixed)]
        if first > 0:
            ends += [
                move.start(r.grad_sum_h, r.keep),
                move.start(r.dq_h.at[:, pl.ds(0, low)], r.dq_low.at[:, pl.ds(0, low)]),
                move.start(r.dkv_h.at[:, pl.ds(0, low)], r.dkv_low.at[:, pl.ds(0, low)]),
                move.start(
                    r.dkv_h.at[:, pl.ds(width, low)], r.dkv_low.at[:, pl.ds(width, low)]
                ),
            ]
    spread_pairs(r.qm, r.q, 64**-0.5, pairs)
    turn_tiles(r.kt, r.kv, 0, pairs)
    spread_pairs(r.gm, r.grad_att, 1.0, pairs)
    row_products(r, r.grad_att, pairs)
    attention_backward(r, core, decoder, pairs)
    r.dq_low[:, low:high] = r.dq[:, low:high].astype(bf16)
    for start in (0, width):
        span = slice(start + low, start + high)
        r.dkv_low[:, span] = r.dkv[:, span].astype(bf16)
    if last == width // LANES:
        wait_all(ends)
        outs += [move.start(r.dq_low, r.dq_low_o), move.start(r.dkv_low, r.dkv_o)]
        r.keep[...] += dot_nt(r.dq_low[...], r.w_mixed[:, :width])
        part = dot_nt(r.dkv_low[...], r.w_mixed[:, width:])
        r.part_other[...] = part[length:, :].astype(bf16)
        r.keep[...] += part[:length, :]
        outs += [move.start(r.part_other, r.part_other_o), move.start(r.keep, r.part_own_o)]
    else:
        outs.append(move.start(r.dq_low.at[:, pl.ds(low, high - low)], r.dq_low_o.at[:, pl.ds(low, high - low)]))
        for start in (0, width):
            span = pl.ds(start + low, high - low)
            outs.append(move.start(r.dkv_low.at[:, span], r.dkv_o.at[:, span]))
    wait_all(outs)


def contract_blocks(r, plan):
    for core in range(2):

        @pl.when(r.meta[1] == core)
        def _(core=core):
            targets = [None] * 4
            for half in range(2):
                target = r.kept_o if half == core else r.sent_o
                targets[2 * half], targets[2 * half + 1] = target.at[0], target.at[1]
            order = (0, 1, 2, 3) if core else (2, 3, 0, 1)
            contract_in_order(r, plan(r), order, targets, Copies(r.sems))


def contract_in_order(r, blocks, order, targets, move):
    loads = dict()
    for slot in order:
        for buffer, sources, at in blocks[slot][1:]:
            if (id(buffer), at) not in loads:
                span = pl.ds(at * CHUNK, CHUNK)
                row = 0
                copies = []
                for source in sources:
                    rows = pl.ds(row, source.shape[0])
                    copies.append(move.start(source.at[:, span], buffer.at[rows, span]))
                    row += source.shape[0]
                loads[id(buffer), at] = copies
    outs = []
    held = dict()
    for slot in order:
        turn, (left, _, left_at), (right, _, right_at) = blocks[slot]
        wait_all(loads.pop((id(left), left_at), ()))
        wait_all(loads.pop((id(right), right_at), ()))
        if held.get(id(turn)) != left_at:
            for row in range(0, left.shape[0], CHUNK):
                block = left[row : row + CHUNK, left_at * CHUNK : (left_at + 1) * CHUNK]
                turn[:, row : row + CHUNK] = jnp.transpose(block)
            held[id(turn)] = left_at
        block = right[:, right_at * CHUNK : (right_at + 1) * CHUNK]
        r.blocks[slot] = dot(turn[:, : right.shape[0]], block).astype(bf16)
        outs.append(move.start(r.blocks.at[slot], targets[slot]))
    wait_all(outs)


def spread_pieces(r, targets):
    z = r.meta[3]
    group, height = r.own_h.shape[:2]
    rows = r.own_h.shape[2] // group
    for core in range(2):
        for x in range(2):

            @pl.when((r.meta[1] == core) & (r.meta[2] == x))
            def _(core=core, x=x):
                move = Copies(r.sems)
                parts = [
                    (r.own_h, core, x),
                    (r.own_x_h, core, 1 - x),
                    (r.other_h, 1 - core, x),
                    (r.other_x_h, 1 - core, 1 - x),
                ]
                loads = [
                    move.start(source, r.pieces.at[place])
                    for place, (source, _, _) in enumerate(parts)
                ]
                outs = []
                slot = 0
                gains = None
                for place, (_, half, side) in enumerate(parts):
                    loads[place].wait()
                    for step in range(group):
                        row = pl.multiple_of(lax.rem(z + (group - step), group) * rows, rows)
                        start = 0
                        for target in targets(r, 2 * half + side, row, rows):
                            r.wide[slot] = r.pieces[place, step, start : start + rows].astype(f32)
                            outs.append(move.start(r.wide.at[slot], target))
                            slot += 1
                            start += rows
                        if start < height:
                            extra = r.pieces[place, step, start:height].astype(f32)
                            gains = extra if gains is None else gains + extra
                r.gains_o[...] = gains[: r.gains_o.shape[0], :]
                wait_all(outs)


def launch(kernel, plan, side, scalars, small, large, outs, scratch, copies, work, previous=None, after=()):
    names = list(scalars) + list(small) + list(large)
    arrays = list(scalars.values()) + list(small.values()) + list(large.values())
    specs = (
        [pl.BlockSpec(memory_space=pltpu.SMEM)] * len(scalars)
        + [pl.BlockSpec(memory_space=pltpu.VMEM)] * len(small)
        + [pl.BlockSpec(memory_space=pl.ANY)] * len(large)
    )
    aliases = dict()
    for position, name in enumerate(outs):
        if previous and name in previous:
            aliases[len(arrays)] = position
            names.append("previous_" + name)
            arrays.append(previous[name])
            specs.append(pl.BlockSpec(memory_space=pl.ANY))
    for array in after:
        names.append("")
        arrays.append(array)
        specs.append(pl.BlockSpec(memory_space=pl.ANY))
    names += list(outs) + list(scratch) + ["sems"]

    def body(*refs):
        r = types.SimpleNamespace(**dict(zip(names, refs)))

        def run():
            if isinstance(plan, int):
                r.micro = plan
                kernel(r)
            else:
                kernel(r, plan)

        if side is None:
            run()
        else:
            pl.when(r.meta[0] == side)(run)

    results = pl.pallas_call(
        body,
        out_shape=[jax.ShapeDtypeStruct(*shape) for shape in outs.values()],
        in_specs=specs,
        out_specs=[
            pl.BlockSpec(memory_space=pltpu.VMEM if shape[0][0] < 8 else pl.ANY)
            for shape in outs.values()
        ],
        scratch_shapes=[
            pltpu.SMEM(*shape) if shape[1] == jnp.int32 else pltpu.VMEM(*shape)
            for shape in scratch.values()
        ]
        + [pltpu.SemaphoreType.DMA((copies,))],
        input_output_aliases=aliases,
        compiler_params=pltpu.CompilerParams(vmem_limit_bytes=58 * 1024 * 1024),
        cost_estimate=pl.CostEstimate(
            flops=work * 10**9, bytes_accessed=1 << 20, transcendentals=0
        ),
    )(*arrays)
    return types.SimpleNamespace(**dict(zip(outs, results)))


def attention_scratch(length, width):
    pairs, q_tiles, k_tiles = width // LANES, length // TILE, 2 * length // TILE
    return dict(
        q=((length, width), bf16),
        kv=((2 * length, 2 * width), bf16),
        qm=((pairs, q_tiles, 2 * TILE, LANES), bf16),
        kdc=((2 * length, LANES), f32),
        docs=((3, 16, width), bf16),
        qd=((length // TILE, 8, TILE), f32),
        bounds=((2, 3 * length // TILE), jnp.int32),
        bias=((TILE, TILE), f32),
        lse=((q_tiles, 8, 2 * TILE), f32),
        att=((length, width), bf16),
        turned=((width, TILE), f32),
    )


def forward_scratch(length, width):
    k_tiles = 2 * length // TILE
    return dict(
        vt=((k_tiles, width, TILE), bf16),
        top=((8, 2 * TILE), f32),
        total=((8, 2 * TILE), f32),
    )


def backward_scratch(length, width):
    pairs, q_tiles, k_tiles = width // LANES, length // TILE, 2 * length // TILE
    return dict(
        kt=((k_tiles, width, TILE), bf16),
        gm=((pairs, q_tiles, 2 * TILE, LANES), bf16),
        delta=((q_tiles, 8, 2 * TILE), f32),
        dkv=((2 * length, 2 * width), f32),
        dq=((length, width), f32),
        dkv_low=((2 * length, 2 * width), bf16),
        part_other=((length, width), bf16),
        dq_low=((length, width), bf16),
    )


def for_sending(shard):

    def short(part):
        return part.astype(jnp.bfloat16) if part.dtype == jnp.float32 else part

    return jax.tree.map(short, shard)


def from_behind(block, axis, distance):
    devices = range(lax.axis_size(axis))
    route = [(i - distance, i) for i in devices if i - distance in devices]
    return lax.ppermute(block, axis, route)


def from_root(shard, axis, root):
    mine = lax.axis_index(axis) == root
    return lax.psum(jnp.where(mine, shard, jnp.zeros_like(shard)), axis)


def matmul(left_side, right_side):
    return jnp.einsum("rsd,de->rse", left_side, right_side, preferred_element_type=jnp.float32)


def matmul_back(left_side, right_side):
    return jnp.einsum("rse,de->rsd", left_side, right_side, preferred_element_type=jnp.float32)


def contract(left_side, right_side):
    return jnp.einsum("rsd,rse->de", left_side, right_side, preferred_element_type=jnp.float32)


def normalize(values, gain_row):
    center = values - jnp.mean(values, axis=-1, keepdims=True)
    inverse = lax.rsqrt(jnp.mean(center * center, axis=-1, keepdims=True) + epsilon)
    standard = center * inverse
    return (standard * gain_row, standard, inverse)


def normalize_back(grad_out, standard, gain_row, inverse):
    scaled = grad_out * gain_row
    grad_in = inverse * (
        scaled
        - jnp.mean(scaled, axis=-1, keepdims=True)
        - standard * jnp.mean(scaled * standard, axis=-1, keepdims=True)
    )
    return (grad_in, jnp.sum(grad_out * standard, axis=(0, 1)))


def allowed_mask(query_docs, key_docs, query_place, key_place, causal):
    same_doc = query_docs[:, :, None] == key_docs[:, None, :]
    earlier = query_place[:, None] >= key_place[None, :]
    return (same_doc & (earlier | jnp.logical_not(causal)))[:, None]


def attend(queries, keys_local, values_local, query_docs, key_docs, causal, is_cross):
    rows_here, shard_len, model_width = queries.shape
    head_dim = model_width // HEADS
    score_scale = head_dim ** (-0.5)
    query_place = lax.axis_index("seq") * shard_len + jnp.arange(shard_len)
    query_heads = queries.reshape(rows_here, shard_len, HEADS, head_dim)

    def absorb(state_tuple, pieces):
        running_top, running_total, running_sum = state_tuple
        key_piece, value_piece, doc_piece = pieces
        piece_len = key_piece.shape[1]
        raw_scores = jnp.einsum(
            "rqhd,rkhd->rhqk",
            query_heads,
            key_piece.reshape(rows_here, piece_len, HEADS, head_dim),
            preferred_element_type=jnp.float32,
        )
        allowed = allowed_mask(query_docs, doc_piece, query_place, jnp.arange(piece_len), causal)
        scores = jnp.where(allowed, raw_scores * score_scale, negative_big)
        new_top = jnp.maximum(running_top, jnp.max(scores, axis=-1))
        weights = jnp.where(allowed, jnp.exp(scores - new_top[..., None]), 0.0)
        new_total = jnp.sum(weights, axis=-1)
        product = jnp.einsum(
            "rhqk,rkhd->rhqd",
            weights.astype(jnp.bfloat16),
            value_piece.reshape(rows_here, piece_len, HEADS, head_dim),
            preferred_element_type=jnp.float32,
        )
        return (new_top, new_total, product)

    init_state = (
        jnp.full((rows_here, HEADS, shard_len), negative_big, jnp.float32),
        jnp.zeros((rows_here, HEADS, shard_len), jnp.float32),
        jnp.zeros((rows_here, HEADS, shard_len, head_dim), jnp.float32),
    )
    if is_cross:
        final_top, final_total, final_sum = absorb(
            init_state,
            (
                lax.all_gather(keys_local, "seq", axis=1, tiled=True),
                lax.all_gather(values_local, "seq", axis=1, tiled=True),
                lax.all_gather(for_sending(key_docs), "seq", axis=1, tiled=True),
            ),
        )
    else:
        final_top, final_total, final_sum = absorb(
            init_state,
            (
                lax.all_gather(keys_local, "seq", axis=1, tiled=True),
                lax.all_gather(values_local, "seq", axis=1, tiled=True),
                lax.all_gather(key_docs, "seq", axis=1, tiled=True),
            ),
        )
    attended = (
        (final_sum / final_total[..., None])
        .transpose(0, 2, 1, 3)
        .reshape(rows_here, shard_len, model_width)
    )
    return (attended, final_top + jnp.log(final_total))


def attend_back(
    queries,
    keys_local,
    values_local,
    query_docs,
    key_docs,
    causal,
    log_total,
    grad_attended,
    is_cross,
):
    rows_here, shard_len, model_width = queries.shape
    head_dim = model_width // HEADS
    score_scale = head_dim ** (-0.5)
    query_place = lax.axis_index("seq") * shard_len + jnp.arange(shard_len)
    if is_cross:
        keys_full, values_full, docs_full = (
            lax.all_gather(keys_local, "seq", axis=1, tiled=True),
            lax.all_gather(values_local, "seq", axis=1, tiled=True),
            lax.all_gather(for_sending(key_docs), "seq", axis=1, tiled=True).astype(key_docs.dtype),
        )
    else:
        keys_full, values_full, docs_full = (
            lax.all_gather(keys_local, "seq", axis=1, tiled=True),
            lax.all_gather(values_local, "seq", axis=1, tiled=True),
            lax.all_gather(key_docs, "seq", axis=1, tiled=True),
        )
    full_len = keys_full.shape[1]
    query_heads = queries.reshape(rows_here, shard_len, HEADS, head_dim)
    key_heads = keys_full.reshape(rows_here, full_len, HEADS, head_dim)
    value_heads = values_full.reshape(rows_here, full_len, HEADS, head_dim)
    grad_heads = grad_attended.reshape(rows_here, shard_len, HEADS, head_dim)
    raw_scores = jnp.einsum(
        "rqhd,rkhd->rhqk", query_heads, key_heads, preferred_element_type=jnp.float32
    )
    allowed = allowed_mask(query_docs, docs_full, query_place, jnp.arange(full_len), causal)
    shifted = jnp.where(allowed, raw_scores * score_scale - log_total[..., None], negative_big)
    probs = jnp.where(allowed, jnp.exp(shifted), 0.0)
    grad_probs = jnp.einsum(
        "rqhd,rkhd->rhqk", grad_heads, value_heads, preferred_element_type=jnp.float32
    )
    delta = jnp.sum(probs * grad_probs, axis=-1)
    grad_scores = (probs * (grad_probs - delta[..., None]) * score_scale).astype(jnp.bfloat16)
    grad_queries = jnp.einsum(
        "rhqk,rkhd->rqhd", grad_scores, key_heads, preferred_element_type=jnp.float32
    ).reshape(rows_here, shard_len, model_width)
    probs_low = probs.astype(jnp.bfloat16)

    def key_terms(span):
        grad_keys = jnp.einsum(
            "rhqk,rqhd->krhd", grad_scores, query_heads, preferred_element_type=jnp.float32
        )
        grad_values = jnp.einsum(
            "rhqk,rqhd->krhd", probs_low, grad_heads, preferred_element_type=jnp.float32
        )
        return jnp.concatenate(
            [
                grad_keys.reshape(span, rows_here, model_width),
                grad_values.reshape(span, rows_here, model_width),
            ],
            axis=-1,
        )

    if is_cross:
        pair_terms = lax.psum_scatter(
            key_terms(shard_len * lax.axis_size("seq")).astype(jnp.bfloat16),
            "seq",
            scatter_dimension=0,
            tiled=True,
        ).astype(jnp.float32)
    else:
        pair_terms = lax.psum_scatter(
            key_terms(shard_len * lax.axis_size("seq")).astype(jnp.bfloat16),
            "seq",
            scatter_dimension=0,
            tiled=True,
        ).astype(jnp.float32)
    return (grad_queries, pair_terms.transpose(1, 0, 2))


def layer_forward(hidden_in, doc_own, memory, memory_docs, weights, is_decoder):
    (
        qkv_weight,
        out_weight,
        in_weight,
        down_weight,
        gains_pair,
        query_weight,
        pair_weight,
        cross_weight,
        cross_gains,
    ) = weights
    model_width = hidden_in.shape[-1]
    mixed = matmul(hidden_in, qkv_weight).astype(jnp.bfloat16)
    attended, self_lse = attend(
        mixed[..., :model_width],
        mixed[..., model_width : 2 * model_width],
        mixed[..., 2 * model_width :],
        doc_own,
        doc_own,
        is_decoder,
        False,
    )
    attended = attended.astype(jnp.bfloat16)
    first, first_unit, first_inv = normalize(
        hidden_in.astype(jnp.float32) + matmul(attended, out_weight), gains_pair[0]
    )
    first_low = first.astype(jnp.bfloat16)
    cross_queries = matmul(first_low, query_weight).astype(jnp.bfloat16)
    pair = matmul(memory, pair_weight).astype(jnp.bfloat16)
    cross_att, cross_lse = attend(
        cross_queries,
        pair[..., :model_width],
        pair[..., model_width:],
        doc_own,
        memory_docs,
        False,
        True,
    )
    cross_att = cross_att.astype(jnp.bfloat16)
    second_cross, second_unit, second_inv = normalize(
        first + matmul(cross_att, cross_weight), cross_gains
    )
    second = jnp.where(is_decoder, second_cross, first)
    second_low = second.astype(jnp.bfloat16)
    upward = matmul(second_low, in_weight)
    active = jax.nn.silu(upward).astype(jnp.bfloat16)
    result, third_unit, third_inv = normalize(second + matmul(active, down_weight), gains_pair[1])
    saved = {
        "mixed": mixed,
        "attended": attended,
        "self_lse": self_lse,
        "first_unit": first_unit,
        "first_inv": first_inv,
        "first_low": first_low,
        "cross_queries": cross_queries,
        "pair": pair,
        "cross_att": cross_att,
        "cross_lse": cross_lse,
        "second_unit": second_unit,
        "second_inv": second_inv,
        "second_low": second_low,
        "upward": upward,
        "active": active,
        "third_unit": third_unit,
        "third_inv": third_inv,
    }
    return (result, saved)


def layer_backward(
    grad_result, saved, hidden_in, doc_own, memory, memory_docs, weights, is_decoder
):
    (
        qkv_weight,
        out_weight,
        in_weight,
        down_weight,
        gains_pair,
        query_weight,
        pair_weight,
        cross_weight,
        cross_gains,
    ) = weights
    model_width = hidden_in.shape[-1]
    grad_third, grad_gain_late = normalize_back(
        grad_result, saved["third_unit"], gains_pair[1], saved["third_inv"]
    )
    down_grad = grad_third.astype(jnp.bfloat16)
    grad_down_w = contract(saved["active"], down_grad)
    grad_active = matmul_back(down_grad, down_weight).astype(jnp.bfloat16)
    sigmoid_up = jax.nn.sigmoid(saved["upward"])
    grad_upward = (
        grad_active.astype(jnp.float32)
        * (sigmoid_up + saved["upward"] * sigmoid_up * (1.0 - sigmoid_up))
    ).astype(jnp.bfloat16)
    grad_in_w = contract(saved["second_low"], grad_upward)
    grad_second = grad_third + matmul_back(grad_upward, in_weight)
    grad_cross_sum, grad_cross_gain = normalize_back(
        grad_second, saved["second_unit"], cross_gains, saved["second_inv"]
    )
    decoder_flag = is_decoder.astype(jnp.float32)
    grad_cross_sum = grad_cross_sum * decoder_flag
    grad_cross_gain = grad_cross_gain * decoder_flag
    cross_branch = grad_cross_sum.astype(jnp.bfloat16)
    grad_cross_w = contract(saved["cross_att"], cross_branch)
    grad_cross_att = matmul_back(cross_branch, cross_weight).astype(jnp.bfloat16)
    pair = saved["pair"]
    grad_cross_q, grad_pair = attend_back(
        saved["cross_queries"],
        pair[..., :model_width],
        pair[..., model_width:],
        doc_own,
        memory_docs,
        False,
        saved["cross_lse"],
        grad_cross_att,
        True,
    )
    grad_cross_q = grad_cross_q.astype(jnp.bfloat16)
    grad_pair = grad_pair.astype(jnp.bfloat16)
    grad_query_w = contract(saved["first_low"], grad_cross_q)
    grad_pair_w = contract(memory, grad_pair)
    grad_memory = matmul_back(grad_pair, pair_weight)
    grad_first = jnp.where(
        is_decoder, grad_cross_sum + matmul_back(grad_cross_q, query_weight), grad_second
    )
    grad_first_sum, grad_gain_early = normalize_back(
        grad_first, saved["first_unit"], gains_pair[0], saved["first_inv"]
    )
    self_branch = grad_first_sum.astype(jnp.bfloat16)
    grad_out_w = contract(saved["attended"], self_branch)
    grad_attended = matmul_back(self_branch, out_weight).astype(jnp.bfloat16)
    mixed = saved["mixed"]
    grad_queries, grad_pair_self = attend_back(
        mixed[..., :model_width],
        mixed[..., model_width : 2 * model_width],
        mixed[..., 2 * model_width :],
        doc_own,
        doc_own,
        is_decoder,
        saved["self_lse"],
        grad_attended,
        False,
    )
    grad_mixed = jnp.concatenate([grad_queries, grad_pair_self], axis=-1).astype(jnp.bfloat16)
    grad_qkv_w = contract(hidden_in, grad_mixed)
    grad_hidden = grad_first_sum + matmul_back(grad_mixed, qkv_weight)
    layer_grads = (
        grad_qkv_w,
        grad_out_w,
        grad_in_w,
        grad_down_w,
        jnp.stack([grad_gain_early, grad_gain_late]),
        grad_query_w,
        grad_pair_w,
        grad_cross_w,
        grad_cross_gain,
    )
    return (grad_hidden, grad_memory, layer_grads)


def any_rows(
    layer_input,
    segment_ids,
    attn_qkv,
    attn_out,
    ffn_in,
    ffn_out,
    norm_gain,
    cross_query,
    cross_pair,
    cross_out,
    cross_gain,
    out_cotangent,
):
    micro_count = layer_input.shape[1]
    section_index = lax.axis_index("section")
    is_decoder = section_index == 1
    weights = (
        attn_qkv[0],
        attn_out[0],
        ffn_in[0],
        ffn_out[0],
        norm_gain[0],
        cross_query,
        cross_pair,
        cross_out,
        cross_gain,
    )
    inputs_all = layer_input[0]
    docs_all = segment_ids[0]
    slot_ids = jnp.arange(micro_count)
    received = (jnp.zeros_like(inputs_all[0]), jnp.zeros_like(docs_all[0]))
    results = jnp.zeros_like(inputs_all)
    memories = []
    memory_doc_list = []
    for step_index in range(micro_count + 1):
        batch_index = step_index - section_index
        is_valid = (batch_index >= 0) & (batch_index < micro_count)
        chosen = jnp.clip(batch_index, 0, micro_count - 1)
        hidden_in = lax.dynamic_index_in_dim(inputs_all, chosen, 0, keepdims=False)
        doc_own = lax.dynamic_index_in_dim(docs_all, chosen, 0, keepdims=False)
        memory = received[0]
        memory_docs = jnp.where(is_valid & is_decoder, received[1], doc_own)
        memories.append(memory)
        memory_doc_list.append(memory_docs)
        result, saved = layer_forward(hidden_in, doc_own, memory, memory_docs, weights, is_decoder)
        low_result = result.astype(jnp.bfloat16)
        writing = (slot_ids == chosen) & is_valid
        results = jnp.where(writing[:, None, None, None], low_result[None], results)
        if step_index < micro_count:
            received = from_behind((low_result, doc_own), "section", 1)
    memory_stack = jnp.stack(memories)
    memory_doc_stack = jnp.stack(memory_doc_list)
    totals = tuple((jnp.zeros(weight.shape, jnp.float32) for weight in weights))
    input_grads = jnp.zeros(inputs_all.shape, jnp.float32)
    returned = jnp.zeros(inputs_all.shape[1:], jnp.float32)
    for step_index in range(micro_count + 1):
        batch_index = micro_count - step_index - section_index
        is_valid = (batch_index >= 0) & (batch_index < micro_count)
        chosen = jnp.clip(batch_index, 0, micro_count - 1)
        forward_step = jnp.clip(batch_index + section_index, 0, micro_count)
        hidden_in = lax.dynamic_index_in_dim(inputs_all, chosen, 0, keepdims=False)
        doc_own = lax.dynamic_index_in_dim(docs_all, chosen, 0, keepdims=False)
        memory = lax.dynamic_index_in_dim(memory_stack, forward_step, 0, keepdims=False)
        memory_docs = lax.dynamic_index_in_dim(memory_doc_stack, forward_step, 0, keepdims=False)
        discarded, saved = layer_forward(
            hidden_in, doc_own, memory, memory_docs, weights, is_decoder
        )
        cotangent = jnp.where(
            is_decoder,
            lax.dynamic_index_in_dim(out_cotangent, chosen, 0, keepdims=False).astype(jnp.float32),
            returned,
        )
        grad_hidden, grad_memory, layer_grads = layer_backward(
            cotangent, saved, hidden_in, doc_own, memory, memory_docs, weights, is_decoder
        )
        valid_flag = is_valid.astype(jnp.float32)
        totals = tuple(
            (running + valid_flag * fresh for running, fresh in zip(totals, layer_grads))
        )
        writing = (slot_ids == chosen) & is_valid
        input_grads = jnp.where(writing[:, None, None, None], grad_hidden[None], input_grads)
        if step_index < micro_count:
            returned = from_behind(grad_memory.astype(jnp.bfloat16), "section", -1).astype(
                grad_memory.dtype
            )
    group_sums = lax.psum(
        (
            totals[0],
            totals[1],
            totals[2],
            totals[3],
            totals[4],
            totals[5],
            totals[6],
            totals[7],
            totals[8],
        ),
        ("seq", "dp"),
    )
    section_sums = group_sums[:5]
    cross_sums = (
        from_root(group_sums[5].astype(jnp.bfloat16), "section", 1).astype(jnp.float32),
        from_root(group_sums[6].astype(jnp.bfloat16), "section", 1).astype(jnp.float32),
        from_root(group_sums[7].astype(jnp.bfloat16), "section", 1).astype(jnp.float32),
        from_root(group_sums[8].astype(jnp.bfloat16), "section", 1).astype(jnp.float32),
    )
    return (
        results[None],
        input_grads[None],
        section_sums[0][None],
        section_sums[1][None],
        section_sums[2][None],
        section_sums[3][None],
        section_sums[4][None],
        cross_sums[0],
        cross_sums[1],
        cross_sums[2],
        cross_sums[3],
    )


def split_rows(
    layer_input,
    segment_ids,
    attn_qkv,
    attn_out,
    ffn_in,
    ffn_out,
    norm_gain,
    cross_query,
    cross_pair,
    cross_out,
    cross_gain,
    out_cotangent,
):
    micros = layer_input.shape[1]
    length, width = layer_input.shape[3:]
    hidden = ffn_in.shape[-1]
    q_tiles = length // TILE
    group = lax.axis_size("dp") // 2
    axes = ("section", "seq", "dp")
    decoder = lax.axis_index("section") == 1
    flag = decoder.astype(jnp.int32)
    x = lax.axis_index("seq")
    core = lax.rem(lax.axis_index("dp"), 2)
    z = lax.axis_index("dp") // 2
    places = [(t, i, k, c) for t in range(2) for i in range(2) for k in range(group) for c in range(2)]

    def number(t, i, k, c):
        return ((t * 2 + i) * group + k) * 2 + c

    def send(values, target, section=None):
        route = [
            (number(*place), number(*target(*place)))
            for place in places
            if section in (None, place[0]) and target(*place)
        ]
        return lax.ppermute(values, axes, route)

    def to_core(t, i, k, c):
        return (t, i, k, 1 - c)

    def to_x(t, i, k, c):
        return (t, 1 - i, k, c)

    def to_row(t, i, k, c):
        return (t, c, k, i)

    def to_decoder(t, i, k, c):
        return (1, i, k, c) if t == 0 else None

    def to_encoder(t, i, k, c):
        return (0, i, k, c) if t == 1 else None

    def fence(values, *before):
        return lax.optimization_barrier((values,) + before)[0]

    def exchange(values):
        return send(values, to_core)

    low = ((length, width), bf16)
    wide = ((length, width), f32)
    marked = ((length + 16, width), bf16)
    both = ((2 * length, width), bf16)
    keys_all = ((2 * length, 2 * width), bf16)
    mixing = ((width, 3 * width), bf16)
    inner = ((length, hidden), bf16)
    lse = ((q_tiles, 8, 2 * TILE), f32)
    stat = ((length, LANES), f32)
    square = ((width, width), bf16)
    rising = ((width, hidden), bf16)
    falling = ((hidden, width), bf16)
    gain_rows = ((8, width), f32)

    meta = jnp.stack([flag, core, x, z]).astype(jnp.int32)
    numbers = segment_ids[0, :, 0].astype(bf16)
    padding = jnp.zeros((15, width), bf16)
    with_numbers = [
        jnp.concatenate([layer_input[0, micro, 0], numbers[micro][None], padding])
        for micro in range(micros)
    ]
    own = [send(with_numbers[0], to_row)]
    for micro in range(1, micros):
        own.append(send(fence(with_numbers[micro], own[-1]), to_row))
    other = [exchange(own[0])]

    plain = dict(meta=meta)
    small = dict(gains=norm_gain[0])
    forward, memories, memories_other = [], [], []
    for micro in range(micros):
        call = launch(
            self_forward,
            micro,
            None,
            plain,
            small,
            dict(
                x_own_h=own[micro],
                x_other_h=other[micro],
                w_mixed_h=attn_qkv[0],
                w_out_h=attn_out[0],
                w_in_h=ffn_in[0],
                w_down_h=ffn_out[0],
            ),
            dict(
                q_o=low,
                kv_o=keys_all,
                att_o=low,
                lse_o=lse,
                unit1_o=wide,
                inv1_o=stat,
                first_low_o=low,
                memory_o=marked,
                ffn_low_o=low,
                act_o=inner,
                slope_o=inner,
                unit2_o=wide,
                inv2_o=stat,
            ),
            dict(
                **attention_scratch(length, width),
                **forward_scratch(length, width),
                x=both,
                w_mixed=mixing,
                w_out=square,
                w_in=rising,
                w_down=falling,
                unit1=wide,
                inv1=stat,
                first_low=low,
                memory=marked,
                act=inner,
                slope=inner,
                unit2=wide,
                inv2=stat,
                sum=wide,
            ),
            28,
            26,
            after=(forward[0].lse_o,) if micro else (),
        )
        forward.append(call)
        memories.append(send(call.memory_o, to_decoder))
        if micro + 1 < micros:
            other.append(exchange(fence(own[micro + 1], call.lse_o)))

    for micro in range(micros):
        memories_other.append(exchange(fence(memories[micro], forward[-1].lse_o)))
    cotangent = send(fence(out_cotangent[:, 0], forward[0].lse_o), to_row)

    cross, grads_memory, made = [], [], []
    after = (forward[-1].lse_o,)
    for micro in range(micros):
        done = forward[micro]
        call = launch(
            cross_both_ways,
            micro,
            1,
            plain,
            dict(**small, cross_gain=cross_gain[None]),
            dict(
                x_own_h=own[micro],
                memory_own_h=memories[micro],
                memory_other_h=memories_other[micro],
                w_pair_h=cross_pair,
                first_low_h=done.first_low_o,
                unit1_h=done.unit1_o,
                w_query_h=cross_query,
                w_cross_h=cross_out,
                w_in_h=ffn_in[0],
                w_down_h=ffn_out[0],
                cot_h=cotangent,
            ),
            dict(
                att_o=low,
                ffn_low_o=low,
                act_o=inner,
                decoded_o=low,
                down_grad_o=low,
                up_grad_o=inner,
                gain_grads_o=gain_rows,
                branch_o=low,
                dq_low_o=low,
                dkv_o=keys_all,
                part_own_o=wide,
                part_other_o=low,
                grad_first_o=wide,
            ),
            dict(
                **attention_scratch(length, width),
                **forward_scratch(length, width),
                **backward_scratch(length, width),
                x=both,
                w_pair=((width, 2 * width), bf16),
                first_low=low,
                unit1=wide,
                w_query=square,
                w_cross=square,
                w_in=rising,
                w_down=falling,
                cot=low,
                unit2=wide,
                inv2=stat,
                second_low=low,
                act=inner,
                slope=inner,
                sum=wide,
                decoded=low,
                keep=wide,
                down_grad=low,
                up_grad=inner,
                gain_grads=gain_rows,
                branch=low,
                part_own=wide,
            ),
            36,
            44,
            dict(act_o=done.act_o, ffn_low_o=done.ffn_low_o),
            after,
        )
        cross.append(call)
        away = call.part_other_o
        if micro:
            away = fence(away, grads_memory[-1])
        total = call.part_own_o + exchange(away).astype(f32)
        made.append(total.astype(bf16))
        after = (made[micro],)
        grads_memory.append(send(made[micro], to_encoder))

    def backward_feed(micro, after):
        done, late = forward[micro], cross[micro]
        return launch(
            feed_backward_alone,
            micro,
            0,
            plain,
            dict(gains=norm_gain[0]),
            dict(
                grad_memory_h=grads_memory[micro],
                unit2_h=done.unit2_o,
                inv2_h=done.inv2_o,
                slope_h=done.slope_o,
                w_in_h=ffn_in[0],
                w_down_h=ffn_out[0],
            ),
            dict(gain_late_o=gain_rows, down_grad_o=low, up_grad_o=inner, grad_first_o=wide),
            dict(
                cot=low,
                unit2=wide,
                inv2=stat,
                slope=inner,
                w_in=rising,
                w_down=falling,
                gain_grads=gain_rows,
                keep=wide,
                down_grad=low,
                up_grad=inner,
                sum=wide,
            ),
            12,
            10,
            dict(
                down_grad_o=late.down_grad_o, up_grad_o=late.up_grad_o, grad_first_o=late.grad_first_o
            ),
            after,
        )

    def backward_self(micro, side, grad_first, previous=None, after=(), halfway=None):
        done = forward[micro]
        heads = width // LANES
        given = dict(
            x_own_h=own[micro],
            x_other_h=other[micro],
            q_h=done.q_o,
            kv_h=done.kv_o,
            att_h=done.att_o,
            lse_h=done.lse_o,
        )
        ahead = dict(
            grad_first_h=grad_first,
            unit1_h=done.unit1_o,
            inv1_h=done.inv1_o,
            w_out_h=attn_out[0],
        )
        makes = dict(dq_low_o=low, dkv_o=keys_all)
        makes_first = dict(gain_early_o=gain_rows, branch_o=low)
        makes_last = dict(part_own_o=wide, part_other_o=low)
        scratch = dict(
            **attention_scratch(length, width),
            **backward_scratch(length, width),
            w_out=square,
            w_mixed=mixing,
            unit1=wide,
            inv1=stat,
            keep=wide,
            branch=low,
            grad_att=low,
            gain_grads=gain_rows,
        )

        def part(first, last, large, outs, work, previous, after):
            return launch(
                self_backward,
                (micro, first, last),
                side,
                plain,
                small,
                dict(**given, **large),
                dict(**makes, **outs),
                scratch,
                28,
                work,
                previous,
                after,
            )

        if halfway is None:
            large = dict(**ahead, w_mixed_h=attn_qkv[0])
            outs = dict(**makes_first, **makes_last)
            return part(0, heads, large, outs, 22, previous, after)
        outs = dict(**makes_first, grad_sum_o=wide, grad_att_o=low)
        one = part(0, heads // 2, ahead, outs, 12, None, after)
        large = dict(
            w_mixed_h=attn_qkv[0],
            grad_sum_h=one.grad_sum_o,
            grad_att_h=one.grad_att_o,
            dq_h=one.dq_low_o,
            dkv_h=one.dkv_o,
        )
        two = part(heads // 2, heads, large, makes_last, 12, None, halfway(one))
        return types.SimpleNamespace(**{**vars(one), **vars(two)})

    def weight_grads(plan, side, arrays, scratch, after=()):
        blocks = ((2, width, width), bf16)
        call = launch(
            contract_blocks,
            plan,
            side,
            plain,
            dict(),
            arrays,
            dict(sent_o=blocks, kept_o=blocks),
            dict(**scratch, blocks=((4, width, width), bf16)),
            36,
            8,
            after=after,
        )
        return call.sent_o, call.kept_o

    def first_sums(halves, section=None):
        sent, kept = halves
        got = send(sent, to_core, section)

        def block(side):
            return sum(
                lax.dynamic_index_in_dim(part, side, 0, keepdims=False).astype(f32)
                for part in (kept, got)
            )

        return block(1 - x).astype(bf16), block(x)

    def middle_sums(sums, section=None):
        away, total = sums
        return (total + send(away, to_x, section).astype(f32)).astype(bf16)

    def last_sums(totals, *later):
        rows = width // group
        shares = jnp.concatenate([total.reshape(group, rows, width) for total in totals], axis=1)

        def share(step):
            return lax.dynamic_index_in_dim(shares, lax.rem(z + step, group), 0, keepdims=False)

        parts = [share(0)]
        for step in range(1, group):
            parts.append(send(share(step), along_z(step)))
        if later:
            parts = [fence(part, *later) for part in parts]
        return sum(part.astype(f32) for part in parts).astype(bf16)

    def along_z(step):
        return lambda t, i, k, c: (t, i, (k + step) % group, c)

    def gather_z(share):
        return [share] + [send(share, along_z(step)) for step in range(1, group)]

    def gain_block(rows):
        filled = jnp.concatenate([jnp.stack(rows), jnp.zeros((16 - len(rows), width), f32)])
        return filled.astype(bf16)

    def spread(targets, own, own_x, outs, parts):
        return launch(
            spread_pieces,
            targets,
            None,
            plain,
            dict(),
            dict(own_h=own, own_x_h=own_x, other_h=exchange(own), other_x_h=exchange(own_x)),
            outs,
            dict(
                pieces=((4,) + own.shape, bf16),
                wide=((4 * group * parts, width // group, width), f32),
            ),
            8 + 4 * group * parts,
            5,
        )

    tokens, all_tokens = micros * length, 2 * micros * length
    turn, turn_all = ((width, tokens), bf16), ((width, all_tokens), bf16)
    narrow, narrow_all = ((tokens, width), bf16), ((all_tokens, width), bf16)
    pair_all = ((all_tokens, 2 * width), bf16)
    deep = ((tokens, hidden), bf16)

    def part_of(buffer, *sources):
        return lambda column: (buffer, sources, column)

    def key_rows(buffer, sources):
        first, second = pl.ds(0, length), pl.ds(length, length)
        return part_of(buffer, *[source.at[rows] for rows in (first, second) for source in sources])

    def cross_plan(r):
        rows = pl.ds(0, length)
        low_part = part_of(r.low, r.low0_h, r.low1_h)
        att_part = part_of(r.att, r.att0_h, r.att1_h)
        dq_part = part_of(r.dq, r.dq0_h, r.dq1_h)
        branch_part = part_of(r.branch, r.branch0_h, r.branch1_h)
        sources = (r.mem0_h, r.mem1_h, r.mem2_h, r.mem3_h)
        mem_part = part_of(r.mem, *[source.at[rows] for source in sources])
        pair_part = key_rows(r.pair, (r.pair0_h, r.pair1_h))
        return [
            (r.turn, low_part(0), dq_part(0)),
            (r.turn_att, att_part(0), branch_part(0)),
            (r.turn_all, mem_part(0), pair_part(0)),
            (r.turn_all, mem_part(0), pair_part(1)),
        ]

    def rising_plan(r):
        low_part = part_of(r.low, r.low0_h, r.low1_h)
        up_part = part_of(r.up, r.up0_h, r.up1_h)
        return [(r.turn, low_part(0), up_part(block)) for block in range(4)]

    def falling_plan(r):
        act_part = part_of(r.act, r.act0_h, r.act1_h)
        down_part = part_of(r.down, r.down0_h, r.down1_h)
        return [(r.turn, act_part(block), down_part(0)) for block in range(4)]

    def self_plan(r):
        rows = pl.ds(0, length)
        sources = (r.x0_h, r.x1_h, r.x2_h, r.x3_h)
        x_part = part_of(r.x, *[source.at[rows] for source in sources])
        dq_part = part_of(r.dq, r.dq0_h, r.dq1_h)
        pair_part = key_rows(r.pair, (r.pair0_h, r.pair1_h))
        att_part = part_of(r.att, r.att0_h, r.att1_h)
        branch_part = part_of(r.branch, r.branch0_h, r.branch1_h)
        return [
            (r.turn_all, x_part(0), dq_part(0)),
            (r.turn_all, x_part(0), pair_part(0)),
            (r.turn_all, x_part(0), pair_part(1)),
            (r.turn, att_part(0), branch_part(0)),
        ]

    last = micros - 1
    feeds, ends = [None] * micros, [None] * micros
    cross_halves = weight_grads(
        cross_plan,
        1,
        dict(
            low0_h=forward[0].first_low_o,
            low1_h=forward[1].first_low_o,
            dq0_h=cross[0].dq_low_o,
            dq1_h=cross[1].dq_low_o,
            att0_h=cross[0].att_o,
            att1_h=cross[1].att_o,
            branch0_h=cross[0].branch_o,
            branch1_h=cross[1].branch_o,
            mem0_h=memories[0],
            mem1_h=memories[1],
            mem2_h=memories_other[0],
            mem3_h=memories_other[1],
            pair0_h=cross[0].dkv_o,
            pair1_h=cross[1].dkv_o,
        ),
        dict(
            low=narrow,
            dq=narrow,
            att=narrow,
            branch=narrow,
            mem=narrow_all,
            pair=pair_all,
            turn=turn,
            turn_att=turn,
            turn_all=turn_all,
        ),
        (made[last],),
    )
    cross_sums = first_sums(cross_halves, 1)
    results = jnp.stack(
        [
            jnp.where(decoder, call.decoded_o, done.memory_o[:length])
            for call, done in zip(cross, forward)
        ]
    )
    results = send(results, to_row)
    latest = made[last]

    def part_sum(micro, *before):
        end = ends[micro]
        away = fence(end.part_other_o, *before)
        total = (end.part_own_o + exchange(away).astype(f32)).astype(bf16)
        return total, send(total, to_row)

    steps = []
    for micro in range(last):
        feeds[micro] = backward_feed(micro, (latest,))
        first = feeds[micro].grad_first_o
        ends[micro] = backward_self(micro, 0, first)
        ends[micro] = backward_self(micro, 1, first, vars(ends[micro]), (cross_sums[0], grads_memory[last]))
        cross_total = middle_sums(cross_sums, 1)
        steps.append(part_sum(micro, cross_total))
        latest = ends[micro].gain_early_o
    feeds[last] = backward_feed(last, (latest,))

    rising_halves = weight_grads(
        rising_plan,
        None,
        dict(
            low0_h=cross[0].ffn_low_o,
            low1_h=cross[1].ffn_low_o,
            up0_h=feeds[0].up_grad_o,
            up1_h=feeds[1].up_grad_o,
        ),
        dict(low=narrow, up=deep, turn=turn),
        (results,) + tuple(step[0] for step in steps),
    )
    rising_sums = first_sums(rising_halves)
    rising_total = middle_sums(rising_sums)
    falling_halves = weight_grads(
        falling_plan,
        None,
        dict(
            act0_h=cross[0].act_o,
            act1_h=cross[1].act_o,
            down0_h=feeds[0].down_grad_o,
            down1_h=feeds[1].down_grad_o,
        ),
        dict(act=deep, down=narrow, turn=turn),
        (rising_sums[0],),
    )
    falling_sent = fence(falling_halves[0], rising_total)
    falling_sums = first_sums((falling_sent, falling_halves[1]))
    falling_total = middle_sums(falling_sums)
    shares = []

    third = sum(call.gain_grads_o[1] for call in cross)

    def halfway(one):
        both = last_sums((rising_total, cross_total), one.gain_early_o)
        rows = width // group
        found = jnp.concatenate([both[rows:], gain_block([third])])
        shares.extend([both[:rows], found, send(found, to_encoder)])
        return (both, falling_total)

    ends[last] = backward_self(
        last,
        None,
        feeds[last].grad_first_o,
        None,
        (falling_sums[0],),
        halfway,
    )
    finished = ends[last].part_own_o
    falling_share = last_sums((falling_total,), ends[last].gain_early_o, finished)
    rising_share, found, arrived = shares
    cross_share = jnp.where(decoder, found, fence(arrived, finished))
    one_own = gather_z(jnp.concatenate([rising_share, falling_share, cross_share]))
    steps.append(part_sum(last, falling_share, arrived, steps[0][1]))

    self_halves = weight_grads(
        self_plan,
        None,
        dict(
            x0_h=own[0],
            x1_h=own[1],
            x2_h=other[0],
            x3_h=other[1],
            dq0_h=ends[0].dq_low_o,
            dq1_h=ends[1].dq_low_o,
            pair0_h=ends[0].dkv_o,
            pair1_h=ends[1].dkv_o,
            att0_h=forward[0].att_o,
            att1_h=forward[1].att_o,
            branch0_h=ends[0].branch_o,
            branch1_h=ends[1].branch_o,
        ),
        dict(
            x=narrow_all,
            dq=narrow,
            pair=pair_all,
            att=narrow,
            branch=narrow,
            turn=turn,
            turn_all=turn_all,
        ),
        (steps[last][0],),
    )
    away, total = first_sums(
        (fence(self_halves[0], one_own[1], one_own[-1], steps[last][1]), self_halves[1])
    )
    self_total = middle_sums((away, total))
    one_own = jnp.stack([one_own[0]] + [fence(part, self_total) for part in one_own[1:]])
    self_share = last_sums((self_total,))
    one_own_x = send(fence(one_own, self_total), to_x)

    early = sum(end.gain_early_o[0] for end in ends)
    late = jnp.where(
        decoder,
        sum(call.gain_grads_o[0] for call in cross),
        sum(call.gain_late_o[0] for call in feeds),
    )
    two_own = jnp.stack(
        gather_z(jnp.concatenate([self_share, gain_block([early, late])]))
    )
    two_own_x = send(fence(two_own, one_own_x), to_x)

    def columns(block):
        return pl.ds(block * width, width)

    def one_targets(r, block, row, rows):
        lines = pl.ds(row, rows)
        feed = [r.up_o.at[lines, columns(block)], r.down_o.at[pl.ds(block * width + row, rows)]]
        if block >= 2:
            return feed + [r.pair_o.at[lines, columns(block - 2)]]
        return feed + [(r.out_o if block else r.query_o).at[lines]]

    def two_targets(r, block, row, rows):
        lines = pl.ds(row, rows)
        return [r.out_o.at[lines] if block == 3 else r.mixed_o.at[lines, columns(block)]]

    square_out = ((width, width), f32)
    one_own_x = fence(one_own_x, two_own)
    one_grads = spread(
        one_targets,
        one_own,
        one_own_x,
        dict(
            up_o=((width, hidden), f32),
            query_o=square_out,
            pair_o=((width, 2 * width), f32),
            down_o=((hidden, width), f32),
            out_o=square_out,
            gains_o=((1, width), f32),
        ),
        3,
    )
    two_own_x = fence(two_own_x, one_grads.gains_o)
    two_grads = spread(
        two_targets,
        two_own,
        two_own_x,
        dict(
            mixed_o=((width, 3 * width), f32),
            out_o=square_out,
            gains_o=((2, width), f32),
        ),
        1,
    )

    grad_input = jnp.stack([step[1] for step in steps])
    return (
        results[None, :, None],
        grad_input.astype(f32)[None, :, None],
        two_grads.mixed_o[None],
        two_grads.out_o[None],
        one_grads.up_o[None],
        one_grads.down_o[None],
        two_grads.gains_o[None],
        one_grads.query_o,
        one_grads.pair_o,
        one_grads.out_o,
        one_grads.gains_o[0],
    )


def shards(*arrays):
    layer_input = arrays[0]
    micros, rows, length = layer_input.shape[1:4]
    simple = (
        lax.axis_size("section") == 2
        and lax.axis_size("seq") == 2
        and lax.axis_size("dp") in (4, 8, 16)
        and (micros, rows) == (2, 1)
        and length == layer_input.shape[-1] == CHUNK
        and arrays[4].shape[-1] == 4 * CHUNK
    )
    return split_rows(*arrays) if simple else any_rows(*arrays)


def solution(mesh):
    in_specs = (
        P("section", None, "dp", "seq", None),
        P("section", None, "dp", "seq"),
        P("section", None, None),
        P("section", None, None),
        P("section", None, None),
        P("section", None, None),
        P("section", None, None),
        P(),
        P(),
        P(),
        P(),
        P(None, "dp", "seq", None),
    )
    out_specs = (
        P("section", None, "dp", "seq", None),
        P("section", None, "dp", "seq", None),
        P("section", None, None),
        P("section", None, None),
        P("section", None, None),
        P("section", None, None),
        P("section", None, None),
        P(),
        P(),
        P(),
        P(),
    )
    return jax.shard_map(shards, mesh=mesh, in_specs=in_specs, out_specs=out_specs, check_vma=False)
```

```python
import types

import jax
import jax.numpy as jnp
from jax import lax
from jax.experimental import pallas as pl
from jax.experimental.pallas import tpu as pltpu
from jax.sharding import PartitionSpec as P

HEADS = 8
TILE = 256
LANES = 128
CHUNK = 512

f32 = jnp.float32
bf16 = jnp.bfloat16
negative_big = -1e30
epsilon = 1e-05


def dot(left, right):
    return lax.dot_general(left, right, (((1,), (0,)), ((), ())), preferred_element_type=f32)


def dot_nt(left, right):
    return lax.dot_general(left, right, (((1,), (1,)), ((), ())), preferred_element_type=f32)


def dot_tn(left, right):
    return lax.dot_general(left, right, (((0,), (0,)), ((), ())), preferred_element_type=f32)


def standardize(values):
    center = values - jnp.mean(values, axis=-1, keepdims=True)
    inverse = lax.rsqrt(jnp.mean(center * center, axis=-1, keepdims=True) + epsilon)
    return center * inverse, inverse


def standardize_back(grad_out, standard, gain_row, inverse):
    scaled = grad_out * gain_row
    grad_in = inverse * (
        scaled
        - jnp.mean(scaled, axis=-1, keepdims=True)
        - standard * jnp.mean(scaled * standard, axis=-1, keepdims=True)
    )
    return grad_in, jnp.sum(grad_out * standard, axis=0, keepdims=True)


class Copies:
    def __init__(self, sems):
        self.sems = sems
        self.used = 0

    def start(self, source, target):
        copy = pltpu.make_async_copy(source, target, self.sems.at[self.used])
        self.used += 1
        copy.start()
        return copy


def wait_all(copies):
    for copy in copies:
        copy.wait()


def spread_pairs(target, source, factor, pairs):
    tiles = target.shape[1]
    half = lax.broadcasted_iota(jnp.int32, (TILE, LANES), 1) < LANES // 2
    first = jnp.where(half, factor, 0.0).astype(bf16)
    second = jnp.where(half, 0.0, factor).astype(bf16)
    for tile in range(tiles):
        for pair in pairs:
            block = source[tile * TILE : (tile + 1) * TILE, pair * LANES : (pair + 1) * LANES]
            target[pair, tile, :TILE, :] = block * first
            target[pair, tile, TILE:, :] = block * second


def turn_tiles(target, source, column, pairs):
    low, high = pairs[0] * LANES, (pairs[-1] + 1) * LANES
    for tile in range(target.shape[0]):
        block = source[tile * TILE : (tile + 1) * TILE, column + low : column + high]
        target[tile, low:high, :] = jnp.transpose(block)


def place_documents(r, copies):
    wait_all(copies)
    q_tiles = r.qd.shape[0]
    for part in range(3):
        row = r.docs[part].astype(f32)[0:1, :]
        for tile in range(q_tiles):
            piece = row[:, tile * TILE : (tile + 1) * TILE]
            slot = part * q_tiles + tile
            r.bounds[0, slot] = jnp.min(piece).astype(jnp.int32)
            r.bounds[1, slot] = jnp.max(piece).astype(jnp.int32)
            if part == 0:
                r.qd[tile] = jnp.broadcast_to(piece, (8, TILE))
        if part > 0:
            for start in range(0, row.shape[1], LANES):
                block = jnp.broadcast_to(row[:, start : start + LANES], (LANES, LANES))
                place = (part - 1) * row.shape[1] + start
                r.kdc[place : place + LANES, :] = jnp.transpose(block)


def load_documents(r, move, queries, own, other):
    rows = pl.ds(r.docs.shape[2], r.docs.shape[1])
    return [
        move.start(source.at[rows], r.docs.at[part])
        for part, source in enumerate((queries, own, other))
    ]


def tile_place(r, core, causal, q_tile, k_tile):
    q_tiles = r.qd.shape[0]
    length = q_tiles * TILE
    owner = jnp.where(k_tile < q_tiles, core, 1 - core)
    k_start = owner * length + lax.rem(k_tile, q_tiles) * TILE
    ahead = core * length + q_tile * TILE - k_start
    ahead = jnp.where(causal == 1, ahead, 2 * length * TILE)
    q_low, q_high = r.bounds[0, q_tile], r.bounds[1, q_tile]
    k_low, k_high = r.bounds[0, q_tiles + k_tile], r.bounds[1, q_tiles + k_tile]
    active = (q_low <= k_high) & (k_low <= q_high) & (ahead > -TILE)
    whole = (q_low == k_high) & (k_low == q_high) & (ahead >= TILE)
    return active, whole, ahead


def each_tile(place, body):
    active, whole, ahead = place
    pl.when(active & jnp.logical_not(whole))(lambda: body(ahead))
    pl.when(whole)(lambda: body(None))


def fill_bias(r, q_tile, k_tile, ahead):
    keys = r.kdc[pl.ds(pl.multiple_of(k_tile * TILE, TILE), TILE), :]
    shift = lax.broadcasted_iota(jnp.int32, (TILE, LANES), 0) - lax.broadcasted_iota(
        jnp.int32, (TILE, LANES), 1
    )
    queries = r.qd[q_tile]
    for start in range(0, TILE, LANES):
        same = keys == queries[0:1, start : start + LANES]
        allowed = same & (shift - start <= ahead)
        r.bias[:, start : start + LANES] = jnp.where(allowed, 0.0, negative_big)


def attention_forward(r, core, causal):
    pairs, q_tiles = r.qm.shape[:2]
    k_tiles = r.vt.shape[0]

    def one_query_tile(q_tile, carry):
        r.top[...] = jnp.full(r.top.shape, negative_big, f32)
        r.total[...] = jnp.zeros(r.total.shape, f32)
        r.turned[...] = jnp.zeros(r.turned.shape, f32)

        def one_key_tile(k_tile, inner):
            def one_tile(ahead):
                if ahead is not None:
                    fill_bias(r, q_tile, k_tile, ahead)
                rows = pl.ds(pl.multiple_of(k_tile * TILE, TILE), TILE)

                def raw(pair):
                    keys = r.kv[rows, pair * LANES : (pair + 1) * LANES]
                    return dot_nt(keys, r.qm[pair, q_tile])

                raw_next = raw(0)
                for pair in range(pairs):
                    scores = raw_next
                    if ahead is not None:
                        bias = r.bias[...]
                        scores = scores + jnp.concatenate([bias, bias], axis=1)
                    if pair + 1 < pairs:
                        raw_next = raw(pair + 1)
                    old_top = r.top[pair : pair + 1, :]
                    new_top = jnp.maximum(old_top, jnp.max(scores, axis=0, keepdims=True))
                    weights = jnp.exp(scores - new_top)
                    shrink = jnp.exp(old_top - new_top)
                    r.top[pair : pair + 1, :] = new_top
                    r.total[pair : pair + 1, :] = r.total[
                        pair : pair + 1, :
                    ] * shrink + jnp.sum(weights, axis=0, keepdims=True)
                    low = weights.astype(bf16)
                    for side in range(2):
                        span = slice(side * TILE, (side + 1) * TILE)
                        head = slice((2 * pair + side) * 64, (2 * pair + side + 1) * 64)
                        r.turned[head, :] = r.turned[head, :] * shrink[:, span] + dot(
                            r.vt[k_tile, head, :], low[:, span]
                        )

            each_tile(tile_place(r, core, causal, q_tile, k_tile), one_tile)
            return inner

        lax.fori_loop(0, k_tiles, one_key_tile, 0)
        for pair in range(pairs):
            total = r.total[pair : pair + 1, :]
            r.lse[q_tile, pair : pair + 1, :] = r.top[pair : pair + 1, :] + jnp.log(total)
            share = 1.0 / total
            for side in range(2):
                span = slice(side * TILE, (side + 1) * TILE)
                head = slice((2 * pair + side) * 64, (2 * pair + side + 1) * 64)
                r.turned[head, :] = r.turned[head, :] * share[:, span]
        rows = pl.ds(pl.multiple_of(q_tile * TILE, TILE), TILE)
        r.att[rows, :] = jnp.transpose(r.turned[...]).astype(bf16)
        return carry

    lax.fori_loop(0, q_tiles, one_query_tile, 0)


def row_products(r, grad_att, pairs):
    low, high = pairs[0] * LANES, (pairs[-1] + 1) * LANES
    for tile in range(r.qm.shape[1]):
        rows = slice(tile * TILE, (tile + 1) * TILE)
        product = jnp.transpose(
            grad_att[rows, low:high].astype(f32) * r.att[rows, low:high].astype(f32)
        )
        for pair in pairs:
            for side in range(2):
                head = (2 * pair + side) * 64 - low
                r.delta[tile, pair : pair + 1, side * TILE : (side + 1) * TILE] = jnp.sum(
                    product[head : head + 64, :], axis=0, keepdims=True
                )


def attention_backward(r, core, causal, pairs):
    q_tiles, k_tiles = r.qm.shape[1], r.kt.shape[0]
    width = r.kt.shape[1]
    low, high = pairs[0] * LANES, (pairs[-1] + 1) * LANES
    for start in (0, width):
        r.dkv[:, start + low : start + high] = jnp.zeros((r.dkv.shape[0], high - low), f32)

    def one_query_tile(q_tile, carry):
        r.turned[low:high, :] = jnp.zeros((high - low, TILE), f32)

        def one_key_tile(k_tile, inner):
            def one_tile(ahead):
                if ahead is not None:
                    fill_bias(r, q_tile, k_tile, ahead)
                rows = pl.ds(pl.multiple_of(k_tile * TILE, TILE), TILE)

                def raw(pair):
                    lanes = slice(pair * LANES, (pair + 1) * LANES)
                    lanes_v = slice(width + pair * LANES, width + (pair + 1) * LANES)
                    return (
                        dot_nt(r.kv[rows, lanes], r.qm[pair, q_tile]),
                        dot_nt(r.kv[rows, lanes_v], r.gm[pair, q_tile]),
                    )

                raw_next = raw(pairs[0])
                for pair in pairs:
                    scores, grad_probs = raw_next
                    if ahead is not None:
                        bias = r.bias[...]
                        scores = scores + jnp.concatenate([bias, bias], axis=1)
                    if pair < pairs[-1]:
                        raw_next = raw(pair + 1)
                    probs = jnp.exp(scores - r.lse[q_tile, pair : pair + 1, :])
                    grad_scores = probs * (grad_probs - r.delta[q_tile, pair : pair + 1, :])
                    probs_low = probs.astype(bf16)
                    grad_low = grad_scores.astype(bf16)
                    lanes = slice(pair * LANES, (pair + 1) * LANES)
                    lanes_v = slice(width + pair * LANES, width + (pair + 1) * LANES)
                    r.dkv[rows, lanes] += dot(grad_low, r.qm[pair, q_tile])
                    r.dkv[rows, lanes_v] += dot(probs_low, r.gm[pair, q_tile])
                    for side in range(2):
                        span = slice(side * TILE, (side + 1) * TILE)
                        head = slice((2 * pair + side) * 64, (2 * pair + side + 1) * 64)
                        r.turned[head, :] += dot(r.kt[k_tile, head, :], grad_low[:, span])

            each_tile(tile_place(r, core, causal, q_tile, k_tile), one_tile)
            return inner

        lax.fori_loop(0, k_tiles, one_key_tile, 0)
        rows = pl.ds(pl.multiple_of(q_tile * TILE, TILE), TILE)
        r.dq[rows, low:high] = jnp.transpose(r.turned[low:high, :]) * (64**-0.5)
        return carry

    lax.fori_loop(0, q_tiles, one_query_tile, 0)


def feed_forward(r, low):
    chunks = [slice(at, at + CHUNK) for at in range(0, r.w_in.shape[1], CHUNK)]
    upward_next = dot(low[...], r.w_in[:, chunks[0]])
    for place, span in enumerate(chunks):
        upward = upward_next
        if place + 1 < len(chunks):
            upward_next = dot(low[...], r.w_in[:, chunks[place + 1]])
        gate = jax.nn.sigmoid(upward)
        active = (upward * gate).astype(bf16)
        r.act[:, span] = active
        r.slope[:, span] = (gate + upward * gate * (1.0 - gate)).astype(r.slope.dtype)
        part = dot(active, r.w_down[span, :])
        if place:
            r.sum[...] += part
        else:
            r.sum[...] = part


def feed_backward(r):
    chunks = [slice(at, at + CHUNK) for at in range(0, r.w_in.shape[1], CHUNK)]
    active_next = dot_nt(r.down_grad[...], r.w_down[chunks[0], :])
    for place, span in enumerate(chunks):
        grad_active = active_next.astype(bf16)
        if place + 1 < len(chunks):
            active_next = dot_nt(r.down_grad[...], r.w_down[chunks[place + 1], :])
        grad_up = (grad_active.astype(f32) * r.slope[:, span].astype(f32)).astype(bf16)
        r.up_grad[:, span] = grad_up
        part = dot_nt(grad_up, r.w_in[:, span])
        if place:
            r.sum[...] += part
        else:
            r.sum[...] = part


def self_forward(r):
    length, width = r.unit1.shape
    decoder, core = r.meta[0], r.meta[1]
    move = Copies(r.sems)
    whole = pl.ds(0, length)
    documents = load_documents(r, move, r.x_own_h, r.x_own_h, r.x_other_h)
    early = [
        move.start(r.x_own_h.at[whole], r.x.at[whole]),
        move.start(r.x_other_h.at[whole], r.x.at[pl.ds(length, length)]),
        move.start(r.w_mixed_h, r.w_mixed),
    ]
    later = [
        move.start(r.w_out_h, r.w_out),
        move.start(r.w_in_h, r.w_in),
        move.start(r.w_down_h, r.w_down),
    ]
    place_documents(r, documents)
    wait_all(early)
    r.q[...] = dot(r.x[:length, :], r.w_mixed[:, :width]).astype(bf16)
    r.kv[...] = dot(r.x[...], r.w_mixed[:, width:]).astype(bf16)
    outs = [move.start(r.q, r.q_o), move.start(r.kv, r.kv_o)]
    pairs = range(width // LANES)
    spread_pairs(r.qm, r.q, 64**-0.5, pairs)
    turn_tiles(r.vt, r.kv, width, pairs)
    attention_forward(r, core, decoder)
    wait_all(later)
    outs += [move.start(r.att, r.att_o), move.start(r.lse, r.lse_o)]
    unit, inverse = standardize(r.x[:length, :].astype(f32) + dot(r.att[...], r.w_out[...]))
    r.unit1[...] = unit
    r.inv1[...] = jnp.broadcast_to(inverse, r.inv1.shape)
    r.first_low[...] = (unit * r.gains[0:1, :]).astype(bf16)
    outs += [
        move.start(r.unit1, r.unit1_o),
        move.start(r.inv1, r.inv1_o),
        move.start(r.first_low, r.first_low_o),
    ]

    @pl.when(decoder == 0)
    def _():
        feed_forward(r, r.first_low)
        late = [
            move.start(r.first_low, r.ffn_low_o),
            move.start(r.act, r.act_o),
            move.start(r.slope, r.slope_o),
        ]
        unit2, inverse2 = standardize(r.unit1[...] * r.gains[0:1, :] + r.sum[...])
        r.memory[:length, :] = (unit2 * r.gains[1:2, :]).astype(bf16)
        r.memory[length:, :] = r.docs[0]
        late += [move.start(r.memory, r.memory_o)]
        r.unit2[...] = unit2
        r.inv2[...] = jnp.broadcast_to(inverse2, r.inv2.shape)
        late += [move.start(r.unit2, r.unit2_o), move.start(r.inv2, r.inv2_o)]
        wait_all(late)

    wait_all(outs)


def cross_both_ways(r):
    length, width = r.unit1_h.shape
    core = r.meta[1]
    move = Copies(r.sems)
    whole = pl.ds(0, length)
    documents = load_documents(r, move, r.x_own_h, r.memory_own_h, r.memory_other_h)
    moves = [
        move.start(r.memory_own_h.at[whole], r.x.at[whole]),
        move.start(r.memory_other_h.at[whole], r.x.at[pl.ds(length, length)]),
        move.start(r.w_pair_h, r.w_pair),
        move.start(r.first_low_h, r.first_low),
        move.start(r.w_query_h, r.w_query),
    ]
    later = [
        move.start(r.unit1_h, r.unit1),
        move.start(r.w_cross_h, r.w_cross),
        move.start(r.w_in_h, r.w_in),
        move.start(r.w_down_h, r.w_down),
        move.start(r.cot_h.at[r.micro], r.cot),
    ]
    place_documents(r, documents)
    wait_all(moves)
    r.kv[...] = dot(r.x[...], r.w_pair[...]).astype(bf16)
    r.q[...] = dot(r.first_low[...], r.w_query[...]).astype(bf16)
    pairs = range(width // LANES)
    spread_pairs(r.qm, r.q, 64**-0.5, pairs)
    turn_tiles(r.vt, r.kv, width, pairs)
    turn_tiles(r.kt, r.kv, 0, pairs)
    attention_forward(r, core, 0)
    outs = [move.start(r.att, r.att_o)]
    wait_all(later)
    first = r.unit1[...] * r.gains[0:1, :]
    unit, inverse = standardize(first + dot(r.att[...], r.w_cross[...]))
    r.unit2[...] = unit
    r.inv2[...] = jnp.broadcast_to(inverse, r.inv2.shape)
    r.second_low[...] = (unit * r.cross_gain[...]).astype(bf16)
    outs += [move.start(r.second_low, r.ffn_low_o)]
    feed_forward(r, r.second_low)
    outs += [move.start(r.act, r.act_o)]
    unit3, inverse3 = standardize(r.unit2[...] * r.cross_gain[...] + r.sum[...])
    r.decoded[...] = (unit3 * r.gains[1:2, :]).astype(bf16)
    outs += [move.start(r.decoded, r.decoded_o)]
    grad_third, gain_late = standardize_back(
        r.cot[...].astype(f32), unit3, r.gains[1:2, :], inverse3
    )
    r.keep[...] = grad_third
    r.down_grad[...] = grad_third.astype(bf16)
    outs += [move.start(r.down_grad, r.down_grad_o)]
    feed_backward(r)
    outs += [move.start(r.up_grad, r.up_grad_o)]
    grad_sum, gain_cross = standardize_back(
        r.keep[...] + r.sum[...], r.unit2[...], r.cross_gain[...], r.inv2[:, 0:1]
    )
    r.gain_grads[...] = jnp.zeros(r.gain_grads.shape, f32)
    r.gain_grads[0:1, :] = gain_late
    r.gain_grads[1:2, :] = gain_cross
    r.keep[...] = grad_sum
    r.branch[...] = grad_sum.astype(bf16)
    outs += [move.start(r.gain_grads, r.gain_grads_o), move.start(r.branch, r.branch_o)]
    r.q[...] = dot_nt(r.branch[...], r.w_cross[...]).astype(bf16)
    spread_pairs(r.gm, r.q, 1.0, pairs)
    row_products(r, r.q, pairs)
    attention_backward(r, core, 0, pairs)
    r.dq_low[...] = r.dq[...].astype(bf16)
    r.keep[...] += dot_nt(r.dq_low[...], r.w_query[...])
    outs += [move.start(r.dq_low, r.dq_low_o), move.start(r.keep, r.grad_first_o)]
    r.dkv_low[...] = r.dkv[...].astype(bf16)
    outs += [move.start(r.dkv_low, r.dkv_o)]
    part = dot_nt(r.dkv_low[...], r.w_pair[...])
    r.part_other[...] = part[length:, :].astype(bf16)
    r.part_own[...] = part[:length, :]
    outs += [move.start(r.part_other, r.part_other_o), move.start(r.part_own, r.part_own_o)]
    wait_all(outs)


def feed_backward_alone(r):
    move = Copies(r.sems)
    early = [
        move.start(r.grad_memory_h, r.cot),
        move.start(r.unit2_h, r.unit2),
        move.start(r.inv2_h, r.inv2),
    ]
    later = [
        move.start(r.w_down_h, r.w_down),
        move.start(r.slope_h, r.slope),
        move.start(r.w_in_h, r.w_in),
    ]
    wait_all(early)
    grad_third, gain_late = standardize_back(
        r.cot[...].astype(f32), r.unit2[...], r.gains[1:2, :], r.inv2[:, 0:1]
    )
    r.gain_grads[...] = jnp.broadcast_to(gain_late, r.gain_grads.shape)
    r.keep[...] = grad_third
    r.down_grad[...] = grad_third.astype(bf16)
    outs = [move.start(r.down_grad, r.down_grad_o), move.start(r.gain_grads, r.gain_late_o)]
    wait_all(later)
    feed_backward(r)
    outs += [move.start(r.up_grad, r.up_grad_o)]
    r.keep[...] += r.sum[...]
    outs += [move.start(r.keep, r.grad_first_o)]
    wait_all(outs)


def self_backward(r, plan):
    r.micro, first, last = plan
    length, width = r.att_h.shape
    decoder, core = r.meta[0], r.meta[1]
    pairs = range(first, last)
    low, high = first * LANES, last * LANES
    move = Copies(r.sems)
    later = [
        move.start(r.q_h, r.q),
        move.start(r.kv_h, r.kv),
        move.start(r.att_h, r.att),
        move.start(r.lse_h, r.lse),
    ]
    if first == 0:
        early = [
            move.start(r.grad_first_h, r.keep),
            move.start(r.unit1_h, r.unit1),
            move.start(r.inv1_h, r.inv1),
            move.start(r.w_out_h, r.w_out),
        ]
    else:
        early = [move.start(r.grad_att_h, r.grad_att)]
    outs = []
    place_documents(r, load_documents(r, move, r.x_own_h, r.x_own_h, r.x_other_h))
    wait_all(early)
    if first == 0:
        grad_sum, gain_early = standardize_back(
            r.keep[...], r.unit1[...], r.gains[0:1, :], r.inv1[:, 0:1]
        )
        r.gain_grads[...] = jnp.broadcast_to(gain_early, r.gain_grads.shape)
        r.keep[...] = grad_sum
        r.branch[...] = grad_sum.astype(bf16)
        r.grad_att[...] = dot_nt(r.branch[...], r.w_out[...]).astype(bf16)
        outs += [move.start(r.gain_grads, r.gain_early_o), move.start(r.branch, r.branch_o)]
        if last < width // LANES:
            outs += [move.start(r.keep, r.grad_sum_o), move.start(r.grad_att, r.grad_att_o)]
    wait_all(later)
    if last == width // LANES:
        ends = [move.start(r.w_mixed_h, r.w_mixed)]
        if first > 0:
            ends += [
                move.start(r.grad_sum_h, r.keep),
                move.start(r.dq_h.at[:, pl.ds(0, low)], r.dq_low.at[:, pl.ds(0, low)]),
                move.start(r.dkv_h.at[:, pl.ds(0, low)], r.dkv_low.at[:, pl.ds(0, low)]),
                move.start(
                    r.dkv_h.at[:, pl.ds(width, low)], r.dkv_low.at[:, pl.ds(width, low)]
                ),
            ]
    spread_pairs(r.qm, r.q, 64**-0.5, pairs)
    turn_tiles(r.kt, r.kv, 0, pairs)
    spread_pairs(r.gm, r.grad_att, 1.0, pairs)
    row_products(r, r.grad_att, pairs)
    attention_backward(r, core, decoder, pairs)
    r.dq_low[:, low:high] = r.dq[:, low:high].astype(bf16)
    for start in (0, width):
        span = slice(start + low, start + high)
        r.dkv_low[:, span] = r.dkv[:, span].astype(bf16)
    if last == width // LANES:
        wait_all(ends)
        outs += [move.start(r.dq_low, r.dq_low_o), move.start(r.dkv_low, r.dkv_o)]
        r.keep[...] += dot_nt(r.dq_low[...], r.w_mixed[:, :width])
        part = dot_nt(r.dkv_low[...], r.w_mixed[:, width:])
        r.part_other[...] = part[length:, :].astype(bf16)
        r.keep[...] += part[:length, :]
        outs += [move.start(r.part_other, r.part_other_o), move.start(r.keep, r.part_own_o)]
    else:
        outs.append(move.start(r.dq_low.at[:, pl.ds(low, high - low)], r.dq_low_o.at[:, pl.ds(low, high - low)]))
        for start in (0, width):
            span = pl.ds(start + low, high - low)
            outs.append(move.start(r.dkv_low.at[:, span], r.dkv_o.at[:, span]))
    wait_all(outs)


def contract_blocks(r, plan):
    for core in range(2):

        @pl.when(r.meta[1] == core)
        def _(core=core):
            targets = [None] * 4
            for half in range(2):
                target = r.kept_o if half == core else r.sent_o
                targets[2 * half], targets[2 * half + 1] = target.at[0], target.at[1]
            order = (0, 1, 2, 3) if core else (2, 3, 0, 1)
            contract_in_order(r, plan(r), order, targets, Copies(r.sems))


def contract_in_order(r, blocks, order, targets, move):
    loads = dict()
    for slot in order:
        for buffer, sources, at in blocks[slot][1:]:
            if (id(buffer), at) not in loads:
                span = pl.ds(at * CHUNK, CHUNK)
                row = 0
                copies = []
                for source in sources:
                    rows = pl.ds(row, source.shape[0])
                    copies.append(move.start(source.at[:, span], buffer.at[rows, span]))
                    row += source.shape[0]
                loads[id(buffer), at] = copies
    outs = []
    held = dict()
    for slot in order:
        turn, (left, _, left_at), (right, _, right_at) = blocks[slot]
        wait_all(loads.pop((id(left), left_at), ()))
        wait_all(loads.pop((id(right), right_at), ()))
        if held.get(id(turn)) != left_at:
            for row in range(0, left.shape[0], CHUNK):
                block = left[row : row + CHUNK, left_at * CHUNK : (left_at + 1) * CHUNK]
                turn[:, row : row + CHUNK] = jnp.transpose(block)
            held[id(turn)] = left_at
        block = right[:, right_at * CHUNK : (right_at + 1) * CHUNK]
        r.blocks[slot] = dot(turn[:, : right.shape[0]], block).astype(bf16)
        outs.append(move.start(r.blocks.at[slot], targets[slot]))
    wait_all(outs)


def spread_pieces(r, targets):
    z = r.meta[3]
    group, height = r.own_h.shape[:2]
    rows = r.own_h.shape[2] // group
    for core in range(2):
        for x in range(2):

            @pl.when((r.meta[1] == core) & (r.meta[2] == x))
            def _(core=core, x=x):
                move = Copies(r.sems)
                parts = [
                    (r.own_h, core, x),
                    (r.own_x_h, core, 1 - x),
                    (r.other_h, 1 - core, x),
                    (r.other_x_h, 1 - core, 1 - x),
                ]
                loads = [
                    move.start(source, r.pieces.at[place])
                    for place, (source, _, _) in enumerate(parts)
                ]
                outs = []
                slot = 0
                gains = None
                for place, (_, half, side) in enumerate(parts):
                    loads[place].wait()
                    for step in range(group):
                        row = pl.multiple_of(lax.rem(z + (group - step), group) * rows, rows)
                        start = 0
                        for target in targets(r, 2 * half + side, row, rows):
                            r.wide[slot] = r.pieces[place, step, start : start + rows].astype(f32)
                            outs.append(move.start(r.wide.at[slot], target))
                            slot += 1
                            start += rows
                        if start < height:
                            extra = r.pieces[place, step, start:height].astype(f32)
                            gains = extra if gains is None else gains + extra
                r.gains_o[...] = gains[: r.gains_o.shape[0], :]
                wait_all(outs)


def launch(kernel, plan, side, scalars, small, large, outs, scratch, copies, work, previous=None, after=()):
    names = list(scalars) + list(small) + list(large)
    arrays = list(scalars.values()) + list(small.values()) + list(large.values())
    specs = (
        [pl.BlockSpec(memory_space=pltpu.SMEM)] * len(scalars)
        + [pl.BlockSpec(memory_space=pltpu.VMEM)] * len(small)
        + [pl.BlockSpec(memory_space=pl.ANY)] * len(large)
    )
    aliases = dict()
    for position, name in enumerate(outs):
        if previous and name in previous:
            aliases[len(arrays)] = position
            names.append("previous_" + name)
            arrays.append(previous[name])
            specs.append(pl.BlockSpec(memory_space=pl.ANY))
    for array in after:
        names.append("")
        arrays.append(array)
        specs.append(pl.BlockSpec(memory_space=pl.ANY))
    names += list(outs) + list(scratch) + ["sems"]

    def body(*refs):
        r = types.SimpleNamespace(**dict(zip(names, refs)))

        def run():
            if isinstance(plan, int):
                r.micro = plan
                kernel(r)
            else:
                kernel(r, plan)

        if side is None:
            run()
        else:
            pl.when(r.meta[0] == side)(run)

    results = pl.pallas_call(
        body,
        out_shape=[jax.ShapeDtypeStruct(*shape) for shape in outs.values()],
        in_specs=specs,
        out_specs=[
            pl.BlockSpec(memory_space=pltpu.VMEM if shape[0][0] < 8 else pl.ANY)
            for shape in outs.values()
        ],
        scratch_shapes=[
            pltpu.SMEM(*shape) if shape[1] == jnp.int32 else pltpu.VMEM(*shape)
            for shape in scratch.values()
        ]
        + [pltpu.SemaphoreType.DMA((copies,))],
        input_output_aliases=aliases,
        compiler_params=pltpu.CompilerParams(vmem_limit_bytes=58 * 1024 * 1024),
        cost_estimate=pl.CostEstimate(
            flops=work * 10**9, bytes_accessed=1 << 20, transcendentals=0
        ),
    )(*arrays)
    return types.SimpleNamespace(**dict(zip(outs, results)))


def attention_scratch(length, width):
    pairs, q_tiles, k_tiles = width // LANES, length // TILE, 2 * length // TILE
    return dict(
        q=((length, width), bf16),
        kv=((2 * length, 2 * width), bf16),
        qm=((pairs, q_tiles, 2 * TILE, LANES), bf16),
        kdc=((2 * length, LANES), f32),
        docs=((3, 16, width), bf16),
        qd=((length // TILE, 8, TILE), f32),
        bounds=((2, 3 * length // TILE), jnp.int32),
        bias=((TILE, TILE), f32),
        lse=((q_tiles, 8, 2 * TILE), f32),
        att=((length, width), bf16),
        turned=((width, TILE), f32),
    )


def forward_scratch(length, width):
    k_tiles = 2 * length // TILE
    return dict(
        vt=((k_tiles, width, TILE), bf16),
        top=((8, 2 * TILE), f32),
        total=((8, 2 * TILE), f32),
    )


def backward_scratch(length, width):
    pairs, q_tiles, k_tiles = width // LANES, length // TILE, 2 * length // TILE
    return dict(
        kt=((k_tiles, width, TILE), bf16),
        gm=((pairs, q_tiles, 2 * TILE, LANES), bf16),
        delta=((q_tiles, 8, 2 * TILE), f32),
        dkv=((2 * length, 2 * width), f32),
        dq=((length, width), f32),
        dkv_low=((2 * length, 2 * width), bf16),
        part_other=((length, width), bf16),
        dq_low=((length, width), bf16),
    )


def for_sending(shard):

    def short(part):
        return part.astype(jnp.bfloat16) if part.dtype == jnp.float32 else part

    return jax.tree.map(short, shard)


def from_behind(block, axis, distance):
    devices = range(lax.axis_size(axis))
    route = [(i - distance, i) for i in devices if i - distance in devices]
    return lax.ppermute(block, axis, route)


def from_root(shard, axis, root):
    mine = lax.axis_index(axis) == root
    return lax.psum(jnp.where(mine, shard, jnp.zeros_like(shard)), axis)


def matmul(left_side, right_side):
    return jnp.einsum("rsd,de->rse", left_side, right_side, preferred_element_type=jnp.float32)


def matmul_back(left_side, right_side):
    return jnp.einsum("rse,de->rsd", left_side, right_side, preferred_element_type=jnp.float32)


def contract(left_side, right_side):
    return jnp.einsum("rsd,rse->de", left_side, right_side, preferred_element_type=jnp.float32)


def normalize(values, gain_row):
    center = values - jnp.mean(values, axis=-1, keepdims=True)
    inverse = lax.rsqrt(jnp.mean(center * center, axis=-1, keepdims=True) + epsilon)
    standard = center * inverse
    return (standard * gain_row, standard, inverse)


def normalize_back(grad_out, standard, gain_row, inverse):
    scaled = grad_out * gain_row
    grad_in = inverse * (
        scaled
        - jnp.mean(scaled, axis=-1, keepdims=True)
        - standard * jnp.mean(scaled * standard, axis=-1, keepdims=True)
    )
    return (grad_in, jnp.sum(grad_out * standard, axis=(0, 1)))


def allowed_mask(query_docs, key_docs, query_place, key_place, causal):
    same_doc = query_docs[:, :, None] == key_docs[:, None, :]
    earlier = query_place[:, None] >= key_place[None, :]
    return (same_doc & (earlier | jnp.logical_not(causal)))[:, None]


def attend(queries, keys_local, values_local, query_docs, key_docs, causal, is_cross):
    rows_here, shard_len, model_width = queries.shape
    head_dim = model_width // HEADS
    score_scale = head_dim ** (-0.5)
    query_place = lax.axis_index("seq") * shard_len + jnp.arange(shard_len)
    query_heads = queries.reshape(rows_here, shard_len, HEADS, head_dim)

    def absorb(state_tuple, pieces):
        running_top, running_total, running_sum = state_tuple
        key_piece, value_piece, doc_piece = pieces
        piece_len = key_piece.shape[1]
        raw_scores = jnp.einsum(
            "rqhd,rkhd->rhqk",
            query_heads,
            key_piece.reshape(rows_here, piece_len, HEADS, head_dim),
            preferred_element_type=jnp.float32,
        )
        allowed = allowed_mask(query_docs, doc_piece, query_place, jnp.arange(piece_len), causal)
        scores = jnp.where(allowed, raw_scores * score_scale, negative_big)
        new_top = jnp.maximum(running_top, jnp.max(scores, axis=-1))
        weights = jnp.where(allowed, jnp.exp(scores - new_top[..., None]), 0.0)
        new_total = jnp.sum(weights, axis=-1)
        product = jnp.einsum(
            "rhqk,rkhd->rhqd",
            weights.astype(jnp.bfloat16),
            value_piece.reshape(rows_here, piece_len, HEADS, head_dim),
            preferred_element_type=jnp.float32,
        )
        return (new_top, new_total, product)

    init_state = (
        jnp.full((rows_here, HEADS, shard_len), negative_big, jnp.float32),
        jnp.zeros((rows_here, HEADS, shard_len), jnp.float32),
        jnp.zeros((rows_here, HEADS, shard_len, head_dim), jnp.float32),
    )
    if is_cross:
        final_top, final_total, final_sum = absorb(
            init_state,
            (
                lax.all_gather(keys_local, "seq", axis=1, tiled=True),
                lax.all_gather(values_local, "seq", axis=1, tiled=True),
                lax.all_gather(for_sending(key_docs), "seq", axis=1, tiled=True),
            ),
        )
    else:
        final_top, final_total, final_sum = absorb(
            init_state,
            (
                lax.all_gather(keys_local, "seq", axis=1, tiled=True),
                lax.all_gather(values_local, "seq", axis=1, tiled=True),
                lax.all_gather(key_docs, "seq", axis=1, tiled=True),
            ),
        )
    attended = (
        (final_sum / final_total[..., None])
        .transpose(0, 2, 1, 3)
        .reshape(rows_here, shard_len, model_width)
    )
    return (attended, final_top + jnp.log(final_total))


def attend_back(
    queries,
    keys_local,
    values_local,
    query_docs,
    key_docs,
    causal,
    log_total,
    grad_attended,
    is_cross,
):
    rows_here, shard_len, model_width = queries.shape
    head_dim = model_width // HEADS
    score_scale = head_dim ** (-0.5)
    query_place = lax.axis_index("seq") * shard_len + jnp.arange(shard_len)
    if is_cross:
        keys_full, values_full, docs_full = (
            lax.all_gather(keys_local, "seq", axis=1, tiled=True),
            lax.all_gather(values_local, "seq", axis=1, tiled=True),
            lax.all_gather(for_sending(key_docs), "seq", axis=1, tiled=True).astype(key_docs.dtype),
        )
    else:
        keys_full, values_full, docs_full = (
            lax.all_gather(keys_local, "seq", axis=1, tiled=True),
            lax.all_gather(values_local, "seq", axis=1, tiled=True),
            lax.all_gather(key_docs, "seq", axis=1, tiled=True),
        )
    full_len = keys_full.shape[1]
    query_heads = queries.reshape(rows_here, shard_len, HEADS, head_dim)
    key_heads = keys_full.reshape(rows_here, full_len, HEADS, head_dim)
    value_heads = values_full.reshape(rows_here, full_len, HEADS, head_dim)
    grad_heads = grad_attended.reshape(rows_here, shard_len, HEADS, head_dim)
    raw_scores = jnp.einsum(
        "rqhd,rkhd->rhqk", query_heads, key_heads, preferred_element_type=jnp.float32
    )
    allowed = allowed_mask(query_docs, docs_full, query_place, jnp.arange(full_len), causal)
    shifted = jnp.where(allowed, raw_scores * score_scale - log_total[..., None], negative_big)
    probs = jnp.where(allowed, jnp.exp(shifted), 0.0)
    grad_probs = jnp.einsum(
        "rqhd,rkhd->rhqk", grad_heads, value_heads, preferred_element_type=jnp.float32
    )
    delta = jnp.sum(probs * grad_probs, axis=-1)
    grad_scores = (probs * (grad_probs - delta[..., None]) * score_scale).astype(jnp.bfloat16)
    grad_queries = jnp.einsum(
        "rhqk,rkhd->rqhd", grad_scores, key_heads, preferred_element_type=jnp.float32
    ).reshape(rows_here, shard_len, model_width)
    probs_low = probs.astype(jnp.bfloat16)

    def key_terms(span):
        grad_keys = jnp.einsum(
            "rhqk,rqhd->krhd", grad_scores, query_heads, preferred_element_type=jnp.float32
        )
        grad_values = jnp.einsum(
            "rhqk,rqhd->krhd", probs_low, grad_heads, preferred_element_type=jnp.float32
        )
        return jnp.concatenate(
            [
                grad_keys.reshape(span, rows_here, model_width),
                grad_values.reshape(span, rows_here, model_width),
            ],
            axis=-1,
        )

    if is_cross:
        pair_terms = lax.psum_scatter(
            key_terms(shard_len * lax.axis_size("seq")).astype(jnp.bfloat16),
            "seq",
            scatter_dimension=0,
            tiled=True,
        ).astype(jnp.float32)
    else:
        pair_terms = lax.psum_scatter(
            key_terms(shard_len * lax.axis_size("seq")).astype(jnp.bfloat16),
            "seq",
            scatter_dimension=0,
            tiled=True,
        ).astype(jnp.float32)
    return (grad_queries, pair_terms.transpose(1, 0, 2))


def layer_forward(hidden_in, doc_own, memory, memory_docs, weights, is_decoder):
    (
        qkv_weight,
        out_weight,
        in_weight,
        down_weight,
        gains_pair,
        query_weight,
        pair_weight,
        cross_weight,
        cross_gains,
    ) = weights
    model_width = hidden_in.shape[-1]
    mixed = matmul(hidden_in, qkv_weight).astype(jnp.bfloat16)
    attended, self_lse = attend(
        mixed[..., :model_width],
        mixed[..., model_width : 2 * model_width],
        mixed[..., 2 * model_width :],
        doc_own,
        doc_own,
        is_decoder,
        False,
    )
    attended = attended.astype(jnp.bfloat16)
    first, first_unit, first_inv = normalize(
        hidden_in.astype(jnp.float32) + matmul(attended, out_weight), gains_pair[0]
    )
    first_low = first.astype(jnp.bfloat16)
    cross_queries = matmul(first_low, query_weight).astype(jnp.bfloat16)
    pair = matmul(memory, pair_weight).astype(jnp.bfloat16)
    cross_att, cross_lse = attend(
        cross_queries,
        pair[..., :model_width],
        pair[..., model_width:],
        doc_own,
        memory_docs,
        False,
        True,
    )
    cross_att = cross_att.astype(jnp.bfloat16)
    second_cross, second_unit, second_inv = normalize(
        first + matmul(cross_att, cross_weight), cross_gains
    )
    second = jnp.where(is_decoder, second_cross, first)
    second_low = second.astype(jnp.bfloat16)
    upward = matmul(second_low, in_weight)
    active = jax.nn.silu(upward).astype(jnp.bfloat16)
    result, third_unit, third_inv = normalize(second + matmul(active, down_weight), gains_pair[1])
    saved = {
        "mixed": mixed,
        "attended": attended,
        "self_lse": self_lse,
        "first_unit": first_unit,
        "first_inv": first_inv,
        "first_low": first_low,
        "cross_queries": cross_queries,
        "pair": pair,
        "cross_att": cross_att,
        "cross_lse": cross_lse,
        "second_unit": second_unit,
        "second_inv": second_inv,
        "second_low": second_low,
        "upward": upward,
        "active": active,
        "third_unit": third_unit,
        "third_inv": third_inv,
    }
    return (result, saved)


def layer_backward(
    grad_result, saved, hidden_in, doc_own, memory, memory_docs, weights, is_decoder
):
    (
        qkv_weight,
        out_weight,
        in_weight,
        down_weight,
        gains_pair,
        query_weight,
        pair_weight,
        cross_weight,
        cross_gains,
    ) = weights
    model_width = hidden_in.shape[-1]
    grad_third, grad_gain_late = normalize_back(
        grad_result, saved["third_unit"], gains_pair[1], saved["third_inv"]
    )
    down_grad = grad_third.astype(jnp.bfloat16)
    grad_down_w = contract(saved["active"], down_grad)
    grad_active = matmul_back(down_grad, down_weight).astype(jnp.bfloat16)
    sigmoid_up = jax.nn.sigmoid(saved["upward"])
    grad_upward = (
        grad_active.astype(jnp.float32)
        * (sigmoid_up + saved["upward"] * sigmoid_up * (1.0 - sigmoid_up))
    ).astype(jnp.bfloat16)
    grad_in_w = contract(saved["second_low"], grad_upward)
    grad_second = grad_third + matmul_back(grad_upward, in_weight)
    grad_cross_sum, grad_cross_gain = normalize_back(
        grad_second, saved["second_unit"], cross_gains, saved["second_inv"]
    )
    decoder_flag = is_decoder.astype(jnp.float32)
    grad_cross_sum = grad_cross_sum * decoder_flag
    grad_cross_gain = grad_cross_gain * decoder_flag
    cross_branch = grad_cross_sum.astype(jnp.bfloat16)
    grad_cross_w = contract(saved["cross_att"], cross_branch)
    grad_cross_att = matmul_back(cross_branch, cross_weight).astype(jnp.bfloat16)
    pair = saved["pair"]
    grad_cross_q, grad_pair = attend_back(
        saved["cross_queries"],
        pair[..., :model_width],
        pair[..., model_width:],
        doc_own,
        memory_docs,
        False,
        saved["cross_lse"],
        grad_cross_att,
        True,
    )
    grad_cross_q = grad_cross_q.astype(jnp.bfloat16)
    grad_pair = grad_pair.astype(jnp.bfloat16)
    grad_query_w = contract(saved["first_low"], grad_cross_q)
    grad_pair_w = contract(memory, grad_pair)
    grad_memory = matmul_back(grad_pair, pair_weight)
    grad_first = jnp.where(
        is_decoder, grad_cross_sum + matmul_back(grad_cross_q, query_weight), grad_second
    )
    grad_first_sum, grad_gain_early = normalize_back(
        grad_first, saved["first_unit"], gains_pair[0], saved["first_inv"]
    )
    self_branch = grad_first_sum.astype(jnp.bfloat16)
    grad_out_w = contract(saved["attended"], self_branch)
    grad_attended = matmul_back(self_branch, out_weight).astype(jnp.bfloat16)
    mixed = saved["mixed"]
    grad_queries, grad_pair_self = attend_back(
        mixed[..., :model_width],
        mixed[..., model_width : 2 * model_width],
        mixed[..., 2 * model_width :],
        doc_own,
        doc_own,
        is_decoder,
        saved["self_lse"],
        grad_attended,
        False,
    )
    grad_mixed = jnp.concatenate([grad_queries, grad_pair_self], axis=-1).astype(jnp.bfloat16)
    grad_qkv_w = contract(hidden_in, grad_mixed)
    grad_hidden = grad_first_sum + matmul_back(grad_mixed, qkv_weight)
    layer_grads = (
        grad_qkv_w,
        grad_out_w,
        grad_in_w,
        grad_down_w,
        jnp.stack([grad_gain_early, grad_gain_late]),
        grad_query_w,
        grad_pair_w,
        grad_cross_w,
        grad_cross_gain,
    )
    return (grad_hidden, grad_memory, layer_grads)


def any_rows(
    layer_input,
    segment_ids,
    attn_qkv,
    attn_out,
    ffn_in,
    ffn_out,
    norm_gain,
    cross_query,
    cross_pair,
    cross_out,
    cross_gain,
    out_cotangent,
):
    micro_count = layer_input.shape[1]
    section_index = lax.axis_index("section")
    is_decoder = section_index == 1
    weights = (
        attn_qkv[0],
        attn_out[0],
        ffn_in[0],
        ffn_out[0],
        norm_gain[0],
        cross_query,
        cross_pair,
        cross_out,
        cross_gain,
    )
    inputs_all = layer_input[0]
    docs_all = segment_ids[0]
    slot_ids = jnp.arange(micro_count)
    received = (jnp.zeros_like(inputs_all[0]), jnp.zeros_like(docs_all[0]))
    results = jnp.zeros_like(inputs_all)
    memories = []
    memory_doc_list = []
    for step_index in range(micro_count + 1):
        batch_index = step_index - section_index
        is_valid = (batch_index >= 0) & (batch_index < micro_count)
        chosen = jnp.clip(batch_index, 0, micro_count - 1)
        hidden_in = lax.dynamic_index_in_dim(inputs_all, chosen, 0, keepdims=False)
        doc_own = lax.dynamic_index_in_dim(docs_all, chosen, 0, keepdims=False)
        memory = received[0]
        memory_docs = jnp.where(is_valid & is_decoder, received[1], doc_own)
        memories.append(memory)
        memory_doc_list.append(memory_docs)
        result, saved = layer_forward(hidden_in, doc_own, memory, memory_docs, weights, is_decoder)
        low_result = result.astype(jnp.bfloat16)
        writing = (slot_ids == chosen) & is_valid
        results = jnp.where(writing[:, None, None, None], low_result[None], results)
        if step_index < micro_count:
            received = from_behind((low_result, doc_own), "section", 1)
    memory_stack = jnp.stack(memories)
    memory_doc_stack = jnp.stack(memory_doc_list)
    totals = tuple((jnp.zeros(weight.shape, jnp.float32) for weight in weights))
    input_grads = jnp.zeros(inputs_all.shape, jnp.float32)
    returned = jnp.zeros(inputs_all.shape[1:], jnp.float32)
    for step_index in range(micro_count + 1):
        batch_index = micro_count - step_index - section_index
        is_valid = (batch_index >= 0) & (batch_index < micro_count)
        chosen = jnp.clip(batch_index, 0, micro_count - 1)
        forward_step = jnp.clip(batch_index + section_index, 0, micro_count)
        hidden_in = lax.dynamic_index_in_dim(inputs_all, chosen, 0, keepdims=False)
        doc_own = lax.dynamic_index_in_dim(docs_all, chosen, 0, keepdims=False)
        memory = lax.dynamic_index_in_dim(memory_stack, forward_step, 0, keepdims=False)
        memory_docs = lax.dynamic_index_in_dim(memory_doc_stack, forward_step, 0, keepdims=False)
        discarded, saved = layer_forward(
            hidden_in, doc_own, memory, memory_docs, weights, is_decoder
        )
        cotangent = jnp.where(
            is_decoder,
            lax.dynamic_index_in_dim(out_cotangent, chosen, 0, keepdims=False).astype(jnp.float32),
            returned,
        )
        grad_hidden, grad_memory, layer_grads = layer_backward(
            cotangent, saved, hidden_in, doc_own, memory, memory_docs, weights, is_decoder
        )
        valid_flag = is_valid.astype(jnp.float32)
        totals = tuple(
            (running + valid_flag * fresh for running, fresh in zip(totals, layer_grads))
        )
        writing = (slot_ids == chosen) & is_valid
        input_grads = jnp.where(writing[:, None, None, None], grad_hidden[None], input_grads)
        if step_index < micro_count:
            returned = from_behind(grad_memory.astype(jnp.bfloat16), "section", -1).astype(
                grad_memory.dtype
            )
    group_sums = lax.psum(
        (
            totals[0],
            totals[1],
            totals[2],
            totals[3],
            totals[4],
            totals[5],
            totals[6],
            totals[7],
            totals[8],
        ),
        ("seq", "dp"),
    )
    section_sums = group_sums[:5]
    cross_sums = (
        from_root(group_sums[5].astype(jnp.bfloat16), "section", 1).astype(jnp.float32),
        from_root(group_sums[6].astype(jnp.bfloat16), "section", 1).astype(jnp.float32),
        from_root(group_sums[7].astype(jnp.bfloat16), "section", 1).astype(jnp.float32),
        from_root(group_sums[8].astype(jnp.bfloat16), "section", 1).astype(jnp.float32),
    )
    return (
        results[None],
        input_grads[None],
        section_sums[0][None],
        section_sums[1][None],
        section_sums[2][None],
        section_sums[3][None],
        section_sums[4][None],
        cross_sums[0],
        cross_sums[1],
        cross_sums[2],
        cross_sums[3],
    )


def split_rows(
    layer_input,
    segment_ids,
    attn_qkv,
    attn_out,
    ffn_in,
    ffn_out,
    norm_gain,
    cross_query,
    cross_pair,
    cross_out,
    cross_gain,
    out_cotangent,
):
    micros = layer_input.shape[1]
    length, width = layer_input.shape[3:]
    hidden = ffn_in.shape[-1]
    q_tiles = length // TILE
    group = lax.axis_size("dp") // 2
    axes = ("section", "seq", "dp")
    decoder = lax.axis_index("section") == 1
    flag = decoder.astype(jnp.int32)
    x = lax.axis_index("seq")
    core = lax.rem(lax.axis_index("dp"), 2)
    z = lax.axis_index("dp") // 2
    places = [(t, i, k, c) for t in range(2) for i in range(2) for k in range(group) for c in range(2)]

    def number(t, i, k, c):
        return ((t * 2 + i) * group + k) * 2 + c

    def send(values, target, section=None):
        route = [
            (number(*place), number(*target(*place)))
            for place in places
            if section in (None, place[0]) and target(*place)
        ]
        return lax.ppermute(values, axes, route)

    def to_core(t, i, k, c):
        return (t, i, k, 1 - c)

    def to_x(t, i, k, c):
        return (t, 1 - i, k, c)

    def to_row(t, i, k, c):
        return (t, c, k, i)

    def to_decoder(t, i, k, c):
        return (1, i, k, c) if t == 0 else None

    def to_encoder(t, i, k, c):
        return (0, i, k, c) if t == 1 else None

    def fence(values, *before):
        return lax.optimization_barrier((values,) + before)[0]

    def exchange(values):
        return send(values, to_core)

    low = ((length, width), bf16)
    wide = ((length, width), f32)
    marked = ((length + 16, width), bf16)
    both = ((2 * length, width), bf16)
    keys_all = ((2 * length, 2 * width), bf16)
    mixing = ((width, 3 * width), bf16)
    inner = ((length, hidden), bf16)
    lse = ((q_tiles, 8, 2 * TILE), f32)
    stat = ((length, LANES), f32)
    square = ((width, width), bf16)
    rising = ((width, hidden), bf16)
    falling = ((hidden, width), bf16)
    gain_rows = ((8, width), f32)

    meta = jnp.stack([flag, core, x, z]).astype(jnp.int32)
    numbers = segment_ids[0, :, 0].astype(bf16)
    padding = jnp.zeros((15, width), bf16)
    with_numbers = [
        jnp.concatenate([layer_input[0, micro, 0], numbers[micro][None], padding])
        for micro in range(micros)
    ]
    own = [send(with_numbers[0], to_row)]
    for micro in range(1, micros):
        own.append(send(fence(with_numbers[micro], own[-1]), to_row))
    other = [exchange(own[0])]

    plain = dict(meta=meta)
    small = dict(gains=norm_gain[0])
    forward, memories, memories_other = [], [], []
    for micro in range(micros):
        call = launch(
            self_forward,
            micro,
            None,
            plain,
            small,
            dict(
                x_own_h=own[micro],
                x_other_h=other[micro],
                w_mixed_h=attn_qkv[0],
                w_out_h=attn_out[0],
                w_in_h=ffn_in[0],
                w_down_h=ffn_out[0],
            ),
            dict(
                q_o=low,
                kv_o=keys_all,
                att_o=low,
                lse_o=lse,
                unit1_o=wide,
                inv1_o=stat,
                first_low_o=low,
                memory_o=marked,
                ffn_low_o=low,
                act_o=inner,
                slope_o=inner,
                unit2_o=wide,
                inv2_o=stat,
            ),
            dict(
                **attention_scratch(length, width),
                **forward_scratch(length, width),
                x=both,
                w_mixed=mixing,
                w_out=square,
                w_in=rising,
                w_down=falling,
                unit1=wide,
                inv1=stat,
                first_low=low,
                memory=marked,
                act=inner,
                slope=inner,
                unit2=wide,
                inv2=stat,
                sum=wide,
            ),
            28,
            26,
            after=(forward[0].lse_o,) if micro else (),
        )
        forward.append(call)
        memories.append(send(call.memory_o, to_decoder))
        if micro + 1 < micros:
            other.append(exchange(fence(own[micro + 1], call.lse_o)))

    for micro in range(micros):
        memories_other.append(exchange(fence(memories[micro], forward[-1].lse_o)))
    cotangent = send(fence(out_cotangent[:, 0], forward[0].lse_o), to_row)

    cross, grads_memory, made = [], [], []
    after = (forward[-1].lse_o,)
    for micro in range(micros):
        done = forward[micro]
        call = launch(
            cross_both_ways,
            micro,
            1,
            plain,
            dict(**small, cross_gain=cross_gain[None]),
            dict(
                x_own_h=own[micro],
                memory_own_h=memories[micro],
                memory_other_h=memories_other[micro],
                w_pair_h=cross_pair,
                first_low_h=done.first_low_o,
                unit1_h=done.unit1_o,
                w_query_h=cross_query,
                w_cross_h=cross_out,
                w_in_h=ffn_in[0],
                w_down_h=ffn_out[0],
                cot_h=cotangent,
            ),
            dict(
                att_o=low,
                ffn_low_o=low,
                act_o=inner,
                decoded_o=low,
                down_grad_o=low,
                up_grad_o=inner,
                gain_grads_o=gain_rows,
                branch_o=low,
                dq_low_o=low,
                dkv_o=keys_all,
                part_own_o=wide,
                part_other_o=low,
                grad_first_o=wide,
            ),
            dict(
                **attention_scratch(length, width),
                **forward_scratch(length, width),
                **backward_scratch(length, width),
                x=both,
                w_pair=((width, 2 * width), bf16),
                first_low=low,
                unit1=wide,
                w_query=square,
                w_cross=square,
                w_in=rising,
                w_down=falling,
                cot=low,
                unit2=wide,
                inv2=stat,
                second_low=low,
                act=inner,
                slope=inner,
                sum=wide,
                decoded=low,
                keep=wide,
                down_grad=low,
                up_grad=inner,
                gain_grads=gain_rows,
                branch=low,
                part_own=wide,
            ),
            36,
            44,
            dict(act_o=done.act_o, ffn_low_o=done.ffn_low_o),
            after,
        )
        cross.append(call)
        away = call.part_other_o
        if micro:
            away = fence(away, grads_memory[-1])
        total = call.part_own_o + exchange(away).astype(f32)
        made.append(total.astype(bf16))
        after = (made[micro],)
        grads_memory.append(send(made[micro], to_encoder))

    def backward_feed(micro, after):
        done, late = forward[micro], cross[micro]
        return launch(
            feed_backward_alone,
            micro,
            0,
            plain,
            dict(gains=norm_gain[0]),
            dict(
                grad_memory_h=grads_memory[micro],
                unit2_h=done.unit2_o,
                inv2_h=done.inv2_o,
                slope_h=done.slope_o,
                w_in_h=ffn_in[0],
                w_down_h=ffn_out[0],
            ),
            dict(gain_late_o=gain_rows, down_grad_o=low, up_grad_o=inner, grad_first_o=wide),
            dict(
                cot=low,
                unit2=wide,
                inv2=stat,
                slope=inner,
                w_in=rising,
                w_down=falling,
                gain_grads=gain_rows,
                keep=wide,
                down_grad=low,
                up_grad=inner,
                sum=wide,
            ),
            12,
            10,
            dict(
                down_grad_o=late.down_grad_o, up_grad_o=late.up_grad_o, grad_first_o=late.grad_first_o
            ),
            after,
        )

    def backward_self(micro, side, grad_first, previous=None, after=(), halfway=None):
        done = forward[micro]
        heads = width // LANES
        given = dict(
            x_own_h=own[micro],
            x_other_h=other[micro],
            q_h=done.q_o,
            kv_h=done.kv_o,
            att_h=done.att_o,
            lse_h=done.lse_o,
        )
        ahead = dict(
            grad_first_h=grad_first,
            unit1_h=done.unit1_o,
            inv1_h=done.inv1_o,
            w_out_h=attn_out[0],
        )
        makes = dict(dq_low_o=low, dkv_o=keys_all)
        makes_first = dict(gain_early_o=gain_rows, branch_o=low)
        makes_last = dict(part_own_o=wide, part_other_o=low)
        scratch = dict(
            **attention_scratch(length, width),
            **backward_scratch(length, width),
            w_out=square,
            w_mixed=mixing,
            unit1=wide,
            inv1=stat,
            keep=wide,
            branch=low,
            grad_att=low,
            gain_grads=gain_rows,
        )

        def part(first, last, large, outs, work, previous, after):
            return launch(
                self_backward,
                (micro, first, last),
                side,
                plain,
                small,
                dict(**given, **large),
                dict(**makes, **outs),
                scratch,
                28,
                work,
                previous,
                after,
            )

        if halfway is None:
            large = dict(**ahead, w_mixed_h=attn_qkv[0])
            outs = dict(**makes_first, **makes_last)
            return part(0, heads, large, outs, 22, previous, after)
        outs = dict(**makes_first, grad_sum_o=wide, grad_att_o=low)
        one = part(0, heads // 2, ahead, outs, 12, None, after)
        large = dict(
            w_mixed_h=attn_qkv[0],
            grad_sum_h=one.grad_sum_o,
            grad_att_h=one.grad_att_o,
            dq_h=one.dq_low_o,
            dkv_h=one.dkv_o,
        )
        two = part(heads // 2, heads, large, makes_last, 12, None, halfway(one))
        return types.SimpleNamespace(**{**vars(one), **vars(two)})

    def weight_grads(plan, side, arrays, scratch, after=()):
        blocks = ((2, width, width), bf16)
        call = launch(
            contract_blocks,
            plan,
            side,
            plain,
            dict(),
            arrays,
            dict(sent_o=blocks, kept_o=blocks),
            dict(**scratch, blocks=((4, width, width), bf16)),
            36,
            8,
            after=after,
        )
        return call.sent_o, call.kept_o

    def first_sums(halves, section=None):
        sent, kept = halves
        got = send(sent, to_core, section)

        def block(side):
            return sum(
                lax.dynamic_index_in_dim(part, side, 0, keepdims=False).astype(f32)
                for part in (kept, got)
            )

        return block(1 - x).astype(bf16), block(x)

    def middle_sums(sums, section=None):
        away, total = sums
        return (total + send(away, to_x, section).astype(f32)).astype(bf16)

    arrivals = []

    def last_sums(totals, *later):
        rows = width // group
        shares = jnp.concatenate([total.reshape(group, rows, width) for total in totals], axis=1)

        def share(step):
            return lax.dynamic_index_in_dim(shares, lax.rem(z + step, group), 0, keepdims=False)

        parts = [share(0)]
        for step in range(1, group):
            parts.append(send(share(step), along_z(step)))
        if later:
            parts = [fence(part, *later) for part in parts]
        arrivals.append(parts[1])
        return sum(part.astype(f32) for part in parts).astype(bf16)

    def along_z(step):
        return lambda t, i, k, c: (t, i, (k + step) % group, c)

    def gather_z(share):
        return [share] + [send(share, along_z(step)) for step in range(1, group)]

    def gain_block(rows):
        filled = jnp.concatenate([jnp.stack(rows), jnp.zeros((16 - len(rows), width), f32)])
        return filled.astype(bf16)

    def spread(targets, own, own_x, outs, parts, after=()):
        return launch(
            spread_pieces,
            targets,
            None,
            plain,
            dict(),
            dict(own_h=own, own_x_h=own_x, other_h=exchange(own), other_x_h=exchange(own_x)),
            outs,
            dict(
                pieces=((4,) + own.shape, bf16),
                wide=((4 * group * parts, width // group, width), f32),
            ),
            8 + 4 * group * parts,
            5,
            after=after,
        )

    tokens, all_tokens = micros * length, 2 * micros * length
    turn, turn_all = ((width, tokens), bf16), ((width, all_tokens), bf16)
    narrow, narrow_all = ((tokens, width), bf16), ((all_tokens, width), bf16)
    pair_all = ((all_tokens, 2 * width), bf16)
    deep = ((tokens, hidden), bf16)

    def part_of(buffer, *sources):
        return lambda column: (buffer, sources, column)

    def key_rows(buffer, sources):
        first, second = pl.ds(0, length), pl.ds(length, length)
        return part_of(buffer, *[source.at[rows] for rows in (first, second) for source in sources])

    def cross_plan(r):
        rows = pl.ds(0, length)
        low_part = part_of(r.low, r.low0_h, r.low1_h)
        att_part = part_of(r.att, r.att0_h, r.att1_h)
        dq_part = part_of(r.dq, r.dq0_h, r.dq1_h)
        branch_part = part_of(r.branch, r.branch0_h, r.branch1_h)
        sources = (r.mem0_h, r.mem1_h, r.mem2_h, r.mem3_h)
        mem_part = part_of(r.mem, *[source.at[rows] for source in sources])
        pair_part = key_rows(r.pair, (r.pair0_h, r.pair1_h))
        return [
            (r.turn, low_part(0), dq_part(0)),
            (r.turn_att, att_part(0), branch_part(0)),
            (r.turn_all, mem_part(0), pair_part(0)),
            (r.turn_all, mem_part(0), pair_part(1)),
        ]

    def rising_plan(r):
        low_part = part_of(r.low, r.low0_h, r.low1_h)
        up_part = part_of(r.up, r.up0_h, r.up1_h)
        return [(r.turn, low_part(0), up_part(block)) for block in range(4)]

    def falling_plan(r):
        act_part = part_of(r.act, r.act0_h, r.act1_h)
        down_part = part_of(r.down, r.down0_h, r.down1_h)
        return [(r.turn, act_part(block), down_part(0)) for block in range(4)]

    def self_plan(r):
        rows = pl.ds(0, length)
        sources = (r.x0_h, r.x1_h, r.x2_h, r.x3_h)
        x_part = part_of(r.x, *[source.at[rows] for source in sources])
        dq_part = part_of(r.dq, r.dq0_h, r.dq1_h)
        pair_part = key_rows(r.pair, (r.pair0_h, r.pair1_h))
        att_part = part_of(r.att, r.att0_h, r.att1_h)
        branch_part = part_of(r.branch, r.branch0_h, r.branch1_h)
        return [
            (r.turn_all, x_part(0), dq_part(0)),
            (r.turn_all, x_part(0), pair_part(0)),
            (r.turn_all, x_part(0), pair_part(1)),
            (r.turn, att_part(0), branch_part(0)),
        ]

    last = micros - 1
    feeds, ends = [None] * micros, [None] * micros
    cross_halves = weight_grads(
        cross_plan,
        1,
        dict(
            low0_h=forward[0].first_low_o,
            low1_h=forward[1].first_low_o,
            dq0_h=cross[0].dq_low_o,
            dq1_h=cross[1].dq_low_o,
            att0_h=cross[0].att_o,
            att1_h=cross[1].att_o,
            branch0_h=cross[0].branch_o,
            branch1_h=cross[1].branch_o,
            mem0_h=memories[0],
            mem1_h=memories[1],
            mem2_h=memories_other[0],
            mem3_h=memories_other[1],
            pair0_h=cross[0].dkv_o,
            pair1_h=cross[1].dkv_o,
        ),
        dict(
            low=narrow,
            dq=narrow,
            att=narrow,
            branch=narrow,
            mem=narrow_all,
            pair=pair_all,
            turn=turn,
            turn_att=turn,
            turn_all=turn_all,
        ),
        (made[last],),
    )
    cross_sums = first_sums(cross_halves, 1)
    results = jnp.stack(
        [
            jnp.where(decoder, call.decoded_o, done.memory_o[:length])
            for call, done in zip(cross, forward)
        ]
    )
    results = send(results, to_row)
    latest = made[last]

    def part_sum(micro, *before):
        end = ends[micro]
        away = fence(end.part_other_o, *before)
        total = (end.part_own_o + exchange(away).astype(f32)).astype(bf16)
        return total, send(total, to_row)

    steps = []
    for micro in range(last):
        feeds[micro] = backward_feed(micro, (latest,))
        first = feeds[micro].grad_first_o
        ends[micro] = backward_self(micro, 0, first)
        ends[micro] = backward_self(micro, 1, first, vars(ends[micro]), (cross_sums[0], grads_memory[last]))
        cross_total = middle_sums(cross_sums, 1)
        steps.append(part_sum(micro, cross_total))
        latest = ends[micro].gain_early_o
    feeds[last] = backward_feed(last, (latest,))

    rising_halves = weight_grads(
        rising_plan,
        None,
        dict(
            low0_h=cross[0].ffn_low_o,
            low1_h=cross[1].ffn_low_o,
            up0_h=feeds[0].up_grad_o,
            up1_h=feeds[1].up_grad_o,
        ),
        dict(low=narrow, up=deep, turn=turn),
        (results,) + tuple(step[0] for step in steps),
    )
    rising_sums = first_sums(rising_halves)
    rising_total = middle_sums(rising_sums)
    falling_halves = weight_grads(
        falling_plan,
        None,
        dict(
            act0_h=cross[0].act_o,
            act1_h=cross[1].act_o,
            down0_h=feeds[0].down_grad_o,
            down1_h=feeds[1].down_grad_o,
        ),
        dict(act=deep, down=narrow, turn=turn),
        (rising_sums[0],),
    )
    falling_sent = fence(falling_halves[0], rising_total)
    falling_sums = first_sums((falling_sent, falling_halves[1]))
    falling_total = middle_sums(falling_sums)
    shares = []

    third = sum(call.gain_grads_o[1] for call in cross)

    def halfway(one):
        both = last_sums((rising_total, cross_total), one.gain_early_o)
        rows = width // group
        found = jnp.concatenate([both[rows:], gain_block([third])])
        shares.extend([both[:rows], found, send(found, to_encoder)])
        return (both, falling_total)

    ends[last] = backward_self(
        last,
        None,
        feeds[last].grad_first_o,
        None,
        (falling_sums[0],),
        halfway,
    )
    finished = ends[last].part_own_o
    falling_share = last_sums((falling_total,), ends[last].gain_early_o, finished)
    rising_share, found, arrived = shares
    cross_share = jnp.where(decoder, found, fence(arrived, finished))
    one_own = gather_z(jnp.concatenate([rising_share, falling_share, cross_share]))
    steps.append(part_sum(last, falling_share, arrived, steps[0][1]))

    self_halves = weight_grads(
        self_plan,
        None,
        dict(
            x0_h=own[0],
            x1_h=own[1],
            x2_h=other[0],
            x3_h=other[1],
            dq0_h=ends[0].dq_low_o,
            dq1_h=ends[1].dq_low_o,
            pair0_h=ends[0].dkv_o,
            pair1_h=ends[1].dkv_o,
            att0_h=forward[0].att_o,
            att1_h=forward[1].att_o,
            branch0_h=ends[0].branch_o,
            branch1_h=ends[1].branch_o,
        ),
        dict(
            x=narrow_all,
            dq=narrow,
            pair=pair_all,
            att=narrow,
            branch=narrow,
            turn=turn,
            turn_all=turn_all,
        ),
        (steps[last][0],),
    )
    away, total = first_sums(
        (fence(self_halves[0], one_own[1], steps[last][1]), self_halves[1])
    )
    self_total = middle_sums((away, total))
    self_share = last_sums((self_total,))
    one_own = jnp.stack([one_own[0]] + [fence(part, arrivals[-1]) for part in one_own[1:]])
    one_own_x = send(one_own, to_x)

    early = sum(end.gain_early_o[0] for end in ends)
    late = jnp.where(
        decoder,
        sum(call.gain_grads_o[0] for call in cross),
        sum(call.gain_late_o[0] for call in feeds),
    )
    two_own = jnp.stack(
        gather_z(jnp.concatenate([self_share, gain_block([early, late])]))
    )
    two_own_x = send(fence(two_own, one_own_x), to_x)

    def columns(block):
        return pl.ds(block * width, width)

    def one_targets(r, block, row, rows):
        lines = pl.ds(row, rows)
        feed = [r.up_o.at[lines, columns(block)], r.down_o.at[pl.ds(block * width + row, rows)]]
        if block >= 2:
            return feed + [r.pair_o.at[lines, columns(block - 2)]]
        return feed + [(r.out_o if block else r.query_o).at[lines]]

    def two_targets(r, block, row, rows):
        lines = pl.ds(row, rows)
        return [r.out_o.at[lines] if block == 3 else r.mixed_o.at[lines, columns(block)]]

    square_out = ((width, width), f32)
    one_own_x = fence(one_own_x, two_own)
    grad_input = jnp.stack([step[1] for step in steps]).astype(f32)
    one_grads = spread(
        one_targets,
        one_own,
        one_own_x,
        dict(
            up_o=((width, hidden), f32),
            query_o=square_out,
            pair_o=((width, 2 * width), f32),
            down_o=((hidden, width), f32),
            out_o=square_out,
            gains_o=((1, width), f32),
        ),
        3,
        (grad_input, results),
    )
    two_own_x = fence(two_own_x, one_grads.gains_o)
    two_grads = spread(
        two_targets,
        two_own,
        two_own_x,
        dict(
            mixed_o=((width, 3 * width), f32),
            out_o=square_out,
            gains_o=((2, width), f32),
        ),
        1,
    )

    return (
        results[None, :, None],
        grad_input[None, :, None],
        two_grads.mixed_o[None],
        two_grads.out_o[None],
        one_grads.up_o[None],
        one_grads.down_o[None],
        two_grads.gains_o[None],
        one_grads.query_o,
        one_grads.pair_o,
        one_grads.out_o,
        one_grads.gains_o[0],
    )


def shards(*arrays):
    layer_input = arrays[0]
    micros, rows, length = layer_input.shape[1:4]
    simple = (
        lax.axis_size("section") == 2
        and lax.axis_size("seq") == 2
        and lax.axis_size("dp") in (4, 8, 16)
        and (micros, rows) == (2, 1)
        and length == layer_input.shape[-1] == CHUNK
        and arrays[4].shape[-1] == 4 * CHUNK
    )
    return split_rows(*arrays) if simple else any_rows(*arrays)


def solution(mesh):
    in_specs = (
        P("section", None, "dp", "seq", None),
        P("section", None, "dp", "seq"),
        P("section", None, None),
        P("section", None, None),
        P("section", None, None),
        P("section", None, None),
        P("section", None, None),
        P(),
        P(),
        P(),
        P(),
        P(None, "dp", "seq", None),
    )
    out_specs = (
        P("section", None, "dp", "seq", None),
        P("section", None, "dp", "seq", None),
        P("section", None, None),
        P("section", None, None),
        P("section", None, None),
        P("section", None, None),
        P("section", None, None),
        P(),
        P(),
        P(),
        P(),
    )
    return jax.shard_map(shards, mesh=mesh, in_specs=in_specs, out_specs=out_specs, check_vma=False)
```

```python
import types

import jax
import jax.numpy as jnp
from jax import lax
from jax.experimental import pallas as pl
from jax.experimental.pallas import tpu as pltpu
from jax.sharding import PartitionSpec as P

HEADS = 8
TILE = 256
LANES = 128
CHUNK = 512

f32 = jnp.float32
bf16 = jnp.bfloat16
negative_big = -1e30
epsilon = 1e-05


def dot(left, right):
    return lax.dot_general(left, right, (((1,), (0,)), ((), ())), preferred_element_type=f32)


def dot_nt(left, right):
    return lax.dot_general(left, right, (((1,), (1,)), ((), ())), preferred_element_type=f32)


def dot_tn(left, right):
    return lax.dot_general(left, right, (((0,), (0,)), ((), ())), preferred_element_type=f32)


def standardize(values):
    center = values - jnp.mean(values, axis=-1, keepdims=True)
    inverse = lax.rsqrt(jnp.mean(center * center, axis=-1, keepdims=True) + epsilon)
    return center * inverse, inverse


def standardize_back(grad_out, standard, gain_row, inverse):
    scaled = grad_out * gain_row
    grad_in = inverse * (
        scaled
        - jnp.mean(scaled, axis=-1, keepdims=True)
        - standard * jnp.mean(scaled * standard, axis=-1, keepdims=True)
    )
    return grad_in, jnp.sum(grad_out * standard, axis=0, keepdims=True)


class Copies:
    def __init__(self, sems):
        self.sems = sems
        self.used = 0

    def start(self, source, target):
        copy = pltpu.make_async_copy(source, target, self.sems.at[self.used])
        self.used += 1
        copy.start()
        return copy


def wait_all(copies):
    for copy in copies:
        copy.wait()


def spread_pairs(target, source, factor, pairs):
    tiles = target.shape[1]
    half = lax.broadcasted_iota(jnp.int32, (TILE, LANES), 1) < LANES // 2
    first = jnp.where(half, factor, 0.0).astype(bf16)
    second = jnp.where(half, 0.0, factor).astype(bf16)
    for tile in range(tiles):
        for pair in pairs:
            block = source[tile * TILE : (tile + 1) * TILE, pair * LANES : (pair + 1) * LANES]
            target[pair, tile, :TILE, :] = block * first
            target[pair, tile, TILE:, :] = block * second


def turn_tiles(target, source, column, pairs):
    low, high = pairs[0] * LANES, (pairs[-1] + 1) * LANES
    for tile in range(target.shape[0]):
        block = source[tile * TILE : (tile + 1) * TILE, column + low : column + high]
        target[tile, low:high, :] = jnp.transpose(block)


def place_documents(r, copies):
    wait_all(copies)
    q_tiles = r.qd.shape[0]
    for part in range(3):
        row = r.docs[part].astype(f32)[0:1, :]
        for tile in range(q_tiles):
            piece = row[:, tile * TILE : (tile + 1) * TILE]
            slot = part * q_tiles + tile
            r.bounds[0, slot] = jnp.min(piece).astype(jnp.int32)
            r.bounds[1, slot] = jnp.max(piece).astype(jnp.int32)
            if part == 0:
                r.qd[tile] = jnp.broadcast_to(piece, (8, TILE))
        if part > 0:
            for start in range(0, row.shape[1], LANES):
                block = jnp.broadcast_to(row[:, start : start + LANES], (LANES, LANES))
                place = (part - 1) * row.shape[1] + start
                r.kdc[place : place + LANES, :] = jnp.transpose(block)


def load_documents(r, move, queries, own, other):
    rows = pl.ds(r.docs.shape[2], r.docs.shape[1])
    return [
        move.start(source.at[rows], r.docs.at[part])
        for part, source in enumerate((queries, own, other))
    ]


def tile_place(r, core, causal, q_tile, k_tile):
    q_tiles = r.qd.shape[0]
    length = q_tiles * TILE
    owner = jnp.where(k_tile < q_tiles, core, 1 - core)
    k_start = owner * length + lax.rem(k_tile, q_tiles) * TILE
    ahead = core * length + q_tile * TILE - k_start
    ahead = jnp.where(causal == 1, ahead, 2 * length * TILE)
    q_low, q_high = r.bounds[0, q_tile], r.bounds[1, q_tile]
    k_low, k_high = r.bounds[0, q_tiles + k_tile], r.bounds[1, q_tiles + k_tile]
    active = (q_low <= k_high) & (k_low <= q_high) & (ahead > -TILE)
    whole = (q_low == k_high) & (k_low == q_high) & (ahead >= TILE)
    return active, whole, ahead


def each_tile(place, body):
    active, whole, ahead = place
    pl.when(active & jnp.logical_not(whole))(lambda: body(ahead))
    pl.when(whole)(lambda: body(None))


def fill_bias(r, q_tile, k_tile, ahead):
    keys = r.kdc[pl.ds(pl.multiple_of(k_tile * TILE, TILE), TILE), :]
    shift = lax.broadcasted_iota(jnp.int32, (TILE, LANES), 0) - lax.broadcasted_iota(
        jnp.int32, (TILE, LANES), 1
    )
    queries = r.qd[q_tile]
    for start in range(0, TILE, LANES):
        same = keys == queries[0:1, start : start + LANES]
        allowed = same & (shift - start <= ahead)
        r.bias[:, start : start + LANES] = jnp.where(allowed, 0.0, negative_big)


def attention_forward(r, core, causal):
    pairs, q_tiles = r.qm.shape[:2]
    k_tiles = r.vt.shape[0]

    def one_query_tile(q_tile, carry):
        r.top[...] = jnp.full(r.top.shape, negative_big, f32)
        r.total[...] = jnp.zeros(r.total.shape, f32)
        r.turned[...] = jnp.zeros(r.turned.shape, f32)

        def one_key_tile(k_tile, inner):
            def one_tile(ahead):
                if ahead is not None:
                    fill_bias(r, q_tile, k_tile, ahead)
                rows = pl.ds(pl.multiple_of(k_tile * TILE, TILE), TILE)

                def raw(pair):
                    keys = r.kv[rows, pair * LANES : (pair + 1) * LANES]
                    return dot_nt(keys, r.qm[pair, q_tile])

                raw_next = raw(0)
                for pair in range(pairs):
                    scores = raw_next
                    if ahead is not None:
                        bias = r.bias[...]
                        scores = scores + jnp.concatenate([bias, bias], axis=1)
                    if pair + 1 < pairs:
                        raw_next = raw(pair + 1)
                    old_top = r.top[pair : pair + 1, :]
                    new_top = jnp.maximum(old_top, jnp.max(scores, axis=0, keepdims=True))
                    weights = jnp.exp(scores - new_top)
                    shrink = jnp.exp(old_top - new_top)
                    r.top[pair : pair + 1, :] = new_top
                    r.total[pair : pair + 1, :] = r.total[
                        pair : pair + 1, :
                    ] * shrink + jnp.sum(weights, axis=0, keepdims=True)
                    low = weights.astype(bf16)
                    for side in range(2):
                        span = slice(side * TILE, (side + 1) * TILE)
                        head = slice((2 * pair + side) * 64, (2 * pair + side + 1) * 64)
                        r.turned[head, :] = r.turned[head, :] * shrink[:, span] + dot(
                            r.vt[k_tile, head, :], low[:, span]
                        )

            each_tile(tile_place(r, core, causal, q_tile, k_tile), one_tile)
            return inner

        lax.fori_loop(0, k_tiles, one_key_tile, 0)
        for pair in range(pairs):
            total = r.total[pair : pair + 1, :]
            r.lse[q_tile, pair : pair + 1, :] = r.top[pair : pair + 1, :] + jnp.log(total)
            share = 1.0 / total
            for side in range(2):
                span = slice(side * TILE, (side + 1) * TILE)
                head = slice((2 * pair + side) * 64, (2 * pair + side + 1) * 64)
                r.turned[head, :] = r.turned[head, :] * share[:, span]
        rows = pl.ds(pl.multiple_of(q_tile * TILE, TILE), TILE)
        r.att[rows, :] = jnp.transpose(r.turned[...]).astype(bf16)
        return carry

    lax.fori_loop(0, q_tiles, one_query_tile, 0)


def row_products(r, grad_att, pairs):
    low, high = pairs[0] * LANES, (pairs[-1] + 1) * LANES
    for tile in range(r.qm.shape[1]):
        rows = slice(tile * TILE, (tile + 1) * TILE)
        product = jnp.transpose(
            grad_att[rows, low:high].astype(f32) * r.att[rows, low:high].astype(f32)
        )
        for pair in pairs:
            for side in range(2):
                head = (2 * pair + side) * 64 - low
                r.delta[tile, pair : pair + 1, side * TILE : (side + 1) * TILE] = jnp.sum(
                    product[head : head + 64, :], axis=0, keepdims=True
                )


def attention_backward(r, core, causal, pairs):
    q_tiles, k_tiles = r.qm.shape[1], r.kt.shape[0]
    width = r.kt.shape[1]
    low, high = pairs[0] * LANES, (pairs[-1] + 1) * LANES
    for start in (0, width):
        r.dkv[:, start + low : start + high] = jnp.zeros((r.dkv.shape[0], high - low), f32)

    def one_query_tile(q_tile, carry):
        r.turned[low:high, :] = jnp.zeros((high - low, TILE), f32)

        def one_key_tile(k_tile, inner):
            def one_tile(ahead):
                if ahead is not None:
                    fill_bias(r, q_tile, k_tile, ahead)
                rows = pl.ds(pl.multiple_of(k_tile * TILE, TILE), TILE)

                def raw(pair):
                    lanes = slice(pair * LANES, (pair + 1) * LANES)
                    lanes_v = slice(width + pair * LANES, width + (pair + 1) * LANES)
                    return (
                        dot_nt(r.kv[rows, lanes], r.qm[pair, q_tile]),
                        dot_nt(r.kv[rows, lanes_v], r.gm[pair, q_tile]),
                    )

                raw_next = raw(pairs[0])
                for pair in pairs:
                    scores, grad_probs = raw_next
                    if ahead is not None:
                        bias = r.bias[...]
                        scores = scores + jnp.concatenate([bias, bias], axis=1)
                    if pair < pairs[-1]:
                        raw_next = raw(pair + 1)
                    probs = jnp.exp(scores - r.lse[q_tile, pair : pair + 1, :])
                    grad_scores = probs * (grad_probs - r.delta[q_tile, pair : pair + 1, :])
                    probs_low = probs.astype(bf16)
                    grad_low = grad_scores.astype(bf16)
                    lanes = slice(pair * LANES, (pair + 1) * LANES)
                    lanes_v = slice(width + pair * LANES, width + (pair + 1) * LANES)
                    r.dkv[rows, lanes] += dot(grad_low, r.qm[pair, q_tile])
                    r.dkv[rows, lanes_v] += dot(probs_low, r.gm[pair, q_tile])
                    for side in range(2):
                        span = slice(side * TILE, (side + 1) * TILE)
                        head = slice((2 * pair + side) * 64, (2 * pair + side + 1) * 64)
                        r.turned[head, :] += dot(r.kt[k_tile, head, :], grad_low[:, span])

            each_tile(tile_place(r, core, causal, q_tile, k_tile), one_tile)
            return inner

        lax.fori_loop(0, k_tiles, one_key_tile, 0)
        rows = pl.ds(pl.multiple_of(q_tile * TILE, TILE), TILE)
        r.dq[rows, low:high] = jnp.transpose(r.turned[low:high, :]) * (64**-0.5)
        return carry

    lax.fori_loop(0, q_tiles, one_query_tile, 0)


def feed_forward(r, low):
    chunks = [slice(at, at + CHUNK) for at in range(0, r.w_in.shape[1], CHUNK)]
    upward_next = dot(low[...], r.w_in[:, chunks[0]])
    for place, span in enumerate(chunks):
        upward = upward_next
        if place + 1 < len(chunks):
            upward_next = dot(low[...], r.w_in[:, chunks[place + 1]])
        gate = jax.nn.sigmoid(upward)
        active = (upward * gate).astype(bf16)
        r.act[:, span] = active
        r.slope[:, span] = (gate + upward * gate * (1.0 - gate)).astype(r.slope.dtype)
        part = dot(active, r.w_down[span, :])
        if place:
            r.sum[...] += part
        else:
            r.sum[...] = part


def feed_backward(r):
    chunks = [slice(at, at + CHUNK) for at in range(0, r.w_in.shape[1], CHUNK)]
    active_next = dot_nt(r.down_grad[...], r.w_down[chunks[0], :])
    for place, span in enumerate(chunks):
        grad_active = active_next.astype(bf16)
        if place + 1 < len(chunks):
            active_next = dot_nt(r.down_grad[...], r.w_down[chunks[place + 1], :])
        grad_up = (grad_active.astype(f32) * r.slope[:, span].astype(f32)).astype(bf16)
        r.up_grad[:, span] = grad_up
        part = dot_nt(grad_up, r.w_in[:, span])
        if place:
            r.sum[...] += part
        else:
            r.sum[...] = part


def self_forward(r):
    length, width = r.unit1.shape
    decoder, core = r.meta[0], r.meta[1]
    move = Copies(r.sems)
    whole = pl.ds(0, length)
    documents = load_documents(r, move, r.x_own_h, r.x_own_h, r.x_other_h)
    early = [
        move.start(r.x_own_h.at[whole], r.x.at[whole]),
        move.start(r.x_other_h.at[whole], r.x.at[pl.ds(length, length)]),
        move.start(r.w_mixed_h, r.w_mixed),
    ]
    later = [
        move.start(r.w_out_h, r.w_out),
        move.start(r.w_in_h, r.w_in),
        move.start(r.w_down_h, r.w_down),
    ]
    place_documents(r, documents)
    wait_all(early)
    r.q[...] = dot(r.x[:length, :], r.w_mixed[:, :width]).astype(bf16)
    r.kv[...] = dot(r.x[...], r.w_mixed[:, width:]).astype(bf16)
    outs = [move.start(r.q, r.q_o), move.start(r.kv, r.kv_o)]
    pairs = range(width // LANES)
    spread_pairs(r.qm, r.q, 64**-0.5, pairs)
    turn_tiles(r.vt, r.kv, width, pairs)
    attention_forward(r, core, decoder)
    wait_all(later)
    outs += [move.start(r.att, r.att_o), move.start(r.lse, r.lse_o)]
    unit, inverse = standardize(r.x[:length, :].astype(f32) + dot(r.att[...], r.w_out[...]))
    r.unit1[...] = unit
    r.inv1[...] = jnp.broadcast_to(inverse, r.inv1.shape)
    r.first_low[...] = (unit * r.gains[0:1, :]).astype(bf16)
    outs += [
        move.start(r.unit1, r.unit1_o),
        move.start(r.inv1, r.inv1_o),
        move.start(r.first_low, r.first_low_o),
    ]

    @pl.when(decoder == 0)
    def _():
        feed_forward(r, r.first_low)
        late = [
            move.start(r.first_low, r.ffn_low_o),
            move.start(r.act, r.act_o),
            move.start(r.slope, r.slope_o),
        ]
        unit2, inverse2 = standardize(r.unit1[...] * r.gains[0:1, :] + r.sum[...])
        r.memory[:length, :] = (unit2 * r.gains[1:2, :]).astype(bf16)
        r.memory[length:, :] = r.docs[0]
        late += [move.start(r.memory, r.memory_o)]
        r.unit2[...] = unit2
        r.inv2[...] = jnp.broadcast_to(inverse2, r.inv2.shape)
        late += [move.start(r.unit2, r.unit2_o), move.start(r.inv2, r.inv2_o)]
        wait_all(late)

    wait_all(outs)


def cross_both_ways(r):
    length, width = r.unit1_h.shape
    core = r.meta[1]
    move = Copies(r.sems)
    whole = pl.ds(0, length)
    documents = load_documents(r, move, r.x_own_h, r.memory_own_h, r.memory_other_h)
    moves = [
        move.start(r.memory_own_h.at[whole], r.x.at[whole]),
        move.start(r.memory_other_h.at[whole], r.x.at[pl.ds(length, length)]),
        move.start(r.w_pair_h, r.w_pair),
        move.start(r.first_low_h, r.first_low),
        move.start(r.w_query_h, r.w_query),
    ]
    later = [
        move.start(r.unit1_h, r.unit1),
        move.start(r.w_cross_h, r.w_cross),
        move.start(r.w_in_h, r.w_in),
        move.start(r.w_down_h, r.w_down),
        move.start(r.cot_h.at[r.micro], r.cot),
    ]
    place_documents(r, documents)
    wait_all(moves)
    r.kv[...] = dot(r.x[...], r.w_pair[...]).astype(bf16)
    r.q[...] = dot(r.first_low[...], r.w_query[...]).astype(bf16)
    pairs = range(width // LANES)
    spread_pairs(r.qm, r.q, 64**-0.5, pairs)
    turn_tiles(r.vt, r.kv, width, pairs)
    turn_tiles(r.kt, r.kv, 0, pairs)
    attention_forward(r, core, 0)
    outs = [move.start(r.att, r.att_o)]
    wait_all(later)
    first = r.unit1[...] * r.gains[0:1, :]
    unit, inverse = standardize(first + dot(r.att[...], r.w_cross[...]))
    r.unit2[...] = unit
    r.inv2[...] = jnp.broadcast_to(inverse, r.inv2.shape)
    r.second_low[...] = (unit * r.cross_gain[...]).astype(bf16)
    outs += [move.start(r.second_low, r.ffn_low_o)]
    feed_forward(r, r.second_low)
    outs += [move.start(r.act, r.act_o)]
    unit3, inverse3 = standardize(r.unit2[...] * r.cross_gain[...] + r.sum[...])
    r.decoded[...] = (unit3 * r.gains[1:2, :]).astype(bf16)
    outs += [move.start(r.decoded, r.decoded_o)]
    grad_third, gain_late = standardize_back(
        r.cot[...].astype(f32), unit3, r.gains[1:2, :], inverse3
    )
    r.keep[...] = grad_third
    r.down_grad[...] = grad_third.astype(bf16)
    outs += [move.start(r.down_grad, r.down_grad_o)]
    feed_backward(r)
    outs += [move.start(r.up_grad, r.up_grad_o)]
    grad_sum, gain_cross = standardize_back(
        r.keep[...] + r.sum[...], r.unit2[...], r.cross_gain[...], r.inv2[:, 0:1]
    )
    r.gain_grads[...] = jnp.zeros(r.gain_grads.shape, f32)
    r.gain_grads[0:1, :] = gain_late
    r.gain_grads[1:2, :] = gain_cross
    r.keep[...] = grad_sum
    r.branch[...] = grad_sum.astype(bf16)
    outs += [move.start(r.gain_grads, r.gain_grads_o), move.start(r.branch, r.branch_o)]
    r.q[...] = dot_nt(r.branch[...], r.w_cross[...]).astype(bf16)
    spread_pairs(r.gm, r.q, 1.0, pairs)
    row_products(r, r.q, pairs)
    attention_backward(r, core, 0, pairs)
    r.dq_low[...] = r.dq[...].astype(bf16)
    r.keep[...] += dot_nt(r.dq_low[...], r.w_query[...])
    outs += [move.start(r.dq_low, r.dq_low_o), move.start(r.keep, r.grad_first_o)]
    r.dkv_low[...] = r.dkv[...].astype(bf16)
    outs += [move.start(r.dkv_low, r.dkv_o)]
    part = dot_nt(r.dkv_low[...], r.w_pair[...])
    r.part_other[...] = part[length:, :].astype(bf16)
    r.part_own[...] = part[:length, :]
    outs += [move.start(r.part_other, r.part_other_o), move.start(r.part_own, r.part_own_o)]
    wait_all(outs)


def feed_backward_alone(r):
    move = Copies(r.sems)
    early = [
        move.start(r.grad_memory_h, r.cot),
        move.start(r.unit2_h, r.unit2),
        move.start(r.inv2_h, r.inv2),
    ]
    later = [
        move.start(r.w_down_h, r.w_down),
        move.start(r.slope_h, r.slope),
        move.start(r.w_in_h, r.w_in),
    ]
    wait_all(early)
    grad_third, gain_late = standardize_back(
        r.cot[...].astype(f32), r.unit2[...], r.gains[1:2, :], r.inv2[:, 0:1]
    )
    r.gain_grads[...] = jnp.broadcast_to(gain_late, r.gain_grads.shape)
    r.keep[...] = grad_third
    r.down_grad[...] = grad_third.astype(bf16)
    outs = [move.start(r.down_grad, r.down_grad_o), move.start(r.gain_grads, r.gain_late_o)]
    wait_all(later)
    feed_backward(r)
    outs += [move.start(r.up_grad, r.up_grad_o)]
    r.keep[...] += r.sum[...]
    outs += [move.start(r.keep, r.grad_first_o)]
    wait_all(outs)


def self_backward(r, plan):
    r.micro, first, last = plan
    length, width = r.att_h.shape
    decoder, core = r.meta[0], r.meta[1]
    pairs = range(first, last)
    low, high = first * LANES, last * LANES
    move = Copies(r.sems)
    later = [
        move.start(r.q_h, r.q),
        move.start(r.kv_h, r.kv),
        move.start(r.att_h, r.att),
        move.start(r.lse_h, r.lse),
    ]
    if first == 0:
        early = [
            move.start(r.grad_first_h, r.keep),
            move.start(r.unit1_h, r.unit1),
            move.start(r.inv1_h, r.inv1),
            move.start(r.w_out_h, r.w_out),
        ]
    else:
        early = [move.start(r.grad_att_h, r.grad_att)]
    outs = []
    place_documents(r, load_documents(r, move, r.x_own_h, r.x_own_h, r.x_other_h))
    wait_all(early)
    if first == 0:
        grad_sum, gain_early = standardize_back(
            r.keep[...], r.unit1[...], r.gains[0:1, :], r.inv1[:, 0:1]
        )
        r.gain_grads[...] = jnp.broadcast_to(gain_early, r.gain_grads.shape)
        r.keep[...] = grad_sum
        r.branch[...] = grad_sum.astype(bf16)
        r.grad_att[...] = dot_nt(r.branch[...], r.w_out[...]).astype(bf16)
        outs += [move.start(r.gain_grads, r.gain_early_o), move.start(r.branch, r.branch_o)]
        if last < width // LANES:
            outs += [move.start(r.keep, r.grad_sum_o), move.start(r.grad_att, r.grad_att_o)]
    wait_all(later)
    if last == width // LANES:
        ends = [move.start(r.w_mixed_h, r.w_mixed)]
        if first > 0:
            ends += [
                move.start(r.grad_sum_h, r.keep),
                move.start(r.dq_h.at[:, pl.ds(0, low)], r.dq_low.at[:, pl.ds(0, low)]),
                move.start(r.dkv_h.at[:, pl.ds(0, low)], r.dkv_low.at[:, pl.ds(0, low)]),
                move.start(
                    r.dkv_h.at[:, pl.ds(width, low)], r.dkv_low.at[:, pl.ds(width, low)]
                ),
            ]
    spread_pairs(r.qm, r.q, 64**-0.5, pairs)
    turn_tiles(r.kt, r.kv, 0, pairs)
    spread_pairs(r.gm, r.grad_att, 1.0, pairs)
    row_products(r, r.grad_att, pairs)
    attention_backward(r, core, decoder, pairs)
    r.dq_low[:, low:high] = r.dq[:, low:high].astype(bf16)
    for start in (0, width):
        span = slice(start + low, start + high)
        r.dkv_low[:, span] = r.dkv[:, span].astype(bf16)
    if last == width // LANES:
        wait_all(ends)
        outs += [move.start(r.dq_low, r.dq_low_o), move.start(r.dkv_low, r.dkv_o)]
        r.keep[...] += dot_nt(r.dq_low[...], r.w_mixed[:, :width])
        part = dot_nt(r.dkv_low[...], r.w_mixed[:, width:])
        r.part_other[...] = part[length:, :].astype(bf16)
        r.keep[...] += part[:length, :]
        outs += [move.start(r.part_other, r.part_other_o), move.start(r.keep, r.part_own_o)]
    else:
        outs.append(move.start(r.dq_low.at[:, pl.ds(low, high - low)], r.dq_low_o.at[:, pl.ds(low, high - low)]))
        for start in (0, width):
            span = pl.ds(start + low, high - low)
            outs.append(move.start(r.dkv_low.at[:, span], r.dkv_o.at[:, span]))
    wait_all(outs)


def contract_blocks(r, plan):
    for core in range(2):

        @pl.when(r.meta[1] == core)
        def _(core=core):
            targets = [None] * 4
            for half in range(2):
                target = r.kept_o if half == core else r.sent_o
                targets[2 * half], targets[2 * half + 1] = target.at[0], target.at[1]
            order = (0, 1, 2, 3) if core else (2, 3, 0, 1)
            contract_in_order(r, plan(r), order, targets, Copies(r.sems))


def contract_in_order(r, blocks, order, targets, move):
    loads = dict()
    for slot in order:
        for buffer, sources, at in blocks[slot][1:]:
            if (id(buffer), at) not in loads:
                span = pl.ds(at * CHUNK, CHUNK)
                row = 0
                copies = []
                for source in sources:
                    rows = pl.ds(row, source.shape[0])
                    copies.append(move.start(source.at[:, span], buffer.at[rows, span]))
                    row += source.shape[0]
                loads[id(buffer), at] = copies
    outs = []
    held = dict()
    for slot in order:
        turn, (left, _, left_at), (right, _, right_at) = blocks[slot]
        wait_all(loads.pop((id(left), left_at), ()))
        wait_all(loads.pop((id(right), right_at), ()))
        if held.get(id(turn)) != left_at:
            for row in range(0, left.shape[0], CHUNK):
                block = left[row : row + CHUNK, left_at * CHUNK : (left_at + 1) * CHUNK]
                turn[:, row : row + CHUNK] = jnp.transpose(block)
            held[id(turn)] = left_at
        block = right[:, right_at * CHUNK : (right_at + 1) * CHUNK]
        r.blocks[slot] = dot(turn[:, : right.shape[0]], block).astype(bf16)
        outs.append(move.start(r.blocks.at[slot], targets[slot]))
    wait_all(outs)


def spread_pieces(r, targets):
    z = r.meta[3]
    group, height = r.own_h.shape[:2]
    rows = r.own_h.shape[2] // group
    for core in range(2):
        for x in range(2):

            @pl.when((r.meta[1] == core) & (r.meta[2] == x))
            def _(core=core, x=x):
                move = Copies(r.sems)
                parts = [
                    (r.own_h, core, x),
                    (r.own_x_h, core, 1 - x),
                    (r.other_h, 1 - core, x),
                    (r.other_x_h, 1 - core, 1 - x),
                ]
                loads = [
                    move.start(source, r.pieces.at[place])
                    for place, (source, _, _) in enumerate(parts)
                ]
                outs = []
                slot = 0
                gains = None
                for place, (_, half, side) in enumerate(parts):
                    loads[place].wait()
                    for step in range(group):
                        row = pl.multiple_of(lax.rem(z + (group - step), group) * rows, rows)
                        start = 0
                        for target in targets(r, 2 * half + side, row, rows):
                            r.wide[slot] = r.pieces[place, step, start : start + rows].astype(f32)
                            outs.append(move.start(r.wide.at[slot], target))
                            slot += 1
                            start += rows
                        if start < height:
                            extra = r.pieces[place, step, start:height].astype(f32)
                            gains = extra if gains is None else gains + extra
                if gains is not None:
                    r.gains_o[...] = gains[: r.gains_o.shape[0], :]
                wait_all(outs)


def launch(kernel, plan, side, scalars, small, large, outs, scratch, copies, work, previous=None, after=()):
    names = list(scalars) + list(small) + list(large)
    arrays = list(scalars.values()) + list(small.values()) + list(large.values())
    specs = (
        [pl.BlockSpec(memory_space=pltpu.SMEM)] * len(scalars)
        + [pl.BlockSpec(memory_space=pltpu.VMEM)] * len(small)
        + [pl.BlockSpec(memory_space=pl.ANY)] * len(large)
    )
    aliases = dict()
    for position, name in enumerate(outs):
        if previous and name in previous:
            aliases[len(arrays)] = position
            names.append("previous_" + name)
            arrays.append(previous[name])
            specs.append(pl.BlockSpec(memory_space=pl.ANY))
    for array in after:
        names.append("")
        arrays.append(array)
        specs.append(pl.BlockSpec(memory_space=pl.ANY))
    names += list(outs) + list(scratch) + ["sems"]

    def body(*refs):
        r = types.SimpleNamespace(**dict(zip(names, refs)))

        def run():
            if isinstance(plan, int):
                r.micro = plan
                kernel(r)
            else:
                kernel(r, plan)

        if side is None:
            run()
        else:
            pl.when(r.meta[0] == side)(run)

    results = pl.pallas_call(
        body,
        out_shape=[jax.ShapeDtypeStruct(*shape) for shape in outs.values()],
        in_specs=specs,
        out_specs=[
            pl.BlockSpec(memory_space=pltpu.VMEM if shape[0][0] < 8 else pl.ANY)
            for shape in outs.values()
        ],
        scratch_shapes=[
            pltpu.SMEM(*shape) if shape[1] == jnp.int32 else pltpu.VMEM(*shape)
            for shape in scratch.values()
        ]
        + [pltpu.SemaphoreType.DMA((copies,))],
        input_output_aliases=aliases,
        compiler_params=pltpu.CompilerParams(vmem_limit_bytes=58 * 1024 * 1024),
        cost_estimate=pl.CostEstimate(
            flops=work * 10**9, bytes_accessed=1 << 20, transcendentals=0
        ),
    )(*arrays)
    return types.SimpleNamespace(**dict(zip(outs, results)))


def attention_scratch(length, width):
    pairs, q_tiles, k_tiles = width // LANES, length // TILE, 2 * length // TILE
    return dict(
        q=((length, width), bf16),
        kv=((2 * length, 2 * width), bf16),
        qm=((pairs, q_tiles, 2 * TILE, LANES), bf16),
        kdc=((2 * length, LANES), f32),
        docs=((3, 16, width), bf16),
        qd=((length // TILE, 8, TILE), f32),
        bounds=((2, 3 * length // TILE), jnp.int32),
        bias=((TILE, TILE), f32),
        lse=((q_tiles, 8, 2 * TILE), f32),
        att=((length, width), bf16),
        turned=((width, TILE), f32),
    )


def forward_scratch(length, width):
    k_tiles = 2 * length // TILE
    return dict(
        vt=((k_tiles, width, TILE), bf16),
        top=((8, 2 * TILE), f32),
        total=((8, 2 * TILE), f32),
    )


def backward_scratch(length, width):
    pairs, q_tiles, k_tiles = width // LANES, length // TILE, 2 * length // TILE
    return dict(
        kt=((k_tiles, width, TILE), bf16),
        gm=((pairs, q_tiles, 2 * TILE, LANES), bf16),
        delta=((q_tiles, 8, 2 * TILE), f32),
        dkv=((2 * length, 2 * width), f32),
        dq=((length, width), f32),
        dkv_low=((2 * length, 2 * width), bf16),
        part_other=((length, width), bf16),
        dq_low=((length, width), bf16),
    )


def for_sending(shard):

    def short(part):
        return part.astype(jnp.bfloat16) if part.dtype == jnp.float32 else part

    return jax.tree.map(short, shard)


def from_behind(block, axis, distance):
    devices = range(lax.axis_size(axis))
    route = [(i - distance, i) for i in devices if i - distance in devices]
    return lax.ppermute(block, axis, route)


def from_root(shard, axis, root):
    mine = lax.axis_index(axis) == root
    return lax.psum(jnp.where(mine, shard, jnp.zeros_like(shard)), axis)


def matmul(left_side, right_side):
    return jnp.einsum("rsd,de->rse", left_side, right_side, preferred_element_type=jnp.float32)


def matmul_back(left_side, right_side):
    return jnp.einsum("rse,de->rsd", left_side, right_side, preferred_element_type=jnp.float32)


def contract(left_side, right_side):
    return jnp.einsum("rsd,rse->de", left_side, right_side, preferred_element_type=jnp.float32)


def normalize(values, gain_row):
    center = values - jnp.mean(values, axis=-1, keepdims=True)
    inverse = lax.rsqrt(jnp.mean(center * center, axis=-1, keepdims=True) + epsilon)
    standard = center * inverse
    return (standard * gain_row, standard, inverse)


def normalize_back(grad_out, standard, gain_row, inverse):
    scaled = grad_out * gain_row
    grad_in = inverse * (
        scaled
        - jnp.mean(scaled, axis=-1, keepdims=True)
        - standard * jnp.mean(scaled * standard, axis=-1, keepdims=True)
    )
    return (grad_in, jnp.sum(grad_out * standard, axis=(0, 1)))


def allowed_mask(query_docs, key_docs, query_place, key_place, causal):
    same_doc = query_docs[:, :, None] == key_docs[:, None, :]
    earlier = query_place[:, None] >= key_place[None, :]
    return (same_doc & (earlier | jnp.logical_not(causal)))[:, None]


def attend(queries, keys_local, values_local, query_docs, key_docs, causal, is_cross):
    rows_here, shard_len, model_width = queries.shape
    head_dim = model_width // HEADS
    score_scale = head_dim ** (-0.5)
    query_place = lax.axis_index("seq") * shard_len + jnp.arange(shard_len)
    query_heads = queries.reshape(rows_here, shard_len, HEADS, head_dim)

    def absorb(state_tuple, pieces):
        running_top, running_total, running_sum = state_tuple
        key_piece, value_piece, doc_piece = pieces
        piece_len = key_piece.shape[1]
        raw_scores = jnp.einsum(
            "rqhd,rkhd->rhqk",
            query_heads,
            key_piece.reshape(rows_here, piece_len, HEADS, head_dim),
            preferred_element_type=jnp.float32,
        )
        allowed = allowed_mask(query_docs, doc_piece, query_place, jnp.arange(piece_len), causal)
        scores = jnp.where(allowed, raw_scores * score_scale, negative_big)
        new_top = jnp.maximum(running_top, jnp.max(scores, axis=-1))
        weights = jnp.where(allowed, jnp.exp(scores - new_top[..., None]), 0.0)
        new_total = jnp.sum(weights, axis=-1)
        product = jnp.einsum(
            "rhqk,rkhd->rhqd",
            weights.astype(jnp.bfloat16),
            value_piece.reshape(rows_here, piece_len, HEADS, head_dim),
            preferred_element_type=jnp.float32,
        )
        return (new_top, new_total, product)

    init_state = (
        jnp.full((rows_here, HEADS, shard_len), negative_big, jnp.float32),
        jnp.zeros((rows_here, HEADS, shard_len), jnp.float32),
        jnp.zeros((rows_here, HEADS, shard_len, head_dim), jnp.float32),
    )
    if is_cross:
        final_top, final_total, final_sum = absorb(
            init_state,
            (
                lax.all_gather(keys_local, "seq", axis=1, tiled=True),
                lax.all_gather(values_local, "seq", axis=1, tiled=True),
                lax.all_gather(for_sending(key_docs), "seq", axis=1, tiled=True),
            ),
        )
    else:
        final_top, final_total, final_sum = absorb(
            init_state,
            (
                lax.all_gather(keys_local, "seq", axis=1, tiled=True),
                lax.all_gather(values_local, "seq", axis=1, tiled=True),
                lax.all_gather(key_docs, "seq", axis=1, tiled=True),
            ),
        )
    attended = (
        (final_sum / final_total[..., None])
        .transpose(0, 2, 1, 3)
        .reshape(rows_here, shard_len, model_width)
    )
    return (attended, final_top + jnp.log(final_total))


def attend_back(
    queries,
    keys_local,
    values_local,
    query_docs,
    key_docs,
    causal,
    log_total,
    grad_attended,
    is_cross,
):
    rows_here, shard_len, model_width = queries.shape
    head_dim = model_width // HEADS
    score_scale = head_dim ** (-0.5)
    query_place = lax.axis_index("seq") * shard_len + jnp.arange(shard_len)
    if is_cross:
        keys_full, values_full, docs_full = (
            lax.all_gather(keys_local, "seq", axis=1, tiled=True),
            lax.all_gather(values_local, "seq", axis=1, tiled=True),
            lax.all_gather(for_sending(key_docs), "seq", axis=1, tiled=True).astype(key_docs.dtype),
        )
    else:
        keys_full, values_full, docs_full = (
            lax.all_gather(keys_local, "seq", axis=1, tiled=True),
            lax.all_gather(values_local, "seq", axis=1, tiled=True),
            lax.all_gather(key_docs, "seq", axis=1, tiled=True),
        )
    full_len = keys_full.shape[1]
    query_heads = queries.reshape(rows_here, shard_len, HEADS, head_dim)
    key_heads = keys_full.reshape(rows_here, full_len, HEADS, head_dim)
    value_heads = values_full.reshape(rows_here, full_len, HEADS, head_dim)
    grad_heads = grad_attended.reshape(rows_here, shard_len, HEADS, head_dim)
    raw_scores = jnp.einsum(
        "rqhd,rkhd->rhqk", query_heads, key_heads, preferred_element_type=jnp.float32
    )
    allowed = allowed_mask(query_docs, docs_full, query_place, jnp.arange(full_len), causal)
    shifted = jnp.where(allowed, raw_scores * score_scale - log_total[..., None], negative_big)
    probs = jnp.where(allowed, jnp.exp(shifted), 0.0)
    grad_probs = jnp.einsum(
        "rqhd,rkhd->rhqk", grad_heads, value_heads, preferred_element_type=jnp.float32
    )
    delta = jnp.sum(probs * grad_probs, axis=-1)
    grad_scores = (probs * (grad_probs - delta[..., None]) * score_scale).astype(jnp.bfloat16)
    grad_queries = jnp.einsum(
        "rhqk,rkhd->rqhd", grad_scores, key_heads, preferred_element_type=jnp.float32
    ).reshape(rows_here, shard_len, model_width)
    probs_low = probs.astype(jnp.bfloat16)

    def key_terms(span):
        grad_keys = jnp.einsum(
            "rhqk,rqhd->krhd", grad_scores, query_heads, preferred_element_type=jnp.float32
        )
        grad_values = jnp.einsum(
            "rhqk,rqhd->krhd", probs_low, grad_heads, preferred_element_type=jnp.float32
        )
        return jnp.concatenate(
            [
                grad_keys.reshape(span, rows_here, model_width),
                grad_values.reshape(span, rows_here, model_width),
            ],
            axis=-1,
        )

    if is_cross:
        pair_terms = lax.psum_scatter(
            key_terms(shard_len * lax.axis_size("seq")).astype(jnp.bfloat16),
            "seq",
            scatter_dimension=0,
            tiled=True,
        ).astype(jnp.float32)
    else:
        pair_terms = lax.psum_scatter(
            key_terms(shard_len * lax.axis_size("seq")).astype(jnp.bfloat16),
            "seq",
            scatter_dimension=0,
            tiled=True,
        ).astype(jnp.float32)
    return (grad_queries, pair_terms.transpose(1, 0, 2))


def layer_forward(hidden_in, doc_own, memory, memory_docs, weights, is_decoder):
    (
        qkv_weight,
        out_weight,
        in_weight,
        down_weight,
        gains_pair,
        query_weight,
        pair_weight,
        cross_weight,
        cross_gains,
    ) = weights
    model_width = hidden_in.shape[-1]
    mixed = matmul(hidden_in, qkv_weight).astype(jnp.bfloat16)
    attended, self_lse = attend(
        mixed[..., :model_width],
        mixed[..., model_width : 2 * model_width],
        mixed[..., 2 * model_width :],
        doc_own,
        doc_own,
        is_decoder,
        False,
    )
    attended = attended.astype(jnp.bfloat16)
    first, first_unit, first_inv = normalize(
        hidden_in.astype(jnp.float32) + matmul(attended, out_weight), gains_pair[0]
    )
    first_low = first.astype(jnp.bfloat16)
    cross_queries = matmul(first_low, query_weight).astype(jnp.bfloat16)
    pair = matmul(memory, pair_weight).astype(jnp.bfloat16)
    cross_att, cross_lse = attend(
        cross_queries,
        pair[..., :model_width],
        pair[..., model_width:],
        doc_own,
        memory_docs,
        False,
        True,
    )
    cross_att = cross_att.astype(jnp.bfloat16)
    second_cross, second_unit, second_inv = normalize(
        first + matmul(cross_att, cross_weight), cross_gains
    )
    second = jnp.where(is_decoder, second_cross, first)
    second_low = second.astype(jnp.bfloat16)
    upward = matmul(second_low, in_weight)
    active = jax.nn.silu(upward).astype(jnp.bfloat16)
    result, third_unit, third_inv = normalize(second + matmul(active, down_weight), gains_pair[1])
    saved = {
        "mixed": mixed,
        "attended": attended,
        "self_lse": self_lse,
        "first_unit": first_unit,
        "first_inv": first_inv,
        "first_low": first_low,
        "cross_queries": cross_queries,
        "pair": pair,
        "cross_att": cross_att,
        "cross_lse": cross_lse,
        "second_unit": second_unit,
        "second_inv": second_inv,
        "second_low": second_low,
        "upward": upward,
        "active": active,
        "third_unit": third_unit,
        "third_inv": third_inv,
    }
    return (result, saved)


def layer_backward(
    grad_result, saved, hidden_in, doc_own, memory, memory_docs, weights, is_decoder
):
    (
        qkv_weight,
        out_weight,
        in_weight,
        down_weight,
        gains_pair,
        query_weight,
        pair_weight,
        cross_weight,
        cross_gains,
    ) = weights
    model_width = hidden_in.shape[-1]
    grad_third, grad_gain_late = normalize_back(
        grad_result, saved["third_unit"], gains_pair[1], saved["third_inv"]
    )
    down_grad = grad_third.astype(jnp.bfloat16)
    grad_down_w = contract(saved["active"], down_grad)
    grad_active = matmul_back(down_grad, down_weight).astype(jnp.bfloat16)
    sigmoid_up = jax.nn.sigmoid(saved["upward"])
    grad_upward = (
        grad_active.astype(jnp.float32)
        * (sigmoid_up + saved["upward"] * sigmoid_up * (1.0 - sigmoid_up))
    ).astype(jnp.bfloat16)
    grad_in_w = contract(saved["second_low"], grad_upward)
    grad_second = grad_third + matmul_back(grad_upward, in_weight)
    grad_cross_sum, grad_cross_gain = normalize_back(
        grad_second, saved["second_unit"], cross_gains, saved["second_inv"]
    )
    decoder_flag = is_decoder.astype(jnp.float32)
    grad_cross_sum = grad_cross_sum * decoder_flag
    grad_cross_gain = grad_cross_gain * decoder_flag
    cross_branch = grad_cross_sum.astype(jnp.bfloat16)
    grad_cross_w = contract(saved["cross_att"], cross_branch)
    grad_cross_att = matmul_back(cross_branch, cross_weight).astype(jnp.bfloat16)
    pair = saved["pair"]
    grad_cross_q, grad_pair = attend_back(
        saved["cross_queries"],
        pair[..., :model_width],
        pair[..., model_width:],
        doc_own,
        memory_docs,
        False,
        saved["cross_lse"],
        grad_cross_att,
        True,
    )
    grad_cross_q = grad_cross_q.astype(jnp.bfloat16)
    grad_pair = grad_pair.astype(jnp.bfloat16)
    grad_query_w = contract(saved["first_low"], grad_cross_q)
    grad_pair_w = contract(memory, grad_pair)
    grad_memory = matmul_back(grad_pair, pair_weight)
    grad_first = jnp.where(
        is_decoder, grad_cross_sum + matmul_back(grad_cross_q, query_weight), grad_second
    )
    grad_first_sum, grad_gain_early = normalize_back(
        grad_first, saved["first_unit"], gains_pair[0], saved["first_inv"]
    )
    self_branch = grad_first_sum.astype(jnp.bfloat16)
    grad_out_w = contract(saved["attended"], self_branch)
    grad_attended = matmul_back(self_branch, out_weight).astype(jnp.bfloat16)
    mixed = saved["mixed"]
    grad_queries, grad_pair_self = attend_back(
        mixed[..., :model_width],
        mixed[..., model_width : 2 * model_width],
        mixed[..., 2 * model_width :],
        doc_own,
        doc_own,
        is_decoder,
        saved["self_lse"],
        grad_attended,
        False,
    )
    grad_mixed = jnp.concatenate([grad_queries, grad_pair_self], axis=-1).astype(jnp.bfloat16)
    grad_qkv_w = contract(hidden_in, grad_mixed)
    grad_hidden = grad_first_sum + matmul_back(grad_mixed, qkv_weight)
    layer_grads = (
        grad_qkv_w,
        grad_out_w,
        grad_in_w,
        grad_down_w,
        jnp.stack([grad_gain_early, grad_gain_late]),
        grad_query_w,
        grad_pair_w,
        grad_cross_w,
        grad_cross_gain,
    )
    return (grad_hidden, grad_memory, layer_grads)


def any_rows(
    layer_input,
    segment_ids,
    attn_qkv,
    attn_out,
    ffn_in,
    ffn_out,
    norm_gain,
    cross_query,
    cross_pair,
    cross_out,
    cross_gain,
    out_cotangent,
):
    micro_count = layer_input.shape[1]
    section_index = lax.axis_index("section")
    is_decoder = section_index == 1
    weights = (
        attn_qkv[0],
        attn_out[0],
        ffn_in[0],
        ffn_out[0],
        norm_gain[0],
        cross_query,
        cross_pair,
        cross_out,
        cross_gain,
    )
    inputs_all = layer_input[0]
    docs_all = segment_ids[0]
    slot_ids = jnp.arange(micro_count)
    received = (jnp.zeros_like(inputs_all[0]), jnp.zeros_like(docs_all[0]))
    results = jnp.zeros_like(inputs_all)
    memories = []
    memory_doc_list = []
    for step_index in range(micro_count + 1):
        batch_index = step_index - section_index
        is_valid = (batch_index >= 0) & (batch_index < micro_count)
        chosen = jnp.clip(batch_index, 0, micro_count - 1)
        hidden_in = lax.dynamic_index_in_dim(inputs_all, chosen, 0, keepdims=False)
        doc_own = lax.dynamic_index_in_dim(docs_all, chosen, 0, keepdims=False)
        memory = received[0]
        memory_docs = jnp.where(is_valid & is_decoder, received[1], doc_own)
        memories.append(memory)
        memory_doc_list.append(memory_docs)
        result, saved = layer_forward(hidden_in, doc_own, memory, memory_docs, weights, is_decoder)
        low_result = result.astype(jnp.bfloat16)
        writing = (slot_ids == chosen) & is_valid
        results = jnp.where(writing[:, None, None, None], low_result[None], results)
        if step_index < micro_count:
            received = from_behind((low_result, doc_own), "section", 1)
    memory_stack = jnp.stack(memories)
    memory_doc_stack = jnp.stack(memory_doc_list)
    totals = tuple((jnp.zeros(weight.shape, jnp.float32) for weight in weights))
    input_grads = jnp.zeros(inputs_all.shape, jnp.float32)
    returned = jnp.zeros(inputs_all.shape[1:], jnp.float32)
    for step_index in range(micro_count + 1):
        batch_index = micro_count - step_index - section_index
        is_valid = (batch_index >= 0) & (batch_index < micro_count)
        chosen = jnp.clip(batch_index, 0, micro_count - 1)
        forward_step = jnp.clip(batch_index + section_index, 0, micro_count)
        hidden_in = lax.dynamic_index_in_dim(inputs_all, chosen, 0, keepdims=False)
        doc_own = lax.dynamic_index_in_dim(docs_all, chosen, 0, keepdims=False)
        memory = lax.dynamic_index_in_dim(memory_stack, forward_step, 0, keepdims=False)
        memory_docs = lax.dynamic_index_in_dim(memory_doc_stack, forward_step, 0, keepdims=False)
        discarded, saved = layer_forward(
            hidden_in, doc_own, memory, memory_docs, weights, is_decoder
        )
        cotangent = jnp.where(
            is_decoder,
            lax.dynamic_index_in_dim(out_cotangent, chosen, 0, keepdims=False).astype(jnp.float32),
            returned,
        )
        grad_hidden, grad_memory, layer_grads = layer_backward(
            cotangent, saved, hidden_in, doc_own, memory, memory_docs, weights, is_decoder
        )
        valid_flag = is_valid.astype(jnp.float32)
        totals = tuple(
            (running + valid_flag * fresh for running, fresh in zip(totals, layer_grads))
        )
        writing = (slot_ids == chosen) & is_valid
        input_grads = jnp.where(writing[:, None, None, None], grad_hidden[None], input_grads)
        if step_index < micro_count:
            returned = from_behind(grad_memory.astype(jnp.bfloat16), "section", -1).astype(
                grad_memory.dtype
            )
    group_sums = lax.psum(
        (
            totals[0],
            totals[1],
            totals[2],
            totals[3],
            totals[4],
            totals[5],
            totals[6],
            totals[7],
            totals[8],
        ),
        ("seq", "dp"),
    )
    section_sums = group_sums[:5]
    cross_sums = (
        from_root(group_sums[5].astype(jnp.bfloat16), "section", 1).astype(jnp.float32),
        from_root(group_sums[6].astype(jnp.bfloat16), "section", 1).astype(jnp.float32),
        from_root(group_sums[7].astype(jnp.bfloat16), "section", 1).astype(jnp.float32),
        from_root(group_sums[8].astype(jnp.bfloat16), "section", 1).astype(jnp.float32),
    )
    return (
        results[None],
        input_grads[None],
        section_sums[0][None],
        section_sums[1][None],
        section_sums[2][None],
        section_sums[3][None],
        section_sums[4][None],
        cross_sums[0],
        cross_sums[1],
        cross_sums[2],
        cross_sums[3],
    )


def split_rows(
    layer_input,
    segment_ids,
    attn_qkv,
    attn_out,
    ffn_in,
    ffn_out,
    norm_gain,
    cross_query,
    cross_pair,
    cross_out,
    cross_gain,
    out_cotangent,
):
    micros = layer_input.shape[1]
    length, width = layer_input.shape[3:]
    hidden = ffn_in.shape[-1]
    q_tiles = length // TILE
    group = lax.axis_size("dp") // 2
    axes = ("section", "seq", "dp")
    decoder = lax.axis_index("section") == 1
    flag = decoder.astype(jnp.int32)
    x = lax.axis_index("seq")
    core = lax.rem(lax.axis_index("dp"), 2)
    z = lax.axis_index("dp") // 2
    places = [(t, i, k, c) for t in range(2) for i in range(2) for k in range(group) for c in range(2)]

    def number(t, i, k, c):
        return ((t * 2 + i) * group + k) * 2 + c

    def send(values, target, section=None):
        route = [
            (number(*place), number(*target(*place)))
            for place in places
            if section in (None, place[0]) and target(*place)
        ]
        return lax.ppermute(values, axes, route)

    def to_core(t, i, k, c):
        return (t, i, k, 1 - c)

    def to_x(t, i, k, c):
        return (t, 1 - i, k, c)

    def to_row(t, i, k, c):
        return (t, c, k, i)

    def to_decoder(t, i, k, c):
        return (1, i, k, c) if t == 0 else None

    def to_encoder(t, i, k, c):
        return (0, i, k, c) if t == 1 else None

    def fence(values, *before):
        return lax.optimization_barrier((values,) + before)[0]

    def exchange(values):
        return send(values, to_core)

    low = ((length, width), bf16)
    wide = ((length, width), f32)
    marked = ((length + 16, width), bf16)
    both = ((2 * length, width), bf16)
    keys_all = ((2 * length, 2 * width), bf16)
    mixing = ((width, 3 * width), bf16)
    inner = ((length, hidden), bf16)
    lse = ((q_tiles, 8, 2 * TILE), f32)
    stat = ((length, LANES), f32)
    square = ((width, width), bf16)
    rising = ((width, hidden), bf16)
    falling = ((hidden, width), bf16)
    gain_rows = ((8, width), f32)

    meta = jnp.stack([flag, core, x, z]).astype(jnp.int32)
    numbers = segment_ids[0, :, 0].astype(bf16)
    padding = jnp.zeros((15, width), bf16)
    with_numbers = [
        jnp.concatenate([layer_input[0, micro, 0], numbers[micro][None], padding])
        for micro in range(micros)
    ]
    own = [send(with_numbers[0], to_row)]
    for micro in range(1, micros):
        own.append(send(fence(with_numbers[micro], own[-1]), to_row))
    other = [exchange(own[0])]

    plain = dict(meta=meta)
    small = dict(gains=norm_gain[0])
    forward, memories, memories_other = [], [], []
    for micro in range(micros):
        call = launch(
            self_forward,
            micro,
            None,
            plain,
            small,
            dict(
                x_own_h=own[micro],
                x_other_h=other[micro],
                w_mixed_h=attn_qkv[0],
                w_out_h=attn_out[0],
                w_in_h=ffn_in[0],
                w_down_h=ffn_out[0],
            ),
            dict(
                q_o=low,
                kv_o=keys_all,
                att_o=low,
                lse_o=lse,
                unit1_o=wide,
                inv1_o=stat,
                first_low_o=low,
                memory_o=marked,
                ffn_low_o=low,
                act_o=inner,
                slope_o=inner,
                unit2_o=wide,
                inv2_o=stat,
            ),
            dict(
                **attention_scratch(length, width),
                **forward_scratch(length, width),
                x=both,
                w_mixed=mixing,
                w_out=square,
                w_in=rising,
                w_down=falling,
                unit1=wide,
                inv1=stat,
                first_low=low,
                memory=marked,
                act=inner,
                slope=inner,
                unit2=wide,
                inv2=stat,
                sum=wide,
            ),
            28,
            26,
            after=(forward[0].lse_o,) if micro else (),
        )
        forward.append(call)
        memories.append(send(call.memory_o, to_decoder))
        if micro + 1 < micros:
            other.append(exchange(fence(own[micro + 1], call.lse_o)))

    for micro in range(micros):
        memories_other.append(exchange(fence(memories[micro], forward[-1].lse_o)))
    cotangent = send(fence(out_cotangent[:, 0], forward[0].lse_o), to_row)

    cross, grads_memory, made = [], [], []
    after = (forward[-1].lse_o,)
    for micro in range(micros):
        done = forward[micro]
        call = launch(
            cross_both_ways,
            micro,
            1,
            plain,
            dict(**small, cross_gain=cross_gain[None]),
            dict(
                x_own_h=own[micro],
                memory_own_h=memories[micro],
                memory_other_h=memories_other[micro],
                w_pair_h=cross_pair,
                first_low_h=done.first_low_o,
                unit1_h=done.unit1_o,
                w_query_h=cross_query,
                w_cross_h=cross_out,
                w_in_h=ffn_in[0],
                w_down_h=ffn_out[0],
                cot_h=cotangent,
            ),
            dict(
                att_o=low,
                ffn_low_o=low,
                act_o=inner,
                decoded_o=low,
                down_grad_o=low,
                up_grad_o=inner,
                gain_grads_o=gain_rows,
                branch_o=low,
                dq_low_o=low,
                dkv_o=keys_all,
                part_own_o=wide,
                part_other_o=low,
                grad_first_o=wide,
            ),
            dict(
                **attention_scratch(length, width),
                **forward_scratch(length, width),
                **backward_scratch(length, width),
                x=both,
                w_pair=((width, 2 * width), bf16),
                first_low=low,
                unit1=wide,
                w_query=square,
                w_cross=square,
                w_in=rising,
                w_down=falling,
                cot=low,
                unit2=wide,
                inv2=stat,
                second_low=low,
                act=inner,
                slope=inner,
                sum=wide,
                decoded=low,
                keep=wide,
                down_grad=low,
                up_grad=inner,
                gain_grads=gain_rows,
                branch=low,
                part_own=wide,
            ),
            36,
            44,
            dict(act_o=done.act_o, ffn_low_o=done.ffn_low_o),
            after,
        )
        cross.append(call)
        away = call.part_other_o
        if micro:
            away = fence(away, grads_memory[-1])
        total = call.part_own_o + exchange(away).astype(f32)
        made.append(total.astype(bf16))
        after = (made[micro],)
        grads_memory.append(send(made[micro], to_encoder))

    def backward_feed(micro, after):
        done, late = forward[micro], cross[micro]
        return launch(
            feed_backward_alone,
            micro,
            0,
            plain,
            dict(gains=norm_gain[0]),
            dict(
                grad_memory_h=grads_memory[micro],
                unit2_h=done.unit2_o,
                inv2_h=done.inv2_o,
                slope_h=done.slope_o,
                w_in_h=ffn_in[0],
                w_down_h=ffn_out[0],
            ),
            dict(gain_late_o=gain_rows, down_grad_o=low, up_grad_o=inner, grad_first_o=wide),
            dict(
                cot=low,
                unit2=wide,
                inv2=stat,
                slope=inner,
                w_in=rising,
                w_down=falling,
                gain_grads=gain_rows,
                keep=wide,
                down_grad=low,
                up_grad=inner,
                sum=wide,
            ),
            12,
            10,
            dict(
                down_grad_o=late.down_grad_o, up_grad_o=late.up_grad_o, grad_first_o=late.grad_first_o
            ),
            after,
        )

    def backward_self(micro, side, grad_first, previous=None, after=(), halfway=None):
        done = forward[micro]
        heads = width // LANES
        given = dict(
            x_own_h=own[micro],
            x_other_h=other[micro],
            q_h=done.q_o,
            kv_h=done.kv_o,
            att_h=done.att_o,
            lse_h=done.lse_o,
        )
        ahead = dict(
            grad_first_h=grad_first,
            unit1_h=done.unit1_o,
            inv1_h=done.inv1_o,
            w_out_h=attn_out[0],
        )
        makes = dict(dq_low_o=low, dkv_o=keys_all)
        makes_first = dict(gain_early_o=gain_rows, branch_o=low)
        makes_last = dict(part_own_o=wide, part_other_o=low)
        scratch = dict(
            **attention_scratch(length, width),
            **backward_scratch(length, width),
            w_out=square,
            w_mixed=mixing,
            unit1=wide,
            inv1=stat,
            keep=wide,
            branch=low,
            grad_att=low,
            gain_grads=gain_rows,
        )

        def part(first, last, large, outs, work, previous, after):
            return launch(
                self_backward,
                (micro, first, last),
                side,
                plain,
                small,
                dict(**given, **large),
                dict(**makes, **outs),
                scratch,
                28,
                work,
                previous,
                after,
            )

        if halfway is None:
            large = dict(**ahead, w_mixed_h=attn_qkv[0])
            outs = dict(**makes_first, **makes_last)
            return part(0, heads, large, outs, 22, previous, after)
        outs = dict(**makes_first, grad_sum_o=wide, grad_att_o=low)
        one = part(0, heads // 2, ahead, outs, 12, None, after)
        large = dict(
            w_mixed_h=attn_qkv[0],
            grad_sum_h=one.grad_sum_o,
            grad_att_h=one.grad_att_o,
            dq_h=one.dq_low_o,
            dkv_h=one.dkv_o,
        )
        two = part(heads // 2, heads, large, makes_last, 12, None, halfway(one))
        return types.SimpleNamespace(**{**vars(one), **vars(two)})

    def weight_grads(plan, side, arrays, scratch, after=()):
        blocks = ((2, width, width), bf16)
        call = launch(
            contract_blocks,
            plan,
            side,
            plain,
            dict(),
            arrays,
            dict(sent_o=blocks, kept_o=blocks),
            dict(**scratch, blocks=((4, width, width), bf16)),
            36,
            8,
            after=after,
        )
        return call.sent_o, call.kept_o

    def first_sums(halves, section=None):
        sent, kept = halves
        got = send(sent, to_core, section)

        def block(side):
            return sum(
                lax.dynamic_index_in_dim(part, side, 0, keepdims=False).astype(f32)
                for part in (kept, got)
            )

        return block(1 - x).astype(bf16), block(x)

    def middle_sums(sums, section=None):
        away, total = sums
        return (total + send(away, to_x, section).astype(f32)).astype(bf16)

    def last_sums(totals, *later):
        rows = width // group
        shares = jnp.concatenate([total.reshape(group, rows, width) for total in totals], axis=1)

        def share(step):
            return lax.dynamic_index_in_dim(shares, lax.rem(z + step, group), 0, keepdims=False)

        parts = [share(0)]
        for step in range(1, group):
            parts.append(send(share(step), along_z(step)))
        if later:
            parts = [fence(part, *later) for part in parts]
        return sum(part.astype(f32) for part in parts).astype(bf16)

    def along_z(step):
        return lambda t, i, k, c: (t, i, (k + step) % group, c)

    def gather_z(share):
        return [share] + [send(share, along_z(step)) for step in range(1, group)]

    def gain_block(rows):
        filled = jnp.concatenate([jnp.stack(rows), jnp.zeros((16 - len(rows), width), f32)])
        return filled.astype(bf16)

    def spread(targets, own, own_x, outs, parts, after=()):
        return launch(
            spread_pieces,
            targets,
            None,
            plain,
            dict(),
            dict(own_h=own, own_x_h=own_x, other_h=exchange(own), other_x_h=exchange(own_x)),
            outs,
            dict(
                pieces=((4,) + own.shape, bf16),
                wide=((4 * group * parts, width // group, width), f32),
            ),
            8 + 4 * group * parts,
            5,
            after=after,
        )

    tokens, all_tokens = micros * length, 2 * micros * length
    turn, turn_all = ((width, tokens), bf16), ((width, all_tokens), bf16)
    narrow, narrow_all = ((tokens, width), bf16), ((all_tokens, width), bf16)
    pair_all = ((all_tokens, 2 * width), bf16)
    deep = ((tokens, hidden), bf16)

    def part_of(buffer, *sources):
        return lambda column: (buffer, sources, column)

    def key_rows(buffer, sources):
        first, second = pl.ds(0, length), pl.ds(length, length)
        return part_of(buffer, *[source.at[rows] for rows in (first, second) for source in sources])

    def cross_plan(r):
        rows = pl.ds(0, length)
        low_part = part_of(r.low, r.low0_h, r.low1_h)
        att_part = part_of(r.att, r.att0_h, r.att1_h)
        dq_part = part_of(r.dq, r.dq0_h, r.dq1_h)
        branch_part = part_of(r.branch, r.branch0_h, r.branch1_h)
        sources = (r.mem0_h, r.mem1_h, r.mem2_h, r.mem3_h)
        mem_part = part_of(r.mem, *[source.at[rows] for source in sources])
        pair_part = key_rows(r.pair, (r.pair0_h, r.pair1_h))
        return [
            (r.turn, low_part(0), dq_part(0)),
            (r.turn_att, att_part(0), branch_part(0)),
            (r.turn_all, mem_part(0), pair_part(0)),
            (r.turn_all, mem_part(0), pair_part(1)),
        ]

    def rising_plan(r):
        low_part = part_of(r.low, r.low0_h, r.low1_h)
        up_part = part_of(r.up, r.up0_h, r.up1_h)
        return [(r.turn, low_part(0), up_part(block)) for block in range(4)]

    def falling_plan(r):
        act_part = part_of(r.act, r.act0_h, r.act1_h)
        down_part = part_of(r.down, r.down0_h, r.down1_h)
        return [(r.turn, act_part(block), down_part(0)) for block in range(4)]

    def self_plan(r):
        rows = pl.ds(0, length)
        sources = (r.x0_h, r.x1_h, r.x2_h, r.x3_h)
        x_part = part_of(r.x, *[source.at[rows] for source in sources])
        dq_part = part_of(r.dq, r.dq0_h, r.dq1_h)
        pair_part = key_rows(r.pair, (r.pair0_h, r.pair1_h))
        att_part = part_of(r.att, r.att0_h, r.att1_h)
        branch_part = part_of(r.branch, r.branch0_h, r.branch1_h)
        return [
            (r.turn_all, x_part(0), dq_part(0)),
            (r.turn_all, x_part(0), pair_part(0)),
            (r.turn_all, x_part(0), pair_part(1)),
            (r.turn, att_part(0), branch_part(0)),
        ]

    last = micros - 1
    feeds, ends = [None] * micros, [None] * micros
    cross_halves = weight_grads(
        cross_plan,
        1,
        dict(
            low0_h=forward[0].first_low_o,
            low1_h=forward[1].first_low_o,
            dq0_h=cross[0].dq_low_o,
            dq1_h=cross[1].dq_low_o,
            att0_h=cross[0].att_o,
            att1_h=cross[1].att_o,
            branch0_h=cross[0].branch_o,
            branch1_h=cross[1].branch_o,
            mem0_h=memories[0],
            mem1_h=memories[1],
            mem2_h=memories_other[0],
            mem3_h=memories_other[1],
            pair0_h=cross[0].dkv_o,
            pair1_h=cross[1].dkv_o,
        ),
        dict(
            low=narrow,
            dq=narrow,
            att=narrow,
            branch=narrow,
            mem=narrow_all,
            pair=pair_all,
            turn=turn,
            turn_att=turn,
            turn_all=turn_all,
        ),
        (made[last],),
    )
    cross_sums = first_sums(cross_halves, 1)
    results = jnp.stack(
        [
            jnp.where(decoder, call.decoded_o, done.memory_o[:length])
            for call, done in zip(cross, forward)
        ]
    )
    results = send(results, to_row)
    latest = made[last]

    def part_sum(micro, *before):
        end = ends[micro]
        away = fence(end.part_other_o, *before)
        total = (end.part_own_o + exchange(away).astype(f32)).astype(bf16)
        return total, send(total, to_row)

    steps = []
    for micro in range(last):
        feeds[micro] = backward_feed(micro, (latest,))
        first = feeds[micro].grad_first_o
        ends[micro] = backward_self(micro, 0, first)
        ends[micro] = backward_self(micro, 1, first, vars(ends[micro]), (cross_sums[0], grads_memory[last]))
        cross_total = middle_sums(cross_sums, 1)
        steps.append(part_sum(micro, cross_total))
        latest = ends[micro].gain_early_o
    feeds[last] = backward_feed(last, (latest,))

    rising_halves = weight_grads(
        rising_plan,
        None,
        dict(
            low0_h=cross[0].ffn_low_o,
            low1_h=cross[1].ffn_low_o,
            up0_h=feeds[0].up_grad_o,
            up1_h=feeds[1].up_grad_o,
        ),
        dict(low=narrow, up=deep, turn=turn),
        (results,) + tuple(step[0] for step in steps),
    )
    rising_sums = first_sums(rising_halves)
    rising_total = middle_sums(rising_sums)
    falling_halves = weight_grads(
        falling_plan,
        None,
        dict(
            act0_h=cross[0].act_o,
            act1_h=cross[1].act_o,
            down0_h=feeds[0].down_grad_o,
            down1_h=feeds[1].down_grad_o,
        ),
        dict(act=deep, down=narrow, turn=turn),
        (rising_sums[0],),
    )
    falling_sent = fence(falling_halves[0], rising_total)
    falling_sums = first_sums((falling_sent, falling_halves[1]))
    falling_total = middle_sums(falling_sums)
    shares = []

    third = sum(call.gain_grads_o[1] for call in cross)

    def halfway(one):
        both = last_sums((rising_total, cross_total), one.gain_early_o)
        rows = width // group
        found = jnp.concatenate([both[rows:], gain_block([third])])
        shares.extend([both[:rows], found, send(found, to_encoder)])
        return (both, falling_total)

    ends[last] = backward_self(
        last,
        None,
        feeds[last].grad_first_o,
        None,
        (falling_sums[0],),
        halfway,
    )
    finished = ends[last].part_own_o
    falling_share = last_sums((falling_total,), ends[last].gain_early_o, finished)
    rising_share, found, arrived = shares
    cross_share = jnp.where(decoder, found, fence(arrived, finished))
    rising_own = gather_z(rising_share)
    one_own = gather_z(jnp.concatenate([falling_share, cross_share]))
    steps.append(part_sum(last, falling_share, arrived, steps[0][1]))

    self_halves = weight_grads(
        self_plan,
        None,
        dict(
            x0_h=own[0],
            x1_h=own[1],
            x2_h=other[0],
            x3_h=other[1],
            dq0_h=ends[0].dq_low_o,
            dq1_h=ends[1].dq_low_o,
            pair0_h=ends[0].dkv_o,
            pair1_h=ends[1].dkv_o,
            att0_h=forward[0].att_o,
            att1_h=forward[1].att_o,
            branch0_h=ends[0].branch_o,
            branch1_h=ends[1].branch_o,
        ),
        dict(
            x=narrow_all,
            dq=narrow,
            pair=pair_all,
            att=narrow,
            branch=narrow,
            turn=turn,
            turn_all=turn_all,
        ),
        (steps[last][0],),
    )
    away, total = first_sums(
        (fence(self_halves[0], *rising_own[1:], steps[last][1]), self_halves[1])
    )
    arrived = fence(send(away, to_x), one_own[1], one_own[-1])
    self_total = (total + arrived.astype(f32)).astype(bf16)
    rising_own = jnp.stack(rising_own)
    rising_own_x = send(fence(rising_own, self_total), to_x)
    self_share = last_sums((self_total,))
    one_own = jnp.stack([one_own[0]] + [fence(part, self_share, rising_own_x) for part in one_own[1:]])
    one_own_x = send(one_own, to_x)

    early = sum(end.gain_early_o[0] for end in ends)
    late = jnp.where(
        decoder,
        sum(call.gain_grads_o[0] for call in cross),
        sum(call.gain_late_o[0] for call in feeds),
    )
    two_own = jnp.stack(
        gather_z(jnp.concatenate([self_share, gain_block([early, late])]))
    )
    two_own_x = send(fence(two_own, one_own_x), to_x)

    def columns(block):
        return pl.ds(block * width, width)

    def rising_targets(r, block, row, rows):
        return [r.up_o.at[pl.ds(row, rows), columns(block)]]

    def one_targets(r, block, row, rows):
        lines = pl.ds(row, rows)
        falling = r.down_o.at[pl.ds(block * width + row, rows)]
        if block >= 2:
            return [falling, r.pair_o.at[lines, columns(block - 2)]]
        return [falling, (r.out_o if block else r.query_o).at[lines]]

    def two_targets(r, block, row, rows):
        lines = pl.ds(row, rows)
        return [r.out_o.at[lines] if block == 3 else r.mixed_o.at[lines, columns(block)]]

    square_out = ((width, width), f32)
    rising_grads = spread(
        rising_targets,
        rising_own,
        fence(rising_own_x, self_total),
        dict(up_o=((width, hidden), f32)),
        1,
    )
    one_own_x = fence(one_own_x, two_own)
    one_grads = spread(
        one_targets,
        one_own,
        one_own_x,
        dict(
            query_o=square_out,
            pair_o=((width, 2 * width), f32),
            down_o=((hidden, width), f32),
            out_o=square_out,
            gains_o=((1, width), f32),
        ),
        2,
        (rising_grads.up_o,),
    )
    two_own_x = fence(two_own_x, one_grads.gains_o)
    two_grads = spread(
        two_targets,
        two_own,
        two_own_x,
        dict(
            mixed_o=((width, 3 * width), f32),
            out_o=square_out,
            gains_o=((2, width), f32),
        ),
        1,
    )

    grad_input = jnp.stack([step[1] for step in steps])
    return (
        results[None, :, None],
        grad_input.astype(f32)[None, :, None],
        two_grads.mixed_o[None],
        two_grads.out_o[None],
        rising_grads.up_o[None],
        one_grads.down_o[None],
        two_grads.gains_o[None],
        one_grads.query_o,
        one_grads.pair_o,
        one_grads.out_o,
        one_grads.gains_o[0],
    )


def shards(*arrays):
    layer_input = arrays[0]
    micros, rows, length = layer_input.shape[1:4]
    simple = (
        lax.axis_size("section") == 2
        and lax.axis_size("seq") == 2
        and lax.axis_size("dp") in (4, 8, 16)
        and (micros, rows) == (2, 1)
        and length == layer_input.shape[-1] == CHUNK
        and arrays[4].shape[-1] == 4 * CHUNK
    )
    return split_rows(*arrays) if simple else any_rows(*arrays)


def solution(mesh):
    in_specs = (
        P("section", None, "dp", "seq", None),
        P("section", None, "dp", "seq"),
        P("section", None, None),
        P("section", None, None),
        P("section", None, None),
        P("section", None, None),
        P("section", None, None),
        P(),
        P(),
        P(),
        P(),
        P(None, "dp", "seq", None),
    )
    out_specs = (
        P("section", None, "dp", "seq", None),
        P("section", None, "dp", "seq", None),
        P("section", None, None),
        P("section", None, None),
        P("section", None, None),
        P("section", None, None),
        P("section", None, None),
        P(),
        P(),
        P(),
        P(),
    )
    return jax.shard_map(shards, mesh=mesh, in_specs=in_specs, out_specs=out_specs, check_vma=False)
```

```python
import types

import jax
import jax.numpy as jnp
from jax import lax
from jax.experimental import pallas as pl
from jax.experimental.pallas import tpu as pltpu
from jax.sharding import PartitionSpec as P

HEADS = 8
TILE = 256
LANES = 128
CHUNK = 512

f32 = jnp.float32
bf16 = jnp.bfloat16
negative_big = -1e30
epsilon = 1e-05


def dot(left, right):
    return lax.dot_general(left, right, (((1,), (0,)), ((), ())), preferred_element_type=f32)


def dot_nt(left, right):
    return lax.dot_general(left, right, (((1,), (1,)), ((), ())), preferred_element_type=f32)


def dot_tn(left, right):
    return lax.dot_general(left, right, (((0,), (0,)), ((), ())), preferred_element_type=f32)


def standardize(values):
    center = values - jnp.mean(values, axis=-1, keepdims=True)
    inverse = lax.rsqrt(jnp.mean(center * center, axis=-1, keepdims=True) + epsilon)
    return center * inverse, inverse


def standardize_back(grad_out, standard, gain_row, inverse):
    scaled = grad_out * gain_row
    grad_in = inverse * (
        scaled
        - jnp.mean(scaled, axis=-1, keepdims=True)
        - standard * jnp.mean(scaled * standard, axis=-1, keepdims=True)
    )
    return grad_in, jnp.sum(grad_out * standard, axis=0, keepdims=True)


class Copies:
    def __init__(self, sems):
        self.sems = sems
        self.used = 0

    def start(self, source, target):
        copy = pltpu.make_async_copy(source, target, self.sems.at[self.used])
        self.used += 1
        copy.start()
        return copy


def wait_all(copies):
    for copy in copies:
        copy.wait()


def spread_pairs(target, source, factor, pairs):
    tiles = target.shape[1]
    half = lax.broadcasted_iota(jnp.int32, (TILE, LANES), 1) < LANES // 2
    first = jnp.where(half, factor, 0.0).astype(bf16)
    second = jnp.where(half, 0.0, factor).astype(bf16)
    for tile in range(tiles):
        for pair in pairs:
            block = source[tile * TILE : (tile + 1) * TILE, pair * LANES : (pair + 1) * LANES]
            target[pair, tile, :TILE, :] = block * first
            target[pair, tile, TILE:, :] = block * second


def turn_tiles(target, source, column, pairs):
    low, high = pairs[0] * LANES, (pairs[-1] + 1) * LANES
    for tile in range(target.shape[0]):
        block = source[tile * TILE : (tile + 1) * TILE, column + low : column + high]
        target[tile, low:high, :] = jnp.transpose(block)


def place_documents(r, copies):
    wait_all(copies)
    q_tiles = r.qd.shape[0]
    for part in range(3):
        row = r.docs[part].astype(f32)[0:1, :]
        for tile in range(q_tiles):
            piece = row[:, tile * TILE : (tile + 1) * TILE]
            slot = part * q_tiles + tile
            r.bounds[0, slot] = jnp.min(piece).astype(jnp.int32)
            r.bounds[1, slot] = jnp.max(piece).astype(jnp.int32)
            if part == 0:
                r.qd[tile] = jnp.broadcast_to(piece, (8, TILE))
        if part > 0:
            for start in range(0, row.shape[1], LANES):
                block = jnp.broadcast_to(row[:, start : start + LANES], (LANES, LANES))
                place = (part - 1) * row.shape[1] + start
                r.kdc[place : place + LANES, :] = jnp.transpose(block)


def load_documents(r, move, queries, own, other):
    rows = pl.ds(r.docs.shape[2], r.docs.shape[1])
    return [
        move.start(source.at[rows], r.docs.at[part])
        for part, source in enumerate((queries, own, other))
    ]


def tile_place(r, core, causal, q_tile, k_tile):
    q_tiles = r.qd.shape[0]
    length = q_tiles * TILE
    owner = jnp.where(k_tile < q_tiles, core, 1 - core)
    k_start = owner * length + lax.rem(k_tile, q_tiles) * TILE
    ahead = core * length + q_tile * TILE - k_start
    ahead = jnp.where(causal == 1, ahead, 2 * length * TILE)
    q_low, q_high = r.bounds[0, q_tile], r.bounds[1, q_tile]
    k_low, k_high = r.bounds[0, q_tiles + k_tile], r.bounds[1, q_tiles + k_tile]
    active = (q_low <= k_high) & (k_low <= q_high) & (ahead > -TILE)
    whole = (q_low == k_high) & (k_low == q_high) & (ahead >= TILE)
    return active, whole, ahead


def each_tile(place, body):
    active, whole, ahead = place
    pl.when(active & jnp.logical_not(whole))(lambda: body(ahead))
    pl.when(whole)(lambda: body(None))


def fill_bias(r, q_tile, k_tile, ahead):
    keys = r.kdc[pl.ds(pl.multiple_of(k_tile * TILE, TILE), TILE), :]
    shift = lax.broadcasted_iota(jnp.int32, (TILE, LANES), 0) - lax.broadcasted_iota(
        jnp.int32, (TILE, LANES), 1
    )
    queries = r.qd[q_tile]
    for start in range(0, TILE, LANES):
        same = keys == queries[0:1, start : start + LANES]
        allowed = same & (shift - start <= ahead)
        r.bias[:, start : start + LANES] = jnp.where(allowed, 0.0, negative_big)


def attention_forward(r, core, causal):
    pairs, q_tiles = r.qm.shape[:2]
    k_tiles = r.vt.shape[0]

    def one_query_tile(q_tile, carry):
        r.top[...] = jnp.full(r.top.shape, negative_big, f32)
        r.total[...] = jnp.zeros(r.total.shape, f32)
        r.turned[...] = jnp.zeros(r.turned.shape, f32)

        def one_key_tile(k_tile, inner):
            def one_tile(ahead):
                if ahead is not None:
                    fill_bias(r, q_tile, k_tile, ahead)
                rows = pl.ds(pl.multiple_of(k_tile * TILE, TILE), TILE)

                def raw(pair):
                    keys = r.kv[rows, pair * LANES : (pair + 1) * LANES]
                    return dot_nt(keys, r.qm[pair, q_tile])

                raw_next = raw(0)
                for pair in range(pairs):
                    scores = raw_next
                    if ahead is not None:
                        bias = r.bias[...]
                        scores = scores + jnp.concatenate([bias, bias], axis=1)
                    if pair + 1 < pairs:
                        raw_next = raw(pair + 1)
                    old_top = r.top[pair : pair + 1, :]
                    new_top = jnp.maximum(old_top, jnp.max(scores, axis=0, keepdims=True))
                    weights = jnp.exp(scores - new_top)
                    shrink = jnp.exp(old_top - new_top)
                    r.top[pair : pair + 1, :] = new_top
                    r.total[pair : pair + 1, :] = r.total[
                        pair : pair + 1, :
                    ] * shrink + jnp.sum(weights, axis=0, keepdims=True)
                    low = weights.astype(bf16)
                    for side in range(2):
                        span = slice(side * TILE, (side + 1) * TILE)
                        head = slice((2 * pair + side) * 64, (2 * pair + side + 1) * 64)
                        r.turned[head, :] = r.turned[head, :] * shrink[:, span] + dot(
                            r.vt[k_tile, head, :], low[:, span]
                        )

            each_tile(tile_place(r, core, causal, q_tile, k_tile), one_tile)
            return inner

        lax.fori_loop(0, k_tiles, one_key_tile, 0)
        for pair in range(pairs):
            total = r.total[pair : pair + 1, :]
            r.lse[q_tile, pair : pair + 1, :] = r.top[pair : pair + 1, :] + jnp.log(total)
            share = 1.0 / total
            for side in range(2):
                span = slice(side * TILE, (side + 1) * TILE)
                head = slice((2 * pair + side) * 64, (2 * pair + side + 1) * 64)
                r.turned[head, :] = r.turned[head, :] * share[:, span]
        rows = pl.ds(pl.multiple_of(q_tile * TILE, TILE), TILE)
        r.att[rows, :] = jnp.transpose(r.turned[...]).astype(bf16)
        return carry

    lax.fori_loop(0, q_tiles, one_query_tile, 0)


def row_products(r, grad_att, pairs):
    low, high = pairs[0] * LANES, (pairs[-1] + 1) * LANES
    for tile in range(r.qm.shape[1]):
        rows = slice(tile * TILE, (tile + 1) * TILE)
        product = jnp.transpose(
            grad_att[rows, low:high].astype(f32) * r.att[rows, low:high].astype(f32)
        )
        for pair in pairs:
            for side in range(2):
                head = (2 * pair + side) * 64 - low
                r.delta[tile, pair : pair + 1, side * TILE : (side + 1) * TILE] = jnp.sum(
                    product[head : head + 64, :], axis=0, keepdims=True
                )


def attention_backward(r, core, causal, pairs):
    q_tiles, k_tiles = r.qm.shape[1], r.kt.shape[0]
    width = r.kt.shape[1]
    low, high = pairs[0] * LANES, (pairs[-1] + 1) * LANES
    for start in (0, width):
        r.dkv[:, start + low : start + high] = jnp.zeros((r.dkv.shape[0], high - low), f32)

    def one_query_tile(q_tile, carry):
        r.turned[low:high, :] = jnp.zeros((high - low, TILE), f32)

        def one_key_tile(k_tile, inner):
            def one_tile(ahead):
                if ahead is not None:
                    fill_bias(r, q_tile, k_tile, ahead)
                rows = pl.ds(pl.multiple_of(k_tile * TILE, TILE), TILE)

                def raw(pair):
                    lanes = slice(pair * LANES, (pair + 1) * LANES)
                    lanes_v = slice(width + pair * LANES, width + (pair + 1) * LANES)
                    return (
                        dot_nt(r.kv[rows, lanes], r.qm[pair, q_tile]),
                        dot_nt(r.kv[rows, lanes_v], r.gm[pair, q_tile]),
                    )

                raw_next = raw(pairs[0])
                for pair in pairs:
                    scores, grad_probs = raw_next
                    if ahead is not None:
                        bias = r.bias[...]
                        scores = scores + jnp.concatenate([bias, bias], axis=1)
                    if pair < pairs[-1]:
                        raw_next = raw(pair + 1)
                    probs = jnp.exp(scores - r.lse[q_tile, pair : pair + 1, :])
                    grad_scores = probs * (grad_probs - r.delta[q_tile, pair : pair + 1, :])
                    probs_low = probs.astype(bf16)
                    grad_low = grad_scores.astype(bf16)
                    lanes = slice(pair * LANES, (pair + 1) * LANES)
                    lanes_v = slice(width + pair * LANES, width + (pair + 1) * LANES)
                    r.dkv[rows, lanes] += dot(grad_low, r.qm[pair, q_tile])
                    r.dkv[rows, lanes_v] += dot(probs_low, r.gm[pair, q_tile])
                    for side in range(2):
                        span = slice(side * TILE, (side + 1) * TILE)
                        head = slice((2 * pair + side) * 64, (2 * pair + side + 1) * 64)
                        r.turned[head, :] += dot(r.kt[k_tile, head, :], grad_low[:, span])

            each_tile(tile_place(r, core, causal, q_tile, k_tile), one_tile)
            return inner

        lax.fori_loop(0, k_tiles, one_key_tile, 0)
        rows = pl.ds(pl.multiple_of(q_tile * TILE, TILE), TILE)
        r.dq[rows, low:high] = jnp.transpose(r.turned[low:high, :]) * (64**-0.5)
        return carry

    lax.fori_loop(0, q_tiles, one_query_tile, 0)


def feed_forward(r, low):
    chunks = [slice(at, at + CHUNK) for at in range(0, r.w_in.shape[1], CHUNK)]
    upward_next = dot(low[...], r.w_in[:, chunks[0]])
    for place, span in enumerate(chunks):
        upward = upward_next
        if place + 1 < len(chunks):
            upward_next = dot(low[...], r.w_in[:, chunks[place + 1]])
        gate = jax.nn.sigmoid(upward)
        active = (upward * gate).astype(bf16)
        r.act[:, span] = active
        r.slope[:, span] = (gate + upward * gate * (1.0 - gate)).astype(r.slope.dtype)
        part = dot(active, r.w_down[span, :])
        if place:
            r.sum[...] += part
        else:
            r.sum[...] = part


def feed_backward(r):
    chunks = [slice(at, at + CHUNK) for at in range(0, r.w_in.shape[1], CHUNK)]
    active_next = dot_nt(r.down_grad[...], r.w_down[chunks[0], :])
    for place, span in enumerate(chunks):
        grad_active = active_next.astype(bf16)
        if place + 1 < len(chunks):
            active_next = dot_nt(r.down_grad[...], r.w_down[chunks[place + 1], :])
        grad_up = (grad_active.astype(f32) * r.slope[:, span].astype(f32)).astype(bf16)
        r.up_grad[:, span] = grad_up
        part = dot_nt(grad_up, r.w_in[:, span])
        if place:
            r.sum[...] += part
        else:
            r.sum[...] = part


def self_forward(r):
    length, width = r.unit1.shape
    decoder, core = r.meta[0], r.meta[1]
    move = Copies(r.sems)
    whole = pl.ds(0, length)
    documents = load_documents(r, move, r.x_own_h, r.x_own_h, r.x_other_h)
    early = [
        move.start(r.x_own_h.at[whole], r.x.at[whole]),
        move.start(r.x_other_h.at[whole], r.x.at[pl.ds(length, length)]),
        move.start(r.w_mixed_h, r.w_mixed),
    ]
    later = [
        move.start(r.w_out_h, r.w_out),
        move.start(r.w_in_h, r.w_in),
        move.start(r.w_down_h, r.w_down),
    ]
    place_documents(r, documents)
    wait_all(early)
    r.q[...] = dot(r.x[:length, :], r.w_mixed[:, :width]).astype(bf16)
    r.kv[...] = dot(r.x[...], r.w_mixed[:, width:]).astype(bf16)
    outs = [move.start(r.q, r.q_o), move.start(r.kv, r.kv_o)]
    pairs = range(width // LANES)
    spread_pairs(r.qm, r.q, 64**-0.5, pairs)
    turn_tiles(r.vt, r.kv, width, pairs)
    attention_forward(r, core, decoder)
    wait_all(later)
    outs += [move.start(r.att, r.att_o), move.start(r.lse, r.lse_o)]
    unit, inverse = standardize(r.x[:length, :].astype(f32) + dot(r.att[...], r.w_out[...]))
    r.unit1[...] = unit
    r.inv1[...] = jnp.broadcast_to(inverse, r.inv1.shape)
    r.first_low[...] = (unit * r.gains[0:1, :]).astype(bf16)
    outs += [
        move.start(r.unit1, r.unit1_o),
        move.start(r.inv1, r.inv1_o),
        move.start(r.first_low, r.first_low_o),
    ]

    @pl.when(decoder == 0)
    def _():
        feed_forward(r, r.first_low)
        late = [
            move.start(r.first_low, r.ffn_low_o),
            move.start(r.act, r.act_o),
            move.start(r.slope, r.slope_o),
        ]
        unit2, inverse2 = standardize(r.unit1[...] * r.gains[0:1, :] + r.sum[...])
        r.memory[:length, :] = (unit2 * r.gains[1:2, :]).astype(bf16)
        r.memory[length:, :] = r.docs[0]
        late += [move.start(r.memory, r.memory_o)]
        r.unit2[...] = unit2
        r.inv2[...] = jnp.broadcast_to(inverse2, r.inv2.shape)
        late += [move.start(r.unit2, r.unit2_o), move.start(r.inv2, r.inv2_o)]
        wait_all(late)

    wait_all(outs)


def cross_both_ways(r):
    length, width = r.unit1_h.shape
    core = r.meta[1]
    move = Copies(r.sems)
    whole = pl.ds(0, length)
    documents = load_documents(r, move, r.x_own_h, r.memory_own_h, r.memory_other_h)
    moves = [
        move.start(r.memory_own_h.at[whole], r.x.at[whole]),
        move.start(r.memory_other_h.at[whole], r.x.at[pl.ds(length, length)]),
        move.start(r.w_pair_h, r.w_pair),
        move.start(r.first_low_h, r.first_low),
        move.start(r.w_query_h, r.w_query),
    ]
    later = [
        move.start(r.unit1_h, r.unit1),
        move.start(r.w_cross_h, r.w_cross),
        move.start(r.w_in_h, r.w_in),
        move.start(r.w_down_h, r.w_down),
        move.start(r.cot_h.at[r.micro], r.cot),
    ]
    place_documents(r, documents)
    wait_all(moves)
    r.kv[...] = dot(r.x[...], r.w_pair[...]).astype(bf16)
    r.q[...] = dot(r.first_low[...], r.w_query[...]).astype(bf16)
    pairs = range(width // LANES)
    spread_pairs(r.qm, r.q, 64**-0.5, pairs)
    turn_tiles(r.vt, r.kv, width, pairs)
    turn_tiles(r.kt, r.kv, 0, pairs)
    attention_forward(r, core, 0)
    outs = [move.start(r.att, r.att_o)]
    wait_all(later)
    first = r.unit1[...] * r.gains[0:1, :]
    unit, inverse = standardize(first + dot(r.att[...], r.w_cross[...]))
    r.unit2[...] = unit
    r.inv2[...] = jnp.broadcast_to(inverse, r.inv2.shape)
    r.second_low[...] = (unit * r.cross_gain[...]).astype(bf16)
    outs += [move.start(r.second_low, r.ffn_low_o)]
    feed_forward(r, r.second_low)
    outs += [move.start(r.act, r.act_o)]
    unit3, inverse3 = standardize(r.unit2[...] * r.cross_gain[...] + r.sum[...])
    r.decoded[...] = (unit3 * r.gains[1:2, :]).astype(bf16)
    outs += [move.start(r.decoded, r.decoded_o)]
    grad_third, gain_late = standardize_back(
        r.cot[...].astype(f32), unit3, r.gains[1:2, :], inverse3
    )
    r.keep[...] = grad_third
    r.down_grad[...] = grad_third.astype(bf16)
    outs += [move.start(r.down_grad, r.down_grad_o)]
    feed_backward(r)
    outs += [move.start(r.up_grad, r.up_grad_o)]
    grad_sum, gain_cross = standardize_back(
        r.keep[...] + r.sum[...], r.unit2[...], r.cross_gain[...], r.inv2[:, 0:1]
    )
    r.gain_grads[...] = jnp.zeros(r.gain_grads.shape, f32)
    r.gain_grads[0:1, :] = gain_late
    r.gain_grads[1:2, :] = gain_cross
    r.keep[...] = grad_sum
    r.branch[...] = grad_sum.astype(bf16)
    outs += [move.start(r.gain_grads, r.gain_grads_o), move.start(r.branch, r.branch_o)]
    r.q[...] = dot_nt(r.branch[...], r.w_cross[...]).astype(bf16)
    spread_pairs(r.gm, r.q, 1.0, pairs)
    row_products(r, r.q, pairs)
    attention_backward(r, core, 0, pairs)
    r.dq_low[...] = r.dq[...].astype(bf16)
    r.keep[...] += dot_nt(r.dq_low[...], r.w_query[...])
    outs += [move.start(r.dq_low, r.dq_low_o), move.start(r.keep, r.grad_first_o)]
    r.dkv_low[...] = r.dkv[...].astype(bf16)
    outs += [move.start(r.dkv_low, r.dkv_o)]
    part = dot_nt(r.dkv_low[...], r.w_pair[...])
    r.part_other[...] = part[length:, :].astype(bf16)
    r.part_own[...] = part[:length, :]
    outs += [move.start(r.part_other, r.part_other_o), move.start(r.part_own, r.part_own_o)]
    wait_all(outs)


def feed_backward_alone(r):
    move = Copies(r.sems)
    early = [
        move.start(r.grad_memory_h, r.cot),
        move.start(r.unit2_h, r.unit2),
        move.start(r.inv2_h, r.inv2),
    ]
    later = [
        move.start(r.w_down_h, r.w_down),
        move.start(r.slope_h, r.slope),
        move.start(r.w_in_h, r.w_in),
    ]
    wait_all(early)
    grad_third, gain_late = standardize_back(
        r.cot[...].astype(f32), r.unit2[...], r.gains[1:2, :], r.inv2[:, 0:1]
    )
    r.gain_grads[...] = jnp.broadcast_to(gain_late, r.gain_grads.shape)
    r.keep[...] = grad_third
    r.down_grad[...] = grad_third.astype(bf16)
    outs = [move.start(r.down_grad, r.down_grad_o), move.start(r.gain_grads, r.gain_late_o)]
    wait_all(later)
    feed_backward(r)
    outs += [move.start(r.up_grad, r.up_grad_o)]
    r.keep[...] += r.sum[...]
    outs += [move.start(r.keep, r.grad_first_o)]
    wait_all(outs)


def self_backward(r, plan):
    r.micro, first, last = plan
    length, width = r.att_h.shape
    decoder, core = r.meta[0], r.meta[1]
    pairs = range(first, last)
    low, high = first * LANES, last * LANES
    move = Copies(r.sems)
    later = [
        move.start(r.q_h, r.q),
        move.start(r.kv_h, r.kv),
        move.start(r.att_h, r.att),
        move.start(r.lse_h, r.lse),
    ]
    if first == 0:
        early = [
            move.start(r.grad_first_h, r.keep),
            move.start(r.unit1_h, r.unit1),
            move.start(r.inv1_h, r.inv1),
            move.start(r.w_out_h, r.w_out),
        ]
    else:
        early = [move.start(r.grad_att_h, r.grad_att)]
    outs = []
    place_documents(r, load_documents(r, move, r.x_own_h, r.x_own_h, r.x_other_h))
    wait_all(early)
    if first == 0:
        grad_sum, gain_early = standardize_back(
            r.keep[...], r.unit1[...], r.gains[0:1, :], r.inv1[:, 0:1]
        )
        r.gain_grads[...] = jnp.broadcast_to(gain_early, r.gain_grads.shape)
        r.keep[...] = grad_sum
        r.branch[...] = grad_sum.astype(bf16)
        r.grad_att[...] = dot_nt(r.branch[...], r.w_out[...]).astype(bf16)
        outs += [move.start(r.gain_grads, r.gain_early_o), move.start(r.branch, r.branch_o)]
        if last < width // LANES:
            outs += [move.start(r.keep, r.grad_sum_o), move.start(r.grad_att, r.grad_att_o)]
    wait_all(later)
    if last == width // LANES:
        ends = [move.start(r.w_mixed_h, r.w_mixed)]
        if first > 0:
            ends += [
                move.start(r.grad_sum_h, r.keep),
                move.start(r.dq_h.at[:, pl.ds(0, low)], r.dq_low.at[:, pl.ds(0, low)]),
                move.start(r.dkv_h.at[:, pl.ds(0, low)], r.dkv_low.at[:, pl.ds(0, low)]),
                move.start(
                    r.dkv_h.at[:, pl.ds(width, low)], r.dkv_low.at[:, pl.ds(width, low)]
                ),
            ]
    spread_pairs(r.qm, r.q, 64**-0.5, pairs)
    turn_tiles(r.kt, r.kv, 0, pairs)
    spread_pairs(r.gm, r.grad_att, 1.0, pairs)
    row_products(r, r.grad_att, pairs)
    attention_backward(r, core, decoder, pairs)
    r.dq_low[:, low:high] = r.dq[:, low:high].astype(bf16)
    for start in (0, width):
        span = slice(start + low, start + high)
        r.dkv_low[:, span] = r.dkv[:, span].astype(bf16)
    if last == width // LANES:
        wait_all(ends)
        outs += [move.start(r.dq_low, r.dq_low_o), move.start(r.dkv_low, r.dkv_o)]
        r.keep[...] += dot_nt(r.dq_low[...], r.w_mixed[:, :width])
        part = dot_nt(r.dkv_low[...], r.w_mixed[:, width:])
        r.part_other[...] = part[length:, :].astype(bf16)
        r.keep[...] += part[:length, :]
        outs += [move.start(r.part_other, r.part_other_o), move.start(r.keep, r.part_own_o)]
    else:
        outs.append(move.start(r.dq_low.at[:, pl.ds(low, high - low)], r.dq_low_o.at[:, pl.ds(low, high - low)]))
        for start in (0, width):
            span = pl.ds(start + low, high - low)
            outs.append(move.start(r.dkv_low.at[:, span], r.dkv_o.at[:, span]))
    wait_all(outs)


def contract_blocks(r, plan):
    for core in range(2):

        @pl.when(r.meta[1] == core)
        def _(core=core):
            targets = [None] * 4
            for half in range(2):
                target = r.kept_o if half == core else r.sent_o
                targets[2 * half], targets[2 * half + 1] = target.at[0], target.at[1]
            order = (0, 1, 2, 3) if core else (2, 3, 0, 1)
            contract_in_order(r, plan(r), order, targets, Copies(r.sems))


def contract_in_order(r, blocks, order, targets, move):
    loads = dict()
    for slot in order:
        for buffer, sources, at in blocks[slot][1:]:
            if (id(buffer), at) not in loads:
                span = pl.ds(at * CHUNK, CHUNK)
                row = 0
                copies = []
                for source in sources:
                    rows = pl.ds(row, source.shape[0])
                    copies.append(move.start(source.at[:, span], buffer.at[rows, span]))
                    row += source.shape[0]
                loads[id(buffer), at] = copies
    outs = []
    held = dict()
    for slot in order:
        turn, (left, _, left_at), (right, _, right_at) = blocks[slot]
        wait_all(loads.pop((id(left), left_at), ()))
        wait_all(loads.pop((id(right), right_at), ()))
        if held.get(id(turn)) != left_at:
            for row in range(0, left.shape[0], CHUNK):
                block = left[row : row + CHUNK, left_at * CHUNK : (left_at + 1) * CHUNK]
                turn[:, row : row + CHUNK] = jnp.transpose(block)
            held[id(turn)] = left_at
        block = right[:, right_at * CHUNK : (right_at + 1) * CHUNK]
        r.blocks[slot] = dot(turn[:, : right.shape[0]], block).astype(bf16)
        outs.append(move.start(r.blocks.at[slot], targets[slot]))
    wait_all(outs)


def spread_pieces(r, targets):
    z = r.meta[3]
    group, height = r.own_h.shape[:2]
    rows = r.own_h.shape[2] // group
    for core in range(2):
        for x in range(2):

            @pl.when((r.meta[1] == core) & (r.meta[2] == x))
            def _(core=core, x=x):
                move = Copies(r.sems)
                parts = [
                    (r.own_h, core, x),
                    (r.own_x_h, core, 1 - x),
                    (r.other_h, 1 - core, x),
                    (r.other_x_h, 1 - core, 1 - x),
                ]
                loads = [
                    move.start(source, r.pieces.at[place])
                    for place, (source, _, _) in enumerate(parts)
                ]
                outs = []
                slot = 0
                gains = None
                for place, (_, half, side) in enumerate(parts):
                    loads[place].wait()
                    for step in range(group):
                        row = pl.multiple_of(lax.rem(z + (group - step), group) * rows, rows)
                        start = 0
                        for target in targets(r, 2 * half + side, row, rows):
                            r.wide[slot] = r.pieces[place, step, start : start + rows].astype(f32)
                            outs.append(move.start(r.wide.at[slot], target))
                            slot += 1
                            start += rows
                        if start < height:
                            extra = r.pieces[place, step, start:height].astype(f32)
                            gains = extra if gains is None else gains + extra
                r.gains_o[...] = gains[: r.gains_o.shape[0], :]
                wait_all(outs)


def launch(kernel, plan, side, scalars, small, large, outs, scratch, copies, work, previous=None, after=()):
    names = list(scalars) + list(small) + list(large)
    arrays = list(scalars.values()) + list(small.values()) + list(large.values())
    specs = (
        [pl.BlockSpec(memory_space=pltpu.SMEM)] * len(scalars)
        + [pl.BlockSpec(memory_space=pltpu.VMEM)] * len(small)
        + [pl.BlockSpec(memory_space=pl.ANY)] * len(large)
    )
    aliases = dict()
    for position, name in enumerate(outs):
        if previous and name in previous:
            aliases[len(arrays)] = position
            names.append("previous_" + name)
            arrays.append(previous[name])
            specs.append(pl.BlockSpec(memory_space=pl.ANY))
    for array in after:
        names.append("")
        arrays.append(array)
        specs.append(pl.BlockSpec(memory_space=pl.ANY))
    names += list(outs) + list(scratch) + ["sems"]

    def body(*refs):
        r = types.SimpleNamespace(**dict(zip(names, refs)))

        def run():
            if isinstance(plan, int):
                r.micro = plan
                kernel(r)
            else:
                kernel(r, plan)

        if side is None:
            run()
        else:
            pl.when(r.meta[0] == side)(run)

    results = pl.pallas_call(
        body,
        out_shape=[jax.ShapeDtypeStruct(*shape) for shape in outs.values()],
        in_specs=specs,
        out_specs=[
            pl.BlockSpec(memory_space=pltpu.VMEM if shape[0][0] < 8 else pl.ANY)
            for shape in outs.values()
        ],
        scratch_shapes=[
            pltpu.SMEM(*shape) if shape[1] == jnp.int32 else pltpu.VMEM(*shape)
            for shape in scratch.values()
        ]
        + [pltpu.SemaphoreType.DMA((copies,))],
        input_output_aliases=aliases,
        compiler_params=pltpu.CompilerParams(vmem_limit_bytes=58 * 1024 * 1024),
        cost_estimate=pl.CostEstimate(
            flops=work * 10**9, bytes_accessed=1 << 20, transcendentals=0
        ),
    )(*arrays)
    return types.SimpleNamespace(**dict(zip(outs, results)))


def attention_scratch(length, width):
    pairs, q_tiles, k_tiles = width // LANES, length // TILE, 2 * length // TILE
    return dict(
        q=((length, width), bf16),
        kv=((2 * length, 2 * width), bf16),
        qm=((pairs, q_tiles, 2 * TILE, LANES), bf16),
        kdc=((2 * length, LANES), f32),
        docs=((3, 16, width), bf16),
        qd=((length // TILE, 8, TILE), f32),
        bounds=((2, 3 * length // TILE), jnp.int32),
        bias=((TILE, TILE), f32),
        lse=((q_tiles, 8, 2 * TILE), f32),
        att=((length, width), bf16),
        turned=((width, TILE), f32),
    )


def forward_scratch(length, width):
    k_tiles = 2 * length // TILE
    return dict(
        vt=((k_tiles, width, TILE), bf16),
        top=((8, 2 * TILE), f32),
        total=((8, 2 * TILE), f32),
    )


def backward_scratch(length, width):
    pairs, q_tiles, k_tiles = width // LANES, length // TILE, 2 * length // TILE
    return dict(
        kt=((k_tiles, width, TILE), bf16),
        gm=((pairs, q_tiles, 2 * TILE, LANES), bf16),
        delta=((q_tiles, 8, 2 * TILE), f32),
        dkv=((2 * length, 2 * width), f32),
        dq=((length, width), f32),
        dkv_low=((2 * length, 2 * width), bf16),
        part_other=((length, width), bf16),
        dq_low=((length, width), bf16),
    )


def for_sending(shard):

    def short(part):
        return part.astype(jnp.bfloat16) if part.dtype == jnp.float32 else part

    return jax.tree.map(short, shard)


def from_behind(block, axis, distance):
    devices = range(lax.axis_size(axis))
    route = [(i - distance, i) for i in devices if i - distance in devices]
    return lax.ppermute(block, axis, route)


def from_root(shard, axis, root):
    mine = lax.axis_index(axis) == root
    return lax.psum(jnp.where(mine, shard, jnp.zeros_like(shard)), axis)


def matmul(left_side, right_side):
    return jnp.einsum("rsd,de->rse", left_side, right_side, preferred_element_type=jnp.float32)


def matmul_back(left_side, right_side):
    return jnp.einsum("rse,de->rsd", left_side, right_side, preferred_element_type=jnp.float32)


def contract(left_side, right_side):
    return jnp.einsum("rsd,rse->de", left_side, right_side, preferred_element_type=jnp.float32)


def normalize(values, gain_row):
    center = values - jnp.mean(values, axis=-1, keepdims=True)
    inverse = lax.rsqrt(jnp.mean(center * center, axis=-1, keepdims=True) + epsilon)
    standard = center * inverse
    return (standard * gain_row, standard, inverse)


def normalize_back(grad_out, standard, gain_row, inverse):
    scaled = grad_out * gain_row
    grad_in = inverse * (
        scaled
        - jnp.mean(scaled, axis=-1, keepdims=True)
        - standard * jnp.mean(scaled * standard, axis=-1, keepdims=True)
    )
    return (grad_in, jnp.sum(grad_out * standard, axis=(0, 1)))


def allowed_mask(query_docs, key_docs, query_place, key_place, causal):
    same_doc = query_docs[:, :, None] == key_docs[:, None, :]
    earlier = query_place[:, None] >= key_place[None, :]
    return (same_doc & (earlier | jnp.logical_not(causal)))[:, None]


def attend(queries, keys_local, values_local, query_docs, key_docs, causal, is_cross):
    rows_here, shard_len, model_width = queries.shape
    head_dim = model_width // HEADS
    score_scale = head_dim ** (-0.5)
    query_place = lax.axis_index("seq") * shard_len + jnp.arange(shard_len)
    query_heads = queries.reshape(rows_here, shard_len, HEADS, head_dim)

    def absorb(state_tuple, pieces):
        running_top, running_total, running_sum = state_tuple
        key_piece, value_piece, doc_piece = pieces
        piece_len = key_piece.shape[1]
        raw_scores = jnp.einsum(
            "rqhd,rkhd->rhqk",
            query_heads,
            key_piece.reshape(rows_here, piece_len, HEADS, head_dim),
            preferred_element_type=jnp.float32,
        )
        allowed = allowed_mask(query_docs, doc_piece, query_place, jnp.arange(piece_len), causal)
        scores = jnp.where(allowed, raw_scores * score_scale, negative_big)
        new_top = jnp.maximum(running_top, jnp.max(scores, axis=-1))
        weights = jnp.where(allowed, jnp.exp(scores - new_top[..., None]), 0.0)
        new_total = jnp.sum(weights, axis=-1)
        product = jnp.einsum(
            "rhqk,rkhd->rhqd",
            weights.astype(jnp.bfloat16),
            value_piece.reshape(rows_here, piece_len, HEADS, head_dim),
            preferred_element_type=jnp.float32,
        )
        return (new_top, new_total, product)

    init_state = (
        jnp.full((rows_here, HEADS, shard_len), negative_big, jnp.float32),
        jnp.zeros((rows_here, HEADS, shard_len), jnp.float32),
        jnp.zeros((rows_here, HEADS, shard_len, head_dim), jnp.float32),
    )
    if is_cross:
        final_top, final_total, final_sum = absorb(
            init_state,
            (
                lax.all_gather(keys_local, "seq", axis=1, tiled=True),
                lax.all_gather(values_local, "seq", axis=1, tiled=True),
                lax.all_gather(for_sending(key_docs), "seq", axis=1, tiled=True),
            ),
        )
    else:
        final_top, final_total, final_sum = absorb(
            init_state,
            (
                lax.all_gather(keys_local, "seq", axis=1, tiled=True),
                lax.all_gather(values_local, "seq", axis=1, tiled=True),
                lax.all_gather(key_docs, "seq", axis=1, tiled=True),
            ),
        )
    attended = (
        (final_sum / final_total[..., None])
        .transpose(0, 2, 1, 3)
        .reshape(rows_here, shard_len, model_width)
    )
    return (attended, final_top + jnp.log(final_total))


def attend_back(
    queries,
    keys_local,
    values_local,
    query_docs,
    key_docs,
    causal,
    log_total,
    grad_attended,
    is_cross,
):
    rows_here, shard_len, model_width = queries.shape
    head_dim = model_width // HEADS
    score_scale = head_dim ** (-0.5)
    query_place = lax.axis_index("seq") * shard_len + jnp.arange(shard_len)
    if is_cross:
        keys_full, values_full, docs_full = (
            lax.all_gather(keys_local, "seq", axis=1, tiled=True),
            lax.all_gather(values_local, "seq", axis=1, tiled=True),
            lax.all_gather(for_sending(key_docs), "seq", axis=1, tiled=True).astype(key_docs.dtype),
        )
    else:
        keys_full, values_full, docs_full = (
            lax.all_gather(keys_local, "seq", axis=1, tiled=True),
            lax.all_gather(values_local, "seq", axis=1, tiled=True),
            lax.all_gather(key_docs, "seq", axis=1, tiled=True),
        )
    full_len = keys_full.shape[1]
    query_heads = queries.reshape(rows_here, shard_len, HEADS, head_dim)
    key_heads = keys_full.reshape(rows_here, full_len, HEADS, head_dim)
    value_heads = values_full.reshape(rows_here, full_len, HEADS, head_dim)
    grad_heads = grad_attended.reshape(rows_here, shard_len, HEADS, head_dim)
    raw_scores = jnp.einsum(
        "rqhd,rkhd->rhqk", query_heads, key_heads, preferred_element_type=jnp.float32
    )
    allowed = allowed_mask(query_docs, docs_full, query_place, jnp.arange(full_len), causal)
    shifted = jnp.where(allowed, raw_scores * score_scale - log_total[..., None], negative_big)
    probs = jnp.where(allowed, jnp.exp(shifted), 0.0)
    grad_probs = jnp.einsum(
        "rqhd,rkhd->rhqk", grad_heads, value_heads, preferred_element_type=jnp.float32
    )
    delta = jnp.sum(probs * grad_probs, axis=-1)
    grad_scores = (probs * (grad_probs - delta[..., None]) * score_scale).astype(jnp.bfloat16)
    grad_queries = jnp.einsum(
        "rhqk,rkhd->rqhd", grad_scores, key_heads, preferred_element_type=jnp.float32
    ).reshape(rows_here, shard_len, model_width)
    probs_low = probs.astype(jnp.bfloat16)

    def key_terms(span):
        grad_keys = jnp.einsum(
            "rhqk,rqhd->krhd", grad_scores, query_heads, preferred_element_type=jnp.float32
        )
        grad_values = jnp.einsum(
            "rhqk,rqhd->krhd", probs_low, grad_heads, preferred_element_type=jnp.float32
        )
        return jnp.concatenate(
            [
                grad_keys.reshape(span, rows_here, model_width),
                grad_values.reshape(span, rows_here, model_width),
            ],
            axis=-1,
        )

    if is_cross:
        pair_terms = lax.psum_scatter(
            key_terms(shard_len * lax.axis_size("seq")).astype(jnp.bfloat16),
            "seq",
            scatter_dimension=0,
            tiled=True,
        ).astype(jnp.float32)
    else:
        pair_terms = lax.psum_scatter(
            key_terms(shard_len * lax.axis_size("seq")).astype(jnp.bfloat16),
            "seq",
            scatter_dimension=0,
            tiled=True,
        ).astype(jnp.float32)
    return (grad_queries, pair_terms.transpose(1, 0, 2))


def layer_forward(hidden_in, doc_own, memory, memory_docs, weights, is_decoder):
    (
        qkv_weight,
        out_weight,
        in_weight,
        down_weight,
        gains_pair,
        query_weight,
        pair_weight,
        cross_weight,
        cross_gains,
    ) = weights
    model_width = hidden_in.shape[-1]
    mixed = matmul(hidden_in, qkv_weight).astype(jnp.bfloat16)
    attended, self_lse = attend(
        mixed[..., :model_width],
        mixed[..., model_width : 2 * model_width],
        mixed[..., 2 * model_width :],
        doc_own,
        doc_own,
        is_decoder,
        False,
    )
    attended = attended.astype(jnp.bfloat16)
    first, first_unit, first_inv = normalize(
        hidden_in.astype(jnp.float32) + matmul(attended, out_weight), gains_pair[0]
    )
    first_low = first.astype(jnp.bfloat16)
    cross_queries = matmul(first_low, query_weight).astype(jnp.bfloat16)
    pair = matmul(memory, pair_weight).astype(jnp.bfloat16)
    cross_att, cross_lse = attend(
        cross_queries,
        pair[..., :model_width],
        pair[..., model_width:],
        doc_own,
        memory_docs,
        False,
        True,
    )
    cross_att = cross_att.astype(jnp.bfloat16)
    second_cross, second_unit, second_inv = normalize(
        first + matmul(cross_att, cross_weight), cross_gains
    )
    second = jnp.where(is_decoder, second_cross, first)
    second_low = second.astype(jnp.bfloat16)
    upward = matmul(second_low, in_weight)
    active = jax.nn.silu(upward).astype(jnp.bfloat16)
    result, third_unit, third_inv = normalize(second + matmul(active, down_weight), gains_pair[1])
    saved = {
        "mixed": mixed,
        "attended": attended,
        "self_lse": self_lse,
        "first_unit": first_unit,
        "first_inv": first_inv,
        "first_low": first_low,
        "cross_queries": cross_queries,
        "pair": pair,
        "cross_att": cross_att,
        "cross_lse": cross_lse,
        "second_unit": second_unit,
        "second_inv": second_inv,
        "second_low": second_low,
        "upward": upward,
        "active": active,
        "third_unit": third_unit,
        "third_inv": third_inv,
    }
    return (result, saved)


def layer_backward(
    grad_result, saved, hidden_in, doc_own, memory, memory_docs, weights, is_decoder
):
    (
        qkv_weight,
        out_weight,
        in_weight,
        down_weight,
        gains_pair,
        query_weight,
        pair_weight,
        cross_weight,
        cross_gains,
    ) = weights
    model_width = hidden_in.shape[-1]
    grad_third, grad_gain_late = normalize_back(
        grad_result, saved["third_unit"], gains_pair[1], saved["third_inv"]
    )
    down_grad = grad_third.astype(jnp.bfloat16)
    grad_down_w = contract(saved["active"], down_grad)
    grad_active = matmul_back(down_grad, down_weight).astype(jnp.bfloat16)
    sigmoid_up = jax.nn.sigmoid(saved["upward"])
    grad_upward = (
        grad_active.astype(jnp.float32)
        * (sigmoid_up + saved["upward"] * sigmoid_up * (1.0 - sigmoid_up))
    ).astype(jnp.bfloat16)
    grad_in_w = contract(saved["second_low"], grad_upward)
    grad_second = grad_third + matmul_back(grad_upward, in_weight)
    grad_cross_sum, grad_cross_gain = normalize_back(
        grad_second, saved["second_unit"], cross_gains, saved["second_inv"]
    )
    decoder_flag = is_decoder.astype(jnp.float32)
    grad_cross_sum = grad_cross_sum * decoder_flag
    grad_cross_gain = grad_cross_gain * decoder_flag
    cross_branch = grad_cross_sum.astype(jnp.bfloat16)
    grad_cross_w = contract(saved["cross_att"], cross_branch)
    grad_cross_att = matmul_back(cross_branch, cross_weight).astype(jnp.bfloat16)
    pair = saved["pair"]
    grad_cross_q, grad_pair = attend_back(
        saved["cross_queries"],
        pair[..., :model_width],
        pair[..., model_width:],
        doc_own,
        memory_docs,
        False,
        saved["cross_lse"],
        grad_cross_att,
        True,
    )
    grad_cross_q = grad_cross_q.astype(jnp.bfloat16)
    grad_pair = grad_pair.astype(jnp.bfloat16)
    grad_query_w = contract(saved["first_low"], grad_cross_q)
    grad_pair_w = contract(memory, grad_pair)
    grad_memory = matmul_back(grad_pair, pair_weight)
    grad_first = jnp.where(
        is_decoder, grad_cross_sum + matmul_back(grad_cross_q, query_weight), grad_second
    )
    grad_first_sum, grad_gain_early = normalize_back(
        grad_first, saved["first_unit"], gains_pair[0], saved["first_inv"]
    )
    self_branch = grad_first_sum.astype(jnp.bfloat16)
    grad_out_w = contract(saved["attended"], self_branch)
    grad_attended = matmul_back(self_branch, out_weight).astype(jnp.bfloat16)
    mixed = saved["mixed"]
    grad_queries, grad_pair_self = attend_back(
        mixed[..., :model_width],
        mixed[..., model_width : 2 * model_width],
        mixed[..., 2 * model_width :],
        doc_own,
        doc_own,
        is_decoder,
        saved["self_lse"],
        grad_attended,
        False,
    )
    grad_mixed = jnp.concatenate([grad_queries, grad_pair_self], axis=-1).astype(jnp.bfloat16)
    grad_qkv_w = contract(hidden_in, grad_mixed)
    grad_hidden = grad_first_sum + matmul_back(grad_mixed, qkv_weight)
    layer_grads = (
        grad_qkv_w,
        grad_out_w,
        grad_in_w,
        grad_down_w,
        jnp.stack([grad_gain_early, grad_gain_late]),
        grad_query_w,
        grad_pair_w,
        grad_cross_w,
        grad_cross_gain,
    )
    return (grad_hidden, grad_memory, layer_grads)


def any_rows(
    layer_input,
    segment_ids,
    attn_qkv,
    attn_out,
    ffn_in,
    ffn_out,
    norm_gain,
    cross_query,
    cross_pair,
    cross_out,
    cross_gain,
    out_cotangent,
):
    micro_count = layer_input.shape[1]
    section_index = lax.axis_index("section")
    is_decoder = section_index == 1
    weights = (
        attn_qkv[0],
        attn_out[0],
        ffn_in[0],
        ffn_out[0],
        norm_gain[0],
        cross_query,
        cross_pair,
        cross_out,
        cross_gain,
    )
    inputs_all = layer_input[0]
    docs_all = segment_ids[0]
    slot_ids = jnp.arange(micro_count)
    received = (jnp.zeros_like(inputs_all[0]), jnp.zeros_like(docs_all[0]))
    results = jnp.zeros_like(inputs_all)
    memories = []
    memory_doc_list = []
    for step_index in range(micro_count + 1):
        batch_index = step_index - section_index
        is_valid = (batch_index >= 0) & (batch_index < micro_count)
        chosen = jnp.clip(batch_index, 0, micro_count - 1)
        hidden_in = lax.dynamic_index_in_dim(inputs_all, chosen, 0, keepdims=False)
        doc_own = lax.dynamic_index_in_dim(docs_all, chosen, 0, keepdims=False)
        memory = received[0]
        memory_docs = jnp.where(is_valid & is_decoder, received[1], doc_own)
        memories.append(memory)
        memory_doc_list.append(memory_docs)
        result, saved = layer_forward(hidden_in, doc_own, memory, memory_docs, weights, is_decoder)
        low_result = result.astype(jnp.bfloat16)
        writing = (slot_ids == chosen) & is_valid
        results = jnp.where(writing[:, None, None, None], low_result[None], results)
        if step_index < micro_count:
            received = from_behind((low_result, doc_own), "section", 1)
    memory_stack = jnp.stack(memories)
    memory_doc_stack = jnp.stack(memory_doc_list)
    totals = tuple((jnp.zeros(weight.shape, jnp.float32) for weight in weights))
    input_grads = jnp.zeros(inputs_all.shape, jnp.float32)
    returned = jnp.zeros(inputs_all.shape[1:], jnp.float32)
    for step_index in range(micro_count + 1):
        batch_index = micro_count - step_index - section_index
        is_valid = (batch_index >= 0) & (batch_index < micro_count)
        chosen = jnp.clip(batch_index, 0, micro_count - 1)
        forward_step = jnp.clip(batch_index + section_index, 0, micro_count)
        hidden_in = lax.dynamic_index_in_dim(inputs_all, chosen, 0, keepdims=False)
        doc_own = lax.dynamic_index_in_dim(docs_all, chosen, 0, keepdims=False)
        memory = lax.dynamic_index_in_dim(memory_stack, forward_step, 0, keepdims=False)
        memory_docs = lax.dynamic_index_in_dim(memory_doc_stack, forward_step, 0, keepdims=False)
        discarded, saved = layer_forward(
            hidden_in, doc_own, memory, memory_docs, weights, is_decoder
        )
        cotangent = jnp.where(
            is_decoder,
            lax.dynamic_index_in_dim(out_cotangent, chosen, 0, keepdims=False).astype(jnp.float32),
            returned,
        )
        grad_hidden, grad_memory, layer_grads = layer_backward(
            cotangent, saved, hidden_in, doc_own, memory, memory_docs, weights, is_decoder
        )
        valid_flag = is_valid.astype(jnp.float32)
        totals = tuple(
            (running + valid_flag * fresh for running, fresh in zip(totals, layer_grads))
        )
        writing = (slot_ids == chosen) & is_valid
        input_grads = jnp.where(writing[:, None, None, None], grad_hidden[None], input_grads)
        if step_index < micro_count:
            returned = from_behind(grad_memory.astype(jnp.bfloat16), "section", -1).astype(
                grad_memory.dtype
            )
    group_sums = lax.psum(
        (
            totals[0],
            totals[1],
            totals[2],
            totals[3],
            totals[4],
            totals[5],
            totals[6],
            totals[7],
            totals[8],
        ),
        ("seq", "dp"),
    )
    section_sums = group_sums[:5]
    cross_sums = (
        from_root(group_sums[5].astype(jnp.bfloat16), "section", 1).astype(jnp.float32),
        from_root(group_sums[6].astype(jnp.bfloat16), "section", 1).astype(jnp.float32),
        from_root(group_sums[7].astype(jnp.bfloat16), "section", 1).astype(jnp.float32),
        from_root(group_sums[8].astype(jnp.bfloat16), "section", 1).astype(jnp.float32),
    )
    return (
        results[None],
        input_grads[None],
        section_sums[0][None],
        section_sums[1][None],
        section_sums[2][None],
        section_sums[3][None],
        section_sums[4][None],
        cross_sums[0],
        cross_sums[1],
        cross_sums[2],
        cross_sums[3],
    )


def split_rows(
    layer_input,
    segment_ids,
    attn_qkv,
    attn_out,
    ffn_in,
    ffn_out,
    norm_gain,
    cross_query,
    cross_pair,
    cross_out,
    cross_gain,
    out_cotangent,
):
    micros = layer_input.shape[1]
    length, width = layer_input.shape[3:]
    hidden = ffn_in.shape[-1]
    q_tiles = length // TILE
    group = lax.axis_size("dp") // 2
    axes = ("section", "seq", "dp")
    decoder = lax.axis_index("section") == 1
    flag = decoder.astype(jnp.int32)
    x = lax.axis_index("seq")
    core = lax.rem(lax.axis_index("dp"), 2)
    z = lax.axis_index("dp") // 2
    places = [(t, i, k, c) for t in range(2) for i in range(2) for k in range(group) for c in range(2)]

    def number(t, i, k, c):
        return ((t * 2 + i) * group + k) * 2 + c

    def send(values, target, section=None):
        route = [
            (number(*place), number(*target(*place)))
            for place in places
            if section in (None, place[0]) and target(*place)
        ]
        return lax.ppermute(values, axes, route)

    def to_core(t, i, k, c):
        return (t, i, k, 1 - c)

    def to_x(t, i, k, c):
        return (t, 1 - i, k, c)

    def to_row(t, i, k, c):
        return (t, c, k, i)

    def to_decoder(t, i, k, c):
        return (1, i, k, c) if t == 0 else None

    def to_encoder(t, i, k, c):
        return (0, i, k, c) if t == 1 else None

    def fence(values, *before):
        return lax.optimization_barrier((values,) + before)[0]

    def exchange(values):
        return send(values, to_core)

    low = ((length, width), bf16)
    wide = ((length, width), f32)
    marked = ((length + 16, width), bf16)
    both = ((2 * length, width), bf16)
    keys_all = ((2 * length, 2 * width), bf16)
    mixing = ((width, 3 * width), bf16)
    inner = ((length, hidden), bf16)
    lse = ((q_tiles, 8, 2 * TILE), f32)
    stat = ((length, LANES), f32)
    square = ((width, width), bf16)
    rising = ((width, hidden), bf16)
    falling = ((hidden, width), bf16)
    gain_rows = ((8, width), f32)

    meta = jnp.stack([flag, core, x, z]).astype(jnp.int32)
    numbers = segment_ids[0, :, 0].astype(bf16)
    padding = jnp.zeros((15, width), bf16)
    with_numbers = [
        jnp.concatenate([layer_input[0, micro, 0], numbers[micro][None], padding])
        for micro in range(micros)
    ]
    own = [send(with_numbers[0], to_row)]
    for micro in range(1, micros):
        own.append(send(fence(with_numbers[micro], own[-1]), to_row))
    other = [exchange(own[0])]

    plain = dict(meta=meta)
    small = dict(gains=norm_gain[0])
    forward, memories, memories_other = [], [], []
    for micro in range(micros):
        call = launch(
            self_forward,
            micro,
            None,
            plain,
            small,
            dict(
                x_own_h=own[micro],
                x_other_h=other[micro],
                w_mixed_h=attn_qkv[0],
                w_out_h=attn_out[0],
                w_in_h=ffn_in[0],
                w_down_h=ffn_out[0],
            ),
            dict(
                q_o=low,
                kv_o=keys_all,
                att_o=low,
                lse_o=lse,
                unit1_o=wide,
                inv1_o=stat,
                first_low_o=low,
                memory_o=marked,
                ffn_low_o=low,
                act_o=inner,
                slope_o=inner,
                unit2_o=wide,
                inv2_o=stat,
            ),
            dict(
                **attention_scratch(length, width),
                **forward_scratch(length, width),
                x=both,
                w_mixed=mixing,
                w_out=square,
                w_in=rising,
                w_down=falling,
                unit1=wide,
                inv1=stat,
                first_low=low,
                memory=marked,
                act=inner,
                slope=inner,
                unit2=wide,
                inv2=stat,
                sum=wide,
            ),
            28,
            26,
            after=(forward[0].lse_o,) if micro else (),
        )
        forward.append(call)
        memories.append(send(call.memory_o, to_decoder))
        if micro + 1 < micros:
            other.append(exchange(fence(own[micro + 1], call.lse_o)))

    for micro in range(micros):
        memories_other.append(exchange(fence(memories[micro], forward[-1].lse_o)))
    cotangent = send(fence(out_cotangent[:, 0], forward[0].lse_o), to_row)

    cross, grads_memory, made = [], [], []
    after = (forward[-1].lse_o,)
    for micro in range(micros):
        done = forward[micro]
        call = launch(
            cross_both_ways,
            micro,
            1,
            plain,
            dict(**small, cross_gain=cross_gain[None]),
            dict(
                x_own_h=own[micro],
                memory_own_h=memories[micro],
                memory_other_h=memories_other[micro],
                w_pair_h=cross_pair,
                first_low_h=done.first_low_o,
                unit1_h=done.unit1_o,
                w_query_h=cross_query,
                w_cross_h=cross_out,
                w_in_h=ffn_in[0],
                w_down_h=ffn_out[0],
                cot_h=cotangent,
            ),
            dict(
                att_o=low,
                ffn_low_o=low,
                act_o=inner,
                decoded_o=low,
                down_grad_o=low,
                up_grad_o=inner,
                gain_grads_o=gain_rows,
                branch_o=low,
                dq_low_o=low,
                dkv_o=keys_all,
                part_own_o=wide,
                part_other_o=low,
                grad_first_o=wide,
            ),
            dict(
                **attention_scratch(length, width),
                **forward_scratch(length, width),
                **backward_scratch(length, width),
                x=both,
                w_pair=((width, 2 * width), bf16),
                first_low=low,
                unit1=wide,
                w_query=square,
                w_cross=square,
                w_in=rising,
                w_down=falling,
                cot=low,
                unit2=wide,
                inv2=stat,
                second_low=low,
                act=inner,
                slope=inner,
                sum=wide,
                decoded=low,
                keep=wide,
                down_grad=low,
                up_grad=inner,
                gain_grads=gain_rows,
                branch=low,
                part_own=wide,
            ),
            36,
            44,
            dict(act_o=done.act_o, ffn_low_o=done.ffn_low_o),
            after,
        )
        cross.append(call)
        away = call.part_other_o
        if micro:
            away = fence(away, grads_memory[-1])
        total = call.part_own_o + exchange(away).astype(f32)
        made.append(total.astype(bf16))
        after = (made[micro],)
        grads_memory.append(send(made[micro], to_encoder))

    def backward_feed(micro, after):
        done, late = forward[micro], cross[micro]
        return launch(
            feed_backward_alone,
            micro,
            0,
            plain,
            dict(gains=norm_gain[0]),
            dict(
                grad_memory_h=grads_memory[micro],
                unit2_h=done.unit2_o,
                inv2_h=done.inv2_o,
                slope_h=done.slope_o,
                w_in_h=ffn_in[0],
                w_down_h=ffn_out[0],
            ),
            dict(gain_late_o=gain_rows, down_grad_o=low, up_grad_o=inner, grad_first_o=wide),
            dict(
                cot=low,
                unit2=wide,
                inv2=stat,
                slope=inner,
                w_in=rising,
                w_down=falling,
                gain_grads=gain_rows,
                keep=wide,
                down_grad=low,
                up_grad=inner,
                sum=wide,
            ),
            12,
            10,
            dict(
                down_grad_o=late.down_grad_o, up_grad_o=late.up_grad_o, grad_first_o=late.grad_first_o
            ),
            after,
        )

    def backward_self(micro, side, grad_first, previous=None, after=(), halfway=None):
        done = forward[micro]
        heads = width // LANES
        given = dict(
            x_own_h=own[micro],
            x_other_h=other[micro],
            q_h=done.q_o,
            kv_h=done.kv_o,
            att_h=done.att_o,
            lse_h=done.lse_o,
        )
        ahead = dict(
            grad_first_h=grad_first,
            unit1_h=done.unit1_o,
            inv1_h=done.inv1_o,
            w_out_h=attn_out[0],
        )
        makes = dict(dq_low_o=low, dkv_o=keys_all)
        makes_first = dict(gain_early_o=gain_rows, branch_o=low)
        makes_last = dict(part_own_o=wide, part_other_o=low)
        scratch = dict(
            **attention_scratch(length, width),
            **backward_scratch(length, width),
            w_out=square,
            w_mixed=mixing,
            unit1=wide,
            inv1=stat,
            keep=wide,
            branch=low,
            grad_att=low,
            gain_grads=gain_rows,
        )

        def part(first, last, large, outs, work, previous, after):
            return launch(
                self_backward,
                (micro, first, last),
                side,
                plain,
                small,
                dict(**given, **large),
                dict(**makes, **outs),
                scratch,
                28,
                work,
                previous,
                after,
            )

        if halfway is None:
            large = dict(**ahead, w_mixed_h=attn_qkv[0])
            outs = dict(**makes_first, **makes_last)
            return part(0, heads, large, outs, 22, previous, after)
        outs = dict(**makes_first, grad_sum_o=wide, grad_att_o=low)
        one = part(0, heads // 2, ahead, outs, 12, None, after)
        large = dict(
            w_mixed_h=attn_qkv[0],
            grad_sum_h=one.grad_sum_o,
            grad_att_h=one.grad_att_o,
            dq_h=one.dq_low_o,
            dkv_h=one.dkv_o,
        )
        two = part(heads // 2, heads, large, makes_last, 12, None, halfway(one))
        return types.SimpleNamespace(**{**vars(one), **vars(two)})

    def weight_grads(plan, side, arrays, scratch, after=()):
        blocks = ((2, width, width), bf16)
        call = launch(
            contract_blocks,
            plan,
            side,
            plain,
            dict(),
            arrays,
            dict(sent_o=blocks, kept_o=blocks),
            dict(**scratch, blocks=((4, width, width), bf16)),
            36,
            8,
            after=after,
        )
        return call.sent_o, call.kept_o

    def first_sums(halves, section=None):
        sent, kept = halves
        got = send(sent, to_core, section)

        def block(side):
            return sum(
                lax.dynamic_index_in_dim(part, side, 0, keepdims=False).astype(f32)
                for part in (kept, got)
            )

        return block(1 - x).astype(bf16), block(x)

    def middle_sums(sums, section=None):
        away, total = sums
        return (total + send(away, to_x, section).astype(f32)).astype(bf16)

    def last_sums(totals, *later):
        rows = width // group
        shares = jnp.concatenate([total.reshape(group, rows, width) for total in totals], axis=1)

        def share(step):
            return lax.dynamic_index_in_dim(shares, lax.rem(z + step, group), 0, keepdims=False)

        parts = [share(0)]
        for step in range(1, group):
            parts.append(send(share(step), along_z(step)))
        if later:
            parts = [fence(part, *later) for part in parts]
        return sum(part.astype(f32) for part in parts).astype(bf16)

    def along_z(step):
        return lambda t, i, k, c: (t, i, (k + step) % group, c)

    def gather_z(share):
        return [share] + [send(share, along_z(step)) for step in range(1, group)]

    def gain_block(rows):
        filled = jnp.concatenate([jnp.stack(rows), jnp.zeros((16 - len(rows), width), f32)])
        return filled.astype(bf16)

    def spread(targets, own, own_x, outs, parts):
        return launch(
            spread_pieces,
            targets,
            None,
            plain,
            dict(),
            dict(own_h=own, own_x_h=own_x, other_h=exchange(own), other_x_h=exchange(own_x)),
            outs,
            dict(
                pieces=((4,) + own.shape, bf16),
                wide=((4 * group * parts, width // group, width), f32),
            ),
            8 + 4 * group * parts,
            5,
        )

    tokens, all_tokens = micros * length, 2 * micros * length
    turn, turn_all = ((width, tokens), bf16), ((width, all_tokens), bf16)
    narrow, narrow_all = ((tokens, width), bf16), ((all_tokens, width), bf16)
    pair_all = ((all_tokens, 2 * width), bf16)
    deep = ((tokens, hidden), bf16)

    def part_of(buffer, *sources):
        return lambda column: (buffer, sources, column)

    def key_rows(buffer, sources):
        first, second = pl.ds(0, length), pl.ds(length, length)
        return part_of(buffer, *[source.at[rows] for rows in (first, second) for source in sources])

    def cross_plan(r):
        rows = pl.ds(0, length)
        low_part = part_of(r.low, r.low0_h, r.low1_h)
        att_part = part_of(r.att, r.att0_h, r.att1_h)
        dq_part = part_of(r.dq, r.dq0_h, r.dq1_h)
        branch_part = part_of(r.branch, r.branch0_h, r.branch1_h)
        sources = (r.mem0_h, r.mem1_h, r.mem2_h, r.mem3_h)
        mem_part = part_of(r.mem, *[source.at[rows] for source in sources])
        pair_part = key_rows(r.pair, (r.pair0_h, r.pair1_h))
        return [
            (r.turn, low_part(0), dq_part(0)),
            (r.turn_att, att_part(0), branch_part(0)),
            (r.turn_all, mem_part(0), pair_part(0)),
            (r.turn_all, mem_part(0), pair_part(1)),
        ]

    def rising_plan(r):
        low_part = part_of(r.low, r.low0_h, r.low1_h)
        up_part = part_of(r.up, r.up0_h, r.up1_h)
        return [(r.turn, low_part(0), up_part(block)) for block in range(4)]

    def falling_plan(r):
        act_part = part_of(r.act, r.act0_h, r.act1_h)
        down_part = part_of(r.down, r.down0_h, r.down1_h)
        return [(r.turn, act_part(block), down_part(0)) for block in range(4)]

    def self_plan(r):
        rows = pl.ds(0, length)
        sources = (r.x0_h, r.x1_h, r.x2_h, r.x3_h)
        x_part = part_of(r.x, *[source.at[rows] for source in sources])
        dq_part = part_of(r.dq, r.dq0_h, r.dq1_h)
        pair_part = key_rows(r.pair, (r.pair0_h, r.pair1_h))
        att_part = part_of(r.att, r.att0_h, r.att1_h)
        branch_part = part_of(r.branch, r.branch0_h, r.branch1_h)
        return [
            (r.turn_all, x_part(0), dq_part(0)),
            (r.turn_all, x_part(0), pair_part(0)),
            (r.turn_all, x_part(0), pair_part(1)),
            (r.turn, att_part(0), branch_part(0)),
        ]

    last = micros - 1
    feeds, ends = [None] * micros, [None] * micros
    cross_halves = weight_grads(
        cross_plan,
        1,
        dict(
            low0_h=forward[0].first_low_o,
            low1_h=forward[1].first_low_o,
            dq0_h=cross[0].dq_low_o,
            dq1_h=cross[1].dq_low_o,
            att0_h=cross[0].att_o,
            att1_h=cross[1].att_o,
            branch0_h=cross[0].branch_o,
            branch1_h=cross[1].branch_o,
            mem0_h=memories[0],
            mem1_h=memories[1],
            mem2_h=memories_other[0],
            mem3_h=memories_other[1],
            pair0_h=cross[0].dkv_o,
            pair1_h=cross[1].dkv_o,
        ),
        dict(
            low=narrow,
            dq=narrow,
            att=narrow,
            branch=narrow,
            mem=narrow_all,
            pair=pair_all,
            turn=turn,
            turn_att=turn,
            turn_all=turn_all,
        ),
        (made[last],),
    )
    cross_sums = first_sums(cross_halves, 1)
    results = jnp.stack(
        [
            jnp.where(decoder, call.decoded_o, done.memory_o[:length])
            for call, done in zip(cross, forward)
        ]
    )
    results = send(results, to_row)
    latest = made[last]

    def part_sum(micro, *before):
        end = ends[micro]
        away = fence(end.part_other_o, *before)
        total = (end.part_own_o + exchange(away).astype(f32)).astype(bf16)
        return total, send(total, to_row)

    steps = []
    for micro in range(last):
        feeds[micro] = backward_feed(micro, (latest,))
        first = feeds[micro].grad_first_o
        ends[micro] = backward_self(micro, 0, first)
        ends[micro] = backward_self(micro, 1, first, vars(ends[micro]), (cross_sums[0], grads_memory[last]))
        cross_total = middle_sums(cross_sums, 1)
        steps.append(part_sum(micro, cross_total))
        latest = ends[micro].gain_early_o
    feeds[last] = backward_feed(last, (latest,))

    rising_halves = weight_grads(
        rising_plan,
        None,
        dict(
            low0_h=cross[0].ffn_low_o,
            low1_h=cross[1].ffn_low_o,
            up0_h=feeds[0].up_grad_o,
            up1_h=feeds[1].up_grad_o,
        ),
        dict(low=narrow, up=deep, turn=turn),
        (results,) + tuple(step[0] for step in steps),
    )
    rising_sums = first_sums(rising_halves)
    rising_total = middle_sums(rising_sums)
    falling_halves = weight_grads(
        falling_plan,
        None,
        dict(
            act0_h=cross[0].act_o,
            act1_h=cross[1].act_o,
            down0_h=feeds[0].down_grad_o,
            down1_h=feeds[1].down_grad_o,
        ),
        dict(act=deep, down=narrow, turn=turn),
        (rising_sums[0],),
    )
    falling_sent = fence(falling_halves[0], rising_total)
    falling_sums = first_sums((falling_sent, falling_halves[1]))
    falling_total = middle_sums(falling_sums)
    shares = []

    third = sum(call.gain_grads_o[1] for call in cross)

    def halfway(one):
        both = last_sums((rising_total, cross_total), one.gain_early_o)
        rows = width // group
        found = jnp.concatenate([both[rows:], gain_block([third])])
        shares.extend([both[:rows], found, send(found, to_encoder)])
        return (both, falling_total)

    ends[last] = backward_self(
        last,
        None,
        feeds[last].grad_first_o,
        None,
        (falling_sums[0],),
        halfway,
    )
    finished = ends[last].part_own_o
    falling_share = last_sums((falling_total,), ends[last].gain_early_o, finished)
    rising_share, found, arrived = shares
    cross_share = jnp.where(decoder, found, fence(arrived, finished))
    one_own = gather_z(jnp.concatenate([rising_share, falling_share, cross_share]))
    steps.append(part_sum(last, falling_share, arrived, steps[0][1]))

    self_halves = weight_grads(
        self_plan,
        None,
        dict(
            x0_h=own[0],
            x1_h=own[1],
            x2_h=other[0],
            x3_h=other[1],
            dq0_h=ends[0].dq_low_o,
            dq1_h=ends[1].dq_low_o,
            pair0_h=ends[0].dkv_o,
            pair1_h=ends[1].dkv_o,
            att0_h=forward[0].att_o,
            att1_h=forward[1].att_o,
            branch0_h=ends[0].branch_o,
            branch1_h=ends[1].branch_o,
        ),
        dict(
            x=narrow_all,
            dq=narrow,
            pair=pair_all,
            att=narrow,
            branch=narrow,
            turn=turn,
            turn_all=turn_all,
        ),
        (steps[last][0],),
    )
    away, total = first_sums(
        (fence(self_halves[0], one_own[1], steps[last][1]), self_halves[1])
    )
    self_total = middle_sums((away, total))
    one_own = jnp.stack([one_own[0]] + [fence(part, self_total) for part in one_own[1:]])
    self_share = last_sums((self_total,))
    one_own_x = send(fence(one_own, self_total), to_x)

    early = sum(end.gain_early_o[0] for end in ends)
    late = jnp.where(
        decoder,
        sum(call.gain_grads_o[0] for call in cross),
        sum(call.gain_late_o[0] for call in feeds),
    )
    two_own = jnp.stack(
        gather_z(jnp.concatenate([self_share, gain_block([early, late])]))
    )
    two_own_x = send(fence(two_own, one_own_x), to_x)

    def columns(block):
        return pl.ds(block * width, width)

    def one_targets(r, block, row, rows):
        lines = pl.ds(row, rows)
        feed = [r.up_o.at[lines, columns(block)], r.down_o.at[pl.ds(block * width + row, rows)]]
        if block >= 2:
            return feed + [r.pair_o.at[lines, columns(block - 2)]]
        return feed + [(r.out_o if block else r.query_o).at[lines]]

    def two_targets(r, block, row, rows):
        lines = pl.ds(row, rows)
        return [r.out_o.at[lines] if block == 3 else r.mixed_o.at[lines, columns(block)]]

    square_out = ((width, width), f32)
    one_own_x = fence(one_own_x, two_own)
    one_grads = spread(
        one_targets,
        one_own,
        one_own_x,
        dict(
            up_o=((width, hidden), f32),
            query_o=square_out,
            pair_o=((width, 2 * width), f32),
            down_o=((hidden, width), f32),
            out_o=square_out,
            gains_o=((1, width), f32),
        ),
        3,
    )
    two_own_x = fence(two_own_x, one_grads.gains_o)
    two_grads = spread(
        two_targets,
        two_own,
        two_own_x,
        dict(
            mixed_o=((width, 3 * width), f32),
            out_o=square_out,
            gains_o=((2, width), f32),
        ),
        1,
    )

    grad_input = jnp.stack([step[1] for step in steps])
    return (
        results[None, :, None],
        grad_input.astype(f32)[None, :, None],
        two_grads.mixed_o[None],
        two_grads.out_o[None],
        one_grads.up_o[None],
        one_grads.down_o[None],
        two_grads.gains_o[None],
        one_grads.query_o,
        one_grads.pair_o,
        one_grads.out_o,
        one_grads.gains_o[0],
    )


def shards(*arrays):
    layer_input = arrays[0]
    micros, rows, length = layer_input.shape[1:4]
    simple = (
        lax.axis_size("section") == 2
        and lax.axis_size("seq") == 2
        and lax.axis_size("dp") in (4, 8, 16)
        and (micros, rows) == (2, 1)
        and length == layer_input.shape[-1] == CHUNK
        and arrays[4].shape[-1] == 4 * CHUNK
    )
    return split_rows(*arrays) if simple else any_rows(*arrays)


def solution(mesh):
    in_specs = (
        P("section", None, "dp", "seq", None),
        P("section", None, "dp", "seq"),
        P("section", None, None),
        P("section", None, None),
        P("section", None, None),
        P("section", None, None),
        P("section", None, None),
        P(),
        P(),
        P(),
        P(),
        P(None, "dp", "seq", None),
    )
    out_specs = (
        P("section", None, "dp", "seq", None),
        P("section", None, "dp", "seq", None),
        P("section", None, None),
        P("section", None, None),
        P("section", None, None),
        P("section", None, None),
        P("section", None, None),
        P(),
        P(),
        P(),
        P(),
    )
    return jax.shard_map(shards, mesh=mesh, in_specs=in_specs, out_specs=out_specs, check_vma=False)
```

```python
import types

import jax
import jax.numpy as jnp
from jax import lax
from jax.experimental import pallas as pl
from jax.experimental.pallas import tpu as pltpu
from jax.sharding import PartitionSpec as P

HEADS = 8
TILE = 256
LANES = 128
CHUNK = 512

f32 = jnp.float32
bf16 = jnp.bfloat16
negative_big = -1e30
epsilon = 1e-05


def dot(left, right):
    return lax.dot_general(left, right, (((1,), (0,)), ((), ())), preferred_element_type=f32)


def dot_nt(left, right):
    return lax.dot_general(left, right, (((1,), (1,)), ((), ())), preferred_element_type=f32)


def dot_tn(left, right):
    return lax.dot_general(left, right, (((0,), (0,)), ((), ())), preferred_element_type=f32)


def standardize(values):
    center = values - jnp.mean(values, axis=-1, keepdims=True)
    inverse = lax.rsqrt(jnp.mean(center * center, axis=-1, keepdims=True) + epsilon)
    return center * inverse, inverse


def standardize_back(grad_out, standard, gain_row, inverse):
    scaled = grad_out * gain_row
    grad_in = inverse * (
        scaled
        - jnp.mean(scaled, axis=-1, keepdims=True)
        - standard * jnp.mean(scaled * standard, axis=-1, keepdims=True)
    )
    return grad_in, jnp.sum(grad_out * standard, axis=0, keepdims=True)


class Copies:
    def __init__(self, sems):
        self.sems = sems
        self.used = 0

    def start(self, source, target):
        copy = pltpu.make_async_copy(source, target, self.sems.at[self.used])
        self.used += 1
        copy.start()
        return copy


def wait_all(copies):
    for copy in copies:
        copy.wait()


def spread_pairs(target, source, factor, pairs):
    tiles = target.shape[1]
    half = lax.broadcasted_iota(jnp.int32, (TILE, LANES), 1) < LANES // 2
    first = jnp.where(half, factor, 0.0).astype(bf16)
    second = jnp.where(half, 0.0, factor).astype(bf16)
    for tile in range(tiles):
        for pair in pairs:
            block = source[tile * TILE : (tile + 1) * TILE, pair * LANES : (pair + 1) * LANES]
            target[pair, tile, :TILE, :] = block * first
            target[pair, tile, TILE:, :] = block * second


def turn_tiles(target, source, column, pairs):
    low, high = pairs[0] * LANES, (pairs[-1] + 1) * LANES
    for tile in range(target.shape[0]):
        block = source[tile * TILE : (tile + 1) * TILE, column + low : column + high]
        target[tile, low:high, :] = jnp.transpose(block)


def place_documents(r, copies):
    wait_all(copies)
    q_tiles = r.qd.shape[0]
    for part in range(3):
        row = r.docs[part].astype(f32)[0:1, :]
        for tile in range(q_tiles):
            piece = row[:, tile * TILE : (tile + 1) * TILE]
            slot = part * q_tiles + tile
            r.bounds[0, slot] = jnp.min(piece).astype(jnp.int32)
            r.bounds[1, slot] = jnp.max(piece).astype(jnp.int32)
            if part == 0:
                r.qd[tile] = jnp.broadcast_to(piece, (8, TILE))
        if part > 0:
            for start in range(0, row.shape[1], LANES):
                block = jnp.broadcast_to(row[:, start : start + LANES], (LANES, LANES))
                place = (part - 1) * row.shape[1] + start
                r.kdc[place : place + LANES, :] = jnp.transpose(block)


def load_documents(r, move, queries, own, other):
    rows = pl.ds(r.docs.shape[2], r.docs.shape[1])
    return [
        move.start(source.at[rows], r.docs.at[part])
        for part, source in enumerate((queries, own, other))
    ]


def tile_place(r, core, causal, q_tile, k_tile):
    q_tiles = r.qd.shape[0]
    length = q_tiles * TILE
    owner = jnp.where(k_tile < q_tiles, core, 1 - core)
    k_start = owner * length + lax.rem(k_tile, q_tiles) * TILE
    ahead = core * length + q_tile * TILE - k_start
    ahead = jnp.where(causal == 1, ahead, 2 * length * TILE)
    q_low, q_high = r.bounds[0, q_tile], r.bounds[1, q_tile]
    k_low, k_high = r.bounds[0, q_tiles + k_tile], r.bounds[1, q_tiles + k_tile]
    active = (q_low <= k_high) & (k_low <= q_high) & (ahead > -TILE)
    whole = (q_low == k_high) & (k_low == q_high) & (ahead >= TILE)
    return active, whole, ahead


def each_tile(place, body):
    active, whole, ahead = place
    pl.when(active & jnp.logical_not(whole))(lambda: body(ahead))
    pl.when(whole)(lambda: body(None))


def fill_bias(r, q_tile, k_tile, ahead):
    keys = r.kdc[pl.ds(pl.multiple_of(k_tile * TILE, TILE), TILE), :]
    shift = lax.broadcasted_iota(jnp.int32, (TILE, LANES), 0) - lax.broadcasted_iota(
        jnp.int32, (TILE, LANES), 1
    )
    queries = r.qd[q_tile]
    for start in range(0, TILE, LANES):
        same = keys == queries[0:1, start : start + LANES]
        allowed = same & (shift - start <= ahead)
        r.bias[:, start : start + LANES] = jnp.where(allowed, 0.0, negative_big)


def attention_forward(r, core, causal):
    pairs, q_tiles = r.qm.shape[:2]
    k_tiles = r.vt.shape[0]

    def one_query_tile(q_tile, carry):
        r.top[...] = jnp.full(r.top.shape, negative_big, f32)
        r.total[...] = jnp.zeros(r.total.shape, f32)
        r.turned[...] = jnp.zeros(r.turned.shape, f32)

        def one_key_tile(k_tile, inner):
            def one_tile(ahead):
                if ahead is not None:
                    fill_bias(r, q_tile, k_tile, ahead)
                rows = pl.ds(pl.multiple_of(k_tile * TILE, TILE), TILE)

                def raw(pair):
                    keys = r.kv[rows, pair * LANES : (pair + 1) * LANES]
                    return dot_nt(keys, r.qm[pair, q_tile])

                raw_next = raw(0)
                for pair in range(pairs):
                    scores = raw_next
                    if ahead is not None:
                        bias = r.bias[...]
                        scores = scores + jnp.concatenate([bias, bias], axis=1)
                    if pair + 1 < pairs:
                        raw_next = raw(pair + 1)
                    old_top = r.top[pair : pair + 1, :]
                    new_top = jnp.maximum(old_top, jnp.max(scores, axis=0, keepdims=True))
                    weights = jnp.exp(scores - new_top)
                    shrink = jnp.exp(old_top - new_top)
                    r.top[pair : pair + 1, :] = new_top
                    r.total[pair : pair + 1, :] = r.total[
                        pair : pair + 1, :
                    ] * shrink + jnp.sum(weights, axis=0, keepdims=True)
                    low = weights.astype(bf16)
                    for side in range(2):
                        span = slice(side * TILE, (side + 1) * TILE)
                        head = slice((2 * pair + side) * 64, (2 * pair + side + 1) * 64)
                        r.turned[head, :] = r.turned[head, :] * shrink[:, span] + dot(
                            r.vt[k_tile, head, :], low[:, span]
                        )

            each_tile(tile_place(r, core, causal, q_tile, k_tile), one_tile)
            return inner

        lax.fori_loop(0, k_tiles, one_key_tile, 0)
        for pair in range(pairs):
            total = r.total[pair : pair + 1, :]
            r.lse[q_tile, pair : pair + 1, :] = r.top[pair : pair + 1, :] + jnp.log(total)
            share = 1.0 / total
            for side in range(2):
                span = slice(side * TILE, (side + 1) * TILE)
                head = slice((2 * pair + side) * 64, (2 * pair + side + 1) * 64)
                r.turned[head, :] = r.turned[head, :] * share[:, span]
        rows = pl.ds(pl.multiple_of(q_tile * TILE, TILE), TILE)
        r.att[rows, :] = jnp.transpose(r.turned[...]).astype(bf16)
        return carry

    lax.fori_loop(0, q_tiles, one_query_tile, 0)


def row_products(r, grad_att, pairs):
    low, high = pairs[0] * LANES, (pairs[-1] + 1) * LANES
    for tile in range(r.qm.shape[1]):
        rows = slice(tile * TILE, (tile + 1) * TILE)
        product = jnp.transpose(
            grad_att[rows, low:high].astype(f32) * r.att[rows, low:high].astype(f32)
        )
        for pair in pairs:
            for side in range(2):
                head = (2 * pair + side) * 64 - low
                r.delta[tile, pair : pair + 1, side * TILE : (side + 1) * TILE] = jnp.sum(
                    product[head : head + 64, :], axis=0, keepdims=True
                )


def attention_backward(r, core, causal, pairs):
    q_tiles, k_tiles = r.qm.shape[1], r.kt.shape[0]
    width = r.kt.shape[1]
    low, high = pairs[0] * LANES, (pairs[-1] + 1) * LANES
    for start in (0, width):
        r.dkv[:, start + low : start + high] = jnp.zeros((r.dkv.shape[0], high - low), f32)

    def one_query_tile(q_tile, carry):
        r.turned[low:high, :] = jnp.zeros((high - low, TILE), f32)

        def one_key_tile(k_tile, inner):
            def one_tile(ahead):
                if ahead is not None:
                    fill_bias(r, q_tile, k_tile, ahead)
                rows = pl.ds(pl.multiple_of(k_tile * TILE, TILE), TILE)

                def raw(pair):
                    lanes = slice(pair * LANES, (pair + 1) * LANES)
                    lanes_v = slice(width + pair * LANES, width + (pair + 1) * LANES)
                    return (
                        dot_nt(r.kv[rows, lanes], r.qm[pair, q_tile]),
                        dot_nt(r.kv[rows, lanes_v], r.gm[pair, q_tile]),
                    )

                raw_next = raw(pairs[0])
                for pair in pairs:
                    scores, grad_probs = raw_next
                    if ahead is not None:
                        bias = r.bias[...]
                        scores = scores + jnp.concatenate([bias, bias], axis=1)
                    if pair < pairs[-1]:
                        raw_next = raw(pair + 1)
                    probs = jnp.exp(scores - r.lse[q_tile, pair : pair + 1, :])
                    grad_scores = probs * (grad_probs - r.delta[q_tile, pair : pair + 1, :])
                    probs_low = probs.astype(bf16)
                    grad_low = grad_scores.astype(bf16)
                    lanes = slice(pair * LANES, (pair + 1) * LANES)
                    lanes_v = slice(width + pair * LANES, width + (pair + 1) * LANES)
                    r.dkv[rows, lanes] += dot(grad_low, r.qm[pair, q_tile])
                    r.dkv[rows, lanes_v] += dot(probs_low, r.gm[pair, q_tile])
                    for side in range(2):
                        span = slice(side * TILE, (side + 1) * TILE)
                        head = slice((2 * pair + side) * 64, (2 * pair + side + 1) * 64)
                        r.turned[head, :] += dot(r.kt[k_tile, head, :], grad_low[:, span])

            each_tile(tile_place(r, core, causal, q_tile, k_tile), one_tile)
            return inner

        lax.fori_loop(0, k_tiles, one_key_tile, 0)
        rows = pl.ds(pl.multiple_of(q_tile * TILE, TILE), TILE)
        r.dq[rows, low:high] = jnp.transpose(r.turned[low:high, :]) * (64**-0.5)
        return carry

    lax.fori_loop(0, q_tiles, one_query_tile, 0)


def feed_forward(r, low):
    chunks = [slice(at, at + CHUNK) for at in range(0, r.w_in.shape[1], CHUNK)]
    upward_next = dot(low[...], r.w_in[:, chunks[0]])
    for place, span in enumerate(chunks):
        upward = upward_next
        if place + 1 < len(chunks):
            upward_next = dot(low[...], r.w_in[:, chunks[place + 1]])
        gate = jax.nn.sigmoid(upward)
        active = (upward * gate).astype(bf16)
        r.act[:, span] = active
        r.slope[:, span] = (gate + upward * gate * (1.0 - gate)).astype(r.slope.dtype)
        part = dot(active, r.w_down[span, :])
        if place:
            r.sum[...] += part
        else:
            r.sum[...] = part


def feed_backward(r):
    chunks = [slice(at, at + CHUNK) for at in range(0, r.w_in.shape[1], CHUNK)]
    active_next = dot_nt(r.down_grad[...], r.w_down[chunks[0], :])
    for place, span in enumerate(chunks):
        grad_active = active_next.astype(bf16)
        if place + 1 < len(chunks):
            active_next = dot_nt(r.down_grad[...], r.w_down[chunks[place + 1], :])
        grad_up = (grad_active.astype(f32) * r.slope[:, span].astype(f32)).astype(bf16)
        r.up_grad[:, span] = grad_up
        part = dot_nt(grad_up, r.w_in[:, span])
        if place:
            r.sum[...] += part
        else:
            r.sum[...] = part


def self_forward(r):
    length, width = r.unit1.shape
    decoder, core = r.meta[0], r.meta[1]
    move = Copies(r.sems)
    whole = pl.ds(0, length)
    documents = load_documents(r, move, r.x_own_h, r.x_own_h, r.x_other_h)
    early = [
        move.start(r.x_own_h.at[whole], r.x.at[whole]),
        move.start(r.x_other_h.at[whole], r.x.at[pl.ds(length, length)]),
        move.start(r.w_mixed_h, r.w_mixed),
    ]
    later = [
        move.start(r.w_out_h, r.w_out),
        move.start(r.w_in_h, r.w_in),
        move.start(r.w_down_h, r.w_down),
    ]
    place_documents(r, documents)
    wait_all(early)
    r.q[...] = dot(r.x[:length, :], r.w_mixed[:, :width]).astype(bf16)
    r.kv[...] = dot(r.x[...], r.w_mixed[:, width:]).astype(bf16)
    outs = [move.start(r.q, r.q_o), move.start(r.kv, r.kv_o)]
    pairs = range(width // LANES)
    spread_pairs(r.qm, r.q, 64**-0.5, pairs)
    turn_tiles(r.vt, r.kv, width, pairs)
    attention_forward(r, core, decoder)
    wait_all(later)
    outs += [move.start(r.att, r.att_o), move.start(r.lse, r.lse_o)]
    unit, inverse = standardize(r.x[:length, :].astype(f32) + dot(r.att[...], r.w_out[...]))
    r.unit1[...] = unit
    r.inv1[...] = jnp.broadcast_to(inverse, r.inv1.shape)
    r.first_low[...] = (unit * r.gains[0:1, :]).astype(bf16)
    outs += [
        move.start(r.unit1, r.unit1_o),
        move.start(r.inv1, r.inv1_o),
        move.start(r.first_low, r.first_low_o),
    ]

    @pl.when(decoder == 0)
    def _():
        feed_forward(r, r.first_low)
        late = [
            move.start(r.first_low, r.ffn_low_o),
            move.start(r.act, r.act_o),
            move.start(r.slope, r.slope_o),
        ]
        unit2, inverse2 = standardize(r.unit1[...] * r.gains[0:1, :] + r.sum[...])
        r.memory[:length, :] = (unit2 * r.gains[1:2, :]).astype(bf16)
        r.memory[length:, :] = r.docs[0]
        late += [move.start(r.memory, r.memory_o)]
        r.unit2[...] = unit2
        r.inv2[...] = jnp.broadcast_to(inverse2, r.inv2.shape)
        late += [move.start(r.unit2, r.unit2_o), move.start(r.inv2, r.inv2_o)]
        wait_all(late)

    wait_all(outs)


def cross_both_ways(r):
    length, width = r.unit1_h.shape
    core = r.meta[1]
    move = Copies(r.sems)
    whole = pl.ds(0, length)
    documents = load_documents(r, move, r.x_own_h, r.memory_own_h, r.memory_other_h)
    moves = [
        move.start(r.memory_own_h.at[whole], r.x.at[whole]),
        move.start(r.memory_other_h.at[whole], r.x.at[pl.ds(length, length)]),
        move.start(r.w_pair_h, r.w_pair),
        move.start(r.first_low_h, r.first_low),
        move.start(r.w_query_h, r.w_query),
    ]
    later = [
        move.start(r.unit1_h, r.unit1),
        move.start(r.w_cross_h, r.w_cross),
        move.start(r.w_in_h, r.w_in),
        move.start(r.w_down_h, r.w_down),
        move.start(r.cot_h.at[r.micro], r.cot),
    ]
    place_documents(r, documents)
    wait_all(moves)
    r.kv[...] = dot(r.x[...], r.w_pair[...]).astype(bf16)
    r.q[...] = dot(r.first_low[...], r.w_query[...]).astype(bf16)
    pairs = range(width // LANES)
    spread_pairs(r.qm, r.q, 64**-0.5, pairs)
    turn_tiles(r.vt, r.kv, width, pairs)
    turn_tiles(r.kt, r.kv, 0, pairs)
    attention_forward(r, core, 0)
    outs = [move.start(r.att, r.att_o)]
    wait_all(later)
    first = r.unit1[...] * r.gains[0:1, :]
    unit, inverse = standardize(first + dot(r.att[...], r.w_cross[...]))
    r.unit2[...] = unit
    r.inv2[...] = jnp.broadcast_to(inverse, r.inv2.shape)
    r.second_low[...] = (unit * r.cross_gain[...]).astype(bf16)
    outs += [move.start(r.second_low, r.ffn_low_o)]
    feed_forward(r, r.second_low)
    outs += [move.start(r.act, r.act_o)]
    unit3, inverse3 = standardize(r.unit2[...] * r.cross_gain[...] + r.sum[...])
    r.decoded[...] = (unit3 * r.gains[1:2, :]).astype(bf16)
    outs += [move.start(r.decoded, r.decoded_o)]
    grad_third, gain_late = standardize_back(
        r.cot[...].astype(f32), unit3, r.gains[1:2, :], inverse3
    )
    r.keep[...] = grad_third
    r.down_grad[...] = grad_third.astype(bf16)
    outs += [move.start(r.down_grad, r.down_grad_o)]
    feed_backward(r)
    outs += [move.start(r.up_grad, r.up_grad_o)]
    grad_sum, gain_cross = standardize_back(
        r.keep[...] + r.sum[...], r.unit2[...], r.cross_gain[...], r.inv2[:, 0:1]
    )
    r.gain_grads[...] = jnp.zeros(r.gain_grads.shape, f32)
    r.gain_grads[0:1, :] = gain_late
    r.gain_grads[1:2, :] = gain_cross
    r.keep[...] = grad_sum
    r.branch[...] = grad_sum.astype(bf16)
    outs += [move.start(r.gain_grads, r.gain_grads_o), move.start(r.branch, r.branch_o)]
    r.q[...] = dot_nt(r.branch[...], r.w_cross[...]).astype(bf16)
    spread_pairs(r.gm, r.q, 1.0, pairs)
    row_products(r, r.q, pairs)
    attention_backward(r, core, 0, pairs)
    r.dq_low[...] = r.dq[...].astype(bf16)
    r.keep[...] += dot_nt(r.dq_low[...], r.w_query[...])
    outs += [move.start(r.dq_low, r.dq_low_o), move.start(r.keep, r.grad_first_o)]
    r.dkv_low[...] = r.dkv[...].astype(bf16)
    outs += [move.start(r.dkv_low, r.dkv_o)]
    part = dot_nt(r.dkv_low[...], r.w_pair[...])
    r.part_other[...] = part[length:, :].astype(bf16)
    r.part_own[...] = part[:length, :]
    outs += [move.start(r.part_other, r.part_other_o), move.start(r.part_own, r.part_own_o)]
    wait_all(outs)


def feed_backward_alone(r):
    move = Copies(r.sems)
    early = [
        move.start(r.grad_memory_h, r.cot),
        move.start(r.unit2_h, r.unit2),
        move.start(r.inv2_h, r.inv2),
    ]
    later = [
        move.start(r.w_down_h, r.w_down),
        move.start(r.slope_h, r.slope),
        move.start(r.w_in_h, r.w_in),
    ]
    wait_all(early)
    grad_third, gain_late = standardize_back(
        r.cot[...].astype(f32), r.unit2[...], r.gains[1:2, :], r.inv2[:, 0:1]
    )
    r.gain_grads[...] = jnp.broadcast_to(gain_late, r.gain_grads.shape)
    r.keep[...] = grad_third
    r.down_grad[...] = grad_third.astype(bf16)
    outs = [move.start(r.down_grad, r.down_grad_o), move.start(r.gain_grads, r.gain_late_o)]
    wait_all(later)
    feed_backward(r)
    outs += [move.start(r.up_grad, r.up_grad_o)]
    r.keep[...] += r.sum[...]
    outs += [move.start(r.keep, r.grad_first_o)]
    wait_all(outs)


def self_backward(r, plan):
    r.micro, first, last = plan
    length, width = r.att_h.shape
    decoder, core = r.meta[0], r.meta[1]
    pairs = range(first, last)
    low, high = first * LANES, last * LANES
    move = Copies(r.sems)
    later = [
        move.start(r.q_h, r.q),
        move.start(r.kv_h, r.kv),
        move.start(r.att_h, r.att),
        move.start(r.lse_h, r.lse),
    ]
    if first == 0:
        early = [
            move.start(r.grad_first_h, r.keep),
            move.start(r.unit1_h, r.unit1),
            move.start(r.inv1_h, r.inv1),
            move.start(r.w_out_h, r.w_out),
        ]
    else:
        early = [move.start(r.grad_att_h, r.grad_att)]
    outs = []
    place_documents(r, load_documents(r, move, r.x_own_h, r.x_own_h, r.x_other_h))
    wait_all(early)
    if first == 0:
        grad_sum, gain_early = standardize_back(
            r.keep[...], r.unit1[...], r.gains[0:1, :], r.inv1[:, 0:1]
        )
        r.gain_grads[...] = jnp.broadcast_to(gain_early, r.gain_grads.shape)
        r.keep[...] = grad_sum
        r.branch[...] = grad_sum.astype(bf16)
        r.grad_att[...] = dot_nt(r.branch[...], r.w_out[...]).astype(bf16)
        outs += [move.start(r.gain_grads, r.gain_early_o), move.start(r.branch, r.branch_o)]
        if last < width // LANES:
            outs += [move.start(r.keep, r.grad_sum_o), move.start(r.grad_att, r.grad_att_o)]
    wait_all(later)
    if last == width // LANES:
        ends = [move.start(r.w_mixed_h, r.w_mixed)]
        if first > 0:
            ends += [
                move.start(r.grad_sum_h, r.keep),
                move.start(r.dq_h.at[:, pl.ds(0, low)], r.dq_low.at[:, pl.ds(0, low)]),
                move.start(r.dkv_h.at[:, pl.ds(0, low)], r.dkv_low.at[:, pl.ds(0, low)]),
                move.start(
                    r.dkv_h.at[:, pl.ds(width, low)], r.dkv_low.at[:, pl.ds(width, low)]
                ),
            ]
    spread_pairs(r.qm, r.q, 64**-0.5, pairs)
    turn_tiles(r.kt, r.kv, 0, pairs)
    spread_pairs(r.gm, r.grad_att, 1.0, pairs)
    row_products(r, r.grad_att, pairs)
    attention_backward(r, core, decoder, pairs)
    r.dq_low[:, low:high] = r.dq[:, low:high].astype(bf16)
    for start in (0, width):
        span = slice(start + low, start + high)
        r.dkv_low[:, span] = r.dkv[:, span].astype(bf16)
    if last == width // LANES:
        wait_all(ends)
        outs += [move.start(r.dq_low, r.dq_low_o), move.start(r.dkv_low, r.dkv_o)]
        r.keep[...] += dot_nt(r.dq_low[...], r.w_mixed[:, :width])
        part = dot_nt(r.dkv_low[...], r.w_mixed[:, width:])
        r.part_other[...] = part[length:, :].astype(bf16)
        r.keep[...] += part[:length, :]
        outs += [move.start(r.part_other, r.part_other_o), move.start(r.keep, r.part_own_o)]
    else:
        outs.append(move.start(r.dq_low.at[:, pl.ds(low, high - low)], r.dq_low_o.at[:, pl.ds(low, high - low)]))
        for start in (0, width):
            span = pl.ds(start + low, high - low)
            outs.append(move.start(r.dkv_low.at[:, span], r.dkv_o.at[:, span]))
    wait_all(outs)


def contract_blocks(r, plan):
    for core in range(2):

        @pl.when(r.meta[1] == core)
        def _(core=core):
            targets = [None] * 4
            for half in range(2):
                target = r.kept_o if half == core else r.sent_o
                targets[2 * half], targets[2 * half + 1] = target.at[0], target.at[1]
            order = (0, 1, 2, 3) if core else (2, 3, 0, 1)
            contract_in_order(r, plan(r), order, targets, Copies(r.sems))


def contract_in_order(r, blocks, order, targets, move):
    loads = dict()
    for slot in order:
        for buffer, sources, at in blocks[slot][1:]:
            if (id(buffer), at) not in loads:
                span = pl.ds(at * CHUNK, CHUNK)
                row = 0
                copies = []
                for source in sources:
                    rows = pl.ds(row, source.shape[0])
                    copies.append(move.start(source.at[:, span], buffer.at[rows, span]))
                    row += source.shape[0]
                loads[id(buffer), at] = copies
    outs = []
    held = dict()
    for slot in order:
        turn, (left, _, left_at), (right, _, right_at) = blocks[slot]
        wait_all(loads.pop((id(left), left_at), ()))
        wait_all(loads.pop((id(right), right_at), ()))
        if held.get(id(turn)) != left_at:
            for row in range(0, left.shape[0], CHUNK):
                block = left[row : row + CHUNK, left_at * CHUNK : (left_at + 1) * CHUNK]
                turn[:, row : row + CHUNK] = jnp.transpose(block)
            held[id(turn)] = left_at
        block = right[:, right_at * CHUNK : (right_at + 1) * CHUNK]
        r.blocks[slot] = dot(turn[:, : right.shape[0]], block).astype(bf16)
        outs.append(move.start(r.blocks.at[slot], targets[slot]))
    wait_all(outs)


def spread_pieces(r, targets):
    z = r.meta[3]
    group, height = r.own_h.shape[:2]
    rows = r.own_h.shape[2] // group
    for core in range(2):
        for x in range(2):

            @pl.when((r.meta[1] == core) & (r.meta[2] == x))
            def _(core=core, x=x):
                move = Copies(r.sems)
                parts = [
                    (r.own_h, core, x),
                    (r.own_x_h, core, 1 - x),
                    (r.other_h, 1 - core, x),
                    (r.other_x_h, 1 - core, 1 - x),
                ]
                loads = [
                    move.start(source, r.pieces.at[place])
                    for place, (source, _, _) in enumerate(parts)
                ]
                outs = []
                slot = 0
                gains = None
                for place, (_, half, side) in enumerate(parts):
                    loads[place].wait()
                    for step in range(group):
                        row = pl.multiple_of(lax.rem(z + (group - step), group) * rows, rows)
                        start = 0
                        for target in targets(r, 2 * half + side, row, rows):
                            r.wide[slot] = r.pieces[place, step, start : start + rows].astype(f32)
                            outs.append(move.start(r.wide.at[slot], target))
                            slot += 1
                            start += rows
                        if start < height:
                            extra = r.pieces[place, step, start:height].astype(f32)
                            gains = extra if gains is None else gains + extra
                r.gains_o[...] = gains[: r.gains_o.shape[0], :]
                wait_all(outs)


def launch(kernel, plan, side, scalars, small, large, outs, scratch, copies, work, previous=None, after=()):
    names = list(scalars) + list(small) + list(large)
    arrays = list(scalars.values()) + list(small.values()) + list(large.values())
    specs = (
        [pl.BlockSpec(memory_space=pltpu.SMEM)] * len(scalars)
        + [pl.BlockSpec(memory_space=pltpu.VMEM)] * len(small)
        + [pl.BlockSpec(memory_space=pl.ANY)] * len(large)
    )
    aliases = dict()
    for position, name in enumerate(outs):
        if previous and name in previous:
            aliases[len(arrays)] = position
            names.append("previous_" + name)
            arrays.append(previous[name])
            specs.append(pl.BlockSpec(memory_space=pl.ANY))
    for array in after:
        names.append("")
        arrays.append(array)
        specs.append(pl.BlockSpec(memory_space=pl.ANY))
    names += list(outs) + list(scratch) + ["sems"]

    def body(*refs):
        r = types.SimpleNamespace(**dict(zip(names, refs)))

        def run():
            if isinstance(plan, int):
                r.micro = plan
                kernel(r)
            else:
                kernel(r, plan)

        if side is None:
            run()
        else:
            pl.when(r.meta[0] == side)(run)

    results = pl.pallas_call(
        body,
        out_shape=[jax.ShapeDtypeStruct(*shape) for shape in outs.values()],
        in_specs=specs,
        out_specs=[
            pl.BlockSpec(memory_space=pltpu.VMEM if shape[0][0] < 8 else pl.ANY)
            for shape in outs.values()
        ],
        scratch_shapes=[
            pltpu.SMEM(*shape) if shape[1] == jnp.int32 else pltpu.VMEM(*shape)
            for shape in scratch.values()
        ]
        + [pltpu.SemaphoreType.DMA((copies,))],
        input_output_aliases=aliases,
        compiler_params=pltpu.CompilerParams(vmem_limit_bytes=58 * 1024 * 1024),
        cost_estimate=pl.CostEstimate(
            flops=work * 10**9, bytes_accessed=1 << 20, transcendentals=0
        ),
    )(*arrays)
    return types.SimpleNamespace(**dict(zip(outs, results)))


def attention_scratch(length, width):
    pairs, q_tiles, k_tiles = width // LANES, length // TILE, 2 * length // TILE
    return dict(
        q=((length, width), bf16),
        kv=((2 * length, 2 * width), bf16),
        qm=((pairs, q_tiles, 2 * TILE, LANES), bf16),
        kdc=((2 * length, LANES), f32),
        docs=((3, 16, width), bf16),
        qd=((length // TILE, 8, TILE), f32),
        bounds=((2, 3 * length // TILE), jnp.int32),
        bias=((TILE, TILE), f32),
        lse=((q_tiles, 8, 2 * TILE), f32),
        att=((length, width), bf16),
        turned=((width, TILE), f32),
    )


def forward_scratch(length, width):
    k_tiles = 2 * length // TILE
    return dict(
        vt=((k_tiles, width, TILE), bf16),
        top=((8, 2 * TILE), f32),
        total=((8, 2 * TILE), f32),
    )


def backward_scratch(length, width):
    pairs, q_tiles, k_tiles = width // LANES, length // TILE, 2 * length // TILE
    return dict(
        kt=((k_tiles, width, TILE), bf16),
        gm=((pairs, q_tiles, 2 * TILE, LANES), bf16),
        delta=((q_tiles, 8, 2 * TILE), f32),
        dkv=((2 * length, 2 * width), f32),
        dq=((length, width), f32),
        dkv_low=((2 * length, 2 * width), bf16),
        part_other=((length, width), bf16),
        dq_low=((length, width), bf16),
    )


def for_sending(shard):

    def short(part):
        return part.astype(jnp.bfloat16) if part.dtype == jnp.float32 else part

    return jax.tree.map(short, shard)


def from_behind(block, axis, distance):
    devices = range(lax.axis_size(axis))
    route = [(i - distance, i) for i in devices if i - distance in devices]
    return lax.ppermute(block, axis, route)


def from_root(shard, axis, root):
    mine = lax.axis_index(axis) == root
    return lax.psum(jnp.where(mine, shard, jnp.zeros_like(shard)), axis)


def matmul(left_side, right_side):
    return jnp.einsum("rsd,de->rse", left_side, right_side, preferred_element_type=jnp.float32)


def matmul_back(left_side, right_side):
    return jnp.einsum("rse,de->rsd", left_side, right_side, preferred_element_type=jnp.float32)


def contract(left_side, right_side):
    return jnp.einsum("rsd,rse->de", left_side, right_side, preferred_element_type=jnp.float32)


def normalize(values, gain_row):
    center = values - jnp.mean(values, axis=-1, keepdims=True)
    inverse = lax.rsqrt(jnp.mean(center * center, axis=-1, keepdims=True) + epsilon)
    standard = center * inverse
    return (standard * gain_row, standard, inverse)


def normalize_back(grad_out, standard, gain_row, inverse):
    scaled = grad_out * gain_row
    grad_in = inverse * (
        scaled
        - jnp.mean(scaled, axis=-1, keepdims=True)
        - standard * jnp.mean(scaled * standard, axis=-1, keepdims=True)
    )
    return (grad_in, jnp.sum(grad_out * standard, axis=(0, 1)))


def allowed_mask(query_docs, key_docs, query_place, key_place, causal):
    same_doc = query_docs[:, :, None] == key_docs[:, None, :]
    earlier = query_place[:, None] >= key_place[None, :]
    return (same_doc & (earlier | jnp.logical_not(causal)))[:, None]


def attend(queries, keys_local, values_local, query_docs, key_docs, causal, is_cross):
    rows_here, shard_len, model_width = queries.shape
    head_dim = model_width // HEADS
    score_scale = head_dim ** (-0.5)
    query_place = lax.axis_index("seq") * shard_len + jnp.arange(shard_len)
    query_heads = queries.reshape(rows_here, shard_len, HEADS, head_dim)

    def absorb(state_tuple, pieces):
        running_top, running_total, running_sum = state_tuple
        key_piece, value_piece, doc_piece = pieces
        piece_len = key_piece.shape[1]
        raw_scores = jnp.einsum(
            "rqhd,rkhd->rhqk",
            query_heads,
            key_piece.reshape(rows_here, piece_len, HEADS, head_dim),
            preferred_element_type=jnp.float32,
        )
        allowed = allowed_mask(query_docs, doc_piece, query_place, jnp.arange(piece_len), causal)
        scores = jnp.where(allowed, raw_scores * score_scale, negative_big)
        new_top = jnp.maximum(running_top, jnp.max(scores, axis=-1))
        weights = jnp.where(allowed, jnp.exp(scores - new_top[..., None]), 0.0)
        new_total = jnp.sum(weights, axis=-1)
        product = jnp.einsum(
            "rhqk,rkhd->rhqd",
            weights.astype(jnp.bfloat16),
            value_piece.reshape(rows_here, piece_len, HEADS, head_dim),
            preferred_element_type=jnp.float32,
        )
        return (new_top, new_total, product)

    init_state = (
        jnp.full((rows_here, HEADS, shard_len), negative_big, jnp.float32),
        jnp.zeros((rows_here, HEADS, shard_len), jnp.float32),
        jnp.zeros((rows_here, HEADS, shard_len, head_dim), jnp.float32),
    )
    if is_cross:
        final_top, final_total, final_sum = absorb(
            init_state,
            (
                lax.all_gather(keys_local, "seq", axis=1, tiled=True),
                lax.all_gather(values_local, "seq", axis=1, tiled=True),
                lax.all_gather(for_sending(key_docs), "seq", axis=1, tiled=True),
            ),
        )
    else:
        final_top, final_total, final_sum = absorb(
            init_state,
            (
                lax.all_gather(keys_local, "seq", axis=1, tiled=True),
                lax.all_gather(values_local, "seq", axis=1, tiled=True),
                lax.all_gather(key_docs, "seq", axis=1, tiled=True),
            ),
        )
    attended = (
        (final_sum / final_total[..., None])
        .transpose(0, 2, 1, 3)
        .reshape(rows_here, shard_len, model_width)
    )
    return (attended, final_top + jnp.log(final_total))


def attend_back(
    queries,
    keys_local,
    values_local,
    query_docs,
    key_docs,
    causal,
    log_total,
    grad_attended,
    is_cross,
):
    rows_here, shard_len, model_width = queries.shape
    head_dim = model_width // HEADS
    score_scale = head_dim ** (-0.5)
    query_place = lax.axis_index("seq") * shard_len + jnp.arange(shard_len)
    if is_cross:
        keys_full, values_full, docs_full = (
            lax.all_gather(keys_local, "seq", axis=1, tiled=True),
            lax.all_gather(values_local, "seq", axis=1, tiled=True),
            lax.all_gather(for_sending(key_docs), "seq", axis=1, tiled=True).astype(key_docs.dtype),
        )
    else:
        keys_full, values_full, docs_full = (
            lax.all_gather(keys_local, "seq", axis=1, tiled=True),
            lax.all_gather(values_local, "seq", axis=1, tiled=True),
            lax.all_gather(key_docs, "seq", axis=1, tiled=True),
        )
    full_len = keys_full.shape[1]
    query_heads = queries.reshape(rows_here, shard_len, HEADS, head_dim)
    key_heads = keys_full.reshape(rows_here, full_len, HEADS, head_dim)
    value_heads = values_full.reshape(rows_here, full_len, HEADS, head_dim)
    grad_heads = grad_attended.reshape(rows_here, shard_len, HEADS, head_dim)
    raw_scores = jnp.einsum(
        "rqhd,rkhd->rhqk", query_heads, key_heads, preferred_element_type=jnp.float32
    )
    allowed = allowed_mask(query_docs, docs_full, query_place, jnp.arange(full_len), causal)
    shifted = jnp.where(allowed, raw_scores * score_scale - log_total[..., None], negative_big)
    probs = jnp.where(allowed, jnp.exp(shifted), 0.0)
    grad_probs = jnp.einsum(
        "rqhd,rkhd->rhqk", grad_heads, value_heads, preferred_element_type=jnp.float32
    )
    delta = jnp.sum(probs * grad_probs, axis=-1)
    grad_scores = (probs * (grad_probs - delta[..., None]) * score_scale).astype(jnp.bfloat16)
    grad_queries = jnp.einsum(
        "rhqk,rkhd->rqhd", grad_scores, key_heads, preferred_element_type=jnp.float32
    ).reshape(rows_here, shard_len, model_width)
    probs_low = probs.astype(jnp.bfloat16)

    def key_terms(span):
        grad_keys = jnp.einsum(
            "rhqk,rqhd->krhd", grad_scores, query_heads, preferred_element_type=jnp.float32
        )
        grad_values = jnp.einsum(
            "rhqk,rqhd->krhd", probs_low, grad_heads, preferred_element_type=jnp.float32
        )
        return jnp.concatenate(
            [
                grad_keys.reshape(span, rows_here, model_width),
                grad_values.reshape(span, rows_here, model_width),
            ],
            axis=-1,
        )

    if is_cross:
        pair_terms = lax.psum_scatter(
            key_terms(shard_len * lax.axis_size("seq")).astype(jnp.bfloat16),
            "seq",
            scatter_dimension=0,
            tiled=True,
        ).astype(jnp.float32)
    else:
        pair_terms = lax.psum_scatter(
            key_terms(shard_len * lax.axis_size("seq")).astype(jnp.bfloat16),
            "seq",
            scatter_dimension=0,
            tiled=True,
        ).astype(jnp.float32)
    return (grad_queries, pair_terms.transpose(1, 0, 2))


def layer_forward(hidden_in, doc_own, memory, memory_docs, weights, is_decoder):
    (
        qkv_weight,
        out_weight,
        in_weight,
        down_weight,
        gains_pair,
        query_weight,
        pair_weight,
        cross_weight,
        cross_gains,
    ) = weights
    model_width = hidden_in.shape[-1]
    mixed = matmul(hidden_in, qkv_weight).astype(jnp.bfloat16)
    attended, self_lse = attend(
        mixed[..., :model_width],
        mixed[..., model_width : 2 * model_width],
        mixed[..., 2 * model_width :],
        doc_own,
        doc_own,
        is_decoder,
        False,
    )
    attended = attended.astype(jnp.bfloat16)
    first, first_unit, first_inv = normalize(
        hidden_in.astype(jnp.float32) + matmul(attended, out_weight), gains_pair[0]
    )
    first_low = first.astype(jnp.bfloat16)
    cross_queries = matmul(first_low, query_weight).astype(jnp.bfloat16)
    pair = matmul(memory, pair_weight).astype(jnp.bfloat16)
    cross_att, cross_lse = attend(
        cross_queries,
        pair[..., :model_width],
        pair[..., model_width:],
        doc_own,
        memory_docs,
        False,
        True,
    )
    cross_att = cross_att.astype(jnp.bfloat16)
    second_cross, second_unit, second_inv = normalize(
        first + matmul(cross_att, cross_weight), cross_gains
    )
    second = jnp.where(is_decoder, second_cross, first)
    second_low = second.astype(jnp.bfloat16)
    upward = matmul(second_low, in_weight)
    active = jax.nn.silu(upward).astype(jnp.bfloat16)
    result, third_unit, third_inv = normalize(second + matmul(active, down_weight), gains_pair[1])
    saved = {
        "mixed": mixed,
        "attended": attended,
        "self_lse": self_lse,
        "first_unit": first_unit,
        "first_inv": first_inv,
        "first_low": first_low,
        "cross_queries": cross_queries,
        "pair": pair,
        "cross_att": cross_att,
        "cross_lse": cross_lse,
        "second_unit": second_unit,
        "second_inv": second_inv,
        "second_low": second_low,
        "upward": upward,
        "active": active,
        "third_unit": third_unit,
        "third_inv": third_inv,
    }
    return (result, saved)


def layer_backward(
    grad_result, saved, hidden_in, doc_own, memory, memory_docs, weights, is_decoder
):
    (
        qkv_weight,
        out_weight,
        in_weight,
        down_weight,
        gains_pair,
        query_weight,
        pair_weight,
        cross_weight,
        cross_gains,
    ) = weights
    model_width = hidden_in.shape[-1]
    grad_third, grad_gain_late = normalize_back(
        grad_result, saved["third_unit"], gains_pair[1], saved["third_inv"]
    )
    down_grad = grad_third.astype(jnp.bfloat16)
    grad_down_w = contract(saved["active"], down_grad)
    grad_active = matmul_back(down_grad, down_weight).astype(jnp.bfloat16)
    sigmoid_up = jax.nn.sigmoid(saved["upward"])
    grad_upward = (
        grad_active.astype(jnp.float32)
        * (sigmoid_up + saved["upward"] * sigmoid_up * (1.0 - sigmoid_up))
    ).astype(jnp.bfloat16)
    grad_in_w = contract(saved["second_low"], grad_upward)
    grad_second = grad_third + matmul_back(grad_upward, in_weight)
    grad_cross_sum, grad_cross_gain = normalize_back(
        grad_second, saved["second_unit"], cross_gains, saved["second_inv"]
    )
    decoder_flag = is_decoder.astype(jnp.float32)
    grad_cross_sum = grad_cross_sum * decoder_flag
    grad_cross_gain = grad_cross_gain * decoder_flag
    cross_branch = grad_cross_sum.astype(jnp.bfloat16)
    grad_cross_w = contract(saved["cross_att"], cross_branch)
    grad_cross_att = matmul_back(cross_branch, cross_weight).astype(jnp.bfloat16)
    pair = saved["pair"]
    grad_cross_q, grad_pair = attend_back(
        saved["cross_queries"],
        pair[..., :model_width],
        pair[..., model_width:],
        doc_own,
        memory_docs,
        False,
        saved["cross_lse"],
        grad_cross_att,
        True,
    )
    grad_cross_q = grad_cross_q.astype(jnp.bfloat16)
    grad_pair = grad_pair.astype(jnp.bfloat16)
    grad_query_w = contract(saved["first_low"], grad_cross_q)
    grad_pair_w = contract(memory, grad_pair)
    grad_memory = matmul_back(grad_pair, pair_weight)
    grad_first = jnp.where(
        is_decoder, grad_cross_sum + matmul_back(grad_cross_q, query_weight), grad_second
    )
    grad_first_sum, grad_gain_early = normalize_back(
        grad_first, saved["first_unit"], gains_pair[0], saved["first_inv"]
    )
    self_branch = grad_first_sum.astype(jnp.bfloat16)
    grad_out_w = contract(saved["attended"], self_branch)
    grad_attended = matmul_back(self_branch, out_weight).astype(jnp.bfloat16)
    mixed = saved["mixed"]
    grad_queries, grad_pair_self = attend_back(
        mixed[..., :model_width],
        mixed[..., model_width : 2 * model_width],
        mixed[..., 2 * model_width :],
        doc_own,
        doc_own,
        is_decoder,
        saved["self_lse"],
        grad_attended,
        False,
    )
    grad_mixed = jnp.concatenate([grad_queries, grad_pair_self], axis=-1).astype(jnp.bfloat16)
    grad_qkv_w = contract(hidden_in, grad_mixed)
    grad_hidden = grad_first_sum + matmul_back(grad_mixed, qkv_weight)
    layer_grads = (
        grad_qkv_w,
        grad_out_w,
        grad_in_w,
        grad_down_w,
        jnp.stack([grad_gain_early, grad_gain_late]),
        grad_query_w,
        grad_pair_w,
        grad_cross_w,
        grad_cross_gain,
    )
    return (grad_hidden, grad_memory, layer_grads)


def any_rows(
    layer_input,
    segment_ids,
    attn_qkv,
    attn_out,
    ffn_in,
    ffn_out,
    norm_gain,
    cross_query,
    cross_pair,
    cross_out,
    cross_gain,
    out_cotangent,
):
    micro_count = layer_input.shape[1]
    section_index = lax.axis_index("section")
    is_decoder = section_index == 1
    weights = (
        attn_qkv[0],
        attn_out[0],
        ffn_in[0],
        ffn_out[0],
        norm_gain[0],
        cross_query,
        cross_pair,
        cross_out,
        cross_gain,
    )
    inputs_all = layer_input[0]
    docs_all = segment_ids[0]
    slot_ids = jnp.arange(micro_count)
    received = (jnp.zeros_like(inputs_all[0]), jnp.zeros_like(docs_all[0]))
    results = jnp.zeros_like(inputs_all)
    memories = []
    memory_doc_list = []
    for step_index in range(micro_count + 1):
        batch_index = step_index - section_index
        is_valid = (batch_index >= 0) & (batch_index < micro_count)
        chosen = jnp.clip(batch_index, 0, micro_count - 1)
        hidden_in = lax.dynamic_index_in_dim(inputs_all, chosen, 0, keepdims=False)
        doc_own = lax.dynamic_index_in_dim(docs_all, chosen, 0, keepdims=False)
        memory = received[0]
        memory_docs = jnp.where(is_valid & is_decoder, received[1], doc_own)
        memories.append(memory)
        memory_doc_list.append(memory_docs)
        result, saved = layer_forward(hidden_in, doc_own, memory, memory_docs, weights, is_decoder)
        low_result = result.astype(jnp.bfloat16)
        writing = (slot_ids == chosen) & is_valid
        results = jnp.where(writing[:, None, None, None], low_result[None], results)
        if step_index < micro_count:
            received = from_behind((low_result, doc_own), "section", 1)
    memory_stack = jnp.stack(memories)
    memory_doc_stack = jnp.stack(memory_doc_list)
    totals = tuple((jnp.zeros(weight.shape, jnp.float32) for weight in weights))
    input_grads = jnp.zeros(inputs_all.shape, jnp.float32)
    returned = jnp.zeros(inputs_all.shape[1:], jnp.float32)
    for step_index in range(micro_count + 1):
        batch_index = micro_count - step_index - section_index
        is_valid = (batch_index >= 0) & (batch_index < micro_count)
        chosen = jnp.clip(batch_index, 0, micro_count - 1)
        forward_step = jnp.clip(batch_index + section_index, 0, micro_count)
        hidden_in = lax.dynamic_index_in_dim(inputs_all, chosen, 0, keepdims=False)
        doc_own = lax.dynamic_index_in_dim(docs_all, chosen, 0, keepdims=False)
        memory = lax.dynamic_index_in_dim(memory_stack, forward_step, 0, keepdims=False)
        memory_docs = lax.dynamic_index_in_dim(memory_doc_stack, forward_step, 0, keepdims=False)
        discarded, saved = layer_forward(
            hidden_in, doc_own, memory, memory_docs, weights, is_decoder
        )
        cotangent = jnp.where(
            is_decoder,
            lax.dynamic_index_in_dim(out_cotangent, chosen, 0, keepdims=False).astype(jnp.float32),
            returned,
        )
        grad_hidden, grad_memory, layer_grads = layer_backward(
            cotangent, saved, hidden_in, doc_own, memory, memory_docs, weights, is_decoder
        )
        valid_flag = is_valid.astype(jnp.float32)
        totals = tuple(
            (running + valid_flag * fresh for running, fresh in zip(totals, layer_grads))
        )
        writing = (slot_ids == chosen) & is_valid
        input_grads = jnp.where(writing[:, None, None, None], grad_hidden[None], input_grads)
        if step_index < micro_count:
            returned = from_behind(grad_memory.astype(jnp.bfloat16), "section", -1).astype(
                grad_memory.dtype
            )
    group_sums = lax.psum(
        (
            totals[0],
            totals[1],
            totals[2],
            totals[3],
            totals[4],
            totals[5],
            totals[6],
            totals[7],
            totals[8],
        ),
        ("seq", "dp"),
    )
    section_sums = group_sums[:5]
    cross_sums = (
        from_root(group_sums[5].astype(jnp.bfloat16), "section", 1).astype(jnp.float32),
        from_root(group_sums[6].astype(jnp.bfloat16), "section", 1).astype(jnp.float32),
        from_root(group_sums[7].astype(jnp.bfloat16), "section", 1).astype(jnp.float32),
        from_root(group_sums[8].astype(jnp.bfloat16), "section", 1).astype(jnp.float32),
    )
    return (
        results[None],
        input_grads[None],
        section_sums[0][None],
        section_sums[1][None],
        section_sums[2][None],
        section_sums[3][None],
        section_sums[4][None],
        cross_sums[0],
        cross_sums[1],
        cross_sums[2],
        cross_sums[3],
    )


def split_rows(
    layer_input,
    segment_ids,
    attn_qkv,
    attn_out,
    ffn_in,
    ffn_out,
    norm_gain,
    cross_query,
    cross_pair,
    cross_out,
    cross_gain,
    out_cotangent,
):
    micros = layer_input.shape[1]
    length, width = layer_input.shape[3:]
    hidden = ffn_in.shape[-1]
    q_tiles = length // TILE
    group = lax.axis_size("dp") // 2
    axes = ("section", "seq", "dp")
    decoder = lax.axis_index("section") == 1
    flag = decoder.astype(jnp.int32)
    x = lax.axis_index("seq")
    core = lax.rem(lax.axis_index("dp"), 2)
    z = lax.axis_index("dp") // 2
    places = [(t, i, k, c) for t in range(2) for i in range(2) for k in range(group) for c in range(2)]

    def number(t, i, k, c):
        return ((t * 2 + i) * group + k) * 2 + c

    def send(values, target, section=None):
        route = [
            (number(*place), number(*target(*place)))
            for place in places
            if section in (None, place[0]) and target(*place)
        ]
        return lax.ppermute(values, axes, route)

    def to_core(t, i, k, c):
        return (t, i, k, 1 - c)

    def to_x(t, i, k, c):
        return (t, 1 - i, k, c)

    def to_row(t, i, k, c):
        return (t, c, k, i)

    def to_decoder(t, i, k, c):
        return (1, i, k, c) if t == 0 else None

    def to_encoder(t, i, k, c):
        return (0, i, k, c) if t == 1 else None

    def fence(values, *before):
        return lax.optimization_barrier((values,) + before)[0]

    def exchange(values):
        return send(values, to_core)

    low = ((length, width), bf16)
    wide = ((length, width), f32)
    marked = ((length + 16, width), bf16)
    both = ((2 * length, width), bf16)
    keys_all = ((2 * length, 2 * width), bf16)
    mixing = ((width, 3 * width), bf16)
    inner = ((length, hidden), bf16)
    lse = ((q_tiles, 8, 2 * TILE), f32)
    stat = ((length, LANES), f32)
    square = ((width, width), bf16)
    rising = ((width, hidden), bf16)
    falling = ((hidden, width), bf16)
    gain_rows = ((8, width), f32)

    meta = jnp.stack([flag, core, x, z]).astype(jnp.int32)
    numbers = segment_ids[0, :, 0].astype(bf16)
    padding = jnp.zeros((15, width), bf16)
    with_numbers = [
        jnp.concatenate([layer_input[0, micro, 0], numbers[micro][None], padding])
        for micro in range(micros)
    ]
    own = [send(with_numbers[0], to_row)]
    for micro in range(1, micros):
        own.append(send(fence(with_numbers[micro], own[-1]), to_row))
    other = [exchange(own[0])]

    plain = dict(meta=meta)
    small = dict(gains=norm_gain[0])
    forward, memories, memories_other = [], [], []
    for micro in range(micros):
        call = launch(
            self_forward,
            micro,
            None,
            plain,
            small,
            dict(
                x_own_h=own[micro],
                x_other_h=other[micro],
                w_mixed_h=attn_qkv[0],
                w_out_h=attn_out[0],
                w_in_h=ffn_in[0],
                w_down_h=ffn_out[0],
            ),
            dict(
                q_o=low,
                kv_o=keys_all,
                att_o=low,
                lse_o=lse,
                unit1_o=wide,
                inv1_o=stat,
                first_low_o=low,
                memory_o=marked,
                ffn_low_o=low,
                act_o=inner,
                slope_o=inner,
                unit2_o=wide,
                inv2_o=stat,
            ),
            dict(
                **attention_scratch(length, width),
                **forward_scratch(length, width),
                x=both,
                w_mixed=mixing,
                w_out=square,
                w_in=rising,
                w_down=falling,
                unit1=wide,
                inv1=stat,
                first_low=low,
                memory=marked,
                act=inner,
                slope=inner,
                unit2=wide,
                inv2=stat,
                sum=wide,
            ),
            28,
            26,
            after=(forward[0].lse_o,) if micro else (),
        )
        forward.append(call)
        memories.append(send(call.memory_o, to_decoder))
        if micro + 1 < micros:
            other.append(exchange(fence(own[micro + 1], call.lse_o)))

    for micro in range(micros):
        memories_other.append(exchange(fence(memories[micro], forward[-1].lse_o)))
    cotangent = send(fence(out_cotangent[:, 0], forward[0].lse_o), to_row)

    cross, grads_memory, made = [], [], []
    after = (forward[-1].lse_o,)
    for micro in range(micros):
        done = forward[micro]
        call = launch(
            cross_both_ways,
            micro,
            1,
            plain,
            dict(**small, cross_gain=cross_gain[None]),
            dict(
                x_own_h=own[micro],
                memory_own_h=memories[micro],
                memory_other_h=memories_other[micro],
                w_pair_h=cross_pair,
                first_low_h=done.first_low_o,
                unit1_h=done.unit1_o,
                w_query_h=cross_query,
                w_cross_h=cross_out,
                w_in_h=ffn_in[0],
                w_down_h=ffn_out[0],
                cot_h=cotangent,
            ),
            dict(
                att_o=low,
                ffn_low_o=low,
                act_o=inner,
                decoded_o=low,
                down_grad_o=low,
                up_grad_o=inner,
                gain_grads_o=gain_rows,
                branch_o=low,
                dq_low_o=low,
                dkv_o=keys_all,
                part_own_o=wide,
                part_other_o=low,
                grad_first_o=wide,
            ),
            dict(
                **attention_scratch(length, width),
                **forward_scratch(length, width),
                **backward_scratch(length, width),
                x=both,
                w_pair=((width, 2 * width), bf16),
                first_low=low,
                unit1=wide,
                w_query=square,
                w_cross=square,
                w_in=rising,
                w_down=falling,
                cot=low,
                unit2=wide,
                inv2=stat,
                second_low=low,
                act=inner,
                slope=inner,
                sum=wide,
                decoded=low,
                keep=wide,
                down_grad=low,
                up_grad=inner,
                gain_grads=gain_rows,
                branch=low,
                part_own=wide,
            ),
            36,
            44,
            dict(act_o=done.act_o, ffn_low_o=done.ffn_low_o),
            after,
        )
        cross.append(call)
        away = call.part_other_o
        if micro:
            away = fence(away, grads_memory[-1])
        total = call.part_own_o + exchange(away).astype(f32)
        made.append(total.astype(bf16))
        after = (made[micro],)
        grads_memory.append(send(made[micro], to_encoder))

    def backward_feed(micro, after):
        done, late = forward[micro], cross[micro]
        return launch(
            feed_backward_alone,
            micro,
            0,
            plain,
            dict(gains=norm_gain[0]),
            dict(
                grad_memory_h=grads_memory[micro],
                unit2_h=done.unit2_o,
                inv2_h=done.inv2_o,
                slope_h=done.slope_o,
                w_in_h=ffn_in[0],
                w_down_h=ffn_out[0],
            ),
            dict(gain_late_o=gain_rows, down_grad_o=low, up_grad_o=inner, grad_first_o=wide),
            dict(
                cot=low,
                unit2=wide,
                inv2=stat,
                slope=inner,
                w_in=rising,
                w_down=falling,
                gain_grads=gain_rows,
                keep=wide,
                down_grad=low,
                up_grad=inner,
                sum=wide,
            ),
            12,
            10,
            dict(
                down_grad_o=late.down_grad_o, up_grad_o=late.up_grad_o, grad_first_o=late.grad_first_o
            ),
            after,
        )

    def backward_self(micro, side, grad_first, previous=None, after=(), halfway=None):
        done = forward[micro]
        heads = width // LANES
        given = dict(
            x_own_h=own[micro],
            x_other_h=other[micro],
            q_h=done.q_o,
            kv_h=done.kv_o,
            att_h=done.att_o,
            lse_h=done.lse_o,
        )
        ahead = dict(
            grad_first_h=grad_first,
            unit1_h=done.unit1_o,
            inv1_h=done.inv1_o,
            w_out_h=attn_out[0],
        )
        makes = dict(dq_low_o=low, dkv_o=keys_all)
        makes_first = dict(gain_early_o=gain_rows, branch_o=low)
        makes_last = dict(part_own_o=wide, part_other_o=low)
        scratch = dict(
            **attention_scratch(length, width),
            **backward_scratch(length, width),
            w_out=square,
            w_mixed=mixing,
            unit1=wide,
            inv1=stat,
            keep=wide,
            branch=low,
            grad_att=low,
            gain_grads=gain_rows,
        )

        def part(first, last, large, outs, work, previous, after):
            return launch(
                self_backward,
                (micro, first, last),
                side,
                plain,
                small,
                dict(**given, **large),
                dict(**makes, **outs),
                scratch,
                28,
                work,
                previous,
                after,
            )

        if halfway is None:
            large = dict(**ahead, w_mixed_h=attn_qkv[0])
            outs = dict(**makes_first, **makes_last)
            return part(0, heads, large, outs, 22, previous, after)
        outs = dict(**makes_first, grad_sum_o=wide, grad_att_o=low)
        one = part(0, heads // 2, ahead, outs, 12, None, after)
        large = dict(
            w_mixed_h=attn_qkv[0],
            grad_sum_h=one.grad_sum_o,
            grad_att_h=one.grad_att_o,
            dq_h=one.dq_low_o,
            dkv_h=one.dkv_o,
        )
        two = part(heads // 2, heads, large, makes_last, 12, None, halfway(one))
        return types.SimpleNamespace(**{**vars(one), **vars(two)})

    def weight_grads(plan, side, arrays, scratch, after=()):
        blocks = ((2, width, width), bf16)
        call = launch(
            contract_blocks,
            plan,
            side,
            plain,
            dict(),
            arrays,
            dict(sent_o=blocks, kept_o=blocks),
            dict(**scratch, blocks=((4, width, width), bf16)),
            36,
            8,
            after=after,
        )
        return call.sent_o, call.kept_o

    def first_sums(halves, section=None):
        sent, kept = halves
        got = send(sent, to_core, section)

        def block(side):
            return sum(
                lax.dynamic_index_in_dim(part, side, 0, keepdims=False).astype(f32)
                for part in (kept, got)
            )

        return block(1 - x).astype(bf16), block(x)

    def middle_sums(sums, section=None):
        away, total = sums
        return (total + send(away, to_x, section).astype(f32)).astype(bf16)

    def last_sums(totals, *later):
        rows = width // group
        shares = jnp.concatenate([total.reshape(group, rows, width) for total in totals], axis=1)

        def share(step):
            return lax.dynamic_index_in_dim(shares, lax.rem(z + step, group), 0, keepdims=False)

        parts = [share(0)]
        for step in range(1, group):
            parts.append(send(share(step), along_z(step)))
        if later:
            parts = [fence(part, *later) for part in parts]
        return sum(part.astype(f32) for part in parts).astype(bf16)

    def along_z(step):
        return lambda t, i, k, c: (t, i, (k + step) % group, c)

    def gather_z(share):
        return [share] + [send(share, along_z(step)) for step in range(1, group)]

    def gain_block(rows):
        filled = jnp.concatenate([jnp.stack(rows), jnp.zeros((16 - len(rows), width), f32)])
        return filled.astype(bf16)

    def spread(targets, own, own_x, outs, parts):
        return launch(
            spread_pieces,
            targets,
            None,
            plain,
            dict(),
            dict(own_h=own, own_x_h=own_x, other_h=exchange(own), other_x_h=exchange(own_x)),
            outs,
            dict(
                pieces=((4,) + own.shape, bf16),
                wide=((4 * group * parts, width // group, width), f32),
            ),
            8 + 4 * group * parts,
            5,
        )

    tokens, all_tokens = micros * length, 2 * micros * length
    turn, turn_all = ((width, tokens), bf16), ((width, all_tokens), bf16)
    narrow, narrow_all = ((tokens, width), bf16), ((all_tokens, width), bf16)
    pair_all = ((all_tokens, 2 * width), bf16)
    deep = ((tokens, hidden), bf16)

    def part_of(buffer, *sources):
        return lambda column: (buffer, sources, column)

    def key_rows(buffer, sources):
        first, second = pl.ds(0, length), pl.ds(length, length)
        return part_of(buffer, *[source.at[rows] for rows in (first, second) for source in sources])

    def cross_plan(r):
        rows = pl.ds(0, length)
        low_part = part_of(r.low, r.low0_h, r.low1_h)
        att_part = part_of(r.att, r.att0_h, r.att1_h)
        dq_part = part_of(r.dq, r.dq0_h, r.dq1_h)
        branch_part = part_of(r.branch, r.branch0_h, r.branch1_h)
        sources = (r.mem0_h, r.mem1_h, r.mem2_h, r.mem3_h)
        mem_part = part_of(r.mem, *[source.at[rows] for source in sources])
        pair_part = key_rows(r.pair, (r.pair0_h, r.pair1_h))
        return [
            (r.turn, low_part(0), dq_part(0)),
            (r.turn_att, att_part(0), branch_part(0)),
            (r.turn_all, mem_part(0), pair_part(0)),
            (r.turn_all, mem_part(0), pair_part(1)),
        ]

    def rising_plan(r):
        low_part = part_of(r.low, r.low0_h, r.low1_h)
        up_part = part_of(r.up, r.up0_h, r.up1_h)
        return [(r.turn, low_part(0), up_part(block)) for block in range(4)]

    def falling_plan(r):
        act_part = part_of(r.act, r.act0_h, r.act1_h)
        down_part = part_of(r.down, r.down0_h, r.down1_h)
        return [(r.turn, act_part(block), down_part(0)) for block in range(4)]

    def self_plan(r):
        rows = pl.ds(0, length)
        sources = (r.x0_h, r.x1_h, r.x2_h, r.x3_h)
        x_part = part_of(r.x, *[source.at[rows] for source in sources])
        dq_part = part_of(r.dq, r.dq0_h, r.dq1_h)
        pair_part = key_rows(r.pair, (r.pair0_h, r.pair1_h))
        att_part = part_of(r.att, r.att0_h, r.att1_h)
        branch_part = part_of(r.branch, r.branch0_h, r.branch1_h)
        return [
            (r.turn_all, x_part(0), dq_part(0)),
            (r.turn_all, x_part(0), pair_part(0)),
            (r.turn_all, x_part(0), pair_part(1)),
            (r.turn, att_part(0), branch_part(0)),
        ]

    last = micros - 1
    feeds, ends = [None] * micros, [None] * micros
    cross_halves = weight_grads(
        cross_plan,
        1,
        dict(
            low0_h=forward[0].first_low_o,
            low1_h=forward[1].first_low_o,
            dq0_h=cross[0].dq_low_o,
            dq1_h=cross[1].dq_low_o,
            att0_h=cross[0].att_o,
            att1_h=cross[1].att_o,
            branch0_h=cross[0].branch_o,
            branch1_h=cross[1].branch_o,
            mem0_h=memories[0],
            mem1_h=memories[1],
            mem2_h=memories_other[0],
            mem3_h=memories_other[1],
            pair0_h=cross[0].dkv_o,
            pair1_h=cross[1].dkv_o,
        ),
        dict(
            low=narrow,
            dq=narrow,
            att=narrow,
            branch=narrow,
            mem=narrow_all,
            pair=pair_all,
            turn=turn,
            turn_att=turn,
            turn_all=turn_all,
        ),
        (made[last],),
    )
    cross_sums = first_sums(cross_halves, 1)
    results = jnp.stack(
        [
            jnp.where(decoder, call.decoded_o, done.memory_o[:length])
            for call, done in zip(cross, forward)
        ]
    )
    results = send(results, to_row)
    latest = made[last]

    def part_sum(micro, *before):
        end = ends[micro]
        away = fence(end.part_other_o, *before)
        total = (end.part_own_o + exchange(away).astype(f32)).astype(bf16)
        return total, send(total, to_row)

    steps = []
    for micro in range(last):
        feeds[micro] = backward_feed(micro, (latest,))
        first = feeds[micro].grad_first_o
        ends[micro] = backward_self(micro, 0, first)
        ends[micro] = backward_self(micro, 1, first, vars(ends[micro]), (cross_sums[0], grads_memory[last]))
        cross_total = middle_sums(cross_sums, 1)
        steps.append(part_sum(micro, cross_total))
        latest = ends[micro].gain_early_o
    feeds[last] = backward_feed(last, (latest,))

    rising_halves = weight_grads(
        rising_plan,
        None,
        dict(
            low0_h=cross[0].ffn_low_o,
            low1_h=cross[1].ffn_low_o,
            up0_h=feeds[0].up_grad_o,
            up1_h=feeds[1].up_grad_o,
        ),
        dict(low=narrow, up=deep, turn=turn),
        (results,) + tuple(step[0] for step in steps),
    )
    rising_sums = first_sums(rising_halves)
    rising_total = middle_sums(rising_sums)
    falling_halves = weight_grads(
        falling_plan,
        None,
        dict(
            act0_h=cross[0].act_o,
            act1_h=cross[1].act_o,
            down0_h=feeds[0].down_grad_o,
            down1_h=feeds[1].down_grad_o,
        ),
        dict(act=deep, down=narrow, turn=turn),
        (rising_sums[0],),
    )
    falling_sent = fence(falling_halves[0], rising_total)
    falling_sums = first_sums((falling_sent, falling_halves[1]))
    falling_total = middle_sums(falling_sums)
    shares = []

    third = sum(call.gain_grads_o[1] for call in cross)

    def halfway(one):
        both = last_sums((rising_total, cross_total), one.gain_early_o)
        rows = width // group
        found = jnp.concatenate([both[rows:], gain_block([third])])
        shares.extend([both[:rows], found, send(found, to_encoder)])
        return (both, falling_total)

    ends[last] = backward_self(
        last,
        None,
        feeds[last].grad_first_o,
        None,
        (falling_sums[0],),
        halfway,
    )
    finished = ends[last].part_own_o
    falling_share = last_sums((falling_total,), ends[last].gain_early_o, finished)
    rising_share, found, arrived = shares
    cross_share = jnp.where(decoder, found, fence(arrived, finished))
    one_own = gather_z(jnp.concatenate([rising_share, falling_share, cross_share]))
    steps.append(part_sum(last, falling_share, arrived, steps[0][1]))

    self_halves = weight_grads(
        self_plan,
        None,
        dict(
            x0_h=own[0],
            x1_h=own[1],
            x2_h=other[0],
            x3_h=other[1],
            dq0_h=ends[0].dq_low_o,
            dq1_h=ends[1].dq_low_o,
            pair0_h=ends[0].dkv_o,
            pair1_h=ends[1].dkv_o,
            att0_h=forward[0].att_o,
            att1_h=forward[1].att_o,
            branch0_h=ends[0].branch_o,
            branch1_h=ends[1].branch_o,
        ),
        dict(
            x=narrow_all,
            dq=narrow,
            pair=pair_all,
            att=narrow,
            branch=narrow,
            turn=turn,
            turn_all=turn_all,
        ),
        (steps[last][0],),
    )
    away, total = first_sums(
        (fence(self_halves[0], one_own[1], one_own[-1], steps[last][1]), self_halves[1])
    )
    self_total = middle_sums((away, total))
    self_share = last_sums((self_total,))
    sooner = sorted({0, 1, group - 1})
    later = [piece for piece in range(group) if piece not in sooner]
    for piece in range(1, group):
        ahead = self_total if piece in sooner else self_share
        one_own[piece] = fence(one_own[piece], ahead)
    one_own_x = [None] * group
    for pieces in (sooner, later):
        if pieces:
            moved = send(jnp.stack([one_own[piece] for piece in pieces]), to_x)
            for place, piece in enumerate(pieces):
                one_own_x[piece] = moved[place]
    one_own, one_own_x = jnp.stack(one_own), jnp.stack(one_own_x)

    early = sum(end.gain_early_o[0] for end in ends)
    late = jnp.where(
        decoder,
        sum(call.gain_grads_o[0] for call in cross),
        sum(call.gain_late_o[0] for call in feeds),
    )
    two_own = jnp.stack(
        gather_z(jnp.concatenate([self_share, gain_block([early, late])]))
    )
    two_own_x = send(fence(two_own, one_own_x), to_x)

    def columns(block):
        return pl.ds(block * width, width)

    def one_targets(r, block, row, rows):
        lines = pl.ds(row, rows)
        feed = [r.up_o.at[lines, columns(block)], r.down_o.at[pl.ds(block * width + row, rows)]]
        if block >= 2:
            return feed + [r.pair_o.at[lines, columns(block - 2)]]
        return feed + [(r.out_o if block else r.query_o).at[lines]]

    def two_targets(r, block, row, rows):
        lines = pl.ds(row, rows)
        return [r.out_o.at[lines] if block == 3 else r.mixed_o.at[lines, columns(block)]]

    square_out = ((width, width), f32)
    one_own_x = fence(one_own_x, two_own)
    one_grads = spread(
        one_targets,
        one_own,
        one_own_x,
        dict(
            up_o=((width, hidden), f32),
            query_o=square_out,
            pair_o=((width, 2 * width), f32),
            down_o=((hidden, width), f32),
            out_o=square_out,
            gains_o=((1, width), f32),
        ),
        3,
    )
    two_own_x = fence(two_own_x, one_grads.gains_o)
    two_grads = spread(
        two_targets,
        two_own,
        two_own_x,
        dict(
            mixed_o=((width, 3 * width), f32),
            out_o=square_out,
            gains_o=((2, width), f32),
        ),
        1,
    )

    grad_input = jnp.stack([step[1] for step in steps])
    return (
        results[None, :, None],
        grad_input.astype(f32)[None, :, None],
        two_grads.mixed_o[None],
        two_grads.out_o[None],
        one_grads.up_o[None],
        one_grads.down_o[None],
        two_grads.gains_o[None],
        one_grads.query_o,
        one_grads.pair_o,
        one_grads.out_o,
        one_grads.gains_o[0],
    )


def shards(*arrays):
    layer_input = arrays[0]
    micros, rows, length = layer_input.shape[1:4]
    simple = (
        lax.axis_size("section") == 2
        and lax.axis_size("seq") == 2
        and lax.axis_size("dp") in (4, 8, 16)
        and (micros, rows) == (2, 1)
        and length == layer_input.shape[-1] == CHUNK
        and arrays[4].shape[-1] == 4 * CHUNK
    )
    return split_rows(*arrays) if simple else any_rows(*arrays)


def solution(mesh):
    in_specs = (
        P("section", None, "dp", "seq", None),
        P("section", None, "dp", "seq"),
        P("section", None, None),
        P("section", None, None),
        P("section", None, None),
        P("section", None, None),
        P("section", None, None),
        P(),
        P(),
        P(),
        P(),
        P(None, "dp", "seq", None),
    )
    out_specs = (
        P("section", None, "dp", "seq", None),
        P("section", None, "dp", "seq", None),
        P("section", None, None),
        P("section", None, None),
        P("section", None, None),
        P("section", None, None),
        P("section", None, None),
        P(),
        P(),
        P(),
        P(),
    )
    return jax.shard_map(shards, mesh=mesh, in_specs=in_specs, out_specs=out_specs, check_vma=False)
```
